32 devices in a mesh: img: 4 (over y, core), row: 8 (over z, x).
Axes of the slice: x: 2, y: 2, z: 4, core: 2. Of those that a mesh axis runs over, the one named last changes fastest.
Arguments:
- image_small: float32 [16, 32, 1024], P('img', 'row'), may hold values from -6 to 6
- image_large: float32 [12, 64, 2048], P('img', 'row'), may hold values from -6 to 6
- teacher_small: float32 [16, 32, 32], P('img', 'row'), may hold values from 0 to 0.0625
- teacher_large: float32 [12, 64, 64], P('img', 'row'), may hold values from 0 to 0.03125
- upstream_small: float32 [16, 32, 1024], P('img', 'row'), may hold values from -1.2 to 1.2
- upstream_large: float32 [12, 64, 2048], P('img', 'row'), may hold values from -1.2 to 1.2
- conv_first: float32 [3, 3, 32, 32], replicated, may hold values from -0.375 to 0.375
- gain_first: float32 [32], replicated, may hold values from 0.1 to 1.9
- bias_first: float32 [32], replicated, may hold values from -3 to 3
- conv_second: float32 [3, 3, 32, 32], replicated, may hold values from -0.375 to 0.375
- gain_second: float32 [32], replicated, may hold values from 0.1 to 1.9
- bias_second: float32 [32], replicated, may hold values from -3 to 3
Outputs:
- out_small: float32 [16, 32, 1024], P('img', 'row')
- out_large: float32 [12, 64, 2048], P('img', 'row')
- back_small: float32 [16, 32, 1024], P('img', 'row')
- back_large: float32 [12, 64, 2048], P('img', 'row')
- first_conv_grad: float32 [3, 3, 32, 32], replicated
- first_gain_grad: float32 [32], replicated
- first_bias_grad: float32 [32], replicated
- second_conv_grad: float32 [3, 3, 32, 32], replicated
- second_gain_grad: float32 [32], replicated
- second_bias_grad: float32 [32], replicated
The draws below stay inside these ranges and needn't reach their ends.
All inputs are finite; a program needn't handle non-finite values.
Results may differ from the reference program's by a relative error of at most 0.0003.
Values sent between devices are 32-bit elements; how exact they have to be, the bound alone decides.
No kernel may reach another device: no remote copies, remote signals or barrier semaphores. Data moves between devices by JAX's collectives and lax.ppermute only.
A program may use at most 64 MiB of HBM per device.

```python
import jax
import jax.numpy as jnp
from jax import lax

C = 32
HS = 32
HL = 64
N_SMALL = 16
N_LARGE = 12
PIXELS = 65536


def shard_levels(stream_key, shape, cuts, least, largest):
    level, own = 1.0, jax.random.fold_in(stream_key, 6)
    for dim, shards_of in cuts:
        heights = jnp.exp(jax.random.uniform(jax.random.fold_in(own, dim), (shards_of,), jnp.float32, least / len(cuts), largest / len(cuts)))
        level = level * jnp.repeat(heights, shape[dim] // shards_of).reshape([-1 if axis == dim else 1 for axis in range(len(shape))])
    return level


def noise(stream_key, extent, spread, bound, split=(), kind=jnp.bfloat16):
    array = jax.random.normal(stream_key, extent, jnp.float32) * spread
    if len(split) > 0:
        array = shard_levels(stream_key, extent, split, -0.22, 0.18) * array
    return jnp.clip(array, min=-bound, max=bound).astype(kind)


def setup_inputs(seed: int = 0) -> dict:
    keys = jax.random.split(jax.random.key(seed), 13)
    return {
        "image_small": noise(keys[0], (N_SMALL, HS, HS * C), 1.0, 6.0, ((0, 4), (1, 8)), jnp.float32),
        "image_large": noise(keys[1], (N_LARGE, HL, HL * C), 1.0, 6.0, ((0, 4), (1, 8)), jnp.float32),
        "teacher_small": jnp.clip(0.0625 * jax.random.uniform(keys[2], (N_SMALL, HS, HS), jnp.float32) ** shard_levels(keys[2], (N_SMALL, HS, HS), ((0, 4), (1, 8)), -0.2, 0.2), 0.0, 0.0625),
        "teacher_large": jnp.clip(0.03125 * jax.random.uniform(keys[3], (N_LARGE, HL, HL), jnp.float32) ** shard_levels(keys[3], (N_LARGE, HL, HL), ((0, 4), (1, 8)), -0.2, 0.2), 0.0, 0.03125),
        "upstream_small": noise(keys[4], (N_SMALL, HS, HS * C), 0.2, 1.2, ((0, 4), (1, 8)), jnp.float32),
        "upstream_large": noise(keys[5], (N_LARGE, HL, HL * C), 0.2, 1.2, ((0, 4), (1, 8)), jnp.float32),
        "conv_first": noise(keys[6], (3, 3, C, C), (9 * C) ** -0.5, 0.375, (), jnp.float32),
        "gain_first": jnp.clip(1.0 + 0.18 * jax.random.normal(keys[7], (C,), jnp.float32), 0.1, 1.9),
        "bias_first": noise(keys[8], (C,), 0.5, 3.0, (), jnp.float32),
        "conv_second": noise(keys[9], (3, 3, C, C), (9 * C) ** -0.5, 0.375, (), jnp.float32),
        "gain_second": jnp.clip(1.0 + 0.18 * jax.random.normal(keys[10], (C,), jnp.float32), 0.1, 1.9),
        "bias_second": noise(keys[11], (C,), 0.5, 3.0, (), jnp.float32),
    }


@jax.custom_vjp
def low(v):
    return lax.optimization_barrier(v.astype(jnp.bfloat16)).astype(jnp.float32)

@jax.custom_vjp
def low_back(v):
    return v

def low_keep(v):
    return (low(v), None)

def low_pass(kept, grad):
    return (grad,)

def back_keep(v):
    return (v, None)

def back_low(kept, grad):
    return (low(grad),)
low.defvjp(low_keep, low_pass)
low_back.defvjp(back_keep, back_low)
norm_eps = 1e-05
map_eps = 1e-06
beta_weight = 1000.0

def conv_same(field, kernel):
    return lax.conv_general_dilated(field, kernel, (1, 1), ((1, 1), (1, 1)), dimension_numbers=('NHWC', 'HWIO', 'NHWC'), precision=lax.Precision.HIGHEST)

def norm_act(fields, gain, bias):
    total = sum((lax.optimization_barrier(jnp.sum(field, axis=(0, 1, 2))) for field in fields))
    center = total / PIXELS
    variance = sum((lax.optimization_barrier(jnp.sum(jnp.square(field - center), axis=(0, 1, 2))) for field in fields)) / PIXELS
    scale = lax.rsqrt(variance + norm_eps)
    return [jax.nn.gelu((field - center) * scale * gain + bias, approximate=True) for field in fields]

def map_loss(output, teacher):
    maps = lax.optimization_barrier(jnp.mean(output * output, axis=3))
    roots = jnp.sqrt(lax.optimization_barrier(jnp.sum(maps * maps, axis=(1, 2))) + map_eps)
    normal = maps / roots[:, None, None]
    return 0.5 * beta_weight * jnp.sum(jnp.square(normal - teacher))

def reference(image_small, image_large, teacher_small, teacher_large, upstream_small, upstream_large, conv_first, gain_first, bias_first, conv_second, gain_second, bias_second):

    def objective(small, large, kernel_one, gain_one, bias_one, kernel_two, gain_two, bias_two):
        fields = [small.reshape(N_SMALL, HS, HS, C), large.reshape(N_LARGE, HL, HL, C)]
        first = norm_act(fields, gain_one, bias_one)
        hidden = [conv_same(field, kernel_one) for field in first]
        second = norm_act(hidden, gain_two, bias_two)
        outputs = [field + conv_same(act, kernel_two) for field, act in zip(fields, second)]
        total = jnp.sum(outputs[0] * upstream_small.reshape(outputs[0].shape)) + jnp.sum(outputs[1] * upstream_large.reshape(outputs[1].shape))
        total = total + map_loss(outputs[0], teacher_small) + map_loss(outputs[1], teacher_large)
        return (total, (outputs[0], outputs[1]))
    total, pullback, outputs = jax.vjp(objective, image_small, image_large, conv_first, gain_first, bias_first, conv_second, gain_second, bias_second, has_aux=True)
    grads = pullback(jnp.ones_like(total))
    return (outputs[0].reshape(image_small.shape), outputs[1].reshape(image_large.shape), grads[0], grads[1], grads[2], grads[3], grads[4], grads[5], grads[6], grads[7])
```

```python
import jax
import jax.numpy as jnp
from jax import lax
from jax.sharding import PartitionSpec as P

C = 32
HS = 32
HL = 64

norm_eps = 1e-05
map_eps = 1e-06
beta_weight = 1000.0
AXES = ("img", "row")


def gather_direct(vector, axes):
    count = 1
    for axis in axes:
        count *= lax.axis_size(axis)
    copies = jnp.broadcast_to(vector[None], (count,) + vector.shape)
    return lax.all_to_all(copies, axes, 0, 0, tiled=True)


def gather_shifts(vector, axis):
    peers = lax.axis_size(axis)
    parts = [vector]
    for step in range(1, peers):
        parts.append(lax.ppermute(vector, axis, [(i, (i + step) % peers) for i in range(peers)]))
    return jnp.stack(parts)


def rims(fields):
    peers = lax.axis_size("row")
    last = jnp.concatenate([field[:, -1].reshape(-1) for field in fields])
    first = jnp.concatenate([field[:, 0].reshape(-1) for field in fields])
    above = lax.ppermute(last, "row", [(i, i + 1) for i in range(peers - 1)])
    below = lax.ppermute(first, "row", [(i + 1, i) for i in range(peers - 1)])
    result = []
    offset = 0
    for field in fields:
        images, _, width, chans = field.shape
        size = images * width * chans
        result.append(
            (
                above[offset : offset + size].reshape(images, 1, width, chans),
                below[offset : offset + size].reshape(images, 1, width, chans),
            )
        )
        offset += size
    return result


def edge_mask():
    at = lax.axis_index("row")
    return (at > 0).astype(jnp.float32), (at < lax.axis_size("row") - 1).astype(jnp.float32)


def padded(fields, edges, function):
    top, bottom = edge_mask()
    return [
        jnp.concatenate([function(above) * top, function(field), function(below) * bottom], axis=1)
        for field, (above, below) in zip(fields, edges)
    ]


def conv_rows(field, kernel):
    return lax.conv_general_dilated(
        field, kernel, (1, 1), ((0, 0), (1, 1)), dimension_numbers=("NHWC", "HWIO", "NHWC"), precision=lax.Precision.HIGHEST
    )


def flipped(kernel):
    return jnp.transpose(kernel[::-1, ::-1], (0, 1, 3, 2))


def kernel_grad(padded_list, upstream_list, kernel):
    total = jnp.zeros(kernel.shape, jnp.float32)
    for field, upstream in zip(padded_list, upstream_list):
        total = total + jax.vjp(lambda weights: conv_rows(field, weights), kernel)[1](upstream)[0]
    return total


def gelu_tanh(value):
    return jax.nn.gelu(value, approximate=True)


def channel_sums(fields):
    return sum((jnp.sum(field, axis=(0, 1, 2)) for field in fields))


def local_moments(fields):
    count = float(sum(f.shape[0] * f.shape[1] * f.shape[2] for f in fields))
    center = channel_sums(fields) / count
    spread = channel_sums([jnp.square(field - center) for field in fields])
    return jnp.concatenate([center, spread]), count


def merge_moments(gathered, count):
    means, spreads = gathered[:, :C], gathered[:, C:]
    center = jnp.mean(means, axis=0)
    variance = jnp.mean(spreads, axis=0) / count + jnp.mean(jnp.square(means - center), axis=0)
    return center, lax.rsqrt(variance + norm_eps)


def local(
    image_small, image_large, teacher_small, teacher_large, upstream_small, upstream_large,
    conv_first, gain_first, bias_first, conv_second, gain_second, bias_second,
):
    devices = lax.axis_size("img") * lax.axis_size("row")
    fields = [
        image_small.reshape(image_small.shape[0], image_small.shape[1], HS, C),
        image_large.reshape(image_large.shape[0], image_large.shape[1], HL, C),
    ]
    input_rims = rims(fields)
    moments, count = local_moments(fields)
    pixels = count * devices
    center_one, scale_one = merge_moments(gather_direct(moments, AXES), count)

    def shift_one(value):
        return (value - center_one) * scale_one * gain_first + bias_first

    padded_one = padded(fields, input_rims, lambda v: gelu_tanh(shift_one(v)))
    hidden = [conv_rows(value, conv_first) for value in padded_one]
    hidden_rims = rims(hidden)
    moments, _ = local_moments(hidden)
    by_row = gather_shifts(moments, "row")
    by_all = gather_shifts(by_row, "img").reshape(devices, 2 * C)
    center_two, scale_two = merge_moments(by_all, count)

    def shift_two(value):
        return (value - center_two) * scale_two * gain_second + bias_second

    padded_two = padded(hidden, hidden_rims, lambda v: gelu_tanh(shift_two(v)))
    outputs = [field + conv_rows(value, conv_second) for field, value in zip(fields, padded_two)]
    teachers = [teacher_small, teacher_large]
    maps = [jnp.mean(output * output, axis=3) for output in outputs]
    squares = [jnp.sum(value * value, axis=(1, 2)) for value in maps]
    crosses = [jnp.sum(value * teacher, axis=(1, 2)) for value, teacher in zip(maps, teachers)]
    images = [image_small.shape[0], image_large.shape[0]]
    sums = jnp.sum(gather_direct(jnp.concatenate(squares + crosses), ("row",)), axis=0)
    square = jnp.split(sums[: images[0] + images[1]], [images[0]])
    cross = jnp.split(sums[images[0] + images[1] :], [images[0]])
    upstream = []
    for value, teacher, s, x, output, up in zip(maps, teachers, square, cross, outputs, [upstream_small, upstream_large]):
        root = jnp.sqrt(s + map_eps)
        inner = beta_weight * (s / (root * root) - x / root)
        root, inner = root[:, None, None], inner[:, None, None]
        normal = value / root
        map_grad = (beta_weight * (normal - teacher) - normal * inner) / root
        upstream.append(up.reshape(output.shape) + map_grad[..., None] * (2.0 / C) * output)
    grad_rims = rims(upstream)
    kernel_two = kernel_grad(padded_two, upstream, conv_second)
    second_grad = [conv_rows(v, flipped(conv_second)) for v in padded(upstream, grad_rims, lambda v: v)]
    pre_two = [jax.vjp(gelu_tanh, shift_two(v))[1](g)[0] for v, g in zip(hidden, second_grad)]
    normed_two = [(v - center_two) * scale_two for v in hidden]
    pre_rims = rims(pre_two)
    parts = jnp.concatenate([channel_sums(pre_two), channel_sums([g * v for g, v in zip(pre_two, normed_two)])])
    sums_two = jnp.sum(lax.all_gather(parts, AXES), axis=0)
    bias_two_grad, gain_two_grad = sums_two[:C], sums_two[C:]
    normed_rims = [tuple((v - center_two) * scale_two for v in pair) for pair in hidden_rims]

    def back_two(grad, normed):
        return gain_second * scale_two * (grad - bias_two_grad / pixels - normed * gain_two_grad / pixels)

    top, bottom = edge_mask()
    hidden_grad = [back_two(g, n) for g, n in zip(pre_two, normed_two)]
    padded_grad = [
        jnp.concatenate([back_two(gr[0], nr[0]) * top, g, back_two(gr[1], nr[1]) * bottom], axis=1)
        for g, gr, nr in zip(hidden_grad, pre_rims, normed_rims)
    ]
    kernel_one = kernel_grad(padded_one, hidden_grad, conv_first)
    first_grad = [conv_rows(v, flipped(conv_first)) for v in padded_grad]
    pre_one = [jax.vjp(gelu_tanh, shift_one(v))[1](g)[0] for v, g in zip(fields, first_grad)]
    normed_one = [(v - center_one) * scale_one for v in fields]
    parts = jnp.concatenate([channel_sums(pre_one), channel_sums([g * v for g, v in zip(pre_one, normed_one)])])
    grads = jnp.concatenate([kernel_one.reshape(devices, -1), kernel_two.reshape(devices, -1)], axis=1)
    packed = jnp.concatenate([jnp.broadcast_to(parts, (devices, 2 * C)), grads], axis=1)
    summed = jnp.sum(lax.all_to_all(packed, AXES, 0, 0, tiled=True), axis=0)
    bias_one_grad, gain_one_grad = summed[:C], summed[C : 2 * C]
    kernels = gather_direct(summed[2 * C :], AXES)
    half = kernels.shape[1] // 2
    kernel_one_sum = kernels[:, :half].reshape(conv_first.shape)
    kernel_two_sum = kernels[:, half:].reshape(conv_second.shape)
    back = [
        up + gain_first * scale_one * (g - bias_one_grad / pixels - n * gain_one_grad / pixels)
        for up, g, n in zip(upstream, pre_one, normed_one)
    ]
    return (
        outputs[0].reshape(image_small.shape),
        outputs[1].reshape(image_large.shape),
        back[0].reshape(image_small.shape),
        back[1].reshape(image_large.shape),
        kernel_one_sum, gain_one_grad, bias_one_grad,
        kernel_two_sum, gain_two_grad, bias_two_grad,
    )


def solution(mesh):
    split, whole = P("img", "row", None), P()
    return jax.shard_map(
        local, mesh=mesh, in_specs=(split,) * 6 + (whole,) * 6, out_specs=(split,) * 4 + (whole,) * 6, check_vma=False
    )
```

```python
import functools
import math

import jax
import jax.numpy as jnp
from jax import lax
from jax.experimental import pallas as pl
from jax.experimental.pallas import tpu as pltpu
from jax.sharding import PartitionSpec as P

C = 32
HS = 32
HL = 64

norm_eps = 1e-05
map_eps = 1e-06
beta_weight = 1000.0
AXES = ("img", "row")
BLOCK = 8
LANES = BLOCK * C
TAPS = 3
DEPTH = TAPS * (LANES + 128)
ROOT = math.sqrt(2.0 / math.pi)
CUBE = 0.044715
F32 = jnp.float32


class Sizes:
    def __init__(self, small, large, devices, peers):
        self.images = (small[0], large[0])
        self.rows = (small[1], large[1])
        self.blocks = (HS // BLOCK, HL // BLOCK)
        self.step = tuple(n * r for n, r in zip(self.images, self.rows))
        self.count = tuple(b * s for b, s in zip(self.blocks, self.step))
        self.edge = tuple(b * n for b, n in zip(self.blocks, self.images))
        self.start = (self.count[1], 0)
        self.rim = (self.edge[1], 0)
        self.total = sum(self.count)
        self.rims = sum(self.edge)
        self.all_images = sum(self.images)
        self.slots = -(-self.all_images // 8) * 8
        self.devices = devices
        self.peers = peers
        self.here = float(self.total * BLOCK)
        self.pixels = self.here * devices


def dot(left, right):
    return lax.dot_general(left, right, (((1,), (0,)), ((), ())), precision=lax.Precision.HIGHEST, preferred_element_type=F32)


def gelu(s):
    return 0.5 * s * (1.0 + jnp.tanh(ROOT * (s + CUBE * s * s * s)))


def gelu_slope(s):
    square = s * s
    t = jnp.tanh(ROOT * s * (1.0 + CUBE * square))
    return 0.5 * (1.0 + t) + 0.5 * s * (1.0 - t * t) * ROOT * (1.0 + 3.0 * CUBE * square)


def fold(row):
    half = row[:, :128] + row[:, 128:]
    half = half + pltpu.roll(half, 64, 1)
    return half + pltpu.roll(half, 32, 1)


def wide(row):
    return jnp.concatenate([row, row], axis=1)


def store_copies(ref, first, second):
    both = jnp.concatenate([first, second], axis=0)
    ref[...] = jnp.broadcast_to(both[None], ref.shape)


def moments(z, value, ref):
    center = fold(jnp.sum(value, axis=0, keepdims=True)) / z.here
    off = value - wide(center)
    store_copies(ref, center, fold(jnp.sum(off * off, axis=0, keepdims=True)))


def merged(z, ref):
    gathered = ref[...]
    mean = jnp.mean(gathered, axis=0)
    center = mean[0:1]
    off = gathered[:, 0, :] - center
    variance = mean[1:2] / z.here + jnp.mean(off * off, axis=0, keepdims=True)
    return wide(center), wide(lax.rsqrt(variance + norm_eps))


def take_rims(z, ref, top, bottom):
    for k in (0, 1):
        rows = z.rows[k]
        out = pl.ds(z.rim[k], z.edge[k])
        for h in (0, 1):
            lanes = pl.ds(128 * h, 128)
            top[out, lanes] = ref[h, pl.ds(z.start[k], z.edge[k], stride=rows), :]
            bottom[out, lanes] = ref[h, pl.ds(z.start[k] + rows - 1, z.edge[k], stride=rows), :]


def put_halves(ref, value):
    ref[0] = value[:, :128]
    ref[1] = value[:, 128:]


def to_matrix(z, refs, half_ref):
    for k in (0, 1):
        for j in range(z.blocks[k]):
            at = z.start[k] + j * z.step[k]
            for i in range(z.images[k]):
                for h in (0, 1):
                    half_ref[h, pl.ds(at + i * z.rows[k], z.rows[k]), :] = refs[k][i, :, pl.ds(LANES * j + 128 * h, 128)]


def from_matrix(z, half_ref, refs):
    for k in (0, 1):
        for j in range(z.blocks[k]):
            at = z.start[k] + j * z.step[k]
            for i in range(z.images[k]):
                for h in (0, 1):
                    refs[k][i, :, pl.ds(LANES * j + 128 * h, 128)] = half_ref[h, pl.ds(at + i * z.rows[k], z.rows[k]), :]


def pad_shapes(z):
    return [(TAPS, 2, z.count[k] + 2 * z.step[k], 128) for k in (0, 1)]


def fill_pad(z, pads, value, above, below):
    for k in (0, 1):
        ref, step, count, rows = pads[k], z.step[k], z.count[k], z.rows[k]
        for h in (0, 1):
            lanes = slice(128 * h, 128 * h + 128)
            part = value[z.start[k] : z.start[k] + count, lanes]
            for a in range(TAPS):
                ref[a, h, pl.ds(0, step), :] = jnp.zeros((step, 128), F32)
                ref[a, h, pl.ds(step + count, step), :] = jnp.zeros((step, 128), F32)
            ref[1, h, pl.ds(step, count), :] = part
            ref[0, h, pl.ds(step, count), :] = ref[1, h, pl.ds(step - 1, count), :]
            ref[2, h, pl.ds(step, count), :] = ref[1, h, pl.ds(step + 1, count), :]
            ref[0, h, pl.ds(step, z.edge[k], stride=rows), :] = above[z.rim[k] : z.rim[k] + z.edge[k], lanes]
            ref[2, h, pl.ds(step + rows - 1, z.edge[k], stride=rows), :] = below[z.rim[k] : z.rim[k] + z.edge[k], lanes]


def operand(z, pads):
    lane = lax.broadcasted_iota(jnp.int32, (1, 128), 1)
    parts = []
    for k in (1, 0):
        ref, step, count = pads[k], z.step[k], z.count[k]
        columns = []
        for a in range(TAPS):
            before = ref[a, 1, pl.ds(0, count), :]
            after = ref[a, 0, pl.ds(2 * step, count), :]
            columns += [
                ref[a, 0, pl.ds(step, count), :],
                ref[a, 1, pl.ds(step, count), :],
                jnp.where(lane >= 96, before, jnp.where(lane < 32, after, 0.0)),
            ]
        parts.append(jnp.concatenate(columns, axis=1))
    return jnp.concatenate(parts, axis=0)


def edges(z):
    at = lax.axis_index("row")
    return jnp.where(at > 0, 1.0, 0.0).astype(F32), jnp.where(at < z.peers - 1, 1.0, 0.0).astype(F32)


def image_of(z, rims, rows):
    m = lax.broadcasted_iota(jnp.int32, (rows, z.slots), 0)
    slot = lax.broadcasted_iota(jnp.int32, (rows, z.slots), 1)
    start = z.rim if rims else z.start
    height = (1, 1) if rims else z.rows
    small, large = m - start[0], m
    image = jnp.where(
        m >= start[0],
        (small // height[0]) % z.images[0],
        z.images[0] + (large // height[1]) % z.images[1],
    )
    return jnp.where(image == slot, 1.0, 0.0).astype(F32)


def channel_mean():
    a = lax.broadcasted_iota(jnp.int32, (LANES, LANES), 0) // C
    b = lax.broadcasted_iota(jnp.int32, (LANES, LANES), 1) // C
    return jnp.where(a == b, 1.0 / C, 0.0).astype(F32)


def start_kernel(z, small, large, x_ref, copies, top, bottom, half):
    to_matrix(z, (small, large), half)
    take_rims(z, half, top, bottom)
    value = jnp.concatenate([half[0], half[1]], axis=1)
    x_ref[...] = value
    moments(z, value, copies)


def prepare_kernel(z, up_small, up_large, t_small, t_large, first, second, u_ref, t_ref, w1, w2, w1t, w2t, top, bottom, half, half_t, flat):
    to_matrix(z, (up_small, up_large), half)
    u_ref[...] = jnp.concatenate([half[0], half[1]], axis=1)
    take_rims(z, half, top.at[0], bottom.at[0])
    for k, ref in ((0, t_small), (1, t_large)):
        width = (HS, HL)[k]
        n = z.step[k]
        for i in range(z.images[k]):
            flat[pl.ds(i * z.rows[k], z.rows[k]), pl.ds(0, width)] = ref[i]
        pixel = lax.broadcasted_iota(jnp.int32, (width, width * C), 0)
        lane = lax.broadcasted_iota(jnp.int32, (width, width * C), 1) // C
        spread = dot(flat[pl.ds(0, n), pl.ds(0, width)], jnp.where(pixel == lane, 1.0, 0.0).astype(F32))
        for j in range(z.blocks[k]):
            for h in (0, 1):
                at = LANES * j + 128 * h
                half_t[h, pl.ds(z.start[k] + j * n, n), :] = spread[:, at : at + 128]
    t_ref[...] = jnp.concatenate([half_t[0], half_t[1]], axis=1)
    take_rims(z, half_t, top.at[1], bottom.at[1])
    row = lax.broadcasted_iota(jnp.int32, (LANES, LANES), 0) // C
    lane = lax.broadcasted_iota(jnp.int32, (LANES, LANES), 1) // C
    edge_row, edge_lane = row[:128], lane[:128]
    left = (edge_row == 3) & (edge_lane == 0)
    right = (edge_row == 0) & (edge_lane == BLOCK - 1)
    for source, forward, backward in ((first, w1, w1t), (second, w2, w2t)):
        for a in range(TAPS):
            tiles, turned = [], []
            for b in range(TAPS):
                tap = source[a, b]
                tap = jnp.concatenate([tap] * 4, axis=1)
                tap = jnp.concatenate([tap] * 4, axis=0)
                tiles.append(tap)
                turned.append(tap.T)
            for taps, ref, at in ((tiles, forward, a), (turned[::-1], backward, TAPS - 1 - a)):
                base = at * (LANES + 128)
                main = jnp.zeros((LANES, LANES), F32)
                for b in range(TAPS):
                    line = jnp.concatenate([taps[b], taps[b]], axis=1)
                    full = jnp.concatenate([line, line], axis=0)
                    main = jnp.where(row - lane + 1 == b, full, main)
                ref[pl.ds(base, LANES), :] = main
                before = jnp.concatenate([taps[0], taps[0]], axis=1)
                after = jnp.concatenate([taps[2], taps[2]], axis=1)
                ref[pl.ds(base + LANES, 128), :] = jnp.where(left, before, jnp.where(right, after, 0.0))


def first_kernel(z, x, above, below, gathered, affine, weight, hidden, pad_s, pad_l, stats, copies, top, bottom, half):
    center, scale = merged(z, gathered)
    gain, bias = affine[0:1], affine[1:2]
    has_above, has_below = edges(z)

    def act(v):
        return gelu((v - center) * scale * gain + bias)

    pads = (pad_s, pad_l)
    fill_pad(z, pads, act(x[...]), act(above[...]) * has_above, act(below[...]) * has_below)
    value = dot(operand(z, pads), weight[...])
    hidden[...] = value
    put_halves(half, value)
    take_rims(z, half, top, bottom)
    stats[0:1] = center
    stats[1:2] = scale
    moments(z, value, copies)


def second_kernel(z, hidden, above, below, gathered, affine, weight, x, teacher, out_s, out_l, out, pad_s, pad_l, stats, copies, top, bottom, half):
    center, scale = merged(z, gathered)
    gain, bias = affine[2:3], affine[3:4]
    has_above, has_below = edges(z)

    def act(v):
        return gelu((v - center) * scale * gain + bias)

    pads = (pad_s, pad_l)
    fill_pad(z, pads, act(hidden[...]), act(above[...]) * has_above, act(below[...]) * has_below)
    value = x[...] + dot(operand(z, pads), weight[...])
    out[...] = value
    put_halves(half, value)
    take_rims(z, half, top, bottom)
    from_matrix(z, half, (out_s, out_l))
    stats[0:1] = center
    stats[1:2] = scale
    amap = dot(value * value, channel_mean())
    both = jnp.concatenate([amap * amap, amap * teacher[...]], axis=1)
    owner = image_of(z, False, z.total)
    sums = lax.dot_general(owner, both, (((0,), (0,)), ((), ())), precision=lax.Precision.HIGHEST, preferred_element_type=F32)
    square = jnp.sum(sums[:, :LANES], axis=1, keepdims=True) / C
    cross = jnp.sum(sums[:, LANES:], axis=1, keepdims=True) / C
    lane = lax.broadcasted_iota(jnp.int32, (z.slots, 128), 1)
    copies[...] = jnp.broadcast_to(jnp.where(lane < 64, square, cross)[None], copies.shape)


def upstream_kernel(z, gathered, out, above, below, up, teacher, more_above, more_below, weight, hidden, stats, affine, dout, dshift, copies, top, bottom, pad_s, pad_l, half):
    sums = jnp.sum(gathered[...], axis=0)
    square, cross = sums[:, 0:1], sums[:, 64:65]
    inverse = lax.rsqrt(square + map_eps)
    inner = beta_weight * (square * inverse - cross) * inverse
    lane = lax.broadcasted_iota(jnp.int32, (z.slots, LANES), 1)
    pair = jnp.concatenate([jnp.broadcast_to(inverse, (z.slots, LANES)), jnp.broadcast_to(inner, (z.slots, LANES))], axis=1)
    mean = channel_mean()

    def grad(o, u, t, rims):
        per_row = dot(image_of(z, rims, o.shape[0]), pair)
        inv, inn = per_row[:, :LANES], per_row[:, LANES:]
        q = dot(o * o, mean) * inv
        return u + (beta_weight * (q - t) - q * inn) * inv * (2.0 / C) * o

    has_above, has_below = edges(z)
    value = grad(out[...], up[...], teacher[...], False)
    dout[...] = value
    pads = (pad_s, pad_l)
    fill_pad(
        z,
        pads,
        value,
        grad(above[...], more_above[0], more_above[1], True) * has_above,
        grad(below[...], more_below[0], more_below[1], True) * has_below,
    )
    back = dot(operand(z, pads), weight[...])
    normed = (hidden[...] - stats[0:1]) * stats[1:2]
    pre = back * gelu_slope(normed * affine[2:3] + affine[3:4])
    dshift[...] = pre
    put_halves(half, pre)
    take_rims(z, half, top, bottom)
    store_copies(copies, fold(jnp.sum(pre, axis=0, keepdims=True)), fold(jnp.sum(pre * normed, axis=0, keepdims=True)))


def tap_sums(product, column, rows):
    lane = lax.broadcasted_iota(jnp.int32, (1, LANES), 1) // C
    edge = lax.broadcasted_iota(jnp.int32, (1, 128), 1) // C
    packed = [jnp.zeros((rows, 128), F32) for _ in range(3)]
    for a in range(TAPS):
        base = a * (LANES + 128)
        for b in range(TAPS):
            total = jnp.zeros((rows, LANES), F32)
            for p in range(BLOCK):
                part = column(product, p)
                if 0 <= p + b - 1 < BLOCK:
                    total = total + jnp.where(lane == p + b - 1, part[:, base : base + LANES], 0.0)
                else:
                    side = jnp.where(edge == (3 if b == 0 else 0), part[:, base + LANES : base + LANES + 128], 0.0)
                    total = total + jnp.concatenate([side, jnp.zeros((rows, 128), F32)], axis=1)
            narrow = fold(total)
            tap = a * TAPS + b
            packed[tap // 4] = jnp.where(edge == tap % 4, narrow, packed[tap // 4])
    return jnp.concatenate(packed, axis=1)


def kernel_grad_kernel(z, dout, dshift, hidden, stats, pad2_s, pad2_l, pad1_s, pad1_l, packed):
    left = operand(z, (pad2_s, pad2_l))

    def blocks(product, p):
        return product[p * C : p * C + C]

    packed[:, pl.ds(0, 384)] = tap_sums(dot(dout[...].T, left), blocks, C)
    left = operand(z, (pad1_s, pad1_l))
    packed[:, pl.ds(384, 384)] = tap_sums(dot(dshift[...].T, left), blocks, C)
    normed = (hidden[...] - stats[0:1]) * stats[1:2]
    packed[:, pl.ds(768, 384)] = tap_sums(dot(normed.T, left), blocks, C)
    ones = jnp.broadcast_to(jnp.sum(left, axis=0, keepdims=True), (C, DEPTH))
    packed[:, pl.ds(1152, 384)] = tap_sums(ones, lambda product, p: product, C)


def sum_kernel(parts, copies):
    copies[...] = jnp.broadcast_to(jnp.sum(parts[...], axis=0, keepdims=True), copies.shape)


def norm_sums(ref):
    sums = jnp.sum(ref[...], axis=0)
    return sums[0:1], sums[1:2]


def hidden_kernel(z, gathered, dshift, above, below, hidden, hidden_above, hidden_below, stats, affine, weight, x, first_stats, pre_ref, copies, gain_out, bias_out, pad_s, pad_l):
    bias_sum, gain_sum = norm_sums(gathered)
    bias_out[...] = bias_sum[:, :C]
    gain_out[...] = gain_sum[:, :C]
    bias_mean, gain_mean = wide(bias_sum) / z.pixels, wide(gain_sum) / z.pixels
    center, scale, gain = stats[0:1], stats[1:2], affine[2:3]
    has_above, has_below = edges(z)

    def back(d, h):
        return gain * scale * (d - bias_mean - (h - center) * scale * gain_mean)

    pads = (pad_s, pad_l)
    fill_pad(
        z,
        pads,
        back(dshift[...], hidden[...]),
        back(above[...], hidden_above[...]) * has_above,
        back(below[...], hidden_below[...]) * has_below,
    )
    grad = dot(operand(z, pads), weight[...])
    normed = (x[...] - first_stats[0:1]) * first_stats[1:2]
    pre = grad * gelu_slope(normed * affine[0:1] + affine[1:2])
    pre_ref[...] = pre
    store_copies(copies, fold(jnp.sum(pre, axis=0, keepdims=True)), fold(jnp.sum(pre * normed, axis=0, keepdims=True)))


def back_kernel(z, gathered, pre, x, stats, affine, dout, back_s, back_l, gain_out, bias_out, half):
    bias_sum, gain_sum = norm_sums(gathered)
    bias_out[...] = bias_sum[:, :C]
    gain_out[...] = gain_sum[:, :C]
    bias_mean, gain_mean = wide(bias_sum) / z.pixels, wide(gain_sum) / z.pixels
    scale = stats[1:2]
    normed = (x[...] - stats[0:1]) * scale
    value = dout[...] + affine[0:1] * scale * (pre[...] - bias_mean - normed * gain_mean)
    put_halves(half, value)
    from_matrix(z, half, (back_s, back_l))


def finish_kernel(z, total, gathered, stats, affine, one, two):
    bias_sum, gain_sum = norm_sums(gathered)
    factor = affine[2:3, :128] * stats[1:2, :128]
    value = total[...]
    second = value[:, :384].T
    g1, g2, f = value[:, 384:768].T, value[:, 768:1152].T, value[:, 1152:1536].T
    lanes = slice(0, C)
    first = factor[:, lanes] * (g1 - (bias_sum[:, lanes] / z.pixels) * f - (gain_sum[:, lanes] / z.pixels) * g2)
    for a in range(TAPS):
        for b in range(TAPS):
            at = (a * TAPS + b) * C
            one[a, b] = first[at : at + C]
            two[a, b] = second[at : at + C]


def call(body, outs, scratch=()):
    vmem = pl.BlockSpec(memory_space=pltpu.VMEM)

    def run(*args):
        return pl.pallas_call(
            body,
            out_shape=[jax.ShapeDtypeStruct(shape, F32) for shape in outs],
            in_specs=[vmem] * len(args),
            out_specs=[vmem] * len(outs),
            scratch_shapes=[pltpu.VMEM(shape, F32) for shape in scratch],
            compiler_params=pltpu.CompilerParams(vmem_limit_bytes=32 * 1024 * 1024),
        )(*args)

    return run


def exchange(copies, axes):
    return lax.all_to_all(copies, axes, 0, 0, tiled=True)


def neighbours(z, top, bottom):
    above = lax.ppermute(bottom, "row", [(i, i + 1) for i in range(z.peers - 1)])
    below = lax.ppermute(top, "row", [(i + 1, i) for i in range(z.peers - 1)])
    return above, below


def local(
    image_small, image_large, teacher_small, teacher_large, upstream_small, upstream_large,
    conv_first, gain_first, bias_first, conv_second, gain_second, bias_second,
):
    peers = lax.axis_size("row")
    devices = lax.axis_size("img") * peers
    z = Sizes(image_small.shape, image_large.shape, devices, peers)
    body = lambda function: functools.partial(function, z)
    full, rim, half = (z.total, LANES), (z.rims, LANES), (2, z.total, 128)
    pads, pair, stats = pad_shapes(z), (devices, 2, 128), (2, LANES)
    weight = (DEPTH, LANES)
    affine = jnp.tile(jnp.stack([gain_first, bias_first, gain_second, bias_second]), (1, BLOCK))

    x, copies, top, bottom = call(body(start_kernel), [full, pair, rim, rim], [half])(image_small, image_large)
    x_above, x_below = neighbours(z, top, bottom)
    gathered_one = exchange(copies, AXES)
    up, teacher, w1, w2, w1t, w2t, top, bottom = call(
        body(prepare_kernel),
        [full, full] + [weight] * 4 + [(2,) + rim] * 2,
        [half, half, (max(z.step), HL)],
    )(upstream_small, upstream_large, teacher_small, teacher_large, conv_first, conv_second)
    more_above, more_below = neighbours(z, top, bottom)

    hidden, pad1_s, pad1_l, stats_one, copies, top, bottom = call(
        body(first_kernel), [full] + pads + [stats, pair, rim, rim], [half]
    )(x, x_above, x_below, gathered_one, affine, w1)
    h_above, h_below = neighbours(z, top, bottom)
    gathered_two = exchange(copies, AXES)

    out_s, out_l, out, pad2_s, pad2_l, stats_two, copies, top, bottom = call(
        body(second_kernel),
        [image_small.shape, image_large.shape, full] + pads + [stats, (peers, z.slots, 128), rim, rim],
        [half],
    )(hidden, h_above, h_below, gathered_two, affine, w2, x, teacher)
    o_above, o_below = neighbours(z, top, bottom)
    sums = exchange(copies, ("row",))

    dout, dshift, copies, top, bottom = call(
        body(upstream_kernel), [full, full, pair, rim, rim], pads + [half]
    )(sums, out, o_above, o_below, up, teacher, more_above, more_below, w2t, hidden, stats_two, affine)
    d_above, d_below = neighbours(z, top, bottom)
    gathered_back = exchange(copies, AXES)

    (packed,) = call(body(kernel_grad_kernel), [(C, 4 * 384)])(
        dout, dshift, hidden, stats_two, pad2_s, pad2_l, pad1_s, pad1_l
    )
    parts = exchange(packed.reshape(devices, -1), AXES)
    (copies_grad,) = call(sum_kernel, [parts.shape])(parts)
    total = exchange(copies_grad, AXES).reshape(packed.shape)

    pre, copies, gain_two, bias_two = call(body(hidden_kernel), [full, pair, (1, C), (1, C)], pads)(
        gathered_back, dshift, d_above, d_below, hidden, h_above, h_below, stats_two, affine, w1t, x, stats_one
    )
    gathered_last = exchange(copies, AXES)
    back_s, back_l, gain_one, bias_one = call(
        body(back_kernel), [image_small.shape, image_large.shape, (1, C), (1, C)], [half]
    )(gathered_last, pre, x, stats_one, affine, dout)
    one, two = call(body(finish_kernel), [conv_first.shape, conv_second.shape])(total, gathered_back, stats_two, affine)
    return (
        out_s, out_l, back_s, back_l,
        one, gain_one.reshape(C), bias_one.reshape(C),
        two, gain_two.reshape(C), bias_two.reshape(C),
    )


def solution(mesh):
    split, whole = P("img", "row", None), P()
    return jax.shard_map(
        local, mesh=mesh, in_specs=(split,) * 6 + (whole,) * 6, out_specs=(split,) * 4 + (whole,) * 6, check_vma=False
    )
```

```python
import functools
import math

import jax
import jax.numpy as jnp
from jax import lax
from jax.experimental import pallas as pl
from jax.experimental.pallas import tpu as pltpu
from jax.sharding import PartitionSpec as P

C = 32
HS = 32
HL = 64
HEIGHTS = (HS, HL)

norm_eps = 1e-05
map_eps = 1e-06
beta_weight = 1000.0
AXES = ("img", "row")
BLOCK = 8
LANES = BLOCK * C
TAPS = 3
WIDTH = LANES + 128
DEPTH = TAPS * WIDTH
REACH = 4
ROOT = math.sqrt(2.0 / math.pi)
CUBE = 0.044715
F32 = jnp.float32
BF16 = jnp.bfloat16
HIGHEST = lax.Precision.HIGHEST
BIAS, GAIN, SECOND, LEFT, NORMED, ONES = 0, 1, 2, 11, 20, 29
BACK_LANES = 1280
LAST_SECOND, LAST_FIRST, LAST_LANES = 2, 11, 640


class Sizes:
    def __init__(self, small, large, devices, peers):
        self.images = (small[0], large[0])
        self.rows = (small[1], large[1])
        self.blocks = (HS // BLOCK, HL // BLOCK)
        self.step = tuple(n * r for n, r in zip(self.images, self.rows))
        self.count = tuple(b * s for b, s in zip(self.blocks, self.step))
        self.edge = tuple(b * n for b, n in zip(self.blocks, self.images))
        self.start = (self.count[1], 0)
        self.rim = (self.edge[1], 0)
        self.total = sum(self.count)
        self.rims = sum(self.edge)
        self.slots = -(-sum(self.images) // 8) * 8
        self.guard = -(-max(self.images) // 8) * 8
        self.devices = devices
        self.peers = peers
        self.here = float(self.total * BLOCK)
        self.pixels = self.here * devices

    def pads(self):
        return [((TAPS, 2, self.count[k] + 2 * self.step[k], 128), F32) for k in (0, 1)]

    def chains(self, depth):
        return [((2, 2 * self.guard + (depth + 1) * self.rims, 128), F32)] * 2


def split(value):
    high = value.astype(BF16)
    return high, (value - high.astype(F32)).astype(BF16)


def dot(left, right):
    return lax.dot_general(left, right, (((1,), (0,)), ((), ())), preferred_element_type=F32)


def product(left, right):
    if left[0].shape[1] % 128:
        return dot(left[0], right[0]) + (dot(left[0], right[1]) + dot(left[1], right[0]))
    return dot(
        jnp.concatenate([left[0], left[0], left[1]], axis=1), jnp.concatenate([right[0], right[1], right[0]], axis=0)
    )


def exact_dot(left, right):
    return lax.dot_general(left, right, (((1,), (0,)), ((), ())), precision=HIGHEST, preferred_element_type=F32)


def gelu(s):
    return 0.5 * s * (1.0 + jnp.tanh(ROOT * (s + CUBE * s * s * s)))


def gelu_slope(s):
    square = s * s
    t = jnp.tanh(ROOT * s * (1.0 + CUBE * square))
    return 0.5 * (1.0 + t) + 0.5 * s * (1.0 - t * t) * ROOT * (1.0 + 3.0 * CUBE * square)


def spread_groups(row):
    row = row + pltpu.roll(row, 64, 1)
    return row + pltpu.roll(row, 32, 1)


def fold(row):
    return spread_groups(row[:, :128] + row[:, 128:])


def wide(row):
    return jnp.concatenate([row, row], axis=1)


def group_of(rows=1, lanes=128):
    return lax.broadcasted_iota(jnp.int32, (rows, lanes), 1) // C


def column_sum(value):
    return jnp.sum(value, axis=0, keepdims=True)


def moments(z, value, ref):
    center = fold(column_sum(value)) / z.here
    off = value - wide(center)
    both = jnp.concatenate([center, fold(column_sum(off * off))], axis=0)
    ref[...] = jnp.broadcast_to(both[None], ref.shape)


def merged(z, ref):
    gathered = ref[...]
    mean = jnp.mean(gathered, axis=0)
    center = mean[0:1]
    off = gathered[:, 0, :] - center
    variance = mean[1:2] / z.here + jnp.mean(off * off, axis=0, keepdims=True)
    return wide(center), wide(lax.rsqrt(variance + norm_eps))


def put_halves(ref, value):
    ref[0] = value[:, :128]
    ref[1] = value[:, 128:]


def whole(ref):
    return jnp.concatenate([ref[0], ref[1]], axis=1)


def to_matrix(z, refs, half):
    for k in (0, 1):
        for j in range(z.blocks[k]):
            at = z.start[k] + j * z.step[k]
            for i in range(z.images[k]):
                for h in (0, 1):
                    half[h, pl.ds(at + i * z.rows[k], z.rows[k]), :] = refs[k][i, :, pl.ds(LANES * j + 128 * h, 128)]


def from_matrix(z, half, refs):
    for k in (0, 1):
        for j in range(z.blocks[k]):
            at = z.start[k] + j * z.step[k]
            for i in range(z.images[k]):
                for h in (0, 1):
                    refs[k][i, :, pl.ds(LANES * j + 128 * h, 128)] = half[h, pl.ds(at + i * z.rows[k], z.rows[k]), :]


def take_rims(z, half, depth, bottom, top, lane):
    out = pl.ds(lane, 128)
    for k in (0, 1):
        for d in range(1, depth + 1):
            to_bottom = pl.ds((depth - d) * z.rims + z.rim[k], z.edge[k])
            to_top = pl.ds((d - 1) * z.rims + z.rim[k], z.edge[k])
            if d <= z.rows[k]:
                bottom[to_bottom, out] = half[pl.ds(z.start[k] + z.rows[k] - d, z.edge[k], stride=z.rows[k]), :]
                top[to_top, out] = half[pl.ds(z.start[k] + d - 1, z.edge[k], stride=z.rows[k]), :]
            else:
                bottom[to_bottom, out] = jnp.zeros((z.edge[k], 128), F32)
                top[to_top, out] = jnp.zeros((z.edge[k], 128), F32)


def inside(z, depth, above):
    at = lax.axis_index("row")
    large = lax.broadcasted_iota(jnp.int32, (z.rims, 1), 0) < z.rim[0]
    parts = []
    for n in range(depth):
        if above:
            ok = [jnp.where(at * rows >= depth - n, 1.0, 0.0) for rows in z.rows]
        else:
            ok = [jnp.where((at + 1) * rows + n + 1 <= height, 1.0, 0.0) for rows, height in zip(z.rows, HEIGHTS)]
        parts.append(jnp.where(large, ok[1], ok[0]).astype(F32))
    return jnp.concatenate(parts, axis=0)


def fill_pads(z, pads, value, above, below):
    for k in (0, 1):
        ref, step, count, rows = pads[k], z.step[k], z.count[k], z.rows[k]
        rim = slice(z.rim[k], z.rim[k] + z.edge[k])
        for h in (0, 1):
            lanes = slice(128 * h, 128 * h + 128)
            for a in range(TAPS):
                ref[a, h, pl.ds(0, step), :] = jnp.zeros((step, 128), F32)
                ref[a, h, pl.ds(step + count, step), :] = jnp.zeros((step, 128), F32)
            ref[1, h, pl.ds(step, count), :] = value[z.start[k] : z.start[k] + count, lanes]
            ref[0, h, pl.ds(step, count), :] = ref[1, h, pl.ds(step - 1, count), :]
            ref[2, h, pl.ds(step, count), :] = ref[1, h, pl.ds(step + 1, count), :]
            ref[0, h, pl.ds(step, z.edge[k], stride=rows), :] = above[rim, lanes]
            ref[2, h, pl.ds(step + rows - 1, z.edge[k], stride=rows), :] = below[rim, lanes]


def band_operand(z, pads):
    lane = lax.broadcasted_iota(jnp.int32, (1, 128), 1)
    parts = []
    for k in (1, 0):
        ref, step, count = pads[k], z.step[k], z.count[k]
        columns = []
        for a in range(TAPS):
            before = ref[a, 1, pl.ds(0, count), :]
            after = ref[a, 0, pl.ds(2 * step, count), :]
            columns += [
                ref[a, 0, pl.ds(step, count), :],
                ref[a, 1, pl.ds(step, count), :],
                jnp.where(lane >= 96, before, jnp.where(lane < 32, after, 0.0)),
            ]
        parts.append(jnp.concatenate(columns, axis=1))
    return jnp.concatenate(parts, axis=0)


def rim_operand(z, chain, depth):
    rows, g = (depth + 1) * z.rims, z.guard
    lane = lax.broadcasted_iota(jnp.int32, (1, 128), 1)
    m = lax.broadcasted_iota(jnp.int32, (z.rims, 1), 0)
    large = m < z.rim[0]
    has_before = jnp.where(large, m, m - z.rim[0]) >= jnp.where(large, z.images[1], z.images[0])
    has_after = m < jnp.where(large, z.rim[0] - z.images[1], z.rims - z.images[0])
    take = [(lane >= 96) & has_before & large, (lane >= 96) & has_before & ~large, (lane < 32) & has_after & large, (lane < 32) & has_after & ~large]
    columns = []
    for r in range(depth + 1):
        at = g + r * z.rims
        edge = jnp.zeros((z.rims, 128), F32)
        for mask, half, shift in zip(take, (1, 1, 0, 0), (-z.images[1], -z.images[0], z.images[1], z.images[0])):
            edge = jnp.where(mask, chain[half, pl.ds(at + shift, z.rims), :], edge)
        columns.append(jnp.concatenate([chain[0, pl.ds(at, z.rims), :], chain[1, pl.ds(at, z.rims), :], edge], axis=1))
    return jnp.concatenate(
        [jnp.concatenate(columns[n : n + TAPS], axis=1) for n in range(depth - 1)], axis=0
    )


def convolve(z, own, above, below, depth, pads, chains, weight):
    r = z.rims
    fill_pads(z, pads, own, above[(depth - 1) * r :], below[:r])
    parts = [band_operand(z, pads)]
    if depth > 1:
        for side, (rim, chain) in enumerate(zip((above, below), chains)):
            rim_at, own_at = (z.guard, z.guard + depth * r) if side == 0 else (z.guard + r, z.guard)
            for h in (0, 1):
                chain[h, pl.ds(rim_at, depth * r), :] = rim[:, 128 * h : 128 * h + 128]
                for k in (0, 1):
                    row = z.step[k] + (0 if side == 0 else z.rows[k] - 1)
                    chain[h, pl.ds(own_at + z.rim[k], z.edge[k]), :] = pads[k][1, h, pl.ds(row, z.edge[k], stride=z.rows[k]), :]
            parts.append(rim_operand(z, chain, depth))
    result = product(split(jnp.concatenate(parts, axis=0)), (weight[0], weight[1]))
    n = z.total + (depth - 1) * r
    return result[: z.total], result[z.total : n], result[n:]


def image_slots(z, shape, rim_rows, along):
    m = lax.broadcasted_iota(jnp.int32, shape, along)
    slot = lax.broadcasted_iota(jnp.int32, shape, 1 - along)
    if rim_rows:
        m = m % z.rims
    start = z.rim[0] if rim_rows else z.start[0]
    height = (1, 1) if rim_rows else z.rows
    image = jnp.where(
        m >= start,
        ((m - start) // height[0]) % z.images[0],
        z.images[0] + (m // height[1]) % z.images[1],
    )
    return jnp.where(image == slot, 1.0, 0.0).astype(F32)


def channel_mean():
    a = lax.broadcasted_iota(jnp.int32, (LANES, 128), 0) // C
    b = lax.broadcasted_iota(jnp.int32, (LANES, 128), 1)
    return jnp.where(a == b, 1.0 / C, 0.0).astype(F32)


def to_channels():
    a = lax.broadcasted_iota(jnp.int32, (128, LANES), 0)
    b = lax.broadcasted_iota(jnp.int32, (128, LANES), 1) // C
    return jnp.where(a == b, 1.0, 0.0).astype(F32)


def attention(value):
    return exact_dot(value * value, channel_mean())


def start_all(copies):
    for copy in copies:
        copy.start()


def wait_all(copies):
    for copy in copies:
        copy.wait()


def start_kernel(z, small, large, x, bottom, top, copies, raw_s, raw_l, half, kept, sems):
    loads = [pltpu.make_async_copy(small, raw_s, sems.at[0]), pltpu.make_async_copy(large, raw_l, sems.at[1])]
    start_all(loads)
    wait_all(loads)
    to_matrix(z, (raw_s, raw_l), half)
    value = whole(half)
    moments(z, value, kept)
    send = pltpu.make_async_copy(kept, copies, sems.at[2])
    send.start()
    x[...] = value
    for h in (0, 1):
        take_rims(z, half.at[h], REACH, bottom, top, 128 * h)
    send.wait()


def toeplitz(taps, ref):
    row = lax.broadcasted_iota(jnp.int32, (LANES, LANES), 0) // C
    lane = lax.broadcasted_iota(jnp.int32, (LANES, LANES), 1) // C
    left = (row[:128] == 3) & (lane[:128] == 0)
    right = (row[:128] == 0) & (lane[:128] == BLOCK - 1)
    for a in range(TAPS):
        lines = [jnp.concatenate([taps[a][b], taps[a][b]], axis=1) for b in range(TAPS)]
        main = jnp.zeros((LANES, LANES), F32)
        for b in range(TAPS):
            main = jnp.where(row - lane + 1 == b, jnp.concatenate([lines[b], lines[b]], axis=0), main)
        edge = jnp.where(left, lines[0], jnp.where(right, lines[2], 0.0))
        for n, part in enumerate(split(jnp.concatenate([main, edge], axis=0))):
            ref[n, pl.ds(a * WIDTH, WIDTH), :] = part


def prepare_kernel(z, up_s, up_l, t_s, t_l, first, second, g1, b1, g2, b2, weights, affine, teacher, bottom, top, raw, ut_half, kept_w, kept_rims, kept_t, rows, sems):
    refs = (up_s, up_l, t_s, t_l, first, second, g1, b1, g2, b2)
    targets = tuple(raw) + tuple(rows.at[pl.ds(n, 1), :] for n in range(4))
    loads = [pltpu.make_async_copy(a, b, sems.at[n]) for n, (a, b) in enumerate(zip(refs, targets))]
    start_all(loads)
    wait_all(loads)
    raw_us, raw_ul, raw_ts, raw_tl, raw_1, raw_2 = raw
    stores = []
    for n, source in ((0, raw_1), (1, raw_2)):
        tiles = []
        for a in range(TAPS):
            line = [jnp.concatenate([source[a, b]] * 4, axis=1) for b in range(TAPS)]
            tiles.append([jnp.concatenate([tap] * 4, axis=0) for tap in line])
        toeplitz(tiles, kept_w.at[n])
        turned = [[tiles[TAPS - 1 - a][TAPS - 1 - b].T for b in range(TAPS)] for a in range(TAPS)]
        toeplitz(turned, kept_w.at[3 - n])
    stores.append(pltpu.make_async_copy(kept_w, weights, sems.at[10]))
    stores[-1].start()
    affine[...] = jnp.concatenate([rows[...]] * BLOCK, axis=1)
    half, teach = ut_half
    to_matrix(z, (raw_us, raw_ul), half)
    teach[...] = jnp.zeros(teach.shape, F32)
    for k, ref in ((0, raw_ts), (1, raw_tl)):
        for i in range(z.images[k]):
            value = ref[i]
            for j in range(z.blocks[k]):
                at = z.start[k] + j * z.step[k] + i * z.rows[k]
                teach[pl.ds(at, z.rows[k]), pl.ds(0, BLOCK)] = value[:, j * BLOCK : (j + 1) * BLOCK]
    kept_bottom, kept_top = kept_rims
    for h in (0, 1):
        take_rims(z, half.at[h], 2, kept_bottom, kept_top, 128 * h)
    take_rims(z, teach, 2, kept_bottom, kept_top, LANES)
    stores += [
        pltpu.make_async_copy(teach, teacher, sems.at[11]),
        pltpu.make_async_copy(kept_bottom, bottom, sems.at[12]),
        pltpu.make_async_copy(kept_top, top, sems.at[13]),
    ]
    start_all(stores[1:])
    wait_all(stores)


def normed_by(stats):
    return lambda v: (v - stats[0:1]) * stats[1:2]


def first_kernel(z, x, above, below, gathered, affine, weights, hidden, h_above, h_below, stats, copies, pads, chains, kept_w, kept, sems):
    load = pltpu.make_async_copy(weights.at[0], kept_w, sems.at[0])
    load.start()
    center, scale = merged(z, gathered)
    gain, bias = affine[0:1], affine[1:2]

    def act(v):
        return gelu((v - center) * scale * gain + bias)

    own, up, down = act(x[...]), act(above[...]) * inside(z, 4, True), act(below[...]) * inside(z, 4, False)
    load.wait()
    own, up, down = convolve(z, own, up, down, 4, pads, chains, kept_w)
    moments(z, own, kept)
    send = pltpu.make_async_copy(kept, copies, sems.at[1])
    send.start()
    hidden[...] = own
    h_above[...] = up
    h_below[...] = down
    stats[0:1] = center
    stats[1:2] = scale
    send.wait()


def second_kernel(z, hidden, h_above, h_below, gathered, affine, weights, x, x_above, x_below, teacher, out, o_above, o_below, near, stats, copies, pads, chains, kept_w, kept_t, kept, sems):
    loads = [pltpu.make_async_copy(weights.at[1], kept_w, sems.at[0]), pltpu.make_async_copy(teacher, kept_t, sems.at[1])]
    start_all(loads)
    center, scale = merged(z, gathered)
    gain, bias = affine[2:3], affine[3:4]
    r = z.rims

    def act(v):
        return gelu((v - center) * scale * gain + bias)

    own = act(hidden[...])
    up, down = act(h_above[...]) * inside(z, 3, True), act(h_below[...]) * inside(z, 3, False)
    wait_all(loads)
    own, up, down = convolve(z, own, up, down, 3, pads, chains, kept_w)
    own = x[...] + own
    amap = attention(own)
    both = jnp.concatenate([amap * amap, amap * kept_t[...]], axis=1)
    sums = exact_dot(image_slots(z, (z.slots, z.total), False, 1), both)
    square = jnp.sum(sums[:, :128], axis=1, keepdims=True)
    cross = jnp.sum(sums[:, 128:], axis=1, keepdims=True)
    lane = lax.broadcasted_iota(jnp.int32, (z.slots, 128), 1)
    kept[...] = jnp.broadcast_to(jnp.where(lane < 64, square, cross)[None], kept.shape)
    send = pltpu.make_async_copy(kept, copies, sems.at[2])
    send.start()
    out[...] = own
    o_above[...] = x_above[pl.ds(2 * r, 2 * r), :] + up
    o_below[...] = x_below[pl.ds(0, 2 * r), :] + down
    near[0] = x_above[pl.ds(3 * r, r), :]
    near[1] = x_below[pl.ds(0, r), :]
    near[2] = h_above[pl.ds(2 * r, r), :]
    near[3] = h_below[pl.ds(0, r), :]
    stats[0:1] = center
    stats[1:2] = scale
    send.wait()


def tap_sums(product_of, rows, tiles, first_group):
    group = group_of()
    for a in range(TAPS):
        for b in range(TAPS):
            halves = [None, None]
            for p in range(BLOCK):
                q = p + b - 1
                at = a * WIDTH + (LANES if q in (-1, BLOCK) else q // 4 * 128)
                q %= BLOCK
                part = product_of(p, at)
                halves[q // 4] = part if halves[q // 4] is None else jnp.where(group == q % 4, part, halves[q // 4])
            sums = spread_groups(halves[0] + halves[1])
            tile, slot = divmod(first_group + a * TAPS + b, 4)
            tiles[tile] = jnp.where(group == slot, sums, tiles[tile])


def tap_product(grad, operand_split):
    result = product(split(grad.T), operand_split)
    return lambda p, lane: result[p * C : p * C + C, lane : lane + 128]


def operands_kernel(z, x, hidden, near, first_stats, stats, affine, out, out_s, out_l, lefts, packed, pads, half, kept, sems):
    put_halves(half, out[...])
    from_matrix(z, half, (out_s, out_l))
    above, below = inside(z, 1, True), inside(z, 1, False)
    stores = []
    tiles = [jnp.zeros((C, 128), F32) for _ in range(BACK_LANES // 128)]
    normed = normed_by(stats)(hidden[...])
    for n, (value, rims, line, at) in enumerate(((x, 0, first_stats, 0), (hidden, 2, stats, 2))):
        unit = normed_by(line)
        gain, bias = affine[at : at + 1], affine[at + 1 : at + 2]

        def act(v):
            return gelu(unit(v) * gain + bias)

        fill_pads(z, pads, act(value[...]), act(near[rims]) * above, act(near[rims + 1]) * below)
        left = band_operand(z, pads)
        parts = split(left)
        for m in (0, 1):
            kept[n, m] = parts[m]
        stores.append(pltpu.make_async_copy(kept.at[n], lefts.at[n], sems.at[n]))
        stores[-1].start()
        if n == 0:
            tap_sums(tap_product(normed, parts), C, tiles, NORMED)
            ones = jnp.broadcast_to(column_sum(left), (C, DEPTH))
            tap_sums(lambda p, lane: ones[:, lane : lane + 128], C, tiles, ONES)
    packed[...] = jnp.concatenate(tiles, axis=1)
    wait_all(stores)


def upstream_kernel(z, gathered, out, o_above, o_below, up_s, up_l, teacher, ut_above, ut_below, weights, lefts, hidden, near, stats, affine, packed, dout, dshift, d_above, d_below, slabs, raw_s, raw_l, kept_t, kept_above, kept_below, kept_w, kept_left, pads, chains, half, kept, sems):
    loads = [
        pltpu.make_async_copy(a, b, sems.at[n])
        for n, (a, b) in enumerate(
            ((up_s, raw_s), (up_l, raw_l), (teacher, kept_t), (ut_above, kept_above), (ut_below, kept_below), (weights.at[2], kept_w), (lefts, kept_left))
        )
    ]
    start_all(loads)
    sums = jnp.sum(gathered[...], axis=0)
    square, cross = sums[:, 0:1], sums[:, 64:65]
    inverse = lax.rsqrt(square + map_eps)
    inner = beta_weight * (square * inverse - cross) * inverse
    pair = jnp.concatenate([jnp.broadcast_to(inverse, (z.slots, 128)), jnp.broadcast_to(inner, (z.slots, 128))], axis=1)
    wait_all(loads[:5])

    def grad(o, u, t, rim_rows):
        per_row = exact_dot(image_slots(z, (o.shape[0], z.slots), rim_rows, 0), pair)
        inv, inn = per_row[:, :128], per_row[:, 128:]
        q = attention(o) * inv
        factor = (beta_weight * (q - t) - q * inn) * inv * (2.0 / C)
        return u + exact_dot(factor, to_channels()) * o

    to_matrix(z, (raw_s, raw_l), half)
    value = grad(out[...], whole(half), kept_t[...], False)
    up = grad(o_above[...], kept_above[:, :LANES], kept_above[:, LANES:], True) * inside(z, 2, True)
    down = grad(o_below[...], kept_below[:, :LANES], kept_below[:, LANES:], True) * inside(z, 2, False)
    dout[...] = value
    loads[5].wait()
    own, up, down = convolve(z, value, up, down, 2, pads, chains, kept_w)
    unit = normed_by(stats)
    gain, bias = affine[2:3], affine[3:4]
    normed = unit(hidden[...])
    pre = own * gelu_slope(normed * gain + bias)
    dshift[...] = pre
    d_above[...] = up * gelu_slope(unit(near[2]) * gain + bias)
    d_below[...] = down * gelu_slope(unit(near[3]) * gain + bias)
    loads[6].wait()
    tiles = [packed[:, 128 * n : 128 * n + 128] for n in range(BACK_LANES // 128)]
    group = group_of()
    tiles[0] = jnp.where(group == BIAS, fold(column_sum(pre)), jnp.where(group == GAIN, fold(column_sum(pre * normed)), tiles[0]))
    tap_sums(tap_product(value, (kept_left[1, 0], kept_left[1, 1])), C, tiles, SECOND)
    tap_sums(tap_product(pre, (kept_left[0, 0], kept_left[0, 1])), C, tiles, LEFT)
    line = jnp.concatenate(tiles, axis=1)
    for d in range(z.devices):
        kept[d] = line[d % C : d % C + 1]
    send = pltpu.make_async_copy(kept, slabs, sems.at[7])
    send.start()
    send.wait()


def norm_sums(total):
    group = group_of()
    return [wide(spread_groups(jnp.where(group == n, total[:, :128], 0.0))) for n in (BIAS, GAIN)]


def hidden_kernel(z, gathered, dshift, d_above, d_below, hidden, near, stats, affine, weights, x, first_stats, pre_ref, gain_out, bias_out, slabs, pads, kept_w, kept, sems):
    load = pltpu.make_async_copy(weights.at[3], kept_w, sems.at[0])
    load.start()
    total = jnp.sum(gathered[...], axis=0)
    bias_sum, gain_sum = norm_sums(total)
    bias_out[...] = bias_sum[:, :C]
    gain_out[...] = gain_sum[:, :C]
    bias_mean, gain_mean = bias_sum / z.pixels, gain_sum / z.pixels
    unit = normed_by(stats)
    factor = affine[2:3] * stats[1:2]

    def back(d, h):
        return factor * (d - bias_mean - unit(h) * gain_mean)

    own = back(dshift[...], hidden[...])
    up = back(d_above[...], near[2]) * inside(z, 1, True)
    down = back(d_below[...], near[3]) * inside(z, 1, False)
    load.wait()
    grad, _, _ = convolve(z, own, up, down, 1, pads, None, kept_w)
    normed = normed_by(first_stats)(x[...])
    pre = grad * gelu_slope(normed * affine[0:1] + affine[1:2])
    pre_ref[...] = pre
    device = lax.axis_index("img") * z.peers + lax.axis_index("row")
    lane = lax.broadcasted_iota(jnp.int32, (1, 128), 1)
    mine = lane == device % C

    def pick(row):
        return jnp.sum(jnp.where(mine, row[:, :128], 0.0), axis=1, keepdims=True)

    taps = TAPS * TAPS * C
    second, left, against, ones = (total[:, n * C : n * C + taps] for n in (SECOND, LEFT, NORMED, ONES))
    first = pick(factor) * (left - pick(bias_mean) * ones - pick(gain_mean) * against)
    sums = jnp.where(lane < C, fold(column_sum(pre)), fold(column_sum(pre * normed)))
    line = jnp.concatenate([sums[:, : 2 * C], second, first], axis=1)
    kept[...] = jnp.broadcast_to(line[None], kept.shape)
    send = pltpu.make_async_copy(kept, slabs, sems.at[1])
    send.start()
    send.wait()


def back_kernel(z, gathered, pre, x, stats, affine, dout, back_s, back_l, one, two, gain_out, bias_out, half, lines):
    bias_sum, gain_sum = norm_sums(jnp.sum(gathered[:, :, pl.ds(0, 128)], axis=0))
    bias_out[...] = bias_sum[:, :C]
    gain_out[...] = gain_sum[:, :C]
    normed = normed_by(stats)(x[...])
    value = dout[...] + affine[0:1] * stats[1:2] * (pre[...] - bias_sum / z.pixels - normed * (gain_sum / z.pixels))
    put_halves(half, value)
    from_matrix(z, half, (back_s, back_l))
    for d in range(C):
        lines[pl.ds(d, 1), :] = gathered[d]
    turned = lines[...].T
    for ref, group in ((two, LAST_SECOND), (one, LAST_FIRST)):
        for a in range(TAPS):
            for b in range(TAPS):
                at = (group + a * TAPS + b) * C
                ref[a, b] = turned[at : at + C]


def call(body, ins, outs, scratch=(), sems=0):
    space = {"v": pltpu.VMEM, "h": pltpu.HBM}
    shapes = []
    for item in scratch:
        if isinstance(item, list):
            shapes.append([pltpu.VMEM(*s) for s in item])
        else:
            shapes.append(pltpu.VMEM(*item))
    if sems:
        shapes.append(pltpu.SemaphoreType.DMA((sems,)))
    return pl.pallas_call(
        body,
        out_shape=[jax.ShapeDtypeStruct(shape, kind) for _, shape, kind in outs],
        in_specs=[pl.BlockSpec(memory_space=space[s]) for s in ins],
        out_specs=[pl.BlockSpec(memory_space=space[s]) for s, _, _ in outs],
        scratch_shapes=shapes,
        compiler_params=pltpu.CompilerParams(vmem_limit_bytes=40 * 1024 * 1024),
    )


def exchange(copies, axes):
    return lax.all_to_all(copies, axes, 0, 0, tiled=True)


def beyond(z, bottom, top, depth):
    hops = max(-(-depth // rows) for rows in z.rows)
    above, below = [], []
    for hop in range(1, hops + 1):
        above.append(lax.ppermute(bottom, "row", [(i, i + hop) for i in range(z.peers - hop)]))
        below.append(lax.ppermute(top, "row", [(i + hop, i) for i in range(z.peers - hop)]))
    if hops == 1:
        return above[0], below[0]
    up, down = [], []
    for d in range(1, depth + 1):
        for k in (1, 0):
            hop, back = divmod(d - 1, z.rows[k])
            at = (depth - 1 - back) * z.rims + z.rim[k]
            up.append(above[hop][at : at + z.edge[k]])
            at = back * z.rims + z.rim[k]
            down.append(below[hop][at : at + z.edge[k]])
    up = [piece for d in reversed(range(depth)) for piece in up[2 * d : 2 * d + 2]]
    return jnp.concatenate(up, axis=0), jnp.concatenate(down, axis=0)


def local(
    image_small, image_large, teacher_small, teacher_large, upstream_small, upstream_large,
    conv_first, gain_first, bias_first, conv_second, gain_second, bias_second,
):
    peers = lax.axis_size("row")
    devices = lax.axis_size("img") * peers
    z = Sizes(image_small.shape, image_large.shape, devices, peers)
    body = lambda function: functools.partial(function, z)
    r = z.rims
    full, half, pair = (z.total, LANES), (2, z.total, 128), (devices, 2, 128)
    raw = [(image_small.shape, F32), (image_large.shape, F32)]
    weight = (2, DEPTH, LANES)
    f = lambda space, *shape: (space, shape, F32)

    x, bottom, top, copies = call(
        body(start_kernel),
        "hh",
        [("v", full, F32), f("v", REACH * r, LANES), f("v", REACH * r, LANES), ("h", pair, F32)],
        raw + [(half, F32), (pair, F32)],
        3,
    )(image_small, image_large)
    gathered = exchange(copies, AXES)
    x_above, x_below = beyond(z, bottom, top, REACH)
    rim_line = (2 * r, LANES + 128)
    weights, affine, teacher, bottom, top = call(
        body(prepare_kernel),
        "hhhhhhhhhh",
        [("h", (4,) + weight, BF16), f("v", 4, LANES), f("h", z.total, 128), ("h", rim_line, F32), ("h", rim_line, F32)],
        [
            raw + [(a.shape, F32) for a in (teacher_small, teacher_large, conv_first, conv_second)],
            [(half, F32), ((z.total, 128), F32)],
            ((4,) + weight, BF16),
            [(rim_line, F32)] * 2,
            ((8, 128), F32),
            ((4, C), F32),
        ],
        14,
    )(
        upstream_small, upstream_large, teacher_small, teacher_large, conv_first, conv_second,
        *(v.reshape(1, C) for v in (gain_first, bias_first, gain_second, bias_second)),
    )

    hidden, h_above, h_below, stats_one, copies = call(
        body(first_kernel),
        "vvvvvh",
        [("v", full, F32), f("v", 3 * r, LANES), f("v", 3 * r, LANES), f("v", 2, LANES), ("h", pair, F32)],
        [z.pads(), z.chains(4), (weight, BF16), (pair, F32)],
        2,
    )(x, x_above, x_below, gathered, affine, weights)
    bottom, top, copies = lax.optimization_barrier((bottom, top, copies))
    gathered = exchange(copies, AXES)
    ut_above, ut_below = beyond(z, bottom, top, 2)

    map_shape = (peers, z.slots, 128)
    out, o_above, o_below, near, stats_two, copies = call(
        body(second_kernel),
        "vvvvvhvvvh",
        [("v", full, F32), f("v", 2 * r, LANES), f("v", 2 * r, LANES), f("v", 4, r, LANES), f("v", 2, LANES), ("h", map_shape, F32)],
        [z.pads(), z.chains(3), (weight, BF16), ((z.total, 128), F32), (map_shape, F32)],
        3,
    )(hidden, h_above, h_below, gathered, affine, weights, x, x_above, x_below, teacher)
    gathered = exchange(copies, ("row",))

    left = (2, 2, z.total, DEPTH)
    out_s, out_l, lefts, packed = call(
        body(operands_kernel),
        "vvvvvvv",
        [("v", image_small.shape, F32), ("v", image_large.shape, F32), ("h", left, BF16), f("v", C, BACK_LANES)],
        [z.pads(), (half, F32), (left, BF16)],
        2,
    )(x, hidden, near, stats_one, stats_two, affine, out)

    dout, dshift, d_above, d_below, slabs = call(
        body(upstream_kernel),
        "vvvvhhhhhhhvvvvv",
        [("v", full, F32), ("v", full, F32), f("v", r, LANES), f("v", r, LANES), f("h", devices, 1, BACK_LANES)],
        raw
        + [((z.total, 128), F32), (rim_line, F32), (rim_line, F32), (weight, BF16), (left, BF16)]
        + [z.pads(), z.chains(2), (half, F32), ((devices, 1, BACK_LANES), F32)],
        8,
    )(
        gathered, out, o_above, o_below, upstream_small, upstream_large, teacher, ut_above, ut_below, weights, lefts,
        hidden, near, stats_two, affine, packed,
    )
    gathered = exchange(slabs, AXES)

    pre, gain_two, bias_two, slabs = call(
        body(hidden_kernel),
        "vvvvvvvvhvv",
        [("v", full, F32), f("v", 1, C), f("v", 1, C), f("h", devices, 1, LAST_LANES)],
        [z.pads(), (weight, BF16), ((devices, 1, LAST_LANES), F32)],
        2,
    )(gathered, dshift, d_above, d_below, hidden, near, stats_two, affine, weights, x, stats_one)
    gathered = exchange(slabs, AXES)

    back_s, back_l, one, two, gain_one, bias_one = call(
        body(back_kernel),
        "vvvvvv",
        [("v", a.shape, F32) for a in (image_small, image_large, conv_first, conv_second)] + [f("v", 1, C), f("v", 1, C)],
        [(half, F32), ((C, LAST_LANES), F32)],
    )(gathered, pre, x, stats_one, affine, dout)
    return (
        out_s, out_l, back_s, back_l,
        one, gain_one.reshape(C), bias_one.reshape(C),
        two, gain_two.reshape(C), bias_two.reshape(C),
    )


def solution(mesh):
    split_bands, everywhere = P("img", "row", None), P()
    return jax.shard_map(
        local,
        mesh=mesh,
        in_specs=(split_bands,) * 6 + (everywhere,) * 6,
        out_specs=(split_bands,) * 4 + (everywhere,) * 6,
        check_vma=False,
    )
```

```python
import functools
import math

import jax
import jax.numpy as jnp
from jax import lax
from jax.experimental import pallas as pl
from jax.experimental.pallas import tpu as pltpu
from jax.sharding import PartitionSpec as P

C = 32
HS = 32
HL = 64
HEIGHTS = (HS, HL)

norm_eps = 1e-05
map_eps = 1e-06
beta_weight = 1000.0
AXES = ("img", "row")
BLOCK = 8
LANES = BLOCK * C
TAPS = 3
WIDTH = LANES + 128
DEPTH = TAPS * WIDTH
REACH = 4
ROOT = math.sqrt(2.0 / math.pi)
CUBE = 0.044715
F32 = jnp.float32
BF16 = jnp.bfloat16
VMEM_LIMIT = 32 * 1024 * 1024
BIAS, GAIN, SECOND, LEFT, NORMED, ONES = 0, 1, 2, 11, 20, 29
BACK_LANES = 1280
LAST_SECOND, LAST_FIRST, LAST_LANES = 2, 11, 640


class Sizes:
    def __init__(self, small, large, devices, peers):
        self.images = (small[0], large[0])
        self.rows = (small[1], large[1])
        self.blocks = (HS // BLOCK, HL // BLOCK)
        self.step = tuple(n * r for n, r in zip(self.images, self.rows))
        self.count = tuple(b * s for b, s in zip(self.blocks, self.step))
        self.edge = tuple(b * n for b, n in zip(self.blocks, self.images))
        self.start = (self.count[1], 0)
        self.rim = (self.edge[1], 0)
        self.total = sum(self.count)
        self.rims = sum(self.edge)
        self.slots = -(-sum(self.images) // 8) * 8
        self.guard = -(-max(self.images) // 8) * 8
        self.devices = devices
        self.peers = peers
        self.here = float(self.total * BLOCK)
        self.pixels = self.here * devices

    def pads(self):
        return [((TAPS, 2, self.count[k] + 2 * self.step[k], 128), F32) for k in (0, 1)]

    def chains(self, depth):
        return [((2, 2 * self.guard + (depth + 1) * self.rims, 128), F32)] * 2


def split(value):
    high = value.astype(BF16)
    return high, (value - high.astype(F32)).astype(BF16)


def dot(left, right):
    return lax.dot_general(left, right, (((1,), (0,)), ((), ())), preferred_element_type=F32)


def product(left, right):
    if left[0].shape[1] % 128:
        return dot(left[0], right[0]) + (dot(left[0], right[1]) + dot(left[1], right[0]))
    return dot(
        jnp.concatenate([left[0], left[0], left[1]], axis=1), jnp.concatenate([right[0], right[1], right[0]], axis=0)
    )


def spread(left, right):
    right = right.astype(BF16)
    return dot(jnp.concatenate(split(left), axis=1), jnp.concatenate([right, right], axis=0))


def gelu(s):
    return 0.5 * s * (1.0 + jnp.tanh(ROOT * (s + CUBE * s * s * s)))


def gelu_slope(s):
    square = s * s
    t = jnp.tanh(ROOT * s * (1.0 + CUBE * square))
    return 0.5 * (1.0 + t) + 0.5 * s * (1.0 - t * t) * ROOT * (1.0 + 3.0 * CUBE * square)


def spread_groups(row):
    row = row + pltpu.roll(row, 64, 1)
    return row + pltpu.roll(row, 32, 1)


def fold(row):
    return spread_groups(row[:, :128] + row[:, 128:])


def wide(row):
    return jnp.concatenate([row, row], axis=1)


def group_of(rows=1, lanes=128):
    return lax.broadcasted_iota(jnp.int32, (rows, lanes), 1) // C


def column_sum(value):
    return jnp.sum(value, axis=0, keepdims=True)


def moments(z, value, ref):
    center = fold(column_sum(value)) / z.here
    off = value - wide(center)
    both = jnp.concatenate([center, fold(column_sum(off * off))], axis=0)
    ref[...] = jnp.broadcast_to(both[None], ref.shape)


def merged(z, ref):
    gathered = ref[...]
    mean = jnp.mean(gathered, axis=0)
    center = mean[0:1]
    off = gathered[:, 0, :] - center
    variance = mean[1:2] / z.here + jnp.mean(off * off, axis=0, keepdims=True)
    return wide(center), wide(lax.rsqrt(variance + norm_eps))


def put_halves(ref, value):
    ref[0] = value[:, :128]
    ref[1] = value[:, 128:]


def whole(ref):
    return jnp.concatenate([ref[0], ref[1]], axis=1)


def to_matrix(z, refs, half):
    for k in (0, 1):
        for j in range(z.blocks[k]):
            at = z.start[k] + j * z.step[k]
            for i in range(z.images[k]):
                for h in (0, 1):
                    half[h, pl.ds(at + i * z.rows[k], z.rows[k]), :] = refs[k][i, :, pl.ds(LANES * j + 128 * h, 128)]


def from_matrix(z, half, refs):
    for k in (0, 1):
        for j in range(z.blocks[k]):
            at = z.start[k] + j * z.step[k]
            for i in range(z.images[k]):
                for h in (0, 1):
                    refs[k][i, :, pl.ds(LANES * j + 128 * h, 128)] = half[h, pl.ds(at + i * z.rows[k], z.rows[k]), :]


def take_rims(z, half, depth, bottom, top):
    for k in (0, 1):
        for d in range(1, depth + 1):
            to_bottom = pl.ds((depth - d) * z.rims + z.rim[k], z.edge[k])
            to_top = pl.ds((d - 1) * z.rims + z.rim[k], z.edge[k])
            if d <= z.rows[k]:
                bottom[to_bottom, :] = half[pl.ds(z.start[k] + z.rows[k] - d, z.edge[k], stride=z.rows[k]), :]
                top[to_top, :] = half[pl.ds(z.start[k] + d - 1, z.edge[k], stride=z.rows[k]), :]
            else:
                bottom[to_bottom, :] = jnp.zeros((z.edge[k], 128), F32)
                top[to_top, :] = jnp.zeros((z.edge[k], 128), F32)


def inside(z, depth, above):
    at = lax.axis_index("row")
    large = lax.broadcasted_iota(jnp.int32, (z.rims, 1), 0) < z.rim[0]
    parts = []
    for n in range(depth):
        if above:
            ok = [jnp.where(at * rows >= depth - n, 1.0, 0.0) for rows in z.rows]
        else:
            ok = [jnp.where((at + 1) * rows + n + 1 <= height, 1.0, 0.0) for rows, height in zip(z.rows, HEIGHTS)]
        parts.append(jnp.where(large, ok[1], ok[0]).astype(F32))
    return jnp.concatenate(parts, axis=0)


def fill_pads(z, pads, value, above, below):
    for k in (0, 1):
        ref, step, count, rows = pads[k], z.step[k], z.count[k], z.rows[k]
        rim = slice(z.rim[k], z.rim[k] + z.edge[k])
        for h in (0, 1):
            lanes = slice(128 * h, 128 * h + 128)
            for a in range(TAPS):
                ref[a, h, pl.ds(0, step), :] = jnp.zeros((step, 128), F32)
                ref[a, h, pl.ds(step + count, step), :] = jnp.zeros((step, 128), F32)
            ref[1, h, pl.ds(step, count), :] = value[z.start[k] : z.start[k] + count, lanes]
            ref[0, h, pl.ds(step, count), :] = ref[1, h, pl.ds(step - 1, count), :]
            ref[2, h, pl.ds(step, count), :] = ref[1, h, pl.ds(step + 1, count), :]
            ref[0, h, pl.ds(step, z.edge[k], stride=rows), :] = above[rim, lanes]
            ref[2, h, pl.ds(step + rows - 1, z.edge[k], stride=rows), :] = below[rim, lanes]


def band_operand(z, pads):
    lane = lax.broadcasted_iota(jnp.int32, (1, 128), 1)
    parts = []
    for k in (1, 0):
        ref, step, count = pads[k], z.step[k], z.count[k]
        columns = []
        for a in range(TAPS):
            before = ref[a, 1, pl.ds(0, count), :]
            after = ref[a, 0, pl.ds(2 * step, count), :]
            columns += [
                ref[a, 0, pl.ds(step, count), :],
                ref[a, 1, pl.ds(step, count), :],
                jnp.where(lane >= 96, before, jnp.where(lane < 32, after, 0.0)),
            ]
        parts.append(jnp.concatenate(columns, axis=1))
    return jnp.concatenate(parts, axis=0)


def rim_operand(z, chain, depth):
    rows, g = (depth + 1) * z.rims, z.guard
    lane = lax.broadcasted_iota(jnp.int32, (1, 128), 1)
    m = lax.broadcasted_iota(jnp.int32, (z.rims, 1), 0)
    large = m < z.rim[0]
    has_before = jnp.where(large, m, m - z.rim[0]) >= jnp.where(large, z.images[1], z.images[0])
    has_after = m < jnp.where(large, z.rim[0] - z.images[1], z.rims - z.images[0])
    take = [(lane >= 96) & has_before & large, (lane >= 96) & has_before & ~large, (lane < 32) & has_after & large, (lane < 32) & has_after & ~large]
    columns = []
    for r in range(depth + 1):
        at = g + r * z.rims
        edge = jnp.zeros((z.rims, 128), F32)
        for mask, half, shift in zip(take, (1, 1, 0, 0), (-z.images[1], -z.images[0], z.images[1], z.images[0])):
            edge = jnp.where(mask, chain[half, pl.ds(at + shift, z.rims), :], edge)
        columns.append(jnp.concatenate([chain[0, pl.ds(at, z.rims), :], chain[1, pl.ds(at, z.rims), :], edge], axis=1))
    return jnp.concatenate(
        [jnp.concatenate(columns[n : n + TAPS], axis=1) for n in range(depth - 1)], axis=0
    )


def convolve(z, own, above, below, depth, pads, chains, weight):
    r = z.rims
    fill_pads(z, pads, own, above[(depth - 1) * r :], below[:r])
    parts = [band_operand(z, pads)]
    if depth > 1:
        for side, (rim, chain) in enumerate(zip((above, below), chains)):
            rim_at, own_at = (z.guard, z.guard + depth * r) if side == 0 else (z.guard + r, z.guard)
            for h in (0, 1):
                chain[h, pl.ds(rim_at, depth * r), :] = rim[:, 128 * h : 128 * h + 128]
                for k in (0, 1):
                    row = z.step[k] + (0 if side == 0 else z.rows[k] - 1)
                    chain[h, pl.ds(own_at + z.rim[k], z.edge[k]), :] = pads[k][1, h, pl.ds(row, z.edge[k], stride=z.rows[k]), :]
            parts.append(rim_operand(z, chain, depth))
    result = product(split(jnp.concatenate(parts, axis=0)), (weight[0], weight[1]))
    n = z.total + (depth - 1) * r
    return result[: z.total], result[z.total : n], result[n:]


def image_sums(z, value):
    slot = lax.broadcasted_iota(jnp.int32, (z.slots, 1), 0)
    sums = jnp.zeros((z.slots, 128), F32)
    for k in (0, 1):
        line = value[z.start[k] : z.start[k] + z.step[k]]
        for j in range(1, z.blocks[k]):
            at = z.start[k] + j * z.step[k]
            line = line + value[at : at + z.step[k]]
        image = lax.broadcasted_iota(jnp.int32, (z.step[k], 1), 0) // z.rows[k]
        for i in range(z.images[k]):
            sums = jnp.where(slot == i + k * z.images[0], column_sum(jnp.where(image == i, line, 0.0)), sums)
    return sums


def image_rows(z, values, rims):
    parts = []
    for k in (1, 0):
        image = lax.broadcasted_iota(jnp.int32, (z.step[k], 1), 0) // z.rows[k]
        line = jnp.zeros((z.step[k], 128), F32)
        for i in range(z.images[k]):
            at = i + k * z.images[0]
            line = jnp.where(image == i, values[at : at + 1], line)
        parts += [line] * z.blocks[k]
    if rims:
        m = lax.broadcasted_iota(jnp.int32, (z.rims, 1), 0)
        image = jnp.where(m < z.rim[0], z.images[0] + m % z.images[1], (m - z.rim[0]) % z.images[0])
        line = jnp.zeros((z.rims, 128), F32)
        for at in range(sum(z.images)):
            line = jnp.where(image == at, values[at : at + 1], line)
        parts += [line] * rims
    return jnp.concatenate(parts, axis=0)


def channel_mean():
    a = lax.broadcasted_iota(jnp.int32, (LANES, 128), 0) // C
    b = lax.broadcasted_iota(jnp.int32, (LANES, 128), 1)
    return jnp.where(a == b, 1.0 / C, 0.0).astype(F32)


def to_channels():
    a = lax.broadcasted_iota(jnp.int32, (128, LANES), 0)
    b = lax.broadcasted_iota(jnp.int32, (128, LANES), 1) // C
    return jnp.where(a == b, 1.0, 0.0).astype(F32)


def attention(value):
    return spread(value * value, channel_mean())


def start_all(copies):
    for copy in copies:
        copy.start()


def wait_all(copies):
    for copy in copies:
        copy.wait()


def start_kernel(z, small, large, up_s, up_l, t_s, t_l, x, bottom, top, copies, upstream, teacher, raw, halves, kept, kept_u, teach, sems):
    loads = [pltpu.make_async_copy(a, b, sems.at[n]) for n, (a, b) in enumerate(zip((small, large, up_s, up_l, t_s, t_l), raw))]
    start_all(loads)
    r, n = z.rims, REACH * z.rims
    wait_all(loads[:2])
    to_matrix(z, raw[:2], halves[0])
    value = whole(halves[0])
    x[...] = value
    moments(z, value, kept)
    stores = [pltpu.make_async_copy(kept, copies, sems.at[6])]
    stores[0].start()
    wait_all(loads[2:])
    to_matrix(z, raw[2:4], halves[1])
    kept_u[...] = whole(halves[1])
    teach[...] = jnp.zeros(teach.shape, F32)
    for k, ref in ((0, raw[4]), (1, raw[5])):
        for i in range(z.images[k]):
            line = ref[i]
            for j in range(z.blocks[k]):
                at = z.start[k] + j * z.step[k] + i * z.rows[k]
                teach[pl.ds(at, z.rows[k]), pl.ds(0, BLOCK)] = line[:, j * BLOCK : (j + 1) * BLOCK]
    stores += [pltpu.make_async_copy(kept_u, upstream, sems.at[7]), pltpu.make_async_copy(teach, teacher, sems.at[8])]
    start_all(stores[1:])
    for h in (0, 1):
        lanes = pl.ds(128 * h, 128)
        take_rims(z, halves[0].at[h], REACH, bottom.at[pl.ds(0, n), lanes], top.at[pl.ds(0, n), lanes])
        take_rims(z, halves[1].at[h], 2, bottom.at[pl.ds(n, 2 * r), lanes], top.at[pl.ds(n, 2 * r), lanes])
    take_rims(z, teach, 2, bottom.at[pl.ds(n + 2 * r, 2 * r), pl.ds(0, 128)], top.at[pl.ds(n + 2 * r, 2 * r), pl.ds(0, 128)])
    wait_all(stores)


def toeplitz(taps, ref):
    row = lax.broadcasted_iota(jnp.int32, (LANES, LANES), 0) // C
    lane = lax.broadcasted_iota(jnp.int32, (LANES, LANES), 1) // C
    left = (row[:128] == 3) & (lane[:128] == 0)
    right = (row[:128] == 0) & (lane[:128] == BLOCK - 1)
    for a in range(TAPS):
        lines = [jnp.concatenate([taps[a][b], taps[a][b]], axis=1) for b in range(TAPS)]
        main = jnp.zeros((LANES, LANES), F32)
        for b in range(TAPS):
            main = jnp.where(row - lane + 1 == b, jnp.concatenate([lines[b], lines[b]], axis=0), main)
        edge = jnp.where(left, lines[0], jnp.where(right, lines[2], 0.0))
        for n, part in enumerate(split(jnp.concatenate([main, edge], axis=0))):
            ref[n, pl.ds(a * WIDTH, WIDTH), :] = part


def prepare_kernel(z, first, second, g1, b1, g2, b2, weights, affine, raw, kept, rows, sems):
    targets = tuple(raw) + tuple(rows.at[pl.ds(n, 1), :] for n in range(4))
    loads = [pltpu.make_async_copy(a, b, sems.at[n]) for n, (a, b) in enumerate(zip((first, second, g1, b1, g2, b2), targets))]
    start_all(loads)
    wait_all(loads)
    stores = []
    for n, source in enumerate(raw):
        tiles = []
        for a in range(TAPS):
            line = [jnp.concatenate([source[a, b]] * 4, axis=1) for b in range(TAPS)]
            tiles.append([jnp.concatenate([tap] * 4, axis=0) for tap in line])
        turned = [[tiles[TAPS - 1 - a][TAPS - 1 - b].T for b in range(TAPS)] for a in range(TAPS)]
        for at, taps in ((n, tiles), (3 - n, turned)):
            toeplitz(taps, kept.at[at])
            stores.append(pltpu.make_async_copy(kept.at[at], weights.at[at], sems.at[6 + at]))
            stores[-1].start()
    affine[...] = jnp.concatenate([rows[...]] * BLOCK, axis=1)
    wait_all(stores)


def normed_by(stats):
    return lambda v: (v - stats[0:1]) * stats[1:2]


def activation(z, center, scale, gain, bias):
    return lambda v: gelu((v - center) * scale * gain + bias)


def first_kernel(z, x, above, below, gathered, affine, weights, hidden, h_above, h_below, stats, copies, more, pads, chains, kept_w, kept, sems):
    n = REACH * z.rims
    copy = [
        pltpu.make_async_copy(weights.at[0], kept_w, sems.at[0]),
        pltpu.make_async_copy(above.at[pl.ds(n, 4 * z.rims), :], more.at[0], sems.at[2]),
        pltpu.make_async_copy(below.at[pl.ds(n, 4 * z.rims), :], more.at[1], sems.at[3]),
    ]
    start_all(copy)
    center, scale = merged(z, gathered)
    act = activation(z, center, scale, affine[0:1], affine[1:2])
    own = act(x[...])
    up, down = act(above[pl.ds(0, n), :]) * inside(z, 4, True), act(below[pl.ds(0, n), :]) * inside(z, 4, False)
    copy[0].wait()
    own, up, down = convolve(z, own, up, down, 4, pads, chains, kept_w)
    moments(z, own, kept)
    send = pltpu.make_async_copy(kept, copies, sems.at[1])
    send.start()
    hidden[...] = own
    h_above[...] = up
    h_below[...] = down
    stats[0:1] = center
    stats[1:2] = scale
    wait_all(copy[1:] + [send])


def second_kernel(z, hidden, h_above, h_below, gathered, affine, weights, x, x_above, x_below, teacher, out, o_above, o_below, near, stats, copies, pads, chains, kept_w, kept_t, kept, sems):
    loads = [pltpu.make_async_copy(weights.at[1], kept_w, sems.at[0]), pltpu.make_async_copy(teacher, kept_t, sems.at[1])]
    start_all(loads)
    center, scale = merged(z, gathered)
    act = activation(z, center, scale, affine[2:3], affine[3:4])
    r = z.rims
    own = act(hidden[...])
    up, down = act(h_above[...]) * inside(z, 3, True), act(h_below[...]) * inside(z, 3, False)
    wait_all(loads)
    own, up, down = convolve(z, own, up, down, 3, pads, chains, kept_w)
    own = x[...] + own
    amap = attention(own)
    sums = image_sums(z, amap * amap) + pltpu.roll(image_sums(z, amap * kept_t[...]), 64, 1)
    kept[...] = jnp.broadcast_to(sums[None], kept.shape)
    send = pltpu.make_async_copy(kept, copies, sems.at[2])
    send.start()
    out[...] = own
    o_above[...] = x_above[pl.ds(2 * r, 2 * r), :] + up
    o_below[...] = x_below[pl.ds(0, 2 * r), :] + down
    near[0] = h_above[pl.ds(2 * r, r), :]
    near[1] = h_below[pl.ds(0, r), :]
    stats[0:1] = center
    stats[1:2] = scale
    send.wait()


def tap_rows(a, q):
    return a * WIDTH + (LANES + 3 * C if q < 0 else LANES if q == BLOCK else q * C)


def tap_sums(result, tiles, first_group):
    group = group_of()
    for a in range(TAPS):
        for b in range(TAPS):
            total = None
            for h in (0, 1):
                half = None
                for p in range(4 * h, 4 * h + 4):
                    at = tap_rows(a, p + b - 1)
                    part = result[at : at + C, 128 * h : 128 * h + 128]
                    half = part if half is None else jnp.where(group == p % 4, part, half)
                total = half if total is None else total + half
            tile, slot = divmod(first_group + a * TAPS + b, 4)
            tiles[tile] = jnp.where(group == slot, spread_groups(total), tiles[tile])


def tap_counts(column, tiles, first_group):
    group = group_of()
    for a in range(TAPS):
        for b in range(TAPS):
            total = sum(column[tap_rows(a, p + b - 1) : tap_rows(a, p + b - 1) + C] for p in range(BLOCK))
            tile, slot = divmod(first_group + a * TAPS + b, 4)
            tiles[tile] = jnp.where(group == slot, total, tiles[tile])


def turned_operand(z, pads, kept):
    left = band_operand(z, pads).T
    parts = split(left)
    for n in (0, 1):
        kept[n] = parts[n]
    return left


def first_operand_kernel(z, x, above, below, stats, affine, left, counts, pads, kept, sems):
    r = z.rims
    act = activation(z, stats[0:1], stats[1:2], affine[0:1], affine[1:2])
    up, down = act(above[pl.ds(3 * r, r), :]) * inside(z, 1, True), act(below[pl.ds(0, r), :]) * inside(z, 1, False)
    fill_pads(z, pads, act(x[...]), up, down)
    value = turned_operand(z, pads, kept)
    store = pltpu.make_async_copy(kept, left, sems.at[0])
    store.start()
    tiles = [jnp.zeros((C, 128), F32) for _ in range(3)]
    tap_counts(jnp.sum(value, axis=1, keepdims=True), tiles, 0)
    counts[...] = jnp.concatenate(tiles, axis=1)
    store.wait()


def second_operand_kernel(z, hidden, near, stats, affine, out, first_left, counts, out_s, out_l, left, packed, pads, half, kept, kept_left, sems):
    load = pltpu.make_async_copy(first_left, kept_left, sems.at[0])
    load.start()
    put_halves(half, out[...])
    from_matrix(z, half, (out_s, out_l))
    act = activation(z, stats[0:1], stats[1:2], affine[2:3], affine[3:4])
    fill_pads(z, pads, act(hidden[...]), act(near[0]) * inside(z, 1, True), act(near[1]) * inside(z, 1, False))
    turned_operand(z, pads, kept)
    store = pltpu.make_async_copy(kept, left, sems.at[1])
    store.start()
    normed = normed_by(stats)(hidden[...])
    load.wait()
    tiles = [jnp.zeros((C, 128), F32) for _ in range(BACK_LANES // 128)]
    tap_sums(product((kept_left[0], kept_left[1]), split(normed)), tiles, NORMED)
    group = group_of()
    for n in range(TAPS * TAPS):
        tile, slot = divmod(ONES + n, 4)
        line = spread_groups(jnp.where(group == n % 4, counts[:, 128 * (n // 4) : 128 * (n // 4) + 128], 0.0))
        tiles[tile] = jnp.where(group == slot, line, tiles[tile])
    packed[...] = jnp.concatenate(tiles, axis=1)
    store.wait()


def upstream_kernel(z, gathered, out, o_above, o_below, upstream, teacher, more, weights, left_1, left_2, hidden, near, stats, affine, packed, dout, dshift, d_above, d_below, slabs, kept_u, kept_t, kept_more, kept_w, kept_left, pads, chains, kept, sems):
    loads = [
        pltpu.make_async_copy(a, b, sems.at[n])
        for n, (a, b) in enumerate(
            (
                (upstream, kept_u), (teacher, kept_t), (more, kept_more), (weights.at[2], kept_w),
                (left_2, kept_left.at[1]), (left_1, kept_left.at[0]),
            )
        )
    ]
    start_all(loads)
    lane = lax.broadcasted_iota(jnp.int32, (z.slots, 128), 1)
    sums = jnp.sum(gathered[...], axis=0)
    square = jnp.sum(jnp.where(lane < 64, sums, 0.0), axis=1, keepdims=True)
    cross = jnp.sum(jnp.where(lane < 64, 0.0, sums), axis=1, keepdims=True)
    inverse = lax.rsqrt(square + map_eps)
    inner = beta_weight * (square * inverse - cross) * inverse
    shape = (z.slots, 128)
    inv, inn = (image_rows(z, jnp.broadcast_to(v, shape), 4) for v in (inverse, inner))
    r = z.rims
    o = jnp.concatenate([out[...], o_above[...], o_below[...]], axis=0)
    q = attention(o) * inv
    wait_all(loads[:3])
    u = jnp.concatenate([kept_u[...], kept_more[0, pl.ds(0, 2 * r), :], kept_more[1, pl.ds(0, 2 * r), :]], axis=0)
    t = jnp.concatenate([kept_t[...], kept_more[0, pl.ds(2 * r, 2 * r), pl.ds(0, 128)], kept_more[1, pl.ds(2 * r, 2 * r), pl.ds(0, 128)]], axis=0)
    factor = (beta_weight * (q - t) - q * inn) * inv * (2.0 / C)
    grad = u + spread(factor, to_channels()) * o
    value = grad[: z.total]
    up = grad[z.total : z.total + 2 * r] * inside(z, 2, True)
    down = grad[z.total + 2 * r :] * inside(z, 2, False)
    dout[...] = value
    loads[3].wait()
    own, up, down = convolve(z, value, up, down, 2, pads, chains, kept_w)
    unit = normed_by(stats)
    gain, bias = affine[2:3], affine[3:4]
    normed = unit(hidden[...])
    pre = own * gelu_slope(normed * gain + bias)
    dshift[...] = pre
    d_above[...] = up * gelu_slope(unit(near[0]) * gain + bias)
    d_below[...] = down * gelu_slope(unit(near[1]) * gain + bias)
    tiles = [packed[:, 128 * n : 128 * n + 128] for n in range(BACK_LANES // 128)]
    group = group_of()
    tiles[0] = jnp.where(group == BIAS, fold(column_sum(pre)), jnp.where(group == GAIN, fold(column_sum(pre * normed)), tiles[0]))
    loads[4].wait()
    tap_sums(product((kept_left[1, 0], kept_left[1, 1]), split(value)), tiles, SECOND)
    loads[5].wait()
    tap_sums(product((kept_left[0, 0], kept_left[0, 1]), split(pre)), tiles, LEFT)
    line = jnp.concatenate(tiles, axis=1)
    for d in range(z.devices):
        kept[d] = line[d % C : d % C + 1]
    send = pltpu.make_async_copy(kept, slabs, sems.at[6])
    send.start()
    send.wait()


def norm_sums(total):
    group = group_of()
    return [wide(spread_groups(jnp.where(group == n, total[:, :128], 0.0))) for n in (BIAS, GAIN)]


def hidden_kernel(z, gathered, dshift, d_above, d_below, hidden, near, stats, affine, weights, x, first_stats, pre_ref, gain_out, bias_out, slabs, pads, kept_w, kept, sems):
    load = pltpu.make_async_copy(weights.at[3], kept_w, sems.at[0])
    load.start()
    total = jnp.sum(gathered[...], axis=0)
    bias_sum, gain_sum = norm_sums(total)
    bias_out[...] = bias_sum[:, :C]
    gain_out[...] = gain_sum[:, :C]
    bias_mean, gain_mean = bias_sum / z.pixels, gain_sum / z.pixels
    unit = normed_by(stats)
    factor = affine[2:3] * stats[1:2]

    def back(d, h):
        return factor * (d - bias_mean - unit(h) * gain_mean)

    own = back(dshift[...], hidden[...])
    up = back(d_above[...], near[0]) * inside(z, 1, True)
    down = back(d_below[...], near[1]) * inside(z, 1, False)
    load.wait()
    grad, _, _ = convolve(z, own, up, down, 1, pads, None, kept_w)
    normed = normed_by(first_stats)(x[...])
    pre = grad * gelu_slope(normed * affine[0:1] + affine[1:2])
    pre_ref[...] = pre
    lane = lax.broadcasted_iota(jnp.int32, (1, 128), 1)
    taps = TAPS * TAPS * C

    def along(row):
        return jnp.concatenate([row[:, :128]] * 3, axis=1)[:, :taps]

    second, left, against, ones = (total[:, n * C : n * C + taps] for n in (SECOND, LEFT, NORMED, ONES))
    first = along(factor) * (left - along(bias_mean) * ones - along(gain_mean) * against)
    sums = jnp.where(lane < C, fold(column_sum(pre)), fold(column_sum(pre * normed)))
    line = jnp.concatenate([sums[:, : 2 * C], second, first], axis=1)
    kept[...] = jnp.broadcast_to(line[None], kept.shape)
    send = pltpu.make_async_copy(kept, slabs, sems.at[1])
    send.start()
    send.wait()


def back_kernel(z, gathered, pre, x, stats, affine, dout, back_s, back_l, one, two, gain_out, bias_out, half, lines):
    bias_sum, gain_sum = norm_sums(jnp.sum(gathered[:, :, pl.ds(0, 128)], axis=0))
    bias_out[...] = bias_sum[:, :C]
    gain_out[...] = gain_sum[:, :C]
    normed = normed_by(stats)(x[...])
    value = dout[...] + affine[0:1] * stats[1:2] * (pre[...] - bias_sum / z.pixels - normed * (gain_sum / z.pixels))
    put_halves(half, value)
    from_matrix(z, half, (back_s, back_l))
    for d in range(C):
        lines[pl.ds(d, 1), :] = gathered[d]
    for ref, group in ((two, LAST_SECOND), (one, LAST_FIRST)):
        for a in range(TAPS):
            for b in range(TAPS):
                at = (group + a * TAPS + b) * C
                ref[a, b] = lines[:, pl.ds(at, C)]


def call(body, ins, outs, scratch=(), sems=0):
    space = {"v": pltpu.VMEM, "h": pltpu.HBM}
    shapes = []
    for item in scratch:
        if isinstance(item, list):
            shapes.append([pltpu.VMEM(*s) for s in item])
        else:
            shapes.append(pltpu.VMEM(*item))
    if sems:
        shapes.append(pltpu.SemaphoreType.DMA((sems,)))
    run = pl.pallas_call(
        body,
        out_shape=[pltpu.HBM(shape, kind) if s == "h" else jax.ShapeDtypeStruct(shape, kind) for s, shape, kind in outs],
        in_specs=[pl.BlockSpec(memory_space=space[s]) for s in ins],
        out_specs=[pl.BlockSpec(memory_space=space[s]) for s, _, _ in outs],
        scratch_shapes=shapes,
        compiler_params=pltpu.CompilerParams(vmem_limit_bytes=VMEM_LIMIT),
    )
    return lambda *args: run(
        *(pltpu.with_memory_space_constraint(arg, pltpu.HBM) if s == "h" else arg for s, arg in zip(ins, args))
    )


def exchange(copies, axes):
    return lax.all_to_all(copies, axes, 0, 0, tiled=True)


def beyond(z, bottom, top, depths):
    hops = max(-(-depth // rows) for rows in z.rows for depth in depths)
    above, below = [], []
    for hop in range(1, hops + 1):
        above.append(lax.ppermute(bottom, "row", [(i, i + hop) for i in range(z.peers - hop)]))
        below.append(lax.ppermute(top, "row", [(i + hop, i) for i in range(z.peers - hop)]))
    if hops == 1:
        return above[0], below[0]
    up, down = [], []
    base = 0
    for depth in depths:
        for n in range(depth):
            for k in (1, 0):
                hop, back = divmod(depth - 1 - n, z.rows[k])
                at = base + (depth - 1 - back) * z.rims + z.rim[k]
                up.append(above[hop][at : at + z.edge[k]])
                hop, back = divmod(n, z.rows[k])
                at = base + back * z.rims + z.rim[k]
                down.append(below[hop][at : at + z.edge[k]])
        base += depth * z.rims
    return jnp.concatenate(up, axis=0), jnp.concatenate(down, axis=0)


def local(
    image_small, image_large, teacher_small, teacher_large, upstream_small, upstream_large,
    conv_first, gain_first, bias_first, conv_second, gain_second, bias_second,
):
    peers = lax.axis_size("row")
    devices = lax.axis_size("img") * peers
    z = Sizes(image_small.shape, image_large.shape, devices, peers)
    body = lambda function: functools.partial(function, z)
    r = z.rims
    full, half, pair = (z.total, LANES), (2, z.total, 128), (devices, 2, 128)
    weight, left = (2, DEPTH, LANES), (2, DEPTH, z.total)
    images = [image_small, image_large, upstream_small, upstream_large, teacher_small, teacher_large]
    f = lambda space, *shape: (space, shape, F32)
    depths = (REACH, 2, 2)
    rim_rows = sum(depths) * r

    x, bottom, top, copies, upstream, teacher = call(
        body(start_kernel),
        "hhhhhh",
        [("v", full, F32), f("v", rim_rows, LANES), f("v", rim_rows, LANES), ("h", pair, F32), ("h", full, F32), f("h", z.total, 128)],
        [[(a.shape, F32) for a in images], [(half, F32)] * 2, (pair, F32), (full, F32), ((z.total, 128), F32)],
        9,
    )(*images)
    gathered = exchange(copies, AXES)
    above, below = beyond(z, bottom, top, depths)
    weights, affine = call(
        body(prepare_kernel),
        "hhhhhh",
        [("h", (4,) + weight, BF16), f("v", 4, LANES)],
        [[(conv_first.shape, F32)] * 2, ((4,) + weight, BF16), ((4, C), F32)],
        10,
    )(conv_first, conv_second, *(v.reshape(1, C) for v in (gain_first, bias_first, gain_second, bias_second)))

    hidden, h_above, h_below, stats_one, copies, more = call(
        body(first_kernel),
        "vvvvvh",
        [("v", full, F32), f("v", 3 * r, LANES), f("v", 3 * r, LANES), f("v", 2, LANES), ("h", pair, F32), f("h", 2, 4 * r, LANES)],
        [z.pads(), z.chains(4), (weight, BF16), (pair, F32)],
        4,
    )(x, above, below, gathered, affine, weights)
    gathered = exchange(copies, AXES)
    left_one, counts = call(
        body(first_operand_kernel),
        "vvvvv",
        [("h", left, BF16), f("v", C, 384)],
        [z.pads(), (left, BF16)],
        1,
    )(x, above, below, stats_one, affine)
    gathered, counts = lax.optimization_barrier((gathered, counts))

    map_shape = (peers, z.slots, 128)
    out, o_above, o_below, near, stats_two, copies = call(
        body(second_kernel),
        "vvvvvhvvvh",
        [("v", full, F32), f("v", 2 * r, LANES), f("v", 2 * r, LANES), f("v", 2, r, LANES), f("v", 2, LANES), ("h", map_shape, F32)],
        [z.pads(), z.chains(3), (weight, BF16), ((z.total, 128), F32), (map_shape, F32)],
        3,
    )(hidden, h_above, h_below, gathered, affine, weights, x, above, below, teacher)
    gathered = exchange(copies, ("row",))
    out_s, out_l, left_two, packed = call(
        body(second_operand_kernel),
        "vvvvvhv",
        [("v", image_small.shape, F32), ("v", image_large.shape, F32), ("h", left, BF16), f("v", C, BACK_LANES)],
        [z.pads(), (half, F32), (left, BF16), (left, BF16)],
        2,
    )(hidden, near, stats_two, affine, out, left_one, counts)

    dout, dshift, d_above, d_below, slabs = call(
        body(upstream_kernel),
        "vvvvhhhhhhvvvvv",
        [("v", full, F32), ("v", full, F32), f("v", r, LANES), f("v", r, LANES), f("h", devices, 1, BACK_LANES)],
        [(full, F32), ((z.total, 128), F32), ((2, 4 * r, LANES), F32), (weight, BF16), ((2,) + left, BF16)]
        + [z.pads(), z.chains(2), ((devices, 1, BACK_LANES), F32)],
        7,
    )(gathered, out, o_above, o_below, upstream, teacher, more, weights, left_one, left_two, hidden, near, stats_two, affine, packed)
    gathered = exchange(slabs, AXES)

    pre, gain_two, bias_two, slabs = call(
        body(hidden_kernel),
        "vvvvvvvvhvv",
        [("v", full, F32), f("v", 1, C), f("v", 1, C), f("h", devices, 1, LAST_LANES)],
        [z.pads(), (weight, BF16), ((devices, 1, LAST_LANES), F32)],
        2,
    )(gathered, dshift, d_above, d_below, hidden, near, stats_two, affine, weights, x, stats_one)
    gathered = exchange(slabs, AXES)

    back_s, back_l, one, two, gain_one, bias_one = call(
        body(back_kernel),
        "vvvvvv",
        [("v", a.shape, F32) for a in (image_small, image_large, conv_first, conv_second)] + [f("v", 1, C), f("v", 1, C)],
        [(half, F32), ((C, LAST_LANES), F32)],
    )(gathered, pre, x, stats_one, affine, dout)
    return (
        out_s, out_l, back_s, back_l,
        one, gain_one.reshape(C), bias_one.reshape(C),
        two, gain_two.reshape(C), bias_two.reshape(C),
    )


def solution(mesh):
    split_bands, everywhere = P("img", "row", None), P()
    return jax.shard_map(
        local,
        mesh=mesh,
        in_specs=(split_bands,) * 6 + (everywhere,) * 6,
        out_specs=(split_bands,) * 4 + (everywhere,) * 6,
        check_vma=False,
    )
```

```python
import functools
import math

import jax
import jax.numpy as jnp
from jax import lax
from jax.experimental import pallas as pl
from jax.experimental.pallas import tpu as pltpu
from jax.sharding import PartitionSpec as P

C = 32
HS = 32
HL = 64
HEIGHTS = (HS, HL)

norm_eps = 1e-05
map_eps = 1e-06
beta_weight = 1000.0
AXES = ("img", "row")
BLOCK = 8
LANES = BLOCK * C
TAPS = 3
WIDTH = LANES + 128
DEPTH = TAPS * WIDTH
TAP_ROWS = 128 + 2 * C
REACH = 4
ROOT = math.sqrt(2.0 / math.pi)
CUBE = 0.044715
F32 = jnp.float32
BF16 = jnp.bfloat16
VMEM_LIMIT = 32 * 1024 * 1024
BIAS, GAIN, SECOND, LEFT, NORMED, ONES = 0, 1, 2, 11, 20, 29
BACK_LANES = 1280
LAST_SECOND, LAST_FIRST, LAST_LANES = 2, 11, 640


class Sizes:
    def __init__(self, small, large, devices, peers):
        self.images = (small[0], large[0])
        self.rows = (small[1], large[1])
        self.blocks = (HS // BLOCK, HL // BLOCK)
        self.step = tuple(n * r for n, r in zip(self.images, self.rows))
        self.count = tuple(b * s for b, s in zip(self.blocks, self.step))
        self.edge = tuple(b * n for b, n in zip(self.blocks, self.images))
        self.start = (self.count[1], 0)
        self.rim = (self.edge[1], 0)
        self.total = sum(self.count)
        self.rims = sum(self.edge)
        self.slots = -(-sum(self.images) // 8) * 8
        self.guard = -(-max(self.images) // 8) * 8
        self.devices = devices
        self.peers = peers
        self.here = float(self.total * BLOCK)
        self.pixels = self.here * devices

    def pads(self):
        return [((TAPS, 2, self.count[k] + 2 * self.step[k], 128), F32) for k in (0, 1)]

    def chains(self, depth):
        return [((2, 2 * self.guard + (depth + 1) * self.rims, 128), F32)] * 2


def split(value):
    high = value.astype(BF16)
    return high, (value - high.astype(F32)).astype(BF16)


def dot(left, right):
    return lax.dot_general(left, right, (((1,), (0,)), ((), ())), preferred_element_type=F32)


def product(left, right):
    if left[0].shape[1] % 128:
        return dot(left[0], right[0]) + (dot(left[0], right[1]) + dot(left[1], right[0]))
    return dot(
        jnp.concatenate([left[0], left[0], left[1]], axis=1), jnp.concatenate([right[0], right[1], right[0]], axis=0)
    )


def spread(left, right):
    right = right.astype(BF16)
    return dot(jnp.concatenate(split(left), axis=1), jnp.concatenate([right, right], axis=0))


def gelu(s):
    return 0.5 * s * (1.0 + jnp.tanh(ROOT * (s + CUBE * s * s * s)))


def gelu_slope(s):
    square = s * s
    t = jnp.tanh(ROOT * s * (1.0 + CUBE * square))
    return 0.5 * (1.0 + t) + 0.5 * s * (1.0 - t * t) * ROOT * (1.0 + 3.0 * CUBE * square)


def spread_groups(row):
    row = row + pltpu.roll(row, 64, 1)
    return row + pltpu.roll(row, 32, 1)


def fold(row):
    return spread_groups(row[:, :128] + row[:, 128:])


def wide(row):
    return jnp.concatenate([row, row], axis=1)


def group_of(rows=1, lanes=128):
    return lax.broadcasted_iota(jnp.int32, (rows, lanes), 1) // C


def column_sum(value):
    return jnp.sum(value, axis=0, keepdims=True)


def moments(z, value, ref):
    center = fold(column_sum(value)) / z.here
    off = value - wide(center)
    both = jnp.concatenate([center, fold(column_sum(off * off))], axis=0)
    ref[...] = jnp.broadcast_to(both[None], ref.shape)


def merged(z, ref):
    gathered = ref[...]
    mean = jnp.mean(gathered, axis=0)
    center = mean[0:1]
    off = gathered[:, 0, :] - center
    variance = mean[1:2] / z.here + jnp.mean(off * off, axis=0, keepdims=True)
    return wide(center), wide(lax.rsqrt(variance + norm_eps))


def put_halves(ref, value):
    ref[0] = value[:, :128]
    ref[1] = value[:, 128:]


def whole(ref):
    return jnp.concatenate([ref[0], ref[1]], axis=1)


def to_matrix(z, refs, half):
    for k in (0, 1):
        for j in range(z.blocks[k]):
            at = z.start[k] + j * z.step[k]
            for i in range(z.images[k]):
                for h in (0, 1):
                    half[h, pl.ds(at + i * z.rows[k], z.rows[k]), :] = refs[k][i, :, pl.ds(LANES * j + 128 * h, 128)]


def from_matrix(z, half, refs):
    for k in (0, 1):
        for j in range(z.blocks[k]):
            at = z.start[k] + j * z.step[k]
            for i in range(z.images[k]):
                for h in (0, 1):
                    refs[k][i, :, pl.ds(LANES * j + 128 * h, 128)] = half[h, pl.ds(at + i * z.rows[k], z.rows[k]), :]


def take_rims(z, half, depth, bottom, top):
    for k in (0, 1):
        for d in range(1, depth + 1):
            to_bottom = pl.ds((depth - d) * z.rims + z.rim[k], z.edge[k])
            to_top = pl.ds((d - 1) * z.rims + z.rim[k], z.edge[k])
            if d <= z.rows[k]:
                bottom[to_bottom, :] = half[pl.ds(z.start[k] + z.rows[k] - d, z.edge[k], stride=z.rows[k]), :]
                top[to_top, :] = half[pl.ds(z.start[k] + d - 1, z.edge[k], stride=z.rows[k]), :]
            else:
                bottom[to_bottom, :] = jnp.zeros((z.edge[k], 128), F32)
                top[to_top, :] = jnp.zeros((z.edge[k], 128), F32)


def inside(z, depth, above):
    at = lax.axis_index("row")
    large = lax.broadcasted_iota(jnp.int32, (z.rims, 1), 0) < z.rim[0]
    parts = []
    for n in range(depth):
        if above:
            ok = [jnp.where(at * rows >= depth - n, 1.0, 0.0) for rows in z.rows]
        else:
            ok = [jnp.where((at + 1) * rows + n + 1 <= height, 1.0, 0.0) for rows, height in zip(z.rows, HEIGHTS)]
        parts.append(jnp.where(large, ok[1], ok[0]).astype(F32))
    return jnp.concatenate(parts, axis=0)


def fill_pads(z, pads, value, above, below):
    for k in (0, 1):
        ref, step, count, rows = pads[k], z.step[k], z.count[k], z.rows[k]
        rim = slice(z.rim[k], z.rim[k] + z.edge[k])
        for h in (0, 1):
            lanes = slice(128 * h, 128 * h + 128)
            for a in range(TAPS):
                ref[a, h, pl.ds(0, step), :] = jnp.zeros((step, 128), F32)
                ref[a, h, pl.ds(step + count, step), :] = jnp.zeros((step, 128), F32)
            ref[1, h, pl.ds(step, count), :] = value[z.start[k] : z.start[k] + count, lanes]
            ref[0, h, pl.ds(step, count), :] = ref[1, h, pl.ds(step - 1, count), :]
            ref[2, h, pl.ds(step, count), :] = ref[1, h, pl.ds(step + 1, count), :]
            ref[0, h, pl.ds(step, z.edge[k], stride=rows), :] = above[rim, lanes]
            ref[2, h, pl.ds(step + rows - 1, z.edge[k], stride=rows), :] = below[rim, lanes]


def band_operand(z, pads):
    lane = lax.broadcasted_iota(jnp.int32, (1, 128), 1)
    parts = []
    for k in (1, 0):
        ref, step, count = pads[k], z.step[k], z.count[k]
        columns = []
        for a in range(TAPS):
            before = ref[a, 1, pl.ds(0, count), :]
            after = ref[a, 0, pl.ds(2 * step, count), :]
            columns += [
                ref[a, 0, pl.ds(step, count), :],
                ref[a, 1, pl.ds(step, count), :],
                jnp.where(lane >= 96, before, jnp.where(lane < 32, after, 0.0)),
            ]
        parts.append(jnp.concatenate(columns, axis=1))
    return jnp.concatenate(parts, axis=0)


def rim_operand(z, chain, depth):
    rows, g = (depth + 1) * z.rims, z.guard
    lane = lax.broadcasted_iota(jnp.int32, (1, 128), 1)
    m = lax.broadcasted_iota(jnp.int32, (z.rims, 1), 0)
    large = m < z.rim[0]
    has_before = jnp.where(large, m, m - z.rim[0]) >= jnp.where(large, z.images[1], z.images[0])
    has_after = m < jnp.where(large, z.rim[0] - z.images[1], z.rims - z.images[0])
    take = [(lane >= 96) & has_before & large, (lane >= 96) & has_before & ~large, (lane < 32) & has_after & large, (lane < 32) & has_after & ~large]
    columns = []
    for r in range(depth + 1):
        at = g + r * z.rims
        edge = jnp.zeros((z.rims, 128), F32)
        for mask, half, shift in zip(take, (1, 1, 0, 0), (-z.images[1], -z.images[0], z.images[1], z.images[0])):
            edge = jnp.where(mask, chain[half, pl.ds(at + shift, z.rims), :], edge)
        columns.append(jnp.concatenate([chain[0, pl.ds(at, z.rims), :], chain[1, pl.ds(at, z.rims), :], edge], axis=1))
    return jnp.concatenate(
        [jnp.concatenate(columns[n : n + TAPS], axis=1) for n in range(depth - 1)], axis=0
    )


def convolve(z, own, above, below, depth, pads, chains, weight):
    r = z.rims
    fill_pads(z, pads, own, above[(depth - 1) * r :], below[:r])
    parts = [band_operand(z, pads)]
    if depth > 1:
        for side, (rim, chain) in enumerate(zip((above, below), chains)):
            rim_at, own_at = (z.guard, z.guard + depth * r) if side == 0 else (z.guard + r, z.guard)
            for h in (0, 1):
                chain[h, pl.ds(rim_at, depth * r), :] = rim[:, 128 * h : 128 * h + 128]
                for k in (0, 1):
                    row = z.step[k] + (0 if side == 0 else z.rows[k] - 1)
                    chain[h, pl.ds(own_at + z.rim[k], z.edge[k]), :] = pads[k][1, h, pl.ds(row, z.edge[k], stride=z.rows[k]), :]
            parts.append(rim_operand(z, chain, depth))
    result = product(split(jnp.concatenate(parts, axis=0)), (weight_matrix(weight.at[0]), weight_matrix(weight.at[1])))
    n = z.total + (depth - 1) * r
    return result[: z.total], result[z.total : n], result[n:]


def image_sums(z, value):
    slot = lax.broadcasted_iota(jnp.int32, (z.slots, 1), 0)
    sums = jnp.zeros((z.slots, 128), F32)
    for k in (0, 1):
        line = value[z.start[k] : z.start[k] + z.step[k]]
        for j in range(1, z.blocks[k]):
            at = z.start[k] + j * z.step[k]
            line = line + value[at : at + z.step[k]]
        image = lax.broadcasted_iota(jnp.int32, (z.step[k], 1), 0) // z.rows[k]
        for i in range(z.images[k]):
            sums = jnp.where(slot == i + k * z.images[0], column_sum(jnp.where(image == i, line, 0.0)), sums)
    return sums


def image_rows(z, values, rims):
    parts = []
    for k in (1, 0):
        image = lax.broadcasted_iota(jnp.int32, (z.step[k], 1), 0) // z.rows[k]
        line = jnp.zeros((z.step[k], 128), F32)
        for i in range(z.images[k]):
            at = i + k * z.images[0]
            line = jnp.where(image == i, values[at : at + 1], line)
        parts += [line] * z.blocks[k]
    if rims:
        m = lax.broadcasted_iota(jnp.int32, (z.rims, 1), 0)
        image = jnp.where(m < z.rim[0], z.images[0] + m % z.images[1], (m - z.rim[0]) % z.images[0])
        line = jnp.zeros((z.rims, 128), F32)
        for at in range(sum(z.images)):
            line = jnp.where(image == at, values[at : at + 1], line)
        parts += [line] * rims
    return jnp.concatenate(parts, axis=0)


def channel_mean():
    a = lax.broadcasted_iota(jnp.int32, (LANES, 128), 0) // C
    b = lax.broadcasted_iota(jnp.int32, (LANES, 128), 1)
    return jnp.where(a == b, 1.0 / C, 0.0).astype(F32)


def to_channels():
    a = lax.broadcasted_iota(jnp.int32, (128, LANES), 0)
    b = lax.broadcasted_iota(jnp.int32, (128, LANES), 1) // C
    return jnp.where(a == b, 1.0, 0.0).astype(F32)


def attention(value):
    return spread(value * value, channel_mean())


def start_all(copies):
    for copy in copies:
        copy.start()


def wait_all(copies):
    for copy in copies:
        copy.wait()


def start_kernel(z, small, large, up_s, up_l, t_s, t_l, x, bottom, top, copies, upstream, teacher, raw, halves, kept_u, teach, sems):
    loads = [pltpu.make_async_copy(a, b, sems.at[n]) for n, (a, b) in enumerate(zip((small, large, up_s, up_l, t_s, t_l), raw))]
    start_all(loads)
    r, n = z.rims, REACH * z.rims
    wait_all(loads[:2])
    to_matrix(z, raw[:2], halves[0])
    value = whole(halves[0])
    x[...] = value
    moments(z, value, copies)
    wait_all(loads[2:])
    to_matrix(z, raw[2:4], halves[1])
    kept_u[...] = whole(halves[1])
    teach[...] = jnp.zeros(teach.shape, F32)
    tail = n + 2 * r
    for ref in (bottom, top):
        ref[pl.ds(tail, z.slots), :] = jnp.zeros((z.slots, LANES), F32)
    for k, ref in ((0, raw[4]), (1, raw[5])):
        width, rows = HEIGHTS[k], z.rows[k]
        for i in range(z.images[k]):
            line = ref[i]
            for j in range(z.blocks[k]):
                at = z.start[k] + j * z.step[k] + i * rows
                teach[pl.ds(at, rows), pl.ds(0, BLOCK)] = line[:, j * BLOCK : (j + 1) * BLOCK]
            for d in range(2):
                slot = pl.ds(tail + i + k * z.images[0], 1)
                if d < rows:
                    bottom[slot, pl.ds(128 * (1 - d), width)] = line[rows - 1 - d : rows - d]
                    top[slot, pl.ds(128 * d, width)] = line[d : d + 1]
    stores = [pltpu.make_async_copy(kept_u, upstream, sems.at[6]), pltpu.make_async_copy(teach, teacher, sems.at[7])]
    start_all(stores)
    for h in (0, 1):
        lanes = pl.ds(128 * h, 128)
        take_rims(z, halves[0].at[h], REACH, bottom.at[pl.ds(0, n), lanes], top.at[pl.ds(0, n), lanes])
        take_rims(z, halves[1].at[h], 2, bottom.at[pl.ds(n, 2 * r), lanes], top.at[pl.ds(n, 2 * r), lanes])
    wait_all(stores)


def banded(taps, ref):
    row = lax.broadcasted_iota(jnp.int32, (128, 128), 0) // C
    lane = group_of(128)
    for a in range(TAPS):
        main = jnp.zeros((128, 128), F32)
        for b in range(TAPS):
            main = jnp.where(row - lane + 1 == b, taps[a][b], main)
        before = jnp.where(lane[:C] == 0, taps[a][0][:C], 0.0)
        after = jnp.where(lane[:C] == 3, taps[a][2][:C], 0.0)
        for n, part in enumerate(split(jnp.concatenate([main, before, after], axis=0))):
            ref[n, pl.ds(a * TAP_ROWS, TAP_ROWS), :] = part


def weight_matrix(ref):
    rows = []
    zeros = jnp.zeros((128 - C, 128), BF16)
    for a in range(TAPS):
        at = a * TAP_ROWS
        main = ref[pl.ds(at, 128), :]
        before = jnp.concatenate([zeros, ref[pl.ds(at + 128, C), :]], axis=0)
        after = jnp.concatenate([ref[pl.ds(at + 128 + C, C), :], zeros], axis=0)
        rows += [
            jnp.concatenate([main, before], axis=1),
            jnp.concatenate([after, main], axis=1),
            jnp.concatenate([before, after], axis=1),
        ]
    return jnp.concatenate(rows, axis=0)


def prepare_kernel(z, first, second, g1, b1, g2, b2, weights, affine, raw, kept, rows, sems):
    targets = tuple(raw) + tuple(rows.at[pl.ds(n, 1), :] for n in range(4))
    loads = [pltpu.make_async_copy(a, b, sems.at[n]) for n, (a, b) in enumerate(zip((first, second, g1, b1, g2, b2), targets))]
    start_all(loads)
    wait_all(loads)
    stores = []
    for n, source in enumerate(raw):
        tiles = []
        for a in range(TAPS):
            line = [jnp.concatenate([source[a, b]] * 4, axis=1) for b in range(TAPS)]
            tiles.append([jnp.concatenate([tap] * 4, axis=0) for tap in line])
        turned = [[tiles[TAPS - 1 - a][TAPS - 1 - b].T for b in range(TAPS)] for a in range(TAPS)]
        for at, taps in ((n, tiles), (3 - n, turned)):
            banded(taps, kept.at[at])
            stores.append(pltpu.make_async_copy(kept.at[at], weights.at[at], sems.at[6 + at]))
            stores[-1].start()
    affine[...] = jnp.concatenate([rows[...]] * BLOCK, axis=1)
    wait_all(stores)


def normed_by(stats):
    return lambda v: (v - stats[0:1]) * stats[1:2]


def activation(z, center, scale, gain, bias):
    return lambda v: gelu((v - center) * scale * gain + bias)


def first_kernel(z, x, above, below, gathered, affine, weights, hidden, h_above, h_below, stats, copies, more, pads, chains, kept_w, sems):
    n = REACH * z.rims
    copy = [
        pltpu.make_async_copy(weights.at[0], kept_w, sems.at[0]),
        pltpu.make_async_copy(above.at[pl.ds(n, 2 * z.rims + z.slots), :], more.at[0], sems.at[1]),
        pltpu.make_async_copy(below.at[pl.ds(n, 2 * z.rims + z.slots), :], more.at[1], sems.at[2]),
    ]
    start_all(copy)
    center, scale = merged(z, gathered)
    act = activation(z, center, scale, affine[0:1], affine[1:2])
    own = act(x[...])
    up, down = act(above[pl.ds(0, n), :]) * inside(z, 4, True), act(below[pl.ds(0, n), :]) * inside(z, 4, False)
    copy[0].wait()
    own, up, down = convolve(z, own, up, down, 4, pads, chains, kept_w)
    moments(z, own, copies)
    hidden[...] = own
    h_above[...] = up
    h_below[...] = down
    stats[0:1] = center
    stats[1:2] = scale
    wait_all(copy[1:])


def second_kernel(z, hidden, h_above, h_below, gathered, affine, weights, x, x_above, x_below, teacher, out, o_above, o_below, near, stats, copies, pads, chains, kept_w, kept_t, sems):
    loads = [pltpu.make_async_copy(weights.at[1], kept_w, sems.at[0]), pltpu.make_async_copy(teacher, kept_t, sems.at[1])]
    start_all(loads)
    center, scale = merged(z, gathered)
    act = activation(z, center, scale, affine[2:3], affine[3:4])
    r = z.rims
    own = act(hidden[...])
    up, down = act(h_above[...]) * inside(z, 3, True), act(h_below[...]) * inside(z, 3, False)
    wait_all(loads)
    own, up, down = convolve(z, own, up, down, 3, pads, chains, kept_w)
    own = x[...] + own
    amap = attention(own)
    sums = image_sums(z, amap * amap) + pltpu.roll(image_sums(z, amap * kept_t[...]), 64, 1)
    copies[...] = jnp.broadcast_to(sums[None], copies.shape)
    out[...] = own
    o_above[...] = x_above[pl.ds(2 * r, 2 * r), :] + up
    o_below[...] = x_below[pl.ds(0, 2 * r), :] + down
    near[0] = h_above[pl.ds(2 * r, r), :]
    near[1] = h_below[pl.ds(0, r), :]
    stats[0:1] = center
    stats[1:2] = scale


def tap_rows(a, q):
    return a * WIDTH + (LANES + 3 * C if q < 0 else LANES if q == BLOCK else q * C)


def tap_sums(result, tiles, first_group):
    group = group_of()
    for a in range(TAPS):
        for b in range(TAPS):
            total = None
            for h in (0, 1):
                half = None
                for p in range(4 * h, 4 * h + 4):
                    at = tap_rows(a, p + b - 1)
                    part = result[at : at + C, 128 * h : 128 * h + 128]
                    half = part if half is None else jnp.where(group == p % 4, part, half)
                total = half if total is None else total + half
            tile, slot = divmod(first_group + a * TAPS + b, 4)
            tiles[tile] = jnp.where(group == slot, spread_groups(total), tiles[tile])


def tap_counts(column, tiles, first_group):
    group = group_of()
    for a in range(TAPS):
        for b in range(TAPS):
            total = sum(column[tap_rows(a, p + b - 1) : tap_rows(a, p + b - 1) + C] for p in range(BLOCK))
            tile, slot = divmod(first_group + a * TAPS + b, 4)
            tiles[tile] = jnp.where(group == slot, total, tiles[tile])


def turned_operand(z, pads, kept):
    left = band_operand(z, pads).T
    parts = split(left)
    for n in (0, 1):
        kept[n] = parts[n]
    return left


def first_operand_kernel(z, x, above, below, stats, affine, left, counts, pads, kept, sems):
    r = z.rims
    act = activation(z, stats[0:1], stats[1:2], affine[0:1], affine[1:2])
    up, down = act(above[pl.ds(3 * r, r), :]) * inside(z, 1, True), act(below[pl.ds(0, r), :]) * inside(z, 1, False)
    fill_pads(z, pads, act(x[...]), up, down)
    value = turned_operand(z, pads, kept)
    store = pltpu.make_async_copy(kept, left, sems.at[0])
    store.start()
    tiles = [jnp.zeros((C, 128), F32) for _ in range(3)]
    tap_counts(jnp.sum(value, axis=1, keepdims=True), tiles, 0)
    counts[...] = jnp.concatenate(tiles, axis=1)
    store.wait()


def second_operand_kernel(z, hidden, near, stats, affine, out, o_above, o_below, first_left, counts, more, teacher, out_s, out_l, left, packed, teachers, maps, slopes, pads, half, kept, kept_left, kept_packed, kept_t, pixels, sems):
    r = z.rims
    loads = [
        pltpu.make_async_copy(first_left, kept_left, sems.at[0]),
        pltpu.make_async_copy(teacher, kept_t.at[pl.ds(0, z.total), :], sems.at[1]),
        pltpu.make_async_copy(more.at[:, pl.ds(2 * r, z.slots), :], pixels, sems.at[2]),
    ]
    start_all(loads)
    act = activation(z, stats[0:1], stats[1:2], affine[2:3], affine[3:4])
    fill_pads(z, pads, act(hidden[...]), act(near[0]) * inside(z, 1, True), act(near[1]) * inside(z, 1, False))
    turned_operand(z, pads, kept)
    stores = [pltpu.make_async_copy(kept, left, sems.at[3])]
    stores[0].start()
    put_halves(half, out[...])
    from_matrix(z, half, (out_s, out_l))
    unit = normed_by(stats)
    normed = unit(hidden[...])
    slopes[pl.ds(0, z.total), :] = gelu_slope(normed * affine[2:3] + affine[3:4])
    for n in (0, 1):
        slopes[pl.ds(z.total + n * r, r), :] = gelu_slope(unit(near[n]) * affine[2:3] + affine[3:4])
    maps[...] = attention(jnp.concatenate([out[...], o_above[...], o_below[...]], axis=0))
    wait_all(loads)
    kept_t[pl.ds(z.total, 4 * r), :] = jnp.zeros((4 * r, 128), F32)
    for side in (0, 1):
        for d in (0, 1):
            for k in (0, 1):
                slot = pl.ds(k * z.images[0], z.images[k])
                line = pixels[side, slot, pl.ds(128 * d, 128)]
                for j in range(z.blocks[k]):
                    at = z.total + (2 * side + d) * r + z.rim[k] + j * z.images[k]
                    kept_t[pl.ds(at, z.images[k]), pl.ds(0, BLOCK)] = line[:, j * BLOCK : (j + 1) * BLOCK]
    stores.append(pltpu.make_async_copy(kept_t, teachers, sems.at[4]))
    stores[1].start()
    tiles = [jnp.zeros((C, 128), F32) for _ in range(BACK_LANES // 128)]
    tap_sums(product((kept_left[0], kept_left[1]), split(normed)), tiles, NORMED)
    group = group_of()
    for n in range(TAPS * TAPS):
        tile, slot = divmod(ONES + n, 4)
        line = spread_groups(jnp.where(group == n % 4, counts[:, 128 * (n // 4) : 128 * (n // 4) + 128], 0.0))
        tiles[tile] = jnp.where(group == slot, line, tiles[tile])
    kept_packed[...] = jnp.concatenate(tiles, axis=1)
    stores.append(pltpu.make_async_copy(kept_packed, packed, sems.at[5]))
    stores[2].start()
    wait_all(stores)


def upstream_kernel(z, gathered, out, o_above, o_below, upstream, teachers, more, weights, left_1, left_2, packed, maps, slopes, hidden, stats, dout, dshift, d_above, d_below, slabs, kept_u, kept_t, kept_more, kept_w, kept_left, kept_packed, pads, chains, sems):
    r = z.rims
    loads = [
        pltpu.make_async_copy(a, b, sems.at[n])
        for n, (a, b) in enumerate(
            (
                (upstream, kept_u), (teachers, kept_t), (more.at[:, pl.ds(0, 2 * r), :], kept_more), (weights.at[2], kept_w),
                (left_2.at[0], kept_left.at[1, 0]), (left_2.at[1], kept_left.at[1, 1]),
                (left_1.at[0], kept_left.at[0, 0]), (left_1.at[1], kept_left.at[0, 1]), (packed, kept_packed),
            )
        )
    ]
    start_all(loads)
    lane = lax.broadcasted_iota(jnp.int32, (z.slots, 128), 1)
    sums = jnp.sum(gathered[...], axis=0)
    square = jnp.sum(jnp.where(lane < 64, sums, 0.0), axis=1, keepdims=True)
    cross = jnp.sum(jnp.where(lane < 64, 0.0, sums), axis=1, keepdims=True)
    inverse = lax.rsqrt(square + map_eps)
    inner = beta_weight * (square * inverse - cross) * inverse
    shape = (z.slots, 128)
    inv, inn = (image_rows(z, jnp.broadcast_to(v, shape), 4) for v in (inverse, inner))
    q = maps[...] * inv
    o = jnp.concatenate([out[...], o_above[...], o_below[...]], axis=0)
    wait_all(loads[:3])
    u = jnp.concatenate([kept_u[...], kept_more[0], kept_more[1]], axis=0)
    factor = (beta_weight * (q - kept_t[...]) - q * inn) * inv * (2.0 / C)
    grad = u + spread(factor, to_channels()) * o
    value = grad[: z.total]
    up = grad[z.total : z.total + 2 * r] * inside(z, 2, True)
    down = grad[z.total + 2 * r :] * inside(z, 2, False)
    dout[...] = value
    loads[3].wait()
    own, up, down = convolve(z, value, up, down, 2, pads, chains, kept_w)
    normed = normed_by(stats)(hidden[...])
    pre = own * slopes[pl.ds(0, z.total), :]
    dshift[...] = pre
    d_above[...] = up * slopes[pl.ds(z.total, r), :]
    d_below[...] = down * slopes[pl.ds(z.total + r, r), :]
    wait_all(loads[4:])
    tiles = [kept_packed[:, 128 * n : 128 * n + 128] for n in range(BACK_LANES // 128)]
    group = group_of()
    tiles[0] = jnp.where(group == BIAS, fold(column_sum(pre)), jnp.where(group == GAIN, fold(column_sum(pre * normed)), tiles[0]))
    tap_sums(product((kept_left[1, 0], kept_left[1, 1]), split(value)), tiles, SECOND)
    tap_sums(product((kept_left[0, 0], kept_left[0, 1]), split(pre)), tiles, LEFT)
    line = jnp.concatenate(tiles, axis=1)
    for d in range(z.devices):
        slabs[d] = line[d % C : d % C + 1]


def norm_sums(total):
    group = group_of()
    return [wide(spread_groups(jnp.where(group == n, total[:, :128], 0.0))) for n in (BIAS, GAIN)]


def hidden_kernel(z, gathered, dshift, d_above, d_below, hidden, near, stats, affine, weights, x, first_stats, pre_ref, gain_out, bias_out, slabs, pads, kept_w, sems):
    load = pltpu.make_async_copy(weights.at[3], kept_w, sems.at[0])
    load.start()
    total = jnp.sum(gathered[...], axis=0)
    bias_sum, gain_sum = norm_sums(total)
    bias_out[...] = bias_sum[:, :C]
    gain_out[...] = gain_sum[:, :C]
    bias_mean, gain_mean = bias_sum / z.pixels, gain_sum / z.pixels
    unit = normed_by(stats)
    factor = affine[2:3] * stats[1:2]

    def back(d, h):
        return factor * (d - bias_mean - unit(h) * gain_mean)

    own = back(dshift[...], hidden[...])
    up = back(d_above[...], near[0]) * inside(z, 1, True)
    down = back(d_below[...], near[1]) * inside(z, 1, False)
    load.wait()
    grad, _, _ = convolve(z, own, up, down, 1, pads, None, kept_w)
    normed = normed_by(first_stats)(x[...])
    pre = grad * gelu_slope(normed * affine[0:1] + affine[1:2])
    pre_ref[...] = pre
    lane = lax.broadcasted_iota(jnp.int32, (1, 128), 1)
    taps = TAPS * TAPS * C

    def along(row):
        return jnp.concatenate([row[:, :128]] * 3, axis=1)[:, :taps]

    second, left, against, ones = (total[:, n * C : n * C + taps] for n in (SECOND, LEFT, NORMED, ONES))
    first = along(factor) * (left - along(bias_mean) * ones - along(gain_mean) * against)
    sums = jnp.where(lane < C, fold(column_sum(pre)), fold(column_sum(pre * normed)))
    line = jnp.concatenate([sums[:, : 2 * C], second, first], axis=1)
    slabs[...] = jnp.broadcast_to(line[None], slabs.shape)


def back_kernel(z, gathered, pre, x, stats, affine, dout, back_s, back_l, one, two, gain_out, bias_out, half, lines):
    bias_sum, gain_sum = norm_sums(jnp.sum(gathered[:, :, pl.ds(0, 128)], axis=0))
    bias_out[...] = bias_sum[:, :C]
    gain_out[...] = gain_sum[:, :C]
    normed = normed_by(stats)(x[...])
    value = dout[...] + affine[0:1] * stats[1:2] * (pre[...] - bias_sum / z.pixels - normed * (gain_sum / z.pixels))
    put_halves(half, value)
    from_matrix(z, half, (back_s, back_l))
    for d in range(C):
        lines[pl.ds(d, 1), :] = gathered[d]
    for ref, group in ((two, LAST_SECOND), (one, LAST_FIRST)):
        for a in range(TAPS):
            for b in range(TAPS):
                at = (group + a * TAPS + b) * C
                ref[a, b] = lines[:, pl.ds(at, C)]


def call(body, ins, outs, scratch=(), sems=0):
    space = {"v": pltpu.VMEM, "h": pltpu.HBM}
    shapes = []
    for item in scratch:
        if isinstance(item, list):
            shapes.append([pltpu.VMEM(*s) for s in item])
        else:
            shapes.append(pltpu.VMEM(*item))
    if sems:
        shapes.append(pltpu.SemaphoreType.DMA((sems,)))
    run = pl.pallas_call(
        body,
        out_shape=[pltpu.HBM(shape, kind) if s == "h" else jax.ShapeDtypeStruct(shape, kind) for s, shape, kind in outs],
        in_specs=[pl.BlockSpec(memory_space=space[s]) for s in ins],
        out_specs=[pl.BlockSpec(memory_space=space[s]) for s, _, _ in outs],
        scratch_shapes=shapes,
        compiler_params=pltpu.CompilerParams(vmem_limit_bytes=VMEM_LIMIT),
    )
    return lambda *args: run(
        *(pltpu.with_memory_space_constraint(arg, pltpu.HBM) if s == "h" else arg for s, arg in zip(ins, args))
    )


def exchange(copies, axes):
    return lax.all_to_all(copies, axes, 0, 0, tiled=True)


def beyond(z, bottom, top, depths):
    hops = max(-(-depth // rows) for rows in z.rows for depth in depths)
    above, below = [], []
    for hop in range(1, hops + 1):
        above.append(lax.ppermute(bottom, "row", [(i, i + hop) for i in range(z.peers - hop)]))
        below.append(lax.ppermute(top, "row", [(i + hop, i) for i in range(z.peers - hop)]))
    if hops == 1:
        return above[0], below[0]
    up, down = [], []
    base = 0
    for depth in depths:
        for n in range(depth):
            for k in (1, 0):
                hop, back = divmod(depth - 1 - n, z.rows[k])
                at = base + (depth - 1 - back) * z.rims + z.rim[k]
                up.append(above[hop][at : at + z.edge[k]])
                hop, back = divmod(n, z.rows[k])
                at = base + back * z.rims + z.rim[k]
                down.append(below[hop][at : at + z.edge[k]])
        base += depth * z.rims
    up.append(jnp.concatenate([pixel_rows(z, above, base, 1, 1), pixel_rows(z, above, base, 0, 1)], axis=1))
    down.append(jnp.concatenate([pixel_rows(z, below, base, 0, 0), pixel_rows(z, below, base, 1, 0)], axis=1))
    return jnp.concatenate(up, axis=0), jnp.concatenate(down, axis=0)


def pixel_rows(z, bands, base, distance, last):
    lines = []
    for k in (0, 1):
        hop, back = divmod(distance, z.rows[k])
        at = base + k * z.images[0]
        half = 128 * abs(last - back)
        lines.append(bands[hop][at : at + z.images[k], half : half + 128])
    lines.append(jnp.zeros((z.slots - sum(z.images), 128), F32))
    return jnp.concatenate(lines, axis=0)


def local(
    image_small, image_large, teacher_small, teacher_large, upstream_small, upstream_large,
    conv_first, gain_first, bias_first, conv_second, gain_second, bias_second,
):
    peers = lax.axis_size("row")
    devices = lax.axis_size("img") * peers
    z = Sizes(image_small.shape, image_large.shape, devices, peers)
    body = lambda function: functools.partial(function, z)
    r = z.rims
    full, half, pair = (z.total, LANES), (2, z.total, 128), (devices, 2, 128)
    weight, left = (2, TAPS * TAP_ROWS, 128), (2, DEPTH, z.total)
    images = [image_small, image_large, upstream_small, upstream_large, teacher_small, teacher_large]
    f = lambda space, *shape: (space, shape, F32)
    depths = (REACH, 2)
    rim_rows = sum(depths) * r + z.slots

    x, bottom, top, copies, upstream, teacher = call(
        body(start_kernel),
        "hhhhhh",
        [("v", full, F32), f("v", rim_rows, LANES), f("v", rim_rows, LANES), ("v", pair, F32), ("h", full, F32), f("h", z.total, 128)],
        [[(a.shape, F32) for a in images], [(half, F32)] * 2, (full, F32), ((z.total, 128), F32)],
        8,
    )(*images)
    gathered = exchange(copies, AXES)
    above, below = beyond(z, bottom, top, depths)
    weights, affine = call(
        body(prepare_kernel),
        "hhhhhh",
        [("h", (4,) + weight, BF16), f("v", 4, LANES)],
        [[(conv_first.shape, F32)] * 2, ((4,) + weight, BF16), ((4, C), F32)],
        10,
    )(conv_first, conv_second, *(v.reshape(1, C) for v in (gain_first, bias_first, gain_second, bias_second)))

    hidden, h_above, h_below, stats_one, copies, more = call(
        body(first_kernel),
        "vvvvvh",
        [("v", full, F32), f("v", 3 * r, LANES), f("v", 3 * r, LANES), f("v", 2, LANES), ("v", pair, F32), f("h", 2, 2 * r + z.slots, LANES)],
        [z.pads(), z.chains(4), (weight, BF16)],
        3,
    )(x, above, below, gathered, affine, weights)
    gathered = exchange(copies, AXES)
    left_one, counts = call(
        body(first_operand_kernel),
        "vvvvv",
        [("h", left, BF16), f("v", C, 384)],
        [z.pads(), (left, BF16)],
        1,
    )(x, above, below, stats_one, affine)
    gathered, counts = lax.optimization_barrier((gathered, counts))

    map_shape = (peers, z.slots, 128)
    out, o_above, o_below, near, stats_two, copies = call(
        body(second_kernel),
        "vvvvvhvvvh",
        [("v", full, F32), f("v", 2 * r, LANES), f("v", 2 * r, LANES), f("v", 2, r, LANES), f("v", 2, LANES), ("v", map_shape, F32)],
        [z.pads(), z.chains(3), (weight, BF16), ((z.total, 128), F32)],
        2,
    )(hidden, h_above, h_below, gathered, affine, weights, x, above, below, teacher)
    gathered = exchange(copies, ("row",))
    extended = z.total + 4 * r
    out_s, out_l, left_two, packed, teachers, maps, slopes = call(
        body(second_operand_kernel),
        "vvvvvvvhvhh",
        [
            ("v", image_small.shape, F32), ("v", image_large.shape, F32), ("h", left, BF16), f("h", C, BACK_LANES),
            f("h", extended, 128), f("v", extended, 128), f("v", z.total + 2 * r, LANES),
        ],
        [
            z.pads(), (half, F32), (left, BF16), (left, BF16), ((C, BACK_LANES), F32), ((extended, 128), F32),
            ((2, z.slots, LANES), F32),
        ],
        6,
    )(hidden, near, stats_two, affine, out, o_above, o_below, left_one, counts, more, teacher)

    dout, dshift, d_above, d_below, slabs = call(
        body(upstream_kernel),
        "vvvvhhhhhhhvvvv",
        [("v", full, F32), ("v", full, F32), f("v", r, LANES), f("v", r, LANES), f("v", devices, 1, BACK_LANES)],
        [(full, F32), ((extended, 128), F32), ((2, 2 * r, LANES), F32), (weight, BF16), ((2,) + left, BF16), ((C, BACK_LANES), F32)]
        + [z.pads(), z.chains(2)],
        9,
    )(gathered, out, o_above, o_below, upstream, teachers, more, weights, left_one, left_two, packed, maps, slopes, hidden, stats_two)
    gathered = exchange(slabs, AXES)

    pre, gain_two, bias_two, slabs = call(
        body(hidden_kernel),
        "vvvvvvvvhvv",
        [("v", full, F32), f("v", 1, C), f("v", 1, C), f("v", devices, 1, LAST_LANES)],
        [z.pads(), (weight, BF16)],
        1,
    )(gathered, dshift, d_above, d_below, hidden, near, stats_two, affine, weights, x, stats_one)
    gathered = exchange(slabs, AXES)

    back_s, back_l, one, two, gain_one, bias_one = call(
        body(back_kernel),
        "vvvvvv",
        [("v", a.shape, F32) for a in (image_small, image_large, conv_first, conv_second)] + [f("v", 1, C), f("v", 1, C)],
        [(half, F32), ((C, LAST_LANES), F32)],
    )(gathered, pre, x, stats_one, affine, dout)
    return (
        out_s, out_l, back_s, back_l,
        one, gain_one.reshape(C), bias_one.reshape(C),
        two, gain_two.reshape(C), bias_two.reshape(C),
    )


def solution(mesh):
    split_bands, everywhere = P("img", "row", None), P()
    return jax.shard_map(
        local,
        mesh=mesh,
        in_specs=(split_bands,) * 6 + (everywhere,) * 6,
        out_specs=(split_bands,) * 4 + (everywhere,) * 6,
        check_vma=False,
    )
```

```python
import functools
import math

import jax
import jax.numpy as jnp
from jax import lax
from jax.experimental import pallas as pl
from jax.experimental.pallas import tpu as pltpu
from jax.sharding import PartitionSpec as P

C = 32
HS = 32
HL = 64
HEIGHTS = (HS, HL)

norm_eps = 1e-05
map_eps = 1e-06
beta_weight = 1000.0
AXES = ("img", "row")
BLOCK = 8
LANES = BLOCK * C
TAPS = 3
WIDTH = LANES + 128
DEPTH = TAPS * WIDTH
TAP_ROWS = 128 + 2 * C
REACH = 4
ROOT = math.sqrt(2.0 / math.pi)
CUBE = 0.044715
F32 = jnp.float32
BF16 = jnp.bfloat16
VMEM_LIMIT = 32 * 1024 * 1024
BIAS, GAIN, SECOND, LEFT, NORMED, ONES = 0, 1, 2, 11, 20, 29
BACK_LANES = 1280
LAST_SECOND, LAST_FIRST, LAST_LANES = 2, 11, 640


class Sizes:
    def __init__(self, small, large, devices, peers):
        self.images = (small[0], large[0])
        self.rows = (small[1], large[1])
        self.blocks = (HS // BLOCK, HL // BLOCK)
        self.step = tuple(n * r for n, r in zip(self.images, self.rows))
        self.count = tuple(b * s for b, s in zip(self.blocks, self.step))
        self.edge = tuple(b * n for b, n in zip(self.blocks, self.images))
        self.start = (self.count[1], 0)
        self.rim = (self.edge[1], 0)
        self.total = sum(self.count)
        self.rims = sum(self.edge)
        self.slots = -(-sum(self.images) // 8) * 8
        self.guard = -(-max(self.images) // 8) * 8
        self.devices = devices
        self.peers = peers
        self.here = float(self.total * BLOCK)
        self.pixels = self.here * devices

    def pads(self):
        return [((TAPS, 2, self.count[k] + 2 * self.step[k], 128), F32) for k in (0, 1)]

    def chains(self, depth):
        return [((2, 2 * self.guard + (depth + 1) * self.rims, 128), F32)] * 2


def split(value):
    high = value.astype(BF16)
    return high, (value - high.astype(F32)).astype(BF16)


def dot(left, right):
    return lax.dot_general(left, right, (((1,), (0,)), ((), ())), preferred_element_type=F32)


def product(left, right):
    if left[0].shape[1] % 128:
        return dot(left[0], right[0]) + (dot(left[0], right[1]) + dot(left[1], right[0]))
    return dot(
        jnp.concatenate([left[0], left[0], left[1]], axis=1), jnp.concatenate([right[0], right[1], right[0]], axis=0)
    )


def spread(left, right):
    right = right.astype(BF16)
    return dot(jnp.concatenate(split(left), axis=1), jnp.concatenate([right, right], axis=0))


def gelu(s):
    return 0.5 * s * (1.0 + jnp.tanh(ROOT * (s + CUBE * s * s * s)))


def gelu_slope(s):
    square = s * s
    t = jnp.tanh(ROOT * s * (1.0 + CUBE * square))
    return 0.5 * (1.0 + t) + 0.5 * s * (1.0 - t * t) * ROOT * (1.0 + 3.0 * CUBE * square)


def spread_groups(row):
    row = row + pltpu.roll(row, 64, 1)
    return row + pltpu.roll(row, 32, 1)


def fold(row):
    return spread_groups(row[:, :128] + row[:, 128:])


def wide(row):
    return jnp.concatenate([row, row], axis=1)


def group_of(rows=1, lanes=128):
    return lax.broadcasted_iota(jnp.int32, (rows, lanes), 1) // C


def column_sum(value):
    return jnp.sum(value, axis=0, keepdims=True)


def moments(z, value, ref):
    center = fold(column_sum(value)) / z.here
    off = value - wide(center)
    both = jnp.concatenate([center, fold(column_sum(off * off))], axis=0)
    ref[...] = jnp.broadcast_to(both[None], ref.shape)


def merged(z, ref):
    gathered = ref[...]
    mean = jnp.mean(gathered, axis=0)
    center = mean[0:1]
    off = gathered[:, 0, :] - center
    variance = mean[1:2] / z.here + jnp.mean(off * off, axis=0, keepdims=True)
    return wide(center), wide(lax.rsqrt(variance + norm_eps))


def put_halves(ref, value):
    ref[0] = value[:, :128]
    ref[1] = value[:, 128:]


def whole(ref):
    return jnp.concatenate([ref[0], ref[1]], axis=1)


def to_matrix(z, refs, half):
    for k in (0, 1):
        for j in range(z.blocks[k]):
            at = z.start[k] + j * z.step[k]
            for i in range(z.images[k]):
                for h in (0, 1):
                    half[h, pl.ds(at + i * z.rows[k], z.rows[k]), :] = refs[k][i, :, pl.ds(LANES * j + 128 * h, 128)]


def from_matrix(z, half, refs):
    for k in (0, 1):
        for j in range(z.blocks[k]):
            at = z.start[k] + j * z.step[k]
            for i in range(z.images[k]):
                for h in (0, 1):
                    refs[k][i, :, pl.ds(LANES * j + 128 * h, 128)] = half[h, pl.ds(at + i * z.rows[k], z.rows[k]), :]


def take_rims(z, half, depth, bottom, top):
    for k in (0, 1):
        for d in range(1, depth + 1):
            to_bottom = pl.ds((depth - d) * z.rims + z.rim[k], z.edge[k])
            to_top = pl.ds((d - 1) * z.rims + z.rim[k], z.edge[k])
            if d <= z.rows[k]:
                bottom[to_bottom, :] = half[pl.ds(z.start[k] + z.rows[k] - d, z.edge[k], stride=z.rows[k]), :]
                top[to_top, :] = half[pl.ds(z.start[k] + d - 1, z.edge[k], stride=z.rows[k]), :]
            else:
                bottom[to_bottom, :] = jnp.zeros((z.edge[k], 128), F32)
                top[to_top, :] = jnp.zeros((z.edge[k], 128), F32)


def inside(z, depth, above):
    at = lax.axis_index("row")
    large = lax.broadcasted_iota(jnp.int32, (z.rims, 1), 0) < z.rim[0]
    parts = []
    for n in range(depth):
        if above:
            ok = [jnp.where(at * rows >= depth - n, 1.0, 0.0) for rows in z.rows]
        else:
            ok = [jnp.where((at + 1) * rows + n + 1 <= height, 1.0, 0.0) for rows, height in zip(z.rows, HEIGHTS)]
        parts.append(jnp.where(large, ok[1], ok[0]).astype(F32))
    return jnp.concatenate(parts, axis=0)


def fill_pads(z, pads, value, above, below):
    for k in (0, 1):
        ref, step, count, rows = pads[k], z.step[k], z.count[k], z.rows[k]
        rim = slice(z.rim[k], z.rim[k] + z.edge[k])
        for h in (0, 1):
            lanes = slice(128 * h, 128 * h + 128)
            for a in range(TAPS):
                ref[a, h, pl.ds(0, step), :] = jnp.zeros((step, 128), F32)
                ref[a, h, pl.ds(step + count, step), :] = jnp.zeros((step, 128), F32)
            ref[1, h, pl.ds(step, count), :] = value[z.start[k] : z.start[k] + count, lanes]
            ref[0, h, pl.ds(step, count), :] = ref[1, h, pl.ds(step - 1, count), :]
            ref[2, h, pl.ds(step, count), :] = ref[1, h, pl.ds(step + 1, count), :]
            ref[0, h, pl.ds(step, z.edge[k], stride=rows), :] = above[rim, lanes]
            ref[2, h, pl.ds(step + rows - 1, z.edge[k], stride=rows), :] = below[rim, lanes]


def band_operand(z, pads):
    lane = lax.broadcasted_iota(jnp.int32, (1, 128), 1)
    parts = []
    for k in (1, 0):
        ref, step, count = pads[k], z.step[k], z.count[k]
        columns = []
        for a in range(TAPS):
            before = ref[a, 1, pl.ds(0, count), :]
            after = ref[a, 0, pl.ds(2 * step, count), :]
            columns += [
                ref[a, 0, pl.ds(step, count), :],
                ref[a, 1, pl.ds(step, count), :],
                jnp.where(lane >= 96, before, jnp.where(lane < 32, after, 0.0)),
            ]
        parts.append(jnp.concatenate(columns, axis=1))
    return jnp.concatenate(parts, axis=0)


def rim_operand(z, chain, depth):
    rows, g = (depth + 1) * z.rims, z.guard
    lane = lax.broadcasted_iota(jnp.int32, (1, 128), 1)
    m = lax.broadcasted_iota(jnp.int32, (z.rims, 1), 0)
    large = m < z.rim[0]
    has_before = jnp.where(large, m, m - z.rim[0]) >= jnp.where(large, z.images[1], z.images[0])
    has_after = m < jnp.where(large, z.rim[0] - z.images[1], z.rims - z.images[0])
    take = [(lane >= 96) & has_before & large, (lane >= 96) & has_before & ~large, (lane < 32) & has_after & large, (lane < 32) & has_after & ~large]
    columns = []
    for r in range(depth + 1):
        at = g + r * z.rims
        edge = jnp.zeros((z.rims, 128), F32)
        for mask, half, shift in zip(take, (1, 1, 0, 0), (-z.images[1], -z.images[0], z.images[1], z.images[0])):
            edge = jnp.where(mask, chain[half, pl.ds(at + shift, z.rims), :], edge)
        columns.append(jnp.concatenate([chain[0, pl.ds(at, z.rims), :], chain[1, pl.ds(at, z.rims), :], edge], axis=1))
    return jnp.concatenate(
        [jnp.concatenate(columns[n : n + TAPS], axis=1) for n in range(depth - 1)], axis=0
    )


def convolve(z, own, above, below, depth, pads, chains, weight):
    r = z.rims
    fill_pads(z, pads, own, above[(depth - 1) * r :], below[:r])
    parts = [band_operand(z, pads)]
    if depth > 1:
        for side, (rim, chain) in enumerate(zip((above, below), chains)):
            rim_at, own_at = (z.guard, z.guard + depth * r) if side == 0 else (z.guard + r, z.guard)
            for h in (0, 1):
                chain[h, pl.ds(rim_at, depth * r), :] = rim[:, 128 * h : 128 * h + 128]
                for k in (0, 1):
                    row = z.step[k] + (0 if side == 0 else z.rows[k] - 1)
                    chain[h, pl.ds(own_at + z.rim[k], z.edge[k]), :] = pads[k][1, h, pl.ds(row, z.edge[k], stride=z.rows[k]), :]
            parts.append(rim_operand(z, chain, depth))
    result = product(split(jnp.concatenate(parts, axis=0)), (weight_matrix(weight.at[0]), weight_matrix(weight.at[1])))
    n = z.total + (depth - 1) * r
    return result[: z.total], result[z.total : n], result[n:]


def image_sums(z, value):
    slot = lax.broadcasted_iota(jnp.int32, (z.slots, 1), 0)
    sums = jnp.zeros((z.slots, 128), F32)
    for k in (0, 1):
        line = value[z.start[k] : z.start[k] + z.step[k]]
        for j in range(1, z.blocks[k]):
            at = z.start[k] + j * z.step[k]
            line = line + value[at : at + z.step[k]]
        image = lax.broadcasted_iota(jnp.int32, (z.step[k], 1), 0) // z.rows[k]
        for i in range(z.images[k]):
            sums = jnp.where(slot == i + k * z.images[0], column_sum(jnp.where(image == i, line, 0.0)), sums)
    return sums


def image_rows(z, values, rims):
    parts = []
    for k in (1, 0):
        image = lax.broadcasted_iota(jnp.int32, (z.step[k], 1), 0) // z.rows[k]
        line = jnp.zeros((z.step[k], 128), F32)
        for i in range(z.images[k]):
            at = i + k * z.images[0]
            line = jnp.where(image == i, values[at : at + 1], line)
        parts += [line] * z.blocks[k]
    if rims:
        m = lax.broadcasted_iota(jnp.int32, (z.rims, 1), 0)
        image = jnp.where(m < z.rim[0], z.images[0] + m % z.images[1], (m - z.rim[0]) % z.images[0])
        line = jnp.zeros((z.rims, 128), F32)
        for at in range(sum(z.images)):
            line = jnp.where(image == at, values[at : at + 1], line)
        parts += [line] * rims
    return jnp.concatenate(parts, axis=0)


def channel_mean():
    a = lax.broadcasted_iota(jnp.int32, (LANES, 128), 0) // C
    b = lax.broadcasted_iota(jnp.int32, (LANES, 128), 1)
    return jnp.where(a == b, 1.0 / C, 0.0).astype(F32)


def to_channels():
    a = lax.broadcasted_iota(jnp.int32, (128, LANES), 0)
    b = lax.broadcasted_iota(jnp.int32, (128, LANES), 1) // C
    return jnp.where(a == b, 1.0, 0.0).astype(F32)


def attention(value):
    return spread(value * value, channel_mean())


def start_all(copies):
    for copy in copies:
        copy.start()


def wait_all(copies):
    for copy in copies:
        copy.wait()


def start_kernel(z, small, large, up_s, up_l, t_s, t_l, x, bottom, top, copies, raw, half, sems):
    loads = [pltpu.make_async_copy(a, b, sems.at[n]) for n, (a, b) in enumerate(zip((small, large, up_s, up_l, t_s, t_l), raw))]
    start_all(loads)
    r, n = z.rims, REACH * z.rims
    tail = n + 2 * r
    for ref in (bottom, top):
        ref[pl.ds(tail, z.slots), :] = jnp.zeros((z.slots, LANES), F32)
    wait_all(loads[:2])
    to_matrix(z, raw[:2], half)
    value = whole(half)
    x[...] = value
    moments(z, value, copies)
    for h in (0, 1):
        lanes = pl.ds(128 * h, 128)
        take_rims(z, half.at[h], REACH, bottom.at[pl.ds(0, n), lanes], top.at[pl.ds(0, n), lanes])
    wait_all(loads[2:])
    for k in (0, 1):
        width, rows = HEIGHTS[k], z.rows[k]
        for i in range(z.images[k]):
            slot = pl.ds(tail + i + k * z.images[0], 1)
            for d in (0, 1):
                to_bottom, to_top = n + (1 - d) * r + z.rim[k] + i, n + d * r + z.rim[k] + i
                for j in range(z.blocks[k]):
                    lanes, at = pl.ds(LANES * j, LANES), j * z.images[k]
                    if d < rows:
                        bottom[pl.ds(to_bottom + at, 1), :] = raw[2 + k][i, pl.ds(rows - 1 - d, 1), lanes]
                        top[pl.ds(to_top + at, 1), :] = raw[2 + k][i, pl.ds(d, 1), lanes]
                    else:
                        bottom[pl.ds(to_bottom + at, 1), :] = jnp.zeros((1, LANES), F32)
                        top[pl.ds(to_top + at, 1), :] = jnp.zeros((1, LANES), F32)
                if d < rows:
                    bottom[slot, pl.ds(128 * (1 - d), width)] = raw[4 + k][i, pl.ds(rows - 1 - d, 1), :]
                    top[slot, pl.ds(128 * d, width)] = raw[4 + k][i, pl.ds(d, 1), :]


def banded(taps, ref):
    row = lax.broadcasted_iota(jnp.int32, (128, 128), 0) // C
    lane = group_of(128)
    for a in range(TAPS):
        main = jnp.zeros((128, 128), F32)
        for b in range(TAPS):
            main = jnp.where(row - lane + 1 == b, taps[a][b], main)
        before = jnp.where(lane[:C] == 0, taps[a][0][:C], 0.0)
        after = jnp.where(lane[:C] == 3, taps[a][2][:C], 0.0)
        for n, part in enumerate(split(jnp.concatenate([main, before, after], axis=0))):
            ref[n, pl.ds(a * TAP_ROWS, TAP_ROWS), :] = part


def weight_matrix(ref):
    rows = []
    zeros = jnp.zeros((128 - C, 128), BF16)
    for a in range(TAPS):
        at = a * TAP_ROWS
        main = ref[pl.ds(at, 128), :]
        before = jnp.concatenate([zeros, ref[pl.ds(at + 128, C), :]], axis=0)
        after = jnp.concatenate([ref[pl.ds(at + 128 + C, C), :], zeros], axis=0)
        rows += [
            jnp.concatenate([main, before], axis=1),
            jnp.concatenate([after, main], axis=1),
            jnp.concatenate([before, after], axis=1),
        ]
    return jnp.concatenate(rows, axis=0)


def prepare_kernel(z, first, second, up_s, up_l, t_s, t_l, g1, b1, g2, b2, w1, w2, weights, affine, upstream, teacher, raw, kept, kept_u, rows, half, sems):
    targets = tuple(raw) + tuple(rows.at[pl.ds(n, 1), :] for n in range(4))
    refs = (first, second, up_s, up_l, t_s, t_l, g1, b1, g2, b2)
    loads = [pltpu.make_async_copy(a, b, sems.at[n]) for n, (a, b) in enumerate(zip(refs, targets))]
    start_all(loads)
    wait_all(loads)
    to_matrix(z, raw[2:4], half)
    kept_u[...] = whole(half)
    stores = [pltpu.make_async_copy(kept_u, upstream, sems.at[10])]
    stores[0].start()
    for n, (source, forward) in enumerate(zip(raw[:2], (w1, w2))):
        tiles = []
        for a in range(TAPS):
            line = [jnp.concatenate([source[a, b]] * 4, axis=1) for b in range(TAPS)]
            tiles.append([jnp.concatenate([tap] * 4, axis=0) for tap in line])
        turned = [[tiles[TAPS - 1 - a][TAPS - 1 - b].T for b in range(TAPS)] for a in range(TAPS)]
        banded(tiles, forward)
        banded(turned, kept.at[n])
        stores.append(pltpu.make_async_copy(kept.at[n], weights.at[n], sems.at[11 + n]))
        stores[-1].start()
    affine[...] = jnp.concatenate([rows[...]] * BLOCK, axis=1)
    teacher[...] = jnp.zeros(teacher.shape, F32)
    for k, ref in ((0, raw[4]), (1, raw[5])):
        for i in range(z.images[k]):
            line = ref[i]
            for j in range(z.blocks[k]):
                at = z.start[k] + j * z.step[k] + i * z.rows[k]
                teacher[pl.ds(at, z.rows[k]), pl.ds(0, BLOCK)] = line[:, j * BLOCK : (j + 1) * BLOCK]
    wait_all(stores)


def normed_by(stats):
    return lambda v: (v - stats[0:1]) * stats[1:2]


def activation(center, scale, gain, bias):
    factor = scale * gain
    offset = bias - center * factor
    return lambda v: gelu(v * factor + offset)


def first_kernel(z, x, above, below, gathered, affine, weight, hidden, h_above, h_below, stats, copies, pads, chains):
    n = REACH * z.rims
    center, scale = merged(z, gathered)
    act = activation(center, scale, affine[0:1], affine[1:2])
    own = act(x[...])
    up, down = act(above[pl.ds(0, n), :]) * inside(z, 4, True), act(below[pl.ds(0, n), :]) * inside(z, 4, False)
    own, up, down = convolve(z, own, up, down, 4, pads, chains, weight)
    moments(z, own, copies)
    hidden[...] = own
    h_above[...] = up
    h_below[...] = down
    stats[0:1] = center
    stats[1:2] = scale


def second_kernel(z, hidden, h_above, h_below, gathered, affine, weight, x, x_above, x_below, teacher, out, o_above, o_below, near, stats, copies, pads, chains):
    center, scale = merged(z, gathered)
    act = activation(center, scale, affine[2:3], affine[3:4])
    r = z.rims
    own = act(hidden[...])
    up, down = act(h_above[...]) * inside(z, 3, True), act(h_below[...]) * inside(z, 3, False)
    own, up, down = convolve(z, own, up, down, 3, pads, chains, weight)
    own = x[...] + own
    amap = attention(own)
    sums = image_sums(z, amap * amap) + pltpu.roll(image_sums(z, amap * teacher[...]), 64, 1)
    copies[...] = jnp.broadcast_to(sums[None], copies.shape)
    out[...] = own
    o_above[...] = x_above[pl.ds(2 * r, 2 * r), :] + up
    o_below[...] = x_below[pl.ds(0, 2 * r), :] + down
    near[0] = h_above[pl.ds(2 * r, r), :]
    near[1] = h_below[pl.ds(0, r), :]
    stats[0:1] = center
    stats[1:2] = scale


def tap_rows(a, q):
    return a * WIDTH + (LANES + 3 * C if q < 0 else LANES if q == BLOCK else q * C)


def tap_sums(result, tiles, first_group):
    group = group_of()
    for a in range(TAPS):
        for b in range(TAPS):
            total = None
            for h in (0, 1):
                half = None
                for p in range(4 * h, 4 * h + 4):
                    at = tap_rows(a, p + b - 1)
                    part = result[at : at + C, 128 * h : 128 * h + 128]
                    half = part if half is None else jnp.where(group == p % 4, part, half)
                total = half if total is None else total + half
            tile, slot = divmod(first_group + a * TAPS + b, 4)
            tiles[tile] = jnp.where(group == slot, spread_groups(total), tiles[tile])


def tap_counts(column, tiles, first_group):
    group = group_of()
    for a in range(TAPS):
        for b in range(TAPS):
            total = sum(column[tap_rows(a, p + b - 1) : tap_rows(a, p + b - 1) + C] for p in range(BLOCK))
            tile, slot = divmod(first_group + a * TAPS + b, 4)
            tiles[tile] = jnp.where(group == slot, total, tiles[tile])


def turned_operand(z, pads, kept):
    left = band_operand(z, pads).T
    parts = split(left)
    for n in (0, 1):
        kept[n] = parts[n]
    return left


def first_operand_kernel(z, x, above, below, stats, affine, teacher, upstream, weights, left, counts, teachers, spread_u, pads, chains, kept, kept_w, kept_u, pixels, kept_t, kept_c, sems):
    r = z.rims
    loads = [pltpu.make_async_copy(upstream, kept_u, sems.at[0]), pltpu.make_async_copy(weights.at[1], kept_w, sems.at[1])]
    start_all(loads)
    act = activation(stats[0:1], stats[1:2], affine[0:1], affine[1:2])
    up, down = act(above[pl.ds(3 * r, r), :]) * inside(z, 1, True), act(below[pl.ds(0, r), :]) * inside(z, 1, False)
    fill_pads(z, pads, act(x[...]), up, down)
    value = turned_operand(z, pads, kept)
    stores = [pltpu.make_async_copy(kept, left, sems.at[2])]
    stores[0].start()
    tiles = [jnp.zeros((C, 128), F32) for _ in range(3)]
    tap_counts(jnp.sum(value, axis=1, keepdims=True), tiles, 0)
    counts[...] = jnp.concatenate(tiles, axis=1)
    pixels[pl.ds(0, z.total), :] = teacher[...]
    pixels[pl.ds(z.total, 4 * r), :] = jnp.zeros((4 * r, 128), F32)
    n = (REACH + 2) * r
    for side, ref in enumerate((above, below)):
        for d in (0, 1):
            for k in (0, 1):
                line = ref[pl.ds(n + k * z.images[0], z.images[k]), pl.ds(128 * d, 128)]
                for j in range(z.blocks[k]):
                    at = z.total + (2 * side + d) * r + z.rim[k] + j * z.images[k]
                    pixels[pl.ds(at, z.images[k]), pl.ds(0, BLOCK)] = line[:, j * BLOCK : (j + 1) * BLOCK]
    kept_t[...] = spread(pixels[...], to_channels())
    stores.append(pltpu.make_async_copy(kept_t, teachers, sems.at[3]))
    stores[1].start()
    wait_all(loads)
    n = REACH * r
    parts = convolve(
        z, kept_u[...], above[pl.ds(n, 2 * r), :] * inside(z, 2, True), below[pl.ds(n, 2 * r), :] * inside(z, 2, False),
        2, pads, chains, kept_w,
    )
    kept_c[...] = jnp.concatenate(parts, axis=0)
    stores.append(pltpu.make_async_copy(kept_c, spread_u, sems.at[4]))
    stores[2].start()
    wait_all(stores)


def second_operand_kernel(z, hidden, near, stats, affine, out, o_above, o_below, first_left, counts, teachers, spread_u, weights, out_s, out_l, left, packed, shifts, own_map, own_teacher, pads, chains, half, kept, kept_left, kept_packed, kept_t, kept_u, kept_w, kept_s, sems):
    r = z.rims
    loads = [
        pltpu.make_async_copy(teachers, kept_t, sems.at[0]),
        pltpu.make_async_copy(weights.at[1], kept_w, sems.at[1]),
        pltpu.make_async_copy(spread_u, kept_u, sems.at[2]),
        pltpu.make_async_copy(first_left, kept_left, sems.at[3]),
    ]
    start_all(loads)
    act = activation(stats[0:1], stats[1:2], affine[2:3], affine[3:4])
    fill_pads(z, pads, act(hidden[...]), act(near[0]) * inside(z, 1, True), act(near[1]) * inside(z, 1, False))
    turned_operand(z, pads, kept)
    stores = [pltpu.make_async_copy(kept, left, sems.at[4])]
    stores[0].start()
    put_halves(half, out[...])
    from_matrix(z, half, (out_s, out_l))
    normed = normed_by(stats)(jnp.concatenate([hidden[...], near[0], near[1]], axis=0))
    slopes = gelu_slope(normed * affine[2:3] + affine[3:4])
    o = jnp.concatenate([out[...], o_above[...] * inside(z, 2, True), o_below[...] * inside(z, 2, False)], axis=0)
    by_map = spread(attention(o), to_channels()) * o
    wait_all(loads[:3])
    by_teacher = kept_t[...] * o
    own_map[...] = by_map[: z.total]
    own_teacher[...] = by_teacher[: z.total]
    kept_s[0] = kept_u[...] * slopes
    for n, value in ((1, by_map), (2, by_teacher)):
        parts = convolve(
            z, value[: z.total], value[z.total : z.total + 2 * r], value[z.total + 2 * r :], 2, pads, chains, kept_w
        )
        kept_s[n] = jnp.concatenate(parts, axis=0) * slopes
    stores.append(pltpu.make_async_copy(kept_s, shifts, sems.at[5]))
    stores[1].start()
    loads[3].wait()
    tiles = [jnp.zeros((C, 128), F32) for _ in range(BACK_LANES // 128)]
    tap_sums(product((kept_left[0], kept_left[1]), split(normed[: z.total])), tiles, NORMED)
    group = group_of()
    for n in range(TAPS * TAPS):
        tile, slot = divmod(ONES + n, 4)
        line = spread_groups(jnp.where(group == n % 4, counts[:, 128 * (n // 4) : 128 * (n // 4) + 128], 0.0))
        tiles[tile] = jnp.where(group == slot, line, tiles[tile])
    kept_packed[...] = jnp.concatenate(tiles, axis=1)
    stores.append(pltpu.make_async_copy(kept_packed, packed, sems.at[6]))
    stores[2].start()
    wait_all(stores)


def upstream_kernel(z, gathered, upstream, shifts, left_1, left_2, packed, own_map, own_teacher, hidden, stats, dout, dshift, d_above, d_below, slabs, kept_u, kept_s, kept_left, kept_packed, sems):
    r = z.rims
    loads = [
        pltpu.make_async_copy(a, b, sems.at[n])
        for n, (a, b) in enumerate(
            (
                (upstream, kept_u), (shifts, kept_s),
                (left_2.at[0], kept_left.at[1, 0]), (left_2.at[1], kept_left.at[1, 1]),
                (left_1.at[0], kept_left.at[0, 0]), (left_1.at[1], kept_left.at[0, 1]), (packed, kept_packed),
            )
        )
    ]
    start_all(loads)
    lane = lax.broadcasted_iota(jnp.int32, (z.slots, 128), 1)
    sums = jnp.sum(gathered[...], axis=0)
    square = jnp.sum(jnp.where(lane < 64, sums, 0.0), axis=1, keepdims=True)
    cross = jnp.sum(jnp.where(lane < 64, 0.0, sums), axis=1, keepdims=True)
    inverse = lax.rsqrt(square + map_eps)
    inner = beta_weight * (square * inverse - cross) * inverse
    shape = (z.slots, 128)
    for_map = (beta_weight - inner) * inverse * inverse * (2.0 / C)
    for_teacher = beta_weight * inverse * (2.0 / C)
    for_map, for_teacher = (wide(image_rows(z, jnp.broadcast_to(v, shape), 2)) for v in (for_map, for_teacher))
    loads[0].wait()
    value = kept_u[...] + for_map[: z.total] * own_map[...] - for_teacher[: z.total] * own_teacher[...]
    dout[...] = value
    loads[1].wait()
    shift = kept_s[0] + for_map * kept_s[1] - for_teacher * kept_s[2]
    pre = shift[: z.total]
    dshift[...] = pre
    d_above[...] = shift[z.total : z.total + r]
    d_below[...] = shift[z.total + r :]
    normed = normed_by(stats)(hidden[...])
    wait_all(loads[2:4])
    second = product((kept_left[1, 0], kept_left[1, 1]), split(value))
    wait_all(loads[4:])
    first = product((kept_left[0, 0], kept_left[0, 1]), split(pre))
    tiles = [kept_packed[:, 128 * n : 128 * n + 128] for n in range(BACK_LANES // 128)]
    group = group_of()
    tiles[0] = jnp.where(group == BIAS, fold(column_sum(pre)), jnp.where(group == GAIN, fold(column_sum(pre * normed)), tiles[0]))
    tap_sums(second, tiles, SECOND)
    tap_sums(first, tiles, LEFT)
    line = jnp.concatenate(tiles, axis=1)
    for d in range(z.devices):
        slabs[d] = line[d % C : d % C + 1]


def norm_sums(total):
    group = group_of()
    return [wide(spread_groups(jnp.where(group == n, total[:, :128], 0.0))) for n in (BIAS, GAIN)]


def hidden_kernel(z, gathered, dshift, d_above, d_below, hidden, near, stats, affine, weights, x, first_stats, pre_ref, gain_out, bias_out, slabs, pads, kept_w, sems):
    load = pltpu.make_async_copy(weights.at[0], kept_w, sems.at[0])
    load.start()
    total = jnp.sum(gathered[...], axis=0)
    bias_sum, gain_sum = norm_sums(total)
    bias_out[...] = bias_sum[:, :C]
    gain_out[...] = gain_sum[:, :C]
    bias_mean, gain_mean = bias_sum / z.pixels, gain_sum / z.pixels
    unit = normed_by(stats)
    factor = affine[2:3] * stats[1:2]

    def back(d, h):
        return factor * (d - bias_mean - unit(h) * gain_mean)

    own = back(dshift[...], hidden[...])
    up = back(d_above[...], near[0]) * inside(z, 1, True)
    down = back(d_below[...], near[1]) * inside(z, 1, False)
    load.wait()
    grad, _, _ = convolve(z, own, up, down, 1, pads, None, kept_w)
    normed = normed_by(first_stats)(x[...])
    pre = grad * gelu_slope(normed * affine[0:1] + affine[1:2])
    pre_ref[...] = pre
    lane = lax.broadcasted_iota(jnp.int32, (1, 128), 1)
    taps = TAPS * TAPS * C

    def along(row):
        return jnp.concatenate([row[:, :128]] * 3, axis=1)[:, :taps]

    second, left, against, ones = (total[:, n * C : n * C + taps] for n in (SECOND, LEFT, NORMED, ONES))
    first = along(factor) * (left - along(bias_mean) * ones - along(gain_mean) * against)
    sums = jnp.where(lane < C, fold(column_sum(pre)), fold(column_sum(pre * normed)))
    line = jnp.concatenate([sums[:, : 2 * C], second, first], axis=1)
    slabs[...] = jnp.broadcast_to(line[None], slabs.shape)


def back_kernel(z, gathered, pre, x, stats, affine, dout, back_s, back_l, one, two, gain_out, bias_out, half, lines):
    bias_sum, gain_sum = norm_sums(jnp.sum(gathered[:, :, pl.ds(0, 128)], axis=0))
    bias_out[...] = bias_sum[:, :C]
    gain_out[...] = gain_sum[:, :C]
    normed = normed_by(stats)(x[...])
    value = dout[...] + affine[0:1] * stats[1:2] * (pre[...] - bias_sum / z.pixels - normed * (gain_sum / z.pixels))
    put_halves(half, value)
    from_matrix(z, half, (back_s, back_l))
    for d in range(C):
        lines[pl.ds(d, 1), :] = gathered[d]
    for ref, group in ((two, LAST_SECOND), (one, LAST_FIRST)):
        for a in range(TAPS):
            for b in range(TAPS):
                at = (group + a * TAPS + b) * C
                ref[a, b] = lines[:, pl.ds(at, C)]


def call(body, ins, outs, scratch=(), sems=0):
    space = {"v": pltpu.VMEM, "h": pltpu.HBM}
    shapes = []
    for item in scratch:
        if isinstance(item, list):
            shapes.append([pltpu.VMEM(*s) for s in item])
        else:
            shapes.append(pltpu.VMEM(*item))
    if sems:
        shapes.append(pltpu.SemaphoreType.DMA((sems,)))
    run = pl.pallas_call(
        body,
        out_shape=[pltpu.HBM(shape, kind) if s == "h" else jax.ShapeDtypeStruct(shape, kind) for s, shape, kind in outs],
        in_specs=[pl.BlockSpec(memory_space=space[s]) for s in ins],
        out_specs=[pl.BlockSpec(memory_space=space[s]) for s, _, _ in outs],
        scratch_shapes=shapes,
        compiler_params=pltpu.CompilerParams(vmem_limit_bytes=VMEM_LIMIT),
    )
    return lambda *args: run(
        *(pltpu.with_memory_space_constraint(arg, pltpu.HBM) if s == "h" else arg for s, arg in zip(ins, args))
    )


def exchange(copies, axes):
    return lax.all_to_all(copies, axes, 0, 0, tiled=True)


def beyond(z, bottom, top, depths):
    hops = max(-(-depth // rows) for rows in z.rows for depth in depths)
    above, below = [], []
    for hop in range(1, hops + 1):
        above.append(lax.ppermute(bottom, "row", [(i, i + hop) for i in range(z.peers - hop)]))
        below.append(lax.ppermute(top, "row", [(i + hop, i) for i in range(z.peers - hop)]))
    if hops == 1:
        return above[0], below[0]
    up, down = [], []
    base = 0
    for depth in depths:
        for n in range(depth):
            for k in (1, 0):
                hop, back = divmod(depth - 1 - n, z.rows[k])
                at = base + (depth - 1 - back) * z.rims + z.rim[k]
                up.append(above[hop][at : at + z.edge[k]])
                hop, back = divmod(n, z.rows[k])
                at = base + back * z.rims + z.rim[k]
                down.append(below[hop][at : at + z.edge[k]])
        base += depth * z.rims
    up.append(jnp.concatenate([pixel_rows(z, above, base, 1, 1), pixel_rows(z, above, base, 0, 1)], axis=1))
    down.append(jnp.concatenate([pixel_rows(z, below, base, 0, 0), pixel_rows(z, below, base, 1, 0)], axis=1))
    return jnp.concatenate(up, axis=0), jnp.concatenate(down, axis=0)


def pixel_rows(z, bands, base, distance, last):
    lines = []
    for k in (0, 1):
        hop, back = divmod(distance, z.rows[k])
        at = base + k * z.images[0]
        half = 128 * abs(last - back)
        lines.append(bands[hop][at : at + z.images[k], half : half + 128])
    lines.append(jnp.zeros((z.slots - sum(z.images), 128), F32))
    return jnp.concatenate(lines, axis=0)


def local(
    image_small, image_large, teacher_small, teacher_large, upstream_small, upstream_large,
    conv_first, gain_first, bias_first, conv_second, gain_second, bias_second,
):
    peers = lax.axis_size("row")
    devices = lax.axis_size("img") * peers
    z = Sizes(image_small.shape, image_large.shape, devices, peers)
    body = lambda function: functools.partial(function, z)
    r = z.rims
    full, half, pair = (z.total, LANES), (2, z.total, 128), (devices, 2, 128)
    weight, left = (2, TAPS * TAP_ROWS, 128), (2, DEPTH, z.total)
    images = [image_small, image_large, upstream_small, upstream_large, teacher_small, teacher_large]
    f = lambda space, *shape: (space, shape, F32)
    depths = (REACH, 2)
    rim_rows = sum(depths) * r + z.slots

    x, bottom, top, copies = call(
        body(start_kernel),
        "hhhhhh",
        [("v", full, F32), f("v", rim_rows, LANES), f("v", rim_rows, LANES), ("v", pair, F32)],
        [[(a.shape, F32) for a in images], (half, F32)],
        6,
    )(*images)
    gathered = exchange(copies, AXES)
    above, below = beyond(z, bottom, top, depths)
    params = [conv_first, conv_second] + images[2:]
    w1, w2, weights, affine, upstream, teacher = call(
        body(prepare_kernel),
        "hhhhhhhhhh",
        [("v", weight, BF16), ("v", weight, BF16), ("h", (2,) + weight, BF16), f("v", 4, LANES), ("h", full, F32), f("v", z.total, 128)],
        [[(a.shape, F32) for a in params], ((2,) + weight, BF16), (full, F32), ((4, C), F32), (half, F32)],
        13,
    )(*params, *(v.reshape(1, C) for v in (gain_first, bias_first, gain_second, bias_second)))

    hidden, h_above, h_below, stats_one, copies = call(
        body(first_kernel),
        "vvvvvv",
        [("v", full, F32), f("v", 3 * r, LANES), f("v", 3 * r, LANES), f("v", 2, LANES), ("v", pair, F32)],
        [z.pads(), z.chains(4)],
    )(x, above, below, gathered, affine, w1)
    gathered = exchange(copies, AXES)
    extended, near_rows = z.total + 4 * r, z.total + 2 * r
    left_one, counts, teachers, spread_u = call(
        body(first_operand_kernel),
        "vvvvvvhh",
        [("h", left, BF16), f("v", C, 384), f("h", extended, LANES), f("h", near_rows, LANES)],
        [
            z.pads(), z.chains(2), (left, BF16), (weight, BF16), (full, F32), ((extended, 128), F32),
            ((extended, LANES), F32), ((near_rows, LANES), F32),
        ],
        5,
    )(x, above, below, stats_one, affine, teacher, upstream, weights)
    gathered, counts = lax.optimization_barrier((gathered, counts))

    map_shape = (peers, z.slots, 128)
    out, o_above, o_below, near, stats_two, copies = call(
        body(second_kernel),
        "vvvvvvvvvv",
        [("v", full, F32), f("v", 2 * r, LANES), f("v", 2 * r, LANES), f("v", 2, r, LANES), f("v", 2, LANES), ("v", map_shape, F32)],
        [z.pads(), z.chains(3)],
    )(hidden, h_above, h_below, gathered, affine, w2, x, above, below, teacher)
    gathered = exchange(copies, ("row",))
    out_s, out_l, left_two, packed, shifts, own_map, own_teacher = call(
        body(second_operand_kernel),
        "vvvvvvvhvhhh",
        [
            ("v", image_small.shape, F32), ("v", image_large.shape, F32), ("h", left, BF16), f("h", C, BACK_LANES),
            f("h", 3, near_rows, LANES), ("v", full, F32), ("v", full, F32),
        ],
        [
            z.pads(), z.chains(2), (half, F32), (left, BF16), (left, BF16), ((C, BACK_LANES), F32), ((extended, LANES), F32),
            ((near_rows, LANES), F32), (weight, BF16), ((3, near_rows, LANES), F32),
        ],
        7,
    )(hidden, near, stats_two, affine, out, o_above, o_below, left_one, counts, teachers, spread_u, weights)

    dout, dshift, d_above, d_below, slabs = call(
        body(upstream_kernel),
        "vhhhhhvvvv",
        [("v", full, F32), ("v", full, F32), f("v", r, LANES), f("v", r, LANES), f("v", devices, 1, BACK_LANES)],
        [(full, F32), ((3, near_rows, LANES), F32), ((2,) + left, BF16), ((C, BACK_LANES), F32)],
        7,
    )(gathered, upstream, shifts, left_one, left_two, packed, own_map, own_teacher, hidden, stats_two)
    gathered = exchange(slabs, AXES)

    pre, gain_two, bias_two, slabs = call(
        body(hidden_kernel),
        "vvvvvvvvhvv",
        [("v", full, F32), f("v", 1, C), f("v", 1, C), f("v", devices, 1, LAST_LANES)],
        [z.pads(), (weight, BF16)],
        1,
    )(gathered, dshift, d_above, d_below, hidden, near, stats_two, affine, weights, x, stats_one)
    gathered = exchange(slabs, AXES)

    back_s, back_l, one, two, gain_one, bias_one = call(
        body(back_kernel),
        "vvvvvv",
        [("v", a.shape, F32) for a in (image_small, image_large, conv_first, conv_second)] + [f("v", 1, C), f("v", 1, C)],
        [(half, F32), ((C, LAST_LANES), F32)],
    )(gathered, pre, x, stats_one, affine, dout)
    return (
        out_s, out_l, back_s, back_l,
        one, gain_one.reshape(C), bias_one.reshape(C),
        two, gain_two.reshape(C), bias_two.reshape(C),
    )


def solution(mesh):
    split_bands, everywhere = P("img", "row", None), P()
    return jax.shard_map(
        local,
        mesh=mesh,
        in_specs=(split_bands,) * 6 + (everywhere,) * 6,
        out_specs=(split_bands,) * 4 + (everywhere,) * 6,
        check_vma=False,
    )
```

```python
import functools
import math

import jax
import jax.numpy as jnp
from jax import lax
from jax.experimental import pallas as pl
from jax.experimental.pallas import tpu as pltpu
from jax.sharding import PartitionSpec as P

C = 32
HS = 32
HL = 64
HEIGHTS = (HS, HL)

norm_eps = 1e-05
map_eps = 1e-06
beta_weight = 1000.0
AXES = ("img", "row")
BLOCK = 8
LANES = BLOCK * C
TAPS = 3
WIDTH = LANES + 128
DEPTH = TAPS * WIDTH
TAP_ROWS = 128 + 2 * C
REACH = 4
ROOT = math.sqrt(2.0 / math.pi)
CUBE = 0.044715
F32 = jnp.float32
BF16 = jnp.bfloat16
VMEM_LIMIT = 32 * 1024 * 1024
BIAS, GAIN, SECOND, LEFT, NORMED, ONES = 0, 1, 2, 11, 20, 29
BACK_LANES = 1280
LAST_SECOND, LAST_FIRST, LAST_LANES = 2, 11, 640


class Sizes:
    def __init__(self, small, large, devices, peers):
        self.images = (small[0], large[0])
        self.rows = (small[1], large[1])
        self.blocks = (HS // BLOCK, HL // BLOCK)
        self.step = tuple(n * r for n, r in zip(self.images, self.rows))
        self.count = tuple(b * s for b, s in zip(self.blocks, self.step))
        self.edge = tuple(b * n for b, n in zip(self.blocks, self.images))
        self.start = (self.count[1], 0)
        self.rim = (self.edge[1], 0)
        self.total = sum(self.count)
        self.rims = sum(self.edge)
        self.slots = -(-sum(self.images) // 8) * 8
        self.guard = -(-max(self.images) // 8) * 8
        self.devices = devices
        self.peers = peers
        self.here = float(self.total * BLOCK)
        self.pixels = self.here * devices

    def pads(self):
        return [((TAPS, 2, self.count[k] + 2 * self.step[k], 128), F32) for k in (0, 1)]

    def chains(self, depth):
        return [((2, 2 * self.guard + (depth + 1) * self.rims, 128), F32)] * 2


def split(value):
    high = value.astype(BF16)
    return high, (value - high.astype(F32)).astype(BF16)


def dot(left, right):
    return lax.dot_general(left, right, (((1,), (0,)), ((), ())), preferred_element_type=F32)


def product(left, right):
    if left[0].shape[1] % 128:
        return dot(left[0], right[0]) + (dot(left[0], right[1]) + dot(left[1], right[0]))
    return dot(
        jnp.concatenate([left[0], left[0], left[1]], axis=1), jnp.concatenate([right[0], right[1], right[0]], axis=0)
    )


def spread(left, right):
    right = right.astype(BF16)
    return dot(jnp.concatenate(split(left), axis=1), jnp.concatenate([right, right], axis=0))


def gelu(s):
    return 0.5 * s * (1.0 + jnp.tanh(ROOT * (s + CUBE * s * s * s)))


def gelu_slope(s):
    square = s * s
    t = jnp.tanh(ROOT * s * (1.0 + CUBE * square))
    return 0.5 * (1.0 + t) + 0.5 * s * (1.0 - t * t) * ROOT * (1.0 + 3.0 * CUBE * square)


def spread_groups(row):
    row = row + pltpu.roll(row, 64, 1)
    return row + pltpu.roll(row, 32, 1)


def fold(row):
    return spread_groups(row[:, :128] + row[:, 128:])


def wide(row):
    return jnp.concatenate([row, row], axis=1)


def group_of(rows=1, lanes=128):
    return lax.broadcasted_iota(jnp.int32, (rows, lanes), 1) // C


def column_sum(value):
    return jnp.sum(value, axis=0, keepdims=True)


def moments(z, value, ref):
    center = fold(column_sum(value)) / z.here
    off = value - wide(center)
    both = jnp.concatenate([center, fold(column_sum(off * off))], axis=0)
    ref[...] = jnp.broadcast_to(both[None], ref.shape)


def merged(z, ref):
    gathered = ref[...]
    mean = jnp.mean(gathered, axis=0)
    center = mean[0:1]
    off = gathered[:, 0, :] - center
    variance = mean[1:2] / z.here + jnp.mean(off * off, axis=0, keepdims=True)
    return wide(center), wide(lax.rsqrt(variance + norm_eps))


def put_halves(ref, value):
    ref[0] = value[:, :128]
    ref[1] = value[:, 128:]


def whole(ref):
    return jnp.concatenate([ref[0], ref[1]], axis=1)


def to_matrix(z, refs, half):
    for k in (0, 1):
        for j in range(z.blocks[k]):
            at = z.start[k] + j * z.step[k]
            for i in range(z.images[k]):
                for h in (0, 1):
                    half[h, pl.ds(at + i * z.rows[k], z.rows[k]), :] = refs[k][i, :, pl.ds(LANES * j + 128 * h, 128)]


def from_matrix(z, half, refs):
    for k in (0, 1):
        for j in range(z.blocks[k]):
            at = z.start[k] + j * z.step[k]
            for i in range(z.images[k]):
                for h in (0, 1):
                    refs[k][i, :, pl.ds(LANES * j + 128 * h, 128)] = half[h, pl.ds(at + i * z.rows[k], z.rows[k]), :]


def take_rims(z, half, depth, bottom, top):
    for k in (0, 1):
        for d in range(1, depth + 1):
            to_bottom = pl.ds((depth - d) * z.rims + z.rim[k], z.edge[k])
            to_top = pl.ds((d - 1) * z.rims + z.rim[k], z.edge[k])
            if d <= z.rows[k]:
                bottom[to_bottom, :] = half[pl.ds(z.start[k] + z.rows[k] - d, z.edge[k], stride=z.rows[k]), :]
                top[to_top, :] = half[pl.ds(z.start[k] + d - 1, z.edge[k], stride=z.rows[k]), :]
            else:
                bottom[to_bottom, :] = jnp.zeros((z.edge[k], 128), F32)
                top[to_top, :] = jnp.zeros((z.edge[k], 128), F32)


def inside(z, depth, above):
    at = lax.axis_index("row")
    large = lax.broadcasted_iota(jnp.int32, (z.rims, 1), 0) < z.rim[0]
    parts = []
    for n in range(depth):
        if above:
            ok = [jnp.where(at * rows >= depth - n, 1.0, 0.0) for rows in z.rows]
        else:
            ok = [jnp.where((at + 1) * rows + n + 1 <= height, 1.0, 0.0) for rows, height in zip(z.rows, HEIGHTS)]
        parts.append(jnp.where(large, ok[1], ok[0]).astype(F32))
    return jnp.concatenate(parts, axis=0)


def fill_center(z, pads, value):
    for k in (0, 1):
        ref, step, count = pads[k], z.step[k], z.count[k]
        for h in (0, 1):
            ref[1, h, pl.ds(0, step), :] = jnp.zeros((step, 128), F32)
            ref[1, h, pl.ds(step, count), :] = value[z.start[k] : z.start[k] + count, 128 * h : 128 * h + 128]
            ref[1, h, pl.ds(step + count, step), :] = jnp.zeros((step, 128), F32)


def fill_shifted(z, pads, above, below):
    for k in (0, 1):
        ref, step, count, rows = pads[k], z.step[k], z.count[k], z.rows[k]
        rim = slice(z.rim[k], z.rim[k] + z.edge[k])
        for h in (0, 1):
            lanes = slice(128 * h, 128 * h + 128)
            ref[0, h, pl.ds(step, count), :] = ref[1, h, pl.ds(step - 1, count), :]
            ref[2, h, pl.ds(step, count), :] = ref[1, h, pl.ds(step + 1, count), :]
            ref[0, h, pl.ds(step, z.edge[k], stride=rows), :] = above[rim, lanes]
            ref[2, h, pl.ds(step + rows - 1, z.edge[k], stride=rows), :] = below[rim, lanes]


def fill_pads(z, pads, value, above, below):
    fill_center(z, pads, value)
    fill_shifted(z, pads, above, below)
    for k in (0, 1):
        ref, step, count = pads[k], z.step[k], z.count[k]
        for h in (0, 1):
            for a in (0, 2):
                ref[a, h, pl.ds(0, step), :] = jnp.zeros((step, 128), F32)
                ref[a, h, pl.ds(step + count, step), :] = jnp.zeros((step, 128), F32)


def band_operand(z, pads, taps=range(TAPS)):
    lane = lax.broadcasted_iota(jnp.int32, (1, 128), 1)
    parts = []
    for k in (1, 0):
        ref, step, count = pads[k], z.step[k], z.count[k]
        columns = []
        for a in taps:
            before = ref[a, 1, pl.ds(0, count), :]
            after = ref[a, 0, pl.ds(2 * step, count), :]
            columns += [
                ref[a, 0, pl.ds(step, count), :],
                ref[a, 1, pl.ds(step, count), :],
                jnp.where(lane >= 96, before, jnp.where(lane < 32, after, 0.0)),
            ]
        parts.append(jnp.concatenate(columns, axis=1))
    return jnp.concatenate(parts, axis=0)


def rim_operand(z, chain, depth):
    rows, g = (depth + 1) * z.rims, z.guard
    lane = lax.broadcasted_iota(jnp.int32, (1, 128), 1)
    m = lax.broadcasted_iota(jnp.int32, (z.rims, 1), 0)
    large = m < z.rim[0]
    has_before = jnp.where(large, m, m - z.rim[0]) >= jnp.where(large, z.images[1], z.images[0])
    has_after = m < jnp.where(large, z.rim[0] - z.images[1], z.rims - z.images[0])
    take = [(lane >= 96) & has_before & large, (lane >= 96) & has_before & ~large, (lane < 32) & has_after & large, (lane < 32) & has_after & ~large]
    columns = []
    for r in range(depth + 1):
        at = g + r * z.rims
        edge = jnp.zeros((z.rims, 128), F32)
        for mask, half, shift in zip(take, (1, 1, 0, 0), (-z.images[1], -z.images[0], z.images[1], z.images[0])):
            edge = jnp.where(mask, chain[half, pl.ds(at + shift, z.rims), :], edge)
        columns.append(jnp.concatenate([chain[0, pl.ds(at, z.rims), :], chain[1, pl.ds(at, z.rims), :], edge], axis=1))
    return jnp.concatenate(
        [jnp.concatenate(columns[n : n + TAPS], axis=1) for n in range(depth - 1)], axis=0
    )


def convolve(z, own, above, below, depth, pads, chains, weight):
    r = z.rims
    fill_pads(z, pads, own, above[(depth - 1) * r :], below[:r])
    parts = [band_operand(z, pads)]
    if depth > 1:
        for side, (rim, chain) in enumerate(zip((above, below), chains)):
            rim_at, own_at = (z.guard, z.guard + depth * r) if side == 0 else (z.guard + r, z.guard)
            for h in (0, 1):
                chain[h, pl.ds(rim_at, depth * r), :] = rim[:, 128 * h : 128 * h + 128]
                for k in (0, 1):
                    row = z.step[k] + (0 if side == 0 else z.rows[k] - 1)
                    chain[h, pl.ds(own_at + z.rim[k], z.edge[k]), :] = pads[k][1, h, pl.ds(row, z.edge[k], stride=z.rows[k]), :]
            parts.append(rim_operand(z, chain, depth))
    result = product(split(jnp.concatenate(parts, axis=0)), (weight_matrix(weight.at[0]), weight_matrix(weight.at[1])))
    n = z.total + (depth - 1) * r
    return result[: z.total], result[z.total : n], result[n:]


def image_sums(z, value):
    slot = lax.broadcasted_iota(jnp.int32, (z.slots, 1), 0)
    sums = jnp.zeros((z.slots, 128), F32)
    for k in (0, 1):
        line = value[z.start[k] : z.start[k] + z.step[k]]
        for j in range(1, z.blocks[k]):
            at = z.start[k] + j * z.step[k]
            line = line + value[at : at + z.step[k]]
        image = lax.broadcasted_iota(jnp.int32, (z.step[k], 1), 0) // z.rows[k]
        for i in range(z.images[k]):
            sums = jnp.where(slot == i + k * z.images[0], column_sum(jnp.where(image == i, line, 0.0)), sums)
    return sums


def image_rows(z, values, rims):
    parts = []
    for k in (1, 0):
        image = lax.broadcasted_iota(jnp.int32, (z.step[k], 1), 0) // z.rows[k]
        line = jnp.zeros((z.step[k], 128), F32)
        for i in range(z.images[k]):
            at = i + k * z.images[0]
            line = jnp.where(image == i, values[at : at + 1], line)
        parts += [line] * z.blocks[k]
    if rims:
        m = lax.broadcasted_iota(jnp.int32, (z.rims, 1), 0)
        image = jnp.where(m < z.rim[0], z.images[0] + m % z.images[1], (m - z.rim[0]) % z.images[0])
        line = jnp.zeros((z.rims, 128), F32)
        for at in range(sum(z.images)):
            line = jnp.where(image == at, values[at : at + 1], line)
        parts += [line] * rims
    return jnp.concatenate(parts, axis=0)


def channel_mean():
    a = lax.broadcasted_iota(jnp.int32, (LANES, 128), 0) // C
    b = lax.broadcasted_iota(jnp.int32, (LANES, 128), 1)
    return jnp.where(a == b, 1.0 / C, 0.0).astype(F32)


def to_channels():
    a = lax.broadcasted_iota(jnp.int32, (128, LANES), 0)
    b = lax.broadcasted_iota(jnp.int32, (128, LANES), 1) // C
    return jnp.where(a == b, 1.0, 0.0).astype(F32)


def attention(value):
    return spread(value * value, channel_mean())


def start_all(copies):
    for copy in copies:
        copy.start()


def wait_all(copies):
    for copy in copies:
        copy.wait()


def start_kernel(z, small, large, up_s, up_l, t_s, t_l, x, bottom, top, copies, raw, half, sems):
    loads = [pltpu.make_async_copy(a, b, sems.at[n]) for n, (a, b) in enumerate(zip((small, large, up_s, up_l, t_s, t_l), raw))]
    start_all(loads)
    r, n = z.rims, REACH * z.rims
    tail = n + 2 * r
    for ref in (bottom, top):
        ref[pl.ds(tail, z.slots), :] = jnp.zeros((z.slots, LANES), F32)
    wait_all(loads[:2])
    to_matrix(z, raw[:2], half)
    value = whole(half)
    x[...] = value
    moments(z, value, copies)
    for h in (0, 1):
        lanes = pl.ds(128 * h, 128)
        take_rims(z, half.at[h], REACH, bottom.at[pl.ds(0, n), lanes], top.at[pl.ds(0, n), lanes])
    wait_all(loads[2:])
    for k in (0, 1):
        width, rows = HEIGHTS[k], z.rows[k]
        for i in range(z.images[k]):
            slot = pl.ds(tail + i + k * z.images[0], 1)
            for d in (0, 1):
                to_bottom, to_top = n + (1 - d) * r + z.rim[k] + i, n + d * r + z.rim[k] + i
                for j in range(z.blocks[k]):
                    lanes, at = pl.ds(LANES * j, LANES), j * z.images[k]
                    if d < rows:
                        bottom[pl.ds(to_bottom + at, 1), :] = raw[2 + k][i, pl.ds(rows - 1 - d, 1), lanes]
                        top[pl.ds(to_top + at, 1), :] = raw[2 + k][i, pl.ds(d, 1), lanes]
                    else:
                        bottom[pl.ds(to_bottom + at, 1), :] = jnp.zeros((1, LANES), F32)
                        top[pl.ds(to_top + at, 1), :] = jnp.zeros((1, LANES), F32)
                if d < rows:
                    bottom[slot, pl.ds(128 * (1 - d), width)] = raw[4 + k][i, pl.ds(rows - 1 - d, 1), :]
                    top[slot, pl.ds(128 * d, width)] = raw[4 + k][i, pl.ds(d, 1), :]


def banded(taps, ref):
    row = lax.broadcasted_iota(jnp.int32, (128, 128), 0) // C
    lane = group_of(128)
    for a in range(TAPS):
        main = jnp.zeros((128, 128), F32)
        for b in range(TAPS):
            main = jnp.where(row - lane + 1 == b, taps[a][b], main)
        before = jnp.where(lane[:C] == 0, taps[a][0][:C], 0.0)
        after = jnp.where(lane[:C] == 3, taps[a][2][:C], 0.0)
        for n, part in enumerate(split(jnp.concatenate([main, before, after], axis=0))):
            ref[n, pl.ds(a * TAP_ROWS, TAP_ROWS), :] = part


def weight_matrix(ref):
    rows = []
    zeros = jnp.zeros((128 - C, 128), BF16)
    for a in range(TAPS):
        at = a * TAP_ROWS
        main = ref[pl.ds(at, 128), :]
        before = jnp.concatenate([zeros, ref[pl.ds(at + 128, C), :]], axis=0)
        after = jnp.concatenate([ref[pl.ds(at + 128 + C, C), :], zeros], axis=0)
        rows += [
            jnp.concatenate([main, before], axis=1),
            jnp.concatenate([after, main], axis=1),
            jnp.concatenate([before, after], axis=1),
        ]
    return jnp.concatenate(rows, axis=0)


def prepare_kernel(z, first, second, up_s, up_l, t_s, t_l, g1, b1, g2, b2, x, w1, w2, weights, affine, upstream, teacher, x_copy, raw, kept, kept_u, rows, half, sems):
    targets = tuple(raw) + tuple(rows.at[pl.ds(n, 1), :] for n in range(4))
    refs = (first, second, up_s, up_l, t_s, t_l, g1, b1, g2, b2)
    loads = [pltpu.make_async_copy(a, b, sems.at[n]) for n, (a, b) in enumerate(zip(refs, targets))]
    start_all(loads)
    stores = [pltpu.make_async_copy(x, x_copy, sems.at[13])]
    stores[0].start()
    wait_all(loads)
    to_matrix(z, raw[2:4], half)
    kept_u[...] = whole(half)
    stores.append(pltpu.make_async_copy(kept_u, upstream, sems.at[10]))
    stores[1].start()
    for n, (source, forward) in enumerate(zip(raw[:2], (w1, w2))):
        tiles = []
        for a in range(TAPS):
            line = [jnp.concatenate([source[a, b]] * 4, axis=1) for b in range(TAPS)]
            tiles.append([jnp.concatenate([tap] * 4, axis=0) for tap in line])
        turned = [[tiles[TAPS - 1 - a][TAPS - 1 - b].T for b in range(TAPS)] for a in range(TAPS)]
        banded(tiles, forward)
        banded(turned, kept.at[n])
        stores.append(pltpu.make_async_copy(kept.at[n], weights.at[n], sems.at[11 + n]))
        stores[-1].start()
    affine[...] = jnp.concatenate([rows[...]] * BLOCK, axis=1)
    teacher[...] = jnp.zeros(teacher.shape, F32)
    for k, ref in ((0, raw[4]), (1, raw[5])):
        for i in range(z.images[k]):
            line = ref[i]
            for j in range(z.blocks[k]):
                at = z.start[k] + j * z.step[k] + i * z.rows[k]
                teacher[pl.ds(at, z.rows[k]), pl.ds(0, BLOCK)] = line[:, j * BLOCK : (j + 1) * BLOCK]
    wait_all(stores)


def normed_by(stats):
    return lambda v: (v - stats[0:1]) * stats[1:2]


def activation(center, scale, gain, bias):
    factor = scale * gain
    offset = bias - center * factor
    return lambda v: gelu(v * factor + offset)


def first_kernel(z, x, above, below, gathered, affine, weight, hidden, h_above, h_below, stats, copies, pads, chains):
    n = REACH * z.rims
    center, scale = merged(z, gathered)
    act = activation(center, scale, affine[0:1], affine[1:2])
    own = act(x[...])
    up, down = act(above[pl.ds(0, n), :]) * inside(z, 4, True), act(below[pl.ds(0, n), :]) * inside(z, 4, False)
    own, up, down = convolve(z, own, up, down, 4, pads, chains, weight)
    moments(z, own, copies)
    hidden[...] = own
    h_above[...] = up
    h_below[...] = down
    stats[0:1] = center
    stats[1:2] = scale


def second_kernel(z, hidden, h_above, h_below, gathered, affine, weight, x, x_above, x_below, teacher, out, o_above, o_below, near, stats, copies, pads, chains):
    center, scale = merged(z, gathered)
    act = activation(center, scale, affine[2:3], affine[3:4])
    r = z.rims
    own = act(hidden[...])
    up, down = act(h_above[...]) * inside(z, 3, True), act(h_below[...]) * inside(z, 3, False)
    own, up, down = convolve(z, own, up, down, 3, pads, chains, weight)
    own = x[...] + own
    amap = attention(own)
    sums = image_sums(z, amap * amap) + pltpu.roll(image_sums(z, amap * teacher[...]), 64, 1)
    copies[...] = jnp.broadcast_to(sums[None], copies.shape)
    out[...] = own
    o_above[...] = x_above[pl.ds(2 * r, 2 * r), :] + up
    o_below[...] = x_below[pl.ds(0, 2 * r), :] + down
    near[0] = h_above[pl.ds(2 * r, r), :]
    near[1] = h_below[pl.ds(0, r), :]
    stats[0:1] = center
    stats[1:2] = scale


def tap_rows(q):
    return LANES + 3 * C if q < 0 else LANES if q == BLOCK else q * C


def tap_product(z, operand, own, above, below, pads):
    fill_center(z, pads, own)
    fill_shifted(z, pads, above, below)
    columns = []
    for a in range(TAPS):
        for h in (0, 1):
            columns.append(jnp.concatenate([pads[k][TAPS - 1 - a, h, pl.ds(z.step[k], z.count[k]), :] for k in (1, 0)], axis=0))
    return product(operand, split(jnp.concatenate(columns, axis=1)))


def tap_sums(result, tiles, first_group):
    group = group_of()
    for a in range(TAPS):
        for b in range(TAPS):
            total = None
            for h in (0, 1):
                half = None
                for p in range(4 * h, 4 * h + 4):
                    at, lane = tap_rows(p + b - 1), a * LANES + 128 * h
                    part = result[at : at + C, lane : lane + 128]
                    half = part if half is None else jnp.where(group == p % 4, part, half)
                total = half if total is None else total + half
            tile, slot = divmod(first_group + a * TAPS + b, 4)
            tiles[tile] = jnp.where(group == slot, spread_groups(total), tiles[tile])


def tap_counts(z, turned, tiles, first_group):
    group = group_of()
    m = lax.broadcasted_iota(jnp.int32, (1, z.total), 1)
    row = jnp.where(m < z.start[0], m % z.rows[1], (m - z.start[0]) % z.rows[0])
    height = jnp.where(m < z.start[0], z.rows[1], z.rows[0])
    at = lax.axis_index("row")
    lost = {
        0: (row == height - 1) & (at == z.peers - 1),
        2: (row == 0) & (at == 0),
    }
    for a in range(TAPS):
        column = jnp.sum(jnp.where(lost[a], 0.0, turned) if a in lost else turned, axis=1, keepdims=True)
        for b in range(TAPS):
            total = sum(column[tap_rows(p + b - 1) : tap_rows(p + b - 1) + C] for p in range(BLOCK))
            tile, slot = divmod(first_group + a * TAPS + b, 4)
            tiles[tile] = jnp.where(group == slot, total, tiles[tile])


def turned_operand(z, value, pads, kept):
    fill_center(z, pads, value)
    left = band_operand(z, pads, (1,)).T
    parts = split(left)
    for n in (0, 1):
        kept[n] = parts[n]
    return left


def first_operand_kernel(z, x, above, below, stats, affine, teacher, upstream, weights, left, counts, teachers, spread_u, near_u, pads, chains, kept, kept_w, kept_u, pixels, kept_t, kept_c, sems):
    r, own = z.rims, pl.ds(0, z.total)
    loads = [pltpu.make_async_copy(upstream, kept_u.at[own, :], sems.at[0]), pltpu.make_async_copy(weights.at[1], kept_w, sems.at[1])]
    start_all(loads)
    act = activation(stats[0:1], stats[1:2], affine[0:1], affine[1:2])
    value = turned_operand(z, act(x[...]), pads, kept)
    stores = [pltpu.make_async_copy(kept, left, sems.at[2])]
    stores[0].start()
    tiles = [jnp.zeros((C, 128), F32) for _ in range(3)]
    tap_counts(z, value, tiles, 0)
    counts[...] = jnp.concatenate(tiles, axis=1)
    pixels[own, :] = teacher[...]
    pixels[pl.ds(z.total, 4 * r), :] = jnp.zeros((4 * r, 128), F32)
    n = (REACH + 2) * r
    for side, ref in enumerate((above, below)):
        for d in (0, 1):
            for k in (0, 1):
                line = ref[pl.ds(n + k * z.images[0], z.images[k]), pl.ds(128 * d, 128)]
                for j in range(z.blocks[k]):
                    at = z.total + (2 * side + d) * r + z.rim[k] + j * z.images[k]
                    pixels[pl.ds(at, z.images[k]), pl.ds(0, BLOCK)] = line[:, j * BLOCK : (j + 1) * BLOCK]
    kept_t[...] = spread(pixels[...], to_channels())
    stores.append(pltpu.make_async_copy(kept_t, teachers, sems.at[3]))
    stores[1].start()
    n = REACH * r
    up, down = above[pl.ds(n, 2 * r), :] * inside(z, 2, True), below[pl.ds(n, 2 * r), :] * inside(z, 2, False)
    kept_u[pl.ds(z.total, r), :] = up[r:]
    kept_u[pl.ds(z.total + r, r), :] = down[:r]
    wait_all(loads)
    stores.append(pltpu.make_async_copy(kept_u, near_u, sems.at[5]))
    stores[2].start()
    kept_c[...] = jnp.concatenate(convolve(z, kept_u[own, :], up, down, 2, pads, chains, kept_w), axis=0)
    stores.append(pltpu.make_async_copy(kept_c, spread_u, sems.at[4]))
    stores[3].start()
    wait_all(stores)


def second_operand_kernel(z, hidden, near, stats, affine, out, o_above, o_below, first_left, counts, teachers, spread_u, weights, out_copy, left, packed, shifts, by_map, by_teacher, pads, chains, kept_left, kept_packed, kept_t, kept_u, kept_w, kept_s, sems):
    r, total = z.rims, z.total
    loads = [
        pltpu.make_async_copy(teachers, kept_t, sems.at[0]),
        pltpu.make_async_copy(weights.at[1], kept_w, sems.at[1]),
        pltpu.make_async_copy(spread_u, kept_u, sems.at[2]),
        pltpu.make_async_copy(first_left, kept_left, sems.at[3]),
    ]
    start_all(loads)
    stores = [pltpu.make_async_copy(out, out_copy, sems.at[4])]
    stores[0].start()
    normed = normed_by(stats)(jnp.concatenate([hidden[...], near[0], near[1]], axis=0))
    shifted = normed * affine[2:3] + affine[3:4]
    turned_operand(z, gelu(shifted[:total]), pads, left)
    ones = jnp.ones((total, 1), F32)
    masks = jnp.concatenate([ones, inside(z, 1, True), inside(z, 1, False)], axis=0)
    slopes = gelu_slope(shifted) * masks
    o = jnp.concatenate([out[...], o_above[...] * inside(z, 2, True), o_below[...] * inside(z, 2, False)], axis=0)
    for_map = spread(attention(o), to_channels()) * o
    wait_all(loads[:3])
    for_teacher = kept_t[...] * o
    kept_s[0] = kept_u[...] * slopes
    for n, value, ref in ((1, for_map, by_map), (2, for_teacher, by_teacher)):
        own, up, down = value[:total], value[total : total + 2 * r], value[total + 2 * r :]
        ref[...] = jnp.concatenate([own, up[r:], down[:r]], axis=0)
        kept_s[n] = jnp.concatenate(convolve(z, own, up, down, 2, pads, chains, kept_w), axis=0) * slopes
    stores.append(pltpu.make_async_copy(kept_s, shifts, sems.at[5]))
    stores[1].start()
    loads[3].wait()
    normed = normed * masks
    result = tap_product(z, (kept_left[0], kept_left[1]), normed[:total], normed[total : total + r], normed[total + r :], pads)
    tiles = [jnp.zeros((C, 128), F32) for _ in range(BACK_LANES // 128)]
    tap_sums(result, tiles, NORMED)
    group = group_of()
    for n in range(TAPS * TAPS):
        tile, slot = divmod(ONES + n, 4)
        line = spread_groups(jnp.where(group == n % 4, counts[:, 128 * (n // 4) : 128 * (n // 4) + 128], 0.0))
        tiles[tile] = jnp.where(group == slot, line, tiles[tile])
    kept_packed[...] = jnp.concatenate(tiles, axis=1)
    stores.append(pltpu.make_async_copy(kept_packed, packed, sems.at[6]))
    stores[2].start()
    wait_all(stores)


def upstream_kernel(z, gathered, near_u, shifts, left_1, left_2, packed, by_map, by_teacher, hidden, stats, dout, dshift, d_above, d_below, slabs, kept_u, kept_s, kept_left, kept_packed, pads, sems):
    r, total = z.rims, z.total
    loads = [
        pltpu.make_async_copy(a, b, sems.at[n])
        for n, (a, b) in enumerate(((near_u, kept_u), (shifts, kept_s), (left_1, kept_left), (packed, kept_packed)))
    ]
    start_all(loads)
    lane = lax.broadcasted_iota(jnp.int32, (z.slots, 128), 1)
    sums = jnp.sum(gathered[...], axis=0)
    square = jnp.sum(jnp.where(lane < 64, sums, 0.0), axis=1, keepdims=True)
    cross = jnp.sum(jnp.where(lane < 64, 0.0, sums), axis=1, keepdims=True)
    inverse = lax.rsqrt(square + map_eps)
    inner = beta_weight * (square * inverse - cross) * inverse
    shape = (z.slots, 128)
    for_map = (beta_weight - inner) * inverse * inverse * (2.0 / C)
    for_teacher = beta_weight * inverse * (2.0 / C)
    for_map, for_teacher = (wide(image_rows(z, jnp.broadcast_to(v, shape), 2)) for v in (for_map, for_teacher))
    loads[0].wait()
    value = kept_u[...] + for_map * by_map[...] - for_teacher * by_teacher[...]
    dout[...] = value[:total]
    second = tap_product(z, (left_2[0], left_2[1]), value[:total], value[total : total + r], value[total + r :], pads)
    loads[1].wait()
    shift = kept_s[0] + for_map * kept_s[1] - for_teacher * kept_s[2]
    pre, above, below = shift[:total], shift[total : total + r], shift[total + r :]
    dshift[...] = pre
    d_above[...] = above
    d_below[...] = below
    normed = normed_by(stats)(hidden[...])
    wait_all(loads[2:])
    first = tap_product(z, (kept_left[0], kept_left[1]), pre, above, below, pads)
    tiles = [kept_packed[:, 128 * n : 128 * n + 128] for n in range(BACK_LANES // 128)]
    group = group_of()
    tiles[0] = jnp.where(group == BIAS, fold(column_sum(pre)), jnp.where(group == GAIN, fold(column_sum(pre * normed)), tiles[0]))
    tap_sums(second, tiles, SECOND)
    tap_sums(first, tiles, LEFT)
    line = jnp.concatenate(tiles, axis=1)
    for d in range(z.devices):
        slabs[d] = line[d % C : d % C + 1]


def write_kernel(z, out, x, weights, stats, order, out_s, out_l, normed, weight, kept, kept_x, half, sems):
    loads = [pltpu.make_async_copy(a, b, sems.at[n]) for n, (a, b) in enumerate(((out, kept), (x, kept_x), (weights.at[0], weight)))]
    start_all(loads)
    loads[0].wait()
    put_halves(half, kept[...])
    from_matrix(z, half, (out_s, out_l))
    loads[1].wait()
    normed[...] = normed_by(stats)(kept_x[...])
    loads[2].wait()


def norm_sums(total):
    group = group_of()
    return [wide(spread_groups(jnp.where(group == n, total[:, :128], 0.0))) for n in (BIAS, GAIN)]


def hidden_kernel(z, gathered, dshift, d_above, d_below, hidden, near, stats, affine, weight, first_normed, pre_ref, gain_out, bias_out, slabs, pads):
    total = jnp.sum(gathered[...], axis=0)
    bias_sum, gain_sum = norm_sums(total)
    bias_out[...] = bias_sum[:, :C]
    gain_out[...] = gain_sum[:, :C]
    bias_mean, gain_mean = bias_sum / z.pixels, gain_sum / z.pixels
    unit = normed_by(stats)
    factor = affine[2:3] * stats[1:2]

    def back(d, h):
        return factor * (d - bias_mean - unit(h) * gain_mean)

    own = back(dshift[...], hidden[...])
    up = back(d_above[...], near[0]) * inside(z, 1, True)
    down = back(d_below[...], near[1]) * inside(z, 1, False)
    grad, _, _ = convolve(z, own, up, down, 1, pads, None, weight)
    normed = first_normed[...]
    pre = grad * gelu_slope(normed * affine[0:1] + affine[1:2])
    pre_ref[...] = pre
    lane = lax.broadcasted_iota(jnp.int32, (1, 128), 1)
    taps = TAPS * TAPS * C

    def along(row):
        return jnp.concatenate([row[:, :128]] * 3, axis=1)[:, :taps]

    second, left, against, ones = (total[:, n * C : n * C + taps] for n in (SECOND, LEFT, NORMED, ONES))
    first = along(factor) * (left - along(bias_mean) * ones - along(gain_mean) * against)
    sums = jnp.where(lane < C, fold(column_sum(pre)), fold(column_sum(pre * normed)))
    line = jnp.concatenate([sums[:, : 2 * C], second, first], axis=1)
    slabs[...] = jnp.broadcast_to(line[None], slabs.shape)


def back_kernel(z, gathered, pre, normed, stats, affine, dout, back_s, back_l, one, two, gain_out, bias_out, half, lines):
    bias_sum, gain_sum = norm_sums(jnp.sum(gathered[:, :, pl.ds(0, 128)], axis=0))
    bias_out[...] = bias_sum[:, :C]
    gain_out[...] = gain_sum[:, :C]
    value = dout[...] + affine[0:1] * stats[1:2] * (pre[...] - bias_sum / z.pixels - normed[...] * (gain_sum / z.pixels))
    put_halves(half, value)
    from_matrix(z, half, (back_s, back_l))
    for d in range(C):
        lines[pl.ds(d, 1), :] = gathered[d]
    for ref, group in ((two, LAST_SECOND), (one, LAST_FIRST)):
        for a in range(TAPS):
            for b in range(TAPS):
                at = (group + a * TAPS + b) * C
                ref[a, b] = lines[:, pl.ds(at, C)]


def call(body, ins, outs, scratch=(), sems=0):
    space = {"v": pltpu.VMEM, "h": pltpu.HBM}
    shapes = []
    for item in scratch:
        if isinstance(item, list):
            shapes.append([pltpu.VMEM(*s) for s in item])
        else:
            shapes.append(pltpu.VMEM(*item))
    if sems:
        shapes.append(pltpu.SemaphoreType.DMA((sems,)))
    run = pl.pallas_call(
        body,
        out_shape=[pltpu.HBM(shape, kind) if s == "h" else jax.ShapeDtypeStruct(shape, kind) for s, shape, kind in outs],
        in_specs=[pl.BlockSpec(memory_space=space[s]) for s in ins],
        out_specs=[pl.BlockSpec(memory_space=space[s]) for s, _, _ in outs],
        scratch_shapes=shapes,
        compiler_params=pltpu.CompilerParams(vmem_limit_bytes=VMEM_LIMIT),
    )
    return lambda *args: run(
        *(pltpu.with_memory_space_constraint(arg, pltpu.HBM) if s == "h" else arg for s, arg in zip(ins, args))
    )


def exchange(copies, axes):
    return lax.all_to_all(copies, axes, 0, 0, tiled=True)


def beyond(z, bottom, top, depths):
    hops = max(-(-depth // rows) for rows in z.rows for depth in depths)
    above, below = [], []
    for hop in range(1, hops + 1):
        above.append(lax.ppermute(bottom, "row", [(i, i + hop) for i in range(z.peers - hop)]))
        below.append(lax.ppermute(top, "row", [(i + hop, i) for i in range(z.peers - hop)]))
    if hops == 1:
        return above[0], below[0]
    up, down = [], []
    base = 0
    for depth in depths:
        for n in range(depth):
            for k in (1, 0):
                hop, back = divmod(depth - 1 - n, z.rows[k])
                at = base + (depth - 1 - back) * z.rims + z.rim[k]
                up.append(above[hop][at : at + z.edge[k]])
                hop, back = divmod(n, z.rows[k])
                at = base + back * z.rims + z.rim[k]
                down.append(below[hop][at : at + z.edge[k]])
        base += depth * z.rims
    up.append(jnp.concatenate([pixel_rows(z, above, base, 1, 1), pixel_rows(z, above, base, 0, 1)], axis=1))
    down.append(jnp.concatenate([pixel_rows(z, below, base, 0, 0), pixel_rows(z, below, base, 1, 0)], axis=1))
    return jnp.concatenate(up, axis=0), jnp.concatenate(down, axis=0)


def pixel_rows(z, bands, base, distance, last):
    lines = []
    for k in (0, 1):
        hop, back = divmod(distance, z.rows[k])
        at = base + k * z.images[0]
        half = 128 * abs(last - back)
        lines.append(bands[hop][at : at + z.images[k], half : half + 128])
    lines.append(jnp.zeros((z.slots - sum(z.images), 128), F32))
    return jnp.concatenate(lines, axis=0)


def local(
    image_small, image_large, teacher_small, teacher_large, upstream_small, upstream_large,
    conv_first, gain_first, bias_first, conv_second, gain_second, bias_second,
):
    peers = lax.axis_size("row")
    devices = lax.axis_size("img") * peers
    z = Sizes(image_small.shape, image_large.shape, devices, peers)
    body = lambda function: functools.partial(function, z)
    r = z.rims
    full, half, pair = (z.total, LANES), (2, z.total, 128), (devices, 2, 128)
    weight, left = (2, TAPS * TAP_ROWS, 128), (2, WIDTH, z.total)
    images = [image_small, image_large, upstream_small, upstream_large, teacher_small, teacher_large]
    f = lambda space, *shape: (space, shape, F32)
    depths = (REACH, 2)
    rim_rows = sum(depths) * r + z.slots

    x, bottom, top, copies = call(
        body(start_kernel),
        "hhhhhh",
        [("v", full, F32), f("v", rim_rows, LANES), f("v", rim_rows, LANES), ("v", pair, F32)],
        [[(a.shape, F32) for a in images], (half, F32)],
        6,
    )(*images)
    gathered = exchange(copies, AXES)
    above, below = beyond(z, bottom, top, depths)
    params = [conv_first, conv_second] + images[2:]
    w1, w2, weights, affine, upstream, teacher, x_copy = call(
        body(prepare_kernel),
        "hhhhhhhhhhv",
        [("v", weight, BF16), ("v", weight, BF16), ("h", (2,) + weight, BF16), f("v", 4, LANES), ("h", full, F32), f("v", z.total, 128), ("h", full, F32)],
        [[(a.shape, F32) for a in params], ((2,) + weight, BF16), (full, F32), ((4, C), F32), (half, F32)],
        14,
    )(*params, *(v.reshape(1, C) for v in (gain_first, bias_first, gain_second, bias_second)), x)

    hidden, h_above, h_below, stats_one, copies = call(
        body(first_kernel),
        "vvvvvv",
        [("v", full, F32), f("v", 3 * r, LANES), f("v", 3 * r, LANES), f("v", 2, LANES), ("v", pair, F32)],
        [z.pads(), z.chains(4)],
    )(x, above, below, gathered, affine, w1)
    gathered = exchange(copies, AXES)
    extended, near_rows = z.total + 4 * r, z.total + 2 * r
    left_one, counts, teachers, spread_u, near_u = call(
        body(first_operand_kernel),
        "vvvvvvhh",
        [("h", left, BF16), f("v", C, 384), f("h", extended, LANES), f("h", near_rows, LANES), f("h", near_rows, LANES)],
        [
            z.pads(), z.chains(2), (left, BF16), (weight, BF16), ((near_rows, LANES), F32), ((extended, 128), F32),
            ((extended, LANES), F32), ((near_rows, LANES), F32),
        ],
        6,
    )(x, above, below, stats_one, affine, teacher, upstream, weights)
    gathered, counts = lax.optimization_barrier((gathered, counts))

    map_shape = (peers, z.slots, 128)
    out, o_above, o_below, near, stats_two, copies = call(
        body(second_kernel),
        "vvvvvvvvvv",
        [("v", full, F32), f("v", 2 * r, LANES), f("v", 2 * r, LANES), f("v", 2, r, LANES), f("v", 2, LANES), ("v", map_shape, F32)],
        [z.pads(), z.chains(3)],
    )(hidden, h_above, h_below, gathered, affine, w2, x, above, below, teacher)
    gathered = exchange(copies, ("row",))
    out_copy, left_two, packed, shifts, by_map, by_teacher = call(
        body(second_operand_kernel),
        "vvvvvvvhvhhh",
        [
            ("h", full, F32), ("v", left, BF16), f("h", C, BACK_LANES), f("h", 3, near_rows, LANES),
            f("v", near_rows, LANES), f("v", near_rows, LANES),
        ],
        [
            z.pads(), z.chains(2), (left, BF16), ((C, BACK_LANES), F32), ((extended, LANES), F32), ((near_rows, LANES), F32),
            (weight, BF16), ((3, near_rows, LANES), F32),
        ],
        7,
    )(hidden, near, stats_two, affine, out, o_above, o_below, left_one, counts, teachers, spread_u, weights)

    dout, dshift, d_above, d_below, slabs = call(
        body(upstream_kernel),
        "vhhhvhvvvv",
        [("v", full, F32), ("v", full, F32), f("v", r, LANES), f("v", r, LANES), f("v", devices, 1, BACK_LANES)],
        [((near_rows, LANES), F32), ((3, near_rows, LANES), F32), (left, BF16), ((C, BACK_LANES), F32), z.pads()],
        4,
    )(gathered, near_u, shifts, left_one, left_two, packed, by_map, by_teacher, hidden, stats_two)
    gathered = exchange(slabs, AXES)
    out_s, out_l, first_normed, weight_back = call(
        body(write_kernel),
        "hhhvv",
        [("v", image_small.shape, F32), ("v", image_large.shape, F32), ("v", full, F32), ("v", weight, BF16)],
        [(full, F32), (full, F32), (half, F32)],
        3,
    )(out_copy, x_copy, weights, stats_one, d_above)

    pre, gain_two, bias_two, slabs = call(
        body(hidden_kernel),
        "vvvvvvvvvv",
        [("v", full, F32), f("v", 1, C), f("v", 1, C), f("v", devices, 1, LAST_LANES)],
        [z.pads()],
    )(gathered, dshift, d_above, d_below, hidden, near, stats_two, affine, weight_back, first_normed)
    gathered = exchange(slabs, AXES)

    back_s, back_l, one, two, gain_one, bias_one = call(
        body(back_kernel),
        "vvvvvv",
        [("v", a.shape, F32) for a in (image_small, image_large, conv_first, conv_second)] + [f("v", 1, C), f("v", 1, C)],
        [(half, F32), ((C, LAST_LANES), F32)],
    )(gathered, pre, first_normed, stats_one, affine, dout)
    return (
        out_s, out_l, back_s, back_l,
        one, gain_one.reshape(C), bias_one.reshape(C),
        two, gain_two.reshape(C), bias_two.reshape(C),
    )


def solution(mesh):
    split_bands, everywhere = P("img", "row", None), P()
    return jax.shard_map(
        local,
        mesh=mesh,
        in_specs=(split_bands,) * 6 + (everywhere,) * 6,
        out_specs=(split_bands,) * 4 + (everywhere,) * 6,
        check_vma=False,
    )
```

```python
import functools
import math

import jax
import jax.numpy as jnp
from jax import lax
from jax.experimental import pallas as pl
from jax.experimental.pallas import tpu as pltpu
from jax.sharding import PartitionSpec as P

C = 32
HS = 32
HL = 64
HEIGHTS = (HS, HL)

norm_eps = 1e-05
map_eps = 1e-06
beta_weight = 1000.0
AXES = ("img", "row")
BLOCK = 8
LANES = BLOCK * C
TAPS = 3
WIDTH = LANES + 128
DEPTH = TAPS * WIDTH
TAP_ROWS = 128 + 2 * C
REACH = 4
ROOT = math.sqrt(2.0 / math.pi)
CUBE = 0.044715
F32 = jnp.float32
BF16 = jnp.bfloat16
VMEM_LIMIT = 32 * 1024 * 1024
BIAS, GAIN, SECOND, LEFT, NORMED, ONES = 0, 1, 2, 11, 20, 29
BACK_LANES = 1280
LAST_SECOND, LAST_FIRST, LAST_LANES = 2, 11, 640


class Sizes:
    def __init__(self, small, large, devices, peers):
        self.images = (small[0], large[0])
        self.rows = (small[1], large[1])
        self.blocks = (HS // BLOCK, HL // BLOCK)
        self.step = tuple(n * r for n, r in zip(self.images, self.rows))
        self.count = tuple(b * s for b, s in zip(self.blocks, self.step))
        self.edge = tuple(b * n for b, n in zip(self.blocks, self.images))
        self.start = (self.count[1], 0)
        self.rim = (self.edge[1], 0)
        self.total = sum(self.count)
        self.rims = sum(self.edge)
        self.slots = -(-sum(self.images) // 8) * 8
        self.guard = -(-max(self.images) // 8) * 8
        self.devices = devices
        self.peers = peers
        self.here = float(self.total * BLOCK)
        self.pixels = self.here * devices

    def pads(self):
        return [((TAPS, 2, self.count[k] + 2 * self.step[k], 128), F32) for k in (0, 1)]

    def chains(self, depth):
        return [((2, 2 * self.guard + (depth + 1) * self.rims, 128), F32)] * 2


def split(value):
    high = value.astype(BF16)
    return high, (value - high.astype(F32)).astype(BF16)


def dot(left, right):
    return lax.dot_general(left, right, (((1,), (0,)), ((), ())), preferred_element_type=F32)


def product(left, right):
    if left[0].shape[1] % 128:
        return dot(left[0], right[0]) + (dot(left[0], right[1]) + dot(left[1], right[0]))
    return dot(
        jnp.concatenate([left[0], left[0], left[1]], axis=1), jnp.concatenate([right[0], right[1], right[0]], axis=0)
    )


def spread(left, right):
    right = right.astype(BF16)
    return dot(jnp.concatenate(split(left), axis=1), jnp.concatenate([right, right], axis=0))


def gelu(s):
    return 0.5 * s * (1.0 + jnp.tanh(ROOT * (s + CUBE * s * s * s)))


def gelu_slope(s):
    square = s * s
    t = jnp.tanh(ROOT * s * (1.0 + CUBE * square))
    return 0.5 * (1.0 + t) + 0.5 * s * (1.0 - t * t) * ROOT * (1.0 + 3.0 * CUBE * square)


def spread_groups(row):
    row = row + pltpu.roll(row, 64, 1)
    return row + pltpu.roll(row, 32, 1)


def fold(row):
    return spread_groups(row[:, :128] + row[:, 128:])


def wide(row):
    return jnp.concatenate([row, row], axis=1)


def group_of(rows=1, lanes=128):
    return lax.broadcasted_iota(jnp.int32, (rows, lanes), 1) // C


def column_sum(value):
    return jnp.sum(value, axis=0, keepdims=True)


def moments(z, value, ref):
    center = fold(column_sum(value)) / z.here
    off = value - wide(center)
    both = jnp.concatenate([center, fold(column_sum(off * off))], axis=0)
    ref[...] = jnp.broadcast_to(both[None], ref.shape)


def merged(z, ref):
    gathered = ref[...]
    mean = jnp.mean(gathered, axis=0)
    center = mean[0:1]
    off = gathered[:, 0, :] - center
    variance = mean[1:2] / z.here + jnp.mean(off * off, axis=0, keepdims=True)
    return wide(center), wide(lax.rsqrt(variance + norm_eps))


def put_halves(ref, value):
    ref[0] = value[:, :128]
    ref[1] = value[:, 128:]


def whole(ref):
    return jnp.concatenate([ref[0], ref[1]], axis=1)


def to_matrix(z, refs, half):
    for k in (0, 1):
        for j in range(z.blocks[k]):
            at = z.start[k] + j * z.step[k]
            for i in range(z.images[k]):
                for h in (0, 1):
                    half[h, pl.ds(at + i * z.rows[k], z.rows[k]), :] = refs[k][i, :, pl.ds(LANES * j + 128 * h, 128)]


def from_matrix(z, half, refs):
    for k in (0, 1):
        for j in range(z.blocks[k]):
            at = z.start[k] + j * z.step[k]
            for i in range(z.images[k]):
                for h in (0, 1):
                    refs[k][i, :, pl.ds(LANES * j + 128 * h, 128)] = half[h, pl.ds(at + i * z.rows[k], z.rows[k]), :]


def take_rims(z, half, depth, bottom, top):
    for k in (0, 1):
        for d in range(1, depth + 1):
            to_bottom = pl.ds((depth - d) * z.rims + z.rim[k], z.edge[k])
            to_top = pl.ds((d - 1) * z.rims + z.rim[k], z.edge[k])
            if d <= z.rows[k]:
                bottom[to_bottom, :] = half[pl.ds(z.start[k] + z.rows[k] - d, z.edge[k], stride=z.rows[k]), :]
                top[to_top, :] = half[pl.ds(z.start[k] + d - 1, z.edge[k], stride=z.rows[k]), :]
            else:
                bottom[to_bottom, :] = jnp.zeros((z.edge[k], 128), F32)
                top[to_top, :] = jnp.zeros((z.edge[k], 128), F32)


def inside(z, depth, above):
    at = lax.axis_index("row")
    large = lax.broadcasted_iota(jnp.int32, (z.rims, 1), 0) < z.rim[0]
    parts = []
    for n in range(depth):
        if above:
            ok = [jnp.where(at * rows >= depth - n, 1.0, 0.0) for rows in z.rows]
        else:
            ok = [jnp.where((at + 1) * rows + n + 1 <= height, 1.0, 0.0) for rows, height in zip(z.rows, HEIGHTS)]
        parts.append(jnp.where(large, ok[1], ok[0]).astype(F32))
    return jnp.concatenate(parts, axis=0)


def fill_center(z, pads, value):
    for k in (0, 1):
        ref, step, count = pads[k], z.step[k], z.count[k]
        for h in (0, 1):
            ref[1, h, pl.ds(0, step), :] = jnp.zeros((step, 128), F32)
            ref[1, h, pl.ds(step, count), :] = value[z.start[k] : z.start[k] + count, 128 * h : 128 * h + 128]
            ref[1, h, pl.ds(step + count, step), :] = jnp.zeros((step, 128), F32)


def fill_shifted(z, pads, above, below):
    for k in (0, 1):
        ref, step, count, rows = pads[k], z.step[k], z.count[k], z.rows[k]
        rim = slice(z.rim[k], z.rim[k] + z.edge[k])
        for h in (0, 1):
            lanes = slice(128 * h, 128 * h + 128)
            ref[0, h, pl.ds(step, count), :] = ref[1, h, pl.ds(step - 1, count), :]
            ref[2, h, pl.ds(step, count), :] = ref[1, h, pl.ds(step + 1, count), :]
            ref[0, h, pl.ds(step, z.edge[k], stride=rows), :] = above[rim, lanes]
            ref[2, h, pl.ds(step + rows - 1, z.edge[k], stride=rows), :] = below[rim, lanes]


def fill_pads(z, pads, value, above, below):
    fill_center(z, pads, value)
    fill_shifted(z, pads, above, below)
    for k in (0, 1):
        ref, step, count = pads[k], z.step[k], z.count[k]
        for h in (0, 1):
            for a in (0, 2):
                ref[a, h, pl.ds(0, step), :] = jnp.zeros((step, 128), F32)
                ref[a, h, pl.ds(step + count, step), :] = jnp.zeros((step, 128), F32)


def band_operand(z, pads, taps=range(TAPS)):
    lane = lax.broadcasted_iota(jnp.int32, (1, 128), 1)
    parts = []
    for k in (1, 0):
        ref, step, count = pads[k], z.step[k], z.count[k]
        columns = []
        for a in taps:
            before = ref[a, 1, pl.ds(0, count), :]
            after = ref[a, 0, pl.ds(2 * step, count), :]
            columns += [
                ref[a, 0, pl.ds(step, count), :],
                ref[a, 1, pl.ds(step, count), :],
                jnp.where(lane >= 96, before, jnp.where(lane < 32, after, 0.0)),
            ]
        parts.append(jnp.concatenate(columns, axis=1))
    return jnp.concatenate(parts, axis=0)


def rim_operand(z, chain, depth):
    rows, g = (depth + 1) * z.rims, z.guard
    lane = lax.broadcasted_iota(jnp.int32, (1, 128), 1)
    m = lax.broadcasted_iota(jnp.int32, (z.rims, 1), 0)
    large = m < z.rim[0]
    has_before = jnp.where(large, m, m - z.rim[0]) >= jnp.where(large, z.images[1], z.images[0])
    has_after = m < jnp.where(large, z.rim[0] - z.images[1], z.rims - z.images[0])
    take = [(lane >= 96) & has_before & large, (lane >= 96) & has_before & ~large, (lane < 32) & has_after & large, (lane < 32) & has_after & ~large]
    columns = []
    for r in range(depth + 1):
        at = g + r * z.rims
        edge = jnp.zeros((z.rims, 128), F32)
        for mask, half, shift in zip(take, (1, 1, 0, 0), (-z.images[1], -z.images[0], z.images[1], z.images[0])):
            edge = jnp.where(mask, chain[half, pl.ds(at + shift, z.rims), :], edge)
        columns.append(jnp.concatenate([chain[0, pl.ds(at, z.rims), :], chain[1, pl.ds(at, z.rims), :], edge], axis=1))
    return jnp.concatenate(
        [jnp.concatenate(columns[n : n + TAPS], axis=1) for n in range(depth - 1)], axis=0
    )


def convolve(z, own, above, below, depth, pads, chains, weight):
    r = z.rims
    fill_pads(z, pads, own, above[(depth - 1) * r :], below[:r])
    parts = [band_operand(z, pads)]
    if depth > 1:
        for side, (rim, chain) in enumerate(zip((above, below), chains)):
            rim_at, own_at = (z.guard, z.guard + depth * r) if side == 0 else (z.guard + r, z.guard)
            for h in (0, 1):
                chain[h, pl.ds(rim_at, depth * r), :] = rim[:, 128 * h : 128 * h + 128]
                for k in (0, 1):
                    row = z.step[k] + (0 if side == 0 else z.rows[k] - 1)
                    chain[h, pl.ds(own_at + z.rim[k], z.edge[k]), :] = pads[k][1, h, pl.ds(row, z.edge[k], stride=z.rows[k]), :]
            parts.append(rim_operand(z, chain, depth))
    result = product(split(jnp.concatenate(parts, axis=0)), (weight_matrix(weight.at[0]), weight_matrix(weight.at[1])))
    n = z.total + (depth - 1) * r
    return result[: z.total], result[z.total : n], result[n:]


def image_sums(z, value):
    slot = lax.broadcasted_iota(jnp.int32, (z.slots, 1), 0)
    sums = jnp.zeros((z.slots, 128), F32)
    for k in (0, 1):
        line = value[z.start[k] : z.start[k] + z.step[k]]
        for j in range(1, z.blocks[k]):
            at = z.start[k] + j * z.step[k]
            line = line + value[at : at + z.step[k]]
        image = lax.broadcasted_iota(jnp.int32, (z.step[k], 1), 0) // z.rows[k]
        for i in range(z.images[k]):
            sums = jnp.where(slot == i + k * z.images[0], column_sum(jnp.where(image == i, line, 0.0)), sums)
    return sums


def image_rows(z, values, rims):
    parts = []
    for k in (1, 0):
        image = lax.broadcasted_iota(jnp.int32, (z.step[k], 1), 0) // z.rows[k]
        line = jnp.zeros((z.step[k], 128), F32)
        for i in range(z.images[k]):
            at = i + k * z.images[0]
            line = jnp.where(image == i, values[at : at + 1], line)
        parts += [line] * z.blocks[k]
    if rims:
        m = lax.broadcasted_iota(jnp.int32, (z.rims, 1), 0)
        image = jnp.where(m < z.rim[0], z.images[0] + m % z.images[1], (m - z.rim[0]) % z.images[0])
        line = jnp.zeros((z.rims, 128), F32)
        for at in range(sum(z.images)):
            line = jnp.where(image == at, values[at : at + 1], line)
        parts += [line] * rims
    return jnp.concatenate(parts, axis=0)


def channel_mean():
    a = lax.broadcasted_iota(jnp.int32, (LANES, 128), 0) // C
    b = lax.broadcasted_iota(jnp.int32, (LANES, 128), 1)
    return jnp.where(a == b, 1.0 / C, 0.0).astype(F32)


def to_channels():
    a = lax.broadcasted_iota(jnp.int32, (128, LANES), 0)
    b = lax.broadcasted_iota(jnp.int32, (128, LANES), 1) // C
    return jnp.where(a == b, 1.0, 0.0).astype(F32)


def attention(value):
    return spread(value * value, channel_mean())


def start_all(copies):
    for copy in copies:
        copy.start()


def wait_all(copies):
    for copy in copies:
        copy.wait()


def start_kernel(z, small, large, up_s, up_l, t_s, t_l, x, bottom, top, copies, raw, half, sems):
    loads = [pltpu.make_async_copy(a, b, sems.at[n]) for n, (a, b) in enumerate(zip((small, large, up_s, up_l, t_s, t_l), raw))]
    start_all(loads)
    r, n = z.rims, REACH * z.rims
    tail = n + 2 * r
    for ref in (bottom, top):
        ref[pl.ds(tail, z.slots), :] = jnp.zeros((z.slots, LANES), F32)
    wait_all(loads[:2])
    to_matrix(z, raw[:2], half)
    value = whole(half)
    x[...] = value
    moments(z, value, copies)
    for h in (0, 1):
        lanes = pl.ds(128 * h, 128)
        take_rims(z, half.at[h], REACH, bottom.at[pl.ds(0, n), lanes], top.at[pl.ds(0, n), lanes])
    wait_all(loads[2:])
    for k in (0, 1):
        width, rows = HEIGHTS[k], z.rows[k]
        for i in range(z.images[k]):
            slot = pl.ds(tail + i + k * z.images[0], 1)
            for d in (0, 1):
                to_bottom, to_top = n + (1 - d) * r + z.rim[k] + i, n + d * r + z.rim[k] + i
                for j in range(z.blocks[k]):
                    lanes, at = pl.ds(LANES * j, LANES), j * z.images[k]
                    if d < rows:
                        bottom[pl.ds(to_bottom + at, 1), :] = raw[2 + k][i, pl.ds(rows - 1 - d, 1), lanes]
                        top[pl.ds(to_top + at, 1), :] = raw[2 + k][i, pl.ds(d, 1), lanes]
                    else:
                        bottom[pl.ds(to_bottom + at, 1), :] = jnp.zeros((1, LANES), F32)
                        top[pl.ds(to_top + at, 1), :] = jnp.zeros((1, LANES), F32)
                if d < rows:
                    bottom[slot, pl.ds(128 * (1 - d), width)] = raw[4 + k][i, pl.ds(rows - 1 - d, 1), :]
                    top[slot, pl.ds(128 * d, width)] = raw[4 + k][i, pl.ds(d, 1), :]


def banded(taps, ref):
    row = lax.broadcasted_iota(jnp.int32, (128, 128), 0) // C
    lane = group_of(128)
    for a in range(TAPS):
        main = jnp.zeros((128, 128), F32)
        for b in range(TAPS):
            main = jnp.where(row - lane + 1 == b, taps[a][b], main)
        before = jnp.where(lane[:C] == 0, taps[a][0][:C], 0.0)
        after = jnp.where(lane[:C] == 3, taps[a][2][:C], 0.0)
        for n, part in enumerate(split(jnp.concatenate([main, before, after], axis=0))):
            ref[n, pl.ds(a * TAP_ROWS, TAP_ROWS), :] = part


def weight_matrix(ref):
    rows = []
    zeros = jnp.zeros((128 - C, 128), BF16)
    for a in range(TAPS):
        at = a * TAP_ROWS
        main = ref[pl.ds(at, 128), :]
        before = jnp.concatenate([zeros, ref[pl.ds(at + 128, C), :]], axis=0)
        after = jnp.concatenate([ref[pl.ds(at + 128 + C, C), :], zeros], axis=0)
        rows += [
            jnp.concatenate([main, before], axis=1),
            jnp.concatenate([after, main], axis=1),
            jnp.concatenate([before, after], axis=1),
        ]
    return jnp.concatenate(rows, axis=0)


def prepare_kernel(z, first, second, up_s, up_l, t_s, t_l, g1, b1, g2, b2, x, w1, w2, weights, affine, upstream, teacher, x_copy, raw, kept, kept_u, rows, half, sems):
    targets = tuple(raw) + tuple(rows.at[pl.ds(n, 1), :] for n in range(4))
    refs = (first, second, up_s, up_l, t_s, t_l, g1, b1, g2, b2)
    loads = [pltpu.make_async_copy(a, b, sems.at[n]) for n, (a, b) in enumerate(zip(refs, targets))]
    start_all(loads)
    stores = [pltpu.make_async_copy(x, x_copy, sems.at[13])]
    stores[0].start()
    wait_all(loads)
    to_matrix(z, raw[2:4], half)
    kept_u[...] = whole(half)
    stores.append(pltpu.make_async_copy(kept_u, upstream, sems.at[10]))
    stores[1].start()
    for n, (source, forward) in enumerate(zip(raw[:2], (w1, w2))):
        tiles = []
        for a in range(TAPS):
            line = [jnp.concatenate([source[a, b]] * 4, axis=1) for b in range(TAPS)]
            tiles.append([jnp.concatenate([tap] * 4, axis=0) for tap in line])
        turned = [[tiles[TAPS - 1 - a][TAPS - 1 - b].T for b in range(TAPS)] for a in range(TAPS)]
        banded(tiles, forward)
        banded(turned, kept.at[n])
        stores.append(pltpu.make_async_copy(kept.at[n], weights.at[n], sems.at[11 + n]))
        stores[-1].start()
    affine[...] = jnp.concatenate([rows[...]] * BLOCK, axis=1)
    teacher[...] = jnp.zeros(teacher.shape, F32)
    for k, ref in ((0, raw[4]), (1, raw[5])):
        for i in range(z.images[k]):
            line = ref[i]
            for j in range(z.blocks[k]):
                at = z.start[k] + j * z.step[k] + i * z.rows[k]
                teacher[pl.ds(at, z.rows[k]), pl.ds(0, BLOCK)] = line[:, j * BLOCK : (j + 1) * BLOCK]
    wait_all(stores)


def normed_by(stats):
    return lambda v: (v - stats[0:1]) * stats[1:2]


def activation(center, scale, gain, bias):
    factor = scale * gain
    offset = bias - center * factor
    return lambda v: gelu(v * factor + offset)


def first_kernel(z, x, above, below, gathered, affine, weight, hidden, h_above, h_below, stats, copies, pads, chains):
    n = REACH * z.rims
    center, scale = merged(z, gathered)
    act = activation(center, scale, affine[0:1], affine[1:2])
    own = act(x[...])
    up, down = act(above[pl.ds(0, n), :]) * inside(z, 4, True), act(below[pl.ds(0, n), :]) * inside(z, 4, False)
    own, up, down = convolve(z, own, up, down, 4, pads, chains, weight)
    moments(z, own, copies)
    hidden[...] = own
    h_above[...] = up
    h_below[...] = down
    stats[0:1] = center
    stats[1:2] = scale


def second_kernel(z, hidden, h_above, h_below, gathered, affine, weight, x, x_above, x_below, teacher, out, o_above, o_below, near, stats, copies, pads, chains):
    center, scale = merged(z, gathered)
    act = activation(center, scale, affine[2:3], affine[3:4])
    r = z.rims
    own = act(hidden[...])
    up, down = act(h_above[...]) * inside(z, 3, True), act(h_below[...]) * inside(z, 3, False)
    own, up, down = convolve(z, own, up, down, 3, pads, chains, weight)
    own = x[...] + own
    amap = attention(own)
    sums = image_sums(z, amap * amap) + pltpu.roll(image_sums(z, amap * teacher[...]), 64, 1)
    copies[...] = jnp.broadcast_to(sums[None], copies.shape)
    out[...] = own
    o_above[...] = x_above[pl.ds(2 * r, 2 * r), :] + up
    o_below[...] = x_below[pl.ds(0, 2 * r), :] + down
    near[0] = h_above[pl.ds(2 * r, r), :]
    near[1] = h_below[pl.ds(0, r), :]
    stats[0:1] = center
    stats[1:2] = scale


def tap_rows(q):
    return LANES + 3 * C if q < 0 else LANES if q == BLOCK else q * C


def tap_product(z, operand, own, above, below, pads):
    fill_center(z, pads, own)
    fill_shifted(z, pads, above, below)
    columns = []
    for a in range(TAPS):
        for h in (0, 1):
            columns.append(jnp.concatenate([pads[k][TAPS - 1 - a, h, pl.ds(z.step[k], z.count[k]), :] for k in (1, 0)], axis=0))
    return product(operand, split(jnp.concatenate(columns, axis=1)))


def tap_sums(result, tiles, first_group):
    group = group_of()
    for a in range(TAPS):
        for b in range(TAPS):
            total = None
            for h in (0, 1):
                half = None
                for p in range(4 * h, 4 * h + 4):
                    at, lane = tap_rows(p + b - 1), a * LANES + 128 * h
                    part = result[at : at + C, lane : lane + 128]
                    half = part if half is None else jnp.where(group == p % 4, part, half)
                total = half if total is None else total + half
            tile, slot = divmod(first_group + a * TAPS + b, 4)
            tiles[tile] = jnp.where(group == slot, spread_groups(total), tiles[tile])


def tap_counts(z, turned, tiles, first_group):
    group = group_of()
    m = lax.broadcasted_iota(jnp.int32, (1, z.total), 1)
    row = jnp.where(m < z.start[0], m % z.rows[1], (m - z.start[0]) % z.rows[0])
    height = jnp.where(m < z.start[0], z.rows[1], z.rows[0])
    at = lax.axis_index("row")
    lost = {
        0: (row == height - 1) & (at == z.peers - 1),
        2: (row == 0) & (at == 0),
    }
    for a in range(TAPS):
        column = jnp.sum(jnp.where(lost[a], 0.0, turned) if a in lost else turned, axis=1, keepdims=True)
        for b in range(TAPS):
            total = sum(column[tap_rows(p + b - 1) : tap_rows(p + b - 1) + C] for p in range(BLOCK))
            tile, slot = divmod(first_group + a * TAPS + b, 4)
            tiles[tile] = jnp.where(group == slot, total, tiles[tile])


def turned_operand(z, value, pads, kept):
    fill_center(z, pads, value)
    left = band_operand(z, pads, (1,)).T
    parts = split(left)
    for n in (0, 1):
        kept[n] = parts[n]
    return left


def first_operand_kernel(z, x, above, below, stats, affine, teacher, upstream, weights, left, counts, teachers, spread_u, near_u, pads, chains, kept, kept_w, kept_u, pixels, kept_t, kept_c, sems):
    r, own = z.rims, pl.ds(0, z.total)
    loads = [pltpu.make_async_copy(upstream, kept_u.at[own, :], sems.at[0]), pltpu.make_async_copy(weights.at[1], kept_w, sems.at[1])]
    start_all(loads)
    act = activation(stats[0:1], stats[1:2], affine[0:1], affine[1:2])
    value = turned_operand(z, act(x[...]), pads, kept)
    stores = [pltpu.make_async_copy(kept, left, sems.at[2])]
    stores[0].start()
    tiles = [jnp.zeros((C, 128), F32) for _ in range(3)]
    tap_counts(z, value, tiles, 0)
    counts[...] = jnp.concatenate(tiles, axis=1)
    pixels[own, :] = teacher[...]
    pixels[pl.ds(z.total, 4 * r), :] = jnp.zeros((4 * r, 128), F32)
    n = (REACH + 2) * r
    for side, ref in enumerate((above, below)):
        for d in (0, 1):
            for k in (0, 1):
                line = ref[pl.ds(n + k * z.images[0], z.images[k]), pl.ds(128 * d, 128)]
                for j in range(z.blocks[k]):
                    at = z.total + (2 * side + d) * r + z.rim[k] + j * z.images[k]
                    pixels[pl.ds(at, z.images[k]), pl.ds(0, BLOCK)] = line[:, j * BLOCK : (j + 1) * BLOCK]
    kept_t[...] = spread(pixels[...], to_channels())
    stores.append(pltpu.make_async_copy(kept_t, teachers, sems.at[3]))
    stores[1].start()
    n = REACH * r
    up, down = above[pl.ds(n, 2 * r), :] * inside(z, 2, True), below[pl.ds(n, 2 * r), :] * inside(z, 2, False)
    kept_u[pl.ds(z.total, r), :] = up[r:]
    kept_u[pl.ds(z.total + r, r), :] = down[:r]
    wait_all(loads)
    stores.append(pltpu.make_async_copy(kept_u, near_u, sems.at[5]))
    stores[2].start()
    kept_c[...] = jnp.concatenate(convolve(z, kept_u[own, :], up, down, 2, pads, chains, kept_w), axis=0)
    stores.append(pltpu.make_async_copy(kept_c, spread_u, sems.at[4]))
    stores[3].start()
    wait_all(stores)


def second_operand_kernel(z, hidden, near, stats, affine, out, o_above, o_below, first_left, counts, teachers, spread_u, near_u, weights, out_copy, hidden_copy, left, packed, shifts, by_map, by_teacher, up, pads, chains, kept_left, kept_packed, kept_t, kept_u, kept_w, kept_s, sems):
    r, total = z.rims, z.total
    loads = [
        pltpu.make_async_copy(teachers, kept_t, sems.at[0]),
        pltpu.make_async_copy(weights.at[1], kept_w, sems.at[1]),
        pltpu.make_async_copy(spread_u, kept_u, sems.at[2]),
        pltpu.make_async_copy(first_left, kept_left, sems.at[3]),
    ]
    start_all(loads)
    stores = [
        pltpu.make_async_copy(out, out_copy, sems.at[4]),
        pltpu.make_async_copy(hidden, hidden_copy.at[pl.ds(0, total), :], sems.at[7]),
        pltpu.make_async_copy(near.at[0], hidden_copy.at[pl.ds(total, r), :], sems.at[8]),
        pltpu.make_async_copy(near.at[1], hidden_copy.at[pl.ds(total + r, r), :], sems.at[9]),
        pltpu.make_async_copy(near_u, up, sems.at[10]),
    ]
    start_all(stores)
    normed = normed_by(stats)(jnp.concatenate([hidden[...], near[0], near[1]], axis=0))
    shifted = normed * affine[2:3] + affine[3:4]
    turned_operand(z, gelu(shifted[:total]), pads, left)
    ones = jnp.ones((total, 1), F32)
    masks = jnp.concatenate([ones, inside(z, 1, True), inside(z, 1, False)], axis=0)
    slopes = gelu_slope(shifted) * masks
    o = jnp.concatenate([out[...], o_above[...] * inside(z, 2, True), o_below[...] * inside(z, 2, False)], axis=0)
    for_map = spread(attention(o), to_channels()) * o
    wait_all(loads[:3])
    for_teacher = kept_t[...] * o
    kept_s[0] = kept_u[...] * slopes
    for n, value, ref in ((1, for_map, by_map), (2, for_teacher, by_teacher)):
        own, before, after = value[:total], value[total : total + 2 * r], value[total + 2 * r :]
        ref[...] = jnp.concatenate([own, before[r:], after[:r]], axis=0)
        kept_s[n] = jnp.concatenate(convolve(z, own, before, after, 2, pads, chains, kept_w), axis=0) * slopes
    stores.append(pltpu.make_async_copy(kept_s, shifts, sems.at[5]))
    stores[-1].start()
    loads[3].wait()
    normed = normed * masks
    result = tap_product(z, (kept_left[0], kept_left[1]), normed[:total], normed[total : total + r], normed[total + r :], pads)
    tiles = [jnp.zeros((C, 128), F32) for _ in range(BACK_LANES // 128)]
    tap_sums(result, tiles, NORMED)
    group = group_of()
    for n in range(TAPS * TAPS):
        tile, slot = divmod(ONES + n, 4)
        line = spread_groups(jnp.where(group == n % 4, counts[:, 128 * (n // 4) : 128 * (n // 4) + 128], 0.0))
        tiles[tile] = jnp.where(group == slot, line, tiles[tile])
    kept_packed[...] = jnp.concatenate(tiles, axis=1)
    stores.append(pltpu.make_async_copy(kept_packed, packed, sems.at[6]))
    stores[-1].start()
    wait_all(stores)


def upstream_kernel(z, gathered, up, shifts, left_1, left_2, packed, by_map, by_teacher, hidden, stats, dout, dshift, d_above, d_below, slabs, kept_s, kept_left, kept_h, kept_packed, pads, sems):
    r, total = z.rims, z.total
    loads = [
        pltpu.make_async_copy(a, b, sems.at[n])
        for n, (a, b) in enumerate(((shifts, kept_s), (left_1, kept_left), (hidden.at[pl.ds(0, total), :], kept_h), (packed, kept_packed)))
    ]
    start_all(loads)
    lane = lax.broadcasted_iota(jnp.int32, (z.slots, 128), 1)
    sums = jnp.sum(gathered[...], axis=0)
    square = jnp.sum(jnp.where(lane < 64, sums, 0.0), axis=1, keepdims=True)
    cross = jnp.sum(jnp.where(lane < 64, 0.0, sums), axis=1, keepdims=True)
    inverse = lax.rsqrt(square + map_eps)
    inner = beta_weight * (square * inverse - cross) * inverse
    shape = (z.slots, 128)
    for_map = (beta_weight - inner) * inverse * inverse * (2.0 / C)
    for_teacher = beta_weight * inverse * (2.0 / C)
    for_map, for_teacher = (wide(image_rows(z, jnp.broadcast_to(v, shape), 2)) for v in (for_map, for_teacher))
    value = up[...] + for_map * by_map[...] - for_teacher * by_teacher[...]
    dout[...] = value[:total]
    second = tap_product(z, (left_2[0], left_2[1]), value[:total], value[total : total + r], value[total + r :], pads)
    loads[0].wait()
    shift = kept_s[0] + for_map * kept_s[1] - for_teacher * kept_s[2]
    pre, above, below = shift[:total], shift[total : total + r], shift[total + r :]
    dshift[...] = pre
    d_above[...] = above
    d_below[...] = below
    loads[1].wait()
    first = tap_product(z, (kept_left[0], kept_left[1]), pre, above, below, pads)
    wait_all(loads[2:])
    normed = normed_by(stats)(kept_h[...])
    tiles = [kept_packed[:, 128 * n : 128 * n + 128] for n in range(BACK_LANES // 128)]
    group = group_of()
    tiles[0] = jnp.where(group == BIAS, fold(column_sum(pre)), jnp.where(group == GAIN, fold(column_sum(pre * normed)), tiles[0]))
    tap_sums(second, tiles, SECOND)
    tap_sums(first, tiles, LEFT)
    line = jnp.concatenate(tiles, axis=1)
    for d in range(z.devices):
        slabs[d] = line[d % C : d % C + 1]


def write_kernel(z, out, x, hidden, weights, first_stats, stats, order, out_s, out_l, first_normed, normed, weight, kept, kept_x, kept_h, half, sems):
    loads = [pltpu.make_async_copy(a, b, sems.at[n]) for n, (a, b) in enumerate(((out, kept), (x, kept_x), (hidden, kept_h), (weights.at[0], weight)))]
    start_all(loads)
    loads[0].wait()
    put_halves(half, kept[...])
    from_matrix(z, half, (out_s, out_l))
    loads[1].wait()
    first_normed[...] = normed_by(first_stats)(kept_x[...])
    loads[2].wait()
    normed[...] = normed_by(stats)(kept_h[...])
    loads[3].wait()


def norm_sums(total):
    group = group_of()
    return [wide(spread_groups(jnp.where(group == n, total[:, :128], 0.0))) for n in (BIAS, GAIN)]


def hidden_kernel(z, gathered, dshift, d_above, d_below, second_normed, stats, affine, weight, first_normed, pre_ref, gain_out, bias_out, slabs, pads):
    total = jnp.sum(gathered[...], axis=0)
    bias_sum, gain_sum = norm_sums(total)
    bias_out[...] = bias_sum[:, :C]
    gain_out[...] = gain_sum[:, :C]
    bias_mean, gain_mean = bias_sum / z.pixels, gain_sum / z.pixels
    factor = affine[2:3] * stats[1:2]
    r, total_rows = z.rims, z.total

    def back(d, normed):
        return factor * (d - bias_mean - normed * gain_mean)

    own = back(dshift[...], second_normed[pl.ds(0, total_rows), :])
    up = back(d_above[...], second_normed[pl.ds(total_rows, r), :]) * inside(z, 1, True)
    down = back(d_below[...], second_normed[pl.ds(total_rows + r, r), :]) * inside(z, 1, False)
    grad, _, _ = convolve(z, own, up, down, 1, pads, None, weight)
    normed = first_normed[...]
    pre = grad * gelu_slope(normed * affine[0:1] + affine[1:2])
    pre_ref[...] = pre
    lane = lax.broadcasted_iota(jnp.int32, (1, 128), 1)
    taps = TAPS * TAPS * C

    def along(row):
        return jnp.concatenate([row[:, :128]] * 3, axis=1)[:, :taps]

    second, left, against, ones = (total[:, n * C : n * C + taps] for n in (SECOND, LEFT, NORMED, ONES))
    first = along(factor) * (left - along(bias_mean) * ones - along(gain_mean) * against)
    sums = jnp.where(lane < C, fold(column_sum(pre)), fold(column_sum(pre * normed)))
    line = jnp.concatenate([sums[:, : 2 * C], second, first], axis=1)
    slabs[...] = jnp.broadcast_to(line[None], slabs.shape)


def back_kernel(z, gathered, pre, normed, stats, affine, dout, back_s, back_l, one, two, gain_out, bias_out, half, lines):
    bias_sum, gain_sum = norm_sums(jnp.sum(gathered[:, :, pl.ds(0, 128)], axis=0))
    bias_out[...] = bias_sum[:, :C]
    gain_out[...] = gain_sum[:, :C]
    value = dout[...] + affine[0:1] * stats[1:2] * (pre[...] - bias_sum / z.pixels - normed[...] * (gain_sum / z.pixels))
    put_halves(half, value)
    from_matrix(z, half, (back_s, back_l))
    for d in range(C):
        lines[pl.ds(d, 1), :] = gathered[d]
    for ref, group in ((two, LAST_SECOND), (one, LAST_FIRST)):
        for a in range(TAPS):
            for b in range(TAPS):
                at = (group + a * TAPS + b) * C
                ref[a, b] = lines[:, pl.ds(at, C)]


def call(body, ins, outs, scratch=(), sems=0):
    space = {"v": pltpu.VMEM, "h": pltpu.HBM, "V": pltpu.VMEM}
    shapes = []
    for item in scratch:
        if isinstance(item, list):
            shapes.append([pltpu.VMEM(*s) for s in item])
        else:
            shapes.append(pltpu.VMEM(*item))
    if sems:
        shapes.append(pltpu.SemaphoreType.DMA((sems,)))
    run = pl.pallas_call(
        body,
        out_shape=[jax.ShapeDtypeStruct(shape, kind) if s == "v" else space[s](shape, kind) for s, shape, kind in outs],
        in_specs=[pl.BlockSpec(memory_space=space[s]) for s in ins],
        out_specs=[pl.BlockSpec(memory_space=space[s]) for s, _, _ in outs],
        scratch_shapes=shapes,
        compiler_params=pltpu.CompilerParams(vmem_limit_bytes=VMEM_LIMIT),
    )
    return lambda *args: run(
        *(pltpu.with_memory_space_constraint(arg, pltpu.HBM) if s == "h" else arg for s, arg in zip(ins, args))
    )


def exchange(copies, axes):
    return lax.all_to_all(copies, axes, 0, 0, tiled=True)


def beyond(z, bottom, top, depths):
    hops = max(-(-depth // rows) for rows in z.rows for depth in depths)
    above, below = [], []
    for hop in range(1, hops + 1):
        above.append(lax.ppermute(bottom, "row", [(i, i + hop) for i in range(z.peers - hop)]))
        below.append(lax.ppermute(top, "row", [(i + hop, i) for i in range(z.peers - hop)]))
    if hops == 1:
        return above[0], below[0]
    up, down = [], []
    base = 0
    for depth in depths:
        for n in range(depth):
            for k in (1, 0):
                hop, back = divmod(depth - 1 - n, z.rows[k])
                at = base + (depth - 1 - back) * z.rims + z.rim[k]
                up.append(above[hop][at : at + z.edge[k]])
                hop, back = divmod(n, z.rows[k])
                at = base + back * z.rims + z.rim[k]
                down.append(below[hop][at : at + z.edge[k]])
        base += depth * z.rims
    up.append(jnp.concatenate([pixel_rows(z, above, base, 1, 1), pixel_rows(z, above, base, 0, 1)], axis=1))
    down.append(jnp.concatenate([pixel_rows(z, below, base, 0, 0), pixel_rows(z, below, base, 1, 0)], axis=1))
    return jnp.concatenate(up, axis=0), jnp.concatenate(down, axis=0)


def pixel_rows(z, bands, base, distance, last):
    lines = []
    for k in (0, 1):
        hop, back = divmod(distance, z.rows[k])
        at = base + k * z.images[0]
        half = 128 * abs(last - back)
        lines.append(bands[hop][at : at + z.images[k], half : half + 128])
    lines.append(jnp.zeros((z.slots - sum(z.images), 128), F32))
    return jnp.concatenate(lines, axis=0)


def local(
    image_small, image_large, teacher_small, teacher_large, upstream_small, upstream_large,
    conv_first, gain_first, bias_first, conv_second, gain_second, bias_second,
):
    peers = lax.axis_size("row")
    devices = lax.axis_size("img") * peers
    z = Sizes(image_small.shape, image_large.shape, devices, peers)
    body = lambda function: functools.partial(function, z)
    r = z.rims
    full, half, pair = (z.total, LANES), (2, z.total, 128), (devices, 2, 128)
    weight, left = (2, TAPS * TAP_ROWS, 128), (2, WIDTH, z.total)
    images = [image_small, image_large, upstream_small, upstream_large, teacher_small, teacher_large]
    f = lambda space, *shape: (space, shape, F32)
    depths = (REACH, 2)
    rim_rows = sum(depths) * r + z.slots

    x, bottom, top, copies = call(
        body(start_kernel),
        "hhhhhh",
        [("v", full, F32), f("v", rim_rows, LANES), f("v", rim_rows, LANES), ("V", pair, F32)],
        [[(a.shape, F32) for a in images], (half, F32)],
        6,
    )(*images)
    gathered = exchange(copies, AXES)
    above, below = beyond(z, bottom, top, depths)
    params = [conv_first, conv_second] + images[2:]
    w1, w2, weights, affine, upstream, teacher, x_copy = call(
        body(prepare_kernel),
        "hhhhhhhhhhv",
        [("v", weight, BF16), ("v", weight, BF16), ("h", (2,) + weight, BF16), f("v", 4, LANES), ("h", full, F32), f("v", z.total, 128), ("h", full, F32)],
        [[(a.shape, F32) for a in params], ((2,) + weight, BF16), (full, F32), ((4, C), F32), (half, F32)],
        14,
    )(*params, *(v.reshape(1, C) for v in (gain_first, bias_first, gain_second, bias_second)), x)

    hidden, h_above, h_below, stats_one, copies = call(
        body(first_kernel),
        "vvvvvv",
        [("v", full, F32), f("v", 3 * r, LANES), f("v", 3 * r, LANES), f("v", 2, LANES), ("V", pair, F32)],
        [z.pads(), z.chains(4)],
    )(x, above, below, gathered, affine, w1)
    gathered = exchange(copies, AXES)
    extended, near_rows = z.total + 4 * r, z.total + 2 * r
    left_one, counts, teachers, spread_u, near_u = call(
        body(first_operand_kernel),
        "vvvvvvhh",
        [("h", left, BF16), f("v", C, 384), f("h", extended, LANES), f("h", near_rows, LANES), f("h", near_rows, LANES)],
        [
            z.pads(), z.chains(2), (left, BF16), (weight, BF16), ((near_rows, LANES), F32), ((extended, 128), F32),
            ((extended, LANES), F32), ((near_rows, LANES), F32),
        ],
        6,
    )(x, above, below, stats_one, affine, teacher, upstream, weights)
    gathered, counts = lax.optimization_barrier((gathered, counts))

    map_shape = (peers, z.slots, 128)
    out, o_above, o_below, near, stats_two, copies = call(
        body(second_kernel),
        "vvvvvvvvvv",
        [("v", full, F32), f("v", 2 * r, LANES), f("v", 2 * r, LANES), f("v", 2, r, LANES), f("v", 2, LANES), ("V", map_shape, F32)],
        [z.pads(), z.chains(3)],
    )(hidden, h_above, h_below, gathered, affine, w2, x, above, below, teacher)
    gathered = exchange(copies, ("row",))
    out_copy, hidden_copy, left_two, packed, shifts, by_map, by_teacher, up = call(
        body(second_operand_kernel),
        "vvvvvvvhvhhhh",
        [
            ("h", full, F32), f("h", near_rows, LANES), ("v", left, BF16), f("h", C, BACK_LANES), f("h", 3, near_rows, LANES),
            f("v", near_rows, LANES), f("v", near_rows, LANES), f("v", near_rows, LANES),
        ],
        [
            z.pads(), z.chains(2), (left, BF16), ((C, BACK_LANES), F32), ((extended, LANES), F32), ((near_rows, LANES), F32),
            (weight, BF16), ((3, near_rows, LANES), F32),
        ],
        11,
    )(hidden, near, stats_two, affine, out, o_above, o_below, left_one, counts, teachers, spread_u, near_u, weights)

    dout, dshift, d_above, d_below, slabs = call(
        body(upstream_kernel),
        "vvhhvhvvhv",
        [("v", full, F32), ("v", full, F32), f("v", r, LANES), f("v", r, LANES), f("V", devices, 1, BACK_LANES)],
        [((3, near_rows, LANES), F32), (left, BF16), (full, F32), ((C, BACK_LANES), F32), z.pads()],
        4,
    )(gathered, up, shifts, left_one, left_two, packed, by_map, by_teacher, hidden_copy, stats_two)
    gathered = exchange(slabs, AXES)
    out_s, out_l, first_normed, second_normed, weight_back = call(
        body(write_kernel),
        "hhhhvvv",
        [("v", image_small.shape, F32), ("v", image_large.shape, F32), ("v", full, F32), f("v", near_rows, LANES), ("v", weight, BF16)],
        [(full, F32), (full, F32), ((near_rows, LANES), F32), (half, F32)],
        4,
    )(out_copy, x_copy, hidden_copy, weights, stats_one, stats_two, d_above)

    pre, gain_two, bias_two, slabs = call(
        body(hidden_kernel),
        "vvvvvvvvv",
        [("v", full, F32), f("v", 1, C), f("v", 1, C), f("V", devices, 1, LAST_LANES)],
        [z.pads()],
    )(gathered, dshift, d_above, d_below, second_normed, stats_two, affine, weight_back, first_normed)
    gathered = exchange(slabs, AXES)

    back_s, back_l, one, two, gain_one, bias_one = call(
        body(back_kernel),
        "vvvvvv",
        [("v", a.shape, F32) for a in (image_small, image_large, conv_first, conv_second)] + [f("v", 1, C), f("v", 1, C)],
        [(half, F32), ((C, LAST_LANES), F32)],
    )(gathered, pre, first_normed, stats_one, affine, dout)
    return (
        out_s, out_l, back_s, back_l,
        one, gain_one.reshape(C), bias_one.reshape(C),
        two, gain_two.reshape(C), bias_two.reshape(C),
    )


def solution(mesh):
    split_bands, everywhere = P("img", "row", None), P()
    return jax.shard_map(
        local,
        mesh=mesh,
        in_specs=(split_bands,) * 6 + (everywhere,) * 6,
        out_specs=(split_bands,) * 4 + (everywhere,) * 6,
        check_vma=False,
    )
```

```python
import functools
import math

import jax
import jax.numpy as jnp
from jax import lax
from jax.experimental import pallas as pl
from jax.experimental.pallas import tpu as pltpu
from jax.sharding import PartitionSpec as P

C = 32
HS = 32
HL = 64
HEIGHTS = (HS, HL)

norm_eps = 1e-05
map_eps = 1e-06
beta_weight = 1000.0
AXES = ("img", "row")
BLOCK = 8
LANES = BLOCK * C
TAPS = 3
WIDTH = LANES + 128
DEPTH = TAPS * WIDTH
TAP_ROWS = 128 + 2 * C
REACH = 4
ROOT = math.sqrt(2.0 / math.pi)
CUBE = 0.044715
F32 = jnp.float32
BF16 = jnp.bfloat16
VMEM_LIMIT = 32 * 1024 * 1024
BIAS, GAIN, ONES, SECOND, LEFT, HIDDEN = 0, 1, 2, 3, 12, 21
BACK_LANES = 1024
LAST_SECOND, LAST_FIRST, LAST_LANES = 2, 11, 640


class Sizes:
    def __init__(self, small, large, devices, peers):
        self.images = (small[0], large[0])
        self.rows = (small[1], large[1])
        self.blocks = (HS // BLOCK, HL // BLOCK)
        self.step = tuple(n * r for n, r in zip(self.images, self.rows))
        self.count = tuple(b * s for b, s in zip(self.blocks, self.step))
        self.edge = tuple(b * n for b, n in zip(self.blocks, self.images))
        self.start = (self.count[1], 0)
        self.rim = (self.edge[1], 0)
        self.total = sum(self.count)
        self.rims = sum(self.edge)
        self.slots = -(-sum(self.images) // 8) * 8
        self.guard = -(-max(self.images) // 8) * 8
        self.devices = devices
        self.peers = peers
        self.here = float(self.total * BLOCK)
        self.pixels = self.here * devices

    def pads(self):
        return [((TAPS, 2, self.count[k] + 2 * self.step[k], 128), F32) for k in (0, 1)]

    def chains(self, depth):
        return [((2, 2 * self.guard + (depth + 1) * self.rims, 128), F32)] * 2


def split(value):
    high = value.astype(BF16)
    return high, (value - high.astype(F32)).astype(BF16)


def dot(left, right):
    return lax.dot_general(left, right, (((1,), (0,)), ((), ())), preferred_element_type=F32)


def product(left, right):
    if left[0].shape[1] % 128:
        return dot(left[0], right[0]) + (dot(left[0], right[1]) + dot(left[1], right[0]))
    return dot(
        jnp.concatenate([left[0], left[0], left[1]], axis=1), jnp.concatenate([right[0], right[1], right[0]], axis=0)
    )


def spread(left, right):
    right = right.astype(BF16)
    return dot(jnp.concatenate(split(left), axis=1), jnp.concatenate([right, right], axis=0))


def gelu(s):
    return 0.5 * s * (1.0 + jnp.tanh(ROOT * (s + CUBE * s * s * s)))


def gelu_slope(s):
    square = s * s
    t = jnp.tanh(ROOT * s * (1.0 + CUBE * square))
    return 0.5 * (1.0 + t) + 0.5 * s * (1.0 - t * t) * ROOT * (1.0 + 3.0 * CUBE * square)


def spread_groups(row):
    row = row + pltpu.roll(row, 64, 1)
    return row + pltpu.roll(row, 32, 1)


def fold(row):
    return spread_groups(row[:, :128] + row[:, 128:])


def wide(row):
    return jnp.concatenate([row, row], axis=1)


def group_of(rows=1, lanes=128):
    return lax.broadcasted_iota(jnp.int32, (rows, lanes), 1) // C


def column_sum(value):
    return jnp.sum(value, axis=0, keepdims=True)


def pick_group(row, n):
    return spread_groups(jnp.where(group_of() == n, row, 0.0))


def moments(z, value, ref):
    center = fold(column_sum(value)) / z.here
    off = value - wide(center)
    group = group_of()
    line = jnp.where(group == 0, center, jnp.where(group == 1, fold(column_sum(off * off)), 0.0))
    ref[...] = jnp.broadcast_to(line[None], ref.shape)


def merged(z, ref):
    gathered = ref[...]
    mean = jnp.mean(gathered, axis=0)
    off = gathered - mean[None]
    between = jnp.mean(off * off, axis=0)
    variance = pick_group(mean, 1) / z.here + pick_group(between, 0)
    return wide(pick_group(mean, 0)), wide(lax.rsqrt(variance + norm_eps))


def put_halves(ref, value):
    ref[0] = value[:, :128]
    ref[1] = value[:, 128:]


def whole(ref):
    return jnp.concatenate([ref[0], ref[1]], axis=1)


def to_matrix(z, refs, half):
    for k in (0, 1):
        for j in range(z.blocks[k]):
            at = z.start[k] + j * z.step[k]
            for i in range(z.images[k]):
                for h in (0, 1):
                    half[h, pl.ds(at + i * z.rows[k], z.rows[k]), :] = refs[k][i, :, pl.ds(LANES * j + 128 * h, 128)]


def from_matrix(z, half, refs):
    for k in (0, 1):
        for j in range(z.blocks[k]):
            at = z.start[k] + j * z.step[k]
            for i in range(z.images[k]):
                for h in (0, 1):
                    refs[k][i, :, pl.ds(LANES * j + 128 * h, 128)] = half[h, pl.ds(at + i * z.rows[k], z.rows[k]), :]


def take_rims(z, half, depth, bottom, top):
    for k in (0, 1):
        for d in range(1, depth + 1):
            to_bottom = pl.ds((depth - d) * z.rims + z.rim[k], z.edge[k])
            to_top = pl.ds((d - 1) * z.rims + z.rim[k], z.edge[k])
            if d <= z.rows[k]:
                bottom[to_bottom, :] = half[pl.ds(z.start[k] + z.rows[k] - d, z.edge[k], stride=z.rows[k]), :]
                top[to_top, :] = half[pl.ds(z.start[k] + d - 1, z.edge[k], stride=z.rows[k]), :]
            else:
                bottom[to_bottom, :] = jnp.zeros((z.edge[k], 128), F32)
                top[to_top, :] = jnp.zeros((z.edge[k], 128), F32)


def inside(z, depth, above):
    at = lax.axis_index("row")
    large = lax.broadcasted_iota(jnp.int32, (z.rims, 1), 0) < z.rim[0]
    parts = []
    for n in range(depth):
        if above:
            ok = [jnp.where(at * rows >= depth - n, 1.0, 0.0) for rows in z.rows]
        else:
            ok = [jnp.where((at + 1) * rows + n + 1 <= height, 1.0, 0.0) for rows, height in zip(z.rows, HEIGHTS)]
        parts.append(jnp.where(large, ok[1], ok[0]).astype(F32))
    return jnp.concatenate(parts, axis=0)


def fill_center(z, pads, value):
    for k in (0, 1):
        ref, step, count = pads[k], z.step[k], z.count[k]
        for h in (0, 1):
            ref[1, h, pl.ds(0, step), :] = jnp.zeros((step, 128), F32)
            ref[1, h, pl.ds(step, count), :] = value[z.start[k] : z.start[k] + count, 128 * h : 128 * h + 128]
            ref[1, h, pl.ds(step + count, step), :] = jnp.zeros((step, 128), F32)


def fill_shifted(z, pads, above, below):
    for k in (0, 1):
        ref, step, count, rows = pads[k], z.step[k], z.count[k], z.rows[k]
        rim = slice(z.rim[k], z.rim[k] + z.edge[k])
        for h in (0, 1):
            lanes = slice(128 * h, 128 * h + 128)
            ref[0, h, pl.ds(step, count), :] = ref[1, h, pl.ds(step - 1, count), :]
            ref[2, h, pl.ds(step, count), :] = ref[1, h, pl.ds(step + 1, count), :]
            ref[0, h, pl.ds(step, z.edge[k], stride=rows), :] = above[rim, lanes]
            ref[2, h, pl.ds(step + rows - 1, z.edge[k], stride=rows), :] = below[rim, lanes]


def fill_pads(z, pads, value, above, below):
    fill_center(z, pads, value)
    fill_shifted(z, pads, above, below)
    for k in (0, 1):
        ref, step, count = pads[k], z.step[k], z.count[k]
        for h in (0, 1):
            for a in (0, 2):
                ref[a, h, pl.ds(0, step), :] = jnp.zeros((step, 128), F32)
                ref[a, h, pl.ds(step + count, step), :] = jnp.zeros((step, 128), F32)


def band_operand(z, pads, taps=range(TAPS)):
    lane = lax.broadcasted_iota(jnp.int32, (1, 128), 1)
    parts = []
    for k in (1, 0):
        ref, step, count = pads[k], z.step[k], z.count[k]
        columns = []
        for a in taps:
            before = ref[a, 1, pl.ds(0, count), :]
            after = ref[a, 0, pl.ds(2 * step, count), :]
            columns += [
                ref[a, 0, pl.ds(step, count), :],
                ref[a, 1, pl.ds(step, count), :],
                jnp.where(lane >= 96, before, jnp.where(lane < 32, after, 0.0)),
            ]
        parts.append(jnp.concatenate(columns, axis=1))
    return jnp.concatenate(parts, axis=0)


def rim_operand(z, chain, depth):
    rows, g = (depth + 1) * z.rims, z.guard
    lane = lax.broadcasted_iota(jnp.int32, (1, 128), 1)
    m = lax.broadcasted_iota(jnp.int32, (z.rims, 1), 0)
    large = m < z.rim[0]
    has_before = jnp.where(large, m, m - z.rim[0]) >= jnp.where(large, z.images[1], z.images[0])
    has_after = m < jnp.where(large, z.rim[0] - z.images[1], z.rims - z.images[0])
    take = [(lane >= 96) & has_before & large, (lane >= 96) & has_before & ~large, (lane < 32) & has_after & large, (lane < 32) & has_after & ~large]
    columns = []
    for r in range(depth + 1):
        at = g + r * z.rims
        edge = jnp.zeros((z.rims, 128), F32)
        for mask, half, shift in zip(take, (1, 1, 0, 0), (-z.images[1], -z.images[0], z.images[1], z.images[0])):
            edge = jnp.where(mask, chain[half, pl.ds(at + shift, z.rims), :], edge)
        columns.append(jnp.concatenate([chain[0, pl.ds(at, z.rims), :], chain[1, pl.ds(at, z.rims), :], edge], axis=1))
    return jnp.concatenate(
        [jnp.concatenate(columns[n : n + TAPS], axis=1) for n in range(depth - 1)], axis=0
    )


def rim_operands(z, pads, above, below, depth, chains):
    parts = []
    for side, (rim, chain) in enumerate(zip((above, below), chains)):
        rim_at, own_at = (z.guard, z.guard + depth * z.rims) if side == 0 else (z.guard + z.rims, z.guard)
        for h in (0, 1):
            chain[h, pl.ds(rim_at, depth * z.rims), :] = rim[:, 128 * h : 128 * h + 128]
            for k in (0, 1):
                row = z.step[k] + (0 if side == 0 else z.rows[k] - 1)
                chain[h, pl.ds(own_at + z.rim[k], z.edge[k]), :] = pads[k][1, h, pl.ds(row, z.edge[k], stride=z.rows[k]), :]
        parts.append(rim_operand(z, chain, depth))
    return parts


def times(parts, weight):
    return product(split(jnp.concatenate(parts, axis=0)), (weight_matrix(weight.at[0]), weight_matrix(weight.at[1])))


def convolve(z, own, above, below, depth, pads, chains, weight):
    r = z.rims
    fill_pads(z, pads, own, above[(depth - 1) * r :], below[:r])
    parts = [band_operand(z, pads)]
    if depth > 1:
        parts += rim_operands(z, pads, above, below, depth, chains)
    result = times(parts, weight)
    n = z.total + (depth - 1) * r
    return result[: z.total], result[z.total : n], result[n:]


def convolve_rims(z, pads, above, below, depth, chains, weight):
    result = times(rim_operands(z, pads, above, below, depth, chains), weight)
    n = (depth - 1) * z.rims
    return result[:n], result[n:]


def image_sums(z, value):
    slot = lax.broadcasted_iota(jnp.int32, (z.slots, 1), 0)
    sums = jnp.zeros((z.slots, 128), F32)
    for k in (0, 1):
        line = value[z.start[k] : z.start[k] + z.step[k]]
        for j in range(1, z.blocks[k]):
            at = z.start[k] + j * z.step[k]
            line = line + value[at : at + z.step[k]]
        image = lax.broadcasted_iota(jnp.int32, (z.step[k], 1), 0) // z.rows[k]
        for i in range(z.images[k]):
            sums = jnp.where(slot == i + k * z.images[0], column_sum(jnp.where(image == i, line, 0.0)), sums)
    return sums


def image_rows(z, values, rims):
    parts = []
    for k in (1, 0):
        image = lax.broadcasted_iota(jnp.int32, (z.step[k], 1), 0) // z.rows[k]
        line = jnp.zeros((z.step[k], 128), F32)
        for i in range(z.images[k]):
            at = i + k * z.images[0]
            line = jnp.where(image == i, values[:, at : at + 1], line)
        parts += [line] * z.blocks[k]
    if rims:
        m = lax.broadcasted_iota(jnp.int32, (z.rims, 1), 0)
        image = jnp.where(m < z.rim[0], z.images[0] + m % z.images[1], (m - z.rim[0]) % z.images[0])
        line = jnp.zeros((z.rims, 128), F32)
        for at in range(sum(z.images)):
            line = jnp.where(image == at, values[:, at : at + 1], line)
        parts += [line] * rims
    return jnp.concatenate(parts, axis=0)


def channel_mean():
    a = lax.broadcasted_iota(jnp.int32, (LANES, 128), 0) // C
    b = lax.broadcasted_iota(jnp.int32, (LANES, 128), 1)
    return jnp.where(a == b, 1.0 / C, 0.0).astype(F32)


def to_channels():
    a = lax.broadcasted_iota(jnp.int32, (128, LANES), 0)
    b = lax.broadcasted_iota(jnp.int32, (128, LANES), 1) // C
    return jnp.where(a == b, 1.0, 0.0).astype(F32)


def attention(value):
    return spread(value * value, channel_mean())


def start_all(copies):
    for copy in copies:
        copy.start()


def wait_all(copies):
    for copy in copies:
        copy.wait()


def start_kernel(z, small, large, up_s, up_l, t_s, t_l, x, bottom, top, copies, raw, half, sems):
    loads = [pltpu.make_async_copy(a, b, sems.at[n]) for n, (a, b) in enumerate(zip((small, large, up_s, up_l, t_s, t_l), raw))]
    start_all(loads)
    r, n = z.rims, REACH * z.rims
    tail = n + 2 * r
    for ref in (bottom, top):
        ref[pl.ds(tail, z.slots), :] = jnp.zeros((z.slots, LANES), F32)
    wait_all(loads[:2])
    to_matrix(z, raw[:2], half)
    value = whole(half)
    x[...] = value
    moments(z, value, copies)
    for h in (0, 1):
        lanes = pl.ds(128 * h, 128)
        take_rims(z, half.at[h], REACH, bottom.at[pl.ds(0, n), lanes], top.at[pl.ds(0, n), lanes])
    wait_all(loads[2:])
    for k in (0, 1):
        width, rows = HEIGHTS[k], z.rows[k]
        for i in range(z.images[k]):
            slot = pl.ds(tail + i + k * z.images[0], 1)
            for d in (0, 1):
                to_bottom, to_top = n + (1 - d) * r + z.rim[k] + i, n + d * r + z.rim[k] + i
                for j in range(z.blocks[k]):
                    lanes, at = pl.ds(LANES * j, LANES), j * z.images[k]
                    if d < rows:
                        bottom[pl.ds(to_bottom + at, 1), :] = raw[2 + k][i, pl.ds(rows - 1 - d, 1), lanes]
                        top[pl.ds(to_top + at, 1), :] = raw[2 + k][i, pl.ds(d, 1), lanes]
                    else:
                        bottom[pl.ds(to_bottom + at, 1), :] = jnp.zeros((1, LANES), F32)
                        top[pl.ds(to_top + at, 1), :] = jnp.zeros((1, LANES), F32)
                if d < rows:
                    bottom[slot, pl.ds(128 * (1 - d), width)] = raw[4 + k][i, pl.ds(rows - 1 - d, 1), :]
                    top[slot, pl.ds(128 * d, width)] = raw[4 + k][i, pl.ds(d, 1), :]


def banded(taps, ref):
    row = lax.broadcasted_iota(jnp.int32, (128, 128), 0) // C
    lane = group_of(128)
    for a in range(TAPS):
        main = jnp.zeros((128, 128), F32)
        for b in range(TAPS):
            main = jnp.where(row - lane + 1 == b, taps[a][b], main)
        before = jnp.where(lane[:C] == 0, taps[a][0][:C], 0.0)
        after = jnp.where(lane[:C] == 3, taps[a][2][:C], 0.0)
        for n, part in enumerate(split(jnp.concatenate([main, before, after], axis=0))):
            ref[n, pl.ds(a * TAP_ROWS, TAP_ROWS), :] = part


def weight_matrix(ref):
    rows = []
    zeros = jnp.zeros((128 - C, 128), BF16)
    for a in range(TAPS):
        at = a * TAP_ROWS
        main = ref[pl.ds(at, 128), :]
        before = jnp.concatenate([zeros, ref[pl.ds(at + 128, C), :]], axis=0)
        after = jnp.concatenate([ref[pl.ds(at + 128 + C, C), :], zeros], axis=0)
        rows += [
            jnp.concatenate([main, before], axis=1),
            jnp.concatenate([after, main], axis=1),
            jnp.concatenate([before, after], axis=1),
        ]
    return jnp.concatenate(rows, axis=0)


def prepare_kernel(z, first, second, up_s, up_l, t_s, t_l, g1, b1, g2, b2, x, w1, w2, weights, affine, upstream, teacher, x_copy, raw, kept, kept_u, kept_t, rows, half, sems):
    targets = tuple(raw) + tuple(rows.at[pl.ds(n, 1), :] for n in range(4))
    refs = (first, second, up_s, up_l, t_s, t_l, g1, b1, g2, b2)
    loads = [pltpu.make_async_copy(a, b, sems.at[n]) for n, (a, b) in enumerate(zip(refs, targets))]
    start_all(loads)
    stores = [pltpu.make_async_copy(x, x_copy, sems.at[15])]
    stores[0].start()
    wait_all(loads)
    to_matrix(z, raw[2:4], half)
    kept_u[...] = whole(half)
    stores.append(pltpu.make_async_copy(kept_u, upstream, sems.at[10]))
    stores[1].start()
    for n, (source, forward) in enumerate(zip(raw[:2], (w1, w2))):
        tiles = []
        for a in range(TAPS):
            line = [jnp.concatenate([source[a, b]] * 4, axis=1) for b in range(TAPS)]
            tiles.append([jnp.concatenate([tap] * 4, axis=0) for tap in line])
        turned = [[tiles[TAPS - 1 - a][TAPS - 1 - b].T for b in range(TAPS)] for a in range(TAPS)]
        for at, taps in ((n, tiles), (3 - n, turned)):
            banded(taps, kept.at[at])
            stores.append(pltpu.make_async_copy(kept.at[at], weights.at[at], sems.at[11 + at]))
            stores[-1].start()
        forward[...] = kept[n]
    affine[...] = jnp.concatenate([rows[...]] * BLOCK, axis=1)
    kept_t[...] = jnp.zeros(kept_t.shape, F32)
    for k, ref in ((0, raw[4]), (1, raw[5])):
        for i in range(z.images[k]):
            line = ref[i]
            for j in range(z.blocks[k]):
                at = z.start[k] + j * z.step[k] + i * z.rows[k]
                kept_t[pl.ds(at, z.rows[k]), pl.ds(0, BLOCK)] = line[:, j * BLOCK : (j + 1) * BLOCK]
    stores.append(pltpu.make_async_copy(kept_t, teacher, sems.at[16]))
    stores[-1].start()
    wait_all(stores)


def normed_by(stats):
    return lambda v: (v - stats[0:1]) * stats[1:2]


def activation(center, scale, gain, bias):
    factor = scale * gain
    offset = bias - center * factor
    return lambda v: gelu(v * factor + offset)


def first_kernel(z, x, above, below, gathered, affine, weight, hidden, stats, copies, pads):
    center, scale = merged(z, gathered)
    act = activation(center, scale, affine[0:1], affine[1:2])
    r = z.rims
    up, down = act(above[pl.ds(3 * r, r), :]) * inside(z, 1, True), act(below[pl.ds(0, r), :]) * inside(z, 1, False)
    own, _, _ = convolve(z, act(x[...]), up, down, 1, pads, None, weight)
    moments(z, own, copies)
    hidden[...] = own
    stats[0:1] = center
    stats[1:2] = scale


def second_kernel(z, hidden, h_above, h_below, gathered, affine, weight, x, teacher, out, stats, copies, pads, kept_t, sems):
    load = pltpu.make_async_copy(teacher, kept_t, sems.at[0])
    load.start()
    center, scale = merged(z, gathered)
    act = activation(center, scale, affine[2:3], affine[3:4])
    r = z.rims
    up, down = act(h_above[pl.ds(2 * r, r), :]) * inside(z, 1, True), act(h_below[pl.ds(0, r), :]) * inside(z, 1, False)
    own, _, _ = convolve(z, act(hidden[...]), up, down, 1, pads, None, weight)
    own = x[...] + own
    out[...] = own
    amap = attention(own)
    load.wait()
    slot = lax.broadcasted_iota(jnp.int32, (z.slots, 128), 0)
    lane = lax.broadcasted_iota(jnp.int32, (z.slots, 128), 1)
    square, cross = (jnp.sum(image_sums(z, amap * v), axis=1, keepdims=True) for v in (amap, kept_t[...]))
    line = column_sum(jnp.where(lane == slot, square, jnp.where(lane == slot + 64, cross, 0.0)))
    copies[...] = jnp.broadcast_to(line[None], copies.shape)
    stats[0:1] = center
    stats[1:2] = scale


def tap_rows(q):
    return LANES + 3 * C if q < 0 else LANES if q == BLOCK else q * C


def tap_product(z, operand, own, above, below, pads):
    fill_center(z, pads, own)
    fill_shifted(z, pads, above, below)
    columns = []
    for a in range(TAPS):
        for h in (0, 1):
            columns.append(jnp.concatenate([pads[k][TAPS - 1 - a, h, pl.ds(z.step[k], z.count[k]), :] for k in (1, 0)], axis=0))
    return product(operand, split(jnp.concatenate(columns, axis=1)))


def tap_sums(result, tiles, first_group):
    group = group_of()
    for a in range(TAPS):
        for b in range(TAPS):
            total = None
            for h in (0, 1):
                half = None
                for p in range(4 * h, 4 * h + 4):
                    at, lane = tap_rows(p + b - 1), a * LANES + 128 * h
                    part = result[at : at + C, lane : lane + 128]
                    half = part if half is None else jnp.where(group == p % 4, part, half)
                total = half if total is None else total + half
            tile, slot = divmod(first_group + a * TAPS + b, 4)
            tiles[tile] = jnp.where(group == slot, spread_groups(total), tiles[tile])


def tap_counts(z, turned, tiles):
    lane = lax.broadcasted_iota(jnp.int32, (1, 128), 1)
    m = lax.broadcasted_iota(jnp.int32, (1, z.total), 1)
    row = jnp.where(m < z.start[0], m % z.rows[1], (m - z.start[0]) % z.rows[0])
    height = jnp.where(m < z.start[0], z.rows[1], z.rows[0])
    at = lax.axis_index("row")
    lost = {
        0: (row == height - 1) & (at == z.peers - 1),
        2: (row == 0) & (at == 0),
    }
    tile, slot = divmod(ONES * C, 128)
    for a in range(TAPS):
        column = jnp.sum(jnp.where(lost[a], 0.0, turned) if a in lost else turned, axis=1, keepdims=True)
        for b in range(TAPS):
            total = sum(column[tap_rows(p + b - 1) : tap_rows(p + b - 1) + C] for p in range(BLOCK))
            tiles[tile] = jnp.where(lane == slot + a * TAPS + b, total, tiles[tile])


def turned_operand(z, value, pads, kept):
    fill_center(z, pads, value)
    left = band_operand(z, pads, (1,)).T
    parts = split(left)
    for n in (0, 1):
        kept[n] = parts[n]
    return left


def first_operand_kernel(z, x, hidden, above, below, stats, affine, teacher, upstream, weights, h_above, h_below, left, packed, teachers, spread_u, near_u, pads, chains, deep_chains, kept, kept_w, kept_u, pixels, kept_t, kept_c, kept_packed, sems):
    r, own = z.rims, pl.ds(0, z.total)
    loads = [
        pltpu.make_async_copy(weights.at[0], kept_w.at[0], sems.at[0]),
        pltpu.make_async_copy(upstream, kept_u.at[own, :], sems.at[1]),
        pltpu.make_async_copy(weights.at[2], kept_w.at[1], sems.at[2]),
        pltpu.make_async_copy(teacher, pixels.at[own, :], sems.at[3]),
    ]
    start_all(loads)
    act = activation(stats[0:1], stats[1:2], affine[0:1], affine[1:2])
    value = turned_operand(z, act(x[...]), pads, kept)
    stores = [pltpu.make_async_copy(kept, left, sems.at[4])]
    stores[0].start()
    n = REACH * r
    up, down = act(above[pl.ds(0, n), :]) * inside(z, REACH, True), act(below[pl.ds(0, n), :]) * inside(z, REACH, False)
    loads[0].wait()
    up, down = convolve_rims(z, pads, up, down, REACH, deep_chains, kept_w.at[0])
    h_above[...] = up
    h_below[...] = down
    tiles = [jnp.zeros((C, 128), F32) for _ in range(BACK_LANES // 128)]
    tap_counts(z, value, tiles)
    result = tap_product(
        z, (kept[0], kept[1]), hidden[...], up[2 * r :] * inside(z, 1, True), down[:r] * inside(z, 1, False), pads
    )
    tap_sums(result, tiles, HIDDEN)
    kept_packed[...] = jnp.concatenate(tiles, axis=1)
    wait_all(loads[1:])
    pixels[pl.ds(z.total, 4 * r), :] = jnp.zeros((4 * r, 128), F32)
    n = (REACH + 2) * r
    for side, ref in enumerate((above, below)):
        for d in (0, 1):
            for k in (0, 1):
                line = ref[pl.ds(n + k * z.images[0], z.images[k]), pl.ds(128 * d, 128)]
                for j in range(z.blocks[k]):
                    at = z.total + (2 * side + d) * r + z.rim[k] + j * z.images[k]
                    pixels[pl.ds(at, z.images[k]), pl.ds(0, BLOCK)] = line[:, j * BLOCK : (j + 1) * BLOCK]
    kept_t[...] = spread(pixels[...], to_channels())
    n = REACH * r
    up, down = above[pl.ds(n, 2 * r), :] * inside(z, 2, True), below[pl.ds(n, 2 * r), :] * inside(z, 2, False)
    kept_u[pl.ds(z.total, r), :] = up[r:]
    kept_u[pl.ds(z.total + r, r), :] = down[:r]
    stores += [
        pltpu.make_async_copy(kept_packed, packed, sems.at[5]),
        pltpu.make_async_copy(kept_t, teachers, sems.at[6]),
        pltpu.make_async_copy(kept_u, near_u, sems.at[7]),
    ]
    start_all(stores[1:])
    kept_c[...] = jnp.concatenate(convolve(z, kept_u[own, :], up, down, 2, pads, chains, kept_w.at[1]), axis=0)
    stores.append(pltpu.make_async_copy(kept_c, spread_u, sems.at[8]))
    stores[-1].start()
    wait_all(stores)


def second_operand_kernel(z, hidden, h_above, h_below, stats, affine, out, above, below, teachers, spread_u, near_u, weights, out_copy, hidden_copy, left, shifts, by_map, by_teacher, up, pads, chains, deep_chains, kept_t, kept_u, kept_w, kept_s, sems):
    r, total = z.rims, z.total
    loads = [
        pltpu.make_async_copy(weights.at[pl.ds(1, 2)], kept_w, sems.at[0]),
        pltpu.make_async_copy(teachers, kept_t, sems.at[1]),
        pltpu.make_async_copy(spread_u, kept_u, sems.at[2]),
    ]
    start_all(loads)
    stores = [
        pltpu.make_async_copy(near_u, up, sems.at[3]),
        pltpu.make_async_copy(out, out_copy, sems.at[4]),
        pltpu.make_async_copy(hidden, hidden_copy.at[pl.ds(0, total), :], sems.at[5]),
        pltpu.make_async_copy(h_above.at[pl.ds(2 * r, r), :], hidden_copy.at[pl.ds(total, r), :], sems.at[6]),
        pltpu.make_async_copy(h_below.at[pl.ds(0, r), :], hidden_copy.at[pl.ds(total + r, r), :], sems.at[7]),
    ]
    start_all(stores)
    unit = normed_by(stats)
    gain, bias = affine[2:3], affine[3:4]
    shifted = unit(hidden[...]) * gain + bias
    before, after = (unit(ref[...]) * gain + bias for ref in (h_above, h_below))
    turned_operand(z, gelu(shifted), pads, left)
    loads[0].wait()
    o_up, o_down = convolve_rims(
        z, pads, gelu(before) * inside(z, 3, True), gelu(after) * inside(z, 3, False), 3, deep_chains, kept_w.at[0]
    )
    o_up = (above[pl.ds(2 * r, 2 * r), :] + o_up) * inside(z, 2, True)
    o_down = (below[pl.ds(0, 2 * r), :] + o_down) * inside(z, 2, False)
    slopes = jnp.concatenate(
        [gelu_slope(shifted), gelu_slope(before[2 * r :]) * inside(z, 1, True), gelu_slope(after[:r]) * inside(z, 1, False)], axis=0
    )
    o = jnp.concatenate([out[...], o_up, o_down], axis=0)
    for_map = spread(attention(o), to_channels()) * o
    wait_all(loads[1:])
    for_teacher = kept_t[...] * o
    kept_s[0] = kept_u[...] * slopes
    for n, value, ref in ((1, for_map, by_map), (2, for_teacher, by_teacher)):
        own, before, after = value[:total], value[total : total + 2 * r], value[total + 2 * r :]
        ref[...] = jnp.concatenate([own, before[r:], after[:r]], axis=0)
        kept_s[n] = jnp.concatenate(convolve(z, own, before, after, 2, pads, chains, kept_w.at[1]), axis=0) * slopes
    stores.append(pltpu.make_async_copy(kept_s, shifts, sems.at[8]))
    stores[-1].start()
    wait_all(stores)


def upstream_kernel(z, gathered, up, shifts, left_1, left_2, packed, by_map, by_teacher, hidden, stats, dout, dshift, d_above, d_below, slabs, kept_s, kept_left, kept_h, kept_packed, pads, sems):
    r, total = z.rims, z.total
    loads = [
        pltpu.make_async_copy(a, b, sems.at[n])
        for n, (a, b) in enumerate(((shifts, kept_s), (left_1, kept_left), (hidden.at[pl.ds(0, total), :], kept_h), (packed, kept_packed)))
    ]
    start_all(loads)
    square = jnp.sum(gathered[...], axis=0)
    cross = pltpu.roll(square, 64, 1)
    inverse = lax.rsqrt(square + map_eps)
    inner = beta_weight * (square * inverse - cross) * inverse
    for_map = (beta_weight - inner) * inverse * inverse * (2.0 / C)
    for_teacher = beta_weight * inverse * (2.0 / C)
    for_map, for_teacher = (wide(image_rows(z, v, 2)) for v in (for_map, for_teacher))
    value = up[...] + for_map * by_map[...] - for_teacher * by_teacher[...]
    dout[...] = value[:total]
    second = tap_product(z, (left_2[0], left_2[1]), value[:total], value[total : total + r], value[total + r :], pads)
    loads[0].wait()
    shift = kept_s[0] + for_map * kept_s[1] - for_teacher * kept_s[2]
    pre, above, below = shift[:total], shift[total : total + r], shift[total + r :]
    dshift[...] = pre
    d_above[...] = above
    d_below[...] = below
    loads[1].wait()
    first = tap_product(z, (kept_left[0], kept_left[1]), pre, above, below, pads)
    wait_all(loads[2:])
    normed = normed_by(stats)(kept_h[...])
    tiles = [kept_packed[:, 128 * n : 128 * n + 128] for n in range(BACK_LANES // 128)]
    group = group_of()
    tiles[0] = jnp.where(group == BIAS, fold(column_sum(pre)), jnp.where(group == GAIN, fold(column_sum(pre * normed)), tiles[0]))
    tap_sums(second, tiles, SECOND)
    tap_sums(first, tiles, LEFT)
    line = jnp.concatenate(tiles, axis=1)
    for d in range(z.devices):
        slabs[d] = line[d % C : d % C + 1]


def write_kernel(z, out, x, hidden, weights, first_stats, stats, order, out_s, out_l, first_normed, normed, weight, kept, kept_x, kept_h, half, sems):
    loads = [pltpu.make_async_copy(a, b, sems.at[n]) for n, (a, b) in enumerate(((out, kept), (x, kept_x), (hidden, kept_h), (weights.at[3], weight)))]
    start_all(loads)
    loads[0].wait()
    put_halves(half, kept[...])
    from_matrix(z, half, (out_s, out_l))
    loads[1].wait()
    first_normed[...] = normed_by(first_stats)(kept_x[...])
    loads[2].wait()
    normed[...] = normed_by(stats)(kept_h[...])
    loads[3].wait()


def norm_sums(total):
    return [wide(pick_group(total[:, :128], n)) for n in (BIAS, GAIN)]


def hidden_kernel(z, gathered, dshift, d_above, d_below, second_normed, stats, affine, weight, first_normed, pre_ref, gain_out, bias_out, slabs, pads):
    total = jnp.sum(gathered[...], axis=0)
    bias_sum, gain_sum = norm_sums(total)
    bias_out[...] = bias_sum[:, :C]
    gain_out[...] = gain_sum[:, :C]
    bias_mean, gain_mean = bias_sum / z.pixels, gain_sum / z.pixels
    factor = affine[2:3] * stats[1:2]
    r, total_rows = z.rims, z.total

    def back(d, normed):
        return factor * (d - bias_mean - normed * gain_mean)

    own = back(dshift[...], second_normed[pl.ds(0, total_rows), :])
    up = back(d_above[...], second_normed[pl.ds(total_rows, r), :]) * inside(z, 1, True)
    down = back(d_below[...], second_normed[pl.ds(total_rows + r, r), :]) * inside(z, 1, False)
    grad, _, _ = convolve(z, own, up, down, 1, pads, None, weight)
    normed = first_normed[...]
    pre = grad * gelu_slope(normed * affine[0:1] + affine[1:2])
    pre_ref[...] = pre
    lane = lax.broadcasted_iota(jnp.int32, (1, 128), 1)
    taps = TAPS * TAPS * C

    def along(row):
        return jnp.concatenate([row[:, :128]] * 3, axis=1)[:, :taps]

    second, left, against = (total[:, n * C : n * C + taps] for n in (SECOND, LEFT, HIDDEN))
    group = group_of()
    ones = []
    for n in range(3):
        tile = jnp.zeros((1, 128), F32)
        for g in range(4 if n < 2 else 1):
            at = ONES * C + 4 * n + g
            tile = jnp.where(group == g, total[:, at : at + 1], tile)
        ones.append(tile)
    ones = jnp.concatenate(ones, axis=1)[:, :taps]
    against = along(stats[1:2]) * (against - along(stats[0:1]) * ones)
    first = along(factor) * (left - along(bias_mean) * ones - along(gain_mean) * against)
    sums = jnp.where(lane < C, fold(column_sum(pre)), fold(column_sum(pre * normed)))
    line = jnp.concatenate([sums[:, : 2 * C], second, first], axis=1)
    slabs[...] = jnp.broadcast_to(line[None], slabs.shape)


def back_kernel(z, gathered, pre, normed, stats, affine, dout, back_s, back_l, one, two, gain_out, bias_out, half, lines):
    bias_sum, gain_sum = norm_sums(jnp.sum(gathered[:, :, pl.ds(0, 128)], axis=0))
    bias_out[...] = bias_sum[:, :C]
    gain_out[...] = gain_sum[:, :C]
    value = dout[...] + affine[0:1] * stats[1:2] * (pre[...] - bias_sum / z.pixels - normed[...] * (gain_sum / z.pixels))
    put_halves(half, value)
    from_matrix(z, half, (back_s, back_l))
    for d in range(C):
        lines[pl.ds(d, 1), :] = gathered[d]
    for ref, group in ((two, LAST_SECOND), (one, LAST_FIRST)):
        for a in range(TAPS):
            for b in range(TAPS):
                at = (group + a * TAPS + b) * C
                ref[a, b] = lines[:, pl.ds(at, C)]


def call(body, ins, outs, scratch=(), sems=0):
    space = {"v": pltpu.VMEM, "h": pltpu.HBM, "V": pltpu.VMEM}
    shapes = []
    for item in scratch:
        if isinstance(item, list):
            shapes.append([pltpu.VMEM(*s) for s in item])
        else:
            shapes.append(pltpu.VMEM(*item))
    if sems:
        shapes.append(pltpu.SemaphoreType.DMA((sems,)))
    run = pl.pallas_call(
        body,
        out_shape=[jax.ShapeDtypeStruct(shape, kind) if s == "v" else space[s](shape, kind) for s, shape, kind in outs],
        in_specs=[pl.BlockSpec(memory_space=space[s]) for s in ins],
        out_specs=[pl.BlockSpec(memory_space=space[s]) for s, _, _ in outs],
        scratch_shapes=shapes,
        compiler_params=pltpu.CompilerParams(vmem_limit_bytes=VMEM_LIMIT),
    )
    return lambda *args: run(
        *(pltpu.with_memory_space_constraint(arg, pltpu.HBM) if s == "h" else arg for s, arg in zip(ins, args))
    )


def exchange(copies, axes):
    return lax.all_to_all(copies, axes, 0, 0, tiled=True)


def beyond(z, bottom, top, depths):
    hops = max(-(-depth // rows) for rows in z.rows for depth in depths)
    above, below = [], []
    for hop in range(1, hops + 1):
        above.append(lax.ppermute(bottom, "row", [(i, i + hop) for i in range(z.peers - hop)]))
        below.append(lax.ppermute(top, "row", [(i + hop, i) for i in range(z.peers - hop)]))
    if hops == 1:
        return above[0], below[0]
    up, down = [], []
    base = 0
    for depth in depths:
        for n in range(depth):
            for k in (1, 0):
                hop, back = divmod(depth - 1 - n, z.rows[k])
                at = base + (depth - 1 - back) * z.rims + z.rim[k]
                up.append(above[hop][at : at + z.edge[k]])
                hop, back = divmod(n, z.rows[k])
                at = base + back * z.rims + z.rim[k]
                down.append(below[hop][at : at + z.edge[k]])
        base += depth * z.rims
    up.append(jnp.concatenate([pixel_rows(z, above, base, 1, 1), pixel_rows(z, above, base, 0, 1)], axis=1))
    down.append(jnp.concatenate([pixel_rows(z, below, base, 0, 0), pixel_rows(z, below, base, 1, 0)], axis=1))
    return jnp.concatenate(up, axis=0), jnp.concatenate(down, axis=0)


def pixel_rows(z, bands, base, distance, last):
    lines = []
    for k in (0, 1):
        hop, back = divmod(distance, z.rows[k])
        at = base + k * z.images[0]
        half = 128 * abs(last - back)
        lines.append(bands[hop][at : at + z.images[k], half : half + 128])
    lines.append(jnp.zeros((z.slots - sum(z.images), 128), F32))
    return jnp.concatenate(lines, axis=0)


def local(
    image_small, image_large, teacher_small, teacher_large, upstream_small, upstream_large,
    conv_first, gain_first, bias_first, conv_second, gain_second, bias_second,
):
    peers = lax.axis_size("row")
    devices = lax.axis_size("img") * peers
    z = Sizes(image_small.shape, image_large.shape, devices, peers)
    body = lambda function: functools.partial(function, z)
    r = z.rims
    full, half, line = (z.total, LANES), (2, z.total, 128), (devices, 1, 128)
    weight, left = (2, TAPS * TAP_ROWS, 128), (2, WIDTH, z.total)
    images = [image_small, image_large, upstream_small, upstream_large, teacher_small, teacher_large]
    f = lambda space, *shape: (space, shape, F32)
    depths = (REACH, 2)
    rim_rows = sum(depths) * r + z.slots

    x, bottom, top, copies = call(
        body(start_kernel),
        "hhhhhh",
        [("v", full, F32), f("v", rim_rows, LANES), f("v", rim_rows, LANES), ("V", line, F32)],
        [[(a.shape, F32) for a in images], (half, F32)],
        6,
    )(*images)
    gathered = exchange(copies, AXES)
    above, below = beyond(z, bottom, top, depths)
    params = [conv_first, conv_second] + images[2:]
    w1, w2, weights, affine, upstream, teacher, x_copy = call(
        body(prepare_kernel),
        "hhhhhhhhhhv",
        [("v", weight, BF16), ("v", weight, BF16), ("h", (4,) + weight, BF16), f("v", 4, LANES), ("h", full, F32), f("h", z.total, 128), ("h", full, F32)],
        [[(a.shape, F32) for a in params], ((4,) + weight, BF16), (full, F32), ((z.total, 128), F32), ((4, C), F32), (half, F32)],
        17,
    )(*params, *(v.reshape(1, C) for v in (gain_first, bias_first, gain_second, bias_second)), x)

    hidden, stats_one, copies = call(
        body(first_kernel),
        "vvvvvv",
        [("v", full, F32), f("v", 2, LANES), ("V", line, F32)],
        [z.pads()],
    )(x, above, below, gathered, affine, w1)
    gathered = exchange(copies, AXES)
    extended, near_rows = z.total + 4 * r, z.total + 2 * r
    h_above, h_below, left_one, packed, teachers, spread_u, near_u = call(
        body(first_operand_kernel),
        "vvvvvvhhh",
        [
            f("v", 3 * r, LANES), f("v", 3 * r, LANES), ("h", left, BF16), f("h", C, BACK_LANES), f("h", extended, LANES),
            f("h", near_rows, LANES), f("h", near_rows, LANES),
        ],
        [
            z.pads(), z.chains(2), z.chains(REACH), (left, BF16), ((2,) + weight, BF16), ((near_rows, LANES), F32),
            ((extended, 128), F32), ((extended, LANES), F32), ((near_rows, LANES), F32), ((C, BACK_LANES), F32),
        ],
        9,
    )(x, hidden, above, below, stats_one, affine, teacher, upstream, weights)

    map_shape = (peers, 1, 128)
    out, stats_two, copies = call(
        body(second_kernel),
        "vvvvvvvh",
        [("v", full, F32), f("v", 2, LANES), ("V", map_shape, F32)],
        [z.pads(), ((z.total, 128), F32)],
        1,
    )(hidden, h_above, h_below, gathered, affine, w2, x, teacher)
    gathered = exchange(copies, ("row",))
    out_copy, hidden_copy, left_two, shifts, by_map, by_teacher, up = call(
        body(second_operand_kernel),
        "vvvvvvvvhhhh",
        [
            ("h", full, F32), f("h", near_rows, LANES), ("v", left, BF16), f("h", 3, near_rows, LANES),
            f("v", near_rows, LANES), f("v", near_rows, LANES), f("v", near_rows, LANES),
        ],
        [
            z.pads(), z.chains(2), z.chains(3), ((extended, LANES), F32), ((near_rows, LANES), F32),
            ((2,) + weight, BF16), ((3, near_rows, LANES), F32),
        ],
        9,
    )(hidden, h_above, h_below, stats_two, affine, out, above, below, teachers, spread_u, near_u, weights)

    dout, dshift, d_above, d_below, slabs = call(
        body(upstream_kernel),
        "vvhhvhvvhv",
        [("v", full, F32), ("v", full, F32), f("v", r, LANES), f("v", r, LANES), f("V", devices, 1, BACK_LANES)],
        [((3, near_rows, LANES), F32), (left, BF16), (full, F32), ((C, BACK_LANES), F32), z.pads()],
        4,
    )(gathered, up, shifts, left_one, left_two, packed, by_map, by_teacher, hidden_copy, stats_two)
    gathered = exchange(slabs, AXES)
    out_s, out_l, first_normed, second_normed, weight_back = call(
        body(write_kernel),
        "hhhhvvv",
        [("v", image_small.shape, F32), ("v", image_large.shape, F32), ("v", full, F32), f("v", near_rows, LANES), ("v", weight, BF16)],
        [(full, F32), (full, F32), ((near_rows, LANES), F32), (half, F32)],
        4,
    )(out_copy, x_copy, hidden_copy, weights, stats_one, stats_two, d_above)

    pre, gain_two, bias_two, slabs = call(
        body(hidden_kernel),
        "vvvvvvvvv",
        [("v", full, F32), f("v", 1, C), f("v", 1, C), f("V", devices, 1, LAST_LANES)],
        [z.pads()],
    )(gathered, dshift, d_above, d_below, second_normed, stats_two, affine, weight_back, first_normed)
    gathered = exchange(slabs, AXES)

    back_s, back_l, one, two, gain_one, bias_one = call(
        body(back_kernel),
        "vvvvvv",
        [("v", a.shape, F32) for a in (image_small, image_large, conv_first, conv_second)] + [f("v", 1, C), f("v", 1, C)],
        [(half, F32), ((C, LAST_LANES), F32)],
    )(gathered, pre, first_normed, stats_one, affine, dout)
    return (
        out_s, out_l, back_s, back_l,
        one, gain_one.reshape(C), bias_one.reshape(C),
        two, gain_two.reshape(C), bias_two.reshape(C),
    )


def solution(mesh):
    split_bands, everywhere = P("img", "row", None), P()
    return jax.shard_map(
        local,
        mesh=mesh,
        in_specs=(split_bands,) * 6 + (everywhere,) * 6,
        out_specs=(split_bands,) * 4 + (everywhere,) * 6,
        check_vma=False,
    )
```

```python
import functools
import math

import jax
import jax.numpy as jnp
from jax import lax
from jax.experimental import pallas as pl
from jax.experimental.pallas import tpu as pltpu
from jax.sharding import PartitionSpec as P

C = 32
HS = 32
HL = 64
HEIGHTS = (HS, HL)

norm_eps = 1e-05
map_eps = 1e-06
beta_weight = 1000.0
AXES = ("img", "row")
BLOCK = 8
LANES = BLOCK * C
TAPS = 3
WIDTH = LANES + 128
DEPTH = TAPS * WIDTH
TAP_ROWS = 128 + 2 * C
REACH = 4
ROOT = math.sqrt(2.0 / math.pi)
CUBE = 0.044715
F32 = jnp.float32
BF16 = jnp.bfloat16
VMEM_LIMIT = 32 * 1024 * 1024
BIAS, GAIN, SECOND, LEFT, HIDDEN, ONES = 0, 1, 2, 11, 20, 29
BACK_LANES = 1280
LAST_SECOND, LAST_FIRST, LAST_LANES = 2, 11, 640


class Sizes:
    def __init__(self, small, large, devices, peers):
        self.images = (small[0], large[0])
        self.rows = (small[1], large[1])
        self.blocks = (HS // BLOCK, HL // BLOCK)
        self.step = tuple(n * r for n, r in zip(self.images, self.rows))
        self.count = tuple(b * s for b, s in zip(self.blocks, self.step))
        self.edge = tuple(b * n for b, n in zip(self.blocks, self.images))
        self.start = (self.count[1], 0)
        self.rim = (self.edge[1], 0)
        self.total = sum(self.count)
        self.rims = sum(self.edge)
        self.slots = -(-sum(self.images) // 8) * 8
        self.guard = -(-max(self.images) // 8) * 8
        self.devices = devices
        self.peers = peers
        self.here = float(self.total * BLOCK)
        self.pixels = self.here * devices

    def pads(self):
        return [((TAPS, 2, self.count[k] + 2 * self.step[k], 128), F32) for k in (0, 1)]

    def chains(self, depth):
        return [((2, 2 * self.guard + (depth + 1) * self.rims, 128), F32)] * 2


def split(value):
    high = value.astype(BF16)
    return high, (value - high.astype(F32)).astype(BF16)


def dot(left, right):
    return lax.dot_general(left, right, (((1,), (0,)), ((), ())), preferred_element_type=F32)


def product(left, right):
    if left[0].shape[1] % 128:
        return dot(left[0], right[0]) + (dot(left[0], right[1]) + dot(left[1], right[0]))
    return dot(
        jnp.concatenate([left[0], left[0], left[1]], axis=1), jnp.concatenate([right[0], right[1], right[0]], axis=0)
    )


def spread(left, right):
    right = right.astype(BF16)
    return dot(jnp.concatenate(split(left), axis=1), jnp.concatenate([right, right], axis=0))


def gelu(s):
    return 0.5 * s * (1.0 + jnp.tanh(ROOT * (s + CUBE * s * s * s)))


def gelu_slope(s):
    square = s * s
    t = jnp.tanh(ROOT * s * (1.0 + CUBE * square))
    return 0.5 * (1.0 + t) + 0.5 * s * (1.0 - t * t) * ROOT * (1.0 + 3.0 * CUBE * square)


def spread_groups(row):
    row = row + pltpu.roll(row, 64, 1)
    return row + pltpu.roll(row, 32, 1)


def fold(row):
    return spread_groups(row[:, :128] + row[:, 128:])


def wide(row):
    return jnp.concatenate([row, row], axis=1)


def group_of(rows=1, lanes=128):
    return lax.broadcasted_iota(jnp.int32, (rows, lanes), 1) // C


def column_sum(value):
    return jnp.sum(value, axis=0, keepdims=True)


def moments(z, value, ref):
    center = fold(column_sum(value)) / z.here
    off = value - wide(center)
    both = jnp.concatenate([center, fold(column_sum(off * off))], axis=0)
    ref[...] = jnp.broadcast_to(both[None], ref.shape)


def merged(z, ref):
    gathered = ref[...]
    mean = jnp.mean(gathered, axis=0)
    center = mean[0:1]
    off = gathered[:, 0, :] - center
    variance = mean[1:2] / z.here + jnp.mean(off * off, axis=0, keepdims=True)
    return wide(center), wide(lax.rsqrt(variance + norm_eps))


def put_halves(ref, value):
    ref[0] = value[:, :128]
    ref[1] = value[:, 128:]


def whole(ref):
    return jnp.concatenate([ref[0], ref[1]], axis=1)


def to_matrix(z, refs, half):
    for k in (0, 1):
        for j in range(z.blocks[k]):
            at = z.start[k] + j * z.step[k]
            for i in range(z.images[k]):
                for h in (0, 1):
                    half[h, pl.ds(at + i * z.rows[k], z.rows[k]), :] = refs[k][i, :, pl.ds(LANES * j + 128 * h, 128)]


def from_matrix(z, half, refs):
    for k in (0, 1):
        for j in range(z.blocks[k]):
            at = z.start[k] + j * z.step[k]
            for i in range(z.images[k]):
                for h in (0, 1):
                    refs[k][i, :, pl.ds(LANES * j + 128 * h, 128)] = half[h, pl.ds(at + i * z.rows[k], z.rows[k]), :]


def take_rims(z, half, depth, bottom, top):
    for k in (0, 1):
        for d in range(1, depth + 1):
            to_bottom = pl.ds((depth - d) * z.rims + z.rim[k], z.edge[k])
            to_top = pl.ds((d - 1) * z.rims + z.rim[k], z.edge[k])
            if d <= z.rows[k]:
                bottom[to_bottom, :] = half[pl.ds(z.start[k] + z.rows[k] - d, z.edge[k], stride=z.rows[k]), :]
                top[to_top, :] = half[pl.ds(z.start[k] + d - 1, z.edge[k], stride=z.rows[k]), :]
            else:
                bottom[to_bottom, :] = jnp.zeros((z.edge[k], 128), F32)
                top[to_top, :] = jnp.zeros((z.edge[k], 128), F32)


def inside(z, depth, above):
    at = lax.axis_index("row")
    large = lax.broadcasted_iota(jnp.int32, (z.rims, 1), 0) < z.rim[0]
    parts = []
    for n in range(depth):
        if above:
            ok = [jnp.where(at * rows >= depth - n, 1.0, 0.0) for rows in z.rows]
        else:
            ok = [jnp.where((at + 1) * rows + n + 1 <= height, 1.0, 0.0) for rows, height in zip(z.rows, HEIGHTS)]
        parts.append(jnp.where(large, ok[1], ok[0]).astype(F32))
    return jnp.concatenate(parts, axis=0)


def fill_center(z, pads, value):
    for k in (0, 1):
        ref, step, count = pads[k], z.step[k], z.count[k]
        for h in (0, 1):
            ref[1, h, pl.ds(0, step), :] = jnp.zeros((step, 128), F32)
            ref[1, h, pl.ds(step, count), :] = value[z.start[k] : z.start[k] + count, 128 * h : 128 * h + 128]
            ref[1, h, pl.ds(step + count, step), :] = jnp.zeros((step, 128), F32)


def fill_shifted(z, pads, above, below):
    for k in (0, 1):
        ref, step, count, rows = pads[k], z.step[k], z.count[k], z.rows[k]
        rim = slice(z.rim[k], z.rim[k] + z.edge[k])
        for h in (0, 1):
            lanes = slice(128 * h, 128 * h + 128)
            ref[0, h, pl.ds(step, count), :] = ref[1, h, pl.ds(step - 1, count), :]
            ref[2, h, pl.ds(step, count), :] = ref[1, h, pl.ds(step + 1, count), :]
            ref[0, h, pl.ds(step, z.edge[k], stride=rows), :] = above[rim, lanes]
            ref[2, h, pl.ds(step + rows - 1, z.edge[k], stride=rows), :] = below[rim, lanes]


def fill_pads(z, pads, value, above, below):
    fill_center(z, pads, value)
    fill_shifted(z, pads, above, below)
    for k in (0, 1):
        ref, step, count = pads[k], z.step[k], z.count[k]
        for h in (0, 1):
            for a in (0, 2):
                ref[a, h, pl.ds(0, step), :] = jnp.zeros((step, 128), F32)
                ref[a, h, pl.ds(step + count, step), :] = jnp.zeros((step, 128), F32)


def band_operand(z, pads, taps=range(TAPS)):
    lane = lax.broadcasted_iota(jnp.int32, (1, 128), 1)
    parts = []
    for k in (1, 0):
        ref, step, count = pads[k], z.step[k], z.count[k]
        columns = []
        for a in taps:
            before = ref[a, 1, pl.ds(0, count), :]
            after = ref[a, 0, pl.ds(2 * step, count), :]
            columns += [
                ref[a, 0, pl.ds(step, count), :],
                ref[a, 1, pl.ds(step, count), :],
                jnp.where(lane >= 96, before, jnp.where(lane < 32, after, 0.0)),
            ]
        parts.append(jnp.concatenate(columns, axis=1))
    return jnp.concatenate(parts, axis=0)


def rim_operand(z, chain, depth):
    rows, g = (depth + 1) * z.rims, z.guard
    lane = lax.broadcasted_iota(jnp.int32, (1, 128), 1)
    m = lax.broadcasted_iota(jnp.int32, (z.rims, 1), 0)
    large = m < z.rim[0]
    has_before = jnp.where(large, m, m - z.rim[0]) >= jnp.where(large, z.images[1], z.images[0])
    has_after = m < jnp.where(large, z.rim[0] - z.images[1], z.rims - z.images[0])
    take = [(lane >= 96) & has_before & large, (lane >= 96) & has_before & ~large, (lane < 32) & has_after & large, (lane < 32) & has_after & ~large]
    columns = []
    for r in range(depth + 1):
        at = g + r * z.rims
        edge = jnp.zeros((z.rims, 128), F32)
        for mask, half, shift in zip(take, (1, 1, 0, 0), (-z.images[1], -z.images[0], z.images[1], z.images[0])):
            edge = jnp.where(mask, chain[half, pl.ds(at + shift, z.rims), :], edge)
        columns.append(jnp.concatenate([chain[0, pl.ds(at, z.rims), :], chain[1, pl.ds(at, z.rims), :], edge], axis=1))
    return jnp.concatenate(
        [jnp.concatenate(columns[n : n + TAPS], axis=1) for n in range(depth - 1)], axis=0
    )


def convolve(z, own, above, below, depth, pads, chains, weight):
    r = z.rims
    fill_pads(z, pads, own, above[(depth - 1) * r :], below[:r])
    parts = [band_operand(z, pads)]
    if depth > 1:
        for side, (rim, chain) in enumerate(zip((above, below), chains)):
            rim_at, own_at = (z.guard, z.guard + depth * r) if side == 0 else (z.guard + r, z.guard)
            for h in (0, 1):
                chain[h, pl.ds(rim_at, depth * r), :] = rim[:, 128 * h : 128 * h + 128]
                for k in (0, 1):
                    row = z.step[k] + (0 if side == 0 else z.rows[k] - 1)
                    chain[h, pl.ds(own_at + z.rim[k], z.edge[k]), :] = pads[k][1, h, pl.ds(row, z.edge[k], stride=z.rows[k]), :]
            parts.append(rim_operand(z, chain, depth))
    result = product(split(jnp.concatenate(parts, axis=0)), (weight_matrix(weight.at[0]), weight_matrix(weight.at[1])))
    n = z.total + (depth - 1) * r
    return result[: z.total], result[z.total : n], result[n:]


def image_sums(z, value):
    slot = lax.broadcasted_iota(jnp.int32, (z.slots, 1), 0)
    sums = jnp.zeros((z.slots, 128), F32)
    for k in (0, 1):
        line = value[z.start[k] : z.start[k] + z.step[k]]
        for j in range(1, z.blocks[k]):
            at = z.start[k] + j * z.step[k]
            line = line + value[at : at + z.step[k]]
        image = lax.broadcasted_iota(jnp.int32, (z.step[k], 1), 0) // z.rows[k]
        for i in range(z.images[k]):
            sums = jnp.where(slot == i + k * z.images[0], column_sum(jnp.where(image == i, line, 0.0)), sums)
    return sums


def image_rows(z, values, rims):
    parts = []
    for k in (1, 0):
        image = lax.broadcasted_iota(jnp.int32, (z.step[k], 1), 0) // z.rows[k]
        line = jnp.zeros((z.step[k], 128), F32)
        for i in range(z.images[k]):
            at = i + k * z.images[0]
            line = jnp.where(image == i, values[at : at + 1], line)
        parts += [line] * z.blocks[k]
    if rims:
        m = lax.broadcasted_iota(jnp.int32, (z.rims, 1), 0)
        image = jnp.where(m < z.rim[0], z.images[0] + m % z.images[1], (m - z.rim[0]) % z.images[0])
        line = jnp.zeros((z.rims, 128), F32)
        for at in range(sum(z.images)):
            line = jnp.where(image == at, values[at : at + 1], line)
        parts += [line] * rims
    return jnp.concatenate(parts, axis=0)


def channel_mean():
    a = lax.broadcasted_iota(jnp.int32, (LANES, 128), 0) // C
    b = lax.broadcasted_iota(jnp.int32, (LANES, 128), 1)
    return jnp.where(a == b, 1.0 / C, 0.0).astype(F32)


def to_channels():
    a = lax.broadcasted_iota(jnp.int32, (128, LANES), 0)
    b = lax.broadcasted_iota(jnp.int32, (128, LANES), 1) // C
    return jnp.where(a == b, 1.0, 0.0).astype(F32)


def attention(value):
    return spread(value * value, channel_mean())


def start_all(copies):
    for copy in copies:
        copy.start()


def wait_all(copies):
    for copy in copies:
        copy.wait()


def start_kernel(z, small, large, up_s, up_l, t_s, t_l, x, bottom, top, copies, raw, half, sems):
    loads = [pltpu.make_async_copy(a, b, sems.at[n]) for n, (a, b) in enumerate(zip((small, large, up_s, up_l, t_s, t_l), raw))]
    start_all(loads)
    r, n = z.rims, REACH * z.rims
    tail = n + 2 * r
    for ref in (bottom, top):
        ref[pl.ds(tail, z.slots), :] = jnp.zeros((z.slots, LANES), F32)
    wait_all(loads[:2])
    to_matrix(z, raw[:2], half)
    value = whole(half)
    x[...] = value
    moments(z, value, copies)
    for h in (0, 1):
        lanes = pl.ds(128 * h, 128)
        take_rims(z, half.at[h], REACH, bottom.at[pl.ds(0, n), lanes], top.at[pl.ds(0, n), lanes])
    wait_all(loads[2:])
    for k in (0, 1):
        width, rows = HEIGHTS[k], z.rows[k]
        for i in range(z.images[k]):
            slot = pl.ds(tail + i + k * z.images[0], 1)
            for d in (0, 1):
                to_bottom, to_top = n + (1 - d) * r + z.rim[k] + i, n + d * r + z.rim[k] + i
                for j in range(z.blocks[k]):
                    lanes, at = pl.ds(LANES * j, LANES), j * z.images[k]
                    if d < rows:
                        bottom[pl.ds(to_bottom + at, 1), :] = raw[2 + k][i, pl.ds(rows - 1 - d, 1), lanes]
                        top[pl.ds(to_top + at, 1), :] = raw[2 + k][i, pl.ds(d, 1), lanes]
                    else:
                        bottom[pl.ds(to_bottom + at, 1), :] = jnp.zeros((1, LANES), F32)
                        top[pl.ds(to_top + at, 1), :] = jnp.zeros((1, LANES), F32)
                if d < rows:
                    bottom[slot, pl.ds(128 * (1 - d), width)] = raw[4 + k][i, pl.ds(rows - 1 - d, 1), :]
                    top[slot, pl.ds(128 * d, width)] = raw[4 + k][i, pl.ds(d, 1), :]


def banded(taps, ref):
    row = lax.broadcasted_iota(jnp.int32, (128, 128), 0) // C
    lane = group_of(128)
    for a in range(TAPS):
        main = jnp.zeros((128, 128), F32)
        for b in range(TAPS):
            main = jnp.where(row - lane + 1 == b, taps[a][b], main)
        before = jnp.where(lane[:C] == 0, taps[a][0][:C], 0.0)
        after = jnp.where(lane[:C] == 3, taps[a][2][:C], 0.0)
        for n, part in enumerate(split(jnp.concatenate([main, before, after], axis=0))):
            ref[n, pl.ds(a * TAP_ROWS, TAP_ROWS), :] = part


def weight_matrix(ref):
    rows = []
    zeros = jnp.zeros((128 - C, 128), BF16)
    for a in range(TAPS):
        at = a * TAP_ROWS
        main = ref[pl.ds(at, 128), :]
        before = jnp.concatenate([zeros, ref[pl.ds(at + 128, C), :]], axis=0)
        after = jnp.concatenate([ref[pl.ds(at + 128 + C, C), :], zeros], axis=0)
        rows += [
            jnp.concatenate([main, before], axis=1),
            jnp.concatenate([after, main], axis=1),
            jnp.concatenate([before, after], axis=1),
        ]
    return jnp.concatenate(rows, axis=0)


def prepare_kernel(z, first, second, up_s, up_l, t_s, t_l, g1, b1, g2, b2, x, w1, w2, weights, affine, upstream, teacher, x_copy, raw, kept, kept_u, rows, half, sems):
    targets = tuple(raw) + tuple(rows.at[pl.ds(n, 1), :] for n in range(4))
    refs = (first, second, up_s, up_l, t_s, t_l, g1, b1, g2, b2)
    loads = [pltpu.make_async_copy(a, b, sems.at[n]) for n, (a, b) in enumerate(zip(refs, targets))]
    start_all(loads)
    stores = [pltpu.make_async_copy(x, x_copy, sems.at[13])]
    stores[0].start()
    wait_all(loads)
    to_matrix(z, raw[2:4], half)
    kept_u[...] = whole(half)
    stores.append(pltpu.make_async_copy(kept_u, upstream, sems.at[10]))
    stores[1].start()
    for n, (source, forward) in enumerate(zip(raw[:2], (w1, w2))):
        tiles = []
        for a in range(TAPS):
            line = [jnp.concatenate([source[a, b]] * 4, axis=1) for b in range(TAPS)]
            tiles.append([jnp.concatenate([tap] * 4, axis=0) for tap in line])
        turned = [[tiles[TAPS - 1 - a][TAPS - 1 - b].T for b in range(TAPS)] for a in range(TAPS)]
        banded(tiles, forward)
        banded(turned, kept.at[n])
        stores.append(pltpu.make_async_copy(kept.at[n], weights.at[n], sems.at[11 + n]))
        stores[-1].start()
    affine[...] = jnp.concatenate([rows[...]] * BLOCK, axis=1)
    teacher[...] = jnp.zeros(teacher.shape, F32)
    for k, ref in ((0, raw[4]), (1, raw[5])):
        for i in range(z.images[k]):
            line = ref[i]
            for j in range(z.blocks[k]):
                at = z.start[k] + j * z.step[k] + i * z.rows[k]
                teacher[pl.ds(at, z.rows[k]), pl.ds(0, BLOCK)] = line[:, j * BLOCK : (j + 1) * BLOCK]
    wait_all(stores)


def normed_by(stats):
    return lambda v: (v - stats[0:1]) * stats[1:2]


def activation(center, scale, gain, bias):
    factor = scale * gain
    offset = bias - center * factor
    return lambda v: gelu(v * factor + offset)


def first_kernel(z, x, above, below, gathered, affine, weight, hidden, h_above, h_below, stats, copies, pads, chains):
    n = REACH * z.rims
    center, scale = merged(z, gathered)
    act = activation(center, scale, affine[0:1], affine[1:2])
    own = act(x[...])
    up, down = act(above[pl.ds(0, n), :]) * inside(z, 4, True), act(below[pl.ds(0, n), :]) * inside(z, 4, False)
    own, up, down = convolve(z, own, up, down, 4, pads, chains, weight)
    moments(z, own, copies)
    hidden[...] = own
    h_above[...] = up
    h_below[...] = down
    stats[0:1] = center
    stats[1:2] = scale


def second_kernel(z, hidden, h_above, h_below, gathered, affine, weight, x, x_above, x_below, teacher, out, o_above, o_below, near, stats, copies, pads, chains):
    center, scale = merged(z, gathered)
    act = activation(center, scale, affine[2:3], affine[3:4])
    r = z.rims
    own = act(hidden[...])
    up, down = act(h_above[...]) * inside(z, 3, True), act(h_below[...]) * inside(z, 3, False)
    own, up, down = convolve(z, own, up, down, 3, pads, chains, weight)
    own = x[...] + own
    amap = attention(own)
    sums = image_sums(z, amap * amap) + pltpu.roll(image_sums(z, amap * teacher[...]), 64, 1)
    copies[...] = jnp.broadcast_to(sums[None], copies.shape)
    out[...] = own
    o_above[...] = x_above[pl.ds(2 * r, 2 * r), :] + up
    o_below[...] = x_below[pl.ds(0, 2 * r), :] + down
    near[0] = h_above[pl.ds(2 * r, r), :]
    near[1] = h_below[pl.ds(0, r), :]
    stats[0:1] = center
    stats[1:2] = scale


def tap_rows(q):
    return 128 + 3 * C if q < 0 else 128 if q == 4 else q * C


def tap_product(z, operand, own, above, below, pads):
    fill_center(z, pads, own)
    fill_shifted(z, pads, above, below)
    columns = []
    for a in range(TAPS):
        columns.append(
            jnp.concatenate([pads[k][TAPS - 1 - a, h, pl.ds(z.step[k], z.count[k]), :] for h in (0, 1) for k in (1, 0)], axis=0)
        )
    return product(operand, split(jnp.concatenate(columns, axis=1)))


def tap_sums(result, tiles, first_group):
    group = group_of()
    for a in range(TAPS):
        for b in range(TAPS):
            total = None
            for p in range(4):
                at = tap_rows(p + b - 1)
                part = result[at : at + C, 128 * a : 128 * a + 128]
                total = part if total is None else jnp.where(group == p, part, total)
            tile, slot = divmod(first_group + a * TAPS + b, 4)
            tiles[tile] = jnp.where(group == slot, spread_groups(total), tiles[tile])


def tap_counts(z, turned, tiles, first_group):
    group = group_of()
    m = lax.broadcasted_iota(jnp.int32, (1, 2 * z.total), 1) % z.total
    row = jnp.where(m < z.start[0], m % z.rows[1], (m - z.start[0]) % z.rows[0])
    height = jnp.where(m < z.start[0], z.rows[1], z.rows[0])
    at = lax.axis_index("row")
    lost = {
        0: (row == height - 1) & (at == z.peers - 1),
        2: (row == 0) & (at == 0),
    }
    for a in range(TAPS):
        column = jnp.sum(jnp.where(lost[a], 0.0, turned) if a in lost else turned, axis=1, keepdims=True)
        for b in range(TAPS):
            total = sum(column[tap_rows(p + b - 1) : tap_rows(p + b - 1) + C] for p in range(4))
            tile, slot = divmod(first_group + a * TAPS + b, 4)
            tiles[tile] = jnp.where(group == slot, total, tiles[tile])


def turned_operand(z, value, pads, kept):
    fill_center(z, pads, value)
    lane = lax.broadcasted_iota(jnp.int32, (1, 128), 1)
    halves = ([], [])
    for k in (1, 0):
        ref, step, count = pads[k], z.step[k], z.count[k]
        low, high = ref[1, 0, pl.ds(step, count), :], ref[1, 1, pl.ds(step, count), :]
        before, after = ref[1, 1, pl.ds(0, count), :], ref[1, 0, pl.ds(2 * step, count), :]
        for part, main, left, right in ((halves[0], low, before, high), (halves[1], high, low, after)):
            part.append(jnp.concatenate([main, jnp.where(lane >= 96, left, jnp.where(lane < 32, right, 0.0))], axis=1))
    turned = jnp.concatenate(halves[0] + halves[1], axis=0).T
    parts = split(turned)
    for n in (0, 1):
        kept[n] = parts[n]
    return turned


def first_operand_kernel(z, x, hidden, h_above, h_below, above, below, stats, affine, teacher, upstream, weights, left, packed, teachers, spread_u, near_u, pads, chains, kept, kept_w, kept_u, pixels, kept_t, kept_c, kept_packed, sems):
    r, own = z.rims, pl.ds(0, z.total)
    loads = [pltpu.make_async_copy(upstream, kept_u.at[own, :], sems.at[0]), pltpu.make_async_copy(weights.at[1], kept_w, sems.at[1])]
    start_all(loads)
    act = activation(stats[0:1], stats[1:2], affine[0:1], affine[1:2])
    value = turned_operand(z, act(x[...]), pads, kept)
    stores = [pltpu.make_async_copy(kept, left, sems.at[2])]
    stores[0].start()
    tiles = [jnp.zeros((C, 128), F32) for _ in range(BACK_LANES // 128)]
    tap_counts(z, value, tiles, ONES)
    result = tap_product(
        z, (kept[0], kept[1]), hidden[...], h_above[pl.ds(2 * r, r), :] * inside(z, 1, True), h_below[pl.ds(0, r), :] * inside(z, 1, False), pads
    )
    tap_sums(result, tiles, HIDDEN)
    kept_packed[...] = jnp.concatenate(tiles, axis=1)
    stores.append(pltpu.make_async_copy(kept_packed, packed, sems.at[6]))
    stores[1].start()
    pixels[own, :] = teacher[...]
    pixels[pl.ds(z.total, 4 * r), :] = jnp.zeros((4 * r, 128), F32)
    n = (REACH + 2) * r
    for side, ref in enumerate((above, below)):
        for d in (0, 1):
            for k in (0, 1):
                line = ref[pl.ds(n + k * z.images[0], z.images[k]), pl.ds(128 * d, 128)]
                for j in range(z.blocks[k]):
                    at = z.total + (2 * side + d) * r + z.rim[k] + j * z.images[k]
                    pixels[pl.ds(at, z.images[k]), pl.ds(0, BLOCK)] = line[:, j * BLOCK : (j + 1) * BLOCK]
    kept_t[...] = spread(pixels[...], to_channels())
    stores.append(pltpu.make_async_copy(kept_t, teachers, sems.at[3]))
    stores[2].start()
    n = REACH * r
    up, down = above[pl.ds(n, 2 * r), :] * inside(z, 2, True), below[pl.ds(n, 2 * r), :] * inside(z, 2, False)
    kept_u[pl.ds(z.total, r), :] = up[r:]
    kept_u[pl.ds(z.total + r, r), :] = down[:r]
    wait_all(loads)
    stores.append(pltpu.make_async_copy(kept_u, near_u, sems.at[5]))
    stores[3].start()
    kept_c[...] = jnp.concatenate(convolve(z, kept_u[own, :], up, down, 2, pads, chains, kept_w), axis=0)
    stores.append(pltpu.make_async_copy(kept_c, spread_u, sems.at[4]))
    stores[4].start()
    wait_all(stores)


def second_operand_kernel(z, hidden, near, stats, affine, out, o_above, o_below, teachers, spread_u, near_u, weights, out_copy, hidden_copy, left, shifts, by_map, by_teacher, up, pads, chains, kept_t, kept_u, kept_w, kept_s, sems):
    r, total = z.rims, z.total
    loads = [
        pltpu.make_async_copy(teachers, kept_t, sems.at[0]),
        pltpu.make_async_copy(weights.at[1], kept_w, sems.at[1]),
        pltpu.make_async_copy(spread_u, kept_u, sems.at[2]),
    ]
    start_all(loads)
    stores = [
        pltpu.make_async_copy(out, out_copy, sems.at[4]),
        pltpu.make_async_copy(hidden, hidden_copy.at[pl.ds(0, total), :], sems.at[7]),
        pltpu.make_async_copy(near.at[0], hidden_copy.at[pl.ds(total, r), :], sems.at[8]),
        pltpu.make_async_copy(near.at[1], hidden_copy.at[pl.ds(total + r, r), :], sems.at[9]),
        pltpu.make_async_copy(near_u, up, sems.at[10]),
    ]
    start_all(stores)
    normed = normed_by(stats)(jnp.concatenate([hidden[...], near[0], near[1]], axis=0))
    shifted = normed * affine[2:3] + affine[3:4]
    turned_operand(z, gelu(shifted[:total]), pads, left)
    ones = jnp.ones((total, 1), F32)
    masks = jnp.concatenate([ones, inside(z, 1, True), inside(z, 1, False)], axis=0)
    slopes = gelu_slope(shifted) * masks
    o = jnp.concatenate([out[...], o_above[...] * inside(z, 2, True), o_below[...] * inside(z, 2, False)], axis=0)
    for_map = spread(attention(o), to_channels()) * o
    wait_all(loads)
    for_teacher = kept_t[...] * o
    kept_s[0] = kept_u[...] * slopes
    for n, value, ref in ((1, for_map, by_map), (2, for_teacher, by_teacher)):
        own, before, after = value[:total], value[total : total + 2 * r], value[total + 2 * r :]
        ref[...] = jnp.concatenate([own, before[r:], after[:r]], axis=0)
        kept_s[n] = jnp.concatenate(convolve(z, own, before, after, 2, pads, chains, kept_w), axis=0) * slopes
    stores.append(pltpu.make_async_copy(kept_s, shifts, sems.at[5]))
    stores[-1].start()
    wait_all(stores)


def upstream_kernel(z, gathered, up, shifts, left_1, left_2, packed, by_map, by_teacher, hidden, stats, dout, dshift, d_above, d_below, slabs, kept_s, kept_left, kept_h, kept_packed, pads, sems):
    r, total = z.rims, z.total
    loads = [
        pltpu.make_async_copy(a, b, sems.at[n])
        for n, (a, b) in enumerate(((shifts, kept_s), (left_1, kept_left), (hidden.at[pl.ds(0, total), :], kept_h), (packed, kept_packed)))
    ]
    start_all(loads)
    lane = lax.broadcasted_iota(jnp.int32, (z.slots, 128), 1)
    sums = jnp.sum(gathered[...], axis=0)
    square = jnp.sum(jnp.where(lane < 64, sums, 0.0), axis=1, keepdims=True)
    cross = jnp.sum(jnp.where(lane < 64, 0.0, sums), axis=1, keepdims=True)
    inverse = lax.rsqrt(square + map_eps)
    inner = beta_weight * (square * inverse - cross) * inverse
    shape = (z.slots, 128)
    for_map = (beta_weight - inner) * inverse * inverse * (2.0 / C)
    for_teacher = beta_weight * inverse * (2.0 / C)
    for_map, for_teacher = (wide(image_rows(z, jnp.broadcast_to(v, shape), 2)) for v in (for_map, for_teacher))
    value = up[...] + for_map * by_map[...] - for_teacher * by_teacher[...]
    dout[...] = value[:total]
    second = tap_product(z, (left_2[0], left_2[1]), value[:total], value[total : total + r], value[total + r :], pads)
    loads[0].wait()
    shift = kept_s[0] + for_map * kept_s[1] - for_teacher * kept_s[2]
    pre, above, below = shift[:total], shift[total : total + r], shift[total + r :]
    dshift[...] = pre
    d_above[...] = above
    d_below[...] = below
    loads[1].wait()
    first = tap_product(z, (kept_left[0], kept_left[1]), pre, above, below, pads)
    wait_all(loads[2:])
    normed = normed_by(stats)(kept_h[...])
    tiles = [kept_packed[:, 128 * n : 128 * n + 128] for n in range(BACK_LANES // 128)]
    group = group_of()
    tiles[0] = jnp.where(group == BIAS, fold(column_sum(pre)), jnp.where(group == GAIN, fold(column_sum(pre * normed)), tiles[0]))
    tap_sums(second, tiles, SECOND)
    tap_sums(first, tiles, LEFT)
    line = jnp.concatenate(tiles, axis=1)
    for d in range(z.devices):
        slabs[d] = line[d % C : d % C + 1]


def write_kernel(z, out, x, hidden, weights, first_stats, stats, order, out_s, out_l, first_normed, normed, weight, kept, kept_x, kept_h, half, sems):
    loads = [pltpu.make_async_copy(a, b, sems.at[n]) for n, (a, b) in enumerate(((out, kept), (x, kept_x), (hidden, kept_h), (weights.at[0], weight)))]
    start_all(loads)
    loads[0].wait()
    put_halves(half, kept[...])
    from_matrix(z, half, (out_s, out_l))
    loads[1].wait()
    first_normed[...] = normed_by(first_stats)(kept_x[...])
    loads[2].wait()
    normed[...] = normed_by(stats)(kept_h[...])
    loads[3].wait()


def norm_sums(total):
    group = group_of()
    return [wide(spread_groups(jnp.where(group == n, total[:, :128], 0.0))) for n in (BIAS, GAIN)]


def hidden_kernel(z, gathered, dshift, d_above, d_below, second_normed, stats, affine, weight, first_normed, pre_ref, gain_out, bias_out, slabs, pads):
    total = jnp.sum(gathered[...], axis=0)
    bias_sum, gain_sum = norm_sums(total)
    bias_out[...] = bias_sum[:, :C]
    gain_out[...] = gain_sum[:, :C]
    bias_mean, gain_mean = bias_sum / z.pixels, gain_sum / z.pixels
    factor = affine[2:3] * stats[1:2]
    r, total_rows = z.rims, z.total

    def back(d, normed):
        return factor * (d - bias_mean - normed * gain_mean)

    own = back(dshift[...], second_normed[pl.ds(0, total_rows), :])
    up = back(d_above[...], second_normed[pl.ds(total_rows, r), :]) * inside(z, 1, True)
    down = back(d_below[...], second_normed[pl.ds(total_rows + r, r), :]) * inside(z, 1, False)
    grad, _, _ = convolve(z, own, up, down, 1, pads, None, weight)
    normed = first_normed[...]
    pre = grad * gelu_slope(normed * affine[0:1] + affine[1:2])
    pre_ref[...] = pre
    lane = lax.broadcasted_iota(jnp.int32, (1, 128), 1)
    taps = TAPS * TAPS * C

    def along(row):
        return jnp.concatenate([row[:, :128]] * 3, axis=1)[:, :taps]

    second, left, against, ones = (total[:, n * C : n * C + taps] for n in (SECOND, LEFT, HIDDEN, ONES))
    against = along(stats[1:2]) * (against - along(stats[0:1]) * ones)
    first = along(factor) * (left - along(bias_mean) * ones - along(gain_mean) * against)
    sums = jnp.where(lane < C, fold(column_sum(pre)), fold(column_sum(pre * normed)))
    line = jnp.concatenate([sums[:, : 2 * C], second, first], axis=1)
    slabs[...] = jnp.broadcast_to(line[None], slabs.shape)


def back_kernel(z, gathered, pre, normed, stats, affine, dout, back_s, back_l, one, two, gain_out, bias_out, half, lines):
    bias_sum, gain_sum = norm_sums(jnp.sum(gathered[:, :, pl.ds(0, 128)], axis=0))
    bias_out[...] = bias_sum[:, :C]
    gain_out[...] = gain_sum[:, :C]
    value = dout[...] + affine[0:1] * stats[1:2] * (pre[...] - bias_sum / z.pixels - normed[...] * (gain_sum / z.pixels))
    put_halves(half, value)
    from_matrix(z, half, (back_s, back_l))
    for d in range(C):
        lines[pl.ds(d, 1), :] = gathered[d]
    for ref, group in ((two, LAST_SECOND), (one, LAST_FIRST)):
        for a in range(TAPS):
            for b in range(TAPS):
                at = (group + a * TAPS + b) * C
                ref[a, b] = lines[:, pl.ds(at, C)]


def call(body, ins, outs, scratch=(), sems=0):
    space = {"v": pltpu.VMEM, "h": pltpu.HBM, "V": pltpu.VMEM}
    shapes = []
    for item in scratch:
        if isinstance(item, list):
            shapes.append([pltpu.VMEM(*s) for s in item])
        else:
            shapes.append(pltpu.VMEM(*item))
    if sems:
        shapes.append(pltpu.SemaphoreType.DMA((sems,)))
    run = pl.pallas_call(
        body,
        out_shape=[jax.ShapeDtypeStruct(shape, kind) if s == "v" else space[s](shape, kind) for s, shape, kind in outs],
        in_specs=[pl.BlockSpec(memory_space=space[s]) for s in ins],
        out_specs=[pl.BlockSpec(memory_space=space[s]) for s, _, _ in outs],
        scratch_shapes=shapes,
        compiler_params=pltpu.CompilerParams(vmem_limit_bytes=VMEM_LIMIT),
    )
    return lambda *args: run(
        *(pltpu.with_memory_space_constraint(arg, pltpu.HBM) if s == "h" else arg for s, arg in zip(ins, args))
    )


def exchange(copies, axes):
    return lax.all_to_all(copies, axes, 0, 0, tiled=True)


def beyond(z, bottom, top, depths):
    hops = max(-(-depth // rows) for rows in z.rows for depth in depths)
    above, below = [], []
    for hop in range(1, hops + 1):
        above.append(lax.ppermute(bottom, "row", [(i, i + hop) for i in range(z.peers - hop)]))
        below.append(lax.ppermute(top, "row", [(i + hop, i) for i in range(z.peers - hop)]))
    if hops == 1:
        return above[0], below[0]
    up, down = [], []
    base = 0
    for depth in depths:
        for n in range(depth):
            for k in (1, 0):
                hop, back = divmod(depth - 1 - n, z.rows[k])
                at = base + (depth - 1 - back) * z.rims + z.rim[k]
                up.append(above[hop][at : at + z.edge[k]])
                hop, back = divmod(n, z.rows[k])
                at = base + back * z.rims + z.rim[k]
                down.append(below[hop][at : at + z.edge[k]])
        base += depth * z.rims
    up.append(jnp.concatenate([pixel_rows(z, above, base, 1, 1), pixel_rows(z, above, base, 0, 1)], axis=1))
    down.append(jnp.concatenate([pixel_rows(z, below, base, 0, 0), pixel_rows(z, below, base, 1, 0)], axis=1))
    return jnp.concatenate(up, axis=0), jnp.concatenate(down, axis=0)


def pixel_rows(z, bands, base, distance, last):
    lines = []
    for k in (0, 1):
        hop, back = divmod(distance, z.rows[k])
        at = base + k * z.images[0]
        half = 128 * abs(last - back)
        lines.append(bands[hop][at : at + z.images[k], half : half + 128])
    lines.append(jnp.zeros((z.slots - sum(z.images), 128), F32))
    return jnp.concatenate(lines, axis=0)


def local(
    image_small, image_large, teacher_small, teacher_large, upstream_small, upstream_large,
    conv_first, gain_first, bias_first, conv_second, gain_second, bias_second,
):
    peers = lax.axis_size("row")
    devices = lax.axis_size("img") * peers
    z = Sizes(image_small.shape, image_large.shape, devices, peers)
    body = lambda function: functools.partial(function, z)
    r = z.rims
    full, half, pair = (z.total, LANES), (2, z.total, 128), (devices, 2, 128)
    weight, left = (2, TAPS * TAP_ROWS, 128), (2, 256, 2 * z.total)
    images = [image_small, image_large, upstream_small, upstream_large, teacher_small, teacher_large]
    f = lambda space, *shape: (space, shape, F32)
    depths = (REACH, 2)
    rim_rows = sum(depths) * r + z.slots

    x, bottom, top, copies = call(
        body(start_kernel),
        "hhhhhh",
        [("v", full, F32), f("v", rim_rows, LANES), f("v", rim_rows, LANES), ("V", pair, F32)],
        [[(a.shape, F32) for a in images], (half, F32)],
        6,
    )(*images)
    gathered = exchange(copies, AXES)
    above, below = beyond(z, bottom, top, depths)
    params = [conv_first, conv_second] + images[2:]
    w1, w2, weights, affine, upstream, teacher, x_copy = call(
        body(prepare_kernel),
        "hhhhhhhhhhv",
        [("v", weight, BF16), ("v", weight, BF16), ("h", (2,) + weight, BF16), f("v", 4, LANES), ("h", full, F32), f("v", z.total, 128), ("h", full, F32)],
        [[(a.shape, F32) for a in params], ((2,) + weight, BF16), (full, F32), ((4, C), F32), (half, F32)],
        14,
    )(*params, *(v.reshape(1, C) for v in (gain_first, bias_first, gain_second, bias_second)), x)

    hidden, h_above, h_below, stats_one, copies = call(
        body(first_kernel),
        "vvvvvv",
        [("v", full, F32), f("v", 3 * r, LANES), f("v", 3 * r, LANES), f("v", 2, LANES), ("V", pair, F32)],
        [z.pads(), z.chains(4)],
    )(x, above, below, gathered, affine, w1)
    gathered = exchange(copies, AXES)
    extended, near_rows = z.total + 4 * r, z.total + 2 * r
    left_one, packed, teachers, spread_u, near_u = call(
        body(first_operand_kernel),
        "vvvvvvvvvhh",
        [("h", left, BF16), f("h", C, BACK_LANES), f("h", extended, LANES), f("h", near_rows, LANES), f("h", near_rows, LANES)],
        [
            z.pads(), z.chains(2), (left, BF16), (weight, BF16), ((near_rows, LANES), F32), ((extended, 128), F32),
            ((extended, LANES), F32), ((near_rows, LANES), F32), ((C, BACK_LANES), F32),
        ],
        7,
    )(x, hidden, h_above, h_below, above, below, stats_one, affine, teacher, upstream, weights)
    gathered, near_u = lax.optimization_barrier((gathered, near_u))

    map_shape = (peers, z.slots, 128)
    out, o_above, o_below, near, stats_two, copies = call(
        body(second_kernel),
        "vvvvvvvvvv",
        [("v", full, F32), f("v", 2 * r, LANES), f("v", 2 * r, LANES), f("v", 2, r, LANES), f("v", 2, LANES), ("V", map_shape, F32)],
        [z.pads(), z.chains(3)],
    )(hidden, h_above, h_below, gathered, affine, w2, x, above, below, teacher)
    gathered = exchange(copies, ("row",))
    out_copy, hidden_copy, left_two, shifts, by_map, by_teacher, up = call(
        body(second_operand_kernel),
        "vvvvvvvhhhh",
        [
            ("h", full, F32), f("h", near_rows, LANES), ("v", left, BF16), f("h", 3, near_rows, LANES),
            f("v", near_rows, LANES), f("v", near_rows, LANES), f("v", near_rows, LANES),
        ],
        [
            z.pads(), z.chains(2), ((extended, LANES), F32), ((near_rows, LANES), F32), (weight, BF16),
            ((3, near_rows, LANES), F32),
        ],
        11,
    )(hidden, near, stats_two, affine, out, o_above, o_below, teachers, spread_u, near_u, weights)

    dout, dshift, d_above, d_below, slabs = call(
        body(upstream_kernel),
        "vvhhvhvvhv",
        [("v", full, F32), ("v", full, F32), f("v", r, LANES), f("v", r, LANES), f("V", devices, 1, BACK_LANES)],
        [((3, near_rows, LANES), F32), (left, BF16), (full, F32), ((C, BACK_LANES), F32), z.pads()],
        4,
    )(gathered, up, shifts, left_one, left_two, packed, by_map, by_teacher, hidden_copy, stats_two)
    gathered = exchange(slabs, AXES)
    out_s, out_l, first_normed, second_normed, weight_back = call(
        body(write_kernel),
        "hhhhvvv",
        [("v", image_small.shape, F32), ("v", image_large.shape, F32), ("v", full, F32), f("v", near_rows, LANES), ("v", weight, BF16)],
        [(full, F32), (full, F32), ((near_rows, LANES), F32), (half, F32)],
        4,
    )(out_copy, x_copy, hidden_copy, weights, stats_one, stats_two, d_above)

    pre, gain_two, bias_two, slabs = call(
        body(hidden_kernel),
        "vvvvvvvvv",
        [("v", full, F32), f("v", 1, C), f("v", 1, C), f("V", devices, 1, LAST_LANES)],
        [z.pads()],
    )(gathered, dshift, d_above, d_below, second_normed, stats_two, affine, weight_back, first_normed)
    gathered = exchange(slabs, AXES)

    back_s, back_l, one, two, gain_one, bias_one = call(
        body(back_kernel),
        "vvvvvv",
        [("v", a.shape, F32) for a in (image_small, image_large, conv_first, conv_second)] + [f("v", 1, C), f("v", 1, C)],
        [(half, F32), ((C, LAST_LANES), F32)],
    )(gathered, pre, first_normed, stats_one, affine, dout)
    return (
        out_s, out_l, back_s, back_l,
        one, gain_one.reshape(C), bias_one.reshape(C),
        two, gain_two.reshape(C), bias_two.reshape(C),
    )


def solution(mesh):
    split_bands, everywhere = P("img", "row", None), P()
    return jax.shard_map(
        local,
        mesh=mesh,
        in_specs=(split_bands,) * 6 + (everywhere,) * 6,
        out_specs=(split_bands,) * 4 + (everywhere,) * 6,
        check_vma=False,
    )
```

```python
import functools
import math

import jax
import jax.numpy as jnp
from jax import lax
from jax.experimental import pallas as pl
from jax.experimental.pallas import tpu as pltpu
from jax.sharding import PartitionSpec as P

C = 32
HS = 32
HL = 64
HEIGHTS = (HS, HL)

norm_eps = 1e-05
map_eps = 1e-06
beta_weight = 1000.0
AXES = ("img", "row")
BLOCK = 8
LANES = BLOCK * C
TAPS = 3
WIDTH = LANES + 128
DEPTH = TAPS * WIDTH
TAP_ROWS = 128 + 2 * C
REACH = 4
ROOT = math.sqrt(2.0 / math.pi)
CUBE = 0.044715
F32 = jnp.float32
BF16 = jnp.bfloat16
VMEM_LIMIT = 32 * 1024 * 1024
BIAS, GAIN, SECOND, LEFT, HIDDEN, ONES = 0, 1, 2, 11, 20, 29
BACK_LANES = 1280
LAST_SECOND, LAST_FIRST, LAST_LANES = 2, 11, 640


class Sizes:
    def __init__(self, small, large, devices, peers):
        self.images = (small[0], large[0])
        self.rows = (small[1], large[1])
        self.blocks = (HS // BLOCK, HL // BLOCK)
        self.step = tuple(n * r for n, r in zip(self.images, self.rows))
        self.count = tuple(b * s for b, s in zip(self.blocks, self.step))
        self.edge = tuple(b * n for b, n in zip(self.blocks, self.images))
        self.start = (self.count[1], 0)
        self.rim = (self.edge[1], 0)
        self.total = sum(self.count)
        self.rims = sum(self.edge)
        self.slots = -(-sum(self.images) // 8) * 8
        self.guard = -(-max(self.images) // 8) * 8
        self.devices = devices
        self.peers = peers
        self.here = float(self.total * BLOCK)
        self.pixels = self.here * devices

    def pads(self):
        return [((TAPS, 2, self.count[k] + 2 * self.step[k], 128), F32) for k in (0, 1)]

    def chains(self, depth):
        return [((2, 2 * self.guard + (depth + 1) * self.rims, 128), F32)] * 2


def split(value):
    high = value.astype(BF16)
    return high, (value - high.astype(F32)).astype(BF16)


def dot(left, right):
    return lax.dot_general(left, right, (((1,), (0,)), ((), ())), preferred_element_type=F32)


def product(left, right):
    if left[0].shape[1] % 128:
        return dot(left[0], right[0]) + (dot(left[0], right[1]) + dot(left[1], right[0]))
    return dot(
        jnp.concatenate([left[0], left[0], left[1]], axis=1), jnp.concatenate([right[0], right[1], right[0]], axis=0)
    )


def spread(left, right):
    right = right.astype(BF16)
    return dot(jnp.concatenate(split(left), axis=1), jnp.concatenate([right, right], axis=0))


def gelu(s):
    return 0.5 * s * (1.0 + jnp.tanh(ROOT * (s + CUBE * s * s * s)))


def gelu_slope(s):
    square = s * s
    t = jnp.tanh(ROOT * s * (1.0 + CUBE * square))
    return 0.5 * (1.0 + t) + 0.5 * s * (1.0 - t * t) * ROOT * (1.0 + 3.0 * CUBE * square)


def spread_groups(row):
    row = row + pltpu.roll(row, 64, 1)
    return row + pltpu.roll(row, 32, 1)


def fold(row):
    return spread_groups(row[:, :128] + row[:, 128:])


def wide(row):
    return jnp.concatenate([row, row], axis=1)


def group_of(rows=1, lanes=128):
    return lax.broadcasted_iota(jnp.int32, (rows, lanes), 1) // C


def column_sum(value):
    return jnp.sum(value, axis=0, keepdims=True)


def moments(z, value, ref):
    center = fold(column_sum(value)) / z.here
    off = value - wide(center)
    both = jnp.concatenate([center, fold(column_sum(off * off))], axis=0)
    ref[...] = jnp.broadcast_to(both[None], ref.shape)


def merged(z, ref):
    gathered = ref[...]
    mean = jnp.mean(gathered, axis=0)
    off = gathered - mean[None]
    between = jnp.mean(off * off, axis=0)
    variance = mean[1:2] / z.here + between[0:1]
    return wide(mean[0:1]), wide(lax.rsqrt(variance + norm_eps))


def put_halves(ref, value):
    ref[0] = value[:, :128]
    ref[1] = value[:, 128:]


def whole(ref):
    return jnp.concatenate([ref[0], ref[1]], axis=1)


def to_matrix(z, refs, half):
    for k in (0, 1):
        for j in range(z.blocks[k]):
            at = z.start[k] + j * z.step[k]
            for i in range(z.images[k]):
                for h in (0, 1):
                    half[h, pl.ds(at + i * z.rows[k], z.rows[k]), :] = refs[k][i, :, pl.ds(LANES * j + 128 * h, 128)]


def from_matrix(z, half, refs):
    for k in (0, 1):
        for j in range(z.blocks[k]):
            at = z.start[k] + j * z.step[k]
            for i in range(z.images[k]):
                for h in (0, 1):
                    refs[k][i, :, pl.ds(LANES * j + 128 * h, 128)] = half[h, pl.ds(at + i * z.rows[k], z.rows[k]), :]


def take_rims(z, half, depth, bottom, top):
    for k in (0, 1):
        for d in range(1, depth + 1):
            to_bottom = pl.ds((depth - d) * z.rims + z.rim[k], z.edge[k])
            to_top = pl.ds((d - 1) * z.rims + z.rim[k], z.edge[k])
            if d <= z.rows[k]:
                bottom[to_bottom, :] = half[pl.ds(z.start[k] + z.rows[k] - d, z.edge[k], stride=z.rows[k]), :]
                top[to_top, :] = half[pl.ds(z.start[k] + d - 1, z.edge[k], stride=z.rows[k]), :]
            else:
                bottom[to_bottom, :] = jnp.zeros((z.edge[k], 128), F32)
                top[to_top, :] = jnp.zeros((z.edge[k], 128), F32)


def inside(z, depth, above):
    at = lax.axis_index("row")
    large = lax.broadcasted_iota(jnp.int32, (z.rims, 1), 0) < z.rim[0]
    parts = []
    for n in range(depth):
        if above:
            ok = [jnp.where(at * rows >= depth - n, 1.0, 0.0) for rows in z.rows]
        else:
            ok = [jnp.where((at + 1) * rows + n + 1 <= height, 1.0, 0.0) for rows, height in zip(z.rows, HEIGHTS)]
        parts.append(jnp.where(large, ok[1], ok[0]).astype(F32))
    return jnp.concatenate(parts, axis=0)


def fill_center(z, pads, value):
    for k in (0, 1):
        ref, step, count = pads[k], z.step[k], z.count[k]
        for h in (0, 1):
            ref[1, h, pl.ds(0, step), :] = jnp.zeros((step, 128), F32)
            ref[1, h, pl.ds(step, count), :] = value[z.start[k] : z.start[k] + count, 128 * h : 128 * h + 128]
            ref[1, h, pl.ds(step + count, step), :] = jnp.zeros((step, 128), F32)


def fill_shifted(z, pads, above, below):
    for k in (0, 1):
        ref, step, count, rows = pads[k], z.step[k], z.count[k], z.rows[k]
        rim = slice(z.rim[k], z.rim[k] + z.edge[k])
        for h in (0, 1):
            lanes = slice(128 * h, 128 * h + 128)
            ref[0, h, pl.ds(step, count), :] = ref[1, h, pl.ds(step - 1, count), :]
            ref[2, h, pl.ds(step, count), :] = ref[1, h, pl.ds(step + 1, count), :]
            ref[0, h, pl.ds(step, z.edge[k], stride=rows), :] = above[rim, lanes]
            ref[2, h, pl.ds(step + rows - 1, z.edge[k], stride=rows), :] = below[rim, lanes]


def fill_pads(z, pads, value, above, below):
    fill_center(z, pads, value)
    fill_shifted(z, pads, above, below)
    for k in (0, 1):
        ref, step, count = pads[k], z.step[k], z.count[k]
        for h in (0, 1):
            for a in (0, 2):
                ref[a, h, pl.ds(0, step), :] = jnp.zeros((step, 128), F32)
                ref[a, h, pl.ds(step + count, step), :] = jnp.zeros((step, 128), F32)


def band_operand(z, pads, taps=range(TAPS)):
    lane = lax.broadcasted_iota(jnp.int32, (1, 128), 1)
    parts = []
    for k in (1, 0):
        ref, step, count = pads[k], z.step[k], z.count[k]
        columns = []
        for a in taps:
            before = ref[a, 1, pl.ds(0, count), :]
            after = ref[a, 0, pl.ds(2 * step, count), :]
            columns += [
                ref[a, 0, pl.ds(step, count), :],
                ref[a, 1, pl.ds(step, count), :],
                jnp.where(lane >= 96, before, jnp.where(lane < 32, after, 0.0)),
            ]
        parts.append(jnp.concatenate(columns, axis=1))
    return jnp.concatenate(parts, axis=0)


def rim_operand(z, chain, depth):
    rows, g = (depth + 1) * z.rims, z.guard
    lane = lax.broadcasted_iota(jnp.int32, (1, 128), 1)
    m = lax.broadcasted_iota(jnp.int32, (z.rims, 1), 0)
    large = m < z.rim[0]
    has_before = jnp.where(large, m, m - z.rim[0]) >= jnp.where(large, z.images[1], z.images[0])
    has_after = m < jnp.where(large, z.rim[0] - z.images[1], z.rims - z.images[0])
    take = [(lane >= 96) & has_before & large, (lane >= 96) & has_before & ~large, (lane < 32) & has_after & large, (lane < 32) & has_after & ~large]
    columns = []
    for r in range(depth + 1):
        at = g + r * z.rims
        edge = jnp.zeros((z.rims, 128), F32)
        for mask, half, shift in zip(take, (1, 1, 0, 0), (-z.images[1], -z.images[0], z.images[1], z.images[0])):
            edge = jnp.where(mask, chain[half, pl.ds(at + shift, z.rims), :], edge)
        columns.append(jnp.concatenate([chain[0, pl.ds(at, z.rims), :], chain[1, pl.ds(at, z.rims), :], edge], axis=1))
    return jnp.concatenate(
        [jnp.concatenate(columns[n : n + TAPS], axis=1) for n in range(depth - 1)], axis=0
    )


def convolve(z, own, above, below, depth, pads, chains, weight):
    r = z.rims
    fill_pads(z, pads, own, above[(depth - 1) * r :], below[:r])
    parts = [band_operand(z, pads)]
    if depth > 1:
        for side, (rim, chain) in enumerate(zip((above, below), chains)):
            rim_at, own_at = (z.guard, z.guard + depth * r) if side == 0 else (z.guard + r, z.guard)
            for h in (0, 1):
                chain[h, pl.ds(rim_at, depth * r), :] = rim[:, 128 * h : 128 * h + 128]
                for k in (0, 1):
                    row = z.step[k] + (0 if side == 0 else z.rows[k] - 1)
                    chain[h, pl.ds(own_at + z.rim[k], z.edge[k]), :] = pads[k][1, h, pl.ds(row, z.edge[k], stride=z.rows[k]), :]
            parts.append(rim_operand(z, chain, depth))
    result = product(split(jnp.concatenate(parts, axis=0)), (weight_matrix(weight.at[0]), weight_matrix(weight.at[1])))
    n = z.total + (depth - 1) * r
    return result[: z.total], result[z.total : n], result[n:]


def image_sums(z, value):
    slot = lax.broadcasted_iota(jnp.int32, (z.slots, 1), 0)
    sums = jnp.zeros((z.slots, 128), F32)
    for k in (0, 1):
        line = value[z.start[k] : z.start[k] + z.step[k]]
        for j in range(1, z.blocks[k]):
            at = z.start[k] + j * z.step[k]
            line = line + value[at : at + z.step[k]]
        image = lax.broadcasted_iota(jnp.int32, (z.step[k], 1), 0) // z.rows[k]
        for i in range(z.images[k]):
            sums = jnp.where(slot == i + k * z.images[0], column_sum(jnp.where(image == i, line, 0.0)), sums)
    return sums


def image_rows(z, values, rims):
    parts = []
    for k in (1, 0):
        image = lax.broadcasted_iota(jnp.int32, (z.step[k], 1), 0) // z.rows[k]
        line = jnp.zeros((z.step[k], 128), F32)
        for i in range(z.images[k]):
            at = i + k * z.images[0]
            line = jnp.where(image == i, values[at : at + 1], line)
        parts += [line] * z.blocks[k]
    if rims:
        m = lax.broadcasted_iota(jnp.int32, (z.rims, 1), 0)
        image = jnp.where(m < z.rim[0], z.images[0] + m % z.images[1], (m - z.rim[0]) % z.images[0])
        line = jnp.zeros((z.rims, 128), F32)
        for at in range(sum(z.images)):
            line = jnp.where(image == at, values[at : at + 1], line)
        parts += [line] * rims
    return jnp.concatenate(parts, axis=0)


def channel_mean():
    a = lax.broadcasted_iota(jnp.int32, (LANES, 128), 0) // C
    b = lax.broadcasted_iota(jnp.int32, (LANES, 128), 1) % 64
    return jnp.where(a == b, 1.0 / C, 0.0).astype(F32)


def to_channels():
    a = lax.broadcasted_iota(jnp.int32, (128, LANES), 0)
    b = lax.broadcasted_iota(jnp.int32, (128, LANES), 1) // C
    return jnp.where(a == b, 1.0, 0.0).astype(F32)


def attention(value):
    return spread(value * value, channel_mean())


def start_all(copies):
    for copy in copies:
        copy.start()


def wait_all(copies):
    for copy in copies:
        copy.wait()


def start_kernel(z, small, large, up_s, up_l, t_s, t_l, x, bottom, top, copies, raw, half, sems):
    loads = [pltpu.make_async_copy(a, b, sems.at[n]) for n, (a, b) in enumerate(zip((small, large, up_s, up_l, t_s, t_l), raw))]
    start_all(loads)
    r, n = z.rims, REACH * z.rims
    tail = n + 2 * r
    for ref in (bottom, top):
        ref[pl.ds(tail, z.slots), :] = jnp.zeros((z.slots, LANES), F32)
    wait_all(loads[:2])
    to_matrix(z, raw[:2], half)
    value = whole(half)
    x[...] = value
    moments(z, value, copies)
    for h in (0, 1):
        lanes = pl.ds(128 * h, 128)
        take_rims(z, half.at[h], REACH, bottom.at[pl.ds(0, n), lanes], top.at[pl.ds(0, n), lanes])
    wait_all(loads[2:])
    for k in (0, 1):
        width, rows = HEIGHTS[k], z.rows[k]
        for i in range(z.images[k]):
            slot = pl.ds(tail + i + k * z.images[0], 1)
            for d in (0, 1):
                to_bottom, to_top = n + (1 - d) * r + z.rim[k] + i, n + d * r + z.rim[k] + i
                for j in range(z.blocks[k]):
                    lanes, at = pl.ds(LANES * j, LANES), j * z.images[k]
                    if d < rows:
                        bottom[pl.ds(to_bottom + at, 1), :] = raw[2 + k][i, pl.ds(rows - 1 - d, 1), lanes]
                        top[pl.ds(to_top + at, 1), :] = raw[2 + k][i, pl.ds(d, 1), lanes]
                    else:
                        bottom[pl.ds(to_bottom + at, 1), :] = jnp.zeros((1, LANES), F32)
                        top[pl.ds(to_top + at, 1), :] = jnp.zeros((1, LANES), F32)
                if d < rows:
                    bottom[slot, pl.ds(128 * (1 - d), width)] = raw[4 + k][i, pl.ds(rows - 1 - d, 1), :]
                    top[slot, pl.ds(128 * d, width)] = raw[4 + k][i, pl.ds(d, 1), :]


def banded(taps, ref):
    row = lax.broadcasted_iota(jnp.int32, (128, 128), 0) // C
    lane = group_of(128)
    for a in range(TAPS):
        main = jnp.zeros((128, 128), F32)
        for b in range(TAPS):
            main = jnp.where(row - lane + 1 == b, taps[a][b], main)
        before = jnp.where(lane[:C] == 0, taps[a][0][:C], 0.0)
        after = jnp.where(lane[:C] == 3, taps[a][2][:C], 0.0)
        for n, part in enumerate(split(jnp.concatenate([main, before, after], axis=0))):
            ref[n, pl.ds(a * TAP_ROWS, TAP_ROWS), :] = part


def weight_matrix(ref):
    rows = []
    zeros = jnp.zeros((128 - C, 128), BF16)
    for a in range(TAPS):
        at = a * TAP_ROWS
        main = ref[pl.ds(at, 128), :]
        before = jnp.concatenate([zeros, ref[pl.ds(at + 128, C), :]], axis=0)
        after = jnp.concatenate([ref[pl.ds(at + 128 + C, C), :], zeros], axis=0)
        rows += [
            jnp.concatenate([main, before], axis=1),
            jnp.concatenate([after, main], axis=1),
            jnp.concatenate([before, after], axis=1),
        ]
    return jnp.concatenate(rows, axis=0)


def prepare_kernel(z, first, second, up_s, up_l, t_s, t_l, g1, b1, g2, b2, x, w1, w2, weights, affine, upstream, teacher, x_copy, raw, kept, kept_u, rows, half, sems):
    targets = tuple(raw) + tuple(rows.at[pl.ds(n, 1), :] for n in range(4))
    refs = (first, second, up_s, up_l, t_s, t_l, g1, b1, g2, b2)
    loads = [pltpu.make_async_copy(a, b, sems.at[n]) for n, (a, b) in enumerate(zip(refs, targets))]
    start_all(loads)
    stores = [pltpu.make_async_copy(x, x_copy, sems.at[13])]
    stores[0].start()
    wait_all(loads)
    to_matrix(z, raw[2:4], half)
    kept_u[...] = whole(half)
    stores.append(pltpu.make_async_copy(kept_u, upstream, sems.at[10]))
    stores[1].start()
    for n, (source, forward) in enumerate(zip(raw[:2], (w1, w2))):
        tiles = []
        for a in range(TAPS):
            line = [jnp.concatenate([source[a, b]] * 4, axis=1) for b in range(TAPS)]
            tiles.append([jnp.concatenate([tap] * 4, axis=0) for tap in line])
        turned = [[tiles[TAPS - 1 - a][TAPS - 1 - b].T for b in range(TAPS)] for a in range(TAPS)]
        banded(tiles, forward)
        banded(turned, kept.at[n])
        stores.append(pltpu.make_async_copy(kept.at[n], weights.at[n], sems.at[11 + n]))
        stores[-1].start()
    affine[...] = jnp.concatenate([rows[...]] * BLOCK, axis=1)
    teacher[...] = jnp.zeros(teacher.shape, F32)
    for k, ref in ((0, raw[4]), (1, raw[5])):
        for i in range(z.images[k]):
            line = ref[i]
            for j in range(z.blocks[k]):
                at = z.start[k] + j * z.step[k] + i * z.rows[k]
                for lane in (0, 64):
                    teacher[pl.ds(at, z.rows[k]), pl.ds(lane, BLOCK)] = line[:, j * BLOCK : (j + 1) * BLOCK]
    wait_all(stores)


def normed_by(stats):
    return lambda v: (v - stats[0:1]) * stats[1:2]


def activation(center, scale, gain, bias):
    factor = scale * gain
    offset = bias - center * factor
    return lambda v: gelu(v * factor + offset)


def first_kernel(z, x, above, below, gathered, affine, weight, hidden, h_above, h_below, stats, copies, pads, chains):
    n = REACH * z.rims
    center, scale = merged(z, gathered)
    act = activation(center, scale, affine[0:1], affine[1:2])
    own = act(x[...])
    up, down = act(above[pl.ds(0, n), :]) * inside(z, 4, True), act(below[pl.ds(0, n), :]) * inside(z, 4, False)
    own, up, down = convolve(z, own, up, down, 4, pads, chains, weight)
    moments(z, own, copies)
    hidden[...] = own
    h_above[...] = up
    h_below[...] = down
    stats[0:1] = center
    stats[1:2] = scale


def second_kernel(z, hidden, h_above, h_below, gathered, affine, weight, x, x_above, x_below, teacher, out, o_above, o_below, near, stats, copies, pads, chains):
    center, scale = merged(z, gathered)
    act = activation(center, scale, affine[2:3], affine[3:4])
    r = z.rims
    own = act(hidden[...])
    up, down = act(h_above[...]) * inside(z, 3, True), act(h_below[...]) * inside(z, 3, False)
    own, up, down = convolve(z, own, up, down, 3, pads, chains, weight)
    own = x[...] + own
    amap = attention(own)
    lane = lax.broadcasted_iota(jnp.int32, (1, 128), 1)
    sums = image_sums(z, amap * jnp.where(lane < 64, amap, teacher[...]))
    copies[...] = jnp.broadcast_to(sums[None], copies.shape)
    out[...] = own
    o_above[...] = x_above[pl.ds(2 * r, 2 * r), :] + up
    o_below[...] = x_below[pl.ds(0, 2 * r), :] + down
    near[0] = h_above[pl.ds(2 * r, r), :]
    near[1] = h_below[pl.ds(0, r), :]
    stats[0:1] = center
    stats[1:2] = scale


def tap_rows(q):
    return 128 + 3 * C if q < 0 else 128 if q == 4 else q * C


def tap_product(z, operand, own, above, below, pads):
    fill_center(z, pads, own)
    fill_shifted(z, pads, above, below)
    columns = []
    for a in range(TAPS):
        columns.append(
            jnp.concatenate([pads[k][TAPS - 1 - a, h, pl.ds(z.step[k], z.count[k]), :] for h in (0, 1) for k in (1, 0)], axis=0)
        )
    return product(operand, split(jnp.concatenate(columns, axis=1)))


def tap_sums(result, tiles, first_group):
    group = group_of()
    for a in range(TAPS):
        for b in range(TAPS):
            total = None
            for p in range(4):
                at = tap_rows(p + b - 1)
                part = result[at : at + C, 128 * a : 128 * a + 128]
                total = part if total is None else jnp.where(group == p, part, total)
            tile, slot = divmod(first_group + a * TAPS + b, 4)
            tiles[tile] = jnp.where(group == slot, spread_groups(total), tiles[tile])


def tap_counts(z, turned, tiles, first_group):
    group = group_of()
    m = lax.broadcasted_iota(jnp.int32, (1, 2 * z.total), 1) % z.total
    row = jnp.where(m < z.start[0], m % z.rows[1], (m - z.start[0]) % z.rows[0])
    height = jnp.where(m < z.start[0], z.rows[1], z.rows[0])
    at = lax.axis_index("row")
    lost = {
        0: (row == height - 1) & (at == z.peers - 1),
        2: (row == 0) & (at == 0),
    }
    for a in range(TAPS):
        column = jnp.sum(jnp.where(lost[a], 0.0, turned) if a in lost else turned, axis=1, keepdims=True)
        for b in range(TAPS):
            total = sum(column[tap_rows(p + b - 1) : tap_rows(p + b - 1) + C] for p in range(4))
            tile, slot = divmod(first_group + a * TAPS + b, 4)
            tiles[tile] = jnp.where(group == slot, total, tiles[tile])


def turned_operand(z, value, pads, kept):
    fill_center(z, pads, value)
    lane = lax.broadcasted_iota(jnp.int32, (1, 128), 1)
    halves = ([], [])
    for k in (1, 0):
        ref, step, count = pads[k], z.step[k], z.count[k]
        low, high = ref[1, 0, pl.ds(step, count), :], ref[1, 1, pl.ds(step, count), :]
        before, after = ref[1, 1, pl.ds(0, count), :], ref[1, 0, pl.ds(2 * step, count), :]
        for part, main, left, right in ((halves[0], low, before, high), (halves[1], high, low, after)):
            part.append(jnp.concatenate([main, jnp.where(lane >= 96, left, jnp.where(lane < 32, right, 0.0))], axis=1))
    turned = jnp.concatenate(halves[0] + halves[1], axis=0).T
    parts = split(turned)
    for n in (0, 1):
        kept[n] = parts[n]
    return turned


def first_operand_kernel(z, x, hidden, h_above, h_below, above, below, stats, affine, teacher, upstream, weights, left, packed, teachers, spread_u, near_u, pads, chains, kept, kept_w, kept_u, pixels, kept_t, kept_c, kept_packed, sems):
    r, own = z.rims, pl.ds(0, z.total)
    loads = [pltpu.make_async_copy(upstream, kept_u.at[own, :], sems.at[0]), pltpu.make_async_copy(weights.at[1], kept_w, sems.at[1])]
    start_all(loads)
    act = activation(stats[0:1], stats[1:2], affine[0:1], affine[1:2])
    value = turned_operand(z, act(x[...]), pads, kept)
    stores = [pltpu.make_async_copy(kept, left, sems.at[2])]
    stores[0].start()
    tiles = [jnp.zeros((C, 128), F32) for _ in range(BACK_LANES // 128)]
    tap_counts(z, value, tiles, ONES)
    result = tap_product(
        z, (kept[0], kept[1]), hidden[...], h_above[pl.ds(2 * r, r), :] * inside(z, 1, True), h_below[pl.ds(0, r), :] * inside(z, 1, False), pads
    )
    tap_sums(result, tiles, HIDDEN)
    kept_packed[...] = jnp.concatenate(tiles, axis=1)
    stores.append(pltpu.make_async_copy(kept_packed, packed, sems.at[6]))
    stores[1].start()
    pixels[own, :] = teacher[...]
    pixels[pl.ds(z.total, 4 * r), :] = jnp.zeros((4 * r, 128), F32)
    n = (REACH + 2) * r
    for side, ref in enumerate((above, below)):
        for d in (0, 1):
            for k in (0, 1):
                line = ref[pl.ds(n + k * z.images[0], z.images[k]), pl.ds(128 * d, 128)]
                for j in range(z.blocks[k]):
                    at = z.total + (2 * side + d) * r + z.rim[k] + j * z.images[k]
                    pixels[pl.ds(at, z.images[k]), pl.ds(0, BLOCK)] = line[:, j * BLOCK : (j + 1) * BLOCK]
    kept_t[...] = spread(pixels[...], to_channels())
    stores.append(pltpu.make_async_copy(kept_t, teachers, sems.at[3]))
    stores[2].start()
    n = REACH * r
    up, down = above[pl.ds(n, 2 * r), :] * inside(z, 2, True), below[pl.ds(n, 2 * r), :] * inside(z, 2, False)
    kept_u[pl.ds(z.total, r), :] = up[r:]
    kept_u[pl.ds(z.total + r, r), :] = down[:r]
    wait_all(loads)
    stores.append(pltpu.make_async_copy(kept_u, near_u, sems.at[5]))
    stores[3].start()
    kept_c[...] = jnp.concatenate(convolve(z, kept_u[own, :], up, down, 2, pads, chains, kept_w), axis=0)
    stores.append(pltpu.make_async_copy(kept_c, spread_u, sems.at[4]))
    stores[4].start()
    wait_all(stores)


def second_operand_kernel(z, hidden, near, stats, affine, out, o_above, o_below, teachers, spread_u, near_u, weights, out_copy, hidden_copy, left, shifts, by_map, by_teacher, up, pads, chains, kept_t, kept_u, kept_w, kept_s, sems):
    r, total = z.rims, z.total
    loads = [
        pltpu.make_async_copy(teachers, kept_t, sems.at[0]),
        pltpu.make_async_copy(weights.at[1], kept_w, sems.at[1]),
        pltpu.make_async_copy(spread_u, kept_u, sems.at[2]),
    ]
    start_all(loads)
    stores = [
        pltpu.make_async_copy(out, out_copy, sems.at[4]),
        pltpu.make_async_copy(hidden, hidden_copy.at[pl.ds(0, total), :], sems.at[7]),
        pltpu.make_async_copy(near.at[0], hidden_copy.at[pl.ds(total, r), :], sems.at[8]),
        pltpu.make_async_copy(near.at[1], hidden_copy.at[pl.ds(total + r, r), :], sems.at[9]),
        pltpu.make_async_copy(near_u, up, sems.at[10]),
    ]
    start_all(stores)
    normed = normed_by(stats)(jnp.concatenate([hidden[...], near[0], near[1]], axis=0))
    shifted = normed * affine[2:3] + affine[3:4]
    turned_operand(z, gelu(shifted[:total]), pads, left)
    ones = jnp.ones((total, 1), F32)
    masks = jnp.concatenate([ones, inside(z, 1, True), inside(z, 1, False)], axis=0)
    slopes = gelu_slope(shifted) * masks
    o = jnp.concatenate([out[...], o_above[...] * inside(z, 2, True), o_below[...] * inside(z, 2, False)], axis=0)
    for_map = spread(attention(o), to_channels()) * o
    wait_all(loads)
    for_teacher = kept_t[...] * o
    kept_s[0] = kept_u[...] * slopes
    for n, value, ref in ((1, for_map, by_map), (2, for_teacher, by_teacher)):
        own, before, after = value[:total], value[total : total + 2 * r], value[total + 2 * r :]
        ref[...] = jnp.concatenate([own, before[r:], after[:r]], axis=0)
        kept_s[n] = jnp.concatenate(convolve(z, own, before, after, 2, pads, chains, kept_w), axis=0) * slopes
    stores.append(pltpu.make_async_copy(kept_s, shifts, sems.at[5]))
    stores[-1].start()
    wait_all(stores)


def upstream_kernel(z, gathered, up, shifts, left_1, left_2, packed, by_map, by_teacher, hidden, stats, dout, dshift, d_above, d_below, slabs, kept_s, kept_left, kept_h, kept_packed, pads, more_pads, sems):
    r, total = z.rims, z.total
    loads = [
        pltpu.make_async_copy(a, b, sems.at[n])
        for n, (a, b) in enumerate(((shifts, kept_s), (left_1, kept_left), (hidden.at[pl.ds(0, total), :], kept_h), (packed, kept_packed)))
    ]
    start_all(loads)
    lane = lax.broadcasted_iota(jnp.int32, (z.slots, 128), 1)
    sums = jnp.sum(gathered[...], axis=0)
    square = jnp.sum(jnp.where(lane < 64, sums, 0.0), axis=1, keepdims=True)
    cross = jnp.sum(jnp.where(lane < 64, 0.0, sums), axis=1, keepdims=True)
    inverse = lax.rsqrt(square + map_eps)
    inner = beta_weight * (square * inverse - cross) * inverse
    shape = (z.slots, 128)
    for_map = (beta_weight - inner) * inverse * inverse * (2.0 / C)
    for_teacher = beta_weight * inverse * (2.0 / C)
    for_map, for_teacher = (wide(image_rows(z, jnp.broadcast_to(v, shape), 2)) for v in (for_map, for_teacher))
    value = up[...] + for_map * by_map[...] - for_teacher * by_teacher[...]
    dout[...] = value[:total]
    wait_all(loads[:2])
    shift = kept_s[0] + for_map * kept_s[1] - for_teacher * kept_s[2]
    pre, above, below = shift[:total], shift[total : total + r], shift[total + r :]
    dshift[...] = pre
    d_above[...] = above
    d_below[...] = below
    second = tap_product(z, (left_2[0], left_2[1]), value[:total], value[total : total + r], value[total + r :], pads)
    first = tap_product(z, (kept_left[0], kept_left[1]), pre, above, below, more_pads)
    wait_all(loads[2:])
    normed = normed_by(stats)(kept_h[...])
    tiles = [kept_packed[:, 128 * n : 128 * n + 128] for n in range(BACK_LANES // 128)]
    group = group_of()
    tiles[0] = jnp.where(group == BIAS, fold(column_sum(pre)), jnp.where(group == GAIN, fold(column_sum(pre * normed)), tiles[0]))
    tap_sums(second, tiles, SECOND)
    tap_sums(first, tiles, LEFT)
    line = jnp.concatenate(tiles, axis=1)
    for d in range(z.devices):
        slabs[d] = line[d % C : d % C + 1]


def write_kernel(z, out, x, hidden, weights, first_stats, stats, order, out_s, out_l, first_normed, normed, weight, kept, kept_x, kept_h, half, sems):
    loads = [pltpu.make_async_copy(a, b, sems.at[n]) for n, (a, b) in enumerate(((out, kept), (x, kept_x), (hidden, kept_h), (weights.at[0], weight)))]
    start_all(loads)
    loads[0].wait()
    put_halves(half, kept[...])
    from_matrix(z, half, (out_s, out_l))
    loads[1].wait()
    first_normed[...] = normed_by(first_stats)(kept_x[...])
    loads[2].wait()
    normed[...] = normed_by(stats)(kept_h[...])
    loads[3].wait()


def norm_sums(total):
    group = group_of()
    return [wide(spread_groups(jnp.where(group == n, total[:, :128], 0.0))) for n in (BIAS, GAIN)]


def hidden_kernel(z, gathered, dshift, d_above, d_below, second_normed, stats, affine, weight, first_normed, pre_ref, gain_out, bias_out, slabs, pads):
    total = jnp.sum(gathered[...], axis=0)
    bias_sum, gain_sum = norm_sums(total)
    bias_out[...] = bias_sum[:, :C]
    gain_out[...] = gain_sum[:, :C]
    bias_mean, gain_mean = bias_sum / z.pixels, gain_sum / z.pixels
    factor = affine[2:3] * stats[1:2]
    r, total_rows = z.rims, z.total

    def back(d, normed):
        return factor * (d - bias_mean - normed * gain_mean)

    own = back(dshift[...], second_normed[pl.ds(0, total_rows), :])
    up = back(d_above[...], second_normed[pl.ds(total_rows, r), :]) * inside(z, 1, True)
    down = back(d_below[...], second_normed[pl.ds(total_rows + r, r), :]) * inside(z, 1, False)
    grad, _, _ = convolve(z, own, up, down, 1, pads, None, weight)
    normed = first_normed[...]
    pre = grad * gelu_slope(normed * affine[0:1] + affine[1:2])
    pre_ref[...] = pre
    lane = lax.broadcasted_iota(jnp.int32, (1, 128), 1)
    taps = TAPS * TAPS * C

    def along(row):
        return jnp.concatenate([row[:, :128]] * 3, axis=1)[:, :taps]

    second, left, against, ones = (total[:, n * C : n * C + taps] for n in (SECOND, LEFT, HIDDEN, ONES))
    against = along(stats[1:2]) * (against - along(stats[0:1]) * ones)
    first = along(factor) * (left - along(bias_mean) * ones - along(gain_mean) * against)
    sums = jnp.where(lane < C, fold(column_sum(pre)), fold(column_sum(pre * normed)))
    line = jnp.concatenate([sums[:, : 2 * C], second, first], axis=1)
    slabs[...] = jnp.broadcast_to(line[None], slabs.shape)


def back_kernel(z, gathered, pre, normed, stats, affine, dout, back_s, back_l, one, two, gain_out, bias_out, half, lines):
    bias_sum, gain_sum = norm_sums(jnp.sum(gathered[:, :, pl.ds(0, 128)], axis=0))
    bias_out[...] = bias_sum[:, :C]
    gain_out[...] = gain_sum[:, :C]
    value = dout[...] + affine[0:1] * stats[1:2] * (pre[...] - bias_sum / z.pixels - normed[...] * (gain_sum / z.pixels))
    put_halves(half, value)
    from_matrix(z, half, (back_s, back_l))
    for d in range(C):
        lines[pl.ds(d, 1), :] = gathered[d]
    for ref, group in ((two, LAST_SECOND), (one, LAST_FIRST)):
        for a in range(TAPS):
            for b in range(TAPS):
                at = (group + a * TAPS + b) * C
                ref[a, b] = lines[:, pl.ds(at, C)]


def call(body, ins, outs, scratch=(), sems=0):
    space = {"v": pltpu.VMEM, "h": pltpu.HBM, "V": pltpu.VMEM}
    shapes = []
    for item in scratch:
        if isinstance(item, list):
            shapes.append([pltpu.VMEM(*s) for s in item])
        else:
            shapes.append(pltpu.VMEM(*item))
    if sems:
        shapes.append(pltpu.SemaphoreType.DMA((sems,)))
    run = pl.pallas_call(
        body,
        out_shape=[jax.ShapeDtypeStruct(shape, kind) if s == "v" else space[s](shape, kind) for s, shape, kind in outs],
        in_specs=[pl.BlockSpec(memory_space=space[s]) for s in ins],
        out_specs=[pl.BlockSpec(memory_space=space[s]) for s, _, _ in outs],
        scratch_shapes=shapes,
        compiler_params=pltpu.CompilerParams(vmem_limit_bytes=VMEM_LIMIT),
    )
    return lambda *args: run(
        *(pltpu.with_memory_space_constraint(arg, pltpu.HBM) if s == "h" else arg for s, arg in zip(ins, args))
    )


def exchange(copies, axes):
    return lax.all_to_all(copies, axes, 0, 0, tiled=True)


def beyond(z, bottom, top, depths):
    hops = max(-(-depth // rows) for rows in z.rows for depth in depths)
    above, below = [], []
    for hop in range(1, hops + 1):
        above.append(lax.ppermute(bottom, "row", [(i, i + hop) for i in range(z.peers - hop)]))
        below.append(lax.ppermute(top, "row", [(i + hop, i) for i in range(z.peers - hop)]))
    if hops == 1:
        return above[0], below[0]
    up, down = [], []
    base = 0
    for depth in depths:
        for n in range(depth):
            for k in (1, 0):
                hop, back = divmod(depth - 1 - n, z.rows[k])
                at = base + (depth - 1 - back) * z.rims + z.rim[k]
                up.append(above[hop][at : at + z.edge[k]])
                hop, back = divmod(n, z.rows[k])
                at = base + back * z.rims + z.rim[k]
                down.append(below[hop][at : at + z.edge[k]])
        base += depth * z.rims
    up.append(jnp.concatenate([pixel_rows(z, above, base, 1, 1), pixel_rows(z, above, base, 0, 1)], axis=1))
    down.append(jnp.concatenate([pixel_rows(z, below, base, 0, 0), pixel_rows(z, below, base, 1, 0)], axis=1))
    return jnp.concatenate(up, axis=0), jnp.concatenate(down, axis=0)


def pixel_rows(z, bands, base, distance, last):
    lines = []
    for k in (0, 1):
        hop, back = divmod(distance, z.rows[k])
        at = base + k * z.images[0]
        half = 128 * abs(last - back)
        lines.append(bands[hop][at : at + z.images[k], half : half + 128])
    lines.append(jnp.zeros((z.slots - sum(z.images), 128), F32))
    return jnp.concatenate(lines, axis=0)


def local(
    image_small, image_large, teacher_small, teacher_large, upstream_small, upstream_large,
    conv_first, gain_first, bias_first, conv_second, gain_second, bias_second,
):
    peers = lax.axis_size("row")
    devices = lax.axis_size("img") * peers
    z = Sizes(image_small.shape, image_large.shape, devices, peers)
    body = lambda function: functools.partial(function, z)
    r = z.rims
    full, half, pair = (z.total, LANES), (2, z.total, 128), (devices, 2, 128)
    weight, left = (2, TAPS * TAP_ROWS, 128), (2, 256, 2 * z.total)
    images = [image_small, image_large, upstream_small, upstream_large, teacher_small, teacher_large]
    f = lambda space, *shape: (space, shape, F32)
    depths = (REACH, 2)
    rim_rows = sum(depths) * r + z.slots

    x, bottom, top, copies = call(
        body(start_kernel),
        "hhhhhh",
        [("v", full, F32), f("v", rim_rows, LANES), f("v", rim_rows, LANES), ("V", pair, F32)],
        [[(a.shape, F32) for a in images], (half, F32)],
        6,
    )(*images)
    gathered = exchange(copies, AXES)
    above, below = beyond(z, bottom, top, depths)
    params = [conv_first, conv_second] + images[2:]
    w1, w2, weights, affine, upstream, teacher, x_copy = call(
        body(prepare_kernel),
        "hhhhhhhhhhv",
        [("v", weight, BF16), ("v", weight, BF16), ("h", (2,) + weight, BF16), f("v", 4, LANES), ("h", full, F32), f("v", z.total, 128), ("h", full, F32)],
        [[(a.shape, F32) for a in params], ((2,) + weight, BF16), (full, F32), ((4, C), F32), (half, F32)],
        14,
    )(*params, *(v.reshape(1, C) for v in (gain_first, bias_first, gain_second, bias_second)), x)

    hidden, h_above, h_below, stats_one, copies = call(
        body(first_kernel),
        "vvvvvv",
        [("v", full, F32), f("v", 3 * r, LANES), f("v", 3 * r, LANES), f("v", 2, LANES), ("V", pair, F32)],
        [z.pads(), z.chains(4)],
    )(x, above, below, gathered, affine, w1)
    gathered = exchange(copies, AXES)
    extended, near_rows = z.total + 4 * r, z.total + 2 * r
    left_one, packed, teachers, spread_u, near_u = call(
        body(first_operand_kernel),
        "vvvvvvvvvhh",
        [("h", left, BF16), f("h", C, BACK_LANES), f("h", extended, LANES), f("h", near_rows, LANES), f("h", near_rows, LANES)],
        [
            z.pads(), z.chains(2), (left, BF16), (weight, BF16), ((near_rows, LANES), F32), ((extended, 128), F32),
            ((extended, LANES), F32), ((near_rows, LANES), F32), ((C, BACK_LANES), F32),
        ],
        7,
    )(x, hidden, h_above, h_below, above, below, stats_one, affine, teacher, upstream, weights)
    gathered, near_u = lax.optimization_barrier((gathered, near_u))

    map_shape = (peers, z.slots, 128)
    out, o_above, o_below, near, stats_two, copies = call(
        body(second_kernel),
        "vvvvvvvvvv",
        [("v", full, F32), f("v", 2 * r, LANES), f("v", 2 * r, LANES), f("v", 2, r, LANES), f("v", 2, LANES), ("V", map_shape, F32)],
        [z.pads(), z.chains(3)],
    )(hidden, h_above, h_below, gathered, affine, w2, x, above, below, teacher)
    gathered = exchange(copies, ("row",))
    out_copy, hidden_copy, left_two, shifts, by_map, by_teacher, up = call(
        body(second_operand_kernel),
        "vvvvvvvhhhh",
        [
            ("h", full, F32), f("h", near_rows, LANES), ("v", left, BF16), f("h", 3, near_rows, LANES),
            f("v", near_rows, LANES), f("v", near_rows, LANES), f("v", near_rows, LANES),
        ],
        [
            z.pads(), z.chains(2), ((extended, LANES), F32), ((near_rows, LANES), F32), (weight, BF16),
            ((3, near_rows, LANES), F32),
        ],
        11,
    )(hidden, near, stats_two, affine, out, o_above, o_below, teachers, spread_u, near_u, weights)

    dout, dshift, d_above, d_below, slabs = call(
        body(upstream_kernel),
        "vvhhvhvvhv",
        [("v", full, F32), ("v", full, F32), f("v", r, LANES), f("v", r, LANES), f("V", devices, 1, BACK_LANES)],
        [((3, near_rows, LANES), F32), (left, BF16), (full, F32), ((C, BACK_LANES), F32), z.pads(), z.pads()],
        4,
    )(gathered, up, shifts, left_one, left_two, packed, by_map, by_teacher, hidden_copy, stats_two)
    gathered = exchange(slabs, AXES)
    out_s, out_l, first_normed, second_normed, weight_back = call(
        body(write_kernel),
        "hhhhvvv",
        [("v", image_small.shape, F32), ("v", image_large.shape, F32), ("v", full, F32), f("v", near_rows, LANES), ("v", weight, BF16)],
        [(full, F32), (full, F32), ((near_rows, LANES), F32), (half, F32)],
        4,
    )(out_copy, x_copy, hidden_copy, weights, stats_one, stats_two, d_above)

    pre, gain_two, bias_two, slabs = call(
        body(hidden_kernel),
        "vvvvvvvvv",
        [("v", full, F32), f("v", 1, C), f("v", 1, C), f("V", devices, 1, LAST_LANES)],
        [z.pads()],
    )(gathered, dshift, d_above, d_below, second_normed, stats_two, affine, weight_back, first_normed)
    gathered = exchange(slabs, AXES)

    back_s, back_l, one, two, gain_one, bias_one = call(
        body(back_kernel),
        "vvvvvv",
        [("v", a.shape, F32) for a in (image_small, image_large, conv_first, conv_second)] + [f("v", 1, C), f("v", 1, C)],
        [(half, F32), ((C, LAST_LANES), F32)],
    )(gathered, pre, first_normed, stats_one, affine, dout)
    return (
        out_s, out_l, back_s, back_l,
        one, gain_one.reshape(C), bias_one.reshape(C),
        two, gain_two.reshape(C), bias_two.reshape(C),
    )


def solution(mesh):
    split_bands, everywhere = P("img", "row", None), P()
    return jax.shard_map(
        local,
        mesh=mesh,
        in_specs=(split_bands,) * 6 + (everywhere,) * 6,
        out_specs=(split_bands,) * 4 + (everywhere,) * 6,
        check_vma=False,
    )
```

```python
import functools
import math

import jax
import jax.numpy as jnp
from jax import lax
from jax.experimental import pallas as pl
from jax.experimental.pallas import tpu as pltpu
from jax.sharding import PartitionSpec as P

C = 32
HS = 32
HL = 64
HEIGHTS = (HS, HL)

norm_eps = 1e-05
map_eps = 1e-06
beta_weight = 1000.0
AXES = ("img", "row")
BLOCK = 8
LANES = BLOCK * C
TAPS = 3
WIDTH = LANES + 128
DEPTH = TAPS * WIDTH
TAP_ROWS = 128 + 2 * C
REACH = 4
ROOT = math.sqrt(2.0 / math.pi)
CUBE = 0.044715
F32 = jnp.float32
BF16 = jnp.bfloat16
VMEM_LIMIT = 32 * 1024 * 1024
BIAS, GAIN, SECOND, LEFT, HIDDEN, ONES = 0, 1, 2, 11, 20, 29
BACK_LANES = 1280
LAST_SECOND, LAST_FIRST, LAST_LANES = 2, 11, 640


class Sizes:
    def __init__(self, small, large, devices, peers):
        self.images = (small[0], large[0])
        self.rows = (small[1], large[1])
        self.blocks = (HS // BLOCK, HL // BLOCK)
        self.step = tuple(n * r for n, r in zip(self.images, self.rows))
        self.count = tuple(b * s for b, s in zip(self.blocks, self.step))
        self.edge = tuple(b * n for b, n in zip(self.blocks, self.images))
        self.start = (self.count[1], 0)
        self.rim = (self.edge[1], 0)
        self.total = sum(self.count)
        self.rims = sum(self.edge)
        self.slots = -(-sum(self.images) // 8) * 8
        self.guard = -(-max(self.images) // 8) * 8
        self.devices = devices
        self.peers = peers
        self.here = float(self.total * BLOCK)
        self.pixels = self.here * devices

    def pads(self):
        return [((TAPS, 2, self.count[k] + 2 * self.step[k], 128), F32) for k in (0, 1)]

    def chains(self, depth):
        return [((2, 2 * self.guard + (depth + 1) * self.rims, 128), F32)] * 2


def split(value):
    high = value.astype(BF16)
    return high, (value - high.astype(F32)).astype(BF16)


def dot(left, right):
    return lax.dot_general(left, right, (((1,), (0,)), ((), ())), preferred_element_type=F32)


def product(left, right):
    if left[0].shape[1] % 128:
        return dot(left[0], right[0]) + (dot(left[0], right[1]) + dot(left[1], right[0]))
    return dot(
        jnp.concatenate([left[0], left[0], left[1]], axis=1), jnp.concatenate([right[0], right[1], right[0]], axis=0)
    )


def spread(left, right):
    right = right.astype(BF16)
    return dot(jnp.concatenate(split(left), axis=1), jnp.concatenate([right, right], axis=0))


def gelu(s):
    return 0.5 * s * (1.0 + jnp.tanh(ROOT * (s + CUBE * s * s * s)))


def gelu_slope(s):
    square = s * s
    t = jnp.tanh(ROOT * s * (1.0 + CUBE * square))
    return 0.5 * (1.0 + t) + 0.5 * s * (1.0 - t * t) * ROOT * (1.0 + 3.0 * CUBE * square)


def spread_groups(row):
    row = row + pltpu.roll(row, 64, 1)
    return row + pltpu.roll(row, 32, 1)


def fold(row):
    return spread_groups(row[:, :128] + row[:, 128:])


def wide(row):
    return jnp.concatenate([row, row], axis=1)


def group_of(rows=1, lanes=128):
    return lax.broadcasted_iota(jnp.int32, (rows, lanes), 1) // C


def column_sum(value):
    return jnp.sum(value, axis=0, keepdims=True)


def send_lines(z, ref, lines):
    for n, line in enumerate(lines):
        ref[pl.ds(n, z.devices, stride=len(lines)), :] = jnp.broadcast_to(line, (z.devices, 128))


def moments(z, value, ref):
    few = min(8, z.total)
    pivot = fold(column_sum(value[:few])) / float(few * BLOCK)
    off = value - wide(pivot)
    first, second = fold(column_sum(off)), fold(column_sum(off * off))
    send_lines(z, ref, [pivot + first / z.here, second - first * first / z.here])


def merged(z, ref):
    means = ref[pl.ds(0, z.devices, stride=2), :]
    center = jnp.mean(means, axis=0, keepdims=True)
    off = means - center
    within = jnp.mean(ref[pl.ds(1, z.devices, stride=2), :], axis=0, keepdims=True)
    variance = within / z.here + jnp.mean(off * off, axis=0, keepdims=True)
    return wide(center), wide(lax.rsqrt(variance + norm_eps))


def put_halves(ref, value):
    ref[0] = value[:, :128]
    ref[1] = value[:, 128:]


def whole(ref):
    return jnp.concatenate([ref[0], ref[1]], axis=1)


def to_matrix(z, refs, half):
    for k in (0, 1):
        for j in range(z.blocks[k]):
            at = z.start[k] + j * z.step[k]
            for i in range(z.images[k]):
                for h in (0, 1):
                    half[h, pl.ds(at + i * z.rows[k], z.rows[k]), :] = refs[k][i, :, pl.ds(LANES * j + 128 * h, 128)]


def from_matrix(z, half, refs):
    for k in (0, 1):
        for j in range(z.blocks[k]):
            at = z.start[k] + j * z.step[k]
            for i in range(z.images[k]):
                for h in (0, 1):
                    refs[k][i, :, pl.ds(LANES * j + 128 * h, 128)] = half[h, pl.ds(at + i * z.rows[k], z.rows[k]), :]


def take_rims(z, half, depth, bottom, top):
    for k in (0, 1):
        for d in range(1, depth + 1):
            to_bottom = pl.ds((depth - d) * z.rims + z.rim[k], z.edge[k])
            to_top = pl.ds((d - 1) * z.rims + z.rim[k], z.edge[k])
            if d <= z.rows[k]:
                bottom[to_bottom, :] = half[pl.ds(z.start[k] + z.rows[k] - d, z.edge[k], stride=z.rows[k]), :]
                top[to_top, :] = half[pl.ds(z.start[k] + d - 1, z.edge[k], stride=z.rows[k]), :]
            else:
                bottom[to_bottom, :] = jnp.zeros((z.edge[k], 128), F32)
                top[to_top, :] = jnp.zeros((z.edge[k], 128), F32)


def inside(z, depth, above):
    at = lax.axis_index("row")
    large = lax.broadcasted_iota(jnp.int32, (z.rims, 1), 0) < z.rim[0]
    parts = []
    for n in range(depth):
        if above:
            ok = [jnp.where(at * rows >= depth - n, 1.0, 0.0) for rows in z.rows]
        else:
            ok = [jnp.where((at + 1) * rows + n + 1 <= height, 1.0, 0.0) for rows, height in zip(z.rows, HEIGHTS)]
        parts.append(jnp.where(large, ok[1], ok[0]).astype(F32))
    return jnp.concatenate(parts, axis=0)


def clear_guards(z, pads, a):
    for k in (0, 1):
        pads[k][a, 1, pl.ds(0, z.step[k]), :] = jnp.zeros((z.step[k], 128), F32)
        pads[k][a, 0, pl.ds(z.step[k] + z.count[k], z.step[k]), :] = jnp.zeros((z.step[k], 128), F32)


def fill_center(z, pads, value):
    clear_guards(z, pads, 1)
    for k in (0, 1):
        for h in (0, 1):
            pads[k][1, h, pl.ds(z.step[k], z.count[k]), :] = value[z.start[k] : z.start[k] + z.count[k], 128 * h : 128 * h + 128]


def fill_shifted(z, pads, above, below):
    for k in (0, 1):
        ref, step, count, rows = pads[k], z.step[k], z.count[k], z.rows[k]
        rim = slice(z.rim[k], z.rim[k] + z.edge[k])
        for h in (0, 1):
            lanes = slice(128 * h, 128 * h + 128)
            ref[0, h, pl.ds(step, count), :] = ref[1, h, pl.ds(step - 1, count), :]
            ref[2, h, pl.ds(step, count), :] = ref[1, h, pl.ds(step + 1, count), :]
            ref[0, h, pl.ds(step, z.edge[k], stride=rows), :] = above[rim, lanes]
            ref[2, h, pl.ds(step + rows - 1, z.edge[k], stride=rows), :] = below[rim, lanes]


def fill_pads(z, pads, value, above, below):
    fill_center(z, pads, value)
    fill_shifted(z, pads, above, below)
    for a in (0, 2):
        clear_guards(z, pads, a)


def band_operand(z, pads, taps=range(TAPS)):
    lane = lax.broadcasted_iota(jnp.int32, (1, 128), 1)
    parts = []
    for k in (1, 0):
        ref, step, count = pads[k], z.step[k], z.count[k]
        columns = []
        for a in taps:
            before = ref[a, 1, pl.ds(0, count), :]
            after = ref[a, 0, pl.ds(2 * step, count), :]
            columns += [
                ref[a, 0, pl.ds(step, count), :],
                ref[a, 1, pl.ds(step, count), :],
                jnp.where(lane >= 96, before, jnp.where(lane < 32, after, 0.0)),
            ]
        parts.append(jnp.concatenate(columns, axis=1))
    return jnp.concatenate(parts, axis=0)


def rim_operand(z, chain, depth):
    rows, g = (depth + 1) * z.rims, z.guard
    lane = lax.broadcasted_iota(jnp.int32, (1, 128), 1)
    m = lax.broadcasted_iota(jnp.int32, (z.rims, 1), 0)
    large = m < z.rim[0]
    has_before = jnp.where(large, m, m - z.rim[0]) >= jnp.where(large, z.images[1], z.images[0])
    has_after = m < jnp.where(large, z.rim[0] - z.images[1], z.rims - z.images[0])
    take = [(lane >= 96) & has_before & large, (lane >= 96) & has_before & ~large, (lane < 32) & has_after & large, (lane < 32) & has_after & ~large]
    columns = []
    for r in range(depth + 1):
        at = g + r * z.rims
        edge = jnp.zeros((z.rims, 128), F32)
        for mask, half, shift in zip(take, (1, 1, 0, 0), (-z.images[1], -z.images[0], z.images[1], z.images[0])):
            edge = jnp.where(mask, chain[half, pl.ds(at + shift, z.rims), :], edge)
        columns.append(jnp.concatenate([chain[0, pl.ds(at, z.rims), :], chain[1, pl.ds(at, z.rims), :], edge], axis=1))
    return jnp.concatenate(
        [jnp.concatenate(columns[n : n + TAPS], axis=1) for n in range(depth - 1)], axis=0
    )


def convolve(z, own, above, below, depth, pads, chains, weight):
    r = z.rims
    fill_pads(z, pads, own, above[(depth - 1) * r :], below[:r])
    parts = [band_operand(z, pads)]
    if depth > 1:
        for side, (rim, chain) in enumerate(zip((above, below), chains)):
            rim_at, own_at = (z.guard, z.guard + depth * r) if side == 0 else (z.guard + r, z.guard)
            for h in (0, 1):
                chain[h, pl.ds(rim_at, depth * r), :] = rim[:, 128 * h : 128 * h + 128]
                for k in (0, 1):
                    row = z.step[k] + (0 if side == 0 else z.rows[k] - 1)
                    chain[h, pl.ds(own_at + z.rim[k], z.edge[k]), :] = pads[k][1, h, pl.ds(row, z.edge[k], stride=z.rows[k]), :]
            parts.append(rim_operand(z, chain, depth))
    result = product(split(jnp.concatenate(parts, axis=0)), (weight_matrix(weight.at[0]), weight_matrix(weight.at[1])))
    n = z.total + (depth - 1) * r
    return result[: z.total], result[z.total : n], result[n:]


def image_sums(z, value):
    slot = lax.broadcasted_iota(jnp.int32, (z.slots, 1), 0)
    sums = jnp.zeros((z.slots, 128), F32)
    for k in (0, 1):
        line = value[z.start[k] : z.start[k] + z.step[k]]
        for j in range(1, z.blocks[k]):
            at = z.start[k] + j * z.step[k]
            line = line + value[at : at + z.step[k]]
        image = lax.broadcasted_iota(jnp.int32, (z.step[k], 1), 0) // z.rows[k]
        for i in range(z.images[k]):
            sums = jnp.where(slot == i + k * z.images[0], column_sum(jnp.where(image == i, line, 0.0)), sums)
    return sums


def image_rows(z, values, rims):
    parts = []
    for k in (1, 0):
        image = lax.broadcasted_iota(jnp.int32, (z.step[k], 1), 0) // z.rows[k]
        line = jnp.zeros((z.step[k], 128), F32)
        for i in range(z.images[k]):
            at = i + k * z.images[0]
            line = jnp.where(image == i, values[at : at + 1], line)
        parts += [line] * z.blocks[k]
    if rims:
        m = lax.broadcasted_iota(jnp.int32, (z.rims, 1), 0)
        image = jnp.where(m < z.rim[0], z.images[0] + m % z.images[1], (m - z.rim[0]) % z.images[0])
        line = jnp.zeros((z.rims, 128), F32)
        for at in range(sum(z.images)):
            line = jnp.where(image == at, values[at : at + 1], line)
        parts += [line] * rims
    return jnp.concatenate(parts, axis=0)


def channel_mean():
    a = lax.broadcasted_iota(jnp.int32, (LANES, 128), 0) // C
    b = lax.broadcasted_iota(jnp.int32, (LANES, 128), 1) % 64
    return jnp.where(a == b, 1.0 / C, 0.0).astype(F32)


def to_channels():
    a = lax.broadcasted_iota(jnp.int32, (128, LANES), 0)
    b = lax.broadcasted_iota(jnp.int32, (128, LANES), 1) // C
    return jnp.where(a == b, 1.0, 0.0).astype(F32)


def attention(value):
    return spread(value * value, channel_mean())


def start_all(copies):
    for copy in copies:
        copy.start()


def wait_all(copies):
    for copy in copies:
        copy.wait()


def start_kernel(z, small, large, up_s, up_l, t_s, t_l, x, bottom, top, copies, raw, half, sems):
    loads = [pltpu.make_async_copy(a, b, sems.at[n]) for n, (a, b) in enumerate(zip((small, large, up_s, up_l, t_s, t_l), raw))]
    start_all(loads)
    r, n = z.rims, REACH * z.rims
    tail = n + 2 * r
    for ref in (bottom, top):
        ref[pl.ds(tail, z.slots), :] = jnp.zeros((z.slots, LANES), F32)
    wait_all(loads[:2])
    to_matrix(z, raw[:2], half)
    value = whole(half)
    x[...] = value
    moments(z, value, copies)
    for h in (0, 1):
        lanes = pl.ds(128 * h, 128)
        take_rims(z, half.at[h], REACH, bottom.at[pl.ds(0, n), lanes], top.at[pl.ds(0, n), lanes])
    wait_all(loads[2:])
    for k in (0, 1):
        width, rows = HEIGHTS[k], z.rows[k]
        for i in range(z.images[k]):
            slot = pl.ds(tail + i + k * z.images[0], 1)
            for d in (0, 1):
                to_bottom, to_top = n + (1 - d) * r + z.rim[k] + i, n + d * r + z.rim[k] + i
                for j in range(z.blocks[k]):
                    lanes, at = pl.ds(LANES * j, LANES), j * z.images[k]
                    if d < rows:
                        bottom[pl.ds(to_bottom + at, 1), :] = raw[2 + k][i, pl.ds(rows - 1 - d, 1), lanes]
                        top[pl.ds(to_top + at, 1), :] = raw[2 + k][i, pl.ds(d, 1), lanes]
                    else:
                        bottom[pl.ds(to_bottom + at, 1), :] = jnp.zeros((1, LANES), F32)
                        top[pl.ds(to_top + at, 1), :] = jnp.zeros((1, LANES), F32)
                if d < rows:
                    bottom[slot, pl.ds(128 * (1 - d), width)] = raw[4 + k][i, pl.ds(rows - 1 - d, 1), :]
                    top[slot, pl.ds(128 * d, width)] = raw[4 + k][i, pl.ds(d, 1), :]


def banded(taps, ref):
    row = lax.broadcasted_iota(jnp.int32, (128, 128), 0) // C
    lane = group_of(128)
    for a in range(TAPS):
        main = jnp.zeros((128, 128), F32)
        for b in range(TAPS):
            main = jnp.where(row - lane + 1 == b, taps[a][b], main)
        before = jnp.where(lane[:C] == 0, taps[a][0][:C], 0.0)
        after = jnp.where(lane[:C] == 3, taps[a][2][:C], 0.0)
        for n, part in enumerate(split(jnp.concatenate([main, before, after], axis=0))):
            ref[n, pl.ds(a * TAP_ROWS, TAP_ROWS), :] = part


def weight_matrix(ref):
    rows = []
    zeros = jnp.zeros((128 - C, 128), BF16)
    for a in range(TAPS):
        at = a * TAP_ROWS
        main = ref[pl.ds(at, 128), :]
        before = jnp.concatenate([zeros, ref[pl.ds(at + 128, C), :]], axis=0)
        after = jnp.concatenate([ref[pl.ds(at + 128 + C, C), :], zeros], axis=0)
        rows += [
            jnp.concatenate([main, before], axis=1),
            jnp.concatenate([after, main], axis=1),
            jnp.concatenate([before, after], axis=1),
        ]
    return jnp.concatenate(rows, axis=0)


def prepare_kernel(z, first, second, up_s, up_l, t_s, t_l, g1, b1, g2, b2, x, w1, w2, weights, affine, upstream, teacher, x_copy, raw, kept, kept_u, rows, half, sems):
    targets = tuple(raw) + tuple(rows.at[pl.ds(n, 1), :] for n in range(4))
    refs = (first, second, up_s, up_l, t_s, t_l, g1, b1, g2, b2)
    loads = [pltpu.make_async_copy(a, b, sems.at[n]) for n, (a, b) in enumerate(zip(refs, targets))]
    start_all(loads)
    stores = [pltpu.make_async_copy(x, x_copy, sems.at[13])]
    stores[0].start()
    wait_all(loads)
    to_matrix(z, raw[2:4], half)
    kept_u[...] = whole(half)
    stores.append(pltpu.make_async_copy(kept_u, upstream, sems.at[10]))
    stores[1].start()
    for n, (source, forward) in enumerate(zip(raw[:2], (w1, w2))):
        tiles = []
        for a in range(TAPS):
            line = [jnp.concatenate([source[a, b]] * 4, axis=1) for b in range(TAPS)]
            tiles.append([jnp.concatenate([tap] * 4, axis=0) for tap in line])
        turned = [[tiles[TAPS - 1 - a][TAPS - 1 - b].T for b in range(TAPS)] for a in range(TAPS)]
        banded(tiles, forward)
        banded(turned, kept.at[n])
        stores.append(pltpu.make_async_copy(kept.at[n], weights.at[n], sems.at[11 + n]))
        stores[-1].start()
    affine[...] = jnp.concatenate([rows[...]] * BLOCK, axis=1)
    teacher[...] = jnp.zeros(teacher.shape, F32)
    for k, ref in ((0, raw[4]), (1, raw[5])):
        for i in range(z.images[k]):
            line = ref[i]
            for j in range(z.blocks[k]):
                at = z.start[k] + j * z.step[k] + i * z.rows[k]
                for lane in (0, 64):
                    teacher[pl.ds(at, z.rows[k]), pl.ds(lane, BLOCK)] = line[:, j * BLOCK : (j + 1) * BLOCK]
    wait_all(stores)


def normed_by(stats):
    return lambda v: (v - stats[0:1]) * stats[1:2]


def activation(center, scale, gain, bias):
    factor = scale * gain
    offset = bias - center * factor
    return lambda v: gelu(v * factor + offset)


def first_kernel(z, x, above, below, gathered, affine, weight, hidden, h_above, h_below, stats, copies, pads, chains):
    n = REACH * z.rims
    center, scale = merged(z, gathered)
    act = activation(center, scale, affine[0:1], affine[1:2])
    own = act(x[...])
    up, down = act(above[pl.ds(0, n), :]) * inside(z, 4, True), act(below[pl.ds(0, n), :]) * inside(z, 4, False)
    own, up, down = convolve(z, own, up, down, 4, pads, chains, weight)
    moments(z, own, copies)
    hidden[...] = own
    h_above[...] = up
    h_below[...] = down
    stats[0:1] = center
    stats[1:2] = scale


def second_kernel(z, hidden, h_above, h_below, gathered, affine, weight, x, x_above, x_below, teacher, out, o_above, o_below, near, stats, copies, pads, chains):
    center, scale = merged(z, gathered)
    act = activation(center, scale, affine[2:3], affine[3:4])
    r = z.rims
    own = act(hidden[...])
    up, down = act(h_above[...]) * inside(z, 3, True), act(h_below[...]) * inside(z, 3, False)
    own, up, down = convolve(z, own, up, down, 3, pads, chains, weight)
    own = x[...] + own
    amap = attention(own)
    lane = lax.broadcasted_iota(jnp.int32, (1, 128), 1)
    sums = image_sums(z, amap * jnp.where(lane < 64, amap, teacher[...]))
    copies[...] = jnp.concatenate([sums] * z.peers, axis=0)
    out[...] = own
    o_above[...] = x_above[pl.ds(2 * r, 2 * r), :] + up
    o_below[...] = x_below[pl.ds(0, 2 * r), :] + down
    near[0] = h_above[pl.ds(2 * r, r), :]
    near[1] = h_below[pl.ds(0, r), :]
    stats[0:1] = center
    stats[1:2] = scale


def tap_rows(q):
    return 128 + 3 * C if q < 0 else 128 if q == 4 else q * C


def tap_product(z, operand, own, above, below, pads):
    fill_center(z, pads, own)
    fill_shifted(z, pads, above, below)
    columns = []
    for a in range(TAPS):
        columns.append(
            jnp.concatenate([pads[k][TAPS - 1 - a, h, pl.ds(z.step[k], z.count[k]), :] for h in (0, 1) for k in (1, 0)], axis=0)
        )
    return product(operand, split(jnp.concatenate(columns, axis=1)))


def tap_sums(result, tiles, first_group):
    group = group_of()
    for a in range(TAPS):
        for b in range(TAPS):
            total = None
            for p in range(4):
                at = tap_rows(p + b - 1)
                part = result[at : at + C, 128 * a : 128 * a + 128]
                total = part if total is None else jnp.where(group == p, part, total)
            tile, slot = divmod(first_group + a * TAPS + b, 4)
            tiles[tile] = jnp.where(group == slot, spread_groups(total), tiles[tile])


def tap_counts(z, turned, tiles, first_group):
    group = group_of()
    m = lax.broadcasted_iota(jnp.int32, (1, 2 * z.total), 1) % z.total
    row = jnp.where(m < z.start[0], m % z.rows[1], (m - z.start[0]) % z.rows[0])
    height = jnp.where(m < z.start[0], z.rows[1], z.rows[0])
    at = lax.axis_index("row")
    lost = {
        0: (row == height - 1) & (at == z.peers - 1),
        2: (row == 0) & (at == 0),
    }
    for a in range(TAPS):
        column = jnp.sum(jnp.where(lost[a], 0.0, turned) if a in lost else turned, axis=1, keepdims=True)
        for b in range(TAPS):
            total = sum(column[tap_rows(p + b - 1) : tap_rows(p + b - 1) + C] for p in range(4))
            tile, slot = divmod(first_group + a * TAPS + b, 4)
            tiles[tile] = jnp.where(group == slot, total, tiles[tile])


def turned_operand(z, value, pads, kept):
    fill_center(z, pads, value)
    lane = lax.broadcasted_iota(jnp.int32, (1, 128), 1)
    halves = ([], [])
    for k in (1, 0):
        ref, step, count = pads[k], z.step[k], z.count[k]
        low, high = ref[1, 0, pl.ds(step, count), :], ref[1, 1, pl.ds(step, count), :]
        before, after = ref[1, 1, pl.ds(0, count), :], ref[1, 0, pl.ds(2 * step, count), :]
        for part, main, left, right in ((halves[0], low, before, high), (halves[1], high, low, after)):
            part.append(jnp.concatenate([main, jnp.where(lane >= 96, left, jnp.where(lane < 32, right, 0.0))], axis=1))
    turned = jnp.concatenate(halves[0] + halves[1], axis=0).T
    parts = split(turned)
    for n in (0, 1):
        kept[n] = parts[n]
    return turned


def first_operand_kernel(z, x, hidden, h_above, h_below, above, below, stats, affine, teacher, upstream, weights, left, packed, teachers, spread_u, near_u, pads, chains, kept, kept_w, kept_u, pixels, kept_t, kept_c, kept_packed, sems):
    r, own = z.rims, pl.ds(0, z.total)
    loads = [pltpu.make_async_copy(upstream, kept_u.at[own, :], sems.at[0]), pltpu.make_async_copy(weights.at[1], kept_w, sems.at[1])]
    start_all(loads)
    act = activation(stats[0:1], stats[1:2], affine[0:1], affine[1:2])
    value = turned_operand(z, act(x[...]), pads, kept)
    stores = [pltpu.make_async_copy(kept, left, sems.at[2])]
    stores[0].start()
    tiles = [jnp.zeros((C, 128), F32) for _ in range(BACK_LANES // 128)]
    tap_counts(z, value, tiles, ONES)
    result = tap_product(
        z, (kept[0], kept[1]), hidden[...], h_above[pl.ds(2 * r, r), :] * inside(z, 1, True), h_below[pl.ds(0, r), :] * inside(z, 1, False), pads
    )
    tap_sums(result, tiles, HIDDEN)
    kept_packed[...] = jnp.concatenate(tiles, axis=1)
    stores.append(pltpu.make_async_copy(kept_packed, packed, sems.at[6]))
    stores[1].start()
    pixels[own, :] = teacher[...]
    pixels[pl.ds(z.total, 4 * r), :] = jnp.zeros((4 * r, 128), F32)
    n = (REACH + 2) * r
    for side, ref in enumerate((above, below)):
        for d in (0, 1):
            for k in (0, 1):
                line = ref[pl.ds(n + k * z.images[0], z.images[k]), pl.ds(128 * d, 128)]
                for j in range(z.blocks[k]):
                    at = z.total + (2 * side + d) * r + z.rim[k] + j * z.images[k]
                    pixels[pl.ds(at, z.images[k]), pl.ds(0, BLOCK)] = line[:, j * BLOCK : (j + 1) * BLOCK]
    kept_t[...] = spread(pixels[...], to_channels())
    stores.append(pltpu.make_async_copy(kept_t, teachers, sems.at[3]))
    stores[2].start()
    n = REACH * r
    up, down = above[pl.ds(n, 2 * r), :] * inside(z, 2, True), below[pl.ds(n, 2 * r), :] * inside(z, 2, False)
    kept_u[pl.ds(z.total, r), :] = up[r:]
    kept_u[pl.ds(z.total + r, r), :] = down[:r]
    wait_all(loads)
    stores.append(pltpu.make_async_copy(kept_u, near_u, sems.at[5]))
    stores[3].start()
    kept_c[...] = jnp.concatenate(convolve(z, kept_u[own, :], up, down, 2, pads, chains, kept_w), axis=0)
    stores.append(pltpu.make_async_copy(kept_c, spread_u, sems.at[4]))
    stores[4].start()
    wait_all(stores)


def second_operand_kernel(z, hidden, near, stats, affine, out, o_above, o_below, teachers, spread_u, near_u, weights, out_copy, hidden_copy, left, shifts, by_map, by_teacher, up, pads, chains, kept_t, kept_u, kept_w, kept_s, sems):
    r, total = z.rims, z.total
    loads = [
        pltpu.make_async_copy(teachers, kept_t, sems.at[0]),
        pltpu.make_async_copy(weights.at[1], kept_w, sems.at[1]),
        pltpu.make_async_copy(spread_u, kept_u, sems.at[2]),
    ]
    start_all(loads)
    stores = [
        pltpu.make_async_copy(out, out_copy, sems.at[4]),
        pltpu.make_async_copy(hidden, hidden_copy.at[pl.ds(0, total), :], sems.at[7]),
        pltpu.make_async_copy(near.at[0], hidden_copy.at[pl.ds(total, r), :], sems.at[8]),
        pltpu.make_async_copy(near.at[1], hidden_copy.at[pl.ds(total + r, r), :], sems.at[9]),
        pltpu.make_async_copy(near_u, up, sems.at[10]),
    ]
    start_all(stores)
    normed = normed_by(stats)(jnp.concatenate([hidden[...], near[0], near[1]], axis=0))
    shifted = normed * affine[2:3] + affine[3:4]
    turned_operand(z, gelu(shifted[:total]), pads, left)
    ones = jnp.ones((total, 1), F32)
    masks = jnp.concatenate([ones, inside(z, 1, True), inside(z, 1, False)], axis=0)
    slopes = gelu_slope(shifted) * masks
    o = jnp.concatenate([out[...], o_above[...] * inside(z, 2, True), o_below[...] * inside(z, 2, False)], axis=0)
    for_map = spread(attention(o), to_channels()) * o
    wait_all(loads)
    for_teacher = kept_t[...] * o
    kept_s[0] = kept_u[...] * slopes
    for n, value, ref in ((1, for_map, by_map), (2, for_teacher, by_teacher)):
        own, before, after = value[:total], value[total : total + 2 * r], value[total + 2 * r :]
        ref[...] = jnp.concatenate([own, before[r:], after[:r]], axis=0)
        kept_s[n] = jnp.concatenate(convolve(z, own, before, after, 2, pads, chains, kept_w), axis=0) * slopes
    stores.append(pltpu.make_async_copy(kept_s, shifts, sems.at[5]))
    stores[-1].start()
    wait_all(stores)


def upstream_kernel(z, gathered, up, shifts, left_1, left_2, packed, by_map, by_teacher, hidden, stats, dout, dshift, d_above, d_below, slabs, kept_s, kept_left, kept_h, kept_packed, pads, more_pads, sems):
    r, total = z.rims, z.total
    loads = [
        pltpu.make_async_copy(a, b, sems.at[n])
        for n, (a, b) in enumerate(((shifts, kept_s), (left_1, kept_left), (hidden.at[pl.ds(0, total), :], kept_h), (packed, kept_packed)))
    ]
    start_all(loads)
    lane = lax.broadcasted_iota(jnp.int32, (z.slots, 128), 1)
    sums = sum(gathered[pl.ds(n * z.slots, z.slots), :] for n in range(z.peers))
    square = jnp.sum(jnp.where(lane < 64, sums, 0.0), axis=1, keepdims=True)
    cross = jnp.sum(jnp.where(lane < 64, 0.0, sums), axis=1, keepdims=True)
    inverse = lax.rsqrt(square + map_eps)
    inner = beta_weight * (square * inverse - cross) * inverse
    shape = (z.slots, 128)
    for_map = (beta_weight - inner) * inverse * inverse * (2.0 / C)
    for_teacher = beta_weight * inverse * (2.0 / C)
    for_map, for_teacher = (wide(image_rows(z, jnp.broadcast_to(v, shape), 2)) for v in (for_map, for_teacher))
    value = up[...] + for_map * by_map[...] - for_teacher * by_teacher[...]
    dout[...] = value[:total]
    wait_all(loads[:2])
    shift = kept_s[0] + for_map * kept_s[1] - for_teacher * kept_s[2]
    pre, above, below = shift[:total], shift[total : total + r], shift[total + r :]
    dshift[...] = pre
    d_above[...] = above
    d_below[...] = below
    second = tap_product(z, (left_2[0], left_2[1]), value[:total], value[total : total + r], value[total + r :], pads)
    first = tap_product(z, (kept_left[0], kept_left[1]), pre, above, below, more_pads)
    wait_all(loads[2:])
    normed = normed_by(stats)(kept_h[...])
    tiles = [kept_packed[:, 128 * n : 128 * n + 128] for n in range(BACK_LANES // 128)]
    group = group_of()
    tiles[0] = jnp.where(group == BIAS, fold(column_sum(pre)), jnp.where(group == GAIN, fold(column_sum(pre * normed)), tiles[0]))
    tap_sums(second, tiles, SECOND)
    tap_sums(first, tiles, LEFT)
    for first_device in range(0, z.devices, C):
        for n, tile in enumerate(tiles):
            slabs[pl.ds(first_device * len(tiles) + n, C, stride=len(tiles)), :] = tile


def write_kernel(z, out, x, hidden, weights, first_stats, stats, order, out_s, out_l, first_normed, normed, weight, kept, kept_x, kept_h, half, sems):
    loads = [pltpu.make_async_copy(a, b, sems.at[n]) for n, (a, b) in enumerate(((out, kept), (x, kept_x), (hidden, kept_h), (weights.at[0], weight)))]
    start_all(loads)
    loads[0].wait()
    put_halves(half, kept[...])
    from_matrix(z, half, (out_s, out_l))
    loads[1].wait()
    first_normed[...] = normed_by(first_stats)(kept_x[...])
    loads[2].wait()
    normed[...] = normed_by(stats)(kept_h[...])
    loads[3].wait()


def norm_sums(total):
    group = group_of()
    return [wide(spread_groups(jnp.where(group == n, total[:, :128], 0.0))) for n in (BIAS, GAIN)]


def hidden_kernel(z, gathered, dshift, d_above, d_below, second_normed, stats, affine, weight, first_normed, pre_ref, gain_out, bias_out, slabs, pads):
    lines = BACK_LANES // 128
    total = jnp.concatenate([column_sum(gathered[pl.ds(n, z.devices, stride=lines), :]) for n in range(lines)], axis=1)
    bias_sum, gain_sum = norm_sums(total)
    bias_out[...] = bias_sum[:, :C]
    gain_out[...] = gain_sum[:, :C]
    bias_mean, gain_mean = bias_sum / z.pixels, gain_sum / z.pixels
    factor = affine[2:3] * stats[1:2]
    r, total_rows = z.rims, z.total

    def back(d, normed):
        return factor * (d - bias_mean - normed * gain_mean)

    own = back(dshift[...], second_normed[pl.ds(0, total_rows), :])
    up = back(d_above[...], second_normed[pl.ds(total_rows, r), :]) * inside(z, 1, True)
    down = back(d_below[...], second_normed[pl.ds(total_rows + r, r), :]) * inside(z, 1, False)
    grad, _, _ = convolve(z, own, up, down, 1, pads, None, weight)
    normed = first_normed[...]
    pre = grad * gelu_slope(normed * affine[0:1] + affine[1:2])
    pre_ref[...] = pre
    lane = lax.broadcasted_iota(jnp.int32, (1, 128), 1)
    taps = TAPS * TAPS * C

    def along(row):
        return jnp.concatenate([row[:, :128]] * 3, axis=1)[:, :taps]

    second, left, against, ones = (total[:, n * C : n * C + taps] for n in (SECOND, LEFT, HIDDEN, ONES))
    against = along(stats[1:2]) * (against - along(stats[0:1]) * ones)
    first = along(factor) * (left - along(bias_mean) * ones - along(gain_mean) * against)
    sums = jnp.where(lane < C, fold(column_sum(pre)), fold(column_sum(pre * normed)))
    line = jnp.concatenate([sums[:, : 2 * C], second, first], axis=1)
    send_lines(z, slabs, [line[:, 128 * n : 128 * n + 128] for n in range(LAST_LANES // 128)])


def back_kernel(z, gathered, pre, normed, stats, affine, dout, back_s, back_l, one, two, gain_out, bias_out, half):
    lines = LAST_LANES // 128
    bias_sum, gain_sum = norm_sums(column_sum(gathered[pl.ds(0, z.devices, stride=lines), :]))
    bias_out[...] = bias_sum[:, :C]
    gain_out[...] = gain_sum[:, :C]
    value = dout[...] + affine[0:1] * stats[1:2] * (pre[...] - bias_sum / z.pixels - normed[...] * (gain_sum / z.pixels))
    put_halves(half, value)
    from_matrix(z, half, (back_s, back_l))
    kernels = jnp.concatenate([gathered[pl.ds(n, C, stride=lines), :] for n in range(lines)], axis=1)
    for ref, group in ((two, LAST_SECOND), (one, LAST_FIRST)):
        for a in range(TAPS):
            for b in range(TAPS):
                at = (group + a * TAPS + b) * C
                ref[a, b] = kernels[:, at : at + C]


def call(body, ins, outs, scratch=(), sems=0):
    space = {"v": pltpu.VMEM, "h": pltpu.HBM, "V": pltpu.VMEM}
    shapes = []
    for item in scratch:
        if isinstance(item, list):
            shapes.append([pltpu.VMEM(*s) for s in item])
        else:
            shapes.append(pltpu.VMEM(*item))
    if sems:
        shapes.append(pltpu.SemaphoreType.DMA((sems,)))
    run = pl.pallas_call(
        body,
        out_shape=[jax.ShapeDtypeStruct(shape, kind) if s == "v" else space[s](shape, kind) for s, shape, kind in outs],
        in_specs=[pl.BlockSpec(memory_space=space[s]) for s in ins],
        out_specs=[pl.BlockSpec(memory_space=space[s]) for s, _, _ in outs],
        scratch_shapes=shapes,
        compiler_params=pltpu.CompilerParams(vmem_limit_bytes=VMEM_LIMIT),
    )
    return lambda *args: run(
        *(pltpu.with_memory_space_constraint(arg, pltpu.HBM) if s == "h" else arg for s, arg in zip(ins, args))
    )


def exchange(lines, axes):
    count = math.prod(lax.axis_size(axis) for axis in axes)
    each = lines.shape[0] // count
    shape = (count, 1, each * 128) if each > 8 or each == 5 else (count, each, 128)
    return lax.all_to_all(lines.reshape(shape), axes, 0, 0, tiled=True).reshape(lines.shape)


def beyond(z, bottom, top, depths):
    hops = max(-(-depth // rows) for rows in z.rows for depth in depths)
    above, below = [], []
    for hop in range(1, hops + 1):
        above.append(lax.ppermute(bottom, "row", [(i, i + hop) for i in range(z.peers - hop)]))
        below.append(lax.ppermute(top, "row", [(i + hop, i) for i in range(z.peers - hop)]))
    if hops == 1:
        return above[0], below[0]
    up, down = [], []
    base = 0
    for depth in depths:
        for n in range(depth):
            for k in (1, 0):
                hop, back = divmod(depth - 1 - n, z.rows[k])
                at = base + (depth - 1 - back) * z.rims + z.rim[k]
                up.append(above[hop][at : at + z.edge[k]])
                hop, back = divmod(n, z.rows[k])
                at = base + back * z.rims + z.rim[k]
                down.append(below[hop][at : at + z.edge[k]])
        base += depth * z.rims
    up.append(jnp.concatenate([pixel_rows(z, above, base, 1, 1), pixel_rows(z, above, base, 0, 1)], axis=1))
    down.append(jnp.concatenate([pixel_rows(z, below, base, 0, 0), pixel_rows(z, below, base, 1, 0)], axis=1))
    return jnp.concatenate(up, axis=0), jnp.concatenate(down, axis=0)


def pixel_rows(z, bands, base, distance, last):
    lines = []
    for k in (0, 1):
        hop, back = divmod(distance, z.rows[k])
        at = base + k * z.images[0]
        half = 128 * abs(last - back)
        lines.append(bands[hop][at : at + z.images[k], half : half + 128])
    lines.append(jnp.zeros((z.slots - sum(z.images), 128), F32))
    return jnp.concatenate(lines, axis=0)


def local(
    image_small, image_large, teacher_small, teacher_large, upstream_small, upstream_large,
    conv_first, gain_first, bias_first, conv_second, gain_second, bias_second,
):
    peers = lax.axis_size("row")
    devices = lax.axis_size("img") * peers
    z = Sizes(image_small.shape, image_large.shape, devices, peers)
    body = lambda function: functools.partial(function, z)
    r = z.rims
    full, half, pair = (z.total, LANES), (2, z.total, 128), (devices * 2, 128)
    weight, left = (2, TAPS * TAP_ROWS, 128), (2, 256, 2 * z.total)
    images = [image_small, image_large, upstream_small, upstream_large, teacher_small, teacher_large]
    f = lambda space, *shape: (space, shape, F32)
    depths = (REACH, 2)
    rim_rows = sum(depths) * r + z.slots

    x, bottom, top, copies = call(
        body(start_kernel),
        "hhhhhh",
        [("v", full, F32), f("v", rim_rows, LANES), f("v", rim_rows, LANES), ("V", pair, F32)],
        [[(a.shape, F32) for a in images], (half, F32)],
        6,
    )(*images)
    gathered = exchange(copies, AXES)
    above, below = beyond(z, bottom, top, depths)
    params = [conv_first, conv_second] + images[2:]
    w1, w2, weights, affine, upstream, teacher, x_copy = call(
        body(prepare_kernel),
        "hhhhhhhhhhv",
        [("v", weight, BF16), ("v", weight, BF16), ("h", (2,) + weight, BF16), f("v", 4, LANES), ("h", full, F32), f("v", z.total, 128), ("h", full, F32)],
        [[(a.shape, F32) for a in params], ((2,) + weight, BF16), (full, F32), ((4, C), F32), (half, F32)],
        14,
    )(*params, *(v.reshape(1, C) for v in (gain_first, bias_first, gain_second, bias_second)), x)

    hidden, h_above, h_below, stats_one, copies = call(
        body(first_kernel),
        "vvvvvv",
        [("v", full, F32), f("v", 3 * r, LANES), f("v", 3 * r, LANES), f("v", 2, LANES), ("V", pair, F32)],
        [z.pads(), z.chains(4)],
    )(x, above, below, gathered, affine, w1)
    gathered = exchange(copies, AXES)
    extended, near_rows = z.total + 4 * r, z.total + 2 * r
    left_one, packed, teachers, spread_u, near_u = call(
        body(first_operand_kernel),
        "vvvvvvvvvhh",
        [("h", left, BF16), f("h", C, BACK_LANES), f("h", extended, LANES), f("h", near_rows, LANES), f("h", near_rows, LANES)],
        [
            z.pads(), z.chains(2), (left, BF16), (weight, BF16), ((near_rows, LANES), F32), ((extended, 128), F32),
            ((extended, LANES), F32), ((near_rows, LANES), F32), ((C, BACK_LANES), F32),
        ],
        7,
    )(x, hidden, h_above, h_below, above, below, stats_one, affine, teacher, upstream, weights)
    gathered, near_u = lax.optimization_barrier((gathered, near_u))

    map_shape = (peers * z.slots, 128)
    out, o_above, o_below, near, stats_two, copies = call(
        body(second_kernel),
        "vvvvvvvvvv",
        [("v", full, F32), f("v", 2 * r, LANES), f("v", 2 * r, LANES), f("v", 2, r, LANES), f("v", 2, LANES), ("V", map_shape, F32)],
        [z.pads(), z.chains(3)],
    )(hidden, h_above, h_below, gathered, affine, w2, x, above, below, teacher)
    gathered = exchange(copies, ("row",))
    out_copy, hidden_copy, left_two, shifts, by_map, by_teacher, up = call(
        body(second_operand_kernel),
        "vvvvvvvhhhh",
        [
            ("h", full, F32), f("h", near_rows, LANES), ("v", left, BF16), f("h", 3, near_rows, LANES),
            f("v", near_rows, LANES), f("v", near_rows, LANES), f("v", near_rows, LANES),
        ],
        [
            z.pads(), z.chains(2), ((extended, LANES), F32), ((near_rows, LANES), F32), (weight, BF16),
            ((3, near_rows, LANES), F32),
        ],
        11,
    )(hidden, near, stats_two, affine, out, o_above, o_below, teachers, spread_u, near_u, weights)

    dout, dshift, d_above, d_below, slabs = call(
        body(upstream_kernel),
        "vvhhvhvvhv",
        [("v", full, F32), ("v", full, F32), f("v", r, LANES), f("v", r, LANES), f("V", devices * BACK_LANES // 128, 128)],
        [((3, near_rows, LANES), F32), (left, BF16), (full, F32), ((C, BACK_LANES), F32), z.pads(), z.pads()],
        4,
    )(gathered, up, shifts, left_one, left_two, packed, by_map, by_teacher, hidden_copy, stats_two)
    gathered = exchange(slabs, AXES)
    out_s, out_l, first_normed, second_normed, weight_back = call(
        body(write_kernel),
        "hhhhvvv",
        [("v", image_small.shape, F32), ("v", image_large.shape, F32), ("v", full, F32), f("v", near_rows, LANES), ("v", weight, BF16)],
        [(full, F32), (full, F32), ((near_rows, LANES), F32), (half, F32)],
        4,
    )(out_copy, x_copy, hidden_copy, weights, stats_one, stats_two, d_above)

    pre, gain_two, bias_two, slabs = call(
        body(hidden_kernel),
        "vvvvvvvvv",
        [("v", full, F32), f("v", 1, C), f("v", 1, C), f("V", devices * LAST_LANES // 128, 128)],
        [z.pads()],
    )(gathered, dshift, d_above, d_below, second_normed, stats_two, affine, weight_back, first_normed)
    gathered = exchange(slabs, AXES)

    back_s, back_l, one, two, gain_one, bias_one = call(
        body(back_kernel),
        "vvvvvv",
        [("v", a.shape, F32) for a in (image_small, image_large, conv_first, conv_second)] + [f("v", 1, C), f("v", 1, C)],
        [(half, F32)],
    )(gathered, pre, first_normed, stats_one, affine, dout)
    return (
        out_s, out_l, back_s, back_l,
        one, gain_one.reshape(C), bias_one.reshape(C),
        two, gain_two.reshape(C), bias_two.reshape(C),
    )


def solution(mesh):
    split_bands, everywhere = P("img", "row", None), P()
    return jax.shard_map(
        local,
        mesh=mesh,
        in_specs=(split_bands,) * 6 + (everywhere,) * 6,
        out_specs=(split_bands,) * 4 + (everywhere,) * 6,
        check_vma=False,
    )
```

```python
import functools
import math

import jax
import jax.numpy as jnp
from jax import lax
from jax.experimental import pallas as pl
from jax.experimental.pallas import tpu as pltpu
from jax.sharding import PartitionSpec as P

C = 32
HS = 32
HL = 64
HEIGHTS = (HS, HL)

norm_eps = 1e-05
map_eps = 1e-06
beta_weight = 1000.0
AXES = ("img", "row")
BLOCK = 8
LANES = BLOCK * C
TAPS = 3
WIDTH = LANES + 128
DEPTH = TAPS * WIDTH
TAP_ROWS = 128 + 2 * C
REACH = 4
ROOT = math.sqrt(2.0 / math.pi)
CUBE = 0.044715
F32 = jnp.float32
BF16 = jnp.bfloat16
VMEM_LIMIT = 32 * 1024 * 1024
BIAS, GAIN, SECOND, LEFT, HIDDEN, ONES = 0, 1, 2, 11, 20, 29
BACK_LANES = 1280
LAST_SECOND, LAST_FIRST, LAST_LANES = 2, 11, 640


class Sizes:
    def __init__(self, small, large, devices, peers):
        self.images = (small[0], large[0])
        self.rows = (small[1], large[1])
        self.blocks = (HS // BLOCK, HL // BLOCK)
        self.step = tuple(n * r for n, r in zip(self.images, self.rows))
        self.count = tuple(b * s for b, s in zip(self.blocks, self.step))
        self.edge = tuple(b * n for b, n in zip(self.blocks, self.images))
        self.start = (self.count[1], 0)
        self.rim = (self.edge[1], 0)
        self.total = sum(self.count)
        self.rims = sum(self.edge)
        self.slots = -(-sum(self.images) // 8) * 8
        self.guard = -(-max(self.images) // 8) * 8
        self.devices = devices
        self.peers = peers
        self.here = float(self.total * BLOCK)
        self.pixels = self.here * devices

    def pads(self):
        return [((TAPS, 2, self.count[k] + 2 * self.step[k], 128), F32) for k in (0, 1)]

    def chains(self, depth):
        return [((2, 2 * self.guard + (depth + 1) * self.rims, 128), F32)] * 2


def split(value):
    high = value.astype(BF16)
    return high, (value - high.astype(F32)).astype(BF16)


def dot(left, right):
    return lax.dot_general(left, right, (((1,), (0,)), ((), ())), preferred_element_type=F32)


def product(left, right):
    if left[0].shape[1] % 128:
        return dot(left[0], right[0]) + (dot(left[0], right[1]) + dot(left[1], right[0]))
    return dot(
        jnp.concatenate([left[0], left[0], left[1]], axis=1), jnp.concatenate([right[0], right[1], right[0]], axis=0)
    )


def spread(left, right):
    right = right.astype(BF16)
    return dot(jnp.concatenate(split(left), axis=1), jnp.concatenate([right, right], axis=0))


def gelu(s):
    return 0.5 * s * (1.0 + jnp.tanh(ROOT * (s + CUBE * s * s * s)))


def gelu_slope(s):
    square = s * s
    t = jnp.tanh(ROOT * s * (1.0 + CUBE * square))
    return 0.5 * (1.0 + t) + 0.5 * s * (1.0 - t * t) * ROOT * (1.0 + 3.0 * CUBE * square)


def spread_groups(row):
    row = row + pltpu.roll(row, 64, 1)
    return row + pltpu.roll(row, 32, 1)


def fold(row):
    return spread_groups(row[:, :128] + row[:, 128:])


def wide(row):
    return jnp.concatenate([row, row], axis=1)


def group_of(rows=1, lanes=128):
    return lax.broadcasted_iota(jnp.int32, (rows, lanes), 1) // C


def column_sum(value):
    return jnp.sum(value, axis=0, keepdims=True)


def send_lines(z, ref, lines):
    for n, line in enumerate(lines):
        ref[pl.ds(n, z.devices, stride=len(lines)), :] = jnp.broadcast_to(line, (z.devices, 128))


def moments(z, value, ref):
    few = min(8, z.total)
    pivot = fold(column_sum(value[:few])) / float(few * BLOCK)
    off = value - wide(pivot)
    first, second = fold(column_sum(off)), fold(column_sum(off * off))
    send_lines(z, ref, [pivot + first / z.here, second - first * first / z.here])


def merged(z, ref):
    means = ref[pl.ds(0, z.devices, stride=2), :]
    center = jnp.mean(means, axis=0, keepdims=True)
    off = means - center
    within = jnp.mean(ref[pl.ds(1, z.devices, stride=2), :], axis=0, keepdims=True)
    variance = within / z.here + jnp.mean(off * off, axis=0, keepdims=True)
    return wide(center), wide(lax.rsqrt(variance + norm_eps))


def put_halves(ref, value):
    ref[0] = value[:, :128]
    ref[1] = value[:, 128:]


def whole(ref):
    return jnp.concatenate([ref[0], ref[1]], axis=1)


def to_matrix(z, refs, half):
    for k in (0, 1):
        for j in range(z.blocks[k]):
            at = z.start[k] + j * z.step[k]
            for i in range(z.images[k]):
                for h in (0, 1):
                    half[h, pl.ds(at + i * z.rows[k], z.rows[k]), :] = refs[k][i, :, pl.ds(LANES * j + 128 * h, 128)]


def from_matrix(z, half, refs):
    for k in (0, 1):
        for j in range(z.blocks[k]):
            at = z.start[k] + j * z.step[k]
            for i in range(z.images[k]):
                for h in (0, 1):
                    refs[k][i, :, pl.ds(LANES * j + 128 * h, 128)] = half[h, pl.ds(at + i * z.rows[k], z.rows[k]), :]


def take_rims(z, half, depth, bottom, top):
    for k in (0, 1):
        for d in range(1, depth + 1):
            to_bottom = pl.ds((depth - d) * z.rims + z.rim[k], z.edge[k])
            to_top = pl.ds((d - 1) * z.rims + z.rim[k], z.edge[k])
            if d <= z.rows[k]:
                bottom[to_bottom, :] = half[pl.ds(z.start[k] + z.rows[k] - d, z.edge[k], stride=z.rows[k]), :]
                top[to_top, :] = half[pl.ds(z.start[k] + d - 1, z.edge[k], stride=z.rows[k]), :]
            else:
                bottom[to_bottom, :] = jnp.zeros((z.edge[k], 128), F32)
                top[to_top, :] = jnp.zeros((z.edge[k], 128), F32)


def inside(z, depth, above):
    at = lax.axis_index("row")
    large = lax.broadcasted_iota(jnp.int32, (z.rims, 1), 0) < z.rim[0]
    parts = []
    for n in range(depth):
        if above:
            ok = [jnp.where(at * rows >= depth - n, 1.0, 0.0) for rows in z.rows]
        else:
            ok = [jnp.where((at + 1) * rows + n + 1 <= height, 1.0, 0.0) for rows, height in zip(z.rows, HEIGHTS)]
        parts.append(jnp.where(large, ok[1], ok[0]).astype(F32))
    return jnp.concatenate(parts, axis=0)


def clear_guards(z, pads, a):
    for k in (0, 1):
        pads[k][a, 1, pl.ds(0, z.step[k]), :] = jnp.zeros((z.step[k], 128), F32)
        pads[k][a, 0, pl.ds(z.step[k] + z.count[k], z.step[k]), :] = jnp.zeros((z.step[k], 128), F32)


def fill_center(z, pads, value):
    clear_guards(z, pads, 1)
    for k in (0, 1):
        for h in (0, 1):
            pads[k][1, h, pl.ds(z.step[k], z.count[k]), :] = value[z.start[k] : z.start[k] + z.count[k], 128 * h : 128 * h + 128]


def fill_shifted(z, pads, above, below):
    for k in (0, 1):
        ref, step, count, rows = pads[k], z.step[k], z.count[k], z.rows[k]
        rim = slice(z.rim[k], z.rim[k] + z.edge[k])
        for h in (0, 1):
            lanes = slice(128 * h, 128 * h + 128)
            ref[0, h, pl.ds(step, count), :] = ref[1, h, pl.ds(step - 1, count), :]
            ref[2, h, pl.ds(step, count), :] = ref[1, h, pl.ds(step + 1, count), :]
            ref[0, h, pl.ds(step, z.edge[k], stride=rows), :] = above[rim, lanes]
            ref[2, h, pl.ds(step + rows - 1, z.edge[k], stride=rows), :] = below[rim, lanes]


def fill_pads(z, pads, value, above, below):
    fill_center(z, pads, value)
    fill_shifted(z, pads, above, below)
    for a in (0, 2):
        clear_guards(z, pads, a)


def band_operand(z, pads, taps=range(TAPS)):
    lane = lax.broadcasted_iota(jnp.int32, (1, 128), 1)
    parts = []
    for k in (1, 0):
        ref, step, count = pads[k], z.step[k], z.count[k]
        columns = []
        for a in taps:
            before = ref[a, 1, pl.ds(0, count), :]
            after = ref[a, 0, pl.ds(2 * step, count), :]
            columns += [
                ref[a, 0, pl.ds(step, count), :],
                ref[a, 1, pl.ds(step, count), :],
                jnp.where(lane >= 96, before, jnp.where(lane < 32, after, 0.0)),
            ]
        parts.append(jnp.concatenate(columns, axis=1))
    return jnp.concatenate(parts, axis=0)


def rim_operand(z, chain, depth):
    rows, g = (depth + 1) * z.rims, z.guard
    lane = lax.broadcasted_iota(jnp.int32, (1, 128), 1)
    m = lax.broadcasted_iota(jnp.int32, (z.rims, 1), 0)
    large = m < z.rim[0]
    has_before = jnp.where(large, m, m - z.rim[0]) >= jnp.where(large, z.images[1], z.images[0])
    has_after = m < jnp.where(large, z.rim[0] - z.images[1], z.rims - z.images[0])
    take = [(lane >= 96) & has_before & large, (lane >= 96) & has_before & ~large, (lane < 32) & has_after & large, (lane < 32) & has_after & ~large]
    columns = []
    for r in range(depth + 1):
        at = g + r * z.rims
        edge = jnp.zeros((z.rims, 128), F32)
        for mask, half, shift in zip(take, (1, 1, 0, 0), (-z.images[1], -z.images[0], z.images[1], z.images[0])):
            edge = jnp.where(mask, chain[half, pl.ds(at + shift, z.rims), :], edge)
        columns.append(jnp.concatenate([chain[0, pl.ds(at, z.rims), :], chain[1, pl.ds(at, z.rims), :], edge], axis=1))
    return jnp.concatenate(
        [jnp.concatenate(columns[n : n + TAPS], axis=1) for n in range(depth - 1)], axis=0
    )


def rim_operands(z, pads, above, below, depth, chains):
    parts = []
    for side, (rim, chain) in enumerate(zip((above, below), chains)):
        rim_at, own_at = (z.guard, z.guard + depth * z.rims) if side == 0 else (z.guard + z.rims, z.guard)
        for h in (0, 1):
            chain[h, pl.ds(rim_at, depth * z.rims), :] = rim[:, 128 * h : 128 * h + 128]
            for k in (0, 1):
                row = z.step[k] + (0 if side == 0 else z.rows[k] - 1)
                chain[h, pl.ds(own_at + z.rim[k], z.edge[k]), :] = pads[k][1, h, pl.ds(row, z.edge[k], stride=z.rows[k]), :]
        parts.append(rim_operand(z, chain, depth))
    return parts


def times(parts, weight):
    return product(split(jnp.concatenate(parts, axis=0)), (weight_matrix(weight.at[0]), weight_matrix(weight.at[1])))


def convolve(z, own, above, below, depth, pads, chains, weight):
    r = z.rims
    fill_pads(z, pads, own, above[(depth - 1) * r :], below[:r])
    parts = [band_operand(z, pads)]
    if depth > 1:
        parts += rim_operands(z, pads, above, below, depth, chains)
    result = times(parts, weight)
    n = z.total + (depth - 1) * r
    return result[: z.total], result[z.total : n], result[n:]


def convolve_rims(z, pads, above, below, depth, chains, weight):
    result = times(rim_operands(z, pads, above, below, depth, chains), weight)
    n = (depth - 1) * z.rims
    return result[:n], result[n:]


def image_sums(z, value):
    slot = lax.broadcasted_iota(jnp.int32, (z.slots, 1), 0)
    sums = jnp.zeros((z.slots, 128), F32)
    for k in (0, 1):
        line = value[z.start[k] : z.start[k] + z.step[k]]
        for j in range(1, z.blocks[k]):
            at = z.start[k] + j * z.step[k]
            line = line + value[at : at + z.step[k]]
        image = lax.broadcasted_iota(jnp.int32, (z.step[k], 1), 0) // z.rows[k]
        for i in range(z.images[k]):
            sums = jnp.where(slot == i + k * z.images[0], column_sum(jnp.where(image == i, line, 0.0)), sums)
    return sums


def image_rows(z, values, rims):
    parts = []
    for k in (1, 0):
        image = lax.broadcasted_iota(jnp.int32, (z.step[k], 1), 0) // z.rows[k]
        line = jnp.zeros((z.step[k], 128), F32)
        for i in range(z.images[k]):
            at = i + k * z.images[0]
            line = jnp.where(image == i, values[at : at + 1], line)
        parts += [line] * z.blocks[k]
    if rims:
        m = lax.broadcasted_iota(jnp.int32, (z.rims, 1), 0)
        image = jnp.where(m < z.rim[0], z.images[0] + m % z.images[1], (m - z.rim[0]) % z.images[0])
        line = jnp.zeros((z.rims, 128), F32)
        for at in range(sum(z.images)):
            line = jnp.where(image == at, values[at : at + 1], line)
        parts += [line] * rims
    return jnp.concatenate(parts, axis=0)


def channel_mean():
    a = lax.broadcasted_iota(jnp.int32, (LANES, 128), 0) // C
    b = lax.broadcasted_iota(jnp.int32, (LANES, 128), 1) % 64
    return jnp.where(a == b, 1.0 / C, 0.0).astype(F32)


def to_channels():
    a = lax.broadcasted_iota(jnp.int32, (128, LANES), 0)
    b = lax.broadcasted_iota(jnp.int32, (128, LANES), 1) // C
    return jnp.where(a == b, 1.0, 0.0).astype(F32)


def attention(value):
    return spread(value * value, channel_mean())


def start_all(copies):
    for copy in copies:
        copy.start()


def wait_all(copies):
    for copy in copies:
        copy.wait()


def start_kernel(z, small, large, up_s, up_l, t_s, t_l, x, bottom, top, copies, raw, half, sems):
    loads = [pltpu.make_async_copy(a, b, sems.at[n]) for n, (a, b) in enumerate(zip((small, large, up_s, up_l, t_s, t_l), raw))]
    start_all(loads)
    r, n = z.rims, REACH * z.rims
    tail = n + 2 * r
    for ref in (bottom, top):
        ref[pl.ds(tail, z.slots), :] = jnp.zeros((z.slots, LANES), F32)
    wait_all(loads[:2])
    to_matrix(z, raw[:2], half)
    value = whole(half)
    x[...] = value
    moments(z, value, copies)
    for h in (0, 1):
        lanes = pl.ds(128 * h, 128)
        take_rims(z, half.at[h], REACH, bottom.at[pl.ds(0, n), lanes], top.at[pl.ds(0, n), lanes])
    wait_all(loads[2:])
    for k in (0, 1):
        width, rows = HEIGHTS[k], z.rows[k]
        for i in range(z.images[k]):
            slot = pl.ds(tail + i + k * z.images[0], 1)
            for d in (0, 1):
                to_bottom, to_top = n + (1 - d) * r + z.rim[k] + i, n + d * r + z.rim[k] + i
                for j in range(z.blocks[k]):
                    lanes, at = pl.ds(LANES * j, LANES), j * z.images[k]
                    if d < rows:
                        bottom[pl.ds(to_bottom + at, 1), :] = raw[2 + k][i, pl.ds(rows - 1 - d, 1), lanes]
                        top[pl.ds(to_top + at, 1), :] = raw[2 + k][i, pl.ds(d, 1), lanes]
                    else:
                        bottom[pl.ds(to_bottom + at, 1), :] = jnp.zeros((1, LANES), F32)
                        top[pl.ds(to_top + at, 1), :] = jnp.zeros((1, LANES), F32)
                if d < rows:
                    bottom[slot, pl.ds(128 * (1 - d), width)] = raw[4 + k][i, pl.ds(rows - 1 - d, 1), :]
                    top[slot, pl.ds(128 * d, width)] = raw[4 + k][i, pl.ds(d, 1), :]


def banded(taps, ref):
    row = lax.broadcasted_iota(jnp.int32, (128, 128), 0) // C
    lane = group_of(128)
    for a in range(TAPS):
        main = jnp.zeros((128, 128), F32)
        for b in range(TAPS):
            main = jnp.where(row - lane + 1 == b, taps[a][b], main)
        before = jnp.where(lane[:C] == 0, taps[a][0][:C], 0.0)
        after = jnp.where(lane[:C] == 3, taps[a][2][:C], 0.0)
        for n, part in enumerate(split(jnp.concatenate([main, before, after], axis=0))):
            ref[n, pl.ds(a * TAP_ROWS, TAP_ROWS), :] = part


def weight_matrix(ref):
    rows = []
    zeros = jnp.zeros((128 - C, 128), BF16)
    for a in range(TAPS):
        at = a * TAP_ROWS
        main = ref[pl.ds(at, 128), :]
        before = jnp.concatenate([zeros, ref[pl.ds(at + 128, C), :]], axis=0)
        after = jnp.concatenate([ref[pl.ds(at + 128 + C, C), :], zeros], axis=0)
        rows += [
            jnp.concatenate([main, before], axis=1),
            jnp.concatenate([after, main], axis=1),
            jnp.concatenate([before, after], axis=1),
        ]
    return jnp.concatenate(rows, axis=0)


def prepare_kernel(z, first, second, up_s, up_l, t_s, t_l, g1, b1, g2, b2, x, w1, w2, weights, affine, upstream, teacher, x_copy, raw, kept, kept_u, rows, half, sems):
    targets = tuple(raw) + tuple(rows.at[pl.ds(n, 1), :] for n in range(4))
    refs = (first, second, up_s, up_l, t_s, t_l, g1, b1, g2, b2)
    loads = [pltpu.make_async_copy(a, b, sems.at[n]) for n, (a, b) in enumerate(zip(refs, targets))]
    start_all(loads)
    stores = [pltpu.make_async_copy(x, x_copy, sems.at[15])]
    stores[0].start()
    wait_all(loads)
    to_matrix(z, raw[2:4], half)
    kept_u[...] = whole(half)
    stores.append(pltpu.make_async_copy(kept_u, upstream, sems.at[10]))
    stores[1].start()
    for n, (source, forward) in enumerate(zip(raw[:2], (w1, w2))):
        tiles = []
        for a in range(TAPS):
            line = [jnp.concatenate([source[a, b]] * 4, axis=1) for b in range(TAPS)]
            tiles.append([jnp.concatenate([tap] * 4, axis=0) for tap in line])
        turned = [[tiles[TAPS - 1 - a][TAPS - 1 - b].T for b in range(TAPS)] for a in range(TAPS)]
        for at, taps in ((n, tiles), (3 - n, turned)):
            banded(taps, kept.at[at])
            stores.append(pltpu.make_async_copy(kept.at[at], weights.at[at], sems.at[11 + at]))
            stores[-1].start()
        forward[...] = kept[n]
    affine[...] = jnp.concatenate([rows[...]] * BLOCK, axis=1)
    teacher[...] = jnp.zeros(teacher.shape, F32)
    for k, ref in ((0, raw[4]), (1, raw[5])):
        for i in range(z.images[k]):
            line = ref[i]
            for j in range(z.blocks[k]):
                at = z.start[k] + j * z.step[k] + i * z.rows[k]
                for lane in (0, 64):
                    teacher[pl.ds(at, z.rows[k]), pl.ds(lane, BLOCK)] = line[:, j * BLOCK : (j + 1) * BLOCK]
    wait_all(stores)


def normed_by(stats):
    return lambda v: (v - stats[0:1]) * stats[1:2]


def activation(center, scale, gain, bias):
    factor = scale * gain
    offset = bias - center * factor
    return lambda v: gelu(v * factor + offset)


def first_kernel(z, x, above, below, gathered, affine, weight, hidden, stats, copies, pads):
    center, scale = merged(z, gathered)
    act = activation(center, scale, affine[0:1], affine[1:2])
    r = z.rims
    up, down = act(above[pl.ds(3 * r, r), :]) * inside(z, 1, True), act(below[pl.ds(0, r), :]) * inside(z, 1, False)
    own, _, _ = convolve(z, act(x[...]), up, down, 1, pads, None, weight)
    moments(z, own, copies)
    hidden[...] = own
    stats[0:1] = center
    stats[1:2] = scale


def second_kernel(z, hidden, h_above, h_below, gathered, affine, weight, x, teacher, out, stats, copies, pads):
    center, scale = merged(z, gathered)
    act = activation(center, scale, affine[2:3], affine[3:4])
    r = z.rims
    up, down = act(h_above[pl.ds(2 * r, r), :]) * inside(z, 1, True), act(h_below[pl.ds(0, r), :]) * inside(z, 1, False)
    own, _, _ = convolve(z, act(hidden[...]), up, down, 1, pads, None, weight)
    own = x[...] + own
    amap = attention(own)
    lane = lax.broadcasted_iota(jnp.int32, (1, 128), 1)
    sums = image_sums(z, amap * jnp.where(lane < 64, amap, teacher[...]))
    copies[...] = jnp.concatenate([sums] * z.peers, axis=0)
    out[...] = own
    stats[0:1] = center
    stats[1:2] = scale


def tap_rows(q):
    return 128 + 3 * C if q < 0 else 128 if q == 4 else q * C


def tap_product(z, operand, own, above, below, pads):
    fill_center(z, pads, own)
    fill_shifted(z, pads, above, below)
    columns = []
    for a in range(TAPS):
        columns.append(
            jnp.concatenate([pads[k][TAPS - 1 - a, h, pl.ds(z.step[k], z.count[k]), :] for h in (0, 1) for k in (1, 0)], axis=0)
        )
    return product(operand, split(jnp.concatenate(columns, axis=1)))


def tap_sums(result, tiles, first_group):
    group = group_of()
    for a in range(TAPS):
        for b in range(TAPS):
            total = None
            for p in range(4):
                at = tap_rows(p + b - 1)
                part = result[at : at + C, 128 * a : 128 * a + 128]
                total = part if total is None else jnp.where(group == p, part, total)
            tile, slot = divmod(first_group + a * TAPS + b, 4)
            tiles[tile] = jnp.where(group == slot, spread_groups(total), tiles[tile])


def tap_counts(z, turned, tiles, first_group):
    group = group_of()
    m = lax.broadcasted_iota(jnp.int32, (1, 2 * z.total), 1) % z.total
    row = jnp.where(m < z.start[0], m % z.rows[1], (m - z.start[0]) % z.rows[0])
    height = jnp.where(m < z.start[0], z.rows[1], z.rows[0])
    at = lax.axis_index("row")
    lost = {
        0: (row == height - 1) & (at == z.peers - 1),
        2: (row == 0) & (at == 0),
    }
    for a in range(TAPS):
        column = jnp.sum(jnp.where(lost[a], 0.0, turned) if a in lost else turned, axis=1, keepdims=True)
        for b in range(TAPS):
            total = sum(column[tap_rows(p + b - 1) : tap_rows(p + b - 1) + C] for p in range(4))
            tile, slot = divmod(first_group + a * TAPS + b, 4)
            tiles[tile] = jnp.where(group == slot, total, tiles[tile])


def turned_operand(z, value, pads, kept):
    fill_center(z, pads, value)
    lane = lax.broadcasted_iota(jnp.int32, (1, 128), 1)
    halves = ([], [])
    for k in (1, 0):
        ref, step, count = pads[k], z.step[k], z.count[k]
        low, high = ref[1, 0, pl.ds(step, count), :], ref[1, 1, pl.ds(step, count), :]
        before, after = ref[1, 1, pl.ds(0, count), :], ref[1, 0, pl.ds(2 * step, count), :]
        for part, main, left, right in ((halves[0], low, before, high), (halves[1], high, low, after)):
            part.append(jnp.concatenate([main, jnp.where(lane >= 96, left, jnp.where(lane < 32, right, 0.0))], axis=1))
    turned = jnp.concatenate(halves[0] + halves[1], axis=0).T
    parts = split(turned)
    for n in (0, 1):
        kept[n] = parts[n]
    return turned


def first_operand_kernel(z, x, hidden, above, below, stats, affine, teacher, upstream, weights, h_above, h_below, left, packed, teachers, spread_u, near_u, near_x, pads, chains, deep_chains, kept, kept_w, kept_u, pixels, kept_t, kept_c, kept_packed, sems):
    r, own = z.rims, pl.ds(0, z.total)
    loads = [
        pltpu.make_async_copy(weights.at[0], kept_w.at[0], sems.at[0]),
        pltpu.make_async_copy(upstream, kept_u.at[own, :], sems.at[1]),
        pltpu.make_async_copy(weights.at[2], kept_w.at[1], sems.at[7]),
    ]
    start_all(loads)
    stores = [
        pltpu.make_async_copy(above.at[pl.ds(2 * r, 2 * r), :], near_x.at[0], sems.at[8]),
        pltpu.make_async_copy(below.at[pl.ds(0, 2 * r), :], near_x.at[1], sems.at[9]),
    ]
    start_all(stores)
    act = activation(stats[0:1], stats[1:2], affine[0:1], affine[1:2])
    value = turned_operand(z, act(x[...]), pads, kept)
    stores.append(pltpu.make_async_copy(kept, left, sems.at[2]))
    stores[-1].start()
    n = REACH * r
    up, down = act(above[pl.ds(0, n), :]) * inside(z, REACH, True), act(below[pl.ds(0, n), :]) * inside(z, REACH, False)
    loads[0].wait()
    up, down = convolve_rims(z, pads, up, down, REACH, deep_chains, kept_w.at[0])
    h_above[...] = up
    h_below[...] = down
    tiles = [jnp.zeros((C, 128), F32) for _ in range(BACK_LANES // 128)]
    tap_counts(z, value, tiles, ONES)
    result = tap_product(
        z, (kept[0], kept[1]), hidden[...], up[2 * r :] * inside(z, 1, True), down[:r] * inside(z, 1, False), pads
    )
    tap_sums(result, tiles, HIDDEN)
    kept_packed[...] = jnp.concatenate(tiles, axis=1)
    stores.append(pltpu.make_async_copy(kept_packed, packed, sems.at[6]))
    stores[-1].start()
    pixels[own, :] = teacher[...]
    pixels[pl.ds(z.total, 4 * r), :] = jnp.zeros((4 * r, 128), F32)
    n = (REACH + 2) * r
    for side, ref in enumerate((above, below)):
        for d in (0, 1):
            for k in (0, 1):
                line = ref[pl.ds(n + k * z.images[0], z.images[k]), pl.ds(128 * d, 128)]
                for j in range(z.blocks[k]):
                    at = z.total + (2 * side + d) * r + z.rim[k] + j * z.images[k]
                    pixels[pl.ds(at, z.images[k]), pl.ds(0, BLOCK)] = line[:, j * BLOCK : (j + 1) * BLOCK]
    kept_t[...] = spread(pixels[...], to_channels())
    stores.append(pltpu.make_async_copy(kept_t, teachers, sems.at[3]))
    stores[-1].start()
    n = REACH * r
    up, down = above[pl.ds(n, 2 * r), :] * inside(z, 2, True), below[pl.ds(n, 2 * r), :] * inside(z, 2, False)
    kept_u[pl.ds(z.total, r), :] = up[r:]
    kept_u[pl.ds(z.total + r, r), :] = down[:r]
    wait_all(loads[1:])
    stores.append(pltpu.make_async_copy(kept_u, near_u, sems.at[5]))
    stores[-1].start()
    kept_c[...] = jnp.concatenate(convolve(z, kept_u[own, :], up, down, 2, pads, chains, kept_w.at[1]), axis=0)
    stores.append(pltpu.make_async_copy(kept_c, spread_u, sems.at[4]))
    stores[-1].start()
    wait_all(stores)


def second_operand_kernel(z, hidden, h_above, h_below, stats, affine, out, near_x, teachers, spread_u, near_u, weights, out_copy, hidden_copy, left, shifts, by_map, by_teacher, up, pads, chains, deep_chains, kept_x, kept_t, kept_u, kept_w, kept_s, sems):
    r, total = z.rims, z.total
    loads = [
        pltpu.make_async_copy(weights.at[1], kept_w.at[0], sems.at[0]),
        pltpu.make_async_copy(near_x, kept_x, sems.at[1]),
        pltpu.make_async_copy(weights.at[2], kept_w.at[1], sems.at[2]),
        pltpu.make_async_copy(teachers, kept_t, sems.at[3]),
        pltpu.make_async_copy(spread_u, kept_u, sems.at[6]),
    ]
    start_all(loads)
    stores = [
        pltpu.make_async_copy(near_u, up, sems.at[10]),
        pltpu.make_async_copy(out, out_copy, sems.at[4]),
        pltpu.make_async_copy(hidden, hidden_copy.at[pl.ds(0, total), :], sems.at[7]),
        pltpu.make_async_copy(h_above.at[pl.ds(2 * r, r), :], hidden_copy.at[pl.ds(total, r), :], sems.at[8]),
        pltpu.make_async_copy(h_below.at[pl.ds(0, r), :], hidden_copy.at[pl.ds(total + r, r), :], sems.at[9]),
    ]
    start_all(stores)
    unit = normed_by(stats)
    gain, bias = affine[2:3], affine[3:4]
    shifted = unit(hidden[...]) * gain + bias
    before, after = (unit(ref[...]) * gain + bias for ref in (h_above, h_below))
    turned_operand(z, gelu(shifted), pads, left)
    slopes = jnp.concatenate(
        [gelu_slope(shifted), gelu_slope(before[2 * r :]) * inside(z, 1, True), gelu_slope(after[:r]) * inside(z, 1, False)], axis=0
    )
    loads[0].wait()
    o_up, o_down = convolve_rims(
        z, pads, gelu(before) * inside(z, 3, True), gelu(after) * inside(z, 3, False), 3, deep_chains, kept_w.at[0]
    )
    loads[1].wait()
    o = jnp.concatenate([out[...], (kept_x[0] + o_up) * inside(z, 2, True), (kept_x[1] + o_down) * inside(z, 2, False)], axis=0)
    for_map = spread(attention(o), to_channels()) * o
    wait_all(loads[2:])
    for_teacher = kept_t[...] * o
    kept_s[0] = kept_u[...] * slopes
    for n, value, ref in ((1, for_map, by_map), (2, for_teacher, by_teacher)):
        own, before, after = value[:total], value[total : total + 2 * r], value[total + 2 * r :]
        ref[...] = jnp.concatenate([own, before[r:], after[:r]], axis=0)
        kept_s[n] = jnp.concatenate(convolve(z, own, before, after, 2, pads, chains, kept_w.at[1]), axis=0) * slopes
    stores.append(pltpu.make_async_copy(kept_s, shifts, sems.at[5]))
    stores[-1].start()
    wait_all(stores)


def upstream_kernel(z, gathered, up, shifts, left_1, left_2, packed, by_map, by_teacher, hidden, stats, dout, dshift, d_above, d_below, slabs, kept_s, kept_left, kept_h, kept_packed, pads, more_pads, sems):
    r, total = z.rims, z.total
    loads = [
        pltpu.make_async_copy(a, b, sems.at[n])
        for n, (a, b) in enumerate(((shifts, kept_s), (left_1, kept_left), (hidden.at[pl.ds(0, total), :], kept_h), (packed, kept_packed)))
    ]
    start_all(loads)
    lane = lax.broadcasted_iota(jnp.int32, (z.slots, 128), 1)
    sums = sum(gathered[pl.ds(n * z.slots, z.slots), :] for n in range(z.peers))
    square = jnp.sum(jnp.where(lane < 64, sums, 0.0), axis=1, keepdims=True)
    cross = jnp.sum(jnp.where(lane < 64, 0.0, sums), axis=1, keepdims=True)
    inverse = lax.rsqrt(square + map_eps)
    inner = beta_weight * (square * inverse - cross) * inverse
    shape = (z.slots, 128)
    for_map = (beta_weight - inner) * inverse * inverse * (2.0 / C)
    for_teacher = beta_weight * inverse * (2.0 / C)
    for_map, for_teacher = (wide(image_rows(z, jnp.broadcast_to(v, shape), 2)) for v in (for_map, for_teacher))
    value = up[...] + for_map * by_map[...] - for_teacher * by_teacher[...]
    dout[...] = value[:total]
    wait_all(loads[:2])
    shift = kept_s[0] + for_map * kept_s[1] - for_teacher * kept_s[2]
    pre, above, below = shift[:total], shift[total : total + r], shift[total + r :]
    dshift[...] = pre
    d_above[...] = above
    d_below[...] = below
    second = tap_product(z, (left_2[0], left_2[1]), value[:total], value[total : total + r], value[total + r :], pads)
    first = tap_product(z, (kept_left[0], kept_left[1]), pre, above, below, more_pads)
    wait_all(loads[2:])
    normed = normed_by(stats)(kept_h[...])
    tiles = [kept_packed[:, 128 * n : 128 * n + 128] for n in range(BACK_LANES // 128)]
    group = group_of()
    tiles[0] = jnp.where(group == BIAS, fold(column_sum(pre)), jnp.where(group == GAIN, fold(column_sum(pre * normed)), tiles[0]))
    tap_sums(second, tiles, SECOND)
    tap_sums(first, tiles, LEFT)
    line = jnp.concatenate(tiles, axis=1)
    for d in range(z.devices):
        slabs[d] = line[d % C : d % C + 1]


def write_kernel(z, out, x, hidden, weights, first_stats, stats, order, out_s, out_l, first_normed, normed, weight, kept, kept_x, kept_h, half, sems):
    loads = [pltpu.make_async_copy(a, b, sems.at[n]) for n, (a, b) in enumerate(((out, kept), (x, kept_x), (hidden, kept_h), (weights.at[3], weight)))]
    start_all(loads)
    loads[0].wait()
    put_halves(half, kept[...])
    from_matrix(z, half, (out_s, out_l))
    loads[1].wait()
    first_normed[...] = normed_by(first_stats)(kept_x[...])
    loads[2].wait()
    normed[...] = normed_by(stats)(kept_h[...])
    loads[3].wait()


def norm_sums(total):
    group = group_of()
    return [wide(spread_groups(jnp.where(group == n, total[:, :128], 0.0))) for n in (BIAS, GAIN)]


def hidden_kernel(z, gathered, dshift, d_above, d_below, second_normed, stats, affine, weight, first_normed, pre_ref, gain_out, bias_out, slabs, pads):
    total = jnp.sum(gathered[...], axis=0)
    bias_sum, gain_sum = norm_sums(total)
    bias_out[...] = bias_sum[:, :C]
    gain_out[...] = gain_sum[:, :C]
    bias_mean, gain_mean = bias_sum / z.pixels, gain_sum / z.pixels
    factor = affine[2:3] * stats[1:2]
    r, total_rows = z.rims, z.total

    def back(d, normed):
        return factor * (d - bias_mean - normed * gain_mean)

    own = back(dshift[...], second_normed[pl.ds(0, total_rows), :])
    up = back(d_above[...], second_normed[pl.ds(total_rows, r), :]) * inside(z, 1, True)
    down = back(d_below[...], second_normed[pl.ds(total_rows + r, r), :]) * inside(z, 1, False)
    grad, _, _ = convolve(z, own, up, down, 1, pads, None, weight)
    normed = first_normed[...]
    pre = grad * gelu_slope(normed * affine[0:1] + affine[1:2])
    pre_ref[...] = pre
    lane = lax.broadcasted_iota(jnp.int32, (1, 128), 1)
    taps = TAPS * TAPS * C

    def along(row):
        return jnp.concatenate([row[:, :128]] * 3, axis=1)[:, :taps]

    second, left, against, ones = (total[:, n * C : n * C + taps] for n in (SECOND, LEFT, HIDDEN, ONES))
    against = along(stats[1:2]) * (against - along(stats[0:1]) * ones)
    first = along(factor) * (left - along(bias_mean) * ones - along(gain_mean) * against)
    sums = jnp.where(lane < C, fold(column_sum(pre)), fold(column_sum(pre * normed)))
    line = jnp.concatenate([sums[:, : 2 * C], second, first], axis=1)
    slabs[...] = jnp.broadcast_to(line[None], slabs.shape)


def back_kernel(z, gathered, pre, normed, stats, affine, dout, back_s, back_l, one, two, gain_out, bias_out, half, lines):
    bias_sum, gain_sum = norm_sums(jnp.sum(gathered[:, :, pl.ds(0, 128)], axis=0))
    bias_out[...] = bias_sum[:, :C]
    gain_out[...] = gain_sum[:, :C]
    value = dout[...] + affine[0:1] * stats[1:2] * (pre[...] - bias_sum / z.pixels - normed[...] * (gain_sum / z.pixels))
    put_halves(half, value)
    from_matrix(z, half, (back_s, back_l))
    for d in range(C):
        lines[pl.ds(d, 1), :] = gathered[d]
    for ref, group in ((two, LAST_SECOND), (one, LAST_FIRST)):
        for a in range(TAPS):
            for b in range(TAPS):
                at = (group + a * TAPS + b) * C
                ref[a, b] = lines[:, pl.ds(at, C)]


def call(body, ins, outs, scratch=(), sems=0):
    space = {"v": pltpu.VMEM, "h": pltpu.HBM, "V": pltpu.VMEM}
    shapes = []
    for item in scratch:
        if isinstance(item, list):
            shapes.append([pltpu.VMEM(*s) for s in item])
        else:
            shapes.append(pltpu.VMEM(*item))
    if sems:
        shapes.append(pltpu.SemaphoreType.DMA((sems,)))
    run = pl.pallas_call(
        body,
        out_shape=[jax.ShapeDtypeStruct(shape, kind) if s == "v" else space[s](shape, kind) for s, shape, kind in outs],
        in_specs=[pl.BlockSpec(memory_space=space[s]) for s in ins],
        out_specs=[pl.BlockSpec(memory_space=space[s]) for s, _, _ in outs],
        scratch_shapes=shapes,
        compiler_params=pltpu.CompilerParams(vmem_limit_bytes=VMEM_LIMIT),
    )
    return lambda *args: run(
        *(pltpu.with_memory_space_constraint(arg, pltpu.HBM) if s == "h" else arg for s, arg in zip(ins, args))
    )


def exchange(lines, axes):
    shape = lines.shape
    if len(shape) == 2:
        lines = lines.reshape(math.prod(lax.axis_size(axis) for axis in axes), -1, 128)
    return lax.all_to_all(lines, axes, 0, 0, tiled=True).reshape(shape)


def beyond(z, bottom, top, depths):
    hops = max(-(-depth // rows) for rows in z.rows for depth in depths)
    above, below = [], []
    for hop in range(1, hops + 1):
        above.append(lax.ppermute(bottom, "row", [(i, i + hop) for i in range(z.peers - hop)]))
        below.append(lax.ppermute(top, "row", [(i + hop, i) for i in range(z.peers - hop)]))
    if hops == 1:
        return above[0], below[0]
    up, down = [], []
    base = 0
    for depth in depths:
        for n in range(depth):
            for k in (1, 0):
                hop, back = divmod(depth - 1 - n, z.rows[k])
                at = base + (depth - 1 - back) * z.rims + z.rim[k]
                up.append(above[hop][at : at + z.edge[k]])
                hop, back = divmod(n, z.rows[k])
                at = base + back * z.rims + z.rim[k]
                down.append(below[hop][at : at + z.edge[k]])
        base += depth * z.rims
    up.append(jnp.concatenate([pixel_rows(z, above, base, 1, 1), pixel_rows(z, above, base, 0, 1)], axis=1))
    down.append(jnp.concatenate([pixel_rows(z, below, base, 0, 0), pixel_rows(z, below, base, 1, 0)], axis=1))
    return jnp.concatenate(up, axis=0), jnp.concatenate(down, axis=0)


def pixel_rows(z, bands, base, distance, last):
    lines = []
    for k in (0, 1):
        hop, back = divmod(distance, z.rows[k])
        at = base + k * z.images[0]
        half = 128 * abs(last - back)
        lines.append(bands[hop][at : at + z.images[k], half : half + 128])
    lines.append(jnp.zeros((z.slots - sum(z.images), 128), F32))
    return jnp.concatenate(lines, axis=0)


def local(
    image_small, image_large, teacher_small, teacher_large, upstream_small, upstream_large,
    conv_first, gain_first, bias_first, conv_second, gain_second, bias_second,
):
    peers = lax.axis_size("row")
    devices = lax.axis_size("img") * peers
    z = Sizes(image_small.shape, image_large.shape, devices, peers)
    body = lambda function: functools.partial(function, z)
    r = z.rims
    full, half, pair = (z.total, LANES), (2, z.total, 128), (2 * devices, 128)
    weight, left = (2, TAPS * TAP_ROWS, 128), (2, 256, 2 * z.total)
    images = [image_small, image_large, upstream_small, upstream_large, teacher_small, teacher_large]
    f = lambda space, *shape: (space, shape, F32)
    depths = (REACH, 2)
    rim_rows = sum(depths) * r + z.slots

    x, bottom, top, copies = call(
        body(start_kernel),
        "hhhhhh",
        [("v", full, F32), f("v", rim_rows, LANES), f("v", rim_rows, LANES), ("V", pair, F32)],
        [[(a.shape, F32) for a in images], (half, F32)],
        6,
    )(*images)
    gathered = exchange(copies, AXES)
    above, below = beyond(z, bottom, top, depths)
    params = [conv_first, conv_second] + images[2:]
    w1, w2, weights, affine, upstream, teacher, x_copy = call(
        body(prepare_kernel),
        "hhhhhhhhhhv",
        [("v", weight, BF16), ("v", weight, BF16), ("h", (4,) + weight, BF16), f("v", 4, LANES), ("h", full, F32), f("v", z.total, 128), ("h", full, F32)],
        [[(a.shape, F32) for a in params], ((4,) + weight, BF16), (full, F32), ((4, C), F32), (half, F32)],
        16,
    )(*params, *(v.reshape(1, C) for v in (gain_first, bias_first, gain_second, bias_second)), x)

    hidden, stats_one, copies = call(
        body(first_kernel),
        "vvvvvv",
        [("v", full, F32), f("v", 2, LANES), ("V", pair, F32)],
        [z.pads()],
    )(x, above, below, gathered, affine, w1)
    gathered = exchange(copies, AXES)
    extended, near_rows = z.total + 4 * r, z.total + 2 * r
    h_above, h_below, left_one, packed, teachers, spread_u, near_u, near_x = call(
        body(first_operand_kernel),
        "vvvvvvvhh",
        [
            f("v", 3 * r, LANES), f("v", 3 * r, LANES), ("h", left, BF16), f("h", C, BACK_LANES), f("h", extended, LANES),
            f("h", near_rows, LANES), f("h", near_rows, LANES), f("h", 2, 2 * r, LANES),
        ],
        [
            z.pads(), z.chains(2), z.chains(REACH), (left, BF16), ((2,) + weight, BF16), ((near_rows, LANES), F32),
            ((extended, 128), F32), ((extended, LANES), F32), ((near_rows, LANES), F32), ((C, BACK_LANES), F32),
        ],
        10,
    )(x, hidden, above, below, stats_one, affine, teacher, upstream, weights)

    map_shape = (peers * z.slots, 128)
    out, stats_two, copies = call(
        body(second_kernel),
        "vvvvvvvv",
        [("v", full, F32), f("v", 2, LANES), ("V", map_shape, F32)],
        [z.pads()],
    )(hidden, h_above, h_below, gathered, affine, w2, x, teacher)
    gathered = exchange(copies, ("row",))
    out_copy, hidden_copy, left_two, shifts, by_map, by_teacher, up = call(
        body(second_operand_kernel),
        "vvvvvvhhhhh",
        [
            ("h", full, F32), f("h", near_rows, LANES), ("v", left, BF16), f("h", 3, near_rows, LANES),
            f("v", near_rows, LANES), f("v", near_rows, LANES), f("v", near_rows, LANES),
        ],
        [
            z.pads(), z.chains(2), z.chains(3), ((2, 2 * r, LANES), F32), ((extended, LANES), F32), ((near_rows, LANES), F32),
            ((2,) + weight, BF16), ((3, near_rows, LANES), F32),
        ],
        11,
    )(hidden, h_above, h_below, stats_two, affine, out, near_x, teachers, spread_u, near_u, weights)

    dout, dshift, d_above, d_below, slabs = call(
        body(upstream_kernel),
        "vvhhvhvvhv",
        [("v", full, F32), ("v", full, F32), f("v", r, LANES), f("v", r, LANES), f("V", devices, 1, BACK_LANES)],
        [((3, near_rows, LANES), F32), (left, BF16), (full, F32), ((C, BACK_LANES), F32), z.pads(), z.pads()],
        4,
    )(gathered, up, shifts, left_one, left_two, packed, by_map, by_teacher, hidden_copy, stats_two)
    gathered = exchange(slabs, AXES)
    out_s, out_l, first_normed, second_normed, weight_back = call(
        body(write_kernel),
        "hhhhvvv",
        [("v", image_small.shape, F32), ("v", image_large.shape, F32), ("v", full, F32), f("v", near_rows, LANES), ("v", weight, BF16)],
        [(full, F32), (full, F32), ((near_rows, LANES), F32), (half, F32)],
        4,
    )(out_copy, x_copy, hidden_copy, weights, stats_one, stats_two, d_above)

    pre, gain_two, bias_two, slabs = call(
        body(hidden_kernel),
        "vvvvvvvvv",
        [("v", full, F32), f("v", 1, C), f("v", 1, C), f("V", devices, 1, LAST_LANES)],
        [z.pads()],
    )(gathered, dshift, d_above, d_below, second_normed, stats_two, affine, weight_back, first_normed)
    gathered = exchange(slabs, AXES)

    back_s, back_l, one, two, gain_one, bias_one = call(
        body(back_kernel),
        "vvvvvv",
        [("v", a.shape, F32) for a in (image_small, image_large, conv_first, conv_second)] + [f("v", 1, C), f("v", 1, C)],
        [(half, F32), ((C, LAST_LANES), F32)],
    )(gathered, pre, first_normed, stats_one, affine, dout)
    return (
        out_s, out_l, back_s, back_l,
        one, gain_one.reshape(C), bias_one.reshape(C),
        two, gain_two.reshape(C), bias_two.reshape(C),
    )


def solution(mesh):
    split_bands, everywhere = P("img", "row", None), P()
    return jax.shard_map(
        local,
        mesh=mesh,
        in_specs=(split_bands,) * 6 + (everywhere,) * 6,
        out_specs=(split_bands,) * 4 + (everywhere,) * 6,
        check_vma=False,
    )
```

```python
import functools
import math

import jax
import jax.numpy as jnp
from jax import lax
from jax.experimental import pallas as pl
from jax.experimental.pallas import tpu as pltpu
from jax.sharding import PartitionSpec as P

C = 32
HS = 32
HL = 64
HEIGHTS = (HS, HL)

norm_eps = 1e-05
map_eps = 1e-06
beta_weight = 1000.0
AXES = ("img", "row")
BLOCK = 8
LANES = BLOCK * C
TAPS = 3
WIDTH = LANES + 128
DEPTH = TAPS * WIDTH
TAP_ROWS = 128 + 2 * C
REACH = 4
ROOT = math.sqrt(2.0 / math.pi)
CUBE = 0.044715
F32 = jnp.float32
BF16 = jnp.bfloat16
VMEM_LIMIT = 32 * 1024 * 1024
BIAS, GAIN, SECOND, LEFT, HIDDEN, ONES = 0, 1, 2, 11, 20, 29
BACK_LANES = 1280
LAST_SECOND, LAST_FIRST, LAST_LANES = 2, 11, 640


class Sizes:
    def __init__(self, small, large, devices, peers):
        self.images = (small[0], large[0])
        self.rows = (small[1], large[1])
        self.blocks = (HS // BLOCK, HL // BLOCK)
        self.step = tuple(n * r for n, r in zip(self.images, self.rows))
        self.count = tuple(b * s for b, s in zip(self.blocks, self.step))
        self.edge = tuple(b * n for b, n in zip(self.blocks, self.images))
        self.start = (self.count[1], 0)
        self.rim = (self.edge[1], 0)
        self.total = sum(self.count)
        self.rims = sum(self.edge)
        self.slots = -(-sum(self.images) // 8) * 8
        self.guard = -(-max(self.images) // 8) * 8
        self.devices = devices
        self.peers = peers
        self.here = float(self.total * BLOCK)
        self.pixels = self.here * devices

    def pads(self):
        return [((TAPS, 2, self.count[k] + 2 * self.step[k], 128), F32) for k in (0, 1)]

    def chains(self, depth):
        return [((2, 2 * self.guard + (depth + 1) * self.rims, 128), F32)] * 2


def split(value):
    high = value.astype(BF16)
    return high, (value - high.astype(F32)).astype(BF16)


def dot(left, right):
    return lax.dot_general(left, right, (((1,), (0,)), ((), ())), preferred_element_type=F32)


def product(left, right):
    if left[0].shape[1] % 128:
        return dot(left[0], right[0]) + (dot(left[0], right[1]) + dot(left[1], right[0]))
    return dot(
        jnp.concatenate([left[0], left[0], left[1]], axis=1), jnp.concatenate([right[0], right[1], right[0]], axis=0)
    )


def spread(left, right):
    right = right.astype(BF16)
    return dot(jnp.concatenate(split(left), axis=1), jnp.concatenate([right, right], axis=0))


def gelu(s):
    return 0.5 * s * (1.0 + jnp.tanh(ROOT * (s + CUBE * s * s * s)))


def gelu_slope(s):
    square = s * s
    t = jnp.tanh(ROOT * s * (1.0 + CUBE * square))
    return 0.5 * (1.0 + t) + 0.5 * s * (1.0 - t * t) * ROOT * (1.0 + 3.0 * CUBE * square)


def spread_groups(row):
    row = row + pltpu.roll(row, 64, 1)
    return row + pltpu.roll(row, 32, 1)


def fold(row):
    return spread_groups(row[:, :128] + row[:, 128:])


def wide(row):
    return jnp.concatenate([row, row], axis=1)


def group_of(rows=1, lanes=128):
    return lax.broadcasted_iota(jnp.int32, (rows, lanes), 1) // C


def column_sum(value):
    return jnp.sum(value, axis=0, keepdims=True)


def send_lines(z, ref, lines):
    for n, line in enumerate(lines):
        ref[pl.ds(n, z.devices, stride=len(lines)), :] = jnp.broadcast_to(line, (z.devices, 128))


def moments(z, value, ref):
    few = min(8, z.total)
    pivot = fold(column_sum(value[:few])) / float(few * BLOCK)
    off = value - wide(pivot)
    first, second = fold(column_sum(off)), fold(column_sum(off * off))
    send_lines(z, ref, [pivot + first / z.here, second - first * first / z.here])


def merged(z, ref):
    means = ref[pl.ds(0, z.devices, stride=2), :]
    center = jnp.mean(means, axis=0, keepdims=True)
    off = means - center
    within = jnp.mean(ref[pl.ds(1, z.devices, stride=2), :], axis=0, keepdims=True)
    variance = within / z.here + jnp.mean(off * off, axis=0, keepdims=True)
    return wide(center), wide(lax.rsqrt(variance + norm_eps))


def put_halves(ref, value):
    ref[0] = value[:, :128]
    ref[1] = value[:, 128:]


def whole(ref):
    return jnp.concatenate([ref[0], ref[1]], axis=1)


def to_matrix(z, refs, half):
    for k in (0, 1):
        for j in range(z.blocks[k]):
            at = z.start[k] + j * z.step[k]
            for i in range(z.images[k]):
                for h in (0, 1):
                    half[h, pl.ds(at + i * z.rows[k], z.rows[k]), :] = refs[k][i, :, pl.ds(LANES * j + 128 * h, 128)]


def from_matrix(z, half, refs):
    for k in (0, 1):
        for j in range(z.blocks[k]):
            at = z.start[k] + j * z.step[k]
            for i in range(z.images[k]):
                for h in (0, 1):
                    refs[k][i, :, pl.ds(LANES * j + 128 * h, 128)] = half[h, pl.ds(at + i * z.rows[k], z.rows[k]), :]


def take_rims(z, half, depth, bottom, top):
    for k in (0, 1):
        for d in range(1, depth + 1):
            to_bottom = pl.ds((depth - d) * z.rims + z.rim[k], z.edge[k])
            to_top = pl.ds((d - 1) * z.rims + z.rim[k], z.edge[k])
            if d <= z.rows[k]:
                bottom[to_bottom, :] = half[pl.ds(z.start[k] + z.rows[k] - d, z.edge[k], stride=z.rows[k]), :]
                top[to_top, :] = half[pl.ds(z.start[k] + d - 1, z.edge[k], stride=z.rows[k]), :]
            else:
                bottom[to_bottom, :] = jnp.zeros((z.edge[k], 128), F32)
                top[to_top, :] = jnp.zeros((z.edge[k], 128), F32)


def inside(z, depth, above):
    at = lax.axis_index("row")
    large = lax.broadcasted_iota(jnp.int32, (z.rims, 1), 0) < z.rim[0]
    parts = []
    for n in range(depth):
        if above:
            ok = [jnp.where(at * rows >= depth - n, 1.0, 0.0) for rows in z.rows]
        else:
            ok = [jnp.where((at + 1) * rows + n + 1 <= height, 1.0, 0.0) for rows, height in zip(z.rows, HEIGHTS)]
        parts.append(jnp.where(large, ok[1], ok[0]).astype(F32))
    return jnp.concatenate(parts, axis=0)


def clear_guards(z, pads, a):
    for k in (0, 1):
        pads[k][a, 1, pl.ds(0, z.step[k]), :] = jnp.zeros((z.step[k], 128), F32)
        pads[k][a, 0, pl.ds(z.step[k] + z.count[k], z.step[k]), :] = jnp.zeros((z.step[k], 128), F32)


def fill_center(z, pads, value):
    clear_guards(z, pads, 1)
    for k in (0, 1):
        for h in (0, 1):
            pads[k][1, h, pl.ds(z.step[k], z.count[k]), :] = value[z.start[k] : z.start[k] + z.count[k], 128 * h : 128 * h + 128]


def fill_shifted(z, pads, above, below):
    for k in (0, 1):
        ref, step, count, rows = pads[k], z.step[k], z.count[k], z.rows[k]
        rim = slice(z.rim[k], z.rim[k] + z.edge[k])
        for h in (0, 1):
            lanes = slice(128 * h, 128 * h + 128)
            ref[0, h, pl.ds(step, count), :] = ref[1, h, pl.ds(step - 1, count), :]
            ref[2, h, pl.ds(step, count), :] = ref[1, h, pl.ds(step + 1, count), :]
            ref[0, h, pl.ds(step, z.edge[k], stride=rows), :] = above[rim, lanes]
            ref[2, h, pl.ds(step + rows - 1, z.edge[k], stride=rows), :] = below[rim, lanes]


def fill_pads(z, pads, value, above, below):
    fill_center(z, pads, value)
    fill_shifted(z, pads, above, below)
    for a in (0, 2):
        clear_guards(z, pads, a)


def band_operand(z, pads, taps=range(TAPS)):
    lane = lax.broadcasted_iota(jnp.int32, (1, 128), 1)
    parts = []
    for k in (1, 0):
        ref, step, count = pads[k], z.step[k], z.count[k]
        columns = []
        for a in taps:
            before = ref[a, 1, pl.ds(0, count), :]
            after = ref[a, 0, pl.ds(2 * step, count), :]
            columns += [
                ref[a, 0, pl.ds(step, count), :],
                ref[a, 1, pl.ds(step, count), :],
                jnp.where(lane >= 96, before, jnp.where(lane < 32, after, 0.0)),
            ]
        parts.append(jnp.concatenate(columns, axis=1))
    return jnp.concatenate(parts, axis=0)


def rim_operand(z, chain, depth):
    rows, g = (depth + 1) * z.rims, z.guard
    lane = lax.broadcasted_iota(jnp.int32, (1, 128), 1)
    m = lax.broadcasted_iota(jnp.int32, (z.rims, 1), 0)
    large = m < z.rim[0]
    has_before = jnp.where(large, m, m - z.rim[0]) >= jnp.where(large, z.images[1], z.images[0])
    has_after = m < jnp.where(large, z.rim[0] - z.images[1], z.rims - z.images[0])
    take = [(lane >= 96) & has_before & large, (lane >= 96) & has_before & ~large, (lane < 32) & has_after & large, (lane < 32) & has_after & ~large]
    columns = []
    for r in range(depth + 1):
        at = g + r * z.rims
        edge = jnp.zeros((z.rims, 128), F32)
        for mask, half, shift in zip(take, (1, 1, 0, 0), (-z.images[1], -z.images[0], z.images[1], z.images[0])):
            edge = jnp.where(mask, chain[half, pl.ds(at + shift, z.rims), :], edge)
        columns.append(jnp.concatenate([chain[0, pl.ds(at, z.rims), :], chain[1, pl.ds(at, z.rims), :], edge], axis=1))
    return jnp.concatenate(
        [jnp.concatenate(columns[n : n + TAPS], axis=1) for n in range(depth - 1)], axis=0
    )


def rim_operands(z, pads, above, below, depth, chains):
    parts = []
    for side, (rim, chain) in enumerate(zip((above, below), chains)):
        rim_at, own_at = (z.guard, z.guard + depth * z.rims) if side == 0 else (z.guard + z.rims, z.guard)
        for h in (0, 1):
            chain[h, pl.ds(rim_at, depth * z.rims), :] = rim[:, 128 * h : 128 * h + 128]
            for k in (0, 1):
                row = z.step[k] + (0 if side == 0 else z.rows[k] - 1)
                chain[h, pl.ds(own_at + z.rim[k], z.edge[k]), :] = pads[k][1, h, pl.ds(row, z.edge[k], stride=z.rows[k]), :]
        parts.append(rim_operand(z, chain, depth))
    return parts


def times(parts, weight):
    return product(split(jnp.concatenate(parts, axis=0)), (weight_matrix(weight.at[0]), weight_matrix(weight.at[1])))


def convolve(z, own, above, below, depth, pads, chains, weight):
    (result,) = convolve_each(z, [(own, above, below)], depth, pads, chains, weight)
    return result


def convolve_each(z, fields, depth, pads, chains, weight):
    r = z.rims
    parts = []
    for own, above, below in fields:
        fill_pads(z, pads, own, above[(depth - 1) * r :], below[:r])
        parts.append(band_operand(z, pads))
        if depth > 1:
            parts += rim_operands(z, pads, above, below, depth, chains)
    result = times(parts, weight)
    n = (depth - 1) * r
    split_at = [(at, at + z.total, at + z.total + n, at + z.total + 2 * n) for at in range(0, result.shape[0], z.total + 2 * n)]
    return [(result[a:b], result[b:c], result[c:d]) for a, b, c, d in split_at]


def convolve_rims(z, pads, above, below, depth, chains, weight):
    result = times(rim_operands(z, pads, above, below, depth, chains), weight)
    n = (depth - 1) * z.rims
    return result[:n], result[n:]


def image_sums(z, value):
    slot = lax.broadcasted_iota(jnp.int32, (z.slots, 1), 0)
    sums = jnp.zeros((z.slots, 128), F32)
    for k in (0, 1):
        line = value[z.start[k] : z.start[k] + z.step[k]]
        for j in range(1, z.blocks[k]):
            at = z.start[k] + j * z.step[k]
            line = line + value[at : at + z.step[k]]
        image = lax.broadcasted_iota(jnp.int32, (z.step[k], 1), 0) // z.rows[k]
        for i in range(z.images[k]):
            sums = jnp.where(slot == i + k * z.images[0], column_sum(jnp.where(image == i, line, 0.0)), sums)
    return sums


def image_rows(z, values, rims):
    parts = []
    for k in (1, 0):
        image = lax.broadcasted_iota(jnp.int32, (z.step[k], 1), 0) // z.rows[k]
        line = jnp.zeros((z.step[k], 128), F32)
        for i in range(z.images[k]):
            at = i + k * z.images[0]
            line = jnp.where(image == i, values[at : at + 1], line)
        parts += [line] * z.blocks[k]
    if rims:
        m = lax.broadcasted_iota(jnp.int32, (z.rims, 1), 0)
        image = jnp.where(m < z.rim[0], z.images[0] + m % z.images[1], (m - z.rim[0]) % z.images[0])
        line = jnp.zeros((z.rims, 128), F32)
        for at in range(sum(z.images)):
            line = jnp.where(image == at, values[at : at + 1], line)
        parts += [line] * rims
    return jnp.concatenate(parts, axis=0)


def channel_mean():
    a = lax.broadcasted_iota(jnp.int32, (LANES, 128), 0) // C
    b = lax.broadcasted_iota(jnp.int32, (LANES, 128), 1) % 64
    return jnp.where(a == b, 1.0 / C, 0.0).astype(F32)


def to_channels():
    a = lax.broadcasted_iota(jnp.int32, (128, LANES), 0)
    b = lax.broadcasted_iota(jnp.int32, (128, LANES), 1) // C
    return jnp.where(a == b, 1.0, 0.0).astype(F32)


def attention(value):
    return spread(value * value, channel_mean())


def start_all(copies):
    for copy in copies:
        copy.start()


def wait_all(copies):
    for copy in copies:
        copy.wait()


def start_kernel(z, small, large, up_s, up_l, t_s, t_l, x, bottom, top, copies, raw, half, sems):
    loads = [pltpu.make_async_copy(a, b, sems.at[n]) for n, (a, b) in enumerate(zip((small, large, up_s, up_l, t_s, t_l), raw))]
    start_all(loads)
    r, n = z.rims, REACH * z.rims
    tail = n + 2 * r
    for ref in (bottom, top):
        ref[pl.ds(tail, z.slots), :] = jnp.zeros((z.slots, LANES), F32)
    wait_all(loads[:2])
    to_matrix(z, raw[:2], half)
    value = whole(half)
    x[...] = value
    moments(z, value, copies)
    for h in (0, 1):
        lanes = pl.ds(128 * h, 128)
        take_rims(z, half.at[h], REACH, bottom.at[pl.ds(0, n), lanes], top.at[pl.ds(0, n), lanes])
    wait_all(loads[2:])
    for k in (0, 1):
        width, rows = HEIGHTS[k], z.rows[k]
        for i in range(z.images[k]):
            slot = pl.ds(tail + i + k * z.images[0], 1)
            for d in (0, 1):
                to_bottom, to_top = n + (1 - d) * r + z.rim[k] + i, n + d * r + z.rim[k] + i
                for j in range(z.blocks[k]):
                    lanes, at = pl.ds(LANES * j, LANES), j * z.images[k]
                    if d < rows:
                        bottom[pl.ds(to_bottom + at, 1), :] = raw[2 + k][i, pl.ds(rows - 1 - d, 1), lanes]
                        top[pl.ds(to_top + at, 1), :] = raw[2 + k][i, pl.ds(d, 1), lanes]
                    else:
                        bottom[pl.ds(to_bottom + at, 1), :] = jnp.zeros((1, LANES), F32)
                        top[pl.ds(to_top + at, 1), :] = jnp.zeros((1, LANES), F32)
                if d < rows:
                    bottom[slot, pl.ds(128 * (1 - d), width)] = raw[4 + k][i, pl.ds(rows - 1 - d, 1), :]
                    top[slot, pl.ds(128 * d, width)] = raw[4 + k][i, pl.ds(d, 1), :]


def banded(taps, ref):
    row = lax.broadcasted_iota(jnp.int32, (128, 128), 0) // C
    lane = group_of(128)
    for a in range(TAPS):
        main = jnp.zeros((128, 128), F32)
        for b in range(TAPS):
            main = jnp.where(row - lane + 1 == b, taps[a][b], main)
        before = jnp.where(lane[:C] == 0, taps[a][0][:C], 0.0)
        after = jnp.where(lane[:C] == 3, taps[a][2][:C], 0.0)
        for n, part in enumerate(split(jnp.concatenate([main, before, after], axis=0))):
            ref[n, pl.ds(a * TAP_ROWS, TAP_ROWS), :] = part


def weight_matrix(ref):
    rows = []
    zeros = jnp.zeros((128 - C, 128), BF16)
    for a in range(TAPS):
        at = a * TAP_ROWS
        main = ref[pl.ds(at, 128), :]
        before = jnp.concatenate([zeros, ref[pl.ds(at + 128, C), :]], axis=0)
        after = jnp.concatenate([ref[pl.ds(at + 128 + C, C), :], zeros], axis=0)
        rows += [
            jnp.concatenate([main, before], axis=1),
            jnp.concatenate([after, main], axis=1),
            jnp.concatenate([before, after], axis=1),
        ]
    return jnp.concatenate(rows, axis=0)


def prepare_kernel(z, first, second, up_s, up_l, t_s, t_l, g1, b1, g2, b2, x, w1, w2, weights, affine, upstream, teacher, x_copy, raw, kept, kept_u, rows, half, sems):
    targets = tuple(raw) + tuple(rows.at[pl.ds(n, 1), :] for n in range(4))
    refs = (first, second, up_s, up_l, t_s, t_l, g1, b1, g2, b2)
    loads = [pltpu.make_async_copy(a, b, sems.at[n]) for n, (a, b) in enumerate(zip(refs, targets))]
    start_all(loads)
    stores = [pltpu.make_async_copy(x, x_copy, sems.at[15])]
    stores[0].start()
    wait_all(loads)
    to_matrix(z, raw[2:4], half)
    kept_u[...] = whole(half)
    stores.append(pltpu.make_async_copy(kept_u, upstream, sems.at[10]))
    stores[1].start()
    for n, (source, forward) in enumerate(zip(raw[:2], (w1, w2))):
        tiles = []
        for a in range(TAPS):
            line = [jnp.concatenate([source[a, b]] * 4, axis=1) for b in range(TAPS)]
            tiles.append([jnp.concatenate([tap] * 4, axis=0) for tap in line])
        turned = [[tiles[TAPS - 1 - a][TAPS - 1 - b].T for b in range(TAPS)] for a in range(TAPS)]
        for at, taps in ((n, tiles), (3 - n, turned)):
            banded(taps, kept.at[at])
            stores.append(pltpu.make_async_copy(kept.at[at], weights.at[at], sems.at[11 + at]))
            stores[-1].start()
        forward[...] = kept[n]
    affine[...] = jnp.concatenate([rows[...]] * BLOCK, axis=1)
    teacher[...] = jnp.zeros(teacher.shape, F32)
    for k, ref in ((0, raw[4]), (1, raw[5])):
        for i in range(z.images[k]):
            line = ref[i]
            for j in range(z.blocks[k]):
                at = z.start[k] + j * z.step[k] + i * z.rows[k]
                for lane in (0, 64):
                    teacher[pl.ds(at, z.rows[k]), pl.ds(lane, BLOCK)] = line[:, j * BLOCK : (j + 1) * BLOCK]
    wait_all(stores)


def normed_by(stats):
    return lambda v: (v - stats[0:1]) * stats[1:2]


def activation(center, scale, gain, bias):
    factor = scale * gain
    offset = bias - center * factor
    return lambda v: gelu(v * factor + offset)


def first_kernel(z, x, above, below, gathered, affine, weight, hidden, stats, copies, pads):
    center, scale = merged(z, gathered)
    act = activation(center, scale, affine[0:1], affine[1:2])
    r = z.rims
    up, down = act(above[pl.ds(3 * r, r), :]) * inside(z, 1, True), act(below[pl.ds(0, r), :]) * inside(z, 1, False)
    own, _, _ = convolve(z, act(x[...]), up, down, 1, pads, None, weight)
    moments(z, own, copies)
    hidden[...] = own
    stats[0:1] = center
    stats[1:2] = scale


def second_kernel(z, hidden, h_above, h_below, gathered, affine, weight, x, x_above, x_below, teacher, out, o_above, o_below, near, stats, copies, pads, chains):
    center, scale = merged(z, gathered)
    act = activation(center, scale, affine[2:3], affine[3:4])
    r = z.rims
    own = act(hidden[...])
    up, down = act(h_above[...]) * inside(z, 3, True), act(h_below[...]) * inside(z, 3, False)
    own, up, down = convolve(z, own, up, down, 3, pads, chains, weight)
    own = x[...] + own
    amap = attention(own)
    lane = lax.broadcasted_iota(jnp.int32, (1, 128), 1)
    sums = image_sums(z, amap * jnp.where(lane < 64, amap, teacher[...]))
    copies[...] = jnp.concatenate([sums] * z.peers, axis=0)
    out[...] = own
    o_above[...] = x_above[pl.ds(2 * r, 2 * r), :] + up
    o_below[...] = x_below[pl.ds(0, 2 * r), :] + down
    near[0] = h_above[pl.ds(2 * r, r), :]
    near[1] = h_below[pl.ds(0, r), :]
    stats[0:1] = center
    stats[1:2] = scale


def tap_rows(q):
    return 128 + 3 * C if q < 0 else 128 if q == 4 else q * C


def tap_product(z, operand, own, above, below, pads):
    fill_center(z, pads, own)
    fill_shifted(z, pads, above, below)
    columns = []
    for a in range(TAPS):
        columns.append(
            jnp.concatenate([pads[k][TAPS - 1 - a, h, pl.ds(z.step[k], z.count[k]), :] for h in (0, 1) for k in (1, 0)], axis=0)
        )
    return product(operand, split(jnp.concatenate(columns, axis=1)))


def tap_sums(result, tiles, first_group):
    group = group_of()
    for a in range(TAPS):
        for b in range(TAPS):
            total = None
            for p in range(4):
                at = tap_rows(p + b - 1)
                part = result[at : at + C, 128 * a : 128 * a + 128]
                total = part if total is None else jnp.where(group == p, part, total)
            tile, slot = divmod(first_group + a * TAPS + b, 4)
            tiles[tile] = jnp.where(group == slot, spread_groups(total), tiles[tile])


def tap_counts(z, turned, tiles, first_group):
    group = group_of()
    m = lax.broadcasted_iota(jnp.int32, (1, 2 * z.total), 1) % z.total
    row = jnp.where(m < z.start[0], m % z.rows[1], (m - z.start[0]) % z.rows[0])
    height = jnp.where(m < z.start[0], z.rows[1], z.rows[0])
    at = lax.axis_index("row")
    lost = {
        0: (row == height - 1) & (at == z.peers - 1),
        2: (row == 0) & (at == 0),
    }
    for a in range(TAPS):
        column = jnp.sum(jnp.where(lost[a], 0.0, turned) if a in lost else turned, axis=1, keepdims=True)
        for b in range(TAPS):
            total = sum(column[tap_rows(p + b - 1) : tap_rows(p + b - 1) + C] for p in range(4))
            tile, slot = divmod(first_group + a * TAPS + b, 4)
            tiles[tile] = jnp.where(group == slot, total, tiles[tile])


def turned_operand(z, value, pads, kept):
    fill_center(z, pads, value)
    lane = lax.broadcasted_iota(jnp.int32, (1, 128), 1)
    halves = ([], [])
    for k in (1, 0):
        ref, step, count = pads[k], z.step[k], z.count[k]
        low, high = ref[1, 0, pl.ds(step, count), :], ref[1, 1, pl.ds(step, count), :]
        before, after = ref[1, 1, pl.ds(0, count), :], ref[1, 0, pl.ds(2 * step, count), :]
        for part, main, left, right in ((halves[0], low, before, high), (halves[1], high, low, after)):
            part.append(jnp.concatenate([main, jnp.where(lane >= 96, left, jnp.where(lane < 32, right, 0.0))], axis=1))
    turned = jnp.concatenate(halves[0] + halves[1], axis=0).T
    parts = split(turned)
    for n in (0, 1):
        kept[n] = parts[n]
    return turned


def first_operand_kernel(z, x, hidden, above, below, stats, affine, teacher, upstream, weights, h_above, h_below, left, packed, teachers, wide_u, pads, deep_chains, kept, kept_w, kept_u, pixels, kept_t, kept_packed, sems):
    r, own = z.rims, pl.ds(0, z.total)
    loads = [
        pltpu.make_async_copy(weights.at[0], kept_w, sems.at[0]),
        pltpu.make_async_copy(upstream, kept_u.at[own, :], sems.at[1]),
    ]
    start_all(loads)
    stores = []
    act = activation(stats[0:1], stats[1:2], affine[0:1], affine[1:2])
    value = turned_operand(z, act(x[...]), pads, kept)
    stores.append(pltpu.make_async_copy(kept, left, sems.at[2]))
    stores[-1].start()
    n = REACH * r
    up, down = act(above[pl.ds(0, n), :]) * inside(z, REACH, True), act(below[pl.ds(0, n), :]) * inside(z, REACH, False)
    loads[0].wait()
    up, down = convolve_rims(z, pads, up, down, REACH, deep_chains, kept_w)
    h_above[...] = up
    h_below[...] = down
    tiles = [jnp.zeros((C, 128), F32) for _ in range(BACK_LANES // 128)]
    tap_counts(z, value, tiles, ONES)
    result = tap_product(
        z, (kept[0], kept[1]), hidden[...], up[2 * r :] * inside(z, 1, True), down[:r] * inside(z, 1, False), pads
    )
    tap_sums(result, tiles, HIDDEN)
    kept_packed[...] = jnp.concatenate(tiles, axis=1)
    stores.append(pltpu.make_async_copy(kept_packed, packed, sems.at[6]))
    stores[-1].start()
    pixels[own, :] = teacher[...]
    pixels[pl.ds(z.total, 4 * r), :] = jnp.zeros((4 * r, 128), F32)
    n = (REACH + 2) * r
    for side, ref in enumerate((above, below)):
        for d in (0, 1):
            for k in (0, 1):
                line = ref[pl.ds(n + k * z.images[0], z.images[k]), pl.ds(128 * d, 128)]
                for j in range(z.blocks[k]):
                    at = z.total + (2 * side + d) * r + z.rim[k] + j * z.images[k]
                    pixels[pl.ds(at, z.images[k]), pl.ds(0, BLOCK)] = line[:, j * BLOCK : (j + 1) * BLOCK]
    kept_t[...] = spread(pixels[...], to_channels())
    stores.append(pltpu.make_async_copy(kept_t, teachers, sems.at[3]))
    stores[-1].start()
    n = REACH * r
    kept_u[pl.ds(z.total, 2 * r), :] = above[pl.ds(n, 2 * r), :] * inside(z, 2, True)
    kept_u[pl.ds(z.total + 2 * r, 2 * r), :] = below[pl.ds(n, 2 * r), :] * inside(z, 2, False)
    loads[1].wait()
    stores.append(pltpu.make_async_copy(kept_u, wide_u, sems.at[5]))
    stores[-1].start()
    wait_all(stores)


def second_operand_kernel(z, hidden, near, stats, affine, out, o_above, o_below, teachers, wide_u, weights, out_copy, hidden_copy, left, shifts, by_map, by_teacher, up, pads, chains, kept_t, kept_u, kept_w, kept_s, sems):
    r, total = z.rims, z.total
    loads = [
        pltpu.make_async_copy(teachers, kept_t, sems.at[0]),
        pltpu.make_async_copy(weights.at[2], kept_w, sems.at[1]),
        pltpu.make_async_copy(wide_u, kept_u, sems.at[2]),
    ]
    start_all(loads)
    stores = [
        pltpu.make_async_copy(out, out_copy, sems.at[4]),
        pltpu.make_async_copy(hidden, hidden_copy.at[pl.ds(0, total), :], sems.at[5]),
        pltpu.make_async_copy(near.at[0], hidden_copy.at[pl.ds(total, r), :], sems.at[6]),
        pltpu.make_async_copy(near.at[1], hidden_copy.at[pl.ds(total + r, r), :], sems.at[7]),
    ]
    start_all(stores)
    normed = normed_by(stats)(jnp.concatenate([hidden[...], near[0], near[1]], axis=0))
    shifted = normed * affine[2:3] + affine[3:4]
    turned_operand(z, gelu(shifted[:total]), pads, left)
    ones = jnp.ones((total, 1), F32)
    slopes = gelu_slope(shifted) * jnp.concatenate([ones, inside(z, 1, True), inside(z, 1, False)], axis=0)
    o = jnp.concatenate([out[...], o_above[...] * inside(z, 2, True), o_below[...] * inside(z, 2, False)], axis=0)
    for_map = spread(attention(o), to_channels()) * o
    wait_all(loads)
    fields = []
    for value, ref in ((kept_u[...], up), (for_map, by_map), (kept_t[...] * o, by_teacher)):
        own, before, after = value[:total], value[total : total + 2 * r], value[total + 2 * r :]
        ref[...] = jnp.concatenate([own, before[r:], after[:r]], axis=0)
        fields.append((own, before, after))
    for n, parts in enumerate(convolve_each(z, fields, 2, pads, chains, kept_w)):
        kept_s[n] = jnp.concatenate(parts, axis=0) * slopes
        stores.append(pltpu.make_async_copy(kept_s.at[n], shifts.at[n], sems.at[8 + n]))
        stores[-1].start()
    wait_all(stores)


def upstream_kernel(z, gathered, up, shifts, left_1, left_2, packed, by_map, by_teacher, hidden, stats, dout, dshift, d_above, d_below, slabs, kept_s, kept_left, kept_h, kept_packed, pads, more_pads, sems):
    r, total = z.rims, z.total
    loads = [
        pltpu.make_async_copy(a, b, sems.at[n])
        for n, (a, b) in enumerate(((shifts, kept_s), (left_1, kept_left), (hidden.at[pl.ds(0, total), :], kept_h), (packed, kept_packed)))
    ]
    start_all(loads)
    lane = lax.broadcasted_iota(jnp.int32, (z.slots, 128), 1)
    sums = sum(gathered[pl.ds(n * z.slots, z.slots), :] for n in range(z.peers))
    square = jnp.sum(jnp.where(lane < 64, sums, 0.0), axis=1, keepdims=True)
    cross = jnp.sum(jnp.where(lane < 64, 0.0, sums), axis=1, keepdims=True)
    inverse = lax.rsqrt(square + map_eps)
    inner = beta_weight * (square * inverse - cross) * inverse
    shape = (z.slots, 128)
    for_map = (beta_weight - inner) * inverse * inverse * (2.0 / C)
    for_teacher = beta_weight * inverse * (2.0 / C)
    for_map, for_teacher = (wide(image_rows(z, jnp.broadcast_to(v, shape), 2)) for v in (for_map, for_teacher))
    value = up[...] + for_map * by_map[...] - for_teacher * by_teacher[...]
    dout[...] = value[:total]
    wait_all(loads[:2])
    shift = kept_s[0] + for_map * kept_s[1] - for_teacher * kept_s[2]
    pre, above, below = shift[:total], shift[total : total + r], shift[total + r :]
    dshift[...] = pre
    d_above[...] = above
    d_below[...] = below
    second = tap_product(z, (left_2[0], left_2[1]), value[:total], value[total : total + r], value[total + r :], pads)
    first = tap_product(z, (kept_left[0], kept_left[1]), pre, above, below, more_pads)
    wait_all(loads[2:])
    normed = normed_by(stats)(kept_h[...])
    tiles = [kept_packed[:, 128 * n : 128 * n + 128] for n in range(BACK_LANES // 128)]
    group = group_of()
    tiles[0] = jnp.where(group == BIAS, fold(column_sum(pre)), jnp.where(group == GAIN, fold(column_sum(pre * normed)), tiles[0]))
    tap_sums(second, tiles, SECOND)
    tap_sums(first, tiles, LEFT)
    line = jnp.concatenate(tiles, axis=1)
    for d in range(z.devices):
        slabs[d] = line[d % C : d % C + 1]


def write_kernel(z, out, x, hidden, weights, first_stats, stats, order, out_s, out_l, first_normed, normed, weight, kept, kept_x, kept_h, half, sems):
    loads = [pltpu.make_async_copy(a, b, sems.at[n]) for n, (a, b) in enumerate(((out, kept), (x, kept_x), (hidden, kept_h), (weights.at[3], weight)))]
    start_all(loads)
    loads[0].wait()
    put_halves(half, kept[...])
    from_matrix(z, half, (out_s, out_l))
    loads[1].wait()
    first_normed[...] = normed_by(first_stats)(kept_x[...])
    loads[2].wait()
    normed[...] = normed_by(stats)(kept_h[...])
    loads[3].wait()


def norm_sums(total):
    group = group_of()
    return [wide(spread_groups(jnp.where(group == n, total[:, :128], 0.0))) for n in (BIAS, GAIN)]


def hidden_kernel(z, gathered, dshift, d_above, d_below, second_normed, stats, affine, weight, first_normed, pre_ref, gain_out, bias_out, slabs, pads):
    total = jnp.sum(gathered[...], axis=0)
    bias_sum, gain_sum = norm_sums(total)
    bias_out[...] = bias_sum[:, :C]
    gain_out[...] = gain_sum[:, :C]
    bias_mean, gain_mean = bias_sum / z.pixels, gain_sum / z.pixels
    factor = affine[2:3] * stats[1:2]
    r, total_rows = z.rims, z.total

    def back(d, normed):
        return factor * (d - bias_mean - normed * gain_mean)

    own = back(dshift[...], second_normed[pl.ds(0, total_rows), :])
    up = back(d_above[...], second_normed[pl.ds(total_rows, r), :]) * inside(z, 1, True)
    down = back(d_below[...], second_normed[pl.ds(total_rows + r, r), :]) * inside(z, 1, False)
    grad, _, _ = convolve(z, own, up, down, 1, pads, None, weight)
    normed = first_normed[...]
    pre = grad * gelu_slope(normed * affine[0:1] + affine[1:2])
    pre_ref[...] = pre
    lane = lax.broadcasted_iota(jnp.int32, (1, 128), 1)
    taps = TAPS * TAPS * C

    def along(row):
        return jnp.concatenate([row[:, :128]] * 3, axis=1)[:, :taps]

    second, left, against, ones = (total[:, n * C : n * C + taps] for n in (SECOND, LEFT, HIDDEN, ONES))
    against = along(stats[1:2]) * (against - along(stats[0:1]) * ones)
    first = along(factor) * (left - along(bias_mean) * ones - along(gain_mean) * against)
    sums = jnp.where(lane < C, fold(column_sum(pre)), fold(column_sum(pre * normed)))
    line = jnp.concatenate([sums[:, : 2 * C], second, first], axis=1)
    slabs[...] = jnp.broadcast_to(line[None], slabs.shape)


def back_kernel(z, gathered, pre, normed, stats, affine, dout, back_s, back_l, one, two, gain_out, bias_out, half, lines):
    bias_sum, gain_sum = norm_sums(jnp.sum(gathered[:, :, pl.ds(0, 128)], axis=0))
    bias_out[...] = bias_sum[:, :C]
    gain_out[...] = gain_sum[:, :C]
    value = dout[...] + affine[0:1] * stats[1:2] * (pre[...] - bias_sum / z.pixels - normed[...] * (gain_sum / z.pixels))
    put_halves(half, value)
    from_matrix(z, half, (back_s, back_l))
    for d in range(C):
        lines[pl.ds(d, 1), :] = gathered[d]
    for ref, group in ((two, LAST_SECOND), (one, LAST_FIRST)):
        for a in range(TAPS):
            for b in range(TAPS):
                at = (group + a * TAPS + b) * C
                ref[a, b] = lines[:, pl.ds(at, C)]


def call(body, ins, outs, scratch=(), sems=0):
    space = {"v": pltpu.VMEM, "h": pltpu.HBM, "V": pltpu.VMEM}
    shapes = []
    for item in scratch:
        if isinstance(item, list):
            shapes.append([pltpu.VMEM(*s) for s in item])
        else:
            shapes.append(pltpu.VMEM(*item))
    if sems:
        shapes.append(pltpu.SemaphoreType.DMA((sems,)))
    run = pl.pallas_call(
        body,
        out_shape=[jax.ShapeDtypeStruct(shape, kind) if s == "v" else space[s](shape, kind) for s, shape, kind in outs],
        in_specs=[pl.BlockSpec(memory_space=space[s]) for s in ins],
        out_specs=[pl.BlockSpec(memory_space=space[s]) for s, _, _ in outs],
        scratch_shapes=shapes,
        compiler_params=pltpu.CompilerParams(vmem_limit_bytes=VMEM_LIMIT),
    )
    return lambda *args: run(
        *(pltpu.with_memory_space_constraint(arg, pltpu.HBM) if s == "h" else arg for s, arg in zip(ins, args))
    )


def exchange(lines, axes):
    shape = lines.shape
    if len(shape) == 2:
        lines = lines.reshape(math.prod(lax.axis_size(axis) for axis in axes), -1, 128)
    return lax.all_to_all(lines, axes, 0, 0, tiled=True).reshape(shape)


def beyond(z, bottom, top, depths):
    hops = max(-(-depth // rows) for rows in z.rows for depth in depths)
    above, below = [], []
    for hop in range(1, hops + 1):
        above.append(lax.ppermute(bottom, "row", [(i, i + hop) for i in range(z.peers - hop)]))
        below.append(lax.ppermute(top, "row", [(i + hop, i) for i in range(z.peers - hop)]))
    if hops == 1:
        return above[0], below[0]
    up, down = [], []
    base = 0
    for depth in depths:
        for n in range(depth):
            for k in (1, 0):
                hop, back = divmod(depth - 1 - n, z.rows[k])
                at = base + (depth - 1 - back) * z.rims + z.rim[k]
                up.append(above[hop][at : at + z.edge[k]])
                hop, back = divmod(n, z.rows[k])
                at = base + back * z.rims + z.rim[k]
                down.append(below[hop][at : at + z.edge[k]])
        base += depth * z.rims
    up.append(jnp.concatenate([pixel_rows(z, above, base, 1, 1), pixel_rows(z, above, base, 0, 1)], axis=1))
    down.append(jnp.concatenate([pixel_rows(z, below, base, 0, 0), pixel_rows(z, below, base, 1, 0)], axis=1))
    return jnp.concatenate(up, axis=0), jnp.concatenate(down, axis=0)


def pixel_rows(z, bands, base, distance, last):
    lines = []
    for k in (0, 1):
        hop, back = divmod(distance, z.rows[k])
        at = base + k * z.images[0]
        half = 128 * abs(last - back)
        lines.append(bands[hop][at : at + z.images[k], half : half + 128])
    lines.append(jnp.zeros((z.slots - sum(z.images), 128), F32))
    return jnp.concatenate(lines, axis=0)


def local(
    image_small, image_large, teacher_small, teacher_large, upstream_small, upstream_large,
    conv_first, gain_first, bias_first, conv_second, gain_second, bias_second,
):
    peers = lax.axis_size("row")
    devices = lax.axis_size("img") * peers
    z = Sizes(image_small.shape, image_large.shape, devices, peers)
    body = lambda function: functools.partial(function, z)
    r = z.rims
    full, half, pair = (z.total, LANES), (2, z.total, 128), (2 * devices, 128)
    weight, left = (2, TAPS * TAP_ROWS, 128), (2, 256, 2 * z.total)
    images = [image_small, image_large, upstream_small, upstream_large, teacher_small, teacher_large]
    f = lambda space, *shape: (space, shape, F32)
    depths = (REACH, 2)
    rim_rows = sum(depths) * r + z.slots

    x, bottom, top, copies = call(
        body(start_kernel),
        "hhhhhh",
        [("v", full, F32), f("v", rim_rows, LANES), f("v", rim_rows, LANES), ("V", pair, F32)],
        [[(a.shape, F32) for a in images], (half, F32)],
        6,
    )(*images)
    gathered = exchange(copies, AXES)
    above, below = beyond(z, bottom, top, depths)
    params = [conv_first, conv_second] + images[2:]
    w1, w2, weights, affine, upstream, teacher, x_copy = call(
        body(prepare_kernel),
        "hhhhhhhhhhv",
        [("v", weight, BF16), ("v", weight, BF16), ("h", (4,) + weight, BF16), f("v", 4, LANES), ("h", full, F32), f("v", z.total, 128), ("h", full, F32)],
        [[(a.shape, F32) for a in params], ((4,) + weight, BF16), (full, F32), ((4, C), F32), (half, F32)],
        16,
    )(*params, *(v.reshape(1, C) for v in (gain_first, bias_first, gain_second, bias_second)), x)

    hidden, stats_one, copies = call(
        body(first_kernel),
        "vvvvvv",
        [("v", full, F32), f("v", 2, LANES), ("V", pair, F32)],
        [z.pads()],
    )(x, above, below, gathered, affine, w1)
    gathered = exchange(copies, AXES)
    extended, near_rows = z.total + 4 * r, z.total + 2 * r
    h_above, h_below, left_one, packed, teachers, wide_u = call(
        body(first_operand_kernel),
        "vvvvvvvhh",
        [
            f("v", 3 * r, LANES), f("v", 3 * r, LANES), ("h", left, BF16), f("h", C, BACK_LANES), f("h", extended, LANES),
            f("h", extended, LANES),
        ],
        [
            z.pads(), z.chains(REACH), (left, BF16), (weight, BF16), ((extended, LANES), F32),
            ((extended, 128), F32), ((extended, LANES), F32), ((C, BACK_LANES), F32),
        ],
        7,
    )(x, hidden, above, below, stats_one, affine, teacher, upstream, weights)

    map_shape = (peers * z.slots, 128)
    out, o_above, o_below, near, stats_two, copies = call(
        body(second_kernel),
        "vvvvvvvvvv",
        [("v", full, F32), f("v", 2 * r, LANES), f("v", 2 * r, LANES), f("v", 2, r, LANES), f("v", 2, LANES), ("V", map_shape, F32)],
        [z.pads(), z.chains(3)],
    )(hidden, h_above, h_below, gathered, affine, w2, x, above, below, teacher)
    gathered = exchange(copies, ("row",))
    out_copy, hidden_copy, left_two, shifts, by_map, by_teacher, up = call(
        body(second_operand_kernel),
        "vvvvvvvhhh",
        [
            ("h", full, F32), f("h", near_rows, LANES), ("v", left, BF16), f("h", 3, near_rows, LANES),
            f("v", near_rows, LANES), f("v", near_rows, LANES), f("v", near_rows, LANES),
        ],
        [
            z.pads(), z.chains(2), ((extended, LANES), F32), ((extended, LANES), F32), (weight, BF16), ((3, near_rows, LANES), F32),
        ],
        11,
    )(hidden, near, stats_two, affine, out, o_above, o_below, teachers, wide_u, weights)

    dout, dshift, d_above, d_below, slabs = call(
        body(upstream_kernel),
        "vvhhvhvvhv",
        [("v", full, F32), ("v", full, F32), f("v", r, LANES), f("v", r, LANES), f("V", devices, 1, BACK_LANES)],
        [((3, near_rows, LANES), F32), (left, BF16), (full, F32), ((C, BACK_LANES), F32), z.pads(), z.pads()],
        4,
    )(gathered, up, shifts, left_one, left_two, packed, by_map, by_teacher, hidden_copy, stats_two)
    gathered = exchange(slabs, AXES)
    out_s, out_l, first_normed, second_normed, weight_back = call(
        body(write_kernel),
        "hhhhvvv",
        [("v", image_small.shape, F32), ("v", image_large.shape, F32), ("v", full, F32), f("v", near_rows, LANES), ("v", weight, BF16)],
        [(full, F32), (full, F32), ((near_rows, LANES), F32), (half, F32)],
        4,
    )(out_copy, x_copy, hidden_copy, weights, stats_one, stats_two, d_above)

    pre, gain_two, bias_two, slabs = call(
        body(hidden_kernel),
        "vvvvvvvvv",
        [("v", full, F32), f("v", 1, C), f("v", 1, C), f("V", devices, 1, LAST_LANES)],
        [z.pads()],
    )(gathered, dshift, d_above, d_below, second_normed, stats_two, affine, weight_back, first_normed)
    gathered = exchange(slabs, AXES)

    back_s, back_l, one, two, gain_one, bias_one = call(
        body(back_kernel),
        "vvvvvv",
        [("v", a.shape, F32) for a in (image_small, image_large, conv_first, conv_second)] + [f("v", 1, C), f("v", 1, C)],
        [(half, F32), ((C, LAST_LANES), F32)],
    )(gathered, pre, first_normed, stats_one, affine, dout)
    return (
        out_s, out_l, back_s, back_l,
        one, gain_one.reshape(C), bias_one.reshape(C),
        two, gain_two.reshape(C), bias_two.reshape(C),
    )


def solution(mesh):
    split_bands, everywhere = P("img", "row", None), P()
    return jax.shard_map(
        local,
        mesh=mesh,
        in_specs=(split_bands,) * 6 + (everywhere,) * 6,
        out_specs=(split_bands,) * 4 + (everywhere,) * 6,
        check_vma=False,
    )
```

```python
import functools
import math

import jax
import jax.numpy as jnp
from jax import lax
from jax.experimental import pallas as pl
from jax.experimental.pallas import tpu as pltpu
from jax.sharding import PartitionSpec as P

C = 32
HS = 32
HL = 64
HEIGHTS = (HS, HL)

norm_eps = 1e-05
map_eps = 1e-06
beta_weight = 1000.0
AXES = ("img", "row")
BLOCK = 8
LANES = BLOCK * C
TAPS = 3
WIDTH = LANES + 128
DEPTH = TAPS * WIDTH
TAP_ROWS = 128 + 2 * C
REACH = 4
ROOT = math.sqrt(2.0 / math.pi)
CUBE = 0.044715
F32 = jnp.float32
BF16 = jnp.bfloat16
VMEM_LIMIT = 32 * 1024 * 1024
BIAS, GAIN, SECOND, LEFT, HIDDEN, ONES = 0, 1, 2, 11, 20, 29
BACK_LANES = 1280
LAST_SECOND, LAST_FIRST, LAST_LANES = 2, 11, 640


class Sizes:
    def __init__(self, small, large, devices, peers):
        self.images = (small[0], large[0])
        self.rows = (small[1], large[1])
        self.blocks = (HS // BLOCK, HL // BLOCK)
        self.step = tuple(n * r for n, r in zip(self.images, self.rows))
        self.count = tuple(b * s for b, s in zip(self.blocks, self.step))
        self.edge = tuple(b * n for b, n in zip(self.blocks, self.images))
        self.start = (self.count[1], 0)
        self.rim = (self.edge[1], 0)
        self.total = sum(self.count)
        self.rims = sum(self.edge)
        self.slots = -(-sum(self.images) // 8) * 8
        self.guard = -(-max(self.images) // 8) * 8
        self.devices = devices
        self.peers = peers
        self.here = float(self.total * BLOCK)
        self.pixels = self.here * devices

    def pads(self):
        return [((TAPS, 2, self.count[k] + 2 * self.step[k], 128), F32) for k in (0, 1)]

    def chains(self, depth):
        return [((2, 2 * self.guard + (depth + 1) * self.rims, 128), F32)] * 2


def split(value):
    high = value.astype(BF16)
    return high, (value - high.astype(F32)).astype(BF16)


def dot(left, right):
    return lax.dot_general(left, right, (((1,), (0,)), ((), ())), preferred_element_type=F32)


def product(left, right):
    if left[0].shape[1] % 128:
        return dot(left[0], right[0]) + (dot(left[0], right[1]) + dot(left[1], right[0]))
    return dot(
        jnp.concatenate([left[0], left[0], left[1]], axis=1), jnp.concatenate([right[0], right[1], right[0]], axis=0)
    )


def spread(left, right):
    right = right.astype(BF16)
    return dot(jnp.concatenate(split(left), axis=1), jnp.concatenate([right, right], axis=0))


def gelu(s):
    return 0.5 * s * (1.0 + jnp.tanh(ROOT * (s + CUBE * s * s * s)))


def gelu_slope(s):
    square = s * s
    t = jnp.tanh(ROOT * s * (1.0 + CUBE * square))
    return 0.5 * (1.0 + t) + 0.5 * s * (1.0 - t * t) * ROOT * (1.0 + 3.0 * CUBE * square)


def spread_groups(row):
    row = row + pltpu.roll(row, 64, 1)
    return row + pltpu.roll(row, 32, 1)


def fold(row):
    return spread_groups(row[:, :128] + row[:, 128:])


def wide(row):
    return jnp.concatenate([row, row], axis=1)


def group_of(rows=1, lanes=128):
    return lax.broadcasted_iota(jnp.int32, (rows, lanes), 1) // C


def column_sum(value):
    return jnp.sum(value, axis=0, keepdims=True)


def send_lines(z, ref, lines):
    for n, line in enumerate(lines):
        ref[pl.ds(n, z.devices, stride=len(lines)), :] = jnp.broadcast_to(line, (z.devices, 128))


def moments(z, value, ref):
    few = min(8, z.total)
    pivot = fold(column_sum(value[:few])) / float(few * BLOCK)
    off = value - wide(pivot)
    first, second = fold(column_sum(off)), fold(column_sum(off * off))
    send_lines(z, ref, [pivot + first / z.here, second - first * first / z.here])


def merged(z, ref):
    means = ref[pl.ds(0, z.devices, stride=2), :]
    center = jnp.mean(means, axis=0, keepdims=True)
    off = means - center
    within = jnp.mean(ref[pl.ds(1, z.devices, stride=2), :], axis=0, keepdims=True)
    variance = within / z.here + jnp.mean(off * off, axis=0, keepdims=True)
    return wide(center), wide(lax.rsqrt(variance + norm_eps))


def put_halves(ref, value):
    ref[0] = value[:, :128]
    ref[1] = value[:, 128:]


def whole(ref):
    return jnp.concatenate([ref[0], ref[1]], axis=1)


def to_matrix(z, refs, half):
    for k in (0, 1):
        for j in range(z.blocks[k]):
            at = z.start[k] + j * z.step[k]
            for i in range(z.images[k]):
                for h in (0, 1):
                    half[h, pl.ds(at + i * z.rows[k], z.rows[k]), :] = refs[k][i, :, pl.ds(LANES * j + 128 * h, 128)]


def from_matrix(z, half, refs):
    for k in (0, 1):
        for j in range(z.blocks[k]):
            at = z.start[k] + j * z.step[k]
            for i in range(z.images[k]):
                for h in (0, 1):
                    refs[k][i, :, pl.ds(LANES * j + 128 * h, 128)] = half[h, pl.ds(at + i * z.rows[k], z.rows[k]), :]


def take_rims(z, half, depth, bottom, top):
    for k in (0, 1):
        for d in range(1, depth + 1):
            to_bottom = pl.ds((depth - d) * z.rims + z.rim[k], z.edge[k])
            to_top = pl.ds((d - 1) * z.rims + z.rim[k], z.edge[k])
            if d <= z.rows[k]:
                bottom[to_bottom, :] = half[pl.ds(z.start[k] + z.rows[k] - d, z.edge[k], stride=z.rows[k]), :]
                top[to_top, :] = half[pl.ds(z.start[k] + d - 1, z.edge[k], stride=z.rows[k]), :]
            else:
                bottom[to_bottom, :] = jnp.zeros((z.edge[k], 128), F32)
                top[to_top, :] = jnp.zeros((z.edge[k], 128), F32)


def inside(z, depth, above):
    at = lax.axis_index("row")
    large = lax.broadcasted_iota(jnp.int32, (z.rims, 1), 0) < z.rim[0]
    parts = []
    for n in range(depth):
        if above:
            ok = [jnp.where(at * rows >= depth - n, 1.0, 0.0) for rows in z.rows]
        else:
            ok = [jnp.where((at + 1) * rows + n + 1 <= height, 1.0, 0.0) for rows, height in zip(z.rows, HEIGHTS)]
        parts.append(jnp.where(large, ok[1], ok[0]).astype(F32))
    return jnp.concatenate(parts, axis=0)


def clear_guards(z, pads, a):
    for k in (0, 1):
        pads[k][a, 1, pl.ds(0, z.step[k]), :] = jnp.zeros((z.step[k], 128), F32)
        pads[k][a, 0, pl.ds(z.step[k] + z.count[k], z.step[k]), :] = jnp.zeros((z.step[k], 128), F32)


def fill_center(z, pads, value):
    clear_guards(z, pads, 1)
    for k in (0, 1):
        for h in (0, 1):
            pads[k][1, h, pl.ds(z.step[k], z.count[k]), :] = value[z.start[k] : z.start[k] + z.count[k], 128 * h : 128 * h + 128]


def fill_shifted(z, pads, above, below):
    for k in (0, 1):
        ref, step, count, rows = pads[k], z.step[k], z.count[k], z.rows[k]
        rim = slice(z.rim[k], z.rim[k] + z.edge[k])
        for h in (0, 1):
            lanes = slice(128 * h, 128 * h + 128)
            ref[0, h, pl.ds(step, count), :] = ref[1, h, pl.ds(step - 1, count), :]
            ref[2, h, pl.ds(step, count), :] = ref[1, h, pl.ds(step + 1, count), :]
            ref[0, h, pl.ds(step, z.edge[k], stride=rows), :] = above[rim, lanes]
            ref[2, h, pl.ds(step + rows - 1, z.edge[k], stride=rows), :] = below[rim, lanes]


def fill_pads(z, pads, value, above, below):
    fill_center(z, pads, value)
    fill_shifted(z, pads, above, below)
    for a in (0, 2):
        clear_guards(z, pads, a)


def band_operand(z, pads, taps=range(TAPS)):
    lane = lax.broadcasted_iota(jnp.int32, (1, 128), 1)
    parts = []
    for k in (1, 0):
        ref, step, count = pads[k], z.step[k], z.count[k]
        columns = []
        for a in taps:
            before = ref[a, 1, pl.ds(0, count), :]
            after = ref[a, 0, pl.ds(2 * step, count), :]
            columns += [
                ref[a, 0, pl.ds(step, count), :],
                ref[a, 1, pl.ds(step, count), :],
                jnp.where(lane >= 96, before, jnp.where(lane < 32, after, 0.0)),
            ]
        parts.append(jnp.concatenate(columns, axis=1))
    return jnp.concatenate(parts, axis=0)


def rim_operand(z, chain, depth):
    rows, g = (depth + 1) * z.rims, z.guard
    lane = lax.broadcasted_iota(jnp.int32, (1, 128), 1)
    m = lax.broadcasted_iota(jnp.int32, (z.rims, 1), 0)
    large = m < z.rim[0]
    has_before = jnp.where(large, m, m - z.rim[0]) >= jnp.where(large, z.images[1], z.images[0])
    has_after = m < jnp.where(large, z.rim[0] - z.images[1], z.rims - z.images[0])
    take = [(lane >= 96) & has_before & large, (lane >= 96) & has_before & ~large, (lane < 32) & has_after & large, (lane < 32) & has_after & ~large]
    columns = []
    for r in range(depth + 1):
        at = g + r * z.rims
        edge = jnp.zeros((z.rims, 128), F32)
        for mask, half, shift in zip(take, (1, 1, 0, 0), (-z.images[1], -z.images[0], z.images[1], z.images[0])):
            edge = jnp.where(mask, chain[half, pl.ds(at + shift, z.rims), :], edge)
        columns.append(jnp.concatenate([chain[0, pl.ds(at, z.rims), :], chain[1, pl.ds(at, z.rims), :], edge], axis=1))
    return jnp.concatenate(
        [jnp.concatenate(columns[n : n + TAPS], axis=1) for n in range(depth - 1)], axis=0
    )


def convolve(z, own, above, below, depth, pads, chains, weight):
    r = z.rims
    fill_pads(z, pads, own, above[(depth - 1) * r :], below[:r])
    parts = [band_operand(z, pads)]
    if depth > 1:
        for side, (rim, chain) in enumerate(zip((above, below), chains)):
            rim_at, own_at = (z.guard, z.guard + depth * r) if side == 0 else (z.guard + r, z.guard)
            for h in (0, 1):
                chain[h, pl.ds(rim_at, depth * r), :] = rim[:, 128 * h : 128 * h + 128]
                for k in (0, 1):
                    row = z.step[k] + (0 if side == 0 else z.rows[k] - 1)
                    chain[h, pl.ds(own_at + z.rim[k], z.edge[k]), :] = pads[k][1, h, pl.ds(row, z.edge[k], stride=z.rows[k]), :]
            parts.append(rim_operand(z, chain, depth))
    result = product(split(jnp.concatenate(parts, axis=0)), (weight_matrix(weight.at[0]), weight_matrix(weight.at[1])))
    n = z.total + (depth - 1) * r
    return result[: z.total], result[z.total : n], result[n:]


def image_sums(z, value):
    slot = lax.broadcasted_iota(jnp.int32, (z.slots, 1), 0)
    sums = jnp.zeros((z.slots, 128), F32)
    for k in (0, 1):
        line = value[z.start[k] : z.start[k] + z.step[k]]
        for j in range(1, z.blocks[k]):
            at = z.start[k] + j * z.step[k]
            line = line + value[at : at + z.step[k]]
        image = lax.broadcasted_iota(jnp.int32, (z.step[k], 1), 0) // z.rows[k]
        for i in range(z.images[k]):
            sums = jnp.where(slot == i + k * z.images[0], column_sum(jnp.where(image == i, line, 0.0)), sums)
    return sums


def image_rows(z, values, rims):
    parts = []
    for k in (1, 0):
        image = lax.broadcasted_iota(jnp.int32, (z.step[k], 1), 0) // z.rows[k]
        line = jnp.zeros((z.step[k], 128), F32)
        for i in range(z.images[k]):
            at = i + k * z.images[0]
            line = jnp.where(image == i, values[at : at + 1], line)
        parts += [line] * z.blocks[k]
    if rims:
        m = lax.broadcasted_iota(jnp.int32, (z.rims, 1), 0)
        image = jnp.where(m < z.rim[0], z.images[0] + m % z.images[1], (m - z.rim[0]) % z.images[0])
        line = jnp.zeros((z.rims, 128), F32)
        for at in range(sum(z.images)):
            line = jnp.where(image == at, values[at : at + 1], line)
        parts += [line] * rims
    return jnp.concatenate(parts, axis=0)


def channel_mean():
    a = lax.broadcasted_iota(jnp.int32, (LANES, 128), 0) // C
    b = lax.broadcasted_iota(jnp.int32, (LANES, 128), 1) % 64
    return jnp.where(a == b, 1.0 / C, 0.0).astype(F32)


def to_channels():
    a = lax.broadcasted_iota(jnp.int32, (128, LANES), 0)
    b = lax.broadcasted_iota(jnp.int32, (128, LANES), 1) // C
    return jnp.where(a == b, 1.0, 0.0).astype(F32)


def attention(value):
    return spread(value * value, channel_mean())


def start_all(copies):
    for copy in copies:
        copy.start()


def wait_all(copies):
    for copy in copies:
        copy.wait()


def start_kernel(z, small, large, up_s, up_l, t_s, t_l, x, bottom, top, copies, raw, half, sems):
    loads = [pltpu.make_async_copy(a, b, sems.at[n]) for n, (a, b) in enumerate(zip((small, large, up_s, up_l, t_s, t_l), raw))]
    start_all(loads)
    r, n = z.rims, REACH * z.rims
    tail = n + 2 * r
    for ref in (bottom, top):
        ref[pl.ds(tail, z.slots), :] = jnp.zeros((z.slots, LANES), F32)
    wait_all(loads[:2])
    to_matrix(z, raw[:2], half)
    value = whole(half)
    x[...] = value
    moments(z, value, copies)
    for h in (0, 1):
        lanes = pl.ds(128 * h, 128)
        take_rims(z, half.at[h], REACH, bottom.at[pl.ds(0, n), lanes], top.at[pl.ds(0, n), lanes])
    wait_all(loads[2:])
    for k in (0, 1):
        width, rows = HEIGHTS[k], z.rows[k]
        for i in range(z.images[k]):
            slot = pl.ds(tail + i + k * z.images[0], 1)
            for d in (0, 1):
                to_bottom, to_top = n + (1 - d) * r + z.rim[k] + i, n + d * r + z.rim[k] + i
                for j in range(z.blocks[k]):
                    lanes, at = pl.ds(LANES * j, LANES), j * z.images[k]
                    if d < rows:
                        bottom[pl.ds(to_bottom + at, 1), :] = raw[2 + k][i, pl.ds(rows - 1 - d, 1), lanes]
                        top[pl.ds(to_top + at, 1), :] = raw[2 + k][i, pl.ds(d, 1), lanes]
                    else:
                        bottom[pl.ds(to_bottom + at, 1), :] = jnp.zeros((1, LANES), F32)
                        top[pl.ds(to_top + at, 1), :] = jnp.zeros((1, LANES), F32)
                if d < rows:
                    bottom[slot, pl.ds(128 * (1 - d), width)] = raw[4 + k][i, pl.ds(rows - 1 - d, 1), :]
                    top[slot, pl.ds(128 * d, width)] = raw[4 + k][i, pl.ds(d, 1), :]


def banded(taps, ref):
    row = lax.broadcasted_iota(jnp.int32, (128, 128), 0) // C
    lane = group_of(128)
    for a in range(TAPS):
        main = jnp.zeros((128, 128), F32)
        for b in range(TAPS):
            main = jnp.where(row - lane + 1 == b, taps[a][b], main)
        before = jnp.where(lane[:C] == 0, taps[a][0][:C], 0.0)
        after = jnp.where(lane[:C] == 3, taps[a][2][:C], 0.0)
        for n, part in enumerate(split(jnp.concatenate([main, before, after], axis=0))):
            ref[n, pl.ds(a * TAP_ROWS, TAP_ROWS), :] = part


def weight_matrix(ref):
    rows = []
    zeros = jnp.zeros((128 - C, 128), BF16)
    for a in range(TAPS):
        at = a * TAP_ROWS
        main = ref[pl.ds(at, 128), :]
        before = jnp.concatenate([zeros, ref[pl.ds(at + 128, C), :]], axis=0)
        after = jnp.concatenate([ref[pl.ds(at + 128 + C, C), :], zeros], axis=0)
        rows += [
            jnp.concatenate([main, before], axis=1),
            jnp.concatenate([after, main], axis=1),
            jnp.concatenate([before, after], axis=1),
        ]
    return jnp.concatenate(rows, axis=0)


def prepare_kernel(z, first, second, up_s, up_l, t_s, t_l, g1, b1, g2, b2, x, w1, w2, weights, affine, upstream, teacher, x_copy, raw, kept, kept_u, rows, half, sems):
    targets = tuple(raw) + tuple(rows.at[pl.ds(n, 1), :] for n in range(4))
    refs = (first, second, up_s, up_l, t_s, t_l, g1, b1, g2, b2)
    loads = [pltpu.make_async_copy(a, b, sems.at[n]) for n, (a, b) in enumerate(zip(refs, targets))]
    start_all(loads)
    stores = [pltpu.make_async_copy(x, x_copy, sems.at[13])]
    stores[0].start()
    wait_all(loads)
    to_matrix(z, raw[2:4], half)
    kept_u[...] = whole(half)
    stores.append(pltpu.make_async_copy(kept_u, upstream, sems.at[10]))
    stores[1].start()
    for n, (source, forward) in enumerate(zip(raw[:2], (w1, w2))):
        tiles = []
        for a in range(TAPS):
            line = [jnp.concatenate([source[a, b]] * 4, axis=1) for b in range(TAPS)]
            tiles.append([jnp.concatenate([tap] * 4, axis=0) for tap in line])
        turned = [[tiles[TAPS - 1 - a][TAPS - 1 - b].T for b in range(TAPS)] for a in range(TAPS)]
        banded(tiles, forward)
        banded(turned, kept.at[n])
        stores.append(pltpu.make_async_copy(kept.at[n], weights.at[n], sems.at[11 + n]))
        stores[-1].start()
    affine[...] = jnp.concatenate([rows[...]] * BLOCK, axis=1)
    teacher[...] = jnp.zeros(teacher.shape, F32)
    for k, ref in ((0, raw[4]), (1, raw[5])):
        for i in range(z.images[k]):
            line = ref[i]
            for j in range(z.blocks[k]):
                at = z.start[k] + j * z.step[k] + i * z.rows[k]
                for lane in (0, 64):
                    teacher[pl.ds(at, z.rows[k]), pl.ds(lane, BLOCK)] = line[:, j * BLOCK : (j + 1) * BLOCK]
    wait_all(stores)


def normed_by(stats):
    return lambda v: (v - stats[0:1]) * stats[1:2]


def activation(center, scale, gain, bias):
    factor = scale * gain
    offset = bias - center * factor
    return lambda v: gelu(v * factor + offset)


def first_kernel(z, x, above, below, gathered, affine, weight, hidden, h_above, h_below, stats, copies, pads, chains):
    n = REACH * z.rims
    center, scale = merged(z, gathered)
    act = activation(center, scale, affine[0:1], affine[1:2])
    own = act(x[...])
    up, down = act(above[pl.ds(0, n), :]) * inside(z, 4, True), act(below[pl.ds(0, n), :]) * inside(z, 4, False)
    own, up, down = convolve(z, own, up, down, 4, pads, chains, weight)
    moments(z, own, copies)
    hidden[...] = own
    h_above[...] = up
    h_below[...] = down
    stats[0:1] = center
    stats[1:2] = scale


def second_kernel(z, hidden, h_above, h_below, gathered, affine, weight, x, x_above, x_below, teacher, out, o_above, o_below, near, stats, copies, pads, chains):
    center, scale = merged(z, gathered)
    act = activation(center, scale, affine[2:3], affine[3:4])
    r = z.rims
    own = act(hidden[...])
    up, down = act(h_above[...]) * inside(z, 3, True), act(h_below[...]) * inside(z, 3, False)
    own, up, down = convolve(z, own, up, down, 3, pads, chains, weight)
    own = x[...] + own
    amap = attention(own)
    lane = lax.broadcasted_iota(jnp.int32, (1, 128), 1)
    sums = image_sums(z, amap * jnp.where(lane < 64, amap, teacher[...]))
    copies[...] = jnp.concatenate([sums] * z.peers, axis=0)
    out[...] = own
    o_above[...] = x_above[pl.ds(2 * r, 2 * r), :] + up
    o_below[...] = x_below[pl.ds(0, 2 * r), :] + down
    near[0] = h_above[pl.ds(2 * r, r), :]
    near[1] = h_below[pl.ds(0, r), :]
    stats[0:1] = center
    stats[1:2] = scale


def tap_rows(q):
    return 128 + 3 * C if q < 0 else 128 if q == 4 else q * C


def tap_product(z, operand, own, above, below, pads):
    fill_center(z, pads, own)
    fill_shifted(z, pads, above, below)
    columns = []
    for a in range(TAPS):
        columns.append(
            jnp.concatenate([pads[k][TAPS - 1 - a, h, pl.ds(z.step[k], z.count[k]), :] for h in (0, 1) for k in (1, 0)], axis=0)
        )
    return product(operand, split(jnp.concatenate(columns, axis=1)))


def tap_sums(result, tiles, first_group):
    group = group_of()
    for a in range(TAPS):
        for b in range(TAPS):
            total = None
            for p in range(4):
                at = tap_rows(p + b - 1)
                part = result[at : at + C, 128 * a : 128 * a + 128]
                total = part if total is None else jnp.where(group == p, part, total)
            tile, slot = divmod(first_group + a * TAPS + b, 4)
            tiles[tile] = jnp.where(group == slot, spread_groups(total), tiles[tile])


def tap_counts(z, turned, tiles, first_group):
    group = group_of()
    m = lax.broadcasted_iota(jnp.int32, (1, 2 * z.total), 1) % z.total
    row = jnp.where(m < z.start[0], m % z.rows[1], (m - z.start[0]) % z.rows[0])
    height = jnp.where(m < z.start[0], z.rows[1], z.rows[0])
    at = lax.axis_index("row")
    lost = {
        0: (row == height - 1) & (at == z.peers - 1),
        2: (row == 0) & (at == 0),
    }
    for a in range(TAPS):
        column = jnp.sum(jnp.where(lost[a], 0.0, turned) if a in lost else turned, axis=1, keepdims=True)
        for b in range(TAPS):
            total = sum(column[tap_rows(p + b - 1) : tap_rows(p + b - 1) + C] for p in range(4))
            tile, slot = divmod(first_group + a * TAPS + b, 4)
            tiles[tile] = jnp.where(group == slot, total, tiles[tile])


def turned_operand(z, value, pads, kept):
    fill_center(z, pads, value)
    lane = lax.broadcasted_iota(jnp.int32, (1, 128), 1)
    halves = ([], [])
    for k in (1, 0):
        ref, step, count = pads[k], z.step[k], z.count[k]
        low, high = ref[1, 0, pl.ds(step, count), :], ref[1, 1, pl.ds(step, count), :]
        before, after = ref[1, 1, pl.ds(0, count), :], ref[1, 0, pl.ds(2 * step, count), :]
        for part, main, left, right in ((halves[0], low, before, high), (halves[1], high, low, after)):
            part.append(jnp.concatenate([main, jnp.where(lane >= 96, left, jnp.where(lane < 32, right, 0.0))], axis=1))
    turned = jnp.concatenate(halves[0] + halves[1], axis=0).T
    parts = split(turned)
    for n in (0, 1):
        kept[n] = parts[n]
    return turned


def first_operand_kernel(z, x, hidden, h_above, h_below, above, below, stats, affine, teacher, upstream, weights, left, packed, teachers, spread_u, near_u, pads, chains, kept, kept_w, kept_u, pixels, kept_t, kept_c, kept_packed, sems):
    r, own = z.rims, pl.ds(0, z.total)
    loads = [pltpu.make_async_copy(upstream, kept_u.at[own, :], sems.at[0]), pltpu.make_async_copy(weights.at[1], kept_w, sems.at[1])]
    start_all(loads)
    act = activation(stats[0:1], stats[1:2], affine[0:1], affine[1:2])
    value = turned_operand(z, act(x[...]), pads, kept)
    stores = [pltpu.make_async_copy(kept, left, sems.at[2])]
    stores[0].start()
    tiles = [jnp.zeros((C, 128), F32) for _ in range(BACK_LANES // 128)]
    tap_counts(z, value, tiles, ONES)
    result = tap_product(
        z, (kept[0], kept[1]), hidden[...], h_above[pl.ds(2 * r, r), :] * inside(z, 1, True), h_below[pl.ds(0, r), :] * inside(z, 1, False), pads
    )
    tap_sums(result, tiles, HIDDEN)
    kept_packed[...] = jnp.concatenate(tiles, axis=1)
    stores.append(pltpu.make_async_copy(kept_packed, packed, sems.at[6]))
    stores[1].start()
    pixels[own, :] = teacher[...]
    pixels[pl.ds(z.total, 4 * r), :] = jnp.zeros((4 * r, 128), F32)
    n = (REACH + 2) * r
    for side, ref in enumerate((above, below)):
        for d in (0, 1):
            for k in (0, 1):
                line = ref[pl.ds(n + k * z.images[0], z.images[k]), pl.ds(128 * d, 128)]
                for j in range(z.blocks[k]):
                    at = z.total + (2 * side + d) * r + z.rim[k] + j * z.images[k]
                    pixels[pl.ds(at, z.images[k]), pl.ds(0, BLOCK)] = line[:, j * BLOCK : (j + 1) * BLOCK]
    kept_t[...] = spread(pixels[...], to_channels())
    stores.append(pltpu.make_async_copy(kept_t, teachers, sems.at[3]))
    stores[2].start()
    n = REACH * r
    up, down = above[pl.ds(n, 2 * r), :] * inside(z, 2, True), below[pl.ds(n, 2 * r), :] * inside(z, 2, False)
    kept_u[pl.ds(z.total, r), :] = up[r:]
    kept_u[pl.ds(z.total + r, r), :] = down[:r]
    wait_all(loads)
    stores.append(pltpu.make_async_copy(kept_u, near_u, sems.at[5]))
    stores[3].start()
    kept_c[...] = jnp.concatenate(convolve(z, kept_u[own, :], up, down, 2, pads, chains, kept_w), axis=0)
    stores.append(pltpu.make_async_copy(kept_c, spread_u, sems.at[4]))
    stores[4].start()
    wait_all(stores)


def second_operand_kernel(z, hidden, near, stats, affine, out, o_above, o_below, teachers, spread_u, near_u, weights, out_copy, hidden_copy, left, shifts, by_map, by_teacher, up, pads, chains, kept_t, kept_u, kept_w, kept_s, sems):
    r, total = z.rims, z.total
    loads = [
        pltpu.make_async_copy(teachers, kept_t, sems.at[0]),
        pltpu.make_async_copy(weights.at[1], kept_w, sems.at[1]),
        pltpu.make_async_copy(spread_u, kept_u, sems.at[2]),
    ]
    start_all(loads)
    stores = [
        pltpu.make_async_copy(out, out_copy, sems.at[4]),
        pltpu.make_async_copy(hidden, hidden_copy.at[pl.ds(0, total), :], sems.at[7]),
        pltpu.make_async_copy(near.at[0], hidden_copy.at[pl.ds(total, r), :], sems.at[8]),
        pltpu.make_async_copy(near.at[1], hidden_copy.at[pl.ds(total + r, r), :], sems.at[9]),
        pltpu.make_async_copy(near_u, up, sems.at[10]),
    ]
    start_all(stores)
    normed = normed_by(stats)(jnp.concatenate([hidden[...], near[0], near[1]], axis=0))
    shifted = normed * affine[2:3] + affine[3:4]
    turned_operand(z, gelu(shifted[:total]), pads, left)
    ones = jnp.ones((total, 1), F32)
    masks = jnp.concatenate([ones, inside(z, 1, True), inside(z, 1, False)], axis=0)
    slopes = gelu_slope(shifted) * masks
    o = jnp.concatenate([out[...], o_above[...] * inside(z, 2, True), o_below[...] * inside(z, 2, False)], axis=0)
    for_map = spread(attention(o), to_channels()) * o
    wait_all(loads)
    for_teacher = kept_t[...] * o
    kept_s[0] = kept_u[...] * slopes
    for n, value, ref in ((1, for_map, by_map), (2, for_teacher, by_teacher)):
        own, before, after = value[:total], value[total : total + 2 * r], value[total + 2 * r :]
        ref[...] = jnp.concatenate([own, before[r:], after[:r]], axis=0)
        kept_s[n] = jnp.concatenate(convolve(z, own, before, after, 2, pads, chains, kept_w), axis=0) * slopes
    stores.append(pltpu.make_async_copy(kept_s, shifts, sems.at[5]))
    stores[-1].start()
    wait_all(stores)


def upstream_kernel(z, gathered, up, shifts, left_1, left_2, packed, by_map, by_teacher, hidden, stats, dout, dshift, d_above, d_below, slabs, kept_s, kept_left, kept_h, kept_packed, pads, more_pads, sems):
    r, total = z.rims, z.total
    loads = [
        pltpu.make_async_copy(a, b, sems.at[n])
        for n, (a, b) in enumerate(((shifts, kept_s), (left_1, kept_left), (hidden.at[pl.ds(0, total), :], kept_h), (packed, kept_packed)))
    ]
    start_all(loads)
    lane = lax.broadcasted_iota(jnp.int32, (z.slots, 128), 1)
    sums = sum(gathered[pl.ds(n * z.slots, z.slots), :] for n in range(z.peers))
    square = jnp.sum(jnp.where(lane < 64, sums, 0.0), axis=1, keepdims=True)
    cross = jnp.sum(jnp.where(lane < 64, 0.0, sums), axis=1, keepdims=True)
    inverse = lax.rsqrt(square + map_eps)
    inner = beta_weight * (square * inverse - cross) * inverse
    shape = (z.slots, 128)
    for_map = (beta_weight - inner) * inverse * inverse * (2.0 / C)
    for_teacher = beta_weight * inverse * (2.0 / C)
    for_map, for_teacher = (wide(image_rows(z, jnp.broadcast_to(v, shape), 2)) for v in (for_map, for_teacher))
    value = up[...] + for_map * by_map[...] - for_teacher * by_teacher[...]
    dout[...] = value[:total]
    wait_all(loads[:2])
    shift = kept_s[0] + for_map * kept_s[1] - for_teacher * kept_s[2]
    pre, above, below = shift[:total], shift[total : total + r], shift[total + r :]
    dshift[...] = pre
    d_above[...] = above
    d_below[...] = below
    second = tap_product(z, (left_2[0], left_2[1]), value[:total], value[total : total + r], value[total + r :], pads)
    first = tap_product(z, (kept_left[0], kept_left[1]), pre, above, below, more_pads)
    wait_all(loads[2:])
    normed = normed_by(stats)(kept_h[...])
    tiles = [kept_packed[:, 128 * n : 128 * n + 128] for n in range(BACK_LANES // 128)]
    group = group_of()
    tiles[0] = jnp.where(group == BIAS, fold(column_sum(pre)), jnp.where(group == GAIN, fold(column_sum(pre * normed)), tiles[0]))
    tap_sums(second, tiles, SECOND)
    tap_sums(first, tiles, LEFT)
    line = jnp.concatenate(tiles, axis=1)
    for d in range(z.devices):
        slabs[d] = line[d % C : d % C + 1]


def write_kernel(z, out, x, hidden, weights, first_stats, stats, order, out_s, out_l, first_normed, normed, weight, kept, kept_x, kept_h, half, sems):
    loads = [pltpu.make_async_copy(a, b, sems.at[n]) for n, (a, b) in enumerate(((out, kept), (x, kept_x), (hidden, kept_h), (weights.at[0], weight)))]
    start_all(loads)
    loads[0].wait()
    put_halves(half, kept[...])
    from_matrix(z, half, (out_s, out_l))
    loads[1].wait()
    first_normed[...] = normed_by(first_stats)(kept_x[...])
    loads[2].wait()
    normed[...] = normed_by(stats)(kept_h[...])
    loads[3].wait()


def norm_sums(total):
    group = group_of()
    return [wide(spread_groups(jnp.where(group == n, total[:, :128], 0.0))) for n in (BIAS, GAIN)]


def hidden_kernel(z, gathered, dshift, d_above, d_below, second_normed, stats, affine, weight, first_normed, pre_ref, gain_out, bias_out, slabs, pads):
    total = jnp.sum(gathered[...], axis=0)
    bias_sum, gain_sum = norm_sums(total)
    bias_out[...] = bias_sum[:, :C]
    gain_out[...] = gain_sum[:, :C]
    bias_mean, gain_mean = bias_sum / z.pixels, gain_sum / z.pixels
    factor = affine[2:3] * stats[1:2]
    r, total_rows = z.rims, z.total

    def back(d, normed):
        return factor * (d - bias_mean - normed * gain_mean)

    own = back(dshift[...], second_normed[pl.ds(0, total_rows), :])
    up = back(d_above[...], second_normed[pl.ds(total_rows, r), :]) * inside(z, 1, True)
    down = back(d_below[...], second_normed[pl.ds(total_rows + r, r), :]) * inside(z, 1, False)
    grad, _, _ = convolve(z, own, up, down, 1, pads, None, weight)
    normed = first_normed[...]
    pre = grad * gelu_slope(normed * affine[0:1] + affine[1:2])
    pre_ref[...] = pre
    lane = lax.broadcasted_iota(jnp.int32, (1, 128), 1)
    taps = TAPS * TAPS * C

    def along(row):
        return jnp.concatenate([row[:, :128]] * 3, axis=1)[:, :taps]

    second, left, against, ones = (total[:, n * C : n * C + taps] for n in (SECOND, LEFT, HIDDEN, ONES))
    against = along(stats[1:2]) * (against - along(stats[0:1]) * ones)
    first = along(factor) * (left - along(bias_mean) * ones - along(gain_mean) * against)
    sums = jnp.where(lane < C, fold(column_sum(pre)), fold(column_sum(pre * normed)))
    line = jnp.concatenate([sums[:, : 2 * C], second, first], axis=1)
    slabs[...] = jnp.broadcast_to(line[None], slabs.shape)


def back_kernel(z, gathered, pre, normed, stats, affine, dout, back_s, back_l, one, two, gain_out, bias_out, half, lines):
    bias_sum, gain_sum = norm_sums(jnp.sum(gathered[:, :, pl.ds(0, 128)], axis=0))
    bias_out[...] = bias_sum[:, :C]
    gain_out[...] = gain_sum[:, :C]
    value = dout[...] + affine[0:1] * stats[1:2] * (pre[...] - bias_sum / z.pixels - normed[...] * (gain_sum / z.pixels))
    put_halves(half, value)
    from_matrix(z, half, (back_s, back_l))
    for d in range(C):
        lines[pl.ds(d, 1), :] = gathered[d]
    for ref, group in ((two, LAST_SECOND), (one, LAST_FIRST)):
        for a in range(TAPS):
            for b in range(TAPS):
                at = (group + a * TAPS + b) * C
                ref[a, b] = lines[:, pl.ds(at, C)]


def call(body, ins, outs, scratch=(), sems=0):
    space = {"v": pltpu.VMEM, "h": pltpu.HBM, "V": pltpu.VMEM}
    shapes = []
    for item in scratch:
        if isinstance(item, list):
            shapes.append([pltpu.VMEM(*s) for s in item])
        else:
            shapes.append(pltpu.VMEM(*item))
    if sems:
        shapes.append(pltpu.SemaphoreType.DMA((sems,)))
    run = pl.pallas_call(
        body,
        out_shape=[jax.ShapeDtypeStruct(shape, kind) if s == "v" else space[s](shape, kind) for s, shape, kind in outs],
        in_specs=[pl.BlockSpec(memory_space=space[s]) for s in ins],
        out_specs=[pl.BlockSpec(memory_space=space[s]) for s, _, _ in outs],
        scratch_shapes=shapes,
        compiler_params=pltpu.CompilerParams(vmem_limit_bytes=VMEM_LIMIT),
    )
    return lambda *args: run(
        *(pltpu.with_memory_space_constraint(arg, pltpu.HBM) if s == "h" else arg for s, arg in zip(ins, args))
    )


def exchange(lines, axes):
    shape = lines.shape
    if len(shape) == 2:
        lines = lines.reshape(math.prod(lax.axis_size(axis) for axis in axes), -1, 128)
    return lax.all_to_all(lines, axes, 0, 0, tiled=True).reshape(shape)


def beyond(z, bottom, top, depths):
    hops = max(-(-depth // rows) for rows in z.rows for depth in depths)
    above, below = [], []
    for hop in range(1, hops + 1):
        above.append(lax.ppermute(bottom, "row", [(i, i + hop) for i in range(z.peers - hop)]))
        below.append(lax.ppermute(top, "row", [(i + hop, i) for i in range(z.peers - hop)]))
    if hops == 1:
        return above[0], below[0]
    up, down = [], []
    base = 0
    for depth in depths:
        for n in range(depth):
            for k in (1, 0):
                hop, back = divmod(depth - 1 - n, z.rows[k])
                at = base + (depth - 1 - back) * z.rims + z.rim[k]
                up.append(above[hop][at : at + z.edge[k]])
                hop, back = divmod(n, z.rows[k])
                at = base + back * z.rims + z.rim[k]
                down.append(below[hop][at : at + z.edge[k]])
        base += depth * z.rims
    up.append(jnp.concatenate([pixel_rows(z, above, base, 1, 1), pixel_rows(z, above, base, 0, 1)], axis=1))
    down.append(jnp.concatenate([pixel_rows(z, below, base, 0, 0), pixel_rows(z, below, base, 1, 0)], axis=1))
    return jnp.concatenate(up, axis=0), jnp.concatenate(down, axis=0)


def pixel_rows(z, bands, base, distance, last):
    lines = []
    for k in (0, 1):
        hop, back = divmod(distance, z.rows[k])
        at = base + k * z.images[0]
        half = 128 * abs(last - back)
        lines.append(bands[hop][at : at + z.images[k], half : half + 128])
    lines.append(jnp.zeros((z.slots - sum(z.images), 128), F32))
    return jnp.concatenate(lines, axis=0)


def local(
    image_small, image_large, teacher_small, teacher_large, upstream_small, upstream_large,
    conv_first, gain_first, bias_first, conv_second, gain_second, bias_second,
):
    peers = lax.axis_size("row")
    devices = lax.axis_size("img") * peers
    z = Sizes(image_small.shape, image_large.shape, devices, peers)
    body = lambda function: functools.partial(function, z)
    r = z.rims
    full, half, pair = (z.total, LANES), (2, z.total, 128), (2 * devices, 128)
    weight, left = (2, TAPS * TAP_ROWS, 128), (2, 256, 2 * z.total)
    images = [image_small, image_large, upstream_small, upstream_large, teacher_small, teacher_large]
    f = lambda space, *shape: (space, shape, F32)
    depths = (REACH, 2)
    rim_rows = sum(depths) * r + z.slots

    x, bottom, top, copies = call(
        body(start_kernel),
        "hhhhhh",
        [("v", full, F32), f("v", rim_rows, LANES), f("v", rim_rows, LANES), ("V", pair, F32)],
        [[(a.shape, F32) for a in images], (half, F32)],
        6,
    )(*images)
    gathered = exchange(copies, AXES)
    above, below = beyond(z, bottom, top, depths)
    params = [conv_first, conv_second] + images[2:]
    w1, w2, weights, affine, upstream, teacher, x_copy = call(
        body(prepare_kernel),
        "hhhhhhhhhhv",
        [("v", weight, BF16), ("v", weight, BF16), ("h", (2,) + weight, BF16), f("v", 4, LANES), ("h", full, F32), f("v", z.total, 128), ("h", full, F32)],
        [[(a.shape, F32) for a in params], ((2,) + weight, BF16), (full, F32), ((4, C), F32), (half, F32)],
        14,
    )(*params, *(v.reshape(1, C) for v in (gain_first, bias_first, gain_second, bias_second)), x)

    hidden, h_above, h_below, stats_one, copies = call(
        body(first_kernel),
        "vvvvvv",
        [("v", full, F32), f("v", 3 * r, LANES), f("v", 3 * r, LANES), f("v", 2, LANES), ("V", pair, F32)],
        [z.pads(), z.chains(4)],
    )(x, above, below, gathered, affine, w1)
    gathered = exchange(copies, AXES)
    extended, near_rows = z.total + 4 * r, z.total + 2 * r
    left_one, packed, teachers, spread_u, near_u = call(
        body(first_operand_kernel),
        "vvvvvvvvvhh",
        [("h", left, BF16), f("h", C, BACK_LANES), f("h", extended, LANES), f("h", near_rows, LANES), f("h", near_rows, LANES)],
        [
            z.pads(), z.chains(2), (left, BF16), (weight, BF16), ((near_rows, LANES), F32), ((extended, 128), F32),
            ((extended, LANES), F32), ((near_rows, LANES), F32), ((C, BACK_LANES), F32),
        ],
        7,
    )(x, hidden, h_above, h_below, above, below, stats_one, affine, teacher, upstream, weights)
    gathered, near_u = lax.optimization_barrier((gathered, near_u))

    map_shape = (peers * z.slots, 128)
    out, o_above, o_below, near, stats_two, copies = call(
        body(second_kernel),
        "vvvvvvvvvv",
        [("v", full, F32), f("v", 2 * r, LANES), f("v", 2 * r, LANES), f("v", 2, r, LANES), f("v", 2, LANES), ("V", map_shape, F32)],
        [z.pads(), z.chains(3)],
    )(hidden, h_above, h_below, gathered, affine, w2, x, above, below, teacher)
    gathered = exchange(copies, ("row",))
    out_copy, hidden_copy, left_two, shifts, by_map, by_teacher, up = call(
        body(second_operand_kernel),
        "vvvvvvvhhhh",
        [
            ("h", full, F32), f("h", near_rows, LANES), ("v", left, BF16), f("h", 3, near_rows, LANES),
            f("v", near_rows, LANES), f("v", near_rows, LANES), f("v", near_rows, LANES),
        ],
        [
            z.pads(), z.chains(2), ((extended, LANES), F32), ((near_rows, LANES), F32), (weight, BF16),
            ((3, near_rows, LANES), F32),
        ],
        11,
    )(hidden, near, stats_two, affine, out, o_above, o_below, teachers, spread_u, near_u, weights)

    dout, dshift, d_above, d_below, slabs = call(
        body(upstream_kernel),
        "vvhhvhvvhv",
        [("v", full, F32), ("v", full, F32), f("v", r, LANES), f("v", r, LANES), f("V", devices, 1, BACK_LANES)],
        [((3, near_rows, LANES), F32), (left, BF16), (full, F32), ((C, BACK_LANES), F32), z.pads(), z.pads()],
        4,
    )(gathered, up, shifts, left_one, left_two, packed, by_map, by_teacher, hidden_copy, stats_two)
    gathered = exchange(slabs, AXES)
    out_s, out_l, first_normed, second_normed, weight_back = call(
        body(write_kernel),
        "hhhhvvv",
        [("v", image_small.shape, F32), ("v", image_large.shape, F32), ("v", full, F32), f("v", near_rows, LANES), ("v", weight, BF16)],
        [(full, F32), (full, F32), ((near_rows, LANES), F32), (half, F32)],
        4,
    )(out_copy, x_copy, hidden_copy, weights, stats_one, stats_two, d_above)

    pre, gain_two, bias_two, slabs = call(
        body(hidden_kernel),
        "vvvvvvvvv",
        [("v", full, F32), f("v", 1, C), f("v", 1, C), f("V", devices, 1, LAST_LANES)],
        [z.pads()],
    )(gathered, dshift, d_above, d_below, second_normed, stats_two, affine, weight_back, first_normed)
    gathered = exchange(slabs, AXES)

    back_s, back_l, one, two, gain_one, bias_one = call(
        body(back_kernel),
        "vvvvvv",
        [("v", a.shape, F32) for a in (image_small, image_large, conv_first, conv_second)] + [f("v", 1, C), f("v", 1, C)],
        [(half, F32), ((C, LAST_LANES), F32)],
    )(gathered, pre, first_normed, stats_one, affine, dout)
    return (
        out_s, out_l, back_s, back_l,
        one, gain_one.reshape(C), bias_one.reshape(C),
        two, gain_two.reshape(C), bias_two.reshape(C),
    )


def solution(mesh):
    split_bands, everywhere = P("img", "row", None), P()
    return jax.shard_map(
        local,
        mesh=mesh,
        in_specs=(split_bands,) * 6 + (everywhere,) * 6,
        out_specs=(split_bands,) * 4 + (everywhere,) * 6,
        check_vma=False,
    )
```

```python
import functools
import math

import jax
import jax.numpy as jnp
from jax import lax
from jax.experimental import pallas as pl
from jax.experimental.pallas import tpu as pltpu
from jax.sharding import PartitionSpec as P

C = 32
HS = 32
HL = 64
HEIGHTS = (HS, HL)

norm_eps = 1e-05
map_eps = 1e-06
beta_weight = 1000.0
AXES = ("img", "row")
BLOCK = 8
LANES = BLOCK * C
TAPS = 3
DEPTH = TAPS * 128 + 256
TAP_ROWS = 128 + 2 * C
REACH = 4
ROOT = math.sqrt(2.0 / math.pi)
CUBE = 0.044715
F32 = jnp.float32
BF16 = jnp.bfloat16
VMEM_LIMIT = 32 * 1024 * 1024
BIAS, GAIN, SECOND, LEFT, HIDDEN, ONES = 0, 1, 2, 11, 20, 29
BACK_LANES = 1280
LAST_SECOND, LAST_FIRST, LAST_LANES = 2, 11, 640


class Sizes:
    def __init__(self, small, large, devices, peers):
        self.images = (small[0], large[0])
        self.rows = (small[1], large[1])
        self.blocks = (HS // BLOCK, HL // BLOCK)
        self.step = tuple(n * r for n, r in zip(self.images, self.rows))
        self.count = tuple(b * s for b, s in zip(self.blocks, self.step))
        self.edge = tuple(b * n for b, n in zip(self.blocks, self.images))
        self.start = (self.count[1], 0)
        self.rim = (self.edge[1], 0)
        self.total = sum(self.count)
        self.rims = sum(self.edge)
        self.slots = -(-sum(self.images) // 8) * 8
        self.guard = -(-max(self.images) // 8) * 8
        self.devices = devices
        self.peers = peers
        self.here = float(self.total * BLOCK)
        self.pixels = self.here * devices

    def pads(self):
        return [((TAPS, 2, self.count[k] + 2 * self.step[k], 128), F32) for k in (0, 1)]

    def chains(self, depth):
        return [((2, 2 * self.guard + (depth + 1) * self.rims, 128), F32)] * 2


def split(value):
    high = value.astype(BF16)
    return high, (value - high.astype(F32)).astype(BF16)


def dot(left, right):
    return lax.dot_general(left, right, (((1,), (0,)), ((), ())), preferred_element_type=F32)


def product(left, right):
    if left[0].shape[1] % 128:
        return dot(left[0], right[0]) + (dot(left[0], right[1]) + dot(left[1], right[0]))
    return dot(
        jnp.concatenate([left[0], left[0], left[1]], axis=1), jnp.concatenate([right[0], right[1], right[0]], axis=0)
    )


def spread(left, right):
    right = right.astype(BF16)
    return dot(jnp.concatenate(split(left), axis=1), jnp.concatenate([right, right], axis=0))


def gelu(s):
    return 0.5 * s * (1.0 + jnp.tanh(ROOT * (s + CUBE * s * s * s)))


def gelu_slope(s):
    square = s * s
    t = jnp.tanh(ROOT * s * (1.0 + CUBE * square))
    return 0.5 * (1.0 + t) + 0.5 * s * (1.0 - t * t) * ROOT * (1.0 + 3.0 * CUBE * square)


def spread_groups(row):
    row = row + pltpu.roll(row, 64, 1)
    return row + pltpu.roll(row, 32, 1)


def fold(row):
    return spread_groups(row[:, :128] + row[:, 128:])


def wide(row):
    return jnp.concatenate([row, row], axis=1)


def group_of(rows=1, lanes=128):
    return lax.broadcasted_iota(jnp.int32, (rows, lanes), 1) // C


def column_sum(value):
    return jnp.sum(value, axis=0, keepdims=True)


def send_lines(z, ref, lines):
    for n, line in enumerate(lines):
        ref[pl.ds(n, z.devices, stride=len(lines)), :] = jnp.broadcast_to(line, (z.devices, 128))


def moments(z, value, ref):
    few = min(8, z.total)
    pivot = fold(column_sum(value[:few])) / float(few * BLOCK)
    off = value - wide(pivot)
    first, second = fold(column_sum(off)), fold(column_sum(off * off))
    send_lines(z, ref, [pivot + first / z.here, second - first * first / z.here])


def merged(z, ref):
    means = ref[pl.ds(0, z.devices, stride=2), :]
    center = jnp.mean(means, axis=0, keepdims=True)
    off = means - center
    within = jnp.mean(ref[pl.ds(1, z.devices, stride=2), :], axis=0, keepdims=True)
    variance = within / z.here + jnp.mean(off * off, axis=0, keepdims=True)
    return wide(center), wide(lax.rsqrt(variance + norm_eps))


def put_halves(ref, value):
    ref[0] = value[:, :128]
    ref[1] = value[:, 128:]


def whole(ref):
    return jnp.concatenate([ref[0], ref[1]], axis=1)


def to_matrix(z, refs, half):
    for k in (0, 1):
        for j in range(z.blocks[k]):
            at = z.start[k] + j * z.step[k]
            for i in range(z.images[k]):
                for h in (0, 1):
                    half[h, pl.ds(at + i * z.rows[k], z.rows[k]), :] = refs[k][i, :, pl.ds(LANES * j + 128 * h, 128)]


def from_matrix(z, half, refs):
    for k in (0, 1):
        for j in range(z.blocks[k]):
            at = z.start[k] + j * z.step[k]
            for i in range(z.images[k]):
                for h in (0, 1):
                    refs[k][i, :, pl.ds(LANES * j + 128 * h, 128)] = half[h, pl.ds(at + i * z.rows[k], z.rows[k]), :]


def take_rims(z, half, depth, bottom, top):
    for k in (0, 1):
        for d in range(1, depth + 1):
            to_bottom = pl.ds((depth - d) * z.rims + z.rim[k], z.edge[k])
            to_top = pl.ds((d - 1) * z.rims + z.rim[k], z.edge[k])
            if d <= z.rows[k]:
                bottom[to_bottom, :] = half[pl.ds(z.start[k] + z.rows[k] - d, z.edge[k], stride=z.rows[k]), :]
                top[to_top, :] = half[pl.ds(z.start[k] + d - 1, z.edge[k], stride=z.rows[k]), :]
            else:
                bottom[to_bottom, :] = jnp.zeros((z.edge[k], 128), F32)
                top[to_top, :] = jnp.zeros((z.edge[k], 128), F32)


def inside(z, depth, above):
    at = lax.axis_index("row")
    large = lax.broadcasted_iota(jnp.int32, (z.rims, 1), 0) < z.rim[0]
    parts = []
    for n in range(depth):
        if above:
            ok = [jnp.where(at * rows >= depth - n, 1.0, 0.0) for rows in z.rows]
        else:
            ok = [jnp.where((at + 1) * rows + n + 1 <= height, 1.0, 0.0) for rows, height in zip(z.rows, HEIGHTS)]
        parts.append(jnp.where(large, ok[1], ok[0]).astype(F32))
    return jnp.concatenate(parts, axis=0)


def clear_guards(z, pads, a):
    for k in (0, 1):
        pads[k][a, 1, pl.ds(0, z.step[k]), :] = jnp.zeros((z.step[k], 128), F32)
        pads[k][a, 0, pl.ds(z.step[k] + z.count[k], z.step[k]), :] = jnp.zeros((z.step[k], 128), F32)


def fill_center(z, pads, value):
    clear_guards(z, pads, 1)
    for k in (0, 1):
        for h in (0, 1):
            pads[k][1, h, pl.ds(z.step[k], z.count[k]), :] = value[z.start[k] : z.start[k] + z.count[k], 128 * h : 128 * h + 128]


def fill_shifted(z, pads, above, below):
    for k in (0, 1):
        ref, step, count, rows = pads[k], z.step[k], z.count[k], z.rows[k]
        rim = slice(z.rim[k], z.rim[k] + z.edge[k])
        for h in (0, 1):
            lanes = slice(128 * h, 128 * h + 128)
            ref[0, h, pl.ds(step, count), :] = ref[1, h, pl.ds(step - 1, count), :]
            ref[2, h, pl.ds(step, count), :] = ref[1, h, pl.ds(step + 1, count), :]
            ref[0, h, pl.ds(step, z.edge[k], stride=rows), :] = above[rim, lanes]
            ref[2, h, pl.ds(step + rows - 1, z.edge[k], stride=rows), :] = below[rim, lanes]


def fill_pads(z, pads, value, above, below):
    fill_center(z, pads, value)
    fill_shifted(z, pads, above, below)
    for a in (0, 2):
        clear_guards(z, pads, a)


def beside(left, right):
    lane = lax.broadcasted_iota(jnp.int32, (1, 128), 1)
    middle = pltpu.roll(jnp.where(lane >= 64, left[1], right[1]), 64, 1)
    return [
        jnp.where(lane >= 96, left[0], jnp.where(lane < 32, right[0], middle)),
        jnp.where(lane >= 96, left[2], jnp.where(lane < 32, right[2], 0.0)),
    ]


def band_operand(z, pads):
    parts = ([], [])
    for k in (1, 0):
        ref, step, count = pads[k], z.step[k], z.count[k]
        low, high = ([ref[a, h, pl.ds(step, count), :] for a in range(TAPS)] for h in (0, 1))
        before = [ref[a, 1, pl.ds(0, count), :] for a in range(TAPS)]
        after = [ref[a, 0, pl.ds(2 * step, count), :] for a in range(TAPS)]
        parts[0].append(jnp.concatenate(low + beside(before, high), axis=1))
        parts[1].append(jnp.concatenate(high + beside(low, after), axis=1))
    return [jnp.concatenate(part, axis=0) for part in parts]


def rim_operand(z, chain, depth):
    m = lax.broadcasted_iota(jnp.int32, (z.rims, 1), 0)
    large = m < z.rim[0]
    has_before = jnp.where(large, m, m - z.rim[0]) >= jnp.where(large, z.images[1], z.images[0])
    has_after = m < jnp.where(large, z.rim[0] - z.images[1], z.rims - z.images[0])
    low, high, before, after = [], [], [], []
    for r in range(depth + 1):
        at = z.guard + r * z.rims
        low.append(chain[0, pl.ds(at, z.rims), :])
        high.append(chain[1, pl.ds(at, z.rims), :])
        shifted = [chain[1, pl.ds(at - images, z.rims), :] for images in z.images]
        before.append(jnp.where(has_before, jnp.where(large, shifted[1], shifted[0]), 0.0))
        shifted = [chain[0, pl.ds(at + images, z.rims), :] for images in z.images]
        after.append(jnp.where(has_after, jnp.where(large, shifted[1], shifted[0]), 0.0))
    parts = ([], [])
    for n in range(depth - 1):
        rows = slice(n, n + TAPS)
        parts[0].append(jnp.concatenate(low[rows] + beside(before[rows], high[rows]), axis=1))
        parts[1].append(jnp.concatenate(high[rows] + beside(low[rows], after[rows]), axis=1))
    return [jnp.concatenate(part, axis=0) for part in parts]


def times(parts, weight):
    left = jnp.concatenate([part[h] for h in (0, 1) for part in parts], axis=0)
    both = jnp.concatenate([weight_matrix(weight.at[0]), weight_matrix(weight.at[1])], axis=1)
    result = dot(jnp.concatenate(split(left), axis=1), jnp.concatenate([both, both], axis=0))
    result = result[:, :128] + result[:, 128:]
    rows = result.shape[0] // 2
    return jnp.concatenate([result[:rows], result[rows:]], axis=1)


def convolve(z, own, above, below, depth, pads, chains, weight):
    r = z.rims
    fill_pads(z, pads, own, above[(depth - 1) * r :], below[:r])
    parts = [band_operand(z, pads)]
    if depth > 1:
        for side, (rim, chain) in enumerate(zip((above, below), chains)):
            rim_at, own_at = (z.guard, z.guard + depth * r) if side == 0 else (z.guard + r, z.guard)
            for h in (0, 1):
                chain[h, pl.ds(rim_at, depth * r), :] = rim[:, 128 * h : 128 * h + 128]
                for k in (0, 1):
                    row = z.step[k] + (0 if side == 0 else z.rows[k] - 1)
                    chain[h, pl.ds(own_at + z.rim[k], z.edge[k]), :] = pads[k][1, h, pl.ds(row, z.edge[k], stride=z.rows[k]), :]
            parts.append(rim_operand(z, chain, depth))
    result = times(parts, weight)
    n = z.total + (depth - 1) * r
    return result[: z.total], result[z.total : n], result[n:]


def image_sums(z, value):
    slot = lax.broadcasted_iota(jnp.int32, (z.slots, 1), 0)
    sums = jnp.zeros((z.slots, 128), F32)
    for k in (0, 1):
        line = value[z.start[k] : z.start[k] + z.step[k]]
        for j in range(1, z.blocks[k]):
            at = z.start[k] + j * z.step[k]
            line = line + value[at : at + z.step[k]]
        image = lax.broadcasted_iota(jnp.int32, (z.step[k], 1), 0) // z.rows[k]
        for i in range(z.images[k]):
            sums = jnp.where(slot == i + k * z.images[0], column_sum(jnp.where(image == i, line, 0.0)), sums)
    return sums


def image_rows(z, values, rims):
    parts = []
    for k in (1, 0):
        image = lax.broadcasted_iota(jnp.int32, (z.step[k], 1), 0) // z.rows[k]
        line = jnp.zeros((z.step[k], 128), F32)
        for i in range(z.images[k]):
            at = i + k * z.images[0]
            line = jnp.where(image == i, values[at : at + 1], line)
        parts += [line] * z.blocks[k]
    if rims:
        m = lax.broadcasted_iota(jnp.int32, (z.rims, 1), 0)
        image = jnp.where(m < z.rim[0], z.images[0] + m % z.images[1], (m - z.rim[0]) % z.images[0])
        line = jnp.zeros((z.rims, 128), F32)
        for at in range(sum(z.images)):
            line = jnp.where(image == at, values[at : at + 1], line)
        parts += [line] * rims
    return jnp.concatenate(parts, axis=0)


def channel_mean():
    a = lax.broadcasted_iota(jnp.int32, (LANES, 128), 0) // C
    b = lax.broadcasted_iota(jnp.int32, (LANES, 128), 1) % 64
    return jnp.where(a == b, 1.0 / C, 0.0).astype(F32)


def to_channels():
    a = lax.broadcasted_iota(jnp.int32, (128, LANES), 0)
    b = lax.broadcasted_iota(jnp.int32, (128, LANES), 1) // C
    return jnp.where(a == b, 1.0, 0.0).astype(F32)


def attention(value):
    return spread(value * value, channel_mean())


def start_all(copies):
    for copy in copies:
        copy.start()


def wait_all(copies):
    for copy in copies:
        copy.wait()


def start_kernel(z, small, large, up_s, up_l, t_s, t_l, x, bottom, top, copies, raw, half, sems):
    loads = [pltpu.make_async_copy(a, b, sems.at[n]) for n, (a, b) in enumerate(zip((small, large, up_s, up_l, t_s, t_l), raw))]
    start_all(loads)
    r, n = z.rims, REACH * z.rims
    tail = n + 2 * r
    for ref in (bottom, top):
        ref[pl.ds(tail, z.slots), :] = jnp.zeros((z.slots, LANES), F32)
    wait_all(loads[:2])
    to_matrix(z, raw[:2], half)
    value = whole(half)
    x[...] = value
    moments(z, value, copies)
    for h in (0, 1):
        lanes = pl.ds(128 * h, 128)
        take_rims(z, half.at[h], REACH, bottom.at[pl.ds(0, n), lanes], top.at[pl.ds(0, n), lanes])
    wait_all(loads[2:])
    for k in (0, 1):
        width, rows = HEIGHTS[k], z.rows[k]
        for i in range(z.images[k]):
            slot = pl.ds(tail + i + k * z.images[0], 1)
            for d in (0, 1):
                to_bottom, to_top = n + (1 - d) * r + z.rim[k] + i, n + d * r + z.rim[k] + i
                for j in range(z.blocks[k]):
                    lanes, at = pl.ds(LANES * j, LANES), j * z.images[k]
                    if d < rows:
                        bottom[pl.ds(to_bottom + at, 1), :] = raw[2 + k][i, pl.ds(rows - 1 - d, 1), lanes]
                        top[pl.ds(to_top + at, 1), :] = raw[2 + k][i, pl.ds(d, 1), lanes]
                    else:
                        bottom[pl.ds(to_bottom + at, 1), :] = jnp.zeros((1, LANES), F32)
                        top[pl.ds(to_top + at, 1), :] = jnp.zeros((1, LANES), F32)
                if d < rows:
                    bottom[slot, pl.ds(128 * (1 - d), width)] = raw[4 + k][i, pl.ds(rows - 1 - d, 1), :]
                    top[slot, pl.ds(128 * d, width)] = raw[4 + k][i, pl.ds(d, 1), :]


def banded(taps, ref):
    row = lax.broadcasted_iota(jnp.int32, (128, 128), 0) // C
    lane = group_of(128)
    for a in range(TAPS):
        main = jnp.zeros((128, 128), F32)
        for b in range(TAPS):
            main = jnp.where(row - lane + 1 == b, taps[a][b], main)
        before = jnp.where(lane[:C] == 0, taps[a][0][:C], 0.0)
        after = jnp.where(lane[:C] == 3, taps[a][2][:C], 0.0)
        for n, part in enumerate(split(jnp.concatenate([main, before, after], axis=0))):
            ref[n, pl.ds(a * TAP_ROWS, TAP_ROWS), :] = part


def weight_matrix(ref):
    main = [ref[pl.ds(a * TAP_ROWS, 128), :] for a in range(TAPS)]
    before, after = ([ref[pl.ds(a * TAP_ROWS + 128 + n * C, C), :] for a in range(TAPS)] for n in (0, 1))
    return jnp.concatenate(
        main + [after[0], before[1], after[1], before[0], after[2], jnp.zeros((2 * C, 128), BF16), before[2]], axis=0
    )


def prepare_kernel(z, first, second, up_s, up_l, t_s, t_l, g1, b1, g2, b2, x, w1, w2, weights, affine, upstream, teacher, x_copy, raw, kept, kept_u, rows, half, sems):
    targets = tuple(raw) + tuple(rows.at[pl.ds(n, 1), :] for n in range(4))
    refs = (first, second, up_s, up_l, t_s, t_l, g1, b1, g2, b2)
    loads = [pltpu.make_async_copy(a, b, sems.at[n]) for n, (a, b) in enumerate(zip(refs, targets))]
    start_all(loads)
    stores = [pltpu.make_async_copy(x, x_copy, sems.at[13])]
    stores[0].start()
    wait_all(loads)
    to_matrix(z, raw[2:4], half)
    kept_u[...] = whole(half)
    stores.append(pltpu.make_async_copy(kept_u, upstream, sems.at[10]))
    stores[1].start()
    for n, (source, forward) in enumerate(zip(raw[:2], (w1, w2))):
        tiles = []
        for a in range(TAPS):
            line = [jnp.concatenate([source[a, b]] * 4, axis=1) for b in range(TAPS)]
            tiles.append([jnp.concatenate([tap] * 4, axis=0) for tap in line])
        turned = [[tiles[TAPS - 1 - a][TAPS - 1 - b].T for b in range(TAPS)] for a in range(TAPS)]
        banded(tiles, forward)
        banded(turned, kept.at[n])
        stores.append(pltpu.make_async_copy(kept.at[n], weights.at[n], sems.at[11 + n]))
        stores[-1].start()
    affine[...] = jnp.concatenate([rows[...]] * BLOCK, axis=1)
    teacher[...] = jnp.zeros(teacher.shape, F32)
    for k, ref in ((0, raw[4]), (1, raw[5])):
        for i in range(z.images[k]):
            line = ref[i]
            for j in range(z.blocks[k]):
                at = z.start[k] + j * z.step[k] + i * z.rows[k]
                for lane in (0, 64):
                    teacher[pl.ds(at, z.rows[k]), pl.ds(lane, BLOCK)] = line[:, j * BLOCK : (j + 1) * BLOCK]
    wait_all(stores)


def normed_by(stats):
    return lambda v: (v - stats[0:1]) * stats[1:2]


def activation(center, scale, gain, bias):
    factor = scale * gain
    offset = bias - center * factor
    return lambda v: gelu(v * factor + offset)


def first_kernel(z, x, above, below, gathered, affine, weight, hidden, h_above, h_below, stats, copies, pads, chains):
    n = REACH * z.rims
    center, scale = merged(z, gathered)
    act = activation(center, scale, affine[0:1], affine[1:2])
    own = act(x[...])
    up, down = act(above[pl.ds(0, n), :]) * inside(z, 4, True), act(below[pl.ds(0, n), :]) * inside(z, 4, False)
    own, up, down = convolve(z, own, up, down, 4, pads, chains, weight)
    moments(z, own, copies)
    hidden[...] = own
    h_above[...] = up
    h_below[...] = down
    stats[0:1] = center
    stats[1:2] = scale


def second_kernel(z, hidden, h_above, h_below, gathered, affine, weight, x, x_above, x_below, teacher, out, o_above, o_below, near, stats, copies, pads, chains):
    center, scale = merged(z, gathered)
    act = activation(center, scale, affine[2:3], affine[3:4])
    r = z.rims
    own = act(hidden[...])
    up, down = act(h_above[...]) * inside(z, 3, True), act(h_below[...]) * inside(z, 3, False)
    own, up, down = convolve(z, own, up, down, 3, pads, chains, weight)
    own = x[...] + own
    amap = attention(own)
    lane = lax.broadcasted_iota(jnp.int32, (1, 128), 1)
    sums = image_sums(z, amap * jnp.where(lane < 64, amap, teacher[...]))
    copies[...] = jnp.concatenate([sums] * z.peers, axis=0)
    out[...] = own
    o_above[...] = x_above[pl.ds(2 * r, 2 * r), :] + up
    o_below[...] = x_below[pl.ds(0, 2 * r), :] + down
    near[0] = h_above[pl.ds(2 * r, r), :]
    near[1] = h_below[pl.ds(0, r), :]
    stats[0:1] = center
    stats[1:2] = scale


def tap_rows(q):
    return 128 + 3 * C if q < 0 else 128 if q == 4 else q * C


def tap_product(z, operand, own, above, below, pads):
    fill_center(z, pads, own)
    fill_shifted(z, pads, above, below)
    columns = []
    for a in range(TAPS):
        columns.append(
            jnp.concatenate([pads[k][TAPS - 1 - a, h, pl.ds(z.step[k], z.count[k]), :] for h in (0, 1) for k in (1, 0)], axis=0)
        )
    return product(operand, split(jnp.concatenate(columns, axis=1)))


def tap_sums(result, tiles, first_group):
    group = group_of()
    for a in range(TAPS):
        for b in range(TAPS):
            total = None
            for p in range(4):
                at = tap_rows(p + b - 1)
                part = result[at : at + C, 128 * a : 128 * a + 128]
                total = part if total is None else jnp.where(group == p, part, total)
            tile, slot = divmod(first_group + a * TAPS + b, 4)
            tiles[tile] = jnp.where(group == slot, spread_groups(total), tiles[tile])


def tap_counts(z, turned, tiles, first_group):
    group = group_of()
    m = lax.broadcasted_iota(jnp.int32, (1, 2 * z.total), 1) % z.total
    row = jnp.where(m < z.start[0], m % z.rows[1], (m - z.start[0]) % z.rows[0])
    height = jnp.where(m < z.start[0], z.rows[1], z.rows[0])
    at = lax.axis_index("row")
    lost = {
        0: (row == height - 1) & (at == z.peers - 1),
        2: (row == 0) & (at == 0),
    }
    for a in range(TAPS):
        column = jnp.sum(jnp.where(lost[a], 0.0, turned) if a in lost else turned, axis=1, keepdims=True)
        for b in range(TAPS):
            total = sum(column[tap_rows(p + b - 1) : tap_rows(p + b - 1) + C] for p in range(4))
            tile, slot = divmod(first_group + a * TAPS + b, 4)
            tiles[tile] = jnp.where(group == slot, total, tiles[tile])


def turned_operand(z, value, pads, kept):
    fill_center(z, pads, value)
    lane = lax.broadcasted_iota(jnp.int32, (1, 128), 1)
    halves = ([], [])
    for k in (1, 0):
        ref, step, count = pads[k], z.step[k], z.count[k]
        low, high = ref[1, 0, pl.ds(step, count), :], ref[1, 1, pl.ds(step, count), :]
        before, after = ref[1, 1, pl.ds(0, count), :], ref[1, 0, pl.ds(2 * step, count), :]
        for part, main, left, right in ((halves[0], low, before, high), (halves[1], high, low, after)):
            part.append(jnp.concatenate([main, jnp.where(lane >= 96, left, jnp.where(lane < 32, right, 0.0))], axis=1))
    turned = jnp.concatenate(halves[0] + halves[1], axis=0).T
    parts = split(turned)
    for n in (0, 1):
        kept[n] = parts[n]
    return turned


def first_operand_kernel(z, x, hidden, h_above, h_below, above, below, stats, affine, teacher, upstream, weights, left, packed, teachers, spread_u, near_u, pads, chains, kept, kept_w, kept_u, pixels, kept_t, kept_c, kept_packed, sems):
    r, own = z.rims, pl.ds(0, z.total)
    loads = [pltpu.make_async_copy(upstream, kept_u.at[own, :], sems.at[0]), pltpu.make_async_copy(weights.at[1], kept_w, sems.at[1])]
    start_all(loads)
    act = activation(stats[0:1], stats[1:2], affine[0:1], affine[1:2])
    value = turned_operand(z, act(x[...]), pads, kept)
    stores = [pltpu.make_async_copy(kept, left, sems.at[2])]
    stores[0].start()
    tiles = [jnp.zeros((C, 128), F32) for _ in range(BACK_LANES // 128)]
    tap_counts(z, value, tiles, ONES)
    result = tap_product(
        z, (kept[0], kept[1]), hidden[...], h_above[pl.ds(2 * r, r), :] * inside(z, 1, True), h_below[pl.ds(0, r), :] * inside(z, 1, False), pads
    )
    tap_sums(result, tiles, HIDDEN)
    kept_packed[...] = jnp.concatenate(tiles, axis=1)
    stores.append(pltpu.make_async_copy(kept_packed, packed, sems.at[6]))
    stores[1].start()
    pixels[own, :] = teacher[...]
    pixels[pl.ds(z.total, 4 * r), :] = jnp.zeros((4 * r, 128), F32)
    n = (REACH + 2) * r
    for side, ref in enumerate((above, below)):
        for d in (0, 1):
            for k in (0, 1):
                line = ref[pl.ds(n + k * z.images[0], z.images[k]), pl.ds(128 * d, 128)]
                for j in range(z.blocks[k]):
                    at = z.total + (2 * side + d) * r + z.rim[k] + j * z.images[k]
                    pixels[pl.ds(at, z.images[k]), pl.ds(0, BLOCK)] = line[:, j * BLOCK : (j + 1) * BLOCK]
    kept_t[...] = spread(pixels[...], to_channels())
    stores.append(pltpu.make_async_copy(kept_t, teachers, sems.at[3]))
    stores[2].start()
    n = REACH * r
    up, down = above[pl.ds(n, 2 * r), :] * inside(z, 2, True), below[pl.ds(n, 2 * r), :] * inside(z, 2, False)
    kept_u[pl.ds(z.total, r), :] = up[r:]
    kept_u[pl.ds(z.total + r, r), :] = down[:r]
    wait_all(loads)
    stores.append(pltpu.make_async_copy(kept_u, near_u, sems.at[5]))
    stores[3].start()
    kept_c[...] = jnp.concatenate(convolve(z, kept_u[own, :], up, down, 2, pads, chains, kept_w), axis=0)
    stores.append(pltpu.make_async_copy(kept_c, spread_u, sems.at[4]))
    stores[4].start()
    wait_all(stores)


def second_operand_kernel(z, hidden, near, stats, affine, out, o_above, o_below, teachers, spread_u, near_u, weights, out_copy, hidden_copy, left, shifts, by_map, by_teacher, up, pads, chains, kept_t, kept_u, kept_w, kept_s, sems):
    r, total = z.rims, z.total
    loads = [
        pltpu.make_async_copy(teachers, kept_t, sems.at[0]),
        pltpu.make_async_copy(weights.at[1], kept_w, sems.at[1]),
        pltpu.make_async_copy(spread_u, kept_u, sems.at[2]),
    ]
    start_all(loads)
    stores = [
        pltpu.make_async_copy(out, out_copy, sems.at[4]),
        pltpu.make_async_copy(hidden, hidden_copy.at[pl.ds(0, total), :], sems.at[7]),
        pltpu.make_async_copy(near.at[0], hidden_copy.at[pl.ds(total, r), :], sems.at[8]),
        pltpu.make_async_copy(near.at[1], hidden_copy.at[pl.ds(total + r, r), :], sems.at[9]),
        pltpu.make_async_copy(near_u, up, sems.at[10]),
    ]
    start_all(stores)
    normed = normed_by(stats)(jnp.concatenate([hidden[...], near[0], near[1]], axis=0))
    shifted = normed * affine[2:3] + affine[3:4]
    turned_operand(z, gelu(shifted[:total]), pads, left)
    ones = jnp.ones((total, 1), F32)
    masks = jnp.concatenate([ones, inside(z, 1, True), inside(z, 1, False)], axis=0)
    slopes = gelu_slope(shifted) * masks
    o = jnp.concatenate([out[...], o_above[...] * inside(z, 2, True), o_below[...] * inside(z, 2, False)], axis=0)
    for_map = spread(attention(o), to_channels()) * o
    wait_all(loads)
    for_teacher = kept_t[...] * o
    kept_s[0] = kept_u[...] * slopes
    for n, value, ref in ((1, for_map, by_map), (2, for_teacher, by_teacher)):
        own, before, after = value[:total], value[total : total + 2 * r], value[total + 2 * r :]
        ref[...] = jnp.concatenate([own, before[r:], after[:r]], axis=0)
        kept_s[n] = jnp.concatenate(convolve(z, own, before, after, 2, pads, chains, kept_w), axis=0) * slopes
    stores.append(pltpu.make_async_copy(kept_s, shifts, sems.at[5]))
    stores[-1].start()
    wait_all(stores)


def upstream_kernel(z, gathered, up, shifts, left_1, left_2, packed, by_map, by_teacher, hidden, stats, dout, dshift, d_above, d_below, slabs, kept_s, kept_left, kept_h, kept_packed, pads, more_pads, sems):
    r, total = z.rims, z.total
    loads = [
        pltpu.make_async_copy(a, b, sems.at[n])
        for n, (a, b) in enumerate(((shifts, kept_s), (left_1, kept_left), (hidden.at[pl.ds(0, total), :], kept_h), (packed, kept_packed)))
    ]
    start_all(loads)
    lane = lax.broadcasted_iota(jnp.int32, (z.slots, 128), 1)
    sums = sum(gathered[pl.ds(n * z.slots, z.slots), :] for n in range(z.peers))
    square = jnp.sum(jnp.where(lane < 64, sums, 0.0), axis=1, keepdims=True)
    cross = jnp.sum(jnp.where(lane < 64, 0.0, sums), axis=1, keepdims=True)
    inverse = lax.rsqrt(square + map_eps)
    inner = beta_weight * (square * inverse - cross) * inverse
    shape = (z.slots, 128)
    for_map = (beta_weight - inner) * inverse * inverse * (2.0 / C)
    for_teacher = beta_weight * inverse * (2.0 / C)
    for_map, for_teacher = (wide(image_rows(z, jnp.broadcast_to(v, shape), 2)) for v in (for_map, for_teacher))
    value = up[...] + for_map * by_map[...] - for_teacher * by_teacher[...]
    dout[...] = value[:total]
    wait_all(loads[:2])
    shift = kept_s[0] + for_map * kept_s[1] - for_teacher * kept_s[2]
    pre, above, below = shift[:total], shift[total : total + r], shift[total + r :]
    dshift[...] = pre
    d_above[...] = above
    d_below[...] = below
    second = tap_product(z, (left_2[0], left_2[1]), value[:total], value[total : total + r], value[total + r :], pads)
    first = tap_product(z, (kept_left[0], kept_left[1]), pre, above, below, more_pads)
    wait_all(loads[2:])
    normed = normed_by(stats)(kept_h[...])
    tiles = [kept_packed[:, 128 * n : 128 * n + 128] for n in range(BACK_LANES // 128)]
    group = group_of()
    tiles[0] = jnp.where(group == BIAS, fold(column_sum(pre)), jnp.where(group == GAIN, fold(column_sum(pre * normed)), tiles[0]))
    tap_sums(second, tiles, SECOND)
    tap_sums(first, tiles, LEFT)
    line = jnp.concatenate(tiles, axis=1)
    for d in range(z.devices):
        slabs[d] = line[d % C : d % C + 1]


def write_kernel(z, out, x, hidden, weights, first_stats, stats, order, out_s, out_l, first_normed, normed, weight, kept, kept_x, kept_h, half, sems):
    loads = [pltpu.make_async_copy(a, b, sems.at[n]) for n, (a, b) in enumerate(((out, kept), (x, kept_x), (hidden, kept_h), (weights.at[0], weight)))]
    start_all(loads)
    loads[0].wait()
    put_halves(half, kept[...])
    from_matrix(z, half, (out_s, out_l))
    loads[1].wait()
    first_normed[...] = normed_by(first_stats)(kept_x[...])
    loads[2].wait()
    normed[...] = normed_by(stats)(kept_h[...])
    loads[3].wait()


def norm_sums(total):
    group = group_of()
    return [wide(spread_groups(jnp.where(group == n, total[:, :128], 0.0))) for n in (BIAS, GAIN)]


def hidden_kernel(z, gathered, dshift, d_above, d_below, second_normed, stats, affine, weight, first_normed, pre_ref, gain_out, bias_out, slabs, pads):
    total = jnp.sum(gathered[...], axis=0)
    bias_sum, gain_sum = norm_sums(total)
    bias_out[...] = bias_sum[:, :C]
    gain_out[...] = gain_sum[:, :C]
    bias_mean, gain_mean = bias_sum / z.pixels, gain_sum / z.pixels
    factor = affine[2:3] * stats[1:2]
    r, total_rows = z.rims, z.total

    def back(d, normed):
        return factor * (d - bias_mean - normed * gain_mean)

    own = back(dshift[...], second_normed[pl.ds(0, total_rows), :])
    up = back(d_above[...], second_normed[pl.ds(total_rows, r), :]) * inside(z, 1, True)
    down = back(d_below[...], second_normed[pl.ds(total_rows + r, r), :]) * inside(z, 1, False)
    grad, _, _ = convolve(z, own, up, down, 1, pads, None, weight)
    normed = first_normed[...]
    pre = grad * gelu_slope(normed * affine[0:1] + affine[1:2])
    pre_ref[...] = pre
    lane = lax.broadcasted_iota(jnp.int32, (1, 128), 1)
    taps = TAPS * TAPS * C

    def along(row):
        return jnp.concatenate([row[:, :128]] * 3, axis=1)[:, :taps]

    second, left, against, ones = (total[:, n * C : n * C + taps] for n in (SECOND, LEFT, HIDDEN, ONES))
    against = along(stats[1:2]) * (against - along(stats[0:1]) * ones)
    first = along(factor) * (left - along(bias_mean) * ones - along(gain_mean) * against)
    sums = jnp.where(lane < C, fold(column_sum(pre)), fold(column_sum(pre * normed)))
    line = jnp.concatenate([sums[:, : 2 * C], second, first], axis=1)
    slabs[...] = jnp.broadcast_to(line[None], slabs.shape)


def back_kernel(z, gathered, pre, normed, stats, affine, dout, back_s, back_l, one, two, gain_out, bias_out, half, lines):
    bias_sum, gain_sum = norm_sums(jnp.sum(gathered[:, :, pl.ds(0, 128)], axis=0))
    bias_out[...] = bias_sum[:, :C]
    gain_out[...] = gain_sum[:, :C]
    value = dout[...] + affine[0:1] * stats[1:2] * (pre[...] - bias_sum / z.pixels - normed[...] * (gain_sum / z.pixels))
    put_halves(half, value)
    from_matrix(z, half, (back_s, back_l))
    for d in range(C):
        lines[pl.ds(d, 1), :] = gathered[d]
    for ref, group in ((two, LAST_SECOND), (one, LAST_FIRST)):
        for a in range(TAPS):
            for b in range(TAPS):
                at = (group + a * TAPS + b) * C
                ref[a, b] = lines[:, pl.ds(at, C)]


def call(body, ins, outs, scratch=(), sems=0):
    space = {"v": pltpu.VMEM, "h": pltpu.HBM, "V": pltpu.VMEM}
    shapes = []
    for item in scratch:
        if isinstance(item, list):
            shapes.append([pltpu.VMEM(*s) for s in item])
        else:
            shapes.append(pltpu.VMEM(*item))
    if sems:
        shapes.append(pltpu.SemaphoreType.DMA((sems,)))
    run = pl.pallas_call(
        body,
        out_shape=[jax.ShapeDtypeStruct(shape, kind) if s == "v" else space[s](shape, kind) for s, shape, kind in outs],
        in_specs=[pl.BlockSpec(memory_space=space[s]) for s in ins],
        out_specs=[pl.BlockSpec(memory_space=space[s]) for s, _, _ in outs],
        scratch_shapes=shapes,
        compiler_params=pltpu.CompilerParams(vmem_limit_bytes=VMEM_LIMIT),
    )
    return lambda *args: run(
        *(pltpu.with_memory_space_constraint(arg, pltpu.HBM) if s == "h" else arg for s, arg in zip(ins, args))
    )


def exchange(lines, axes):
    shape = lines.shape
    if len(shape) == 2:
        lines = lines.reshape(math.prod(lax.axis_size(axis) for axis in axes), -1, 128)
    return lax.all_to_all(lines, axes, 0, 0, tiled=True).reshape(shape)


def beyond(z, bottom, top, depths):
    hops = max(-(-depth // rows) for rows in z.rows for depth in depths)
    above, below = [], []
    for hop in range(1, hops + 1):
        above.append(lax.ppermute(bottom, "row", [(i, i + hop) for i in range(z.peers - hop)]))
        below.append(lax.ppermute(top, "row", [(i + hop, i) for i in range(z.peers - hop)]))
    if hops == 1:
        return above[0], below[0]
    up, down = [], []
    base = 0
    for depth in depths:
        for n in range(depth):
            for k in (1, 0):
                hop, back = divmod(depth - 1 - n, z.rows[k])
                at = base + (depth - 1 - back) * z.rims + z.rim[k]
                up.append(above[hop][at : at + z.edge[k]])
                hop, back = divmod(n, z.rows[k])
                at = base + back * z.rims + z.rim[k]
                down.append(below[hop][at : at + z.edge[k]])
        base += depth * z.rims
    up.append(jnp.concatenate([pixel_rows(z, above, base, 1, 1), pixel_rows(z, above, base, 0, 1)], axis=1))
    down.append(jnp.concatenate([pixel_rows(z, below, base, 0, 0), pixel_rows(z, below, base, 1, 0)], axis=1))
    return jnp.concatenate(up, axis=0), jnp.concatenate(down, axis=0)


def pixel_rows(z, bands, base, distance, last):
    lines = []
    for k in (0, 1):
        hop, back = divmod(distance, z.rows[k])
        at = base + k * z.images[0]
        half = 128 * abs(last - back)
        lines.append(bands[hop][at : at + z.images[k], half : half + 128])
    lines.append(jnp.zeros((z.slots - sum(z.images), 128), F32))
    return jnp.concatenate(lines, axis=0)


def local(
    image_small, image_large, teacher_small, teacher_large, upstream_small, upstream_large,
    conv_first, gain_first, bias_first, conv_second, gain_second, bias_second,
):
    peers = lax.axis_size("row")
    devices = lax.axis_size("img") * peers
    z = Sizes(image_small.shape, image_large.shape, devices, peers)
    body = lambda function: functools.partial(function, z)
    r = z.rims
    full, half, pair = (z.total, LANES), (2, z.total, 128), (2 * devices, 128)
    weight, left = (2, TAPS * TAP_ROWS, 128), (2, 256, 2 * z.total)
    images = [image_small, image_large, upstream_small, upstream_large, teacher_small, teacher_large]
    f = lambda space, *shape: (space, shape, F32)
    depths = (REACH, 2)
    rim_rows = sum(depths) * r + z.slots

    x, bottom, top, copies = call(
        body(start_kernel),
        "hhhhhh",
        [("v", full, F32), f("v", rim_rows, LANES), f("v", rim_rows, LANES), ("V", pair, F32)],
        [[(a.shape, F32) for a in images], (half, F32)],
        6,
    )(*images)
    gathered = exchange(copies, AXES)
    above, below = beyond(z, bottom, top, depths)
    params = [conv_first, conv_second] + images[2:]
    w1, w2, weights, affine, upstream, teacher, x_copy = call(
        body(prepare_kernel),
        "hhhhhhhhhhv",
        [("v", weight, BF16), ("v", weight, BF16), ("h", (2,) + weight, BF16), f("v", 4, LANES), ("h", full, F32), f("v", z.total, 128), ("h", full, F32)],
        [[(a.shape, F32) for a in params], ((2,) + weight, BF16), (full, F32), ((4, C), F32), (half, F32)],
        14,
    )(*params, *(v.reshape(1, C) for v in (gain_first, bias_first, gain_second, bias_second)), x)

    hidden, h_above, h_below, stats_one, copies = call(
        body(first_kernel),
        "vvvvvv",
        [("v", full, F32), f("v", 3 * r, LANES), f("v", 3 * r, LANES), f("v", 2, LANES), ("V", pair, F32)],
        [z.pads(), z.chains(4)],
    )(x, above, below, gathered, affine, w1)
    gathered = exchange(copies, AXES)
    extended, near_rows = z.total + 4 * r, z.total + 2 * r
    left_one, packed, teachers, spread_u, near_u = call(
        body(first_operand_kernel),
        "vvvvvvvvvhh",
        [("h", left, BF16), f("h", C, BACK_LANES), f("h", extended, LANES), f("h", near_rows, LANES), f("h", near_rows, LANES)],
        [
            z.pads(), z.chains(2), (left, BF16), (weight, BF16), ((near_rows, LANES), F32), ((extended, 128), F32),
            ((extended, LANES), F32), ((near_rows, LANES), F32), ((C, BACK_LANES), F32),
        ],
        7,
    )(x, hidden, h_above, h_below, above, below, stats_one, affine, teacher, upstream, weights)
    gathered, near_u = lax.optimization_barrier((gathered, near_u))

    map_shape = (peers * z.slots, 128)
    out, o_above, o_below, near, stats_two, copies = call(
        body(second_kernel),
        "vvvvvvvvvv",
        [("v", full, F32), f("v", 2 * r, LANES), f("v", 2 * r, LANES), f("v", 2, r, LANES), f("v", 2, LANES), ("V", map_shape, F32)],
        [z.pads(), z.chains(3)],
    )(hidden, h_above, h_below, gathered, affine, w2, x, above, below, teacher)
    gathered = exchange(copies, ("row",))
    out_copy, hidden_copy, left_two, shifts, by_map, by_teacher, up = call(
        body(second_operand_kernel),
        "vvvvvvvhhhh",
        [
            ("h", full, F32), f("h", near_rows, LANES), ("v", left, BF16), f("h", 3, near_rows, LANES),
            f("v", near_rows, LANES), f("v", near_rows, LANES), f("v", near_rows, LANES),
        ],
        [
            z.pads(), z.chains(2), ((extended, LANES), F32), ((near_rows, LANES), F32), (weight, BF16),
            ((3, near_rows, LANES), F32),
        ],
        11,
    )(hidden, near, stats_two, affine, out, o_above, o_below, teachers, spread_u, near_u, weights)

    dout, dshift, d_above, d_below, slabs = call(
        body(upstream_kernel),
        "vvhhvhvvhv",
        [("v", full, F32), ("v", full, F32), f("v", r, LANES), f("v", r, LANES), f("V", devices, 1, BACK_LANES)],
        [((3, near_rows, LANES), F32), (left, BF16), (full, F32), ((C, BACK_LANES), F32), z.pads(), z.pads()],
        4,
    )(gathered, up, shifts, left_one, left_two, packed, by_map, by_teacher, hidden_copy, stats_two)
    gathered = exchange(slabs, AXES)
    out_s, out_l, first_normed, second_normed, weight_back = call(
        body(write_kernel),
        "hhhhvvv",
        [("v", image_small.shape, F32), ("v", image_large.shape, F32), ("v", full, F32), f("v", near_rows, LANES), ("v", weight, BF16)],
        [(full, F32), (full, F32), ((near_rows, LANES), F32), (half, F32)],
        4,
    )(out_copy, x_copy, hidden_copy, weights, stats_one, stats_two, d_above)

    pre, gain_two, bias_two, slabs = call(
        body(hidden_kernel),
        "vvvvvvvvv",
        [("v", full, F32), f("v", 1, C), f("v", 1, C), f("V", devices, 1, LAST_LANES)],
        [z.pads()],
    )(gathered, dshift, d_above, d_below, second_normed, stats_two, affine, weight_back, first_normed)
    gathered = exchange(slabs, AXES)

    back_s, back_l, one, two, gain_one, bias_one = call(
        body(back_kernel),
        "vvvvvv",
        [("v", a.shape, F32) for a in (image_small, image_large, conv_first, conv_second)] + [f("v", 1, C), f("v", 1, C)],
        [(half, F32), ((C, LAST_LANES), F32)],
    )(gathered, pre, first_normed, stats_one, affine, dout)
    return (
        out_s, out_l, back_s, back_l,
        one, gain_one.reshape(C), bias_one.reshape(C),
        two, gain_two.reshape(C), bias_two.reshape(C),
    )


def solution(mesh):
    split_bands, everywhere = P("img", "row", None), P()
    return jax.shard_map(
        local,
        mesh=mesh,
        in_specs=(split_bands,) * 6 + (everywhere,) * 6,
        out_specs=(split_bands,) * 4 + (everywhere,) * 6,
        check_vma=False,
    )
```

```python
import functools
import math

import jax
import jax.numpy as jnp
from jax import lax
from jax.experimental import pallas as pl
from jax.experimental.pallas import tpu as pltpu
from jax.sharding import PartitionSpec as P

C = 32
HS = 32
HL = 64
HEIGHTS = (HS, HL)

norm_eps = 1e-05
map_eps = 1e-06
beta_weight = 1000.0
AXES = ("img", "row")
BLOCK = 8
LANES = BLOCK * C
TAPS = 3
DEPTH = TAPS * 128 + 256
TAP_ROWS = 128 + 2 * C
REACH = 4
ROOT = math.sqrt(2.0 / math.pi)
CUBE = 0.044715
F32 = jnp.float32
BF16 = jnp.bfloat16
VMEM_LIMIT = 32 * 1024 * 1024
BIAS, GAIN, SECOND, LEFT, HIDDEN, ONES = 0, 1, 2, 11, 20, 29
BACK_LANES = 1280
LAST_SECOND, LAST_FIRST, LAST_LANES = 2, 11, 640


class Sizes:
    def __init__(self, small, large, devices, peers):
        self.images = (small[0], large[0])
        self.rows = (small[1], large[1])
        self.blocks = (HS // BLOCK, HL // BLOCK)
        self.step = tuple(n * r for n, r in zip(self.images, self.rows))
        self.count = tuple(b * s for b, s in zip(self.blocks, self.step))
        self.edge = tuple(b * n for b, n in zip(self.blocks, self.images))
        self.start = (self.count[1], 0)
        self.rim = (self.edge[1], 0)
        self.total = sum(self.count)
        self.rims = sum(self.edge)
        self.slots = -(-sum(self.images) // 8) * 8
        self.guard = -(-max(self.images) // 8) * 8
        self.devices = devices
        self.peers = peers
        self.here = float(self.total * BLOCK)
        self.pixels = self.here * devices

    def pads(self):
        return [((TAPS, 2, self.count[k] + 2 * self.step[k], 128), F32) for k in (0, 1)]

    def chains(self, depth):
        return [((2, 2 * self.guard + (depth + 1) * self.rims, 128), F32)] * 2


def split(value):
    high = value.astype(BF16)
    return high, (value - high.astype(F32)).astype(BF16)


def dot(left, right):
    return lax.dot_general(left, right, (((1,), (0,)), ((), ())), preferred_element_type=F32)


def product(left, right):
    if left[0].shape[1] % 128:
        return dot(left[0], right[0]) + (dot(left[0], right[1]) + dot(left[1], right[0]))
    return dot(
        jnp.concatenate([left[0], left[0], left[1]], axis=1), jnp.concatenate([right[0], right[1], right[0]], axis=0)
    )


def spread(left, right):
    right = right.astype(BF16)
    return dot(jnp.concatenate(split(left), axis=1), jnp.concatenate([right, right], axis=0))


def gelu(s):
    return 0.5 * s * (1.0 + jnp.tanh(ROOT * (s + CUBE * s * s * s)))


def gelu_slope(s):
    square = s * s
    t = jnp.tanh(ROOT * s * (1.0 + CUBE * square))
    return 0.5 * (1.0 + t) + 0.5 * s * (1.0 - t * t) * ROOT * (1.0 + 3.0 * CUBE * square)


def spread_groups(row):
    row = row + pltpu.roll(row, 64, 1)
    return row + pltpu.roll(row, 32, 1)


def fold(row):
    return spread_groups(row[:, :128] + row[:, 128:])


def wide(row):
    return jnp.concatenate([row, row], axis=1)


def group_of(rows=1, lanes=128):
    return lax.broadcasted_iota(jnp.int32, (rows, lanes), 1) // C


def column_sum(value):
    return jnp.sum(value, axis=0, keepdims=True)


def send_lines(z, ref, lines):
    for n, line in enumerate(lines):
        ref[pl.ds(n, z.devices, stride=len(lines)), :] = jnp.broadcast_to(line, (z.devices, 128))


def moments(z, value, ref):
    few = min(8, z.total)
    pivot = fold(column_sum(value[:few])) / float(few * BLOCK)
    off = value - wide(pivot)
    first, second = fold(column_sum(off)), fold(column_sum(off * off))
    send_lines(z, ref, [pivot + first / z.here, second - first * first / z.here])


def merged(z, ref):
    means = ref[pl.ds(0, z.devices, stride=2), :]
    center = jnp.mean(means, axis=0, keepdims=True)
    off = means - center
    within = jnp.mean(ref[pl.ds(1, z.devices, stride=2), :], axis=0, keepdims=True)
    variance = within / z.here + jnp.mean(off * off, axis=0, keepdims=True)
    return wide(center), wide(lax.rsqrt(variance + norm_eps))


def put_halves(ref, value):
    ref[0] = value[:, :128]
    ref[1] = value[:, 128:]


def whole(ref):
    return jnp.concatenate([ref[0], ref[1]], axis=1)


def to_matrix(z, refs, half):
    for k in (0, 1):
        for j in range(z.blocks[k]):
            at = z.start[k] + j * z.step[k]
            for i in range(z.images[k]):
                for h in (0, 1):
                    half[h, pl.ds(at + i * z.rows[k], z.rows[k]), :] = refs[k][i, :, pl.ds(LANES * j + 128 * h, 128)]


def from_matrix(z, half, refs):
    for k in (0, 1):
        for j in range(z.blocks[k]):
            at = z.start[k] + j * z.step[k]
            for i in range(z.images[k]):
                for h in (0, 1):
                    refs[k][i, :, pl.ds(LANES * j + 128 * h, 128)] = half[h, pl.ds(at + i * z.rows[k], z.rows[k]), :]


def take_rims(z, half, depth, bottom, top):
    for k in (0, 1):
        for d in range(1, depth + 1):
            to_bottom = pl.ds((depth - d) * z.rims + z.rim[k], z.edge[k])
            to_top = pl.ds((d - 1) * z.rims + z.rim[k], z.edge[k])
            if d <= z.rows[k]:
                bottom[to_bottom, :] = half[pl.ds(z.start[k] + z.rows[k] - d, z.edge[k], stride=z.rows[k]), :]
                top[to_top, :] = half[pl.ds(z.start[k] + d - 1, z.edge[k], stride=z.rows[k]), :]
            else:
                bottom[to_bottom, :] = jnp.zeros((z.edge[k], 128), F32)
                top[to_top, :] = jnp.zeros((z.edge[k], 128), F32)


def inside(z, depth, above):
    at = lax.axis_index("row")
    large = lax.broadcasted_iota(jnp.int32, (z.rims, 1), 0) < z.rim[0]
    parts = []
    for n in range(depth):
        if above:
            ok = [jnp.where(at * rows >= depth - n, 1.0, 0.0) for rows in z.rows]
        else:
            ok = [jnp.where((at + 1) * rows + n + 1 <= height, 1.0, 0.0) for rows, height in zip(z.rows, HEIGHTS)]
        parts.append(jnp.where(large, ok[1], ok[0]).astype(F32))
    return jnp.concatenate(parts, axis=0)


def clear_guards(z, pads, a):
    for k in (0, 1):
        pads[k][a, 1, pl.ds(0, z.step[k]), :] = jnp.zeros((z.step[k], 128), F32)
        pads[k][a, 0, pl.ds(z.step[k] + z.count[k], z.step[k]), :] = jnp.zeros((z.step[k], 128), F32)


def fill_center(z, pads, value):
    clear_guards(z, pads, 1)
    for k in (0, 1):
        for h in (0, 1):
            pads[k][1, h, pl.ds(z.step[k], z.count[k]), :] = value[z.start[k] : z.start[k] + z.count[k], 128 * h : 128 * h + 128]


def fill_shifted(z, pads, above, below):
    for k in (0, 1):
        ref, step, count, rows = pads[k], z.step[k], z.count[k], z.rows[k]
        rim = slice(z.rim[k], z.rim[k] + z.edge[k])
        for h in (0, 1):
            lanes = slice(128 * h, 128 * h + 128)
            ref[0, h, pl.ds(step, count), :] = ref[1, h, pl.ds(step - 1, count), :]
            ref[2, h, pl.ds(step, count), :] = ref[1, h, pl.ds(step + 1, count), :]
            ref[0, h, pl.ds(step, z.edge[k], stride=rows), :] = above[rim, lanes]
            ref[2, h, pl.ds(step + rows - 1, z.edge[k], stride=rows), :] = below[rim, lanes]


def fill_pads(z, pads, value, above, below):
    fill_center(z, pads, value)
    fill_shifted(z, pads, above, below)
    for a in (0, 2):
        clear_guards(z, pads, a)


def beside(left, right):
    lane = lax.broadcasted_iota(jnp.int32, (1, 128), 1)
    middle = pltpu.roll(jnp.where(lane >= 64, left[1], right[1]), 64, 1)
    return [
        jnp.where(lane >= 96, left[0], jnp.where(lane < 32, right[0], middle)),
        jnp.where(lane >= 96, left[2], jnp.where(lane < 32, right[2], 0.0)),
    ]


def band_operand(z, pads):
    parts = ([], [])
    for k in (1, 0):
        ref, step, count = pads[k], z.step[k], z.count[k]
        low, high = ([ref[a, h, pl.ds(step, count), :] for a in range(TAPS)] for h in (0, 1))
        before = [ref[a, 1, pl.ds(0, count), :] for a in range(TAPS)]
        after = [ref[a, 0, pl.ds(2 * step, count), :] for a in range(TAPS)]
        parts[0].append(jnp.concatenate(low + beside(before, high), axis=1))
        parts[1].append(jnp.concatenate(high + beside(low, after), axis=1))
    return [jnp.concatenate(part, axis=0) for part in parts]


def rim_operand(z, chain, depth):
    m = lax.broadcasted_iota(jnp.int32, (z.rims, 1), 0)
    large = m < z.rim[0]
    has_before = jnp.where(large, m, m - z.rim[0]) >= jnp.where(large, z.images[1], z.images[0])
    has_after = m < jnp.where(large, z.rim[0] - z.images[1], z.rims - z.images[0])
    low, high, before, after = [], [], [], []
    for r in range(depth + 1):
        at = z.guard + r * z.rims
        low.append(chain[0, pl.ds(at, z.rims), :])
        high.append(chain[1, pl.ds(at, z.rims), :])
        shifted = [chain[1, pl.ds(at - images, z.rims), :] for images in z.images]
        before.append(jnp.where(has_before, jnp.where(large, shifted[1], shifted[0]), 0.0))
        shifted = [chain[0, pl.ds(at + images, z.rims), :] for images in z.images]
        after.append(jnp.where(has_after, jnp.where(large, shifted[1], shifted[0]), 0.0))
    parts = ([], [])
    for n in range(depth - 1):
        rows = slice(n, n + TAPS)
        parts[0].append(jnp.concatenate(low[rows] + beside(before[rows], high[rows]), axis=1))
        parts[1].append(jnp.concatenate(high[rows] + beside(low[rows], after[rows]), axis=1))
    return [jnp.concatenate(part, axis=0) for part in parts]


def times(parts, weight):
    left = jnp.concatenate([part[h] for h in (0, 1) for part in parts], axis=0)
    both = jnp.concatenate([weight_matrix(weight.at[0]), weight_matrix(weight.at[1])], axis=1)
    result = dot(jnp.concatenate(split(left), axis=1), jnp.concatenate([both, both], axis=0))
    result = result[:, :128] + result[:, 128:]
    rows = result.shape[0] // 2
    return jnp.concatenate([result[:rows], result[rows:]], axis=1)


def convolve(z, own, above, below, depth, pads, chains, weight):
    r = z.rims
    fill_pads(z, pads, own, above[(depth - 1) * r :], below[:r])
    parts = [band_operand(z, pads)]
    if depth > 1:
        for side, (rim, chain) in enumerate(zip((above, below), chains)):
            rim_at, own_at = (z.guard, z.guard + depth * r) if side == 0 else (z.guard + r, z.guard)
            for h in (0, 1):
                chain[h, pl.ds(rim_at, depth * r), :] = rim[:, 128 * h : 128 * h + 128]
                for k in (0, 1):
                    row = z.step[k] + (0 if side == 0 else z.rows[k] - 1)
                    chain[h, pl.ds(own_at + z.rim[k], z.edge[k]), :] = pads[k][1, h, pl.ds(row, z.edge[k], stride=z.rows[k]), :]
            parts.append(rim_operand(z, chain, depth))
    result = times(parts, weight)
    n = z.total + (depth - 1) * r
    return result[: z.total], result[z.total : n], result[n:]


def image_sums(z, value):
    slot = lax.broadcasted_iota(jnp.int32, (z.slots, 1), 0)
    sums = jnp.zeros((z.slots, 128), F32)
    for k in (0, 1):
        line = value[z.start[k] : z.start[k] + z.step[k]]
        for j in range(1, z.blocks[k]):
            at = z.start[k] + j * z.step[k]
            line = line + value[at : at + z.step[k]]
        image = lax.broadcasted_iota(jnp.int32, (z.step[k], 1), 0) // z.rows[k]
        for i in range(z.images[k]):
            sums = jnp.where(slot == i + k * z.images[0], column_sum(jnp.where(image == i, line, 0.0)), sums)
    return sums


def image_rows(z, values, rims):
    parts = []
    for k in (1, 0):
        image = lax.broadcasted_iota(jnp.int32, (z.step[k], 1), 0) // z.rows[k]
        line = jnp.zeros((z.step[k], 128), F32)
        for i in range(z.images[k]):
            at = i + k * z.images[0]
            line = jnp.where(image == i, values[at : at + 1], line)
        parts += [line] * z.blocks[k]
    if rims:
        m = lax.broadcasted_iota(jnp.int32, (z.rims, 1), 0)
        image = jnp.where(m < z.rim[0], z.images[0] + m % z.images[1], (m - z.rim[0]) % z.images[0])
        line = jnp.zeros((z.rims, 128), F32)
        for at in range(sum(z.images)):
            line = jnp.where(image == at, values[at : at + 1], line)
        parts += [line] * rims
    return jnp.concatenate(parts, axis=0)


def channel_mean():
    a = lax.broadcasted_iota(jnp.int32, (LANES, 128), 0) // C
    b = lax.broadcasted_iota(jnp.int32, (LANES, 128), 1) % 64
    return jnp.where(a == b, 1.0 / C, 0.0).astype(F32)


def to_channels():
    a = lax.broadcasted_iota(jnp.int32, (128, LANES), 0)
    b = lax.broadcasted_iota(jnp.int32, (128, LANES), 1) // C
    return jnp.where(a == b, 1.0, 0.0).astype(F32)


def attention(value):
    return spread(value * value, channel_mean())


def pieces(source, target):
    return [(source.at[n], target.at[n]) for n in range(source.shape[0])]


def copies_of(pairs, sems, first=0):
    return [pltpu.make_async_copy(a, b, sems.at[first + n]) for n, (a, b) in enumerate(pairs)]


def start_all(copies):
    for copy in copies:
        copy.start()


def wait_all(copies):
    for copy in copies:
        copy.wait()


def start_kernel(z, small, large, up_s, up_l, t_s, t_l, x, bottom, top, copies, raw, half, sems):
    images = [(small, raw[0])] + pieces(large, raw[1])
    rest = [(up_s, raw[2])] + pieces(up_l, raw[3]) + [(t_s, raw[4]), (t_l, raw[5])]
    loads = copies_of(images + rest, sems)
    start_all(loads)
    r, n = z.rims, REACH * z.rims
    tail = n + 2 * r
    for ref in (bottom, top):
        ref[pl.ds(tail, z.slots), :] = jnp.zeros((z.slots, LANES), F32)
    wait_all(loads[: len(images)])
    to_matrix(z, raw[:2], half)
    value = whole(half)
    x[...] = value
    moments(z, value, copies)
    for h in (0, 1):
        lanes = pl.ds(128 * h, 128)
        take_rims(z, half.at[h], REACH, bottom.at[pl.ds(0, n), lanes], top.at[pl.ds(0, n), lanes])
    wait_all(loads[len(images) :])
    for k in (0, 1):
        width, rows = HEIGHTS[k], z.rows[k]
        for i in range(z.images[k]):
            slot = pl.ds(tail + i + k * z.images[0], 1)
            for d in (0, 1):
                to_bottom, to_top = n + (1 - d) * r + z.rim[k] + i, n + d * r + z.rim[k] + i
                for j in range(z.blocks[k]):
                    lanes, at = pl.ds(LANES * j, LANES), j * z.images[k]
                    if d < rows:
                        bottom[pl.ds(to_bottom + at, 1), :] = raw[2 + k][i, pl.ds(rows - 1 - d, 1), lanes]
                        top[pl.ds(to_top + at, 1), :] = raw[2 + k][i, pl.ds(d, 1), lanes]
                    else:
                        bottom[pl.ds(to_bottom + at, 1), :] = jnp.zeros((1, LANES), F32)
                        top[pl.ds(to_top + at, 1), :] = jnp.zeros((1, LANES), F32)
                if d < rows:
                    bottom[slot, pl.ds(128 * (1 - d), width)] = raw[4 + k][i, pl.ds(rows - 1 - d, 1), :]
                    top[slot, pl.ds(128 * d, width)] = raw[4 + k][i, pl.ds(d, 1), :]


def banded(taps, ref):
    row = lax.broadcasted_iota(jnp.int32, (128, 128), 0) // C
    lane = group_of(128)
    for a in range(TAPS):
        main = jnp.zeros((128, 128), F32)
        for b in range(TAPS):
            main = jnp.where(row - lane + 1 == b, taps[a][b], main)
        before = jnp.where(lane[:C] == 0, taps[a][0][:C], 0.0)
        after = jnp.where(lane[:C] == 3, taps[a][2][:C], 0.0)
        for n, part in enumerate(split(jnp.concatenate([main, before, after], axis=0))):
            ref[n, pl.ds(a * TAP_ROWS, TAP_ROWS), :] = part


def weight_matrix(ref):
    main = [ref[pl.ds(a * TAP_ROWS, 128), :] for a in range(TAPS)]
    before, after = ([ref[pl.ds(a * TAP_ROWS + 128 + n * C, C), :] for a in range(TAPS)] for n in (0, 1))
    return jnp.concatenate(
        main + [after[0], before[1], after[1], before[0], after[2], jnp.zeros((2 * C, 128), BF16), before[2]], axis=0
    )


def prepare_kernel(z, first, second, up_s, up_l, t_s, t_l, g1, b1, g2, b2, x, w1, w2, weights, affine, upstream, teacher, x_copy, raw, kept, kept_u, rows, half, sems):
    targets = tuple(raw) + tuple(rows.at[pl.ds(n, 1), :] for n in range(4))
    refs = (first, second, up_s, up_l, t_s, t_l, g1, b1, g2, b2)
    loads = [pltpu.make_async_copy(a, b, sems.at[n]) for n, (a, b) in enumerate(zip(refs, targets))]
    start_all(loads)
    stores = [pltpu.make_async_copy(x, x_copy, sems.at[13])]
    stores[0].start()
    wait_all(loads)
    to_matrix(z, raw[2:4], half)
    kept_u[...] = whole(half)
    stores.append(pltpu.make_async_copy(kept_u, upstream, sems.at[10]))
    stores[1].start()
    for n, (source, forward) in enumerate(zip(raw[:2], (w1, w2))):
        tiles = []
        for a in range(TAPS):
            line = [jnp.concatenate([source[a, b]] * 4, axis=1) for b in range(TAPS)]
            tiles.append([jnp.concatenate([tap] * 4, axis=0) for tap in line])
        turned = [[tiles[TAPS - 1 - a][TAPS - 1 - b].T for b in range(TAPS)] for a in range(TAPS)]
        banded(tiles, forward)
        banded(turned, kept.at[n])
        stores.append(pltpu.make_async_copy(kept.at[n], weights.at[n], sems.at[11 + n]))
        stores[-1].start()
    affine[...] = jnp.concatenate([rows[...]] * BLOCK, axis=1)
    teacher[...] = jnp.zeros(teacher.shape, F32)
    for k, ref in ((0, raw[4]), (1, raw[5])):
        for i in range(z.images[k]):
            line = ref[i]
            for j in range(z.blocks[k]):
                at = z.start[k] + j * z.step[k] + i * z.rows[k]
                for lane in (0, 64):
                    teacher[pl.ds(at, z.rows[k]), pl.ds(lane, BLOCK)] = line[:, j * BLOCK : (j + 1) * BLOCK]
    wait_all(stores)


def normed_by(stats):
    return lambda v: (v - stats[0:1]) * stats[1:2]


def activation(center, scale, gain, bias):
    factor = scale * gain
    offset = bias - center * factor
    return lambda v: gelu(v * factor + offset)


def first_kernel(z, x, above, below, gathered, affine, weight, hidden, h_above, h_below, stats, copies, pads, chains):
    n = REACH * z.rims
    center, scale = merged(z, gathered)
    act = activation(center, scale, affine[0:1], affine[1:2])
    own = act(x[...])
    up, down = act(above[pl.ds(0, n), :]) * inside(z, 4, True), act(below[pl.ds(0, n), :]) * inside(z, 4, False)
    own, up, down = convolve(z, own, up, down, 4, pads, chains, weight)
    moments(z, own, copies)
    hidden[...] = own
    h_above[...] = up
    h_below[...] = down
    stats[0:1] = center
    stats[1:2] = scale


def second_kernel(z, hidden, h_above, h_below, gathered, affine, weight, x, x_above, x_below, teacher, out, o_above, o_below, near, stats, copies, pads, chains):
    center, scale = merged(z, gathered)
    act = activation(center, scale, affine[2:3], affine[3:4])
    r = z.rims
    own = act(hidden[...])
    up, down = act(h_above[...]) * inside(z, 3, True), act(h_below[...]) * inside(z, 3, False)
    own, up, down = convolve(z, own, up, down, 3, pads, chains, weight)
    own = x[...] + own
    amap = attention(own)
    lane = lax.broadcasted_iota(jnp.int32, (1, 128), 1)
    sums = image_sums(z, amap * jnp.where(lane < 64, amap, teacher[...]))
    copies[...] = jnp.concatenate([sums] * z.peers, axis=0)
    out[...] = own
    o_above[...] = x_above[pl.ds(2 * r, 2 * r), :] + up
    o_below[...] = x_below[pl.ds(0, 2 * r), :] + down
    near[0] = h_above[pl.ds(2 * r, r), :]
    near[1] = h_below[pl.ds(0, r), :]
    stats[0:1] = center
    stats[1:2] = scale


def tap_rows(q):
    return 128 + 3 * C if q < 0 else 128 if q == 4 else q * C


def tap_product(z, operand, own, above, below, pads):
    fill_center(z, pads, own)
    fill_shifted(z, pads, above, below)
    columns = []
    for a in range(TAPS):
        columns.append(
            jnp.concatenate([pads[k][TAPS - 1 - a, h, pl.ds(z.step[k], z.count[k]), :] for h in (0, 1) for k in (1, 0)], axis=0)
        )
    return product(operand, split(jnp.concatenate(columns, axis=1)))


def tap_sums(result, tiles, first_group):
    group = group_of()
    for a in range(TAPS):
        for b in range(TAPS):
            total = None
            for p in range(4):
                at = tap_rows(p + b - 1)
                part = result[at : at + C, 128 * a : 128 * a + 128]
                total = part if total is None else jnp.where(group == p, part, total)
            tile, slot = divmod(first_group + a * TAPS + b, 4)
            tiles[tile] = jnp.where(group == slot, spread_groups(total), tiles[tile])


def tap_counts(z, turned, tiles, first_group):
    group = group_of()
    m = lax.broadcasted_iota(jnp.int32, (1, 2 * z.total), 1) % z.total
    row = jnp.where(m < z.start[0], m % z.rows[1], (m - z.start[0]) % z.rows[0])
    height = jnp.where(m < z.start[0], z.rows[1], z.rows[0])
    at = lax.axis_index("row")
    lost = {
        0: (row == height - 1) & (at == z.peers - 1),
        2: (row == 0) & (at == 0),
    }
    for a in range(TAPS):
        column = jnp.sum(jnp.where(lost[a], 0.0, turned) if a in lost else turned, axis=1, keepdims=True)
        for b in range(TAPS):
            total = sum(column[tap_rows(p + b - 1) : tap_rows(p + b - 1) + C] for p in range(4))
            tile, slot = divmod(first_group + a * TAPS + b, 4)
            tiles[tile] = jnp.where(group == slot, total, tiles[tile])


def turned_operand(z, value, pads, kept):
    fill_center(z, pads, value)
    lane = lax.broadcasted_iota(jnp.int32, (1, 128), 1)
    halves = ([], [])
    for k in (1, 0):
        ref, step, count = pads[k], z.step[k], z.count[k]
        low, high = ref[1, 0, pl.ds(step, count), :], ref[1, 1, pl.ds(step, count), :]
        before, after = ref[1, 1, pl.ds(0, count), :], ref[1, 0, pl.ds(2 * step, count), :]
        for part, main, left, right in ((halves[0], low, before, high), (halves[1], high, low, after)):
            part.append(jnp.concatenate([main, jnp.where(lane >= 96, left, jnp.where(lane < 32, right, 0.0))], axis=1))
    turned = jnp.concatenate(halves[0] + halves[1], axis=0).T
    parts = split(turned)
    for n in (0, 1):
        kept[n] = parts[n]
    return turned


def first_operand_kernel(z, x, hidden, h_above, h_below, above, below, stats, affine, teacher, upstream, weights, left, packed, teachers, spread_u, near_u, pads, chains, kept, kept_w, kept_u, pixels, kept_t, kept_c, kept_packed, sems):
    r, own = z.rims, pl.ds(0, z.total)
    loads = [pltpu.make_async_copy(upstream, kept_u.at[own, :], sems.at[0]), pltpu.make_async_copy(weights.at[1], kept_w, sems.at[1])]
    start_all(loads)
    act = activation(stats[0:1], stats[1:2], affine[0:1], affine[1:2])
    value = turned_operand(z, act(x[...]), pads, kept)
    stores = [pltpu.make_async_copy(kept, left, sems.at[2])]
    stores[0].start()
    tiles = [jnp.zeros((C, 128), F32) for _ in range(BACK_LANES // 128)]
    tap_counts(z, value, tiles, ONES)
    result = tap_product(
        z, (kept[0], kept[1]), hidden[...], h_above[pl.ds(2 * r, r), :] * inside(z, 1, True), h_below[pl.ds(0, r), :] * inside(z, 1, False), pads
    )
    tap_sums(result, tiles, HIDDEN)
    kept_packed[...] = jnp.concatenate(tiles, axis=1)
    stores.append(pltpu.make_async_copy(kept_packed, packed, sems.at[6]))
    stores[1].start()
    pixels[own, :] = teacher[...]
    pixels[pl.ds(z.total, 4 * r), :] = jnp.zeros((4 * r, 128), F32)
    n = (REACH + 2) * r
    for side, ref in enumerate((above, below)):
        for d in (0, 1):
            for k in (0, 1):
                line = ref[pl.ds(n + k * z.images[0], z.images[k]), pl.ds(128 * d, 128)]
                for j in range(z.blocks[k]):
                    at = z.total + (2 * side + d) * r + z.rim[k] + j * z.images[k]
                    pixels[pl.ds(at, z.images[k]), pl.ds(0, BLOCK)] = line[:, j * BLOCK : (j + 1) * BLOCK]
    kept_t[...] = spread(pixels[...], to_channels())
    stores.append(pltpu.make_async_copy(kept_t, teachers, sems.at[3]))
    stores[2].start()
    n = REACH * r
    up, down = above[pl.ds(n, 2 * r), :] * inside(z, 2, True), below[pl.ds(n, 2 * r), :] * inside(z, 2, False)
    kept_u[pl.ds(z.total, r), :] = up[r:]
    kept_u[pl.ds(z.total + r, r), :] = down[:r]
    wait_all(loads)
    stores.append(pltpu.make_async_copy(kept_u, near_u, sems.at[5]))
    stores[3].start()
    kept_c[...] = jnp.concatenate(convolve(z, kept_u[own, :], up, down, 2, pads, chains, kept_w), axis=0)
    stores.append(pltpu.make_async_copy(kept_c, spread_u, sems.at[4]))
    stores[4].start()
    wait_all(stores)


def second_operand_kernel(z, hidden, near, stats, affine, out, o_above, o_below, teachers, spread_u, near_u, weights, out_copy, hidden_copy, left, shifts, by_map, by_teacher, up, pads, chains, kept_t, kept_u, kept_w, kept_s, sems):
    r, total = z.rims, z.total
    loads = [
        pltpu.make_async_copy(teachers, kept_t, sems.at[0]),
        pltpu.make_async_copy(weights.at[1], kept_w, sems.at[1]),
        pltpu.make_async_copy(spread_u, kept_u, sems.at[2]),
    ]
    start_all(loads)
    stores = [
        pltpu.make_async_copy(out, out_copy, sems.at[4]),
        pltpu.make_async_copy(hidden, hidden_copy.at[pl.ds(0, total), :], sems.at[7]),
        pltpu.make_async_copy(near.at[0], hidden_copy.at[pl.ds(total, r), :], sems.at[8]),
        pltpu.make_async_copy(near.at[1], hidden_copy.at[pl.ds(total + r, r), :], sems.at[9]),
        pltpu.make_async_copy(near_u, up, sems.at[10]),
    ]
    start_all(stores)
    normed = normed_by(stats)(jnp.concatenate([hidden[...], near[0], near[1]], axis=0))
    shifted = normed * affine[2:3] + affine[3:4]
    turned_operand(z, gelu(shifted[:total]), pads, left)
    ones = jnp.ones((total, 1), F32)
    masks = jnp.concatenate([ones, inside(z, 1, True), inside(z, 1, False)], axis=0)
    slopes = gelu_slope(shifted) * masks
    o = jnp.concatenate([out[...], o_above[...] * inside(z, 2, True), o_below[...] * inside(z, 2, False)], axis=0)
    for_map = spread(attention(o), to_channels()) * o
    wait_all(loads)
    for_teacher = kept_t[...] * o
    kept_s[0] = kept_u[...] * slopes
    stores += copies_of(pieces(kept_s, shifts), sems, 11)
    stores[-3].start()
    for n, value, ref in ((1, for_map, by_map), (2, for_teacher, by_teacher)):
        own, before, after = value[:total], value[total : total + 2 * r], value[total + 2 * r :]
        ref[...] = jnp.concatenate([own, before[r:], after[:r]], axis=0)
        kept_s[n] = jnp.concatenate(convolve(z, own, before, after, 2, pads, chains, kept_w), axis=0) * slopes
        stores[n - 3].start()
    wait_all(stores)


def upstream_kernel(z, gathered, up, shifts, left_1, left_2, packed, by_map, by_teacher, hidden, stats, dout, dshift, d_above, d_below, slabs, kept_s, kept_left, kept_h, kept_packed, pads, more_pads, sems):
    r, total = z.rims, z.total
    loads = copies_of(
        pieces(shifts, kept_s) + pieces(left_1, kept_left) + [(hidden.at[pl.ds(0, total), :], kept_h), (packed, kept_packed)], sems
    )
    start_all(loads)
    lane = lax.broadcasted_iota(jnp.int32, (z.slots, 128), 1)
    sums = sum(gathered[pl.ds(n * z.slots, z.slots), :] for n in range(z.peers))
    square = jnp.sum(jnp.where(lane < 64, sums, 0.0), axis=1, keepdims=True)
    cross = jnp.sum(jnp.where(lane < 64, 0.0, sums), axis=1, keepdims=True)
    inverse = lax.rsqrt(square + map_eps)
    inner = beta_weight * (square * inverse - cross) * inverse
    shape = (z.slots, 128)
    for_map = (beta_weight - inner) * inverse * inverse * (2.0 / C)
    for_teacher = beta_weight * inverse * (2.0 / C)
    for_map, for_teacher = (wide(image_rows(z, jnp.broadcast_to(v, shape), 2)) for v in (for_map, for_teacher))
    value = up[...] + for_map * by_map[...] - for_teacher * by_teacher[...]
    dout[...] = value[:total]
    wait_all(loads[:3])
    shift = kept_s[0] + for_map * kept_s[1] - for_teacher * kept_s[2]
    pre, above, below = shift[:total], shift[total : total + r], shift[total + r :]
    dshift[...] = pre
    d_above[...] = above
    d_below[...] = below
    second = tap_product(z, (left_2[0], left_2[1]), value[:total], value[total : total + r], value[total + r :], pads)
    wait_all(loads[3:5])
    first = tap_product(z, (kept_left[0], kept_left[1]), pre, above, below, more_pads)
    wait_all(loads[5:])
    normed = normed_by(stats)(kept_h[...])
    tiles = [kept_packed[:, 128 * n : 128 * n + 128] for n in range(BACK_LANES // 128)]
    group = group_of()
    tiles[0] = jnp.where(group == BIAS, fold(column_sum(pre)), jnp.where(group == GAIN, fold(column_sum(pre * normed)), tiles[0]))
    tap_sums(second, tiles, SECOND)
    tap_sums(first, tiles, LEFT)
    line = jnp.concatenate(tiles, axis=1)
    for d in range(z.devices):
        slabs[d] = line[d % C : d % C + 1]


def write_kernel(z, out, x, hidden, weights, first_stats, stats, order, out_s, out_l, first_normed, normed, weight, kept, kept_x, kept_h, half, sems):
    loads = [pltpu.make_async_copy(a, b, sems.at[n]) for n, (a, b) in enumerate(((out, kept), (x, kept_x), (hidden, kept_h), (weights.at[0], weight)))]
    start_all(loads)
    loads[0].wait()
    put_halves(half, kept[...])
    from_matrix(z, half, (out_s, out_l))
    loads[1].wait()
    first_normed[...] = normed_by(first_stats)(kept_x[...])
    loads[2].wait()
    normed[...] = normed_by(stats)(kept_h[...])
    loads[3].wait()


def norm_sums(total):
    group = group_of()
    return [wide(spread_groups(jnp.where(group == n, total[:, :128], 0.0))) for n in (BIAS, GAIN)]


def hidden_kernel(z, gathered, dshift, d_above, d_below, second_normed, stats, affine, weight, first_normed, pre_ref, gain_out, bias_out, slabs, pads):
    total = jnp.sum(gathered[...], axis=0)
    bias_sum, gain_sum = norm_sums(total)
    bias_out[...] = bias_sum[:, :C]
    gain_out[...] = gain_sum[:, :C]
    bias_mean, gain_mean = bias_sum / z.pixels, gain_sum / z.pixels
    factor = affine[2:3] * stats[1:2]
    r, total_rows = z.rims, z.total

    def back(d, normed):
        return factor * (d - bias_mean - normed * gain_mean)

    own = back(dshift[...], second_normed[pl.ds(0, total_rows), :])
    up = back(d_above[...], second_normed[pl.ds(total_rows, r), :]) * inside(z, 1, True)
    down = back(d_below[...], second_normed[pl.ds(total_rows + r, r), :]) * inside(z, 1, False)
    grad, _, _ = convolve(z, own, up, down, 1, pads, None, weight)
    normed = first_normed[...]
    pre = grad * gelu_slope(normed * affine[0:1] + affine[1:2])
    pre_ref[...] = pre
    lane = lax.broadcasted_iota(jnp.int32, (1, 128), 1)
    taps = TAPS * TAPS * C

    def along(row):
        return jnp.concatenate([row[:, :128]] * 3, axis=1)[:, :taps]

    second, left, against, ones = (total[:, n * C : n * C + taps] for n in (SECOND, LEFT, HIDDEN, ONES))
    against = along(stats[1:2]) * (against - along(stats[0:1]) * ones)
    first = along(factor) * (left - along(bias_mean) * ones - along(gain_mean) * against)
    sums = jnp.where(lane < C, fold(column_sum(pre)), fold(column_sum(pre * normed)))
    line = jnp.concatenate([sums[:, : 2 * C], second, first], axis=1)
    slabs[...] = jnp.broadcast_to(line[None], slabs.shape)


def back_kernel(z, gathered, pre, normed, stats, affine, dout, back_s, back_l, one, two, gain_out, bias_out, half, lines):
    bias_sum, gain_sum = norm_sums(jnp.sum(gathered[:, :, pl.ds(0, 128)], axis=0))
    bias_out[...] = bias_sum[:, :C]
    gain_out[...] = gain_sum[:, :C]
    value = dout[...] + affine[0:1] * stats[1:2] * (pre[...] - bias_sum / z.pixels - normed[...] * (gain_sum / z.pixels))
    put_halves(half, value)
    from_matrix(z, half, (back_s, back_l))
    for d in range(C):
        lines[pl.ds(d, 1), :] = gathered[d]
    for ref, group in ((two, LAST_SECOND), (one, LAST_FIRST)):
        for a in range(TAPS):
            for b in range(TAPS):
                at = (group + a * TAPS + b) * C
                ref[a, b] = lines[:, pl.ds(at, C)]


def call(body, ins, outs, scratch=(), sems=0):
    space = {"v": pltpu.VMEM, "h": pltpu.HBM, "V": pltpu.VMEM}
    shapes = []
    for item in scratch:
        if isinstance(item, list):
            shapes.append([pltpu.VMEM(*s) for s in item])
        else:
            shapes.append(pltpu.VMEM(*item))
    if sems:
        shapes.append(pltpu.SemaphoreType.DMA((sems,)))
    run = pl.pallas_call(
        body,
        out_shape=[jax.ShapeDtypeStruct(shape, kind) if s == "v" else space[s](shape, kind) for s, shape, kind in outs],
        in_specs=[pl.BlockSpec(memory_space=space[s]) for s in ins],
        out_specs=[pl.BlockSpec(memory_space=space[s]) for s, _, _ in outs],
        scratch_shapes=shapes,
        compiler_params=pltpu.CompilerParams(vmem_limit_bytes=VMEM_LIMIT),
    )
    return lambda *args: run(
        *(pltpu.with_memory_space_constraint(arg, pltpu.HBM) if s == "h" else arg for s, arg in zip(ins, args))
    )


def exchange(lines, axes):
    shape = lines.shape
    if len(shape) == 2:
        lines = lines.reshape(math.prod(lax.axis_size(axis) for axis in axes), -1, 128)
    return lax.all_to_all(lines, axes, 0, 0, tiled=True).reshape(shape)


def beyond(z, bottom, top, depths):
    hops = max(-(-depth // rows) for rows in z.rows for depth in depths)
    above, below = [], []
    for hop in range(1, hops + 1):
        above.append(lax.ppermute(bottom, "row", [(i, i + hop) for i in range(z.peers - hop)]))
        below.append(lax.ppermute(top, "row", [(i + hop, i) for i in range(z.peers - hop)]))
    if hops == 1:
        return above[0], below[0]
    up, down = [], []
    base = 0
    for depth in depths:
        for n in range(depth):
            for k in (1, 0):
                hop, back = divmod(depth - 1 - n, z.rows[k])
                at = base + (depth - 1 - back) * z.rims + z.rim[k]
                up.append(above[hop][at : at + z.edge[k]])
                hop, back = divmod(n, z.rows[k])
                at = base + back * z.rims + z.rim[k]
                down.append(below[hop][at : at + z.edge[k]])
        base += depth * z.rims
    up.append(jnp.concatenate([pixel_rows(z, above, base, 1, 1), pixel_rows(z, above, base, 0, 1)], axis=1))
    down.append(jnp.concatenate([pixel_rows(z, below, base, 0, 0), pixel_rows(z, below, base, 1, 0)], axis=1))
    return jnp.concatenate(up, axis=0), jnp.concatenate(down, axis=0)


def pixel_rows(z, bands, base, distance, last):
    lines = []
    for k in (0, 1):
        hop, back = divmod(distance, z.rows[k])
        at = base + k * z.images[0]
        half = 128 * abs(last - back)
        lines.append(bands[hop][at : at + z.images[k], half : half + 128])
    lines.append(jnp.zeros((z.slots - sum(z.images), 128), F32))
    return jnp.concatenate(lines, axis=0)


def local(
    image_small, image_large, teacher_small, teacher_large, upstream_small, upstream_large,
    conv_first, gain_first, bias_first, conv_second, gain_second, bias_second,
):
    peers = lax.axis_size("row")
    devices = lax.axis_size("img") * peers
    z = Sizes(image_small.shape, image_large.shape, devices, peers)
    body = lambda function: functools.partial(function, z)
    r = z.rims
    full, half, pair = (z.total, LANES), (2, z.total, 128), (2 * devices, 128)
    weight, left = (2, TAPS * TAP_ROWS, 128), (2, 256, 2 * z.total)
    images = [image_small, image_large, upstream_small, upstream_large, teacher_small, teacher_large]
    f = lambda space, *shape: (space, shape, F32)
    depths = (REACH, 2)
    rim_rows = sum(depths) * r + z.slots

    x, bottom, top, copies = call(
        body(start_kernel),
        "hhhhhh",
        [("v", full, F32), f("v", rim_rows, LANES), f("v", rim_rows, LANES), ("V", pair, F32)],
        [[(a.shape, F32) for a in images], (half, F32)],
        4 + 2 * z.images[1],
    )(*images)
    gathered = exchange(copies, AXES)
    above, below = beyond(z, bottom, top, depths)
    params = [conv_first, conv_second] + images[2:]
    w1, w2, weights, affine, upstream, teacher, x_copy = call(
        body(prepare_kernel),
        "hhhhhhhhhhv",
        [("v", weight, BF16), ("v", weight, BF16), ("h", (2,) + weight, BF16), f("v", 4, LANES), ("h", full, F32), f("v", z.total, 128), ("h", full, F32)],
        [[(a.shape, F32) for a in params], ((2,) + weight, BF16), (full, F32), ((4, C), F32), (half, F32)],
        14,
    )(*params, *(v.reshape(1, C) for v in (gain_first, bias_first, gain_second, bias_second)), x)

    hidden, h_above, h_below, stats_one, copies = call(
        body(first_kernel),
        "vvvvvv",
        [("v", full, F32), f("v", 3 * r, LANES), f("v", 3 * r, LANES), f("v", 2, LANES), ("V", pair, F32)],
        [z.pads(), z.chains(4)],
    )(x, above, below, gathered, affine, w1)
    gathered = exchange(copies, AXES)
    extended, near_rows = z.total + 4 * r, z.total + 2 * r
    left_one, packed, teachers, spread_u, near_u = call(
        body(first_operand_kernel),
        "vvvvvvvvvhh",
        [("h", left, BF16), f("h", C, BACK_LANES), f("h", extended, LANES), f("h", near_rows, LANES), f("h", near_rows, LANES)],
        [
            z.pads(), z.chains(2), (left, BF16), (weight, BF16), ((near_rows, LANES), F32), ((extended, 128), F32),
            ((extended, LANES), F32), ((near_rows, LANES), F32), ((C, BACK_LANES), F32),
        ],
        7,
    )(x, hidden, h_above, h_below, above, below, stats_one, affine, teacher, upstream, weights)
    gathered, near_u = lax.optimization_barrier((gathered, near_u))

    map_shape = (peers * z.slots, 128)
    out, o_above, o_below, near, stats_two, copies = call(
        body(second_kernel),
        "vvvvvvvvvv",
        [("v", full, F32), f("v", 2 * r, LANES), f("v", 2 * r, LANES), f("v", 2, r, LANES), f("v", 2, LANES), ("V", map_shape, F32)],
        [z.pads(), z.chains(3)],
    )(hidden, h_above, h_below, gathered, affine, w2, x, above, below, teacher)
    gathered = exchange(copies, ("row",))
    out_copy, hidden_copy, left_two, shifts, by_map, by_teacher, up = call(
        body(second_operand_kernel),
        "vvvvvvvhhhh",
        [
            ("h", full, F32), f("h", near_rows, LANES), ("v", left, BF16), f("h", 3, near_rows, LANES),
            f("v", near_rows, LANES), f("v", near_rows, LANES), f("v", near_rows, LANES),
        ],
        [
            z.pads(), z.chains(2), ((extended, LANES), F32), ((near_rows, LANES), F32), (weight, BF16),
            ((3, near_rows, LANES), F32),
        ],
        14,
    )(hidden, near, stats_two, affine, out, o_above, o_below, teachers, spread_u, near_u, weights)

    dout, dshift, d_above, d_below, slabs = call(
        body(upstream_kernel),
        "vvhhvhvvhv",
        [("v", full, F32), ("v", full, F32), f("v", r, LANES), f("v", r, LANES), f("V", devices, 1, BACK_LANES)],
        [((3, near_rows, LANES), F32), (left, BF16), (full, F32), ((C, BACK_LANES), F32), z.pads(), z.pads()],
        7,
    )(gathered, up, shifts, left_one, left_two, packed, by_map, by_teacher, hidden_copy, stats_two)
    gathered = exchange(slabs, AXES)
    out_s, out_l, first_normed, second_normed, weight_back = call(
        body(write_kernel),
        "hhhhvvv",
        [("v", image_small.shape, F32), ("v", image_large.shape, F32), ("v", full, F32), f("v", near_rows, LANES), ("v", weight, BF16)],
        [(full, F32), (full, F32), ((near_rows, LANES), F32), (half, F32)],
        4,
    )(out_copy, x_copy, hidden_copy, weights, stats_one, stats_two, d_above)

    pre, gain_two, bias_two, slabs = call(
        body(hidden_kernel),
        "vvvvvvvvv",
        [("v", full, F32), f("v", 1, C), f("v", 1, C), f("V", devices, 1, LAST_LANES)],
        [z.pads()],
    )(gathered, dshift, d_above, d_below, second_normed, stats_two, affine, weight_back, first_normed)
    gathered = exchange(slabs, AXES)

    back_s, back_l, one, two, gain_one, bias_one = call(
        body(back_kernel),
        "vvvvvv",
        [("v", a.shape, F32) for a in (image_small, image_large, conv_first, conv_second)] + [f("v", 1, C), f("v", 1, C)],
        [(half, F32), ((C, LAST_LANES), F32)],
    )(gathered, pre, first_normed, stats_one, affine, dout)
    return (
        out_s, out_l, back_s, back_l,
        one, gain_one.reshape(C), bias_one.reshape(C),
        two, gain_two.reshape(C), bias_two.reshape(C),
    )


def solution(mesh):
    split_bands, everywhere = P("img", "row", None), P()
    return jax.shard_map(
        local,
        mesh=mesh,
        in_specs=(split_bands,) * 6 + (everywhere,) * 6,
        out_specs=(split_bands,) * 4 + (everywhere,) * 6,
        check_vma=False,
    )
```

```python
import functools
import math

import jax
import jax.numpy as jnp
from jax import lax
from jax.experimental import pallas as pl
from jax.experimental.pallas import tpu as pltpu
from jax.sharding import PartitionSpec as P

C = 32
HS = 32
HL = 64
HEIGHTS = (HS, HL)

norm_eps = 1e-05
map_eps = 1e-06
beta_weight = 1000.0
AXES = ("img", "row")
BLOCK = 8
LANES = BLOCK * C
TAPS = 3
DEPTH = TAPS * 128 + 256
TAP_ROWS = 128 + 2 * C
REACH = 4
ROOT = math.sqrt(2.0 / math.pi)
CUBE = 0.044715
F32 = jnp.float32
BF16 = jnp.bfloat16
VMEM_LIMIT = 32 * 1024 * 1024
BIAS, GAIN, SECOND, LEFT, HIDDEN, ONES = 0, 1, 2, 11, 20, 29
BACK_LANES = 1280
LAST_SECOND, LAST_FIRST, LAST_LANES = 2, 11, 640


class Sizes:
    def __init__(self, small, large, devices, peers):
        self.images = (small[0], large[0])
        self.rows = (small[1], large[1])
        self.blocks = (HS // BLOCK, HL // BLOCK)
        self.step = tuple(n * r for n, r in zip(self.images, self.rows))
        self.count = tuple(b * s for b, s in zip(self.blocks, self.step))
        self.edge = tuple(b * n for b, n in zip(self.blocks, self.images))
        self.start = (self.count[1], 0)
        self.rim = (self.edge[1], 0)
        self.total = sum(self.count)
        self.rims = sum(self.edge)
        self.slots = -(-sum(self.images) // 8) * 8
        self.guard = -(-max(self.images) // 8) * 8
        self.devices = devices
        self.peers = peers
        self.here = float(self.total * BLOCK)
        self.pixels = self.here * devices

    def pads(self):
        return [((TAPS, 2, self.count[k] + 2 * self.step[k], 128), F32) for k in (0, 1)]

    def chains(self, depth):
        return [((2, 2 * self.guard + (depth + 1) * self.rims, 128), F32)] * 2


def split(value):
    high = value.astype(BF16)
    return high, (value - high.astype(F32)).astype(BF16)


def dot(left, right):
    return lax.dot_general(left, right, (((1,), (0,)), ((), ())), preferred_element_type=F32)


def product(left, right):
    if left[0].shape[1] % 128:
        return dot(left[0], right[0]) + (dot(left[0], right[1]) + dot(left[1], right[0]))
    return dot(
        jnp.concatenate([left[0], left[0], left[1]], axis=1), jnp.concatenate([right[0], right[1], right[0]], axis=0)
    )


def spread(left, right):
    right = right.astype(BF16)
    return dot(jnp.concatenate(split(left), axis=1), jnp.concatenate([right, right], axis=0))


def gelu(s):
    return 0.5 * s * (1.0 + jnp.tanh(ROOT * (s + CUBE * s * s * s)))


def gelu_slope(s):
    square = s * s
    t = jnp.tanh(ROOT * s * (1.0 + CUBE * square))
    return 0.5 * (1.0 + t) + 0.5 * s * (1.0 - t * t) * ROOT * (1.0 + 3.0 * CUBE * square)


def spread_groups(row):
    row = row + pltpu.roll(row, 64, 1)
    return row + pltpu.roll(row, 32, 1)


def fold(row):
    return spread_groups(row[:, :128] + row[:, 128:])


def wide(row):
    return jnp.concatenate([row, row], axis=1)


def group_of(rows=1, lanes=128):
    return lax.broadcasted_iota(jnp.int32, (rows, lanes), 1) // C


def column_sum(value):
    return jnp.sum(value, axis=0, keepdims=True)


def send_lines(z, ref, lines):
    for n, line in enumerate(lines):
        ref[pl.ds(n, z.devices, stride=len(lines)), :] = jnp.broadcast_to(line, (z.devices, 128))


def moments(z, value, ref):
    few = min(8, z.total)
    pivot = fold(column_sum(value[:few])) / float(few * BLOCK)
    off = value - wide(pivot)
    first, second = fold(column_sum(off)), fold(column_sum(off * off))
    send_lines(z, ref, [pivot + first / z.here, second - first * first / z.here])


def merged(z, ref):
    means = ref[pl.ds(0, z.devices, stride=2), :]
    center = jnp.mean(means, axis=0, keepdims=True)
    off = means - center
    within = jnp.mean(ref[pl.ds(1, z.devices, stride=2), :], axis=0, keepdims=True)
    variance = within / z.here + jnp.mean(off * off, axis=0, keepdims=True)
    return wide(center), wide(lax.rsqrt(variance + norm_eps))


def put_halves(ref, value):
    ref[0] = value[:, :128]
    ref[1] = value[:, 128:]


def whole(ref):
    return jnp.concatenate([ref[0], ref[1]], axis=1)


def to_matrix(z, refs, half):
    for k in (0, 1):
        for j in range(z.blocks[k]):
            at = z.start[k] + j * z.step[k]
            for i in range(z.images[k]):
                for h in (0, 1):
                    half[h, pl.ds(at + i * z.rows[k], z.rows[k]), :] = refs[k][i, :, pl.ds(LANES * j + 128 * h, 128)]


def from_matrix(z, half, refs):
    for k in (0, 1):
        for j in range(z.blocks[k]):
            at = z.start[k] + j * z.step[k]
            for i in range(z.images[k]):
                for h in (0, 1):
                    refs[k][i, :, pl.ds(LANES * j + 128 * h, 128)] = half[h, pl.ds(at + i * z.rows[k], z.rows[k]), :]


def take_rims(z, half, depth, bottom, top):
    for k in (0, 1):
        for d in range(1, depth + 1):
            to_bottom = pl.ds((depth - d) * z.rims + z.rim[k], z.edge[k])
            to_top = pl.ds((d - 1) * z.rims + z.rim[k], z.edge[k])
            if d <= z.rows[k]:
                bottom[to_bottom, :] = half[pl.ds(z.start[k] + z.rows[k] - d, z.edge[k], stride=z.rows[k]), :]
                top[to_top, :] = half[pl.ds(z.start[k] + d - 1, z.edge[k], stride=z.rows[k]), :]
            else:
                bottom[to_bottom, :] = jnp.zeros((z.edge[k], 128), F32)
                top[to_top, :] = jnp.zeros((z.edge[k], 128), F32)


def inside(z, depth, above):
    at = lax.axis_index("row")
    large = lax.broadcasted_iota(jnp.int32, (z.rims, 1), 0) < z.rim[0]
    parts = []
    for n in range(depth):
        if above:
            ok = [jnp.where(at * rows >= depth - n, 1.0, 0.0) for rows in z.rows]
        else:
            ok = [jnp.where((at + 1) * rows + n + 1 <= height, 1.0, 0.0) for rows, height in zip(z.rows, HEIGHTS)]
        parts.append(jnp.where(large, ok[1], ok[0]).astype(F32))
    return jnp.concatenate(parts, axis=0)


def clear_guards(z, pads, a):
    for k in (0, 1):
        pads[k][a, 1, pl.ds(0, z.step[k]), :] = jnp.zeros((z.step[k], 128), F32)
        pads[k][a, 0, pl.ds(z.step[k] + z.count[k], z.step[k]), :] = jnp.zeros((z.step[k], 128), F32)


def fill_center(z, pads, value):
    clear_guards(z, pads, 1)
    for k in (0, 1):
        for h in (0, 1):
            pads[k][1, h, pl.ds(z.step[k], z.count[k]), :] = value[z.start[k] : z.start[k] + z.count[k], 128 * h : 128 * h + 128]


def fill_shifted(z, pads, above, below):
    for k in (0, 1):
        ref, step, count, rows = pads[k], z.step[k], z.count[k], z.rows[k]
        rim = slice(z.rim[k], z.rim[k] + z.edge[k])
        for h in (0, 1):
            lanes = slice(128 * h, 128 * h + 128)
            ref[0, h, pl.ds(step, count), :] = ref[1, h, pl.ds(step - 1, count), :]
            ref[2, h, pl.ds(step, count), :] = ref[1, h, pl.ds(step + 1, count), :]
            ref[0, h, pl.ds(step, z.edge[k], stride=rows), :] = above[rim, lanes]
            ref[2, h, pl.ds(step + rows - 1, z.edge[k], stride=rows), :] = below[rim, lanes]


def fill_pads(z, pads, value, above, below):
    fill_center(z, pads, value)
    fill_shifted(z, pads, above, below)
    for a in (0, 2):
        clear_guards(z, pads, a)


def beside(left, right):
    lane = lax.broadcasted_iota(jnp.int32, (1, 128), 1)
    middle = pltpu.roll(jnp.where(lane >= 64, left[1], right[1]), 64, 1)
    return [
        jnp.where(lane >= 96, left[0], jnp.where(lane < 32, right[0], middle)),
        jnp.where(lane >= 96, left[2], jnp.where(lane < 32, right[2], 0.0)),
    ]


def band_operand(z, pads):
    parts = ([], [])
    for k in (1, 0):
        ref, step, count = pads[k], z.step[k], z.count[k]
        low, high = ([ref[a, h, pl.ds(step, count), :] for a in range(TAPS)] for h in (0, 1))
        before = [ref[a, 1, pl.ds(0, count), :] for a in range(TAPS)]
        after = [ref[a, 0, pl.ds(2 * step, count), :] for a in range(TAPS)]
        parts[0].append(jnp.concatenate(low + beside(before, high), axis=1))
        parts[1].append(jnp.concatenate(high + beside(low, after), axis=1))
    return [jnp.concatenate(part, axis=0) for part in parts]


def rim_operand(z, chain, depth):
    m = lax.broadcasted_iota(jnp.int32, (z.rims, 1), 0)
    large = m < z.rim[0]
    has_before = jnp.where(large, m, m - z.rim[0]) >= jnp.where(large, z.images[1], z.images[0])
    has_after = m < jnp.where(large, z.rim[0] - z.images[1], z.rims - z.images[0])
    low, high, before, after = [], [], [], []
    for r in range(depth + 1):
        at = z.guard + r * z.rims
        low.append(chain[0, pl.ds(at, z.rims), :])
        high.append(chain[1, pl.ds(at, z.rims), :])
        shifted = [chain[1, pl.ds(at - images, z.rims), :] for images in z.images]
        before.append(jnp.where(has_before, jnp.where(large, shifted[1], shifted[0]), 0.0))
        shifted = [chain[0, pl.ds(at + images, z.rims), :] for images in z.images]
        after.append(jnp.where(has_after, jnp.where(large, shifted[1], shifted[0]), 0.0))
    parts = ([], [])
    for n in range(depth - 1):
        rows = slice(n, n + TAPS)
        parts[0].append(jnp.concatenate(low[rows] + beside(before[rows], high[rows]), axis=1))
        parts[1].append(jnp.concatenate(high[rows] + beside(low[rows], after[rows]), axis=1))
    return [jnp.concatenate(part, axis=0) for part in parts]


def times(parts, weight):
    left = jnp.concatenate([part[h] for h in (0, 1) for part in parts], axis=0)
    both = jnp.concatenate([weight_matrix(weight.at[0]), weight_matrix(weight.at[1])], axis=1)
    result = dot(jnp.concatenate(split(left), axis=1), jnp.concatenate([both, both], axis=0))
    result = result[:, :128] + result[:, 128:]
    rows = result.shape[0] // 2
    return jnp.concatenate([result[:rows], result[rows:]], axis=1)


def convolve(z, own, above, below, depth, pads, chains, weight):
    r = z.rims
    fill_pads(z, pads, own, above[(depth - 1) * r :], below[:r])
    parts = [band_operand(z, pads)]
    if depth > 1:
        for side, (rim, chain) in enumerate(zip((above, below), chains)):
            rim_at, own_at = (z.guard, z.guard + depth * r) if side == 0 else (z.guard + r, z.guard)
            for h in (0, 1):
                chain[h, pl.ds(rim_at, depth * r), :] = rim[:, 128 * h : 128 * h + 128]
                for k in (0, 1):
                    row = z.step[k] + (0 if side == 0 else z.rows[k] - 1)
                    chain[h, pl.ds(own_at + z.rim[k], z.edge[k]), :] = pads[k][1, h, pl.ds(row, z.edge[k], stride=z.rows[k]), :]
            parts.append(rim_operand(z, chain, depth))
    result = times(parts, weight)
    n = z.total + (depth - 1) * r
    return result[: z.total], result[z.total : n], result[n:]


def image_sums(z, value):
    slot = lax.broadcasted_iota(jnp.int32, (z.slots, 1), 0)
    sums = jnp.zeros((z.slots, 128), F32)
    for k in (0, 1):
        line = value[z.start[k] : z.start[k] + z.step[k]]
        for j in range(1, z.blocks[k]):
            at = z.start[k] + j * z.step[k]
            line = line + value[at : at + z.step[k]]
        image = lax.broadcasted_iota(jnp.int32, (z.step[k], 1), 0) // z.rows[k]
        for i in range(z.images[k]):
            sums = jnp.where(slot == i + k * z.images[0], column_sum(jnp.where(image == i, line, 0.0)), sums)
    return sums


def image_rows(z, values, rims):
    parts = []
    for k in (1, 0):
        image = lax.broadcasted_iota(jnp.int32, (z.step[k], 1), 0) // z.rows[k]
        line = jnp.zeros((z.step[k], 128), F32)
        for i in range(z.images[k]):
            at = i + k * z.images[0]
            line = jnp.where(image == i, values[at : at + 1], line)
        parts += [line] * z.blocks[k]
    if rims:
        m = lax.broadcasted_iota(jnp.int32, (z.rims, 1), 0)
        image = jnp.where(m < z.rim[0], z.images[0] + m % z.images[1], (m - z.rim[0]) % z.images[0])
        line = jnp.zeros((z.rims, 128), F32)
        for at in range(sum(z.images)):
            line = jnp.where(image == at, values[at : at + 1], line)
        parts += [line] * rims
    return jnp.concatenate(parts, axis=0)


def channel_mean():
    a = lax.broadcasted_iota(jnp.int32, (LANES, 128), 0) // C
    b = lax.broadcasted_iota(jnp.int32, (LANES, 128), 1) % 64
    return jnp.where(a == b, 1.0 / C, 0.0).astype(F32)


def to_channels():
    a = lax.broadcasted_iota(jnp.int32, (128, LANES), 0)
    b = lax.broadcasted_iota(jnp.int32, (128, LANES), 1) // C
    return jnp.where(a == b, 1.0, 0.0).astype(F32)


def attention(value):
    return spread(value * value, channel_mean())


def pieces(source, target):
    return [(source.at[n], target.at[n]) for n in range(source.shape[0])]


def copies_of(pairs, sems, first=0):
    return [pltpu.make_async_copy(a, b, sems.at[first + n]) for n, (a, b) in enumerate(pairs)]


def start_all(copies):
    for copy in copies:
        copy.start()


def wait_all(copies):
    for copy in copies:
        copy.wait()


def start_kernel(z, small, large, up_s, up_l, t_s, t_l, x, bottom, top, copies, raw, half, more, sems):
    images = [(small, raw[0])] + pieces(large, raw[1])
    rest = [(up_s, raw[2])] + pieces(up_l, raw[3]) + [(t_s, raw[4]), (t_l, raw[5])]
    loads = copies_of(images + rest, sems)
    start_all(loads)
    r, n = z.rims, REACH * z.rims
    tail = n + 2 * r
    for ref in (bottom, top):
        ref[pl.ds(tail, z.slots), :] = jnp.zeros((z.slots, LANES), F32)
    wait_all(loads[: len(images)])
    to_matrix(z, raw[:2], half)
    value = whole(half)
    x[...] = value
    moments(z, value, copies)
    for h in (0, 1):
        lanes = pl.ds(128 * h, 128)
        take_rims(z, half.at[h], REACH, bottom.at[pl.ds(0, n), lanes], top.at[pl.ds(0, n), lanes])
    wait_all(loads[len(images) :])
    to_matrix(z, raw[2:4], more)
    for h in (0, 1):
        lanes = pl.ds(128 * h, 128)
        take_rims(z, more.at[h], 2, bottom.at[pl.ds(n, 2 * r), lanes], top.at[pl.ds(n, 2 * r), lanes])
    for k in (0, 1):
        width, rows = HEIGHTS[k], z.rows[k]
        for i in range(z.images[k]):
            slot = pl.ds(tail + i + k * z.images[0], 1)
            for d in range(min(2, rows)):
                bottom[slot, pl.ds(128 * (1 - d), width)] = raw[4 + k][i, pl.ds(rows - 1 - d, 1), :]
                top[slot, pl.ds(128 * d, width)] = raw[4 + k][i, pl.ds(d, 1), :]


def banded(taps, ref):
    row = lax.broadcasted_iota(jnp.int32, (128, 128), 0) // C
    lane = group_of(128)
    for a in range(TAPS):
        main = jnp.zeros((128, 128), F32)
        for b in range(TAPS):
            main = jnp.where(row - lane + 1 == b, taps[a][b], main)
        before = jnp.where(lane[:C] == 0, taps[a][0][:C], 0.0)
        after = jnp.where(lane[:C] == 3, taps[a][2][:C], 0.0)
        for n, part in enumerate(split(jnp.concatenate([main, before, after], axis=0))):
            ref[n, pl.ds(a * TAP_ROWS, TAP_ROWS), :] = part


def weight_matrix(ref):
    main = [ref[pl.ds(a * TAP_ROWS, 128), :] for a in range(TAPS)]
    before, after = ([ref[pl.ds(a * TAP_ROWS + 128 + n * C, C), :] for a in range(TAPS)] for n in (0, 1))
    return jnp.concatenate(
        main + [after[0], before[1], after[1], before[0], after[2], jnp.zeros((2 * C, 128), BF16), before[2]], axis=0
    )


def prepare_kernel(z, first, second, up_s, up_l, t_s, t_l, g1, b1, g2, b2, x, w1, w2, weights, affine, upstream, teacher, x_copy, raw, kept, kept_u, rows, half, sems):
    targets = tuple(raw) + tuple(rows.at[pl.ds(n, 1), :] for n in range(4))
    refs = (first, second, up_s, up_l, t_s, t_l, g1, b1, g2, b2)
    loads = [pltpu.make_async_copy(a, b, sems.at[n]) for n, (a, b) in enumerate(zip(refs, targets))]
    start_all(loads)
    stores = [pltpu.make_async_copy(x, x_copy, sems.at[13])]
    stores[0].start()
    wait_all(loads)
    to_matrix(z, raw[2:4], half)
    kept_u[...] = whole(half)
    stores.append(pltpu.make_async_copy(kept_u, upstream, sems.at[10]))
    stores[1].start()
    for n, (source, forward) in enumerate(zip(raw[:2], (w1, w2))):
        tiles = []
        for a in range(TAPS):
            line = [jnp.concatenate([source[a, b]] * 4, axis=1) for b in range(TAPS)]
            tiles.append([jnp.concatenate([tap] * 4, axis=0) for tap in line])
        turned = [[tiles[TAPS - 1 - a][TAPS - 1 - b].T for b in range(TAPS)] for a in range(TAPS)]
        banded(tiles, forward)
        banded(turned, kept.at[n])
        stores.append(pltpu.make_async_copy(kept.at[n], weights.at[n], sems.at[11 + n]))
        stores[-1].start()
    affine[...] = jnp.concatenate([rows[...]] * BLOCK, axis=1)
    teacher[...] = jnp.zeros(teacher.shape, F32)
    for k, ref in ((0, raw[4]), (1, raw[5])):
        for i in range(z.images[k]):
            line = ref[i]
            for j in range(z.blocks[k]):
                at = z.start[k] + j * z.step[k] + i * z.rows[k]
                for lane in (0, 64):
                    teacher[pl.ds(at, z.rows[k]), pl.ds(lane, BLOCK)] = line[:, j * BLOCK : (j + 1) * BLOCK]
    wait_all(stores)


def normed_by(stats):
    return lambda v: (v - stats[0:1]) * stats[1:2]


def activation(center, scale, gain, bias):
    factor = scale * gain
    offset = bias - center * factor
    return lambda v: gelu(v * factor + offset)


def first_kernel(z, x, above, below, gathered, affine, weight, hidden, h_above, h_below, stats, copies, pads, chains):
    n = REACH * z.rims
    center, scale = merged(z, gathered)
    act = activation(center, scale, affine[0:1], affine[1:2])
    own = act(x[...])
    up, down = act(above[pl.ds(0, n), :]) * inside(z, 4, True), act(below[pl.ds(0, n), :]) * inside(z, 4, False)
    own, up, down = convolve(z, own, up, down, 4, pads, chains, weight)
    moments(z, own, copies)
    hidden[...] = own
    h_above[...] = up
    h_below[...] = down
    stats[0:1] = center
    stats[1:2] = scale


def second_kernel(z, hidden, h_above, h_below, gathered, affine, weight, x, x_above, x_below, teacher, out, o_above, o_below, near, stats, copies, pads, chains):
    center, scale = merged(z, gathered)
    act = activation(center, scale, affine[2:3], affine[3:4])
    r = z.rims
    own = act(hidden[...])
    up, down = act(h_above[...]) * inside(z, 3, True), act(h_below[...]) * inside(z, 3, False)
    own, up, down = convolve(z, own, up, down, 3, pads, chains, weight)
    own = x[...] + own
    amap = attention(own)
    lane = lax.broadcasted_iota(jnp.int32, (1, 128), 1)
    sums = image_sums(z, amap * jnp.where(lane < 64, amap, teacher[...]))
    copies[...] = jnp.concatenate([sums] * z.peers, axis=0)
    out[...] = own
    o_above[...] = x_above[pl.ds(2 * r, 2 * r), :] + up
    o_below[...] = x_below[pl.ds(0, 2 * r), :] + down
    near[0] = h_above[pl.ds(2 * r, r), :]
    near[1] = h_below[pl.ds(0, r), :]
    stats[0:1] = center
    stats[1:2] = scale


def tap_rows(q):
    return 128 + 3 * C if q < 0 else 128 if q == 4 else q * C


def tap_product(z, operand, own, above, below, pads):
    fill_center(z, pads, own)
    fill_shifted(z, pads, above, below)
    columns = []
    for a in range(TAPS):
        columns.append(
            jnp.concatenate([pads[k][TAPS - 1 - a, h, pl.ds(z.step[k], z.count[k]), :] for h in (0, 1) for k in (1, 0)], axis=0)
        )
    result = dot(jnp.concatenate(operand, axis=0), jnp.concatenate(split(jnp.concatenate(columns, axis=1)), axis=1))
    rows, lanes = operand[0].shape[0], TAPS * 128
    high, low = result[:rows], result[rows:]
    return (high[:, :lanes] + high[:, lanes:]) + (low[:, :lanes] + low[:, lanes:])


def tap_sums(result, tiles, first_group):
    group = group_of()
    for a in range(TAPS):
        for b in range(TAPS):
            total = None
            for p in range(4):
                at = tap_rows(p + b - 1)
                part = result[at : at + C, 128 * a : 128 * a + 128]
                total = part if total is None else jnp.where(group == p, part, total)
            tile, slot = divmod(first_group + a * TAPS + b, 4)
            tiles[tile] = jnp.where(group == slot, spread_groups(total), tiles[tile])


def tap_counts(z, turned, tiles, first_group):
    group = group_of()
    m = lax.broadcasted_iota(jnp.int32, (1, 2 * z.total), 1) % z.total
    row = jnp.where(m < z.start[0], m % z.rows[1], (m - z.start[0]) % z.rows[0])
    height = jnp.where(m < z.start[0], z.rows[1], z.rows[0])
    at = lax.axis_index("row")
    lost = {
        0: (row == height - 1) & (at == z.peers - 1),
        2: (row == 0) & (at == 0),
    }
    for a in range(TAPS):
        column = jnp.sum(jnp.where(lost[a], 0.0, turned) if a in lost else turned, axis=1, keepdims=True)
        for b in range(TAPS):
            total = sum(column[tap_rows(p + b - 1) : tap_rows(p + b - 1) + C] for p in range(4))
            tile, slot = divmod(first_group + a * TAPS + b, 4)
            tiles[tile] = jnp.where(group == slot, total, tiles[tile])


def turned_operand(z, value, pads, kept):
    fill_center(z, pads, value)
    lane = lax.broadcasted_iota(jnp.int32, (1, 128), 1)
    halves = ([], [])
    for k in (1, 0):
        ref, step, count = pads[k], z.step[k], z.count[k]
        low, high = ref[1, 0, pl.ds(step, count), :], ref[1, 1, pl.ds(step, count), :]
        before, after = ref[1, 1, pl.ds(0, count), :], ref[1, 0, pl.ds(2 * step, count), :]
        for part, main, left, right in ((halves[0], low, before, high), (halves[1], high, low, after)):
            part.append(jnp.concatenate([main, jnp.where(lane >= 96, left, jnp.where(lane < 32, right, 0.0))], axis=1))
    turned = jnp.concatenate(halves[0] + halves[1], axis=0).T
    parts = split(turned)
    for n in (0, 1):
        kept[n] = parts[n]
    return turned


def first_operand_kernel(z, x, hidden, h_above, h_below, above, below, stats, affine, teacher, upstream, weights, left, packed, teachers, spread_u, near_u, pads, chains, kept, kept_w, kept_u, pixels, kept_t, kept_c, kept_packed, sems):
    r, own = z.rims, pl.ds(0, z.total)
    loads = [pltpu.make_async_copy(upstream, kept_u.at[own, :], sems.at[0]), pltpu.make_async_copy(weights.at[1], kept_w, sems.at[1])]
    start_all(loads)
    act = activation(stats[0:1], stats[1:2], affine[0:1], affine[1:2])
    value = turned_operand(z, act(x[...]), pads, kept)
    stores = [pltpu.make_async_copy(kept, left, sems.at[2])]
    stores[0].start()
    tiles = [jnp.zeros((C, 128), F32) for _ in range(BACK_LANES // 128)]
    tap_counts(z, value, tiles, ONES)
    result = tap_product(
        z, (kept[0], kept[1]), hidden[...], h_above[pl.ds(2 * r, r), :] * inside(z, 1, True), h_below[pl.ds(0, r), :] * inside(z, 1, False), pads
    )
    tap_sums(result, tiles, HIDDEN)
    kept_packed[...] = jnp.concatenate(tiles, axis=1)
    stores.append(pltpu.make_async_copy(kept_packed, packed, sems.at[6]))
    stores[1].start()
    pixels[own, :] = teacher[...]
    pixels[pl.ds(z.total, 4 * r), :] = jnp.zeros((4 * r, 128), F32)
    n = (REACH + 2) * r
    for side, ref in enumerate((above, below)):
        for d in (0, 1):
            for k in (0, 1):
                line = ref[pl.ds(n + k * z.images[0], z.images[k]), pl.ds(128 * d, 128)]
                for j in range(z.blocks[k]):
                    at = z.total + (2 * side + d) * r + z.rim[k] + j * z.images[k]
                    pixels[pl.ds(at, z.images[k]), pl.ds(0, BLOCK)] = line[:, j * BLOCK : (j + 1) * BLOCK]
    kept_t[...] = spread(pixels[...], to_channels())
    stores.append(pltpu.make_async_copy(kept_t, teachers, sems.at[3]))
    stores[2].start()
    n = REACH * r
    up, down = above[pl.ds(n, 2 * r), :] * inside(z, 2, True), below[pl.ds(n, 2 * r), :] * inside(z, 2, False)
    kept_u[pl.ds(z.total, r), :] = up[r:]
    kept_u[pl.ds(z.total + r, r), :] = down[:r]
    wait_all(loads)
    stores.append(pltpu.make_async_copy(kept_u, near_u, sems.at[5]))
    stores[3].start()
    kept_c[...] = jnp.concatenate(convolve(z, kept_u[own, :], up, down, 2, pads, chains, kept_w), axis=0)
    stores.append(pltpu.make_async_copy(kept_c, spread_u, sems.at[4]))
    stores[4].start()
    wait_all(stores)


def second_operand_kernel(z, hidden, near, stats, affine, out, o_above, o_below, teachers, spread_u, near_u, weights, out_copy, hidden_copy, left, shifts, by_map, by_teacher, up, pads, chains, kept_t, kept_u, kept_w, kept_s, sems):
    r, total = z.rims, z.total
    loads = [
        pltpu.make_async_copy(teachers, kept_t, sems.at[0]),
        pltpu.make_async_copy(weights.at[1], kept_w, sems.at[1]),
        pltpu.make_async_copy(spread_u, kept_u, sems.at[2]),
    ]
    start_all(loads)
    stores = [
        pltpu.make_async_copy(out, out_copy, sems.at[4]),
        pltpu.make_async_copy(hidden, hidden_copy.at[pl.ds(0, total), :], sems.at[7]),
        pltpu.make_async_copy(near.at[0], hidden_copy.at[pl.ds(total, r), :], sems.at[8]),
        pltpu.make_async_copy(near.at[1], hidden_copy.at[pl.ds(total + r, r), :], sems.at[9]),
        pltpu.make_async_copy(near_u, up, sems.at[10]),
    ]
    start_all(stores)
    normed = normed_by(stats)(jnp.concatenate([hidden[...], near[0], near[1]], axis=0))
    shifted = normed * affine[2:3] + affine[3:4]
    turned_operand(z, gelu(shifted[:total]), pads, left)
    ones = jnp.ones((total, 1), F32)
    masks = jnp.concatenate([ones, inside(z, 1, True), inside(z, 1, False)], axis=0)
    slopes = gelu_slope(shifted) * masks
    o = jnp.concatenate([out[...], o_above[...] * inside(z, 2, True), o_below[...] * inside(z, 2, False)], axis=0)
    for_map = spread(attention(o), to_channels()) * o
    wait_all(loads)
    for_teacher = kept_t[...] * o
    kept_s[0] = kept_u[...] * slopes
    stores += copies_of(pieces(kept_s, shifts), sems, 11)
    stores[-3].start()
    for n, value, ref in ((1, for_map, by_map), (2, for_teacher, by_teacher)):
        own, before, after = value[:total], value[total : total + 2 * r], value[total + 2 * r :]
        ref[...] = jnp.concatenate([own, before[r:], after[:r]], axis=0)
        kept_s[n] = jnp.concatenate(convolve(z, own, before, after, 2, pads, chains, kept_w), axis=0) * slopes
        stores[n - 3].start()
    wait_all(stores)


def upstream_kernel(z, gathered, up, shifts, left_1, left_2, packed, by_map, by_teacher, hidden, stats, dout, dshift, d_above, d_below, slabs, kept_s, kept_left, kept_h, kept_packed, pads, more_pads, sems):
    r, total = z.rims, z.total
    loads = copies_of(
        pieces(shifts, kept_s) + pieces(left_1, kept_left) + [(hidden.at[pl.ds(0, total), :], kept_h), (packed, kept_packed)], sems
    )
    start_all(loads)
    lane = lax.broadcasted_iota(jnp.int32, (z.slots, 128), 1)
    sums = sum(gathered[pl.ds(n * z.slots, z.slots), :] for n in range(z.peers))
    square = jnp.sum(jnp.where(lane < 64, sums, 0.0), axis=1, keepdims=True)
    cross = jnp.sum(jnp.where(lane < 64, 0.0, sums), axis=1, keepdims=True)
    inverse = lax.rsqrt(square + map_eps)
    inner = beta_weight * (square * inverse - cross) * inverse
    shape = (z.slots, 128)
    for_map = (beta_weight - inner) * inverse * inverse * (2.0 / C)
    for_teacher = beta_weight * inverse * (2.0 / C)
    for_map, for_teacher = (wide(image_rows(z, jnp.broadcast_to(v, shape), 2)) for v in (for_map, for_teacher))
    value = up[...] + for_map * by_map[...] - for_teacher * by_teacher[...]
    dout[...] = value[:total]
    wait_all(loads[:3])
    shift = kept_s[0] + for_map * kept_s[1] - for_teacher * kept_s[2]
    pre, above, below = shift[:total], shift[total : total + r], shift[total + r :]
    dshift[...] = pre
    d_above[...] = above
    d_below[...] = below
    second = tap_product(z, (left_2[0], left_2[1]), value[:total], value[total : total + r], value[total + r :], pads)
    wait_all(loads[3:5])
    first = tap_product(z, (kept_left[0], kept_left[1]), pre, above, below, more_pads)
    wait_all(loads[5:])
    normed = normed_by(stats)(kept_h[...])
    tiles = [kept_packed[:, 128 * n : 128 * n + 128] for n in range(BACK_LANES // 128)]
    group = group_of()
    tiles[0] = jnp.where(group == BIAS, fold(column_sum(pre)), jnp.where(group == GAIN, fold(column_sum(pre * normed)), tiles[0]))
    tap_sums(second, tiles, SECOND)
    tap_sums(first, tiles, LEFT)
    line = jnp.concatenate(tiles, axis=1)
    for d in range(z.devices):
        slabs[d] = line[d % C : d % C + 1]


def write_kernel(z, out, x, hidden, weights, first_stats, stats, order, out_s, out_l, first_normed, normed, weight, kept, kept_x, kept_h, half, sems):
    loads = [pltpu.make_async_copy(a, b, sems.at[n]) for n, (a, b) in enumerate(((out, kept), (x, kept_x), (hidden, kept_h), (weights.at[0], weight)))]
    start_all(loads)
    loads[0].wait()
    put_halves(half, kept[...])
    from_matrix(z, half, (out_s, out_l))
    loads[1].wait()
    first_normed[...] = normed_by(first_stats)(kept_x[...])
    loads[2].wait()
    normed[...] = normed_by(stats)(kept_h[...])
    loads[3].wait()


def norm_sums(total):
    group = group_of()
    return [wide(spread_groups(jnp.where(group == n, total[:, :128], 0.0))) for n in (BIAS, GAIN)]


def hidden_kernel(z, gathered, dshift, d_above, d_below, second_normed, stats, affine, weight, first_normed, pre_ref, gain_out, bias_out, slabs, pads):
    total = jnp.sum(gathered[...], axis=0)
    bias_sum, gain_sum = norm_sums(total)
    bias_out[...] = bias_sum[:, :C]
    gain_out[...] = gain_sum[:, :C]
    bias_mean, gain_mean = bias_sum / z.pixels, gain_sum / z.pixels
    factor = affine[2:3] * stats[1:2]
    r, total_rows = z.rims, z.total

    def back(d, normed):
        return factor * (d - bias_mean - normed * gain_mean)

    own = back(dshift[...], second_normed[pl.ds(0, total_rows), :])
    up = back(d_above[...], second_normed[pl.ds(total_rows, r), :]) * inside(z, 1, True)
    down = back(d_below[...], second_normed[pl.ds(total_rows + r, r), :]) * inside(z, 1, False)
    grad, _, _ = convolve(z, own, up, down, 1, pads, None, weight)
    normed = first_normed[...]
    pre = grad * gelu_slope(normed * affine[0:1] + affine[1:2])
    pre_ref[...] = pre
    lane = lax.broadcasted_iota(jnp.int32, (1, 128), 1)
    taps = TAPS * TAPS * C

    def along(row):
        return jnp.concatenate([row[:, :128]] * 3, axis=1)[:, :taps]

    second, left, against, ones = (total[:, n * C : n * C + taps] for n in (SECOND, LEFT, HIDDEN, ONES))
    against = along(stats[1:2]) * (against - along(stats[0:1]) * ones)
    first = along(factor) * (left - along(bias_mean) * ones - along(gain_mean) * against)
    sums = jnp.where(lane < C, fold(column_sum(pre)), fold(column_sum(pre * normed)))
    line = jnp.concatenate([sums[:, : 2 * C], second, first], axis=1)
    slabs[...] = jnp.broadcast_to(line[None], slabs.shape)


def terms_kernel(z, pre, normed, stats, affine, dout, base_s, base_l, slope_s, slope_l, half, more):
    factor = affine[0:1] * stats[1:2]
    put_halves(half, dout[...] + factor * pre[...])
    from_matrix(z, half, (base_s, base_l))
    put_halves(more, factor * normed[...])
    from_matrix(z, more, (slope_s, slope_l))


def back_kernel(z, gathered, base_s, base_l, slope_s, slope_l, stats, affine, back_s, back_l, one, two, gain_out, bias_out, lines):
    bias_sum, gain_sum = norm_sums(jnp.sum(gathered[:, :, pl.ds(0, 128)], axis=0))
    bias_out[...] = bias_sum[:, :C]
    gain_out[...] = gain_sum[:, :C]
    offset = affine[0:1] * stats[1:2] * (bias_sum / z.pixels)
    factor = gain_sum / z.pixels
    for k, (base, slope, back) in enumerate(((base_s, slope_s, back_s), (base_l, slope_l, back_l))):
        line = [jnp.concatenate([v] * z.blocks[k], axis=1) for v in (offset, factor)]
        for i in range(z.images[k]):
            back[i] = base[i] - line[0] - slope[i] * line[1]
    for d in range(C):
        lines[pl.ds(d, 1), :] = gathered[d]
    for ref, group in ((two, LAST_SECOND), (one, LAST_FIRST)):
        for a in range(TAPS):
            for b in range(TAPS):
                at = (group + a * TAPS + b) * C
                ref[a, b] = lines[:, pl.ds(at, C)]


def call(body, ins, outs, scratch=(), sems=0):
    space = {"v": pltpu.VMEM, "h": pltpu.HBM, "V": pltpu.VMEM}
    shapes = []
    for item in scratch:
        if isinstance(item, list):
            shapes.append([pltpu.VMEM(*s) for s in item])
        else:
            shapes.append(pltpu.VMEM(*item))
    if sems:
        shapes.append(pltpu.SemaphoreType.DMA((sems,)))
    run = pl.pallas_call(
        body,
        out_shape=[jax.ShapeDtypeStruct(shape, kind) if s == "v" else space[s](shape, kind) for s, shape, kind in outs],
        in_specs=[pl.BlockSpec(memory_space=space[s]) for s in ins],
        out_specs=[pl.BlockSpec(memory_space=space[s]) for s, _, _ in outs],
        scratch_shapes=shapes,
        compiler_params=pltpu.CompilerParams(vmem_limit_bytes=VMEM_LIMIT),
    )
    return lambda *args: run(
        *(pltpu.with_memory_space_constraint(arg, pltpu.HBM) if s == "h" else arg for s, arg in zip(ins, args))
    )


def exchange(lines, axes):
    shape = lines.shape
    if len(shape) == 2:
        lines = lines.reshape(math.prod(lax.axis_size(axis) for axis in axes), -1, 128)
    return lax.all_to_all(lines, axes, 0, 0, tiled=True).reshape(shape)


def beyond(z, bottom, top, depths):
    hops = max(-(-depth // rows) for rows in z.rows for depth in depths)
    above, below = [], []
    for hop in range(1, hops + 1):
        above.append(lax.ppermute(bottom, "row", [(i, i + hop) for i in range(z.peers - hop)]))
        below.append(lax.ppermute(top, "row", [(i + hop, i) for i in range(z.peers - hop)]))
    if hops == 1:
        return above[0], below[0]
    up, down = [], []
    base = 0
    for depth in depths:
        for n in range(depth):
            for k in (1, 0):
                hop, back = divmod(depth - 1 - n, z.rows[k])
                at = base + (depth - 1 - back) * z.rims + z.rim[k]
                up.append(above[hop][at : at + z.edge[k]])
                hop, back = divmod(n, z.rows[k])
                at = base + back * z.rims + z.rim[k]
                down.append(below[hop][at : at + z.edge[k]])
        base += depth * z.rims
    up.append(jnp.concatenate([pixel_rows(z, above, base, 1, 1), pixel_rows(z, above, base, 0, 1)], axis=1))
    down.append(jnp.concatenate([pixel_rows(z, below, base, 0, 0), pixel_rows(z, below, base, 1, 0)], axis=1))
    return jnp.concatenate(up, axis=0), jnp.concatenate(down, axis=0)


def pixel_rows(z, bands, base, distance, last):
    lines = []
    for k in (0, 1):
        hop, back = divmod(distance, z.rows[k])
        at = base + k * z.images[0]
        half = 128 * abs(last - back)
        lines.append(bands[hop][at : at + z.images[k], half : half + 128])
    lines.append(jnp.zeros((z.slots - sum(z.images), 128), F32))
    return jnp.concatenate(lines, axis=0)


def local(
    image_small, image_large, teacher_small, teacher_large, upstream_small, upstream_large,
    conv_first, gain_first, bias_first, conv_second, gain_second, bias_second,
):
    peers = lax.axis_size("row")
    devices = lax.axis_size("img") * peers
    z = Sizes(image_small.shape, image_large.shape, devices, peers)
    body = lambda function: functools.partial(function, z)
    r = z.rims
    full, half, pair = (z.total, LANES), (2, z.total, 128), (2 * devices, 128)
    weight, left = (2, TAPS * TAP_ROWS, 128), (2, 256, 2 * z.total)
    images = [image_small, image_large, upstream_small, upstream_large, teacher_small, teacher_large]
    f = lambda space, *shape: (space, shape, F32)
    depths = (REACH, 2)
    rim_rows = sum(depths) * r + z.slots

    x, bottom, top, copies = call(
        body(start_kernel),
        "hhhhhh",
        [("v", full, F32), f("v", rim_rows, LANES), f("v", rim_rows, LANES), ("V", pair, F32)],
        [[(a.shape, F32) for a in images], (half, F32), (half, F32)],
        4 + 2 * z.images[1],
    )(*images)
    gathered = exchange(copies, AXES)
    above, below = beyond(z, bottom, top, depths)
    params = [conv_first, conv_second] + images[2:]
    w1, w2, weights, affine, upstream, teacher, x_copy = call(
        body(prepare_kernel),
        "hhhhhhhhhhv",
        [("v", weight, BF16), ("v", weight, BF16), ("h", (2,) + weight, BF16), f("v", 4, LANES), ("h", full, F32), f("v", z.total, 128), ("h", full, F32)],
        [[(a.shape, F32) for a in params], ((2,) + weight, BF16), (full, F32), ((4, C), F32), (half, F32)],
        14,
    )(*params, *(v.reshape(1, C) for v in (gain_first, bias_first, gain_second, bias_second)), x)

    hidden, h_above, h_below, stats_one, copies = call(
        body(first_kernel),
        "vvvvvv",
        [("v", full, F32), f("v", 3 * r, LANES), f("v", 3 * r, LANES), f("v", 2, LANES), ("V", pair, F32)],
        [z.pads(), z.chains(4)],
    )(x, above, below, gathered, affine, w1)
    gathered = exchange(copies, AXES)
    extended, near_rows = z.total + 4 * r, z.total + 2 * r
    left_one, packed, teachers, spread_u, near_u = call(
        body(first_operand_kernel),
        "vvvvvvvvvhh",
        [("h", left, BF16), f("h", C, BACK_LANES), f("h", extended, LANES), f("h", near_rows, LANES), f("h", near_rows, LANES)],
        [
            z.pads(), z.chains(2), (left, BF16), (weight, BF16), ((near_rows, LANES), F32), ((extended, 128), F32),
            ((extended, LANES), F32), ((near_rows, LANES), F32), ((C, BACK_LANES), F32),
        ],
        7,
    )(x, hidden, h_above, h_below, above, below, stats_one, affine, teacher, upstream, weights)
    gathered, near_u = lax.optimization_barrier((gathered, near_u))

    map_shape = (peers * z.slots, 128)
    out, o_above, o_below, near, stats_two, copies = call(
        body(second_kernel),
        "vvvvvvvvvv",
        [("v", full, F32), f("v", 2 * r, LANES), f("v", 2 * r, LANES), f("v", 2, r, LANES), f("v", 2, LANES), ("V", map_shape, F32)],
        [z.pads(), z.chains(3)],
    )(hidden, h_above, h_below, gathered, affine, w2, x, above, below, teacher)
    gathered = exchange(copies, ("row",))
    out_copy, hidden_copy, left_two, shifts, by_map, by_teacher, up = call(
        body(second_operand_kernel),
        "vvvvvvvhhhh",
        [
            ("h", full, F32), f("h", near_rows, LANES), ("v", left, BF16), f("h", 3, near_rows, LANES),
            f("v", near_rows, LANES), f("v", near_rows, LANES), f("v", near_rows, LANES),
        ],
        [
            z.pads(), z.chains(2), ((extended, LANES), F32), ((near_rows, LANES), F32), (weight, BF16),
            ((3, near_rows, LANES), F32),
        ],
        14,
    )(hidden, near, stats_two, affine, out, o_above, o_below, teachers, spread_u, near_u, weights)

    dout, dshift, d_above, d_below, slabs = call(
        body(upstream_kernel),
        "vvhhvhvvhv",
        [("v", full, F32), ("v", full, F32), f("v", r, LANES), f("v", r, LANES), f("V", devices, 1, BACK_LANES)],
        [((3, near_rows, LANES), F32), (left, BF16), (full, F32), ((C, BACK_LANES), F32), z.pads(), z.pads()],
        7,
    )(gathered, up, shifts, left_one, left_two, packed, by_map, by_teacher, hidden_copy, stats_two)
    gathered = exchange(slabs, AXES)
    out_s, out_l, first_normed, second_normed, weight_back = call(
        body(write_kernel),
        "hhhhvvv",
        [("v", image_small.shape, F32), ("v", image_large.shape, F32), ("v", full, F32), f("v", near_rows, LANES), ("v", weight, BF16)],
        [(full, F32), (full, F32), ((near_rows, LANES), F32), (half, F32)],
        4,
    )(out_copy, x_copy, hidden_copy, weights, stats_one, stats_two, d_above)

    pre, gain_two, bias_two, slabs = call(
        body(hidden_kernel),
        "vvvvvvvvv",
        [("v", full, F32), f("v", 1, C), f("v", 1, C), f("V", devices, 1, LAST_LANES)],
        [z.pads()],
    )(gathered, dshift, d_above, d_below, second_normed, stats_two, affine, weight_back, first_normed)
    gathered = exchange(slabs, AXES)

    terms = call(
        body(terms_kernel), "vvvvv", [("v", a.shape, F32) for a in images[:2] * 2], [(half, F32), (half, F32)]
    )(pre, first_normed, stats_one, affine, dout)
    back_s, back_l, one, two, gain_one, bias_one = call(
        body(back_kernel),
        "vvvvvvv",
        [("v", a.shape, F32) for a in (image_small, image_large, conv_first, conv_second)] + [f("v", 1, C), f("v", 1, C)],
        [((C, LAST_LANES), F32)],
    )(gathered, *terms, stats_one, affine)
    return (
        out_s, out_l, back_s, back_l,
        one, gain_one.reshape(C), bias_one.reshape(C),
        two, gain_two.reshape(C), bias_two.reshape(C),
    )


def solution(mesh):
    split_bands, everywhere = P("img", "row", None), P()
    return jax.shard_map(
        local,
        mesh=mesh,
        in_specs=(split_bands,) * 6 + (everywhere,) * 6,
        out_specs=(split_bands,) * 4 + (everywhere,) * 6,
        check_vma=False,
    )
```

```python
import functools
import math

import jax
import jax.numpy as jnp
from jax import lax
from jax.experimental import pallas as pl
from jax.experimental.pallas import tpu as pltpu
from jax.sharding import PartitionSpec as P

C = 32
HS = 32
HL = 64
HEIGHTS = (HS, HL)

norm_eps = 1e-05
map_eps = 1e-06
beta_weight = 1000.0
AXES = ("img", "row")
BLOCK = 8
LANES = BLOCK * C
TAPS = 3
DEPTH = TAPS * 128 + 256
TAP_ROWS = 128 + 2 * C
REACH = 4
ROOT = math.sqrt(2.0 / math.pi)
CUBE = 0.044715
F32 = jnp.float32
BF16 = jnp.bfloat16
VMEM_LIMIT = 32 * 1024 * 1024
BIAS, GAIN, SECOND, LEFT, HIDDEN, ONES = 0, 1, 2, 11, 20, 29
BACK_LANES = 1280
LAST_SECOND, LAST_FIRST, LAST_LANES = 2, 11, 640


class Sizes:
    def __init__(self, small, large, devices, peers):
        self.images = (small[0], large[0])
        self.rows = (small[1], large[1])
        self.blocks = (HS // BLOCK, HL // BLOCK)
        self.step = tuple(n * r for n, r in zip(self.images, self.rows))
        self.count = tuple(b * s for b, s in zip(self.blocks, self.step))
        self.edge = tuple(b * n for b, n in zip(self.blocks, self.images))
        self.start = (self.count[1], 0)
        self.rim = (self.edge[1], 0)
        self.total = sum(self.count)
        self.rims = sum(self.edge)
        self.slots = -(-sum(self.images) // 8) * 8
        self.guard = -(-max(self.images) // 8) * 8
        self.devices = devices
        self.peers = peers
        self.here = float(self.total * BLOCK)
        self.pixels = self.here * devices

    def pads(self):
        return [((TAPS, 2, self.count[k] + 2 * self.step[k], 128), F32) for k in (0, 1)]

    def chains(self, depth):
        return [((2, 2 * self.guard + (depth + 1) * self.rims, 128), F32)] * 2


def split(value):
    high = value.astype(BF16)
    return high, (value - high.astype(F32)).astype(BF16)


def dot(left, right):
    return lax.dot_general(left, right, (((1,), (0,)), ((), ())), preferred_element_type=F32)


def product(left, right):
    if left[0].shape[1] % 128:
        return dot(left[0], right[0]) + (dot(left[0], right[1]) + dot(left[1], right[0]))
    return dot(
        jnp.concatenate([left[0], left[0], left[1]], axis=1), jnp.concatenate([right[0], right[1], right[0]], axis=0)
    )


def spread(left, right):
    right = right.astype(BF16)
    return dot(jnp.concatenate(split(left), axis=1), jnp.concatenate([right, right], axis=0))


def gelu(s):
    return 0.5 * s * (1.0 + jnp.tanh(ROOT * (s + CUBE * s * s * s)))


def gelu_slope(s):
    square = s * s
    t = jnp.tanh(ROOT * s * (1.0 + CUBE * square))
    return 0.5 * (1.0 + t) + 0.5 * s * (1.0 - t * t) * ROOT * (1.0 + 3.0 * CUBE * square)


def spread_groups(row):
    row = row + pltpu.roll(row, 64, 1)
    return row + pltpu.roll(row, 32, 1)


def fold(row):
    return spread_groups(row[:, :128] + row[:, 128:])


def wide(row):
    return jnp.concatenate([row, row], axis=1)


def group_of(rows=1, lanes=128):
    return lax.broadcasted_iota(jnp.int32, (rows, lanes), 1) // C


def column_sum(value):
    return jnp.sum(value, axis=0, keepdims=True)


def send_lines(z, ref, lines):
    for n, line in enumerate(lines):
        ref[pl.ds(n, z.devices, stride=len(lines)), :] = jnp.broadcast_to(line, (z.devices, 128))


def moments(z, value, ref):
    few = min(8, z.total)
    pivot = fold(column_sum(value[:few])) / float(few * BLOCK)
    off = value - wide(pivot)
    first, second = fold(column_sum(off)), fold(column_sum(off * off))
    send_lines(z, ref, [pivot + first / z.here, second - first * first / z.here])


def merged(z, ref):
    means = ref[pl.ds(0, z.devices, stride=2), :]
    center = jnp.mean(means, axis=0, keepdims=True)
    off = means - center
    within = jnp.mean(ref[pl.ds(1, z.devices, stride=2), :], axis=0, keepdims=True)
    variance = within / z.here + jnp.mean(off * off, axis=0, keepdims=True)
    return wide(center), wide(lax.rsqrt(variance + norm_eps))


def put_halves(ref, value):
    ref[0] = value[:, :128]
    ref[1] = value[:, 128:]


def whole(ref):
    return jnp.concatenate([ref[0], ref[1]], axis=1)


def to_matrix(z, refs, half):
    for k in (0, 1):
        for j in range(z.blocks[k]):
            at = z.start[k] + j * z.step[k]
            for i in range(z.images[k]):
                for h in (0, 1):
                    half[h, pl.ds(at + i * z.rows[k], z.rows[k]), :] = refs[k][i, :, pl.ds(LANES * j + 128 * h, 128)]


def from_matrix(z, half, refs):
    for k in (0, 1):
        for j in range(z.blocks[k]):
            at = z.start[k] + j * z.step[k]
            for i in range(z.images[k]):
                for h in (0, 1):
                    refs[k][i, :, pl.ds(LANES * j + 128 * h, 128)] = half[h, pl.ds(at + i * z.rows[k], z.rows[k]), :]


def take_rims(z, half, depth, bottom, top):
    for k in (0, 1):
        for d in range(1, depth + 1):
            to_bottom = pl.ds((depth - d) * z.rims + z.rim[k], z.edge[k])
            to_top = pl.ds((d - 1) * z.rims + z.rim[k], z.edge[k])
            if d <= z.rows[k]:
                bottom[to_bottom, :] = half[pl.ds(z.start[k] + z.rows[k] - d, z.edge[k], stride=z.rows[k]), :]
                top[to_top, :] = half[pl.ds(z.start[k] + d - 1, z.edge[k], stride=z.rows[k]), :]
            else:
                bottom[to_bottom, :] = jnp.zeros((z.edge[k], 128), F32)
                top[to_top, :] = jnp.zeros((z.edge[k], 128), F32)


def inside(z, depth, above):
    at = lax.axis_index("row")
    large = lax.broadcasted_iota(jnp.int32, (z.rims, 1), 0) < z.rim[0]
    parts = []
    for n in range(depth):
        if above:
            ok = [jnp.where(at * rows >= depth - n, 1.0, 0.0) for rows in z.rows]
        else:
            ok = [jnp.where((at + 1) * rows + n + 1 <= height, 1.0, 0.0) for rows, height in zip(z.rows, HEIGHTS)]
        parts.append(jnp.where(large, ok[1], ok[0]).astype(F32))
    return jnp.concatenate(parts, axis=0)


def clear_guards(z, pads, a):
    for k in (0, 1):
        pads[k][a, 1, pl.ds(0, z.step[k]), :] = jnp.zeros((z.step[k], 128), F32)
        pads[k][a, 0, pl.ds(z.step[k] + z.count[k], z.step[k]), :] = jnp.zeros((z.step[k], 128), F32)


def fill_center(z, pads, value):
    clear_guards(z, pads, 1)
    for k in (0, 1):
        for h in (0, 1):
            pads[k][1, h, pl.ds(z.step[k], z.count[k]), :] = value[z.start[k] : z.start[k] + z.count[k], 128 * h : 128 * h + 128]


def fill_shifted(z, pads, above, below):
    for k in (0, 1):
        ref, step, count, rows = pads[k], z.step[k], z.count[k], z.rows[k]
        rim = slice(z.rim[k], z.rim[k] + z.edge[k])
        for h in (0, 1):
            lanes = slice(128 * h, 128 * h + 128)
            ref[0, h, pl.ds(step, count), :] = ref[1, h, pl.ds(step - 1, count), :]
            ref[2, h, pl.ds(step, count), :] = ref[1, h, pl.ds(step + 1, count), :]
            ref[0, h, pl.ds(step, z.edge[k], stride=rows), :] = above[rim, lanes]
            ref[2, h, pl.ds(step + rows - 1, z.edge[k], stride=rows), :] = below[rim, lanes]


def fill_pads(z, pads, value, above, below):
    fill_center(z, pads, value)
    fill_shifted(z, pads, above, below)
    for a in (0, 2):
        clear_guards(z, pads, a)


def beside(left, right):
    lane = lax.broadcasted_iota(jnp.int32, (1, 128), 1)
    middle = pltpu.roll(jnp.where(lane >= 64, left[1], right[1]), 64, 1)
    return [
        jnp.where(lane >= 96, left[0], jnp.where(lane < 32, right[0], middle)),
        jnp.where(lane >= 96, left[2], jnp.where(lane < 32, right[2], 0.0)),
    ]


def band_operand(z, pads):
    parts = ([], [])
    for k in (1, 0):
        ref, step, count = pads[k], z.step[k], z.count[k]
        low, high = ([ref[a, h, pl.ds(step, count), :] for a in range(TAPS)] for h in (0, 1))
        before = [ref[a, 1, pl.ds(0, count), :] for a in range(TAPS)]
        after = [ref[a, 0, pl.ds(2 * step, count), :] for a in range(TAPS)]
        parts[0].append(jnp.concatenate(low + beside(before, high), axis=1))
        parts[1].append(jnp.concatenate(high + beside(low, after), axis=1))
    return [jnp.concatenate(part, axis=0) for part in parts]


def rim_operand(z, chain, depth):
    m = lax.broadcasted_iota(jnp.int32, (z.rims, 1), 0)
    large = m < z.rim[0]
    has_before = jnp.where(large, m, m - z.rim[0]) >= jnp.where(large, z.images[1], z.images[0])
    has_after = m < jnp.where(large, z.rim[0] - z.images[1], z.rims - z.images[0])
    low, high, before, after = [], [], [], []
    for r in range(depth + 1):
        at = z.guard + r * z.rims
        low.append(chain[0, pl.ds(at, z.rims), :])
        high.append(chain[1, pl.ds(at, z.rims), :])
        shifted = [chain[1, pl.ds(at - images, z.rims), :] for images in z.images]
        before.append(jnp.where(has_before, jnp.where(large, shifted[1], shifted[0]), 0.0))
        shifted = [chain[0, pl.ds(at + images, z.rims), :] for images in z.images]
        after.append(jnp.where(has_after, jnp.where(large, shifted[1], shifted[0]), 0.0))
    parts = ([], [])
    for n in range(depth - 1):
        rows = slice(n, n + TAPS)
        parts[0].append(jnp.concatenate(low[rows] + beside(before[rows], high[rows]), axis=1))
        parts[1].append(jnp.concatenate(high[rows] + beside(low[rows], after[rows]), axis=1))
    return [jnp.concatenate(part, axis=0) for part in parts]


def times(parts, weight):
    left = jnp.concatenate([part[h] for h in (0, 1) for part in parts], axis=0)
    both = jnp.concatenate([weight_matrix(weight.at[0]), weight_matrix(weight.at[1])], axis=1)
    result = dot(jnp.concatenate(split(left), axis=1), jnp.concatenate([both, both], axis=0))
    result = result[:, :128] + result[:, 128:]
    rows = result.shape[0] // 2
    return jnp.concatenate([result[:rows], result[rows:]], axis=1)


def convolve(z, own, above, below, depth, pads, chains, weight):
    r = z.rims
    fill_pads(z, pads, own, above[(depth - 1) * r :], below[:r])
    parts = [band_operand(z, pads)]
    if depth > 1:
        for side, (rim, chain) in enumerate(zip((above, below), chains)):
            rim_at, own_at = (z.guard, z.guard + depth * r) if side == 0 else (z.guard + r, z.guard)
            for h in (0, 1):
                chain[h, pl.ds(rim_at, depth * r), :] = rim[:, 128 * h : 128 * h + 128]
                for k in (0, 1):
                    row = z.step[k] + (0 if side == 0 else z.rows[k] - 1)
                    chain[h, pl.ds(own_at + z.rim[k], z.edge[k]), :] = pads[k][1, h, pl.ds(row, z.edge[k], stride=z.rows[k]), :]
            parts.append(rim_operand(z, chain, depth))
    result = times(parts, weight)
    n = z.total + (depth - 1) * r
    return result[: z.total], result[z.total : n], result[n:]


def image_sums(z, value):
    slot = lax.broadcasted_iota(jnp.int32, (z.slots, 1), 0)
    sums = jnp.zeros((z.slots, 128), F32)
    for k in (0, 1):
        line = value[z.start[k] : z.start[k] + z.step[k]]
        for j in range(1, z.blocks[k]):
            at = z.start[k] + j * z.step[k]
            line = line + value[at : at + z.step[k]]
        image = lax.broadcasted_iota(jnp.int32, (z.step[k], 1), 0) // z.rows[k]
        for i in range(z.images[k]):
            sums = jnp.where(slot == i + k * z.images[0], column_sum(jnp.where(image == i, line, 0.0)), sums)
    return sums


def image_rows(z, values, rims):
    parts = []
    for k in (1, 0):
        image = lax.broadcasted_iota(jnp.int32, (z.step[k], 1), 0) // z.rows[k]
        line = jnp.zeros((z.step[k], 128), F32)
        for i in range(z.images[k]):
            at = i + k * z.images[0]
            line = jnp.where(image == i, values[at : at + 1], line)
        parts += [line] * z.blocks[k]
    if rims:
        m = lax.broadcasted_iota(jnp.int32, (z.rims, 1), 0)
        image = jnp.where(m < z.rim[0], z.images[0] + m % z.images[1], (m - z.rim[0]) % z.images[0])
        line = jnp.zeros((z.rims, 128), F32)
        for at in range(sum(z.images)):
            line = jnp.where(image == at, values[at : at + 1], line)
        parts += [line] * rims
    return jnp.concatenate(parts, axis=0)


def channel_mean():
    a = lax.broadcasted_iota(jnp.int32, (LANES, 128), 0) // C
    b = lax.broadcasted_iota(jnp.int32, (LANES, 128), 1) % 64
    return jnp.where(a == b, 1.0 / C, 0.0).astype(F32)


def to_channels():
    a = lax.broadcasted_iota(jnp.int32, (128, LANES), 0)
    b = lax.broadcasted_iota(jnp.int32, (128, LANES), 1) // C
    return jnp.where(a == b, 1.0, 0.0).astype(F32)


def attention(value):
    return spread(value * value, channel_mean())


def pieces(source, target):
    return [(source.at[n], target.at[n]) for n in range(source.shape[0])]


def copies_of(pairs, sems, first=0):
    return [pltpu.make_async_copy(a, b, sems.at[first + n]) for n, (a, b) in enumerate(pairs)]


def start_all(copies):
    for copy in copies:
        copy.start()


def wait_all(copies):
    for copy in copies:
        copy.wait()


def start_kernel(z, small, large, up_s, up_l, t_s, t_l, x, bottom, top, copies, raw, half, sems):
    images = [(small, raw[0])] + pieces(large, raw[1])
    rest = [(up_s, raw[2])] + pieces(up_l, raw[3]) + [(t_s, raw[4]), (t_l, raw[5])]
    loads = copies_of(images + rest, sems)
    start_all(loads)
    r, n = z.rims, REACH * z.rims
    tail = n + 2 * r
    for ref in (bottom, top):
        ref[pl.ds(tail, z.slots), :] = jnp.zeros((z.slots, LANES), F32)
    wait_all(loads[: len(images)])
    to_matrix(z, raw[:2], half)
    value = whole(half)
    x[...] = value
    moments(z, value, copies)
    for h in (0, 1):
        lanes = pl.ds(128 * h, 128)
        take_rims(z, half.at[h], REACH, bottom.at[pl.ds(0, n), lanes], top.at[pl.ds(0, n), lanes])
    wait_all(loads[len(images) :])
    for k in (0, 1):
        width, rows = HEIGHTS[k], z.rows[k]
        for i in range(z.images[k]):
            slot = pl.ds(tail + i + k * z.images[0], 1)
            for d in (0, 1):
                to_bottom, to_top = n + (1 - d) * r + z.rim[k] + i, n + d * r + z.rim[k] + i
                for j in range(z.blocks[k]):
                    lanes, at = pl.ds(LANES * j, LANES), j * z.images[k]
                    if d < rows:
                        bottom[pl.ds(to_bottom + at, 1), :] = raw[2 + k][i, pl.ds(rows - 1 - d, 1), lanes]
                        top[pl.ds(to_top + at, 1), :] = raw[2 + k][i, pl.ds(d, 1), lanes]
                    else:
                        bottom[pl.ds(to_bottom + at, 1), :] = jnp.zeros((1, LANES), F32)
                        top[pl.ds(to_top + at, 1), :] = jnp.zeros((1, LANES), F32)
                if d < rows:
                    bottom[slot, pl.ds(128 * (1 - d), width)] = raw[4 + k][i, pl.ds(rows - 1 - d, 1), :]
                    top[slot, pl.ds(128 * d, width)] = raw[4 + k][i, pl.ds(d, 1), :]


def banded(taps, ref):
    row = lax.broadcasted_iota(jnp.int32, (128, 128), 0) // C
    lane = group_of(128)
    for a in range(TAPS):
        main = jnp.zeros((128, 128), F32)
        for b in range(TAPS):
            main = jnp.where(row - lane + 1 == b, taps[a][b], main)
        before = jnp.where(lane[:C] == 0, taps[a][0][:C], 0.0)
        after = jnp.where(lane[:C] == 3, taps[a][2][:C], 0.0)
        for n, part in enumerate(split(jnp.concatenate([main, before, after], axis=0))):
            ref[n, pl.ds(a * TAP_ROWS, TAP_ROWS), :] = part


def weight_matrix(ref):
    main = [ref[pl.ds(a * TAP_ROWS, 128), :] for a in range(TAPS)]
    before, after = ([ref[pl.ds(a * TAP_ROWS + 128 + n * C, C), :] for a in range(TAPS)] for n in (0, 1))
    return jnp.concatenate(
        main + [after[0], before[1], after[1], before[0], after[2], jnp.zeros((2 * C, 128), BF16), before[2]], axis=0
    )


def prepare_kernel(z, first, second, up_s, up_l, t_s, t_l, g1, b1, g2, b2, x, w1, w2, weights, affine, upstream, teacher, x_copy, raw, kept, kept_u, rows, half, sems):
    targets = tuple(raw) + tuple(rows.at[pl.ds(n, 1), :] for n in range(4))
    refs = (first, second, up_s, up_l, t_s, t_l, g1, b1, g2, b2)
    loads = [pltpu.make_async_copy(a, b, sems.at[n]) for n, (a, b) in enumerate(zip(refs, targets))]
    start_all(loads)
    stores = [pltpu.make_async_copy(x, x_copy, sems.at[13])]
    stores[0].start()
    wait_all(loads)
    to_matrix(z, raw[2:4], half)
    kept_u[...] = whole(half)
    stores.append(pltpu.make_async_copy(kept_u, upstream, sems.at[10]))
    stores[1].start()
    for n, (source, forward) in enumerate(zip(raw[:2], (w1, w2))):
        tiles = []
        for a in range(TAPS):
            line = [jnp.concatenate([source[a, b]] * 4, axis=1) for b in range(TAPS)]
            tiles.append([jnp.concatenate([tap] * 4, axis=0) for tap in line])
        turned = [[tiles[TAPS - 1 - a][TAPS - 1 - b].T for b in range(TAPS)] for a in range(TAPS)]
        banded(tiles, forward)
        banded(turned, kept.at[n])
        stores.append(pltpu.make_async_copy(kept.at[n], weights.at[n], sems.at[11 + n]))
        stores[-1].start()
    affine[...] = jnp.concatenate([rows[...]] * BLOCK, axis=1)
    teacher[...] = jnp.zeros(teacher.shape, F32)
    for k, ref in ((0, raw[4]), (1, raw[5])):
        for i in range(z.images[k]):
            line = ref[i]
            for j in range(z.blocks[k]):
                at = z.start[k] + j * z.step[k] + i * z.rows[k]
                for lane in (0, 64):
                    teacher[pl.ds(at, z.rows[k]), pl.ds(lane, BLOCK)] = line[:, j * BLOCK : (j + 1) * BLOCK]
    wait_all(stores)


def normed_by(stats):
    return lambda v: (v - stats[0:1]) * stats[1:2]


def activation(center, scale, gain, bias):
    factor = scale * gain
    offset = bias - center * factor
    return lambda v: gelu(v * factor + offset)


def first_kernel(z, x, above, below, gathered, affine, weight, hidden, h_above, h_below, stats, copies, pads, chains):
    n = REACH * z.rims
    center, scale = merged(z, gathered)
    act = activation(center, scale, affine[0:1], affine[1:2])
    own = act(x[...])
    up, down = act(above[pl.ds(0, n), :]) * inside(z, 4, True), act(below[pl.ds(0, n), :]) * inside(z, 4, False)
    own, up, down = convolve(z, own, up, down, 4, pads, chains, weight)
    moments(z, own, copies)
    hidden[...] = own
    h_above[...] = up
    h_below[...] = down
    stats[0:1] = center
    stats[1:2] = scale


def second_kernel(z, hidden, h_above, h_below, gathered, affine, weight, x, x_above, x_below, teacher, out, o_above, o_below, near, stats, copies, pads, chains):
    center, scale = merged(z, gathered)
    act = activation(center, scale, affine[2:3], affine[3:4])
    r = z.rims
    own = act(hidden[...])
    up, down = act(h_above[...]) * inside(z, 3, True), act(h_below[...]) * inside(z, 3, False)
    own, up, down = convolve(z, own, up, down, 3, pads, chains, weight)
    own = x[...] + own
    amap = attention(own)
    lane = lax.broadcasted_iota(jnp.int32, (1, 128), 1)
    sums = image_sums(z, amap * jnp.where(lane < 64, amap, teacher[...]))
    copies[...] = jnp.concatenate([sums] * z.peers, axis=0)
    out[...] = own
    o_above[...] = x_above[pl.ds(2 * r, 2 * r), :] + up
    o_below[...] = x_below[pl.ds(0, 2 * r), :] + down
    near[0] = h_above[pl.ds(2 * r, r), :]
    near[1] = h_below[pl.ds(0, r), :]
    stats[0:1] = center
    stats[1:2] = scale


def tap_rows(q):
    return 128 + C if q < 0 else q * C


def tap_product(z, operand, own, above, below, pads):
    fill_center(z, pads, own)
    fill_shifted(z, pads, above, below)
    columns = []
    for a in range(TAPS):
        columns.append(
            jnp.concatenate([pads[k][TAPS - 1 - a, h, pl.ds(z.step[k], z.count[k]), :] for h in (0, 1) for k in (1, 0)], axis=0)
        )
    return product(operand, split(jnp.concatenate(columns, axis=1)))


def tap_sums(result, tiles, first_group):
    group = group_of()
    for a in range(TAPS):
        for b in range(TAPS):
            total = None
            for p in range(4):
                at = tap_rows(p + b - 1)
                part = result[at : at + C, 128 * a : 128 * a + 128]
                total = part if total is None else jnp.where(group == p, part, total)
            tile, slot = divmod(first_group + a * TAPS + b, 4)
            tiles[tile] = jnp.where(group == slot, spread_groups(total), tiles[tile])


def tap_counts(z, turned, tiles, first_group):
    group = group_of()
    m = lax.broadcasted_iota(jnp.int32, (1, 2 * z.total), 1) % z.total
    row = jnp.where(m < z.start[0], m % z.rows[1], (m - z.start[0]) % z.rows[0])
    height = jnp.where(m < z.start[0], z.rows[1], z.rows[0])
    at = lax.axis_index("row")
    lost = {
        0: (row == height - 1) & (at == z.peers - 1),
        2: (row == 0) & (at == 0),
    }
    for a in range(TAPS):
        column = jnp.sum(jnp.where(lost[a], 0.0, turned) if a in lost else turned, axis=1, keepdims=True)
        for b in range(TAPS):
            total = sum(column[tap_rows(p + b - 1) : tap_rows(p + b - 1) + C] for p in range(4))
            tile, slot = divmod(first_group + a * TAPS + b, 4)
            tiles[tile] = jnp.where(group == slot, total, tiles[tile])


def turned_operand(z, value, pads, kept):
    fill_center(z, pads, value)
    lane = lax.broadcasted_iota(jnp.int32, (1, 128), 1)
    halves = ([], [])
    for k in (1, 0):
        ref, step, count = pads[k], z.step[k], z.count[k]
        low, high = ref[1, 0, pl.ds(step, count), :], ref[1, 1, pl.ds(step, count), :]
        before, after = ref[1, 1, pl.ds(0, count), :], ref[1, 0, pl.ds(2 * step, count), :]
        for part, main, left, right in ((halves[0], low, before, high), (halves[1], high, low, after)):
            part.append(jnp.concatenate([main, jnp.where(lane >= 96, left, jnp.where(lane < 32, right, 0.0))], axis=1))
    turned = jnp.concatenate(halves[0] + halves[1], axis=0).T
    turned = jnp.concatenate([turned[: 128 + C], turned[256 - C :]], axis=0)
    parts = split(turned)
    for n in (0, 1):
        kept[n] = parts[n]
    return turned


def first_operand_kernel(z, x, hidden, h_above, h_below, above, below, stats, affine, teacher, upstream, weights, left, packed, teachers, spread_u, near_u, pads, chains, kept, kept_w, kept_u, pixels, kept_t, kept_c, kept_packed, sems):
    r, own = z.rims, pl.ds(0, z.total)
    loads = [pltpu.make_async_copy(upstream, kept_u.at[own, :], sems.at[0]), pltpu.make_async_copy(weights.at[1], kept_w, sems.at[1])]
    start_all(loads)
    act = activation(stats[0:1], stats[1:2], affine[0:1], affine[1:2])
    value = turned_operand(z, act(x[...]), pads, kept)
    stores = [pltpu.make_async_copy(kept, left, sems.at[2])]
    stores[0].start()
    tiles = [jnp.zeros((C, 128), F32) for _ in range(BACK_LANES // 128)]
    tap_counts(z, value, tiles, ONES)
    result = tap_product(
        z, (kept[0], kept[1]), hidden[...], h_above[pl.ds(2 * r, r), :] * inside(z, 1, True), h_below[pl.ds(0, r), :] * inside(z, 1, False), pads
    )
    tap_sums(result, tiles, HIDDEN)
    kept_packed[...] = jnp.concatenate(tiles, axis=1)
    stores.append(pltpu.make_async_copy(kept_packed, packed, sems.at[6]))
    stores[1].start()
    pixels[own, :] = teacher[...]
    pixels[pl.ds(z.total, 4 * r), :] = jnp.zeros((4 * r, 128), F32)
    n = (REACH + 2) * r
    for side, ref in enumerate((above, below)):
        for d in (0, 1):
            for k in (0, 1):
                line = ref[pl.ds(n + k * z.images[0], z.images[k]), pl.ds(128 * d, 128)]
                for j in range(z.blocks[k]):
                    at = z.total + (2 * side + d) * r + z.rim[k] + j * z.images[k]
                    pixels[pl.ds(at, z.images[k]), pl.ds(0, BLOCK)] = line[:, j * BLOCK : (j + 1) * BLOCK]
    kept_t[...] = spread(pixels[...], to_channels())
    stores.append(pltpu.make_async_copy(kept_t, teachers, sems.at[3]))
    stores[2].start()
    n = REACH * r
    up, down = above[pl.ds(n, 2 * r), :] * inside(z, 2, True), below[pl.ds(n, 2 * r), :] * inside(z, 2, False)
    kept_u[pl.ds(z.total, r), :] = up[r:]
    kept_u[pl.ds(z.total + r, r), :] = down[:r]
    wait_all(loads)
    stores.append(pltpu.make_async_copy(kept_u, near_u, sems.at[5]))
    stores[3].start()
    kept_c[...] = jnp.concatenate(convolve(z, kept_u[own, :], up, down, 2, pads, chains, kept_w), axis=0)
    stores.append(pltpu.make_async_copy(kept_c, spread_u, sems.at[4]))
    stores[4].start()
    wait_all(stores)


def second_operand_kernel(z, hidden, near, stats, affine, out, o_above, o_below, teachers, spread_u, near_u, weights, out_copy, hidden_copy, left, shifts, by_map, by_teacher, up, pads, chains, kept_t, kept_u, kept_w, kept_s, sems):
    r, total = z.rims, z.total
    loads = [
        pltpu.make_async_copy(teachers, kept_t, sems.at[0]),
        pltpu.make_async_copy(weights.at[1], kept_w, sems.at[1]),
        pltpu.make_async_copy(spread_u, kept_u, sems.at[2]),
    ]
    start_all(loads)
    stores = [
        pltpu.make_async_copy(out, out_copy, sems.at[4]),
        pltpu.make_async_copy(hidden, hidden_copy.at[pl.ds(0, total), :], sems.at[7]),
        pltpu.make_async_copy(near.at[0], hidden_copy.at[pl.ds(total, r), :], sems.at[8]),
        pltpu.make_async_copy(near.at[1], hidden_copy.at[pl.ds(total + r, r), :], sems.at[9]),
        pltpu.make_async_copy(near_u, up, sems.at[10]),
    ]
    start_all(stores)
    normed = normed_by(stats)(jnp.concatenate([hidden[...], near[0], near[1]], axis=0))
    shifted = normed * affine[2:3] + affine[3:4]
    turned_operand(z, gelu(shifted[:total]), pads, left)
    ones = jnp.ones((total, 1), F32)
    masks = jnp.concatenate([ones, inside(z, 1, True), inside(z, 1, False)], axis=0)
    slopes = gelu_slope(shifted) * masks
    o = jnp.concatenate([out[...], o_above[...] * inside(z, 2, True), o_below[...] * inside(z, 2, False)], axis=0)
    for_map = spread(attention(o), to_channels()) * o
    wait_all(loads)
    for_teacher = kept_t[...] * o
    kept_s[0] = kept_u[...] * slopes
    stores += copies_of(pieces(kept_s, shifts), sems, 11)
    stores[-3].start()
    for n, value, ref in ((1, for_map, by_map), (2, for_teacher, by_teacher)):
        own, before, after = value[:total], value[total : total + 2 * r], value[total + 2 * r :]
        ref[...] = jnp.concatenate([own, before[r:], after[:r]], axis=0)
        kept_s[n] = jnp.concatenate(convolve(z, own, before, after, 2, pads, chains, kept_w), axis=0) * slopes
        stores[n - 3].start()
    wait_all(stores)


def upstream_kernel(z, gathered, up, shifts, left_1, left_2, packed, by_map, by_teacher, hidden, stats, dout, dshift, d_above, d_below, slabs, kept_s, kept_left, kept_h, kept_packed, pads, more_pads, sems):
    r, total = z.rims, z.total
    loads = copies_of(
        pieces(shifts, kept_s) + pieces(left_1, kept_left) + [(hidden.at[pl.ds(0, total), :], kept_h), (packed, kept_packed)], sems
    )
    start_all(loads)
    lane = lax.broadcasted_iota(jnp.int32, (z.slots, 128), 1)
    sums = sum(gathered[pl.ds(n * z.slots, z.slots), :] for n in range(z.peers))
    square = jnp.sum(jnp.where(lane < 64, sums, 0.0), axis=1, keepdims=True)
    cross = jnp.sum(jnp.where(lane < 64, 0.0, sums), axis=1, keepdims=True)
    inverse = lax.rsqrt(square + map_eps)
    inner = beta_weight * (square * inverse - cross) * inverse
    shape = (z.slots, 128)
    for_map = (beta_weight - inner) * inverse * inverse * (2.0 / C)
    for_teacher = beta_weight * inverse * (2.0 / C)
    for_map, for_teacher = (wide(image_rows(z, jnp.broadcast_to(v, shape), 2)) for v in (for_map, for_teacher))
    value = up[...] + for_map * by_map[...] - for_teacher * by_teacher[...]
    dout[...] = value[:total]
    wait_all(loads[:3])
    shift = kept_s[0] + for_map * kept_s[1] - for_teacher * kept_s[2]
    pre, above, below = shift[:total], shift[total : total + r], shift[total + r :]
    dshift[...] = pre
    d_above[...] = above
    d_below[...] = below
    second = tap_product(z, (left_2[0], left_2[1]), value[:total], value[total : total + r], value[total + r :], pads)
    wait_all(loads[3:5])
    first = tap_product(z, (kept_left[0], kept_left[1]), pre, above, below, more_pads)
    wait_all(loads[5:])
    normed = normed_by(stats)(kept_h[...])
    tiles = [kept_packed[:, 128 * n : 128 * n + 128] for n in range(BACK_LANES // 128)]
    group = group_of()
    tiles[0] = jnp.where(group == BIAS, fold(column_sum(pre)), jnp.where(group == GAIN, fold(column_sum(pre * normed)), tiles[0]))
    tap_sums(second, tiles, SECOND)
    tap_sums(first, tiles, LEFT)
    line = jnp.concatenate(tiles, axis=1)
    for d in range(z.devices):
        slabs[d] = line[d % C : d % C + 1]


def write_kernel(z, out, x, hidden, weights, first_stats, stats, order, out_s, out_l, first_normed, normed, weight, kept, kept_x, kept_h, half, sems):
    loads = [pltpu.make_async_copy(a, b, sems.at[n]) for n, (a, b) in enumerate(((out, kept), (x, kept_x), (hidden, kept_h), (weights.at[0], weight)))]
    start_all(loads)
    loads[0].wait()
    put_halves(half, kept[...])
    from_matrix(z, half, (out_s, out_l))
    loads[1].wait()
    first_normed[...] = normed_by(first_stats)(kept_x[...])
    loads[2].wait()
    normed[...] = normed_by(stats)(kept_h[...])
    loads[3].wait()


def norm_sums(total):
    group = group_of()
    return [wide(spread_groups(jnp.where(group == n, total[:, :128], 0.0))) for n in (BIAS, GAIN)]


def hidden_kernel(z, gathered, dshift, d_above, d_below, second_normed, stats, affine, weight, first_normed, pre_ref, gain_out, bias_out, slabs, pads):
    total = jnp.sum(gathered[...], axis=0)
    bias_sum, gain_sum = norm_sums(total)
    bias_out[...] = bias_sum[:, :C]
    gain_out[...] = gain_sum[:, :C]
    bias_mean, gain_mean = bias_sum / z.pixels, gain_sum / z.pixels
    factor = affine[2:3] * stats[1:2]
    r, total_rows = z.rims, z.total

    def back(d, normed):
        return factor * (d - bias_mean - normed * gain_mean)

    own = back(dshift[...], second_normed[pl.ds(0, total_rows), :])
    up = back(d_above[...], second_normed[pl.ds(total_rows, r), :]) * inside(z, 1, True)
    down = back(d_below[...], second_normed[pl.ds(total_rows + r, r), :]) * inside(z, 1, False)
    grad, _, _ = convolve(z, own, up, down, 1, pads, None, weight)
    normed = first_normed[...]
    pre = grad * gelu_slope(normed * affine[0:1] + affine[1:2])
    pre_ref[...] = pre
    lane = lax.broadcasted_iota(jnp.int32, (1, 128), 1)
    taps = TAPS * TAPS * C

    def along(row):
        return jnp.concatenate([row[:, :128]] * 3, axis=1)[:, :taps]

    second, left, against, ones = (total[:, n * C : n * C + taps] for n in (SECOND, LEFT, HIDDEN, ONES))
    against = along(stats[1:2]) * (against - along(stats[0:1]) * ones)
    first = along(factor) * (left - along(bias_mean) * ones - along(gain_mean) * against)
    sums = jnp.where(lane < C, fold(column_sum(pre)), fold(column_sum(pre * normed)))
    line = jnp.concatenate([sums[:, : 2 * C], second, first], axis=1)
    slabs[...] = jnp.broadcast_to(line[None], slabs.shape)


def back_kernel(z, gathered, pre, normed, stats, affine, dout, back_s, back_l, one, two, gain_out, bias_out, half, lines):
    bias_sum, gain_sum = norm_sums(jnp.sum(gathered[:, :, pl.ds(0, 128)], axis=0))
    bias_out[...] = bias_sum[:, :C]
    gain_out[...] = gain_sum[:, :C]
    value = dout[...] + affine[0:1] * stats[1:2] * (pre[...] - bias_sum / z.pixels - normed[...] * (gain_sum / z.pixels))
    put_halves(half, value)
    from_matrix(z, half, (back_s, back_l))
    for d in range(C):
        lines[pl.ds(d, 1), :] = gathered[d]
    for ref, group in ((two, LAST_SECOND), (one, LAST_FIRST)):
        for a in range(TAPS):
            for b in range(TAPS):
                at = (group + a * TAPS + b) * C
                ref[a, b] = lines[:, pl.ds(at, C)]


def call(body, ins, outs, scratch=(), sems=0):
    space = {"v": pltpu.VMEM, "h": pltpu.HBM, "V": pltpu.VMEM}
    shapes = []
    for item in scratch:
        if isinstance(item, list):
            shapes.append([pltpu.VMEM(*s) for s in item])
        else:
            shapes.append(pltpu.VMEM(*item))
    if sems:
        shapes.append(pltpu.SemaphoreType.DMA((sems,)))
    run = pl.pallas_call(
        body,
        out_shape=[jax.ShapeDtypeStruct(shape, kind) if s == "v" else space[s](shape, kind) for s, shape, kind in outs],
        in_specs=[pl.BlockSpec(memory_space=space[s]) for s in ins],
        out_specs=[pl.BlockSpec(memory_space=space[s]) for s, _, _ in outs],
        scratch_shapes=shapes,
        compiler_params=pltpu.CompilerParams(vmem_limit_bytes=VMEM_LIMIT),
    )
    return lambda *args: run(
        *(pltpu.with_memory_space_constraint(arg, pltpu.HBM) if s == "h" else arg for s, arg in zip(ins, args))
    )


def exchange(lines, axes):
    shape = lines.shape
    if len(shape) == 2:
        lines = lines.reshape(math.prod(lax.axis_size(axis) for axis in axes), -1, 128)
    return lax.all_to_all(lines, axes, 0, 0, tiled=True).reshape(shape)


def beyond(z, bottom, top, depths):
    hops = max(-(-depth // rows) for rows in z.rows for depth in depths)
    above, below = [], []
    for hop in range(1, hops + 1):
        above.append(lax.ppermute(bottom, "row", [(i, i + hop) for i in range(z.peers - hop)]))
        below.append(lax.ppermute(top, "row", [(i + hop, i) for i in range(z.peers - hop)]))
    if hops == 1:
        return above[0], below[0]
    up, down = [], []
    base = 0
    for depth in depths:
        for n in range(depth):
            for k in (1, 0):
                hop, back = divmod(depth - 1 - n, z.rows[k])
                at = base + (depth - 1 - back) * z.rims + z.rim[k]
                up.append(above[hop][at : at + z.edge[k]])
                hop, back = divmod(n, z.rows[k])
                at = base + back * z.rims + z.rim[k]
                down.append(below[hop][at : at + z.edge[k]])
        base += depth * z.rims
    up.append(jnp.concatenate([pixel_rows(z, above, base, 1, 1), pixel_rows(z, above, base, 0, 1)], axis=1))
    down.append(jnp.concatenate([pixel_rows(z, below, base, 0, 0), pixel_rows(z, below, base, 1, 0)], axis=1))
    return jnp.concatenate(up, axis=0), jnp.concatenate(down, axis=0)


def pixel_rows(z, bands, base, distance, last):
    lines = []
    for k in (0, 1):
        hop, back = divmod(distance, z.rows[k])
        at = base + k * z.images[0]
        half = 128 * abs(last - back)
        lines.append(bands[hop][at : at + z.images[k], half : half + 128])
    lines.append(jnp.zeros((z.slots - sum(z.images), 128), F32))
    return jnp.concatenate(lines, axis=0)


def local(
    image_small, image_large, teacher_small, teacher_large, upstream_small, upstream_large,
    conv_first, gain_first, bias_first, conv_second, gain_second, bias_second,
):
    peers = lax.axis_size("row")
    devices = lax.axis_size("img") * peers
    z = Sizes(image_small.shape, image_large.shape, devices, peers)
    body = lambda function: functools.partial(function, z)
    r = z.rims
    full, half, pair = (z.total, LANES), (2, z.total, 128), (2 * devices, 128)
    weight, left = (2, TAPS * TAP_ROWS, 128), (2, 128 + 2 * C, 2 * z.total)
    images = [image_small, image_large, upstream_small, upstream_large, teacher_small, teacher_large]
    f = lambda space, *shape: (space, shape, F32)
    depths = (REACH, 2)
    rim_rows = sum(depths) * r + z.slots

    x, bottom, top, copies = call(
        body(start_kernel),
        "hhhhhh",
        [("v", full, F32), f("v", rim_rows, LANES), f("v", rim_rows, LANES), ("V", pair, F32)],
        [[(a.shape, F32) for a in images], (half, F32)],
        4 + 2 * z.images[1],
    )(*images)
    gathered = exchange(copies, AXES)
    above, below = beyond(z, bottom, top, depths)
    params = [conv_first, conv_second] + images[2:]
    w1, w2, weights, affine, upstream, teacher, x_copy = call(
        body(prepare_kernel),
        "hhhhhhhhhhv",
        [("v", weight, BF16), ("v", weight, BF16), ("h", (2,) + weight, BF16), f("v", 4, LANES), ("h", full, F32), f("v", z.total, 128), ("h", full, F32)],
        [[(a.shape, F32) for a in params], ((2,) + weight, BF16), (full, F32), ((4, C), F32), (half, F32)],
        14,
    )(*params, *(v.reshape(1, C) for v in (gain_first, bias_first, gain_second, bias_second)), x)

    hidden, h_above, h_below, stats_one, copies = call(
        body(first_kernel),
        "vvvvvv",
        [("v", full, F32), f("v", 3 * r, LANES), f("v", 3 * r, LANES), f("v", 2, LANES), ("V", pair, F32)],
        [z.pads(), z.chains(4)],
    )(x, above, below, gathered, affine, w1)
    gathered = exchange(copies, AXES)
    extended, near_rows = z.total + 4 * r, z.total + 2 * r
    left_one, packed, teachers, spread_u, near_u = call(
        body(first_operand_kernel),
        "vvvvvvvvvhh",
        [("h", left, BF16), f("h", C, BACK_LANES), f("h", extended, LANES), f("h", near_rows, LANES), f("h", near_rows, LANES)],
        [
            z.pads(), z.chains(2), (left, BF16), (weight, BF16), ((near_rows, LANES), F32), ((extended, 128), F32),
            ((extended, LANES), F32), ((near_rows, LANES), F32), ((C, BACK_LANES), F32),
        ],
        7,
    )(x, hidden, h_above, h_below, above, below, stats_one, affine, teacher, upstream, weights)
    gathered, near_u = lax.optimization_barrier((gathered, near_u))

    map_shape = (peers * z.slots, 128)
    out, o_above, o_below, near, stats_two, copies = call(
        body(second_kernel),
        "vvvvvvvvvv",
        [("v", full, F32), f("v", 2 * r, LANES), f("v", 2 * r, LANES), f("v", 2, r, LANES), f("v", 2, LANES), ("V", map_shape, F32)],
        [z.pads(), z.chains(3)],
    )(hidden, h_above, h_below, gathered, affine, w2, x, above, below, teacher)
    gathered = exchange(copies, ("row",))
    out_copy, hidden_copy, left_two, shifts, by_map, by_teacher, up = call(
        body(second_operand_kernel),
        "vvvvvvvhhhh",
        [
            ("h", full, F32), f("h", near_rows, LANES), ("v", left, BF16), f("h", 3, near_rows, LANES),
            f("v", near_rows, LANES), f("v", near_rows, LANES), f("v", near_rows, LANES),
        ],
        [
            z.pads(), z.chains(2), ((extended, LANES), F32), ((near_rows, LANES), F32), (weight, BF16),
            ((3, near_rows, LANES), F32),
        ],
        14,
    )(hidden, near, stats_two, affine, out, o_above, o_below, teachers, spread_u, near_u, weights)

    dout, dshift, d_above, d_below, slabs = call(
        body(upstream_kernel),
        "vvhhvhvvhv",
        [("v", full, F32), ("v", full, F32), f("v", r, LANES), f("v", r, LANES), f("V", devices, 1, BACK_LANES)],
        [((3, near_rows, LANES), F32), (left, BF16), (full, F32), ((C, BACK_LANES), F32), z.pads(), z.pads()],
        7,
    )(gathered, up, shifts, left_one, left_two, packed, by_map, by_teacher, hidden_copy, stats_two)
    gathered = exchange(slabs, AXES)
    out_s, out_l, first_normed, second_normed, weight_back = call(
        body(write_kernel),
        "hhhhvvv",
        [("v", image_small.shape, F32), ("v", image_large.shape, F32), ("v", full, F32), f("v", near_rows, LANES), ("v", weight, BF16)],
        [(full, F32), (full, F32), ((near_rows, LANES), F32), (half, F32)],
        4,
    )(out_copy, x_copy, hidden_copy, weights, stats_one, stats_two, d_above)

    pre, gain_two, bias_two, slabs = call(
        body(hidden_kernel),
        "vvvvvvvvv",
        [("v", full, F32), f("v", 1, C), f("v", 1, C), f("V", devices, 1, LAST_LANES)],
        [z.pads()],
    )(gathered, dshift, d_above, d_below, second_normed, stats_two, affine, weight_back, first_normed)
    gathered = exchange(slabs, AXES)

    back_s, back_l, one, two, gain_one, bias_one = call(
        body(back_kernel),
        "vvvvvv",
        [("v", a.shape, F32) for a in (image_small, image_large, conv_first, conv_second)] + [f("v", 1, C), f("v", 1, C)],
        [(half, F32), ((C, LAST_LANES), F32)],
    )(gathered, pre, first_normed, stats_one, affine, dout)
    return (
        out_s, out_l, back_s, back_l,
        one, gain_one.reshape(C), bias_one.reshape(C),
        two, gain_two.reshape(C), bias_two.reshape(C),
    )


def solution(mesh):
    split_bands, everywhere = P("img", "row", None), P()
    return jax.shard_map(
        local,
        mesh=mesh,
        in_specs=(split_bands,) * 6 + (everywhere,) * 6,
        out_specs=(split_bands,) * 4 + (everywhere,) * 6,
        check_vma=False,
    )
```

```python
import functools
import math

import jax
import jax.numpy as jnp
from jax import lax
from jax.experimental import pallas as pl
from jax.experimental.pallas import tpu as pltpu
from jax.sharding import PartitionSpec as P

C = 32
HS = 32
HL = 64
HEIGHTS = (HS, HL)

norm_eps = 1e-05
map_eps = 1e-06
beta_weight = 1000.0
AXES = ("img", "row")
BLOCK = 8
LANES = BLOCK * C
TAPS = 3
DEPTH = TAPS * 128 + 256
TAP_ROWS = 128 + 2 * C
REACH = 4
ROOT = math.sqrt(2.0 / math.pi)
CUBE = 0.044715
F32 = jnp.float32
BF16 = jnp.bfloat16
VMEM_LIMIT = 32 * 1024 * 1024
BIAS, GAIN, SECOND, LEFT, HIDDEN, ONES = 0, 1, 2, 11, 20, 29
BACK_LANES = 1280
LAST_SECOND, LAST_FIRST, LAST_LANES = 2, 11, 640


class Sizes:
    def __init__(self, small, large, devices, peers):
        self.images = (small[0], large[0])
        self.rows = (small[1], large[1])
        self.blocks = (HS // BLOCK, HL // BLOCK)
        self.step = tuple(n * r for n, r in zip(self.images, self.rows))
        self.count = tuple(b * s for b, s in zip(self.blocks, self.step))
        self.edge = tuple(b * n for b, n in zip(self.blocks, self.images))
        self.start = (self.count[1], 0)
        self.rim = (self.edge[1], 0)
        self.total = sum(self.count)
        self.rims = sum(self.edge)
        self.slots = -(-sum(self.images) // 8) * 8
        self.guard = -(-max(self.images) // 8) * 8
        self.devices = devices
        self.peers = peers
        self.here = float(self.total * BLOCK)
        self.pixels = self.here * devices

    def pads(self):
        return [((TAPS, 2, self.count[k] + 2 * self.step[k], 128), F32) for k in (0, 1)]

    def chains(self, depth):
        return [((2, 2 * self.guard + (depth + 1) * self.rims, 128), F32)] * 2


def split(value):
    high = value.astype(BF16)
    return high, (value - high.astype(F32)).astype(BF16)


def dot(left, right):
    return lax.dot_general(left, right, (((1,), (0,)), ((), ())), preferred_element_type=F32)


def product(left, right):
    if left[0].shape[1] % 128:
        return dot(left[0], right[0]) + (dot(left[0], right[1]) + dot(left[1], right[0]))
    return dot(
        jnp.concatenate([left[0], left[0], left[1]], axis=1), jnp.concatenate([right[0], right[1], right[0]], axis=0)
    )


def spread(left, right):
    right = right.astype(BF16)
    return dot(jnp.concatenate(split(left), axis=1), jnp.concatenate([right, right], axis=0))


def gelu(s):
    return 0.5 * s * (1.0 + jnp.tanh(ROOT * (s + CUBE * s * s * s)))


def gelu_slope(s):
    square = s * s
    t = jnp.tanh(ROOT * s * (1.0 + CUBE * square))
    return 0.5 * (1.0 + t) + 0.5 * s * (1.0 - t * t) * ROOT * (1.0 + 3.0 * CUBE * square)


def spread_groups(row):
    row = row + pltpu.roll(row, 64, 1)
    return row + pltpu.roll(row, 32, 1)


def fold(row):
    return spread_groups(row[:, :128] + row[:, 128:])


def wide(row):
    return jnp.concatenate([row, row], axis=1)


def group_of(rows=1, lanes=128):
    return lax.broadcasted_iota(jnp.int32, (rows, lanes), 1) // C


def column_sum(value):
    return jnp.sum(value, axis=0, keepdims=True)


def send_lines(z, ref, lines):
    for n, line in enumerate(lines):
        ref[pl.ds(n, z.devices, stride=len(lines)), :] = jnp.broadcast_to(line, (z.devices, 128))


def moments(z, value, ref):
    few = min(8, z.total)
    pivot = fold(column_sum(value[:few])) / float(few * BLOCK)
    off = value - wide(pivot)
    first, second = fold(column_sum(off)), fold(column_sum(off * off))
    send_lines(z, ref, [pivot + first / z.here, second - first * first / z.here])


def merged(z, ref):
    means = ref[pl.ds(0, z.devices, stride=2), :]
    center = jnp.mean(means, axis=0, keepdims=True)
    off = means - center
    within = jnp.mean(ref[pl.ds(1, z.devices, stride=2), :], axis=0, keepdims=True)
    variance = within / z.here + jnp.mean(off * off, axis=0, keepdims=True)
    return wide(center), wide(lax.rsqrt(variance + norm_eps))


def put_halves(ref, value):
    ref[0] = value[:, :128]
    ref[1] = value[:, 128:]


def whole(ref):
    return jnp.concatenate([ref[0], ref[1]], axis=1)


def to_matrix(z, refs, half):
    for k in (0, 1):
        for j in range(z.blocks[k]):
            at = z.start[k] + j * z.step[k]
            for i in range(z.images[k]):
                for h in (0, 1):
                    half[h, pl.ds(at + i * z.rows[k], z.rows[k]), :] = refs[k][i, :, pl.ds(LANES * j + 128 * h, 128)]


def from_matrix(z, half, refs):
    for k in (0, 1):
        for j in range(z.blocks[k]):
            at = z.start[k] + j * z.step[k]
            for i in range(z.images[k]):
                for h in (0, 1):
                    refs[k][i, :, pl.ds(LANES * j + 128 * h, 128)] = half[h, pl.ds(at + i * z.rows[k], z.rows[k]), :]


def take_rims(z, half, depth, bottom, top):
    for k in (0, 1):
        for d in range(1, depth + 1):
            to_bottom = pl.ds((depth - d) * z.rims + z.rim[k], z.edge[k])
            to_top = pl.ds((d - 1) * z.rims + z.rim[k], z.edge[k])
            if d <= z.rows[k]:
                bottom[to_bottom, :] = half[pl.ds(z.start[k] + z.rows[k] - d, z.edge[k], stride=z.rows[k]), :]
                top[to_top, :] = half[pl.ds(z.start[k] + d - 1, z.edge[k], stride=z.rows[k]), :]
            else:
                bottom[to_bottom, :] = jnp.zeros((z.edge[k], 128), F32)
                top[to_top, :] = jnp.zeros((z.edge[k], 128), F32)


def inside(z, depth, above):
    at = lax.axis_index("row")
    large = lax.broadcasted_iota(jnp.int32, (z.rims, 1), 0) < z.rim[0]
    parts = []
    for n in range(depth):
        if above:
            ok = [jnp.where(at * rows >= depth - n, 1.0, 0.0) for rows in z.rows]
        else:
            ok = [jnp.where((at + 1) * rows + n + 1 <= height, 1.0, 0.0) for rows, height in zip(z.rows, HEIGHTS)]
        parts.append(jnp.where(large, ok[1], ok[0]).astype(F32))
    return jnp.concatenate(parts, axis=0)


def clear_guards(z, pads, a):
    for k in (0, 1):
        pads[k][a, 1, pl.ds(0, z.step[k]), :] = jnp.zeros((z.step[k], 128), F32)
        pads[k][a, 0, pl.ds(z.step[k] + z.count[k], z.step[k]), :] = jnp.zeros((z.step[k], 128), F32)


def fill_center(z, pads, value):
    clear_guards(z, pads, 1)
    for k in (0, 1):
        for h in (0, 1):
            pads[k][1, h, pl.ds(z.step[k], z.count[k]), :] = value[z.start[k] : z.start[k] + z.count[k], 128 * h : 128 * h + 128]


def fill_shifted(z, pads, above, below):
    for k in (0, 1):
        ref, step, count, rows = pads[k], z.step[k], z.count[k], z.rows[k]
        rim = slice(z.rim[k], z.rim[k] + z.edge[k])
        for h in (0, 1):
            lanes = slice(128 * h, 128 * h + 128)
            ref[0, h, pl.ds(step, count), :] = ref[1, h, pl.ds(step - 1, count), :]
            ref[2, h, pl.ds(step, count), :] = ref[1, h, pl.ds(step + 1, count), :]
            ref[0, h, pl.ds(step, z.edge[k], stride=rows), :] = above[rim, lanes]
            ref[2, h, pl.ds(step + rows - 1, z.edge[k], stride=rows), :] = below[rim, lanes]


def fill_pads(z, pads, value, above, below):
    fill_center(z, pads, value)
    fill_shifted(z, pads, above, below)
    for a in (0, 2):
        clear_guards(z, pads, a)


def beside(left, right):
    lane = lax.broadcasted_iota(jnp.int32, (1, 128), 1)
    middle = pltpu.roll(jnp.where(lane >= 64, left[1], right[1]), 64, 1)
    return [
        jnp.where(lane >= 96, left[0], jnp.where(lane < 32, right[0], middle)),
        jnp.where(lane >= 96, left[2], jnp.where(lane < 32, right[2], 0.0)),
    ]


def band_operand(z, pads):
    parts = ([], [])
    for k in (1, 0):
        ref, step, count = pads[k], z.step[k], z.count[k]
        low, high = ([ref[a, h, pl.ds(step, count), :] for a in range(TAPS)] for h in (0, 1))
        before = [ref[a, 1, pl.ds(0, count), :] for a in range(TAPS)]
        after = [ref[a, 0, pl.ds(2 * step, count), :] for a in range(TAPS)]
        parts[0].append(jnp.concatenate(low + beside(before, high), axis=1))
        parts[1].append(jnp.concatenate(high + beside(low, after), axis=1))
    return [jnp.concatenate(part, axis=0) for part in parts]


def rim_operand(z, chain, depth):
    m = lax.broadcasted_iota(jnp.int32, (z.rims, 1), 0)
    large = m < z.rim[0]
    has_before = jnp.where(large, m, m - z.rim[0]) >= jnp.where(large, z.images[1], z.images[0])
    has_after = m < jnp.where(large, z.rim[0] - z.images[1], z.rims - z.images[0])
    low, high, before, after = [], [], [], []
    for r in range(depth + 1):
        at = z.guard + r * z.rims
        low.append(chain[0, pl.ds(at, z.rims), :])
        high.append(chain[1, pl.ds(at, z.rims), :])
        shifted = [chain[1, pl.ds(at - images, z.rims), :] for images in z.images]
        before.append(jnp.where(has_before, jnp.where(large, shifted[1], shifted[0]), 0.0))
        shifted = [chain[0, pl.ds(at + images, z.rims), :] for images in z.images]
        after.append(jnp.where(has_after, jnp.where(large, shifted[1], shifted[0]), 0.0))
    parts = ([], [])
    for n in range(depth - 1):
        rows = slice(n, n + TAPS)
        parts[0].append(jnp.concatenate(low[rows] + beside(before[rows], high[rows]), axis=1))
        parts[1].append(jnp.concatenate(high[rows] + beside(low[rows], after[rows]), axis=1))
    return [jnp.concatenate(part, axis=0) for part in parts]


def times(parts, weight):
    left = jnp.concatenate([part[h] for h in (0, 1) for part in parts], axis=0)
    both = jnp.concatenate([weight_matrix(weight.at[0]), weight_matrix(weight.at[1])], axis=1)
    result = dot(jnp.concatenate(split(left), axis=1), jnp.concatenate([both, both], axis=0))
    result = result[:, :128] + result[:, 128:]
    rows = result.shape[0] // 2
    return jnp.concatenate([result[:rows], result[rows:]], axis=1)


def convolve(z, own, above, below, depth, pads, chains, weight):
    r = z.rims
    fill_pads(z, pads, own, above[(depth - 1) * r :], below[:r])
    parts = [band_operand(z, pads)]
    if depth > 1:
        for side, (rim, chain) in enumerate(zip((above, below), chains)):
            rim_at, own_at = (z.guard, z.guard + depth * r) if side == 0 else (z.guard + r, z.guard)
            for h in (0, 1):
                chain[h, pl.ds(rim_at, depth * r), :] = rim[:, 128 * h : 128 * h + 128]
                for k in (0, 1):
                    row = z.step[k] + (0 if side == 0 else z.rows[k] - 1)
                    chain[h, pl.ds(own_at + z.rim[k], z.edge[k]), :] = pads[k][1, h, pl.ds(row, z.edge[k], stride=z.rows[k]), :]
            parts.append(rim_operand(z, chain, depth))
    result = times(parts, weight)
    n = z.total + (depth - 1) * r
    return result[: z.total], result[z.total : n], result[n:]


def image_sums(z, value):
    slot = lax.broadcasted_iota(jnp.int32, (z.slots, 1), 0)
    sums = jnp.zeros((z.slots, 128), F32)
    for k in (0, 1):
        line = value[z.start[k] : z.start[k] + z.step[k]]
        for j in range(1, z.blocks[k]):
            at = z.start[k] + j * z.step[k]
            line = line + value[at : at + z.step[k]]
        image = lax.broadcasted_iota(jnp.int32, (z.step[k], 1), 0) // z.rows[k]
        for i in range(z.images[k]):
            sums = jnp.where(slot == i + k * z.images[0], column_sum(jnp.where(image == i, line, 0.0)), sums)
    return sums


def image_rows(z, values, rims):
    parts = []
    for k in (1, 0):
        image = lax.broadcasted_iota(jnp.int32, (z.step[k], 1), 0) // z.rows[k]
        line = jnp.zeros((z.step[k], 128), F32)
        for i in range(z.images[k]):
            at = i + k * z.images[0]
            line = jnp.where(image == i, values[at : at + 1], line)
        parts += [line] * z.blocks[k]
    if rims:
        m = lax.broadcasted_iota(jnp.int32, (z.rims, 1), 0)
        image = jnp.where(m < z.rim[0], z.images[0] + m % z.images[1], (m - z.rim[0]) % z.images[0])
        line = jnp.zeros((z.rims, 128), F32)
        for at in range(sum(z.images)):
            line = jnp.where(image == at, values[at : at + 1], line)
        parts += [line] * rims
    return jnp.concatenate(parts, axis=0)


def channel_mean():
    a = lax.broadcasted_iota(jnp.int32, (LANES, 128), 0) // C
    b = lax.broadcasted_iota(jnp.int32, (LANES, 128), 1) % 64
    return jnp.where(a == b, 1.0 / C, 0.0).astype(F32)


def to_channels():
    a = lax.broadcasted_iota(jnp.int32, (128, LANES), 0)
    b = lax.broadcasted_iota(jnp.int32, (128, LANES), 1) // C
    return jnp.where(a == b, 1.0, 0.0).astype(F32)


def attention(value):
    return spread(value * value, channel_mean())


def pieces(source, target):
    return [(source.at[n], target.at[n]) for n in range(source.shape[0])]


def copies_of(pairs, sems, first=0):
    return [pltpu.make_async_copy(a, b, sems.at[first + n]) for n, (a, b) in enumerate(pairs)]


def start_all(copies):
    for copy in copies:
        copy.start()


def wait_all(copies):
    for copy in copies:
        copy.wait()


def start_kernel(z, small, large, up_s, up_l, t_s, t_l, x, bottom, top, copies, raw, half, sems):
    images = [(small, raw[0])] + pieces(large, raw[1])
    rest = [(up_s, raw[2])] + pieces(up_l, raw[3]) + [(t_s, raw[4]), (t_l, raw[5])]
    loads = copies_of(images + rest, sems)
    start_all(loads)
    r, n = z.rims, REACH * z.rims
    tail = n + 2 * r
    for ref in (bottom, top):
        ref[pl.ds(tail, z.slots), :] = jnp.zeros((z.slots, LANES), F32)
    wait_all(loads[: len(images)])
    to_matrix(z, raw[:2], half)
    value = whole(half)
    x[...] = value
    moments(z, value, copies)
    for h in (0, 1):
        lanes = pl.ds(128 * h, 128)
        take_rims(z, half.at[h], REACH, bottom.at[pl.ds(0, n), lanes], top.at[pl.ds(0, n), lanes])
    wait_all(loads[len(images) :])
    for k in (0, 1):
        width, rows = HEIGHTS[k], z.rows[k]
        for i in range(z.images[k]):
            slot = pl.ds(tail + i + k * z.images[0], 1)
            for d in (0, 1):
                to_bottom, to_top = n + (1 - d) * r + z.rim[k] + i, n + d * r + z.rim[k] + i
                for j in range(z.blocks[k]):
                    lanes, at = pl.ds(LANES * j, LANES), j * z.images[k]
                    if d < rows:
                        bottom[pl.ds(to_bottom + at, 1), :] = raw[2 + k][i, pl.ds(rows - 1 - d, 1), lanes]
                        top[pl.ds(to_top + at, 1), :] = raw[2 + k][i, pl.ds(d, 1), lanes]
                    else:
                        bottom[pl.ds(to_bottom + at, 1), :] = jnp.zeros((1, LANES), F32)
                        top[pl.ds(to_top + at, 1), :] = jnp.zeros((1, LANES), F32)
                if d < rows:
                    bottom[slot, pl.ds(128 * (1 - d), width)] = raw[4 + k][i, pl.ds(rows - 1 - d, 1), :]
                    top[slot, pl.ds(128 * d, width)] = raw[4 + k][i, pl.ds(d, 1), :]


def banded(taps, ref):
    row = lax.broadcasted_iota(jnp.int32, (128, 128), 0) // C
    lane = group_of(128)
    for a in range(TAPS):
        main = jnp.zeros((128, 128), F32)
        for b in range(TAPS):
            main = jnp.where(row - lane + 1 == b, taps[a][b], main)
        before = jnp.where(lane[:C] == 0, taps[a][0][:C], 0.0)
        after = jnp.where(lane[:C] == 3, taps[a][2][:C], 0.0)
        for n, part in enumerate(split(jnp.concatenate([main, before, after], axis=0))):
            ref[n, pl.ds(a * TAP_ROWS, TAP_ROWS), :] = part


def weight_matrix(ref):
    main = [ref[pl.ds(a * TAP_ROWS, 128), :] for a in range(TAPS)]
    before, after = ([ref[pl.ds(a * TAP_ROWS + 128 + n * C, C), :] for a in range(TAPS)] for n in (0, 1))
    return jnp.concatenate(
        main + [after[0], before[1], after[1], before[0], after[2], jnp.zeros((2 * C, 128), BF16), before[2]], axis=0
    )


def prepare_kernel(z, first, second, up_s, up_l, t_s, t_l, g1, b1, g2, b2, x, w1, w2, weights, affine, upstream, teacher, x_copy, raw, kept, kept_u, rows, half, sems):
    targets = tuple(raw) + tuple(rows.at[pl.ds(n, 1), :] for n in range(4))
    refs = (first, second, up_s, up_l, t_s, t_l, g1, b1, g2, b2)
    loads = [pltpu.make_async_copy(a, b, sems.at[n]) for n, (a, b) in enumerate(zip(refs, targets))]
    start_all(loads)
    stores = [pltpu.make_async_copy(x, x_copy, sems.at[13])]
    stores[0].start()
    wait_all(loads)
    to_matrix(z, raw[2:4], half)
    kept_u[...] = whole(half)
    stores.append(pltpu.make_async_copy(kept_u, upstream, sems.at[10]))
    stores[1].start()
    for n, (source, forward) in enumerate(zip(raw[:2], (w1, w2))):
        tiles = []
        for a in range(TAPS):
            line = [jnp.concatenate([source[a, b]] * 4, axis=1) for b in range(TAPS)]
            tiles.append([jnp.concatenate([tap] * 4, axis=0) for tap in line])
        turned = [[tiles[TAPS - 1 - a][TAPS - 1 - b].T for b in range(TAPS)] for a in range(TAPS)]
        banded(tiles, forward)
        banded(turned, kept.at[n])
        stores.append(pltpu.make_async_copy(kept.at[n], weights.at[n], sems.at[11 + n]))
        stores[-1].start()
    taps = sum(raw[0][a, b] for a in range(TAPS) for b in range(TAPS))
    pivot = dot(jnp.broadcast_to(gelu(rows[1:2]), (8, C)), taps)[0:1]
    affine[...] = jnp.concatenate([jnp.concatenate([rows[...], pivot], axis=0)] * BLOCK, axis=1)
    teacher[...] = jnp.zeros(teacher.shape, F32)
    for k, ref in ((0, raw[4]), (1, raw[5])):
        for i in range(z.images[k]):
            line = ref[i]
            for j in range(z.blocks[k]):
                at = z.start[k] + j * z.step[k] + i * z.rows[k]
                for lane in (0, 64):
                    teacher[pl.ds(at, z.rows[k]), pl.ds(lane, BLOCK)] = line[:, j * BLOCK : (j + 1) * BLOCK]
    wait_all(stores)


def normed_by(stats):
    return lambda v: (v - stats[0:1]) * stats[1:2]


def activation(center, scale, gain, bias):
    factor = scale * gain
    offset = bias - center * factor
    return lambda v: gelu(v * factor + offset)


def first_kernel(z, x, above, below, gathered, affine, weight, hidden, h_above, h_below, stats, copies, pads, chains):
    n = REACH * z.rims
    center, scale = merged(z, gathered)
    act = activation(center, scale, affine[0:1], affine[1:2])
    own = act(x[...])
    up, down = act(above[pl.ds(0, n), :]) * inside(z, 4, True), act(below[pl.ds(0, n), :]) * inside(z, 4, False)
    own, up, down = convolve(z, own, up, down, 4, pads, chains, weight)
    moments(z, own, copies)
    hidden[...] = own
    h_above[...] = up
    h_below[...] = down
    stats[0:1] = center
    stats[1:2] = scale


def second_kernel(z, hidden, h_above, h_below, gathered, affine, weight, x, x_above, x_below, teacher, out, o_above, o_below, near, stats, copies, pads, chains):
    center, scale = merged(z, gathered)
    act = activation(center, scale, affine[2:3], affine[3:4])
    r = z.rims
    own = act(hidden[...])
    up, down = act(h_above[...]) * inside(z, 3, True), act(h_below[...]) * inside(z, 3, False)
    own, up, down = convolve(z, own, up, down, 3, pads, chains, weight)
    own = x[...] + own
    amap = attention(own)
    lane = lax.broadcasted_iota(jnp.int32, (1, 128), 1)
    sums = image_sums(z, amap * jnp.where(lane < 64, amap, teacher[...]))
    copies[...] = jnp.concatenate([sums] * z.peers, axis=0)
    out[...] = own
    o_above[...] = x_above[pl.ds(2 * r, 2 * r), :] + up
    o_below[...] = x_below[pl.ds(0, 2 * r), :] + down
    near[0] = h_above[pl.ds(2 * r, r), :]
    near[1] = h_below[pl.ds(0, r), :]
    stats[0:1] = center
    stats[1:2] = scale


def tap_rows(q):
    return 128 + C if q < 0 else q * C


def tap_product(z, operand, own, above, below, pads):
    fill_center(z, pads, own)
    fill_shifted(z, pads, above, below)
    columns = []
    for a in range(TAPS):
        columns.append(
            jnp.concatenate([pads[k][TAPS - 1 - a, h, pl.ds(z.step[k], z.count[k]), :] for h in (0, 1) for k in (1, 0)], axis=0)
        )
    used = [jnp.concatenate([operand[n, pl.ds(0, 128 + C), :], operand[n, pl.ds(256 - C, C), :]], axis=0) for n in (0, 1)]
    return product(used, split(jnp.concatenate(columns, axis=1)))


def tap_sums(result, tiles, first_group):
    group = group_of()
    for a in range(TAPS):
        for b in range(TAPS):
            total = None
            for p in range(4):
                at = tap_rows(p + b - 1)
                part = result[at : at + C, 128 * a : 128 * a + 128]
                total = part if total is None else jnp.where(group == p, part, total)
            tile, slot = divmod(first_group + a * TAPS + b, 4)
            tiles[tile] = jnp.where(group == slot, spread_groups(total), tiles[tile])


def tap_counts(z, turned, tiles, first_group):
    group = group_of()
    m = lax.broadcasted_iota(jnp.int32, (1, 2 * z.total), 1) % z.total
    row = jnp.where(m < z.start[0], m % z.rows[1], (m - z.start[0]) % z.rows[0])
    height = jnp.where(m < z.start[0], z.rows[1], z.rows[0])
    at = lax.axis_index("row")
    lost = {
        0: (row == height - 1) & (at == z.peers - 1),
        2: (row == 0) & (at == 0),
    }
    for a in range(TAPS):
        column = jnp.sum(jnp.where(lost[a], 0.0, turned) if a in lost else turned, axis=1, keepdims=True)
        used = jnp.concatenate([column[: 128 + C], column[256 - C :]], axis=0)
        for b in range(TAPS):
            total = sum(used[tap_rows(p + b - 1) : tap_rows(p + b - 1) + C] for p in range(4))
            tile, slot = divmod(first_group + a * TAPS + b, 4)
            tiles[tile] = jnp.where(group == slot, total, tiles[tile])


def turned_operand(z, value, pads, kept):
    fill_center(z, pads, value)
    lane = lax.broadcasted_iota(jnp.int32, (1, 128), 1)
    halves = ([], [])
    for k in (1, 0):
        ref, step, count = pads[k], z.step[k], z.count[k]
        low, high = ref[1, 0, pl.ds(step, count), :], ref[1, 1, pl.ds(step, count), :]
        before, after = ref[1, 1, pl.ds(0, count), :], ref[1, 0, pl.ds(2 * step, count), :]
        for part, main, left, right in ((halves[0], low, before, high), (halves[1], high, low, after)):
            part.append(jnp.concatenate([main, jnp.where(lane >= 96, left, jnp.where(lane < 32, right, 0.0))], axis=1))
    turned = jnp.concatenate(halves[0] + halves[1], axis=0).T
    parts = split(turned)
    for n in (0, 1):
        kept[n] = parts[n]
    return turned


def first_operand_kernel(z, x, hidden, h_above, h_below, above, below, stats, affine, teacher, upstream, weights, left, packed, teachers, spread_u, near_u, pads, chains, kept, kept_w, kept_u, pixels, kept_t, kept_c, kept_packed, sems):
    r, own = z.rims, pl.ds(0, z.total)
    loads = [pltpu.make_async_copy(upstream, kept_u.at[own, :], sems.at[0]), pltpu.make_async_copy(weights.at[1], kept_w, sems.at[1])]
    start_all(loads)
    act = activation(stats[0:1], stats[1:2], affine[0:1], affine[1:2])
    value = turned_operand(z, act(x[...]), pads, kept)
    stores = [pltpu.make_async_copy(kept, left, sems.at[2])]
    stores[0].start()
    tiles = [jnp.zeros((C, 128), F32) for _ in range(BACK_LANES // 128)]
    tap_counts(z, value, tiles, ONES)
    pivot = affine[4:5]
    result = tap_product(
        z, kept, hidden[...] - pivot, (h_above[pl.ds(2 * r, r), :] - pivot) * inside(z, 1, True),
        (h_below[pl.ds(0, r), :] - pivot) * inside(z, 1, False), pads,
    )
    tap_sums(result, tiles, HIDDEN)
    kept_packed[...] = jnp.concatenate(tiles, axis=1)
    stores.append(pltpu.make_async_copy(kept_packed, packed, sems.at[6]))
    stores[1].start()
    pixels[own, :] = teacher[...]
    pixels[pl.ds(z.total, 4 * r), :] = jnp.zeros((4 * r, 128), F32)
    n = (REACH + 2) * r
    for side, ref in enumerate((above, below)):
        for d in (0, 1):
            for k in (0, 1):
                line = ref[pl.ds(n + k * z.images[0], z.images[k]), pl.ds(128 * d, 128)]
                for j in range(z.blocks[k]):
                    at = z.total + (2 * side + d) * r + z.rim[k] + j * z.images[k]
                    pixels[pl.ds(at, z.images[k]), pl.ds(0, BLOCK)] = line[:, j * BLOCK : (j + 1) * BLOCK]
    kept_t[...] = spread(pixels[...], to_channels())
    stores.append(pltpu.make_async_copy(kept_t, teachers, sems.at[3]))
    stores[2].start()
    n = REACH * r
    up, down = above[pl.ds(n, 2 * r), :] * inside(z, 2, True), below[pl.ds(n, 2 * r), :] * inside(z, 2, False)
    kept_u[pl.ds(z.total, r), :] = up[r:]
    kept_u[pl.ds(z.total + r, r), :] = down[:r]
    wait_all(loads)
    stores.append(pltpu.make_async_copy(kept_u, near_u, sems.at[5]))
    stores[3].start()
    kept_c[...] = jnp.concatenate(convolve(z, kept_u[own, :], up, down, 2, pads, chains, kept_w), axis=0)
    stores.append(pltpu.make_async_copy(kept_c, spread_u, sems.at[4]))
    stores[4].start()
    wait_all(stores)


def second_operand_kernel(z, hidden, near, stats, affine, out, o_above, o_below, teachers, spread_u, near_u, weights, out_copy, hidden_copy, left, shifts, by_map, by_teacher, up, pads, chains, kept_t, kept_u, kept_w, kept_s, sems):
    r, total = z.rims, z.total
    loads = [
        pltpu.make_async_copy(teachers, kept_t, sems.at[0]),
        pltpu.make_async_copy(weights.at[1], kept_w, sems.at[1]),
        pltpu.make_async_copy(spread_u, kept_u, sems.at[2]),
    ]
    start_all(loads)
    stores = [
        pltpu.make_async_copy(out, out_copy, sems.at[4]),
        pltpu.make_async_copy(hidden, hidden_copy.at[pl.ds(0, total), :], sems.at[7]),
        pltpu.make_async_copy(near.at[0], hidden_copy.at[pl.ds(total, r), :], sems.at[8]),
        pltpu.make_async_copy(near.at[1], hidden_copy.at[pl.ds(total + r, r), :], sems.at[9]),
        pltpu.make_async_copy(near_u, up, sems.at[10]),
    ]
    start_all(stores)
    normed = normed_by(stats)(jnp.concatenate([hidden[...], near[0], near[1]], axis=0))
    shifted = normed * affine[2:3] + affine[3:4]
    turned_operand(z, gelu(shifted[:total]), pads, left)
    ones = jnp.ones((total, 1), F32)
    masks = jnp.concatenate([ones, inside(z, 1, True), inside(z, 1, False)], axis=0)
    slopes = gelu_slope(shifted) * masks
    o = jnp.concatenate([out[...], o_above[...] * inside(z, 2, True), o_below[...] * inside(z, 2, False)], axis=0)
    for_map = spread(attention(o), to_channels()) * o
    wait_all(loads)
    for_teacher = kept_t[...] * o
    kept_s[0] = kept_u[...] * slopes
    stores += copies_of(pieces(kept_s, shifts), sems, 11)
    stores[-3].start()
    for n, value, ref in ((1, for_map, by_map), (2, for_teacher, by_teacher)):
        own, before, after = value[:total], value[total : total + 2 * r], value[total + 2 * r :]
        ref[...] = jnp.concatenate([own, before[r:], after[:r]], axis=0)
        kept_s[n] = jnp.concatenate(convolve(z, own, before, after, 2, pads, chains, kept_w), axis=0) * slopes
        stores[n - 3].start()
    wait_all(stores)


def upstream_kernel(z, gathered, up, shifts, left_1, left_2, packed, by_map, by_teacher, hidden, stats, dout, dshift, d_above, d_below, slabs, kept_s, kept_left, kept_h, kept_packed, pads, more_pads, sems):
    r, total = z.rims, z.total
    loads = copies_of(
        pieces(shifts, kept_s) + pieces(left_1, kept_left) + [(hidden.at[pl.ds(0, total), :], kept_h), (packed, kept_packed)], sems
    )
    start_all(loads)
    lane = lax.broadcasted_iota(jnp.int32, (z.slots, 128), 1)
    sums = sum(gathered[pl.ds(n * z.slots, z.slots), :] for n in range(z.peers))
    square = jnp.sum(jnp.where(lane < 64, sums, 0.0), axis=1, keepdims=True)
    cross = jnp.sum(jnp.where(lane < 64, 0.0, sums), axis=1, keepdims=True)
    inverse = lax.rsqrt(square + map_eps)
    inner = beta_weight * (square * inverse - cross) * inverse
    shape = (z.slots, 128)
    for_map = (beta_weight - inner) * inverse * inverse * (2.0 / C)
    for_teacher = beta_weight * inverse * (2.0 / C)
    for_map, for_teacher = (wide(image_rows(z, jnp.broadcast_to(v, shape), 2)) for v in (for_map, for_teacher))
    value = up[...] + for_map * by_map[...] - for_teacher * by_teacher[...]
    dout[...] = value[:total]
    wait_all(loads[:3])
    shift = kept_s[0] + for_map * kept_s[1] - for_teacher * kept_s[2]
    pre, above, below = shift[:total], shift[total : total + r], shift[total + r :]
    dshift[...] = pre
    d_above[...] = above
    d_below[...] = below
    second = tap_product(z, left_2, value[:total], value[total : total + r], value[total + r :], pads)
    wait_all(loads[3:5])
    first = tap_product(z, kept_left, pre, above, below, more_pads)
    wait_all(loads[5:])
    normed = normed_by(stats)(kept_h[...])
    tiles = [kept_packed[:, 128 * n : 128 * n + 128] for n in range(BACK_LANES // 128)]
    group = group_of()
    tiles[0] = jnp.where(group == BIAS, fold(column_sum(pre)), jnp.where(group == GAIN, fold(column_sum(pre * normed)), tiles[0]))
    tap_sums(second, tiles, SECOND)
    tap_sums(first, tiles, LEFT)
    line = jnp.concatenate(tiles, axis=1)
    for d in range(z.devices):
        slabs[d] = line[d % C : d % C + 1]


def write_kernel(z, out, x, hidden, weights, first_stats, stats, order, out_s, out_l, first_normed, normed, weight, kept, kept_x, kept_h, half, sems):
    loads = [pltpu.make_async_copy(a, b, sems.at[n]) for n, (a, b) in enumerate(((out, kept), (x, kept_x), (hidden, kept_h), (weights.at[0], weight)))]
    start_all(loads)
    loads[0].wait()
    put_halves(half, kept[...])
    from_matrix(z, half, (out_s, out_l))
    loads[1].wait()
    first_normed[...] = normed_by(first_stats)(kept_x[...])
    loads[2].wait()
    normed[...] = normed_by(stats)(kept_h[...])
    loads[3].wait()


def norm_sums(total):
    group = group_of()
    return [wide(spread_groups(jnp.where(group == n, total[:, :128], 0.0))) for n in (BIAS, GAIN)]


def hidden_kernel(z, gathered, dshift, d_above, d_below, second_normed, stats, affine, weight, first_normed, pre_ref, gain_out, bias_out, slabs, pads):
    total = jnp.sum(gathered[...], axis=0)
    bias_sum, gain_sum = norm_sums(total)
    bias_out[...] = bias_sum[:, :C]
    gain_out[...] = gain_sum[:, :C]
    bias_mean, gain_mean = bias_sum / z.pixels, gain_sum / z.pixels
    factor = affine[2:3] * stats[1:2]
    r, total_rows = z.rims, z.total

    def back(d, normed):
        return factor * (d - bias_mean - normed * gain_mean)

    own = back(dshift[...], second_normed[pl.ds(0, total_rows), :])
    up = back(d_above[...], second_normed[pl.ds(total_rows, r), :]) * inside(z, 1, True)
    down = back(d_below[...], second_normed[pl.ds(total_rows + r, r), :]) * inside(z, 1, False)
    grad, _, _ = convolve(z, own, up, down, 1, pads, None, weight)
    normed = first_normed[...]
    pre = grad * gelu_slope(normed * affine[0:1] + affine[1:2])
    pre_ref[...] = pre
    lane = lax.broadcasted_iota(jnp.int32, (1, 128), 1)
    taps = TAPS * TAPS * C

    def along(row):
        return jnp.concatenate([row[:, :128]] * 3, axis=1)[:, :taps]

    second, left, against, ones = (total[:, n * C : n * C + taps] for n in (SECOND, LEFT, HIDDEN, ONES))
    against = along(stats[1:2]) * (against - along(stats[0:1] - affine[4:5]) * ones)
    first = along(factor) * (left - along(bias_mean) * ones - along(gain_mean) * against)
    sums = jnp.where(lane < C, fold(column_sum(pre)), fold(column_sum(pre * normed)))
    line = jnp.concatenate([sums[:, : 2 * C], second, first], axis=1)
    slabs[...] = jnp.broadcast_to(line[None], slabs.shape)


def back_kernel(z, gathered, pre, normed, stats, affine, dout, back_s, back_l, one, two, gain_out, bias_out, half, lines):
    bias_sum, gain_sum = norm_sums(jnp.sum(gathered[:, :, pl.ds(0, 128)], axis=0))
    bias_out[...] = bias_sum[:, :C]
    gain_out[...] = gain_sum[:, :C]
    value = dout[...] + affine[0:1] * stats[1:2] * (pre[...] - bias_sum / z.pixels - normed[...] * (gain_sum / z.pixels))
    put_halves(half, value)
    from_matrix(z, half, (back_s, back_l))
    for d in range(C):
        lines[pl.ds(d, 1), :] = gathered[d]
    for ref, group in ((two, LAST_SECOND), (one, LAST_FIRST)):
        for a in range(TAPS):
            for b in range(TAPS):
                at = (group + a * TAPS + b) * C
                ref[a, b] = lines[:, pl.ds(at, C)]


def call(body, ins, outs, scratch=(), sems=0):
    space = {"v": pltpu.VMEM, "h": pltpu.HBM, "V": pltpu.VMEM}
    shapes = []
    for item in scratch:
        if isinstance(item, list):
            shapes.append([pltpu.VMEM(*s) for s in item])
        else:
            shapes.append(pltpu.VMEM(*item))
    if sems:
        shapes.append(pltpu.SemaphoreType.DMA((sems,)))
    run = pl.pallas_call(
        body,
        out_shape=[jax.ShapeDtypeStruct(shape, kind) if s == "v" else space[s](shape, kind) for s, shape, kind in outs],
        in_specs=[pl.BlockSpec(memory_space=space[s]) for s in ins],
        out_specs=[pl.BlockSpec(memory_space=space[s]) for s, _, _ in outs],
        scratch_shapes=shapes,
        compiler_params=pltpu.CompilerParams(vmem_limit_bytes=VMEM_LIMIT),
    )
    return lambda *args: run(
        *(pltpu.with_memory_space_constraint(arg, pltpu.HBM) if s == "h" else arg for s, arg in zip(ins, args))
    )


def exchange(lines, axes):
    shape = lines.shape
    if len(shape) == 2:
        lines = lines.reshape(math.prod(lax.axis_size(axis) for axis in axes), -1, 128)
    return lax.all_to_all(lines, axes, 0, 0, tiled=True).reshape(shape)


def beyond(z, bottom, top, depths):
    hops = max(-(-depth // rows) for rows in z.rows for depth in depths)
    above, below = [], []
    for hop in range(1, hops + 1):
        above.append(lax.ppermute(bottom, "row", [(i, i + hop) for i in range(z.peers - hop)]))
        below.append(lax.ppermute(top, "row", [(i + hop, i) for i in range(z.peers - hop)]))
    if hops == 1:
        return above[0], below[0]
    up, down = [], []
    base = 0
    for depth in depths:
        for n in range(depth):
            for k in (1, 0):
                hop, back = divmod(depth - 1 - n, z.rows[k])
                at = base + (depth - 1 - back) * z.rims + z.rim[k]
                up.append(above[hop][at : at + z.edge[k]])
                hop, back = divmod(n, z.rows[k])
                at = base + back * z.rims + z.rim[k]
                down.append(below[hop][at : at + z.edge[k]])
        base += depth * z.rims
    up.append(jnp.concatenate([pixel_rows(z, above, base, 1, 1), pixel_rows(z, above, base, 0, 1)], axis=1))
    down.append(jnp.concatenate([pixel_rows(z, below, base, 0, 0), pixel_rows(z, below, base, 1, 0)], axis=1))
    return jnp.concatenate(up, axis=0), jnp.concatenate(down, axis=0)


def pixel_rows(z, bands, base, distance, last):
    lines = []
    for k in (0, 1):
        hop, back = divmod(distance, z.rows[k])
        at = base + k * z.images[0]
        half = 128 * abs(last - back)
        lines.append(bands[hop][at : at + z.images[k], half : half + 128])
    lines.append(jnp.zeros((z.slots - sum(z.images), 128), F32))
    return jnp.concatenate(lines, axis=0)


def local(
    image_small, image_large, teacher_small, teacher_large, upstream_small, upstream_large,
    conv_first, gain_first, bias_first, conv_second, gain_second, bias_second,
):
    peers = lax.axis_size("row")
    devices = lax.axis_size("img") * peers
    z = Sizes(image_small.shape, image_large.shape, devices, peers)
    body = lambda function: functools.partial(function, z)
    r = z.rims
    full, half, pair = (z.total, LANES), (2, z.total, 128), (2 * devices, 128)
    weight, left = (2, TAPS * TAP_ROWS, 128), (2, 256, 2 * z.total)
    images = [image_small, image_large, upstream_small, upstream_large, teacher_small, teacher_large]
    f = lambda space, *shape: (space, shape, F32)
    depths = (REACH, 2)
    rim_rows = sum(depths) * r + z.slots

    x, bottom, top, copies = call(
        body(start_kernel),
        "hhhhhh",
        [("v", full, F32), f("v", rim_rows, LANES), f("v", rim_rows, LANES), ("V", pair, F32)],
        [[(a.shape, F32) for a in images], (half, F32)],
        4 + 2 * z.images[1],
    )(*images)
    gathered = exchange(copies, AXES)
    above, below = beyond(z, bottom, top, depths)
    params = [conv_first, conv_second] + images[2:]
    w1, w2, weights, affine, upstream, teacher, x_copy = call(
        body(prepare_kernel),
        "hhhhhhhhhhv",
        [("v", weight, BF16), ("v", weight, BF16), ("h", (2,) + weight, BF16), f("v", 5, LANES), ("h", full, F32), f("v", z.total, 128), ("h", full, F32)],
        [[(a.shape, F32) for a in params], ((2,) + weight, BF16), (full, F32), ((4, C), F32), (half, F32)],
        14,
    )(*params, *(v.reshape(1, C) for v in (gain_first, bias_first, gain_second, bias_second)), x)

    hidden, h_above, h_below, stats_one, copies = call(
        body(first_kernel),
        "vvvvvv",
        [("v", full, F32), f("v", 3 * r, LANES), f("v", 3 * r, LANES), f("v", 2, LANES), ("V", pair, F32)],
        [z.pads(), z.chains(4)],
    )(x, above, below, gathered, affine, w1)
    gathered = exchange(copies, AXES)
    extended, near_rows = z.total + 4 * r, z.total + 2 * r
    left_one, packed, teachers, spread_u, near_u = call(
        body(first_operand_kernel),
        "vvvvvvvvvhh",
        [("h", left, BF16), f("h", C, BACK_LANES), f("h", extended, LANES), f("h", near_rows, LANES), f("h", near_rows, LANES)],
        [
            z.pads(), z.chains(2), (left, BF16), (weight, BF16), ((near_rows, LANES), F32), ((extended, 128), F32),
            ((extended, LANES), F32), ((near_rows, LANES), F32), ((C, BACK_LANES), F32),
        ],
        7,
    )(x, hidden, h_above, h_below, above, below, stats_one, affine, teacher, upstream, weights)
    gathered, near_u = lax.optimization_barrier((gathered, near_u))

    map_shape = (peers * z.slots, 128)
    out, o_above, o_below, near, stats_two, copies = call(
        body(second_kernel),
        "vvvvvvvvvv",
        [("v", full, F32), f("v", 2 * r, LANES), f("v", 2 * r, LANES), f("v", 2, r, LANES), f("v", 2, LANES), ("V", map_shape, F32)],
        [z.pads(), z.chains(3)],
    )(hidden, h_above, h_below, gathered, affine, w2, x, above, below, teacher)
    gathered = exchange(copies, ("row",))
    out_copy, hidden_copy, left_two, shifts, by_map, by_teacher, up = call(
        body(second_operand_kernel),
        "vvvvvvvhhhh",
        [
            ("h", full, F32), f("h", near_rows, LANES), ("v", left, BF16), f("h", 3, near_rows, LANES),
            f("v", near_rows, LANES), f("v", near_rows, LANES), f("v", near_rows, LANES),
        ],
        [
            z.pads(), z.chains(2), ((extended, LANES), F32), ((near_rows, LANES), F32), (weight, BF16),
            ((3, near_rows, LANES), F32),
        ],
        14,
    )(hidden, near, stats_two, affine, out, o_above, o_below, teachers, spread_u, near_u, weights)

    dout, dshift, d_above, d_below, slabs = call(
        body(upstream_kernel),
        "vvhhvhvvhv",
        [("v", full, F32), ("v", full, F32), f("v", r, LANES), f("v", r, LANES), f("V", devices, 1, BACK_LANES)],
        [((3, near_rows, LANES), F32), (left, BF16), (full, F32), ((C, BACK_LANES), F32), z.pads(), z.pads()],
        7,
    )(gathered, up, shifts, left_one, left_two, packed, by_map, by_teacher, hidden_copy, stats_two)
    gathered = exchange(slabs, AXES)
    out_s, out_l, first_normed, second_normed, weight_back = call(
        body(write_kernel),
        "hhhhvvv",
        [("v", image_small.shape, F32), ("v", image_large.shape, F32), ("v", full, F32), f("v", near_rows, LANES), ("v", weight, BF16)],
        [(full, F32), (full, F32), ((near_rows, LANES), F32), (half, F32)],
        4,
    )(out_copy, x_copy, hidden_copy, weights, stats_one, stats_two, d_above)

    pre, gain_two, bias_two, slabs = call(
        body(hidden_kernel),
        "vvvvvvvvv",
        [("v", full, F32), f("v", 1, C), f("v", 1, C), f("V", devices, 1, LAST_LANES)],
        [z.pads()],
    )(gathered, dshift, d_above, d_below, second_normed, stats_two, affine, weight_back, first_normed)
    gathered = exchange(slabs, AXES)

    back_s, back_l, one, two, gain_one, bias_one = call(
        body(back_kernel),
        "vvvvvv",
        [("v", a.shape, F32) for a in (image_small, image_large, conv_first, conv_second)] + [f("v", 1, C), f("v", 1, C)],
        [(half, F32), ((C, LAST_LANES), F32)],
    )(gathered, pre, first_normed, stats_one, affine, dout)
    return (
        out_s, out_l, back_s, back_l,
        one, gain_one.reshape(C), bias_one.reshape(C),
        two, gain_two.reshape(C), bias_two.reshape(C),
    )


def solution(mesh):
    split_bands, everywhere = P("img", "row", None), P()
    return jax.shard_map(
        local,
        mesh=mesh,
        in_specs=(split_bands,) * 6 + (everywhere,) * 6,
        out_specs=(split_bands,) * 4 + (everywhere,) * 6,
        check_vma=False,
    )
```

```python
import functools
import math

import jax
import jax.numpy as jnp
from jax import lax
from jax.experimental import pallas as pl
from jax.experimental.pallas import tpu as pltpu
from jax.sharding import PartitionSpec as P

C = 32
HS = 32
HL = 64
HEIGHTS = (HS, HL)

norm_eps = 1e-05
map_eps = 1e-06
beta_weight = 1000.0
AXES = ("img", "row")
BLOCK = 8
LANES = BLOCK * C
TAPS = 3
DEPTH = TAPS * 128 + 256
TAP_ROWS = 128 + 2 * C
REACH = 4
ROOT = math.sqrt(2.0 / math.pi)
CUBE = 0.044715
F32 = jnp.float32
BF16 = jnp.bfloat16
VMEM_LIMIT = 32 * 1024 * 1024
BIAS, GAIN, SECOND, LEFT, HIDDEN, ONES = 0, 1, 2, 11, 20, 29
BACK_LANES = 1280
LAST_SECOND, LAST_FIRST, LAST_LANES = 2, 11, 640


class Sizes:
    def __init__(self, small, large, devices, peers):
        self.images = (small[0], large[0])
        self.rows = (small[1], large[1])
        self.blocks = (HS // BLOCK, HL // BLOCK)
        self.step = tuple(n * r for n, r in zip(self.images, self.rows))
        self.count = tuple(b * s for b, s in zip(self.blocks, self.step))
        self.edge = tuple(b * n for b, n in zip(self.blocks, self.images))
        self.start = (self.count[1], 0)
        self.rim = (self.edge[1], 0)
        self.total = sum(self.count)
        self.rims = sum(self.edge)
        self.slots = -(-sum(self.images) // 8) * 8
        self.guard = -(-max(self.images) // 8) * 8
        self.devices = devices
        self.peers = peers
        self.here = float(self.total * BLOCK)
        self.pixels = self.here * devices

    def pads(self):
        return [((TAPS, 2, self.count[k] + 2 * self.step[k], 128), F32) for k in (0, 1)]

    def chains(self, depth):
        return [((2, 2 * self.guard + (depth + 1) * self.rims, 128), F32)] * 2


def split(value):
    high = value.astype(BF16)
    return high, (value - high.astype(F32)).astype(BF16)


def dot(left, right):
    return lax.dot_general(left, right, (((1,), (0,)), ((), ())), preferred_element_type=F32)


def product(left, right):
    if left[0].shape[1] % 128:
        return dot(left[0], right[0]) + (dot(left[0], right[1]) + dot(left[1], right[0]))
    return dot(
        jnp.concatenate([left[0], left[0], left[1]], axis=1), jnp.concatenate([right[0], right[1], right[0]], axis=0)
    )


def spread(left, right):
    right = right.astype(BF16)
    return dot(jnp.concatenate(split(left), axis=1), jnp.concatenate([right, right], axis=0))


def gelu(s):
    return 0.5 * s * (1.0 + jnp.tanh(ROOT * (s + CUBE * s * s * s)))


def gelu_slope(s):
    square = s * s
    t = jnp.tanh(ROOT * s * (1.0 + CUBE * square))
    return 0.5 * (1.0 + t) + 0.5 * s * (1.0 - t * t) * ROOT * (1.0 + 3.0 * CUBE * square)


def spread_groups(row):
    row = row + pltpu.roll(row, 64, 1)
    return row + pltpu.roll(row, 32, 1)


def fold(row):
    return spread_groups(row[:, :128] + row[:, 128:])


def wide(row):
    return jnp.concatenate([row, row], axis=1)


def group_of(rows=1, lanes=128):
    return lax.broadcasted_iota(jnp.int32, (rows, lanes), 1) // C


def column_sum(value):
    return jnp.sum(value, axis=0, keepdims=True)


def send_lines(z, ref, lines):
    for n, line in enumerate(lines):
        ref[pl.ds(n, z.devices, stride=len(lines)), :] = jnp.broadcast_to(line, (z.devices, 128))


def moments(z, value, ref):
    few = min(8, z.total)
    pivot = fold(column_sum(value[:few])) / float(few * BLOCK)
    off = value - wide(pivot)
    first, second = fold(column_sum(off)), fold(column_sum(off * off))
    send_lines(z, ref, [pivot + first / z.here, second - first * first / z.here])


def merged(z, ref):
    means = ref[pl.ds(0, z.devices, stride=2), :]
    center = jnp.mean(means, axis=0, keepdims=True)
    off = means - center
    within = jnp.mean(ref[pl.ds(1, z.devices, stride=2), :], axis=0, keepdims=True)
    variance = within / z.here + jnp.mean(off * off, axis=0, keepdims=True)
    return wide(center), wide(lax.rsqrt(variance + norm_eps))


def put_halves(ref, value):
    ref[0] = value[:, :128]
    ref[1] = value[:, 128:]


def whole(ref):
    return jnp.concatenate([ref[0], ref[1]], axis=1)


def to_matrix(z, refs, half):
    for k in (0, 1):
        for j in range(z.blocks[k]):
            at = z.start[k] + j * z.step[k]
            for i in range(z.images[k]):
                for h in (0, 1):
                    half[h, pl.ds(at + i * z.rows[k], z.rows[k]), :] = refs[k][i, :, pl.ds(LANES * j + 128 * h, 128)]


def from_matrix(z, half, refs):
    for k in (0, 1):
        for j in range(z.blocks[k]):
            at = z.start[k] + j * z.step[k]
            for i in range(z.images[k]):
                for h in (0, 1):
                    refs[k][i, :, pl.ds(LANES * j + 128 * h, 128)] = half[h, pl.ds(at + i * z.rows[k], z.rows[k]), :]


def take_rims(z, half, depth, bottom, top):
    for k in (0, 1):
        for d in range(1, depth + 1):
            to_bottom = pl.ds((depth - d) * z.rims + z.rim[k], z.edge[k])
            to_top = pl.ds((d - 1) * z.rims + z.rim[k], z.edge[k])
            if d <= z.rows[k]:
                bottom[to_bottom, :] = half[pl.ds(z.start[k] + z.rows[k] - d, z.edge[k], stride=z.rows[k]), :]
                top[to_top, :] = half[pl.ds(z.start[k] + d - 1, z.edge[k], stride=z.rows[k]), :]
            else:
                bottom[to_bottom, :] = jnp.zeros((z.edge[k], 128), F32)
                top[to_top, :] = jnp.zeros((z.edge[k], 128), F32)


def inside(z, depth, above):
    at = lax.axis_index("row")
    large = lax.broadcasted_iota(jnp.int32, (z.rims, 1), 0) < z.rim[0]
    parts = []
    for n in range(depth):
        if above:
            ok = [jnp.where(at * rows >= depth - n, 1.0, 0.0) for rows in z.rows]
        else:
            ok = [jnp.where((at + 1) * rows + n + 1 <= height, 1.0, 0.0) for rows, height in zip(z.rows, HEIGHTS)]
        parts.append(jnp.where(large, ok[1], ok[0]).astype(F32))
    return jnp.concatenate(parts, axis=0)


def clear_guards(z, pads, a):
    for k in (0, 1):
        pads[k][a, 1, pl.ds(0, z.step[k]), :] = jnp.zeros((z.step[k], 128), F32)
        pads[k][a, 0, pl.ds(z.step[k] + z.count[k], z.step[k]), :] = jnp.zeros((z.step[k], 128), F32)


def fill_center(z, pads, value):
    clear_guards(z, pads, 1)
    for k in (0, 1):
        for h in (0, 1):
            pads[k][1, h, pl.ds(z.step[k], z.count[k]), :] = value[z.start[k] : z.start[k] + z.count[k], 128 * h : 128 * h + 128]


def fill_shifted(z, pads, above, below):
    for k in (0, 1):
        ref, step, count, rows = pads[k], z.step[k], z.count[k], z.rows[k]
        rim = slice(z.rim[k], z.rim[k] + z.edge[k])
        for h in (0, 1):
            lanes = slice(128 * h, 128 * h + 128)
            ref[0, h, pl.ds(step, count), :] = ref[1, h, pl.ds(step - 1, count), :]
            ref[2, h, pl.ds(step, count), :] = ref[1, h, pl.ds(step + 1, count), :]
            ref[0, h, pl.ds(step, z.edge[k], stride=rows), :] = above[rim, lanes]
            ref[2, h, pl.ds(step + rows - 1, z.edge[k], stride=rows), :] = below[rim, lanes]


def fill_pads(z, pads, value, above, below):
    fill_center(z, pads, value)
    fill_shifted(z, pads, above, below)
    for a in (0, 2):
        clear_guards(z, pads, a)


def beside(left, right):
    lane = lax.broadcasted_iota(jnp.int32, (1, 128), 1)
    middle = pltpu.roll(jnp.where(lane >= 64, left[1], right[1]), 64, 1)
    return [
        jnp.where(lane >= 96, left[0], jnp.where(lane < 32, right[0], middle)),
        jnp.where(lane >= 96, left[2], jnp.where(lane < 32, right[2], 0.0)),
    ]


def band_operand(z, pads):
    parts = ([], [])
    for k in (1, 0):
        ref, step, count = pads[k], z.step[k], z.count[k]
        low, high = ([ref[a, h, pl.ds(step, count), :] for a in range(TAPS)] for h in (0, 1))
        before = [ref[a, 1, pl.ds(0, count), :] for a in range(TAPS)]
        after = [ref[a, 0, pl.ds(2 * step, count), :] for a in range(TAPS)]
        parts[0].append(jnp.concatenate(low + beside(before, high), axis=1))
        parts[1].append(jnp.concatenate(high + beside(low, after), axis=1))
    return [jnp.concatenate(part, axis=0) for part in parts]


def rim_operand(z, chain, depth):
    m = lax.broadcasted_iota(jnp.int32, (z.rims, 1), 0)
    large = m < z.rim[0]
    has_before = jnp.where(large, m, m - z.rim[0]) >= jnp.where(large, z.images[1], z.images[0])
    has_after = m < jnp.where(large, z.rim[0] - z.images[1], z.rims - z.images[0])
    low, high, before, after = [], [], [], []
    for r in range(depth + 1):
        at = z.guard + r * z.rims
        low.append(chain[0, pl.ds(at, z.rims), :])
        high.append(chain[1, pl.ds(at, z.rims), :])
        shifted = [chain[1, pl.ds(at - images, z.rims), :] for images in z.images]
        before.append(jnp.where(has_before, jnp.where(large, shifted[1], shifted[0]), 0.0))
        shifted = [chain[0, pl.ds(at + images, z.rims), :] for images in z.images]
        after.append(jnp.where(has_after, jnp.where(large, shifted[1], shifted[0]), 0.0))
    parts = ([], [])
    for n in range(depth - 1):
        rows = slice(n, n + TAPS)
        parts[0].append(jnp.concatenate(low[rows] + beside(before[rows], high[rows]), axis=1))
        parts[1].append(jnp.concatenate(high[rows] + beside(low[rows], after[rows]), axis=1))
    return [jnp.concatenate(part, axis=0) for part in parts]


def times(parts, weight):
    left = jnp.concatenate([part[h] for h in (0, 1) for part in parts], axis=0)
    both = jnp.concatenate([weight_matrix(weight.at[0]), weight_matrix(weight.at[1])], axis=1)
    result = dot(jnp.concatenate(split(left), axis=1), jnp.concatenate([both, both], axis=0))
    result = result[:, :128] + result[:, 128:]
    rows = result.shape[0] // 2
    return jnp.concatenate([result[:rows], result[rows:]], axis=1)


def convolve(z, own, above, below, depth, pads, chains, weight):
    r = z.rims
    fill_pads(z, pads, own, above[(depth - 1) * r :], below[:r])
    parts = [band_operand(z, pads)]
    if depth > 1:
        for side, (rim, chain) in enumerate(zip((above, below), chains)):
            rim_at, own_at = (z.guard, z.guard + depth * r) if side == 0 else (z.guard + r, z.guard)
            for h in (0, 1):
                chain[h, pl.ds(rim_at, depth * r), :] = rim[:, 128 * h : 128 * h + 128]
                for k in (0, 1):
                    row = z.step[k] + (0 if side == 0 else z.rows[k] - 1)
                    chain[h, pl.ds(own_at + z.rim[k], z.edge[k]), :] = pads[k][1, h, pl.ds(row, z.edge[k], stride=z.rows[k]), :]
            parts.append(rim_operand(z, chain, depth))
    result = times(parts, weight)
    n = z.total + (depth - 1) * r
    return result[: z.total], result[z.total : n], result[n:]


def image_sums(z, value):
    slot = lax.broadcasted_iota(jnp.int32, (z.slots, 1), 0)
    sums = jnp.zeros((z.slots, 128), F32)
    for k in (0, 1):
        line = value[z.start[k] : z.start[k] + z.step[k]]
        for j in range(1, z.blocks[k]):
            at = z.start[k] + j * z.step[k]
            line = line + value[at : at + z.step[k]]
        image = lax.broadcasted_iota(jnp.int32, (z.step[k], 1), 0) // z.rows[k]
        for i in range(z.images[k]):
            sums = jnp.where(slot == i + k * z.images[0], column_sum(jnp.where(image == i, line, 0.0)), sums)
    return sums


def image_rows(z, values, rims):
    parts = []
    for k in (1, 0):
        image = lax.broadcasted_iota(jnp.int32, (z.step[k], 1), 0) // z.rows[k]
        line = jnp.zeros((z.step[k], 128), F32)
        for i in range(z.images[k]):
            at = i + k * z.images[0]
            line = jnp.where(image == i, values[at : at + 1], line)
        parts += [line] * z.blocks[k]
    if rims:
        m = lax.broadcasted_iota(jnp.int32, (z.rims, 1), 0)
        image = jnp.where(m < z.rim[0], z.images[0] + m % z.images[1], (m - z.rim[0]) % z.images[0])
        line = jnp.zeros((z.rims, 128), F32)
        for at in range(sum(z.images)):
            line = jnp.where(image == at, values[at : at + 1], line)
        parts += [line] * rims
    return jnp.concatenate(parts, axis=0)


def channel_mean():
    a = lax.broadcasted_iota(jnp.int32, (LANES, 128), 0) // C
    b = lax.broadcasted_iota(jnp.int32, (LANES, 128), 1) % 64
    return jnp.where(a == b, 1.0 / C, 0.0).astype(F32)


def to_channels():
    a = lax.broadcasted_iota(jnp.int32, (128, LANES), 0)
    b = lax.broadcasted_iota(jnp.int32, (128, LANES), 1) // C
    return jnp.where(a == b, 1.0, 0.0).astype(F32)


def attention(value):
    return spread(value * value, channel_mean())


def pieces(source, target):
    return [(source.at[n], target.at[n]) for n in range(source.shape[0])]


def copies_of(pairs, sems, first=0):
    return [pltpu.make_async_copy(a, b, sems.at[first + n]) for n, (a, b) in enumerate(pairs)]


def start_all(copies):
    for copy in copies:
        copy.start()


def wait_all(copies):
    for copy in copies:
        copy.wait()


def start_kernel(z, small, large, up_s, up_l, t_s, t_l, x, bottom, top, copies, raw, half, kept, sems):
    images = [(small, raw[0])] + pieces(large, raw[1])
    rest = [(up_s, raw[2])] + pieces(up_l, raw[3]) + [(t_s, raw[4]), (t_l, raw[5])]
    loads = copies_of(images + rest, sems)
    start_all(loads)
    r, n = z.rims, REACH * z.rims
    tail = n + 2 * r
    for ref in (bottom, top):
        ref[pl.ds(tail, z.slots), :] = jnp.zeros((z.slots, LANES), F32)
    wait_all(loads[: len(images)])
    to_matrix(z, raw[:2], half)
    value = whole(half)
    moments(z, value, kept)
    send = pltpu.make_async_copy(kept, copies, sems.at[len(loads)])
    send.start()
    x[...] = value
    for h in (0, 1):
        lanes = pl.ds(128 * h, 128)
        take_rims(z, half.at[h], REACH, bottom.at[pl.ds(0, n), lanes], top.at[pl.ds(0, n), lanes])
    wait_all(loads[len(images) :])
    for k in (0, 1):
        width, rows = HEIGHTS[k], z.rows[k]
        for i in range(z.images[k]):
            slot = pl.ds(tail + i + k * z.images[0], 1)
            for d in (0, 1):
                to_bottom, to_top = n + (1 - d) * r + z.rim[k] + i, n + d * r + z.rim[k] + i
                for j in range(z.blocks[k]):
                    lanes, at = pl.ds(LANES * j, LANES), j * z.images[k]
                    if d < rows:
                        bottom[pl.ds(to_bottom + at, 1), :] = raw[2 + k][i, pl.ds(rows - 1 - d, 1), lanes]
                        top[pl.ds(to_top + at, 1), :] = raw[2 + k][i, pl.ds(d, 1), lanes]
                    else:
                        bottom[pl.ds(to_bottom + at, 1), :] = jnp.zeros((1, LANES), F32)
                        top[pl.ds(to_top + at, 1), :] = jnp.zeros((1, LANES), F32)
                if d < rows:
                    bottom[slot, pl.ds(128 * (1 - d), width)] = raw[4 + k][i, pl.ds(rows - 1 - d, 1), :]
                    top[slot, pl.ds(128 * d, width)] = raw[4 + k][i, pl.ds(d, 1), :]
    send.wait()


def banded(taps, ref):
    row = lax.broadcasted_iota(jnp.int32, (128, 128), 0) // C
    lane = group_of(128)
    for a in range(TAPS):
        main = jnp.zeros((128, 128), F32)
        for b in range(TAPS):
            main = jnp.where(row - lane + 1 == b, taps[a][b], main)
        before = jnp.where(lane[:C] == 0, taps[a][0][:C], 0.0)
        after = jnp.where(lane[:C] == 3, taps[a][2][:C], 0.0)
        for n, part in enumerate(split(jnp.concatenate([main, before, after], axis=0))):
            ref[n, pl.ds(a * TAP_ROWS, TAP_ROWS), :] = part


def weight_matrix(ref):
    main = [ref[pl.ds(a * TAP_ROWS, 128), :] for a in range(TAPS)]
    before, after = ([ref[pl.ds(a * TAP_ROWS + 128 + n * C, C), :] for a in range(TAPS)] for n in (0, 1))
    return jnp.concatenate(
        main + [after[0], before[1], after[1], before[0], after[2], jnp.zeros((2 * C, 128), BF16), before[2]], axis=0
    )


def prepare_kernel(z, first, second, up_s, up_l, t_s, t_l, g1, b1, g2, b2, x, w1, w2, weights, affine, upstream, teacher, x_copy, raw, kept, kept_u, rows, half, sems):
    targets = tuple(raw) + tuple(rows.at[pl.ds(n, 1), :] for n in range(4))
    refs = (first, second, up_s, up_l, t_s, t_l, g1, b1, g2, b2)
    loads = [pltpu.make_async_copy(a, b, sems.at[n]) for n, (a, b) in enumerate(zip(refs, targets))]
    start_all(loads)
    stores = [pltpu.make_async_copy(x, x_copy, sems.at[13])]
    stores[0].start()
    wait_all(loads)
    to_matrix(z, raw[2:4], half)
    kept_u[...] = whole(half)
    stores.append(pltpu.make_async_copy(kept_u, upstream, sems.at[10]))
    stores[1].start()
    for n, (source, forward) in enumerate(zip(raw[:2], (w1, w2))):
        tiles = []
        for a in range(TAPS):
            line = [jnp.concatenate([source[a, b]] * 4, axis=1) for b in range(TAPS)]
            tiles.append([jnp.concatenate([tap] * 4, axis=0) for tap in line])
        turned = [[tiles[TAPS - 1 - a][TAPS - 1 - b].T for b in range(TAPS)] for a in range(TAPS)]
        banded(tiles, forward)
        banded(turned, kept.at[n])
        stores.append(pltpu.make_async_copy(kept.at[n], weights.at[n], sems.at[11 + n]))
        stores[-1].start()
    taps = sum(raw[0][a, b] for a in range(TAPS) for b in range(TAPS))
    pivot = dot(jnp.broadcast_to(gelu(rows[1:2]), (8, C)), taps)[0:1]
    affine[...] = jnp.concatenate([jnp.concatenate([rows[...], pivot], axis=0)] * BLOCK, axis=1)
    teacher[...] = jnp.zeros(teacher.shape, F32)
    for k, ref in ((0, raw[4]), (1, raw[5])):
        for i in range(z.images[k]):
            line = ref[i]
            for j in range(z.blocks[k]):
                at = z.start[k] + j * z.step[k] + i * z.rows[k]
                for lane in (0, 64):
                    teacher[pl.ds(at, z.rows[k]), pl.ds(lane, BLOCK)] = line[:, j * BLOCK : (j + 1) * BLOCK]
    wait_all(stores)


def normed_by(stats):
    return lambda v: (v - stats[0:1]) * stats[1:2]


def activation(center, scale, gain, bias):
    factor = scale * gain
    offset = bias - center * factor
    return lambda v: gelu(v * factor + offset)


def first_kernel(z, x, above, below, gathered, affine, weight, hidden, h_above, h_below, stats, copies, pads, chains, kept, sems):
    n = REACH * z.rims
    center, scale = merged(z, gathered)
    act = activation(center, scale, affine[0:1], affine[1:2])
    own = act(x[...])
    up, down = act(above[pl.ds(0, n), :]) * inside(z, 4, True), act(below[pl.ds(0, n), :]) * inside(z, 4, False)
    own, up, down = convolve(z, own, up, down, 4, pads, chains, weight)
    moments(z, own, kept)
    send = pltpu.make_async_copy(kept, copies, sems.at[0])
    send.start()
    hidden[...] = own
    h_above[...] = up
    h_below[...] = down
    stats[0:1] = center
    stats[1:2] = scale
    send.wait()


def second_kernel(z, hidden, h_above, h_below, gathered, affine, weight, x, x_above, x_below, teacher, out, o_above, o_below, near, stats, copies, pads, chains, kept, sems):
    center, scale = merged(z, gathered)
    act = activation(center, scale, affine[2:3], affine[3:4])
    r = z.rims
    own = act(hidden[...])
    up, down = act(h_above[...]) * inside(z, 3, True), act(h_below[...]) * inside(z, 3, False)
    own, up, down = convolve(z, own, up, down, 3, pads, chains, weight)
    own = x[...] + own
    amap = attention(own)
    lane = lax.broadcasted_iota(jnp.int32, (1, 128), 1)
    sums = image_sums(z, amap * jnp.where(lane < 64, amap, teacher[...]))
    kept[...] = jnp.concatenate([sums] * z.peers, axis=0)
    send = pltpu.make_async_copy(kept, copies, sems.at[0])
    send.start()
    out[...] = own
    o_above[...] = x_above[pl.ds(2 * r, 2 * r), :] + up
    o_below[...] = x_below[pl.ds(0, 2 * r), :] + down
    near[0] = h_above[pl.ds(2 * r, r), :]
    near[1] = h_below[pl.ds(0, r), :]
    stats[0:1] = center
    stats[1:2] = scale
    send.wait()


def tap_rows(q):
    return 128 + C if q < 0 else q * C


def tap_product(z, operand, own, above, below, pads):
    fill_center(z, pads, own)
    fill_shifted(z, pads, above, below)
    columns = []
    for a in range(TAPS):
        columns.append(
            jnp.concatenate([pads[k][TAPS - 1 - a, h, pl.ds(z.step[k], z.count[k]), :] for h in (0, 1) for k in (1, 0)], axis=0)
        )
    used = [jnp.concatenate([operand[n, pl.ds(0, 128 + C), :], operand[n, pl.ds(256 - C, C), :]], axis=0) for n in (0, 1)]
    return product(used, split(jnp.concatenate(columns, axis=1)))


def tap_sums(result, tiles, first_group):
    group = group_of()
    for a in range(TAPS):
        for b in range(TAPS):
            total = None
            for p in range(4):
                at = tap_rows(p + b - 1)
                part = result[at : at + C, 128 * a : 128 * a + 128]
                total = part if total is None else jnp.where(group == p, part, total)
            tile, slot = divmod(first_group + a * TAPS + b, 4)
            tiles[tile] = jnp.where(group == slot, spread_groups(total), tiles[tile])


def tap_counts(z, turned, tiles, first_group):
    group = group_of()
    m = lax.broadcasted_iota(jnp.int32, (1, 2 * z.total), 1) % z.total
    row = jnp.where(m < z.start[0], m % z.rows[1], (m - z.start[0]) % z.rows[0])
    height = jnp.where(m < z.start[0], z.rows[1], z.rows[0])
    at = lax.axis_index("row")
    lost = {
        0: (row == height - 1) & (at == z.peers - 1),
        2: (row == 0) & (at == 0),
    }
    for a in range(TAPS):
        column = jnp.sum(jnp.where(lost[a], 0.0, turned) if a in lost else turned, axis=1, keepdims=True)
        used = jnp.concatenate([column[: 128 + C], column[256 - C :]], axis=0)
        for b in range(TAPS):
            total = sum(used[tap_rows(p + b - 1) : tap_rows(p + b - 1) + C] for p in range(4))
            tile, slot = divmod(first_group + a * TAPS + b, 4)
            tiles[tile] = jnp.where(group == slot, total, tiles[tile])


def turned_operand(z, value, pads, kept):
    fill_center(z, pads, value)
    lane = lax.broadcasted_iota(jnp.int32, (1, 128), 1)
    halves = ([], [])
    for k in (1, 0):
        ref, step, count = pads[k], z.step[k], z.count[k]
        low, high = ref[1, 0, pl.ds(step, count), :], ref[1, 1, pl.ds(step, count), :]
        before, after = ref[1, 1, pl.ds(0, count), :], ref[1, 0, pl.ds(2 * step, count), :]
        for part, main, left, right in ((halves[0], low, before, high), (halves[1], high, low, after)):
            part.append(jnp.concatenate([main, jnp.where(lane >= 96, left, jnp.where(lane < 32, right, 0.0))], axis=1))
    turned = jnp.concatenate(halves[0] + halves[1], axis=0).T
    parts = split(turned)
    for n in (0, 1):
        kept[n] = parts[n]
    return turned


def first_operand_kernel(z, x, hidden, h_above, h_below, above, below, stats, affine, teacher, upstream, weights, left, packed, teachers, spread_u, near_u, pads, chains, kept, kept_w, kept_u, pixels, kept_t, kept_c, kept_packed, sems):
    r, own = z.rims, pl.ds(0, z.total)
    loads = [pltpu.make_async_copy(upstream, kept_u.at[own, :], sems.at[0]), pltpu.make_async_copy(weights.at[1], kept_w, sems.at[1])]
    start_all(loads)
    act = activation(stats[0:1], stats[1:2], affine[0:1], affine[1:2])
    value = turned_operand(z, act(x[...]), pads, kept)
    stores = [pltpu.make_async_copy(kept, left, sems.at[2])]
    stores[0].start()
    tiles = [jnp.zeros((C, 128), F32) for _ in range(BACK_LANES // 128)]
    tap_counts(z, value, tiles, ONES)
    pivot = affine[4:5]
    result = tap_product(
        z, kept, hidden[...] - pivot, (h_above[pl.ds(2 * r, r), :] - pivot) * inside(z, 1, True),
        (h_below[pl.ds(0, r), :] - pivot) * inside(z, 1, False), pads,
    )
    tap_sums(result, tiles, HIDDEN)
    kept_packed[...] = jnp.concatenate(tiles, axis=1)
    stores.append(pltpu.make_async_copy(kept_packed, packed, sems.at[6]))
    stores[1].start()
    pixels[own, :] = teacher[...]
    pixels[pl.ds(z.total, 4 * r), :] = jnp.zeros((4 * r, 128), F32)
    n = (REACH + 2) * r
    for side, ref in enumerate((above, below)):
        for d in (0, 1):
            for k in (0, 1):
                line = ref[pl.ds(n + k * z.images[0], z.images[k]), pl.ds(128 * d, 128)]
                for j in range(z.blocks[k]):
                    at = z.total + (2 * side + d) * r + z.rim[k] + j * z.images[k]
                    pixels[pl.ds(at, z.images[k]), pl.ds(0, BLOCK)] = line[:, j * BLOCK : (j + 1) * BLOCK]
    kept_t[...] = spread(pixels[...], to_channels())
    stores.append(pltpu.make_async_copy(kept_t, teachers, sems.at[3]))
    stores[2].start()
    n = REACH * r
    up, down = above[pl.ds(n, 2 * r), :] * inside(z, 2, True), below[pl.ds(n, 2 * r), :] * inside(z, 2, False)
    kept_u[pl.ds(z.total, r), :] = up[r:]
    kept_u[pl.ds(z.total + r, r), :] = down[:r]
    wait_all(loads)
    stores.append(pltpu.make_async_copy(kept_u, near_u, sems.at[5]))
    stores[3].start()
    kept_c[...] = jnp.concatenate(convolve(z, kept_u[own, :], up, down, 2, pads, chains, kept_w), axis=0)
    stores.append(pltpu.make_async_copy(kept_c, spread_u, sems.at[4]))
    stores[4].start()
    wait_all(stores)


def second_operand_kernel(z, hidden, near, stats, affine, out, o_above, o_below, teachers, spread_u, near_u, weights, out_copy, hidden_copy, left, shifts, by_map, by_teacher, up, pads, chains, kept_t, kept_u, kept_w, kept_s, sems):
    r, total = z.rims, z.total
    loads = [
        pltpu.make_async_copy(teachers, kept_t, sems.at[0]),
        pltpu.make_async_copy(weights.at[1], kept_w, sems.at[1]),
        pltpu.make_async_copy(spread_u, kept_u, sems.at[2]),
    ]
    start_all(loads)
    stores = [
        pltpu.make_async_copy(out, out_copy, sems.at[4]),
        pltpu.make_async_copy(hidden, hidden_copy.at[pl.ds(0, total), :], sems.at[7]),
        pltpu.make_async_copy(near.at[0], hidden_copy.at[pl.ds(total, r), :], sems.at[8]),
        pltpu.make_async_copy(near.at[1], hidden_copy.at[pl.ds(total + r, r), :], sems.at[9]),
        pltpu.make_async_copy(near_u, up, sems.at[10]),
    ]
    start_all(stores)
    normed = normed_by(stats)(jnp.concatenate([hidden[...], near[0], near[1]], axis=0))
    shifted = normed * affine[2:3] + affine[3:4]
    turned_operand(z, gelu(shifted[:total]), pads, left)
    ones = jnp.ones((total, 1), F32)
    masks = jnp.concatenate([ones, inside(z, 1, True), inside(z, 1, False)], axis=0)
    slopes = gelu_slope(shifted) * masks
    o = jnp.concatenate([out[...], o_above[...] * inside(z, 2, True), o_below[...] * inside(z, 2, False)], axis=0)
    for_map = spread(attention(o), to_channels()) * o
    wait_all(loads)
    for_teacher = kept_t[...] * o
    kept_s[0] = kept_u[...] * slopes
    stores += copies_of(pieces(kept_s, shifts), sems, 11)
    stores[-3].start()
    for n, value, ref in ((1, for_map, by_map), (2, for_teacher, by_teacher)):
        own, before, after = value[:total], value[total : total + 2 * r], value[total + 2 * r :]
        ref[...] = jnp.concatenate([own, before[r:], after[:r]], axis=0)
        kept_s[n] = jnp.concatenate(convolve(z, own, before, after, 2, pads, chains, kept_w), axis=0) * slopes
        stores[n - 3].start()
    wait_all(stores)


def upstream_kernel(z, gathered, up, shifts, left_1, left_2, packed, by_map, by_teacher, hidden, stats, dout, dshift, d_above, d_below, slabs, kept_s, kept_left, kept_h, kept_packed, pads, more_pads, sems):
    r, total = z.rims, z.total
    loads = copies_of(
        pieces(shifts, kept_s) + pieces(left_1, kept_left) + [(hidden.at[pl.ds(0, total), :], kept_h), (packed, kept_packed)], sems
    )
    start_all(loads)
    lane = lax.broadcasted_iota(jnp.int32, (z.slots, 128), 1)
    sums = sum(gathered[pl.ds(n * z.slots, z.slots), :] for n in range(z.peers))
    square = jnp.sum(jnp.where(lane < 64, sums, 0.0), axis=1, keepdims=True)
    cross = jnp.sum(jnp.where(lane < 64, 0.0, sums), axis=1, keepdims=True)
    inverse = lax.rsqrt(square + map_eps)
    inner = beta_weight * (square * inverse - cross) * inverse
    shape = (z.slots, 128)
    for_map = (beta_weight - inner) * inverse * inverse * (2.0 / C)
    for_teacher = beta_weight * inverse * (2.0 / C)
    for_map, for_teacher = (wide(image_rows(z, jnp.broadcast_to(v, shape), 2)) for v in (for_map, for_teacher))
    value = up[...] + for_map * by_map[...] - for_teacher * by_teacher[...]
    dout[...] = value[:total]
    wait_all(loads[:3])
    shift = kept_s[0] + for_map * kept_s[1] - for_teacher * kept_s[2]
    pre, above, below = shift[:total], shift[total : total + r], shift[total + r :]
    dshift[...] = pre
    d_above[...] = above
    d_below[...] = below
    second = tap_product(z, left_2, value[:total], value[total : total + r], value[total + r :], pads)
    wait_all(loads[3:5])
    first = tap_product(z, kept_left, pre, above, below, more_pads)
    wait_all(loads[5:])
    normed = normed_by(stats)(kept_h[...])
    tiles = [kept_packed[:, 128 * n : 128 * n + 128] for n in range(BACK_LANES // 128)]
    group = group_of()
    tiles[0] = jnp.where(group == BIAS, fold(column_sum(pre)), jnp.where(group == GAIN, fold(column_sum(pre * normed)), tiles[0]))
    tap_sums(second, tiles, SECOND)
    tap_sums(first, tiles, LEFT)
    line = jnp.concatenate(tiles, axis=1)
    for d in range(z.devices):
        slabs[d] = line[d % C : d % C + 1]


def write_kernel(z, out, x, hidden, weights, first_stats, stats, order, out_s, out_l, first_normed, normed, weight, kept, kept_x, kept_h, half, sems):
    loads = [pltpu.make_async_copy(a, b, sems.at[n]) for n, (a, b) in enumerate(((out, kept), (x, kept_x), (hidden, kept_h), (weights.at[0], weight)))]
    start_all(loads)
    loads[0].wait()
    put_halves(half, kept[...])
    from_matrix(z, half, (out_s, out_l))
    loads[1].wait()
    first_normed[...] = normed_by(first_stats)(kept_x[...])
    loads[2].wait()
    normed[...] = normed_by(stats)(kept_h[...])
    loads[3].wait()


def norm_sums(total):
    group = group_of()
    return [wide(spread_groups(jnp.where(group == n, total[:, :128], 0.0))) for n in (BIAS, GAIN)]


def hidden_kernel(z, gathered, dshift, d_above, d_below, second_normed, stats, affine, weight, first_normed, pre_ref, gain_out, bias_out, slabs, pads):
    total = jnp.sum(gathered[...], axis=0)
    bias_sum, gain_sum = norm_sums(total)
    bias_out[...] = bias_sum[:, :C]
    gain_out[...] = gain_sum[:, :C]
    bias_mean, gain_mean = bias_sum / z.pixels, gain_sum / z.pixels
    factor = affine[2:3] * stats[1:2]
    r, total_rows = z.rims, z.total

    def back(d, normed):
        return factor * (d - bias_mean - normed * gain_mean)

    own = back(dshift[...], second_normed[pl.ds(0, total_rows), :])
    up = back(d_above[...], second_normed[pl.ds(total_rows, r), :]) * inside(z, 1, True)
    down = back(d_below[...], second_normed[pl.ds(total_rows + r, r), :]) * inside(z, 1, False)
    grad, _, _ = convolve(z, own, up, down, 1, pads, None, weight)
    normed = first_normed[...]
    pre = grad * gelu_slope(normed * affine[0:1] + affine[1:2])
    pre_ref[...] = pre
    lane = lax.broadcasted_iota(jnp.int32, (1, 128), 1)
    taps = TAPS * TAPS * C

    def along(row):
        return jnp.concatenate([row[:, :128]] * 3, axis=1)[:, :taps]

    second, left, against, ones = (total[:, n * C : n * C + taps] for n in (SECOND, LEFT, HIDDEN, ONES))
    against = along(stats[1:2]) * (against - along(stats[0:1] - affine[4:5]) * ones)
    first = along(factor) * (left - along(bias_mean) * ones - along(gain_mean) * against)
    sums = jnp.where(lane < C, fold(column_sum(pre)), fold(column_sum(pre * normed)))
    line = jnp.concatenate([sums[:, : 2 * C], second, first], axis=1)
    slabs[...] = jnp.broadcast_to(line[None], slabs.shape)


def back_kernel(z, gathered, pre, normed, stats, affine, dout, back_s, back_l, one, two, gain_out, bias_out, half, lines, kept, sems):
    kept_s, kept_l, kept_1, kept_2 = kept
    for d in range(C):
        lines[pl.ds(d, 1), :] = gathered[d]
    for ref, group in ((kept_2, LAST_SECOND), (kept_1, LAST_FIRST)):
        for a in range(TAPS):
            for b in range(TAPS):
                at = (group + a * TAPS + b) * C
                ref[a, b] = lines[:, pl.ds(at, C)]
    stores = copies_of([(kept_1, one), (kept_2, two), (kept_s, back_s), (kept_l, back_l)], sems)
    start_all(stores[:2])
    bias_sum, gain_sum = norm_sums(jnp.sum(gathered[:, :, pl.ds(0, 128)], axis=0))
    bias_out[...] = bias_sum[:, :C]
    gain_out[...] = gain_sum[:, :C]
    bias_mean, gain_mean = bias_sum / z.pixels, gain_sum / z.pixels
    value = dout[...] + affine[0:1] * stats[1:2] * (pre[...] - bias_mean - normed[...] * gain_mean)
    put_halves(half, value)
    from_matrix(z, half, (kept_s, kept_l))
    start_all(stores[2:])
    wait_all(stores)


def call(body, ins, outs, scratch=(), sems=0):
    space = {"v": pltpu.VMEM, "h": pltpu.HBM, "V": pltpu.VMEM}
    shapes = []
    for item in scratch:
        if isinstance(item, list):
            shapes.append([pltpu.VMEM(*s) for s in item])
        else:
            shapes.append(pltpu.VMEM(*item))
    if sems:
        shapes.append(pltpu.SemaphoreType.DMA((sems,)))
    run = pl.pallas_call(
        body,
        out_shape=[jax.ShapeDtypeStruct(shape, kind) if s == "v" else space[s](shape, kind) for s, shape, kind in outs],
        in_specs=[pl.BlockSpec(memory_space=space[s]) for s in ins],
        out_specs=[pl.BlockSpec(memory_space=space[s]) for s, _, _ in outs],
        scratch_shapes=shapes,
        compiler_params=pltpu.CompilerParams(vmem_limit_bytes=VMEM_LIMIT),
    )
    return lambda *args: run(
        *(pltpu.with_memory_space_constraint(arg, pltpu.HBM) if s == "h" else arg for s, arg in zip(ins, args))
    )


def exchange(lines, axes):
    shape = lines.shape
    if len(shape) == 2:
        lines = lines.reshape(math.prod(lax.axis_size(axis) for axis in axes), -1, 128)
    return lax.all_to_all(lines, axes, 0, 0, tiled=True).reshape(shape)


def beyond(z, bottom, top, depths):
    hops = max(-(-depth // rows) for rows in z.rows for depth in depths)
    above, below = [], []
    for hop in range(1, hops + 1):
        above.append(lax.ppermute(bottom, "row", [(i, i + hop) for i in range(z.peers - hop)]))
        below.append(lax.ppermute(top, "row", [(i + hop, i) for i in range(z.peers - hop)]))
    if hops == 1:
        return above[0], below[0]
    up, down = [], []
    base = 0
    for depth in depths:
        for n in range(depth):
            for k in (1, 0):
                hop, back = divmod(depth - 1 - n, z.rows[k])
                at = base + (depth - 1 - back) * z.rims + z.rim[k]
                up.append(above[hop][at : at + z.edge[k]])
                hop, back = divmod(n, z.rows[k])
                at = base + back * z.rims + z.rim[k]
                down.append(below[hop][at : at + z.edge[k]])
        base += depth * z.rims
    up.append(jnp.concatenate([pixel_rows(z, above, base, 1, 1), pixel_rows(z, above, base, 0, 1)], axis=1))
    down.append(jnp.concatenate([pixel_rows(z, below, base, 0, 0), pixel_rows(z, below, base, 1, 0)], axis=1))
    return jnp.concatenate(up, axis=0), jnp.concatenate(down, axis=0)


def pixel_rows(z, bands, base, distance, last):
    lines = []
    for k in (0, 1):
        hop, back = divmod(distance, z.rows[k])
        at = base + k * z.images[0]
        half = 128 * abs(last - back)
        lines.append(bands[hop][at : at + z.images[k], half : half + 128])
    lines.append(jnp.zeros((z.slots - sum(z.images), 128), F32))
    return jnp.concatenate(lines, axis=0)


def local(
    image_small, image_large, teacher_small, teacher_large, upstream_small, upstream_large,
    conv_first, gain_first, bias_first, conv_second, gain_second, bias_second,
):
    peers = lax.axis_size("row")
    devices = lax.axis_size("img") * peers
    z = Sizes(image_small.shape, image_large.shape, devices, peers)
    body = lambda function: functools.partial(function, z)
    r = z.rims
    full, half, pair = (z.total, LANES), (2, z.total, 128), (2 * devices, 128)
    weight, left = (2, TAPS * TAP_ROWS, 128), (2, 256, 2 * z.total)
    images = [image_small, image_large, upstream_small, upstream_large, teacher_small, teacher_large]
    f = lambda space, *shape: (space, shape, F32)
    depths = (REACH, 2)
    rim_rows = sum(depths) * r + z.slots

    x, bottom, top, copies = call(
        body(start_kernel),
        "hhhhhh",
        [("v", full, F32), f("v", rim_rows, LANES), f("v", rim_rows, LANES), ("h", pair, F32)],
        [[(a.shape, F32) for a in images], (half, F32), (pair, F32)],
        5 + 2 * z.images[1],
    )(*images)
    gathered = exchange(copies, AXES)
    above, below = beyond(z, bottom, top, depths)
    params = [conv_first, conv_second] + images[2:]
    w1, w2, weights, affine, upstream, teacher, x_copy = call(
        body(prepare_kernel),
        "hhhhhhhhhhv",
        [("v", weight, BF16), ("v", weight, BF16), ("h", (2,) + weight, BF16), f("v", 5, LANES), ("h", full, F32), f("v", z.total, 128), ("h", full, F32)],
        [[(a.shape, F32) for a in params], ((2,) + weight, BF16), (full, F32), ((4, C), F32), (half, F32)],
        14,
    )(*params, *(v.reshape(1, C) for v in (gain_first, bias_first, gain_second, bias_second)), x)

    hidden, h_above, h_below, stats_one, copies = call(
        body(first_kernel),
        "vvvvvv",
        [("v", full, F32), f("v", 3 * r, LANES), f("v", 3 * r, LANES), f("v", 2, LANES), ("h", pair, F32)],
        [z.pads(), z.chains(4), (pair, F32)],
        1,
    )(x, above, below, gathered, affine, w1)
    gathered = exchange(copies, AXES)
    extended, near_rows = z.total + 4 * r, z.total + 2 * r
    left_one, packed, teachers, spread_u, near_u = call(
        body(first_operand_kernel),
        "vvvvvvvvvhh",
        [("h", left, BF16), f("h", C, BACK_LANES), f("h", extended, LANES), f("h", near_rows, LANES), f("h", near_rows, LANES)],
        [
            z.pads(), z.chains(2), (left, BF16), (weight, BF16), ((near_rows, LANES), F32), ((extended, 128), F32),
            ((extended, LANES), F32), ((near_rows, LANES), F32), ((C, BACK_LANES), F32),
        ],
        7,
    )(x, hidden, h_above, h_below, above, below, stats_one, affine, teacher, upstream, weights)
    gathered, near_u = lax.optimization_barrier((gathered, near_u))

    map_shape = (peers * z.slots, 128)
    out, o_above, o_below, near, stats_two, copies = call(
        body(second_kernel),
        "vvvvvvvvvv",
        [("v", full, F32), f("v", 2 * r, LANES), f("v", 2 * r, LANES), f("v", 2, r, LANES), f("v", 2, LANES), ("h", map_shape, F32)],
        [z.pads(), z.chains(3), (map_shape, F32)],
        1,
    )(hidden, h_above, h_below, gathered, affine, w2, x, above, below, teacher)
    gathered = exchange(copies, ("row",))
    out_copy, hidden_copy, left_two, shifts, by_map, by_teacher, up = call(
        body(second_operand_kernel),
        "vvvvvvvhhhh",
        [
            ("h", full, F32), f("h", near_rows, LANES), ("v", left, BF16), f("h", 3, near_rows, LANES),
            f("v", near_rows, LANES), f("v", near_rows, LANES), f("v", near_rows, LANES),
        ],
        [
            z.pads(), z.chains(2), ((extended, LANES), F32), ((near_rows, LANES), F32), (weight, BF16),
            ((3, near_rows, LANES), F32),
        ],
        14,
    )(hidden, near, stats_two, affine, out, o_above, o_below, teachers, spread_u, near_u, weights)

    dout, dshift, d_above, d_below, slabs = call(
        body(upstream_kernel),
        "vvhhvhvvhv",
        [("v", full, F32), ("v", full, F32), f("v", r, LANES), f("v", r, LANES), f("V", devices, 1, BACK_LANES)],
        [((3, near_rows, LANES), F32), (left, BF16), (full, F32), ((C, BACK_LANES), F32), z.pads(), z.pads()],
        7,
    )(gathered, up, shifts, left_one, left_two, packed, by_map, by_teacher, hidden_copy, stats_two)
    gathered = exchange(slabs, AXES)
    out_s, out_l, first_normed, second_normed, weight_back = call(
        body(write_kernel),
        "hhhhvvv",
        [("v", image_small.shape, F32), ("v", image_large.shape, F32), ("v", full, F32), f("v", near_rows, LANES), ("v", weight, BF16)],
        [(full, F32), (full, F32), ((near_rows, LANES), F32), (half, F32)],
        4,
    )(out_copy, x_copy, hidden_copy, weights, stats_one, stats_two, d_above)

    pre, gain_two, bias_two, slabs = call(
        body(hidden_kernel),
        "vvvvvvvvv",
        [("v", full, F32), f("v", 1, C), f("v", 1, C), f("V", devices, 1, LAST_LANES)],
        [z.pads()],
    )(gathered, dshift, d_above, d_below, second_normed, stats_two, affine, weight_back, first_normed)
    gathered = exchange(slabs, AXES)

    back_s, back_l, one, two, gain_one, bias_one = call(
        body(back_kernel),
        "vvvvvv",
        [("h", a.shape, F32) for a in (image_small, image_large, conv_first, conv_second)] + [f("v", 1, C), f("v", 1, C)],
        [(half, F32), ((C, LAST_LANES), F32), [(a.shape, F32) for a in (image_small, image_large, conv_first, conv_second)]],
        4,
    )(gathered, pre, first_normed, stats_one, affine, dout)
    return (
        out_s, out_l, back_s, back_l,
        one, gain_one.reshape(C), bias_one.reshape(C),
        two, gain_two.reshape(C), bias_two.reshape(C),
    )


def solution(mesh):
    split_bands, everywhere = P("img", "row", None), P()
    return jax.shard_map(
        local,
        mesh=mesh,
        in_specs=(split_bands,) * 6 + (everywhere,) * 6,
        out_specs=(split_bands,) * 4 + (everywhere,) * 6,
        check_vma=False,
    )
```

```python
import functools
import math

import jax
import jax.numpy as jnp
from jax import lax
from jax.experimental import pallas as pl
from jax.experimental.pallas import tpu as pltpu
from jax.sharding import PartitionSpec as P

C = 32
HS = 32
HL = 64
HEIGHTS = (HS, HL)

norm_eps = 1e-05
map_eps = 1e-06
beta_weight = 1000.0
AXES = ("img", "row")
BLOCK = 8
LANES = BLOCK * C
TAPS = 3
DEPTH = TAPS * 128 + 256
TAP_ROWS = 128 + 2 * C
REACH = 4
ROOT = math.sqrt(2.0 / math.pi)
CUBE = 0.044715
F32 = jnp.float32
BF16 = jnp.bfloat16
VMEM_LIMIT = 32 * 1024 * 1024
BIAS, GAIN, SECOND, LEFT, HIDDEN, ONES = 0, 1, 2, 11, 20, 29
BACK_LANES = 1280
LAST_SECOND, LAST_FIRST, LAST_LANES = 2, 11, 640


class Sizes:
    def __init__(self, small, large, devices, peers):
        self.images = (small[0], large[0])
        self.rows = (small[1], large[1])
        self.blocks = (HS // BLOCK, HL // BLOCK)
        self.step = tuple(n * r for n, r in zip(self.images, self.rows))
        self.count = tuple(b * s for b, s in zip(self.blocks, self.step))
        self.edge = tuple(b * n for b, n in zip(self.blocks, self.images))
        self.start = (self.count[1], 0)
        self.rim = (self.edge[1], 0)
        self.total = sum(self.count)
        self.rims = sum(self.edge)
        self.slots = -(-sum(self.images) // 8) * 8
        self.guard = -(-max(self.images) // 8) * 8
        self.devices = devices
        self.peers = peers
        self.here = float(self.total * BLOCK)
        self.pixels = self.here * devices

    def pads(self):
        return [((TAPS, 2, self.count[k] + 2 * self.step[k], 128), F32) for k in (0, 1)]

    def chains(self, depth):
        return [((2, 2 * self.guard + (depth + 1) * self.rims, 128), F32)] * 2


def split(value):
    high = value.astype(BF16)
    return high, (value - high.astype(F32)).astype(BF16)


def dot(left, right):
    return lax.dot_general(left, right, (((1,), (0,)), ((), ())), preferred_element_type=F32)


def product(left, right):
    if left[0].shape[1] % 128:
        return dot(left[0], right[0]) + (dot(left[0], right[1]) + dot(left[1], right[0]))
    return dot(
        jnp.concatenate([left[0], left[0], left[1]], axis=1), jnp.concatenate([right[0], right[1], right[0]], axis=0)
    )


def spread(left, right):
    right = right.astype(BF16)
    return dot(jnp.concatenate(split(left), axis=1), jnp.concatenate([right, right], axis=0))


def gelu(s):
    return 0.5 * s * (1.0 + jnp.tanh(ROOT * (s + CUBE * s * s * s)))


def gelu_slope(s):
    square = s * s
    t = jnp.tanh(ROOT * s * (1.0 + CUBE * square))
    return 0.5 * (1.0 + t) + 0.5 * s * (1.0 - t * t) * ROOT * (1.0 + 3.0 * CUBE * square)


def spread_groups(row):
    row = row + pltpu.roll(row, 64, 1)
    return row + pltpu.roll(row, 32, 1)


def fold(row):
    return spread_groups(row[:, :128] + row[:, 128:])


def wide(row):
    return jnp.concatenate([row, row], axis=1)


def group_of(rows=1, lanes=128):
    return lax.broadcasted_iota(jnp.int32, (rows, lanes), 1) // C


def column_sum(value):
    return jnp.sum(value, axis=0, keepdims=True)


def send_lines(z, ref, lines):
    for n, line in enumerate(lines):
        ref[pl.ds(n, z.devices, stride=len(lines)), :] = jnp.broadcast_to(line, (z.devices, 128))


def moments(z, value, ref):
    few = min(8, z.total)
    pivot = fold(column_sum(value[:few])) / float(few * BLOCK)
    off = value - wide(pivot)
    first, second = fold(column_sum(off)), fold(column_sum(off * off))
    send_lines(z, ref, [pivot + first / z.here, second - first * first / z.here])


def merged(z, ref):
    means = ref[pl.ds(0, z.devices, stride=2), :]
    center = jnp.mean(means, axis=0, keepdims=True)
    off = means - center
    within = jnp.mean(ref[pl.ds(1, z.devices, stride=2), :], axis=0, keepdims=True)
    variance = within / z.here + jnp.mean(off * off, axis=0, keepdims=True)
    return wide(center), wide(lax.rsqrt(variance + norm_eps))


def put_halves(ref, value):
    ref[0] = value[:, :128]
    ref[1] = value[:, 128:]


def whole(ref):
    return jnp.concatenate([ref[0], ref[1]], axis=1)


def to_matrix(z, refs, half):
    for k in (0, 1):
        for j in range(z.blocks[k]):
            at = z.start[k] + j * z.step[k]
            for i in range(z.images[k]):
                for h in (0, 1):
                    half[h, pl.ds(at + i * z.rows[k], z.rows[k]), :] = refs[k][i, :, pl.ds(LANES * j + 128 * h, 128)]


def from_matrix(z, half, refs):
    for k in (0, 1):
        for j in range(z.blocks[k]):
            at = z.start[k] + j * z.step[k]
            for i in range(z.images[k]):
                for h in (0, 1):
                    refs[k][i, :, pl.ds(LANES * j + 128 * h, 128)] = half[h, pl.ds(at + i * z.rows[k], z.rows[k]), :]


def is_even():
    return lax.axis_index("row") % 2 == 0


def put_edges(pair, other, at, last, first):
    even = is_even()
    pair[at] = jnp.where(even, last, first)
    other[at] = jnp.where(even, first, last)


def above_of(pair, other, at):
    return jnp.where(is_even(), other[at], pair[at])


def below_of(pair, other, at):
    return jnp.where(is_even(), pair[at], other[at])


def take_rims(z, half, depth, pair, other):
    everything = pl.ds(0, 128)
    for k in (0, 1):
        nothing = jnp.zeros((z.edge[k], 128), F32)
        for n in range(depth):
            first, last = nothing, nothing
            if depth - n <= z.rows[k]:
                last = half[pl.ds(z.start[k] + z.rows[k] - depth + n, z.edge[k], stride=z.rows[k]), :]
            if n < z.rows[k]:
                first = half[pl.ds(z.start[k] + n, z.edge[k], stride=z.rows[k]), :]
            put_edges(pair, other, (pl.ds(n * z.rims + z.rim[k], z.edge[k]), everything), last, first)


def inside(z, depth, above):
    at = lax.axis_index("row")
    large = lax.broadcasted_iota(jnp.int32, (z.rims, 1), 0) < z.rim[0]
    parts = []
    for n in range(depth):
        if above:
            ok = [jnp.where(at * rows >= depth - n, 1.0, 0.0) for rows in z.rows]
        else:
            ok = [jnp.where((at + 1) * rows + n + 1 <= height, 1.0, 0.0) for rows, height in zip(z.rows, HEIGHTS)]
        parts.append(jnp.where(large, ok[1], ok[0]).astype(F32))
    return jnp.concatenate(parts, axis=0)


def clear_guards(z, pads, a):
    for k in (0, 1):
        pads[k][a, 1, pl.ds(0, z.step[k]), :] = jnp.zeros((z.step[k], 128), F32)
        pads[k][a, 0, pl.ds(z.step[k] + z.count[k], z.step[k]), :] = jnp.zeros((z.step[k], 128), F32)


def fill_center(z, pads, value):
    clear_guards(z, pads, 1)
    for k in (0, 1):
        for h in (0, 1):
            pads[k][1, h, pl.ds(z.step[k], z.count[k]), :] = value[z.start[k] : z.start[k] + z.count[k], 128 * h : 128 * h + 128]


def fill_shifted(z, pads, above, below):
    for k in (0, 1):
        ref, step, count, rows = pads[k], z.step[k], z.count[k], z.rows[k]
        rim = slice(z.rim[k], z.rim[k] + z.edge[k])
        for h in (0, 1):
            lanes = slice(128 * h, 128 * h + 128)
            ref[0, h, pl.ds(step, count), :] = ref[1, h, pl.ds(step - 1, count), :]
            ref[2, h, pl.ds(step, count), :] = ref[1, h, pl.ds(step + 1, count), :]
            ref[0, h, pl.ds(step, z.edge[k], stride=rows), :] = above[rim, lanes]
            ref[2, h, pl.ds(step + rows - 1, z.edge[k], stride=rows), :] = below[rim, lanes]


def fill_pads(z, pads, value, above, below):
    fill_center(z, pads, value)
    fill_shifted(z, pads, above, below)
    for a in (0, 2):
        clear_guards(z, pads, a)


def beside(left, right):
    lane = lax.broadcasted_iota(jnp.int32, (1, 128), 1)
    middle = pltpu.roll(jnp.where(lane >= 64, left[1], right[1]), 64, 1)
    return [
        jnp.where(lane >= 96, left[0], jnp.where(lane < 32, right[0], middle)),
        jnp.where(lane >= 96, left[2], jnp.where(lane < 32, right[2], 0.0)),
    ]


def band_operand(z, pads):
    parts = ([], [])
    for k in (1, 0):
        ref, step, count = pads[k], z.step[k], z.count[k]
        low, high = ([ref[a, h, pl.ds(step, count), :] for a in range(TAPS)] for h in (0, 1))
        before = [ref[a, 1, pl.ds(0, count), :] for a in range(TAPS)]
        after = [ref[a, 0, pl.ds(2 * step, count), :] for a in range(TAPS)]
        parts[0].append(jnp.concatenate(low + beside(before, high), axis=1))
        parts[1].append(jnp.concatenate(high + beside(low, after), axis=1))
    return [jnp.concatenate(part, axis=0) for part in parts]


def rim_operand(z, chain, depth):
    m = lax.broadcasted_iota(jnp.int32, (z.rims, 1), 0)
    large = m < z.rim[0]
    has_before = jnp.where(large, m, m - z.rim[0]) >= jnp.where(large, z.images[1], z.images[0])
    has_after = m < jnp.where(large, z.rim[0] - z.images[1], z.rims - z.images[0])
    low, high, before, after = [], [], [], []
    for r in range(depth + 1):
        at = z.guard + r * z.rims
        low.append(chain[0, pl.ds(at, z.rims), :])
        high.append(chain[1, pl.ds(at, z.rims), :])
        shifted = [chain[1, pl.ds(at - images, z.rims), :] for images in z.images]
        before.append(jnp.where(has_before, jnp.where(large, shifted[1], shifted[0]), 0.0))
        shifted = [chain[0, pl.ds(at + images, z.rims), :] for images in z.images]
        after.append(jnp.where(has_after, jnp.where(large, shifted[1], shifted[0]), 0.0))
    parts = ([], [])
    for n in range(depth - 1):
        rows = slice(n, n + TAPS)
        parts[0].append(jnp.concatenate(low[rows] + beside(before[rows], high[rows]), axis=1))
        parts[1].append(jnp.concatenate(high[rows] + beside(low[rows], after[rows]), axis=1))
    return [jnp.concatenate(part, axis=0) for part in parts]


def times(parts, weight):
    left = jnp.concatenate([part[h] for h in (0, 1) for part in parts], axis=0)
    both = jnp.concatenate([weight_matrix(weight.at[0]), weight_matrix(weight.at[1])], axis=1)
    result = dot(jnp.concatenate(split(left), axis=1), jnp.concatenate([both, both], axis=0))
    result = result[:, :128] + result[:, 128:]
    rows = result.shape[0] // 2
    return jnp.concatenate([result[:rows], result[rows:]], axis=1)


def convolve(z, own, above, below, depth, pads, chains, weight):
    r = z.rims
    fill_pads(z, pads, own, above[(depth - 1) * r :], below[:r])
    parts = [band_operand(z, pads)]
    if depth > 1:
        for side, (rim, chain) in enumerate(zip((above, below), chains)):
            rim_at, own_at = (z.guard, z.guard + depth * r) if side == 0 else (z.guard + r, z.guard)
            for h in (0, 1):
                chain[h, pl.ds(rim_at, depth * r), :] = rim[:, 128 * h : 128 * h + 128]
                for k in (0, 1):
                    row = z.step[k] + (0 if side == 0 else z.rows[k] - 1)
                    chain[h, pl.ds(own_at + z.rim[k], z.edge[k]), :] = pads[k][1, h, pl.ds(row, z.edge[k], stride=z.rows[k]), :]
            parts.append(rim_operand(z, chain, depth))
    result = times(parts, weight)
    n = z.total + (depth - 1) * r
    return result[: z.total], result[z.total : n], result[n:]


def image_sums(z, value):
    slot = lax.broadcasted_iota(jnp.int32, (z.slots, 1), 0)
    sums = jnp.zeros((z.slots, 128), F32)
    for k in (0, 1):
        line = value[z.start[k] : z.start[k] + z.step[k]]
        for j in range(1, z.blocks[k]):
            at = z.start[k] + j * z.step[k]
            line = line + value[at : at + z.step[k]]
        image = lax.broadcasted_iota(jnp.int32, (z.step[k], 1), 0) // z.rows[k]
        for i in range(z.images[k]):
            sums = jnp.where(slot == i + k * z.images[0], column_sum(jnp.where(image == i, line, 0.0)), sums)
    return sums


def image_rows(z, values, rims):
    parts = []
    for k in (1, 0):
        image = lax.broadcasted_iota(jnp.int32, (z.step[k], 1), 0) // z.rows[k]
        line = jnp.zeros((z.step[k], 128), F32)
        for i in range(z.images[k]):
            at = i + k * z.images[0]
            line = jnp.where(image == i, values[at : at + 1], line)
        parts += [line] * z.blocks[k]
    if rims:
        m = lax.broadcasted_iota(jnp.int32, (z.rims, 1), 0)
        image = jnp.where(m < z.rim[0], z.images[0] + m % z.images[1], (m - z.rim[0]) % z.images[0])
        line = jnp.zeros((z.rims, 128), F32)
        for at in range(sum(z.images)):
            line = jnp.where(image == at, values[at : at + 1], line)
        parts += [line] * rims
    return jnp.concatenate(parts, axis=0)


def channel_mean():
    a = lax.broadcasted_iota(jnp.int32, (LANES, 128), 0) // C
    b = lax.broadcasted_iota(jnp.int32, (LANES, 128), 1) % 64
    return jnp.where(a == b, 1.0 / C, 0.0).astype(F32)


def to_channels():
    a = lax.broadcasted_iota(jnp.int32, (128, LANES), 0)
    b = lax.broadcasted_iota(jnp.int32, (128, LANES), 1) // C
    return jnp.where(a == b, 1.0, 0.0).astype(F32)


def attention(value):
    return spread(value * value, channel_mean())


def pieces(source, target):
    return [(source.at[n], target.at[n]) for n in range(source.shape[0])]


def copies_of(pairs, sems, first=0):
    return [pltpu.make_async_copy(a, b, sems.at[first + n]) for n, (a, b) in enumerate(pairs)]


def start_all(copies):
    for copy in copies:
        copy.start()


def wait_all(copies):
    for copy in copies:
        copy.wait()


def start_kernel(z, small, large, up_s, up_l, t_s, t_l, x, pair, other, copies, raw, half, sems):
    images = [(small, raw[0])] + pieces(large, raw[1])
    rest = [(up_s, raw[2])] + pieces(up_l, raw[3]) + [(t_s, raw[4]), (t_l, raw[5])]
    loads = copies_of(images + rest, sems)
    start_all(loads)
    r, n = z.rims, REACH * z.rims
    tail = n + 2 * r
    for ref in (pair, other):
        ref[pl.ds(tail, z.slots), :] = jnp.zeros((z.slots, LANES), F32)
    wait_all(loads[: len(images)])
    to_matrix(z, raw[:2], half)
    value = whole(half)
    x[...] = value
    moments(z, value, copies)
    for h in (0, 1):
        lanes = pl.ds(128 * h, 128)
        take_rims(z, half.at[h], REACH, pair.at[pl.ds(0, n), lanes], other.at[pl.ds(0, n), lanes])
    wait_all(loads[len(images) :])
    for k in (0, 1):
        width, rows = HEIGHTS[k], z.rows[k]
        for i in range(z.images[k]):
            slot = pl.ds(tail + i + k * z.images[0], 1)
            for d in (0, 1):
                has_last, has_first = rows + d >= 2, d < rows
                last, first = pl.ds(max(rows - 2 + d, 0), 1), pl.ds(min(d, rows - 1), 1)
                for j in range(z.blocks[k]):
                    lanes = pl.ds(LANES * j, LANES)
                    at = (pl.ds(n + d * r + z.rim[k] + j * z.images[k] + i, 1), pl.ds(0, LANES))
                    nothing = jnp.zeros((1, LANES), F32)
                    put_edges(
                        pair, other, at,
                        raw[2 + k][i, last, lanes] if has_last else nothing,
                        raw[2 + k][i, first, lanes] if has_first else nothing,
                    )
                nothing = jnp.zeros((1, width), F32)
                put_edges(
                    pair, other, (slot, pl.ds(128 * d, width)),
                    raw[4 + k][i, last, :] if has_last else nothing,
                    raw[4 + k][i, first, :] if has_first else nothing,
                )


def banded(taps, ref):
    row = lax.broadcasted_iota(jnp.int32, (128, 128), 0) // C
    lane = group_of(128)
    for a in range(TAPS):
        main = jnp.zeros((128, 128), F32)
        for b in range(TAPS):
            main = jnp.where(row - lane + 1 == b, taps[a][b], main)
        before = jnp.where(lane[:C] == 0, taps[a][0][:C], 0.0)
        after = jnp.where(lane[:C] == 3, taps[a][2][:C], 0.0)
        for n, part in enumerate(split(jnp.concatenate([main, before, after], axis=0))):
            ref[n, pl.ds(a * TAP_ROWS, TAP_ROWS), :] = part


def weight_matrix(ref):
    main = [ref[pl.ds(a * TAP_ROWS, 128), :] for a in range(TAPS)]
    before, after = ([ref[pl.ds(a * TAP_ROWS + 128 + n * C, C), :] for a in range(TAPS)] for n in (0, 1))
    return jnp.concatenate(
        main + [after[0], before[1], after[1], before[0], after[2], jnp.zeros((2 * C, 128), BF16), before[2]], axis=0
    )


def prepare_kernel(z, first, second, up_s, up_l, t_s, t_l, g1, b1, g2, b2, x, w1, w2, weights, affine, upstream, teacher, x_copy, raw, kept, kept_u, rows, half, sems):
    targets = tuple(raw) + tuple(rows.at[pl.ds(n, 1), :] for n in range(4))
    refs = (first, second, up_s, up_l, t_s, t_l, g1, b1, g2, b2)
    loads = [pltpu.make_async_copy(a, b, sems.at[n]) for n, (a, b) in enumerate(zip(refs, targets))]
    start_all(loads)
    stores = [pltpu.make_async_copy(x, x_copy, sems.at[13])]
    stores[0].start()
    wait_all(loads)
    to_matrix(z, raw[2:4], half)
    kept_u[...] = whole(half)
    stores.append(pltpu.make_async_copy(kept_u, upstream, sems.at[10]))
    stores[1].start()
    for n, (source, forward) in enumerate(zip(raw[:2], (w1, w2))):
        tiles = []
        for a in range(TAPS):
            line = [jnp.concatenate([source[a, b]] * 4, axis=1) for b in range(TAPS)]
            tiles.append([jnp.concatenate([tap] * 4, axis=0) for tap in line])
        turned = [[tiles[TAPS - 1 - a][TAPS - 1 - b].T for b in range(TAPS)] for a in range(TAPS)]
        banded(tiles, forward)
        banded(turned, kept.at[n])
        stores.append(pltpu.make_async_copy(kept.at[n], weights.at[n], sems.at[11 + n]))
        stores[-1].start()
    taps = sum(raw[0][a, b] for a in range(TAPS) for b in range(TAPS))
    pivot = dot(jnp.broadcast_to(gelu(rows[1:2]), (8, C)), taps)[0:1]
    affine[...] = jnp.concatenate([jnp.concatenate([rows[...], pivot], axis=0)] * BLOCK, axis=1)
    teacher[...] = jnp.zeros(teacher.shape, F32)
    for k, ref in ((0, raw[4]), (1, raw[5])):
        for i in range(z.images[k]):
            line = ref[i]
            for j in range(z.blocks[k]):
                at = z.start[k] + j * z.step[k] + i * z.rows[k]
                for lane in (0, 64):
                    teacher[pl.ds(at, z.rows[k]), pl.ds(lane, BLOCK)] = line[:, j * BLOCK : (j + 1) * BLOCK]
    wait_all(stores)


def normed_by(stats):
    return lambda v: (v - stats[0:1]) * stats[1:2]


def activation(center, scale, gain, bias):
    factor = scale * gain
    offset = bias - center * factor
    return lambda v: gelu(v * factor + offset)


def first_kernel(z, x, pair, other, gathered, affine, weight, hidden, h_above, h_below, stats, copies, pads, chains):
    n = REACH * z.rims
    center, scale = merged(z, gathered)
    act = activation(center, scale, affine[0:1], affine[1:2])
    own = act(x[...])
    at = (pl.ds(0, n), pl.ds(0, LANES))
    up, down = act(above_of(pair, other, at)) * inside(z, 4, True), act(below_of(pair, other, at)) * inside(z, 4, False)
    own, up, down = convolve(z, own, up, down, 4, pads, chains, weight)
    moments(z, own, copies)
    hidden[...] = own
    h_above[...] = up
    h_below[...] = down
    stats[0:1] = center
    stats[1:2] = scale


def second_kernel(z, hidden, h_above, h_below, gathered, affine, weight, x, pair, other, teacher, out, o_above, o_below, near, stats, copies, pads, chains):
    center, scale = merged(z, gathered)
    act = activation(center, scale, affine[2:3], affine[3:4])
    r = z.rims
    own = act(hidden[...])
    up, down = act(h_above[...]) * inside(z, 3, True), act(h_below[...]) * inside(z, 3, False)
    own, up, down = convolve(z, own, up, down, 3, pads, chains, weight)
    own = x[...] + own
    amap = attention(own)
    lane = lax.broadcasted_iota(jnp.int32, (1, 128), 1)
    sums = image_sums(z, amap * jnp.where(lane < 64, amap, teacher[...]))
    copies[...] = jnp.concatenate([sums] * z.peers, axis=0)
    out[...] = own
    o_above[...] = above_of(pair, other, (pl.ds(2 * r, 2 * r), pl.ds(0, LANES))) + up
    o_below[...] = below_of(pair, other, (pl.ds(0, 2 * r), pl.ds(0, LANES))) + down
    near[0] = h_above[pl.ds(2 * r, r), :]
    near[1] = h_below[pl.ds(0, r), :]
    stats[0:1] = center
    stats[1:2] = scale


def tap_rows(q):
    return 128 + C if q < 0 else q * C


def tap_product(z, operand, own, above, below, pads):
    fill_center(z, pads, own)
    fill_shifted(z, pads, above, below)
    columns = []
    for a in range(TAPS):
        columns.append(
            jnp.concatenate([pads[k][TAPS - 1 - a, h, pl.ds(z.step[k], z.count[k]), :] for h in (0, 1) for k in (1, 0)], axis=0)
        )
    used = [jnp.concatenate([operand[n, pl.ds(0, 128 + C), :], operand[n, pl.ds(256 - C, C), :]], axis=0) for n in (0, 1)]
    return product(used, split(jnp.concatenate(columns, axis=1)))


def tap_sums(result, tiles, first_group):
    group = group_of()
    for a in range(TAPS):
        for b in range(TAPS):
            total = None
            for p in range(4):
                at = tap_rows(p + b - 1)
                part = result[at : at + C, 128 * a : 128 * a + 128]
                total = part if total is None else jnp.where(group == p, part, total)
            tile, slot = divmod(first_group + a * TAPS + b, 4)
            tiles[tile] = jnp.where(group == slot, spread_groups(total), tiles[tile])


def tap_counts(z, turned, tiles, first_group):
    group = group_of()
    m = lax.broadcasted_iota(jnp.int32, (1, 2 * z.total), 1) % z.total
    row = jnp.where(m < z.start[0], m % z.rows[1], (m - z.start[0]) % z.rows[0])
    height = jnp.where(m < z.start[0], z.rows[1], z.rows[0])
    at = lax.axis_index("row")
    lost = {
        0: (row == height - 1) & (at == z.peers - 1),
        2: (row == 0) & (at == 0),
    }
    for a in range(TAPS):
        column = jnp.sum(jnp.where(lost[a], 0.0, turned) if a in lost else turned, axis=1, keepdims=True)
        used = jnp.concatenate([column[: 128 + C], column[256 - C :]], axis=0)
        for b in range(TAPS):
            total = sum(used[tap_rows(p + b - 1) : tap_rows(p + b - 1) + C] for p in range(4))
            tile, slot = divmod(first_group + a * TAPS + b, 4)
            tiles[tile] = jnp.where(group == slot, total, tiles[tile])


def turned_operand(z, value, pads, kept):
    fill_center(z, pads, value)
    lane = lax.broadcasted_iota(jnp.int32, (1, 128), 1)
    halves = ([], [])
    for k in (1, 0):
        ref, step, count = pads[k], z.step[k], z.count[k]
        low, high = ref[1, 0, pl.ds(step, count), :], ref[1, 1, pl.ds(step, count), :]
        before, after = ref[1, 1, pl.ds(0, count), :], ref[1, 0, pl.ds(2 * step, count), :]
        for part, main, left, right in ((halves[0], low, before, high), (halves[1], high, low, after)):
            part.append(jnp.concatenate([main, jnp.where(lane >= 96, left, jnp.where(lane < 32, right, 0.0))], axis=1))
    turned = jnp.concatenate(halves[0] + halves[1], axis=0).T
    parts = split(turned)
    for n in (0, 1):
        kept[n] = parts[n]
    return turned


def first_operand_kernel(z, x, hidden, h_above, h_below, pair, other, stats, affine, teacher, upstream, weights, left, packed, teachers, spread_u, near_u, pads, chains, kept, kept_w, kept_u, pixels, kept_t, kept_c, kept_packed, sems):
    r, own = z.rims, pl.ds(0, z.total)
    loads = [pltpu.make_async_copy(upstream, kept_u.at[own, :], sems.at[0]), pltpu.make_async_copy(weights.at[1], kept_w, sems.at[1])]
    start_all(loads)
    act = activation(stats[0:1], stats[1:2], affine[0:1], affine[1:2])
    value = turned_operand(z, act(x[...]), pads, kept)
    stores = [pltpu.make_async_copy(kept, left, sems.at[2])]
    stores[0].start()
    tiles = [jnp.zeros((C, 128), F32) for _ in range(BACK_LANES // 128)]
    tap_counts(z, value, tiles, ONES)
    pivot = affine[4:5]
    result = tap_product(
        z, kept, hidden[...] - pivot, (h_above[pl.ds(2 * r, r), :] - pivot) * inside(z, 1, True),
        (h_below[pl.ds(0, r), :] - pivot) * inside(z, 1, False), pads,
    )
    tap_sums(result, tiles, HIDDEN)
    kept_packed[...] = jnp.concatenate(tiles, axis=1)
    stores.append(pltpu.make_async_copy(kept_packed, packed, sems.at[6]))
    stores[1].start()
    pixels[own, :] = teacher[...]
    pixels[pl.ds(z.total, 4 * r), :] = jnp.zeros((4 * r, 128), F32)
    n = (REACH + 2) * r
    for side, beyond_of in enumerate((above_of, below_of)):
        for d in (0, 1):
            for k in (0, 1):
                line = beyond_of(pair, other, (pl.ds(n + k * z.images[0], z.images[k]), pl.ds(128 * d, 128)))
                for j in range(z.blocks[k]):
                    at = z.total + (2 * side + d) * r + z.rim[k] + j * z.images[k]
                    pixels[pl.ds(at, z.images[k]), pl.ds(0, BLOCK)] = line[:, j * BLOCK : (j + 1) * BLOCK]
    kept_t[...] = spread(pixels[...], to_channels())
    stores.append(pltpu.make_async_copy(kept_t, teachers, sems.at[3]))
    stores[2].start()
    n = REACH * r
    at = (pl.ds(n, 2 * r), pl.ds(0, LANES))
    up, down = above_of(pair, other, at) * inside(z, 2, True), below_of(pair, other, at) * inside(z, 2, False)
    kept_u[pl.ds(z.total, r), :] = up[r:]
    kept_u[pl.ds(z.total + r, r), :] = down[:r]
    wait_all(loads)
    stores.append(pltpu.make_async_copy(kept_u, near_u, sems.at[5]))
    stores[3].start()
    kept_c[...] = jnp.concatenate(convolve(z, kept_u[own, :], up, down, 2, pads, chains, kept_w), axis=0)
    stores.append(pltpu.make_async_copy(kept_c, spread_u, sems.at[4]))
    stores[4].start()
    wait_all(stores)


def second_operand_kernel(z, hidden, near, stats, affine, out, o_above, o_below, teachers, spread_u, near_u, weights, out_copy, hidden_copy, left, shifts, by_map, by_teacher, up, pads, chains, kept_t, kept_u, kept_w, kept_s, sems):
    r, total = z.rims, z.total
    loads = [
        pltpu.make_async_copy(teachers, kept_t, sems.at[0]),
        pltpu.make_async_copy(weights.at[1], kept_w, sems.at[1]),
        pltpu.make_async_copy(spread_u, kept_u, sems.at[2]),
    ]
    start_all(loads)
    stores = [
        pltpu.make_async_copy(out, out_copy, sems.at[4]),
        pltpu.make_async_copy(hidden, hidden_copy.at[pl.ds(0, total), :], sems.at[7]),
        pltpu.make_async_copy(near.at[0], hidden_copy.at[pl.ds(total, r), :], sems.at[8]),
        pltpu.make_async_copy(near.at[1], hidden_copy.at[pl.ds(total + r, r), :], sems.at[9]),
        pltpu.make_async_copy(near_u, up, sems.at[10]),
    ]
    start_all(stores)
    normed = normed_by(stats)(jnp.concatenate([hidden[...], near[0], near[1]], axis=0))
    shifted = normed * affine[2:3] + affine[3:4]
    turned_operand(z, gelu(shifted[:total]), pads, left)
    ones = jnp.ones((total, 1), F32)
    masks = jnp.concatenate([ones, inside(z, 1, True), inside(z, 1, False)], axis=0)
    slopes = gelu_slope(shifted) * masks
    o = jnp.concatenate([out[...], o_above[...] * inside(z, 2, True), o_below[...] * inside(z, 2, False)], axis=0)
    for_map = spread(attention(o), to_channels()) * o
    wait_all(loads)
    for_teacher = kept_t[...] * o
    kept_s[0] = kept_u[...] * slopes
    stores += copies_of(pieces(kept_s, shifts), sems, 11)
    stores[-3].start()
    for n, value, ref in ((1, for_map, by_map), (2, for_teacher, by_teacher)):
        own, before, after = value[:total], value[total : total + 2 * r], value[total + 2 * r :]
        ref[...] = jnp.concatenate([own, before[r:], after[:r]], axis=0)
        kept_s[n] = jnp.concatenate(convolve(z, own, before, after, 2, pads, chains, kept_w), axis=0) * slopes
        stores[n - 3].start()
    wait_all(stores)


def upstream_kernel(z, gathered, up, shifts, left_1, left_2, packed, by_map, by_teacher, hidden, stats, dout, dshift, d_above, d_below, slabs, kept_s, kept_left, kept_h, kept_packed, pads, more_pads, sems):
    r, total = z.rims, z.total
    loads = copies_of(
        pieces(shifts, kept_s) + pieces(left_1, kept_left) + [(hidden.at[pl.ds(0, total), :], kept_h), (packed, kept_packed)], sems
    )
    start_all(loads)
    lane = lax.broadcasted_iota(jnp.int32, (z.slots, 128), 1)
    sums = sum(gathered[pl.ds(n * z.slots, z.slots), :] for n in range(z.peers))
    square = jnp.sum(jnp.where(lane < 64, sums, 0.0), axis=1, keepdims=True)
    cross = jnp.sum(jnp.where(lane < 64, 0.0, sums), axis=1, keepdims=True)
    inverse = lax.rsqrt(square + map_eps)
    inner = beta_weight * (square * inverse - cross) * inverse
    shape = (z.slots, 128)
    for_map = (beta_weight - inner) * inverse * inverse * (2.0 / C)
    for_teacher = beta_weight * inverse * (2.0 / C)
    for_map, for_teacher = (wide(image_rows(z, jnp.broadcast_to(v, shape), 2)) for v in (for_map, for_teacher))
    value = up[...] + for_map * by_map[...] - for_teacher * by_teacher[...]
    dout[...] = value[:total]
    wait_all(loads[:3])
    shift = kept_s[0] + for_map * kept_s[1] - for_teacher * kept_s[2]
    pre, above, below = shift[:total], shift[total : total + r], shift[total + r :]
    dshift[...] = pre
    d_above[...] = above
    d_below[...] = below
    second = tap_product(z, left_2, value[:total], value[total : total + r], value[total + r :], pads)
    wait_all(loads[3:5])
    first = tap_product(z, kept_left, pre, above, below, more_pads)
    wait_all(loads[5:])
    normed = normed_by(stats)(kept_h[...])
    tiles = [kept_packed[:, 128 * n : 128 * n + 128] for n in range(BACK_LANES // 128)]
    group = group_of()
    tiles[0] = jnp.where(group == BIAS, fold(column_sum(pre)), jnp.where(group == GAIN, fold(column_sum(pre * normed)), tiles[0]))
    tap_sums(second, tiles, SECOND)
    tap_sums(first, tiles, LEFT)
    line = jnp.concatenate(tiles, axis=1)
    for d in range(z.devices):
        slabs[d] = line[d % C : d % C + 1]


def write_kernel(z, out, x, hidden, weights, first_stats, stats, order, out_s, out_l, first_normed, normed, weight, kept, kept_x, kept_h, half, sems):
    loads = [pltpu.make_async_copy(a, b, sems.at[n]) for n, (a, b) in enumerate(((out, kept), (x, kept_x), (hidden, kept_h), (weights.at[0], weight)))]
    start_all(loads)
    loads[0].wait()
    put_halves(half, kept[...])
    from_matrix(z, half, (out_s, out_l))
    loads[1].wait()
    first_normed[...] = normed_by(first_stats)(kept_x[...])
    loads[2].wait()
    normed[...] = normed_by(stats)(kept_h[...])
    loads[3].wait()


def norm_sums(total):
    group = group_of()
    return [wide(spread_groups(jnp.where(group == n, total[:, :128], 0.0))) for n in (BIAS, GAIN)]


def hidden_kernel(z, gathered, dshift, d_above, d_below, second_normed, stats, affine, weight, first_normed, pre_ref, gain_out, bias_out, slabs, pads):
    total = jnp.sum(gathered[...], axis=0)
    bias_sum, gain_sum = norm_sums(total)
    bias_out[...] = bias_sum[:, :C]
    gain_out[...] = gain_sum[:, :C]
    bias_mean, gain_mean = bias_sum / z.pixels, gain_sum / z.pixels
    factor = affine[2:3] * stats[1:2]
    r, total_rows = z.rims, z.total

    def back(d, normed):
        return factor * (d - bias_mean - normed * gain_mean)

    own = back(dshift[...], second_normed[pl.ds(0, total_rows), :])
    up = back(d_above[...], second_normed[pl.ds(total_rows, r), :]) * inside(z, 1, True)
    down = back(d_below[...], second_normed[pl.ds(total_rows + r, r), :]) * inside(z, 1, False)
    grad, _, _ = convolve(z, own, up, down, 1, pads, None, weight)
    normed = first_normed[...]
    pre = grad * gelu_slope(normed * affine[0:1] + affine[1:2])
    pre_ref[...] = pre
    lane = lax.broadcasted_iota(jnp.int32, (1, 128), 1)
    taps = TAPS * TAPS * C

    def along(row):
        return jnp.concatenate([row[:, :128]] * 3, axis=1)[:, :taps]

    second, left, against, ones = (total[:, n * C : n * C + taps] for n in (SECOND, LEFT, HIDDEN, ONES))
    against = along(stats[1:2]) * (against - along(stats[0:1] - affine[4:5]) * ones)
    first = along(factor) * (left - along(bias_mean) * ones - along(gain_mean) * against)
    sums = jnp.where(lane < C, fold(column_sum(pre)), fold(column_sum(pre * normed)))
    line = jnp.concatenate([sums[:, : 2 * C], second, first], axis=1)
    slabs[...] = jnp.broadcast_to(line[None], slabs.shape)


def back_kernel(z, gathered, pre, normed, stats, affine, dout, back_s, back_l, one, two, gain_out, bias_out, half, lines):
    bias_sum, gain_sum = norm_sums(jnp.sum(gathered[:, :, pl.ds(0, 128)], axis=0))
    bias_out[...] = bias_sum[:, :C]
    gain_out[...] = gain_sum[:, :C]
    value = dout[...] + affine[0:1] * stats[1:2] * (pre[...] - bias_sum / z.pixels - normed[...] * (gain_sum / z.pixels))
    put_halves(half, value)
    from_matrix(z, half, (back_s, back_l))
    for d in range(C):
        lines[pl.ds(d, 1), :] = gathered[d]
    for ref, group in ((two, LAST_SECOND), (one, LAST_FIRST)):
        for a in range(TAPS):
            for b in range(TAPS):
                at = (group + a * TAPS + b) * C
                ref[a, b] = lines[:, pl.ds(at, C)]


def call(body, ins, outs, scratch=(), sems=0):
    space = {"v": pltpu.VMEM, "h": pltpu.HBM, "V": pltpu.VMEM}
    shapes = []
    for item in scratch:
        if isinstance(item, list):
            shapes.append([pltpu.VMEM(*s) for s in item])
        else:
            shapes.append(pltpu.VMEM(*item))
    if sems:
        shapes.append(pltpu.SemaphoreType.DMA((sems,)))
    run = pl.pallas_call(
        body,
        out_shape=[jax.ShapeDtypeStruct(shape, kind) if s == "v" else space[s](shape, kind) for s, shape, kind in outs],
        in_specs=[pl.BlockSpec(memory_space=space[s]) for s in ins],
        out_specs=[pl.BlockSpec(memory_space=space[s]) for s, _, _ in outs],
        scratch_shapes=shapes,
        compiler_params=pltpu.CompilerParams(vmem_limit_bytes=VMEM_LIMIT),
    )
    return lambda *args: run(
        *(pltpu.with_memory_space_constraint(arg, pltpu.HBM) if s == "h" else arg for s, arg in zip(ins, args))
    )


def exchange(lines, axes):
    shape = lines.shape
    if len(shape) == 2:
        lines = lines.reshape(math.prod(lax.axis_size(axis) for axis in axes), -1, 128)
    return lax.all_to_all(lines, axes, 0, 0, tiled=True).reshape(shape)


def beyond(z, pair, other, depths):
    hops = max(-(-depth // rows) for rows in z.rows for depth in depths)
    if hops == 1:
        swap = lambda value, start: lax.ppermute(
            value, "row", [(i + a, i + 1 - a) for i in range(start, z.peers - 1, 2) for a in (0, 1)]
        )
        return swap(pair, 0), swap(other, 1)
    even = is_even()
    bottom, top = jnp.where(even, pair, other), jnp.where(even, other, pair)
    above, below = [], []
    for hop in range(1, hops + 1):
        above.append(lax.ppermute(bottom, "row", [(i, i + hop) for i in range(z.peers - hop)]))
        below.append(lax.ppermute(top, "row", [(i + hop, i) for i in range(z.peers - hop)]))
    up, down = [], []
    base = 0
    for depth in depths:
        for n in range(depth):
            for k in (1, 0):
                hop, back = divmod(depth - 1 - n, z.rows[k])
                at = base + (depth - 1 - back) * z.rims + z.rim[k]
                up.append(above[hop][at : at + z.edge[k]])
                hop, back = divmod(n, z.rows[k])
                at = base + back * z.rims + z.rim[k]
                down.append(below[hop][at : at + z.edge[k]])
        base += depth * z.rims
    up.append(jnp.concatenate([pixel_rows(z, above, base, 1, 1), pixel_rows(z, above, base, 0, 1)], axis=1))
    down.append(jnp.concatenate([pixel_rows(z, below, base, 0, 0), pixel_rows(z, below, base, 1, 0)], axis=1))
    up, down = jnp.concatenate(up, axis=0), jnp.concatenate(down, axis=0)
    return jnp.where(even, down, up), jnp.where(even, up, down)


def pixel_rows(z, bands, base, distance, last):
    lines = []
    for k in (0, 1):
        hop, back = divmod(distance, z.rows[k])
        at = base + k * z.images[0]
        half = 128 * abs(last - back)
        lines.append(bands[hop][at : at + z.images[k], half : half + 128])
    lines.append(jnp.zeros((z.slots - sum(z.images), 128), F32))
    return jnp.concatenate(lines, axis=0)


def local(
    image_small, image_large, teacher_small, teacher_large, upstream_small, upstream_large,
    conv_first, gain_first, bias_first, conv_second, gain_second, bias_second,
):
    peers = lax.axis_size("row")
    devices = lax.axis_size("img") * peers
    z = Sizes(image_small.shape, image_large.shape, devices, peers)
    body = lambda function: functools.partial(function, z)
    r = z.rims
    full, half, pair = (z.total, LANES), (2, z.total, 128), (2 * devices, 128)
    weight, left = (2, TAPS * TAP_ROWS, 128), (2, 256, 2 * z.total)
    images = [image_small, image_large, upstream_small, upstream_large, teacher_small, teacher_large]
    f = lambda space, *shape: (space, shape, F32)
    depths = (REACH, 2)
    rim_rows = sum(depths) * r + z.slots

    x, pair_edge, other_edge, copies = call(
        body(start_kernel),
        "hhhhhh",
        [("v", full, F32), f("v", rim_rows, LANES), f("v", rim_rows, LANES), ("V", pair, F32)],
        [[(a.shape, F32) for a in images], (half, F32)],
        4 + 2 * z.images[1],
    )(*images)
    gathered = exchange(copies, AXES)
    pair_rims, other_rims = beyond(z, pair_edge, other_edge, depths)
    params = [conv_first, conv_second] + images[2:]
    w1, w2, weights, affine, upstream, teacher, x_copy = call(
        body(prepare_kernel),
        "hhhhhhhhhhv",
        [("v", weight, BF16), ("v", weight, BF16), ("h", (2,) + weight, BF16), f("v", 5, LANES), ("h", full, F32), f("v", z.total, 128), ("h", full, F32)],
        [[(a.shape, F32) for a in params], ((2,) + weight, BF16), (full, F32), ((4, C), F32), (half, F32)],
        14,
    )(*params, *(v.reshape(1, C) for v in (gain_first, bias_first, gain_second, bias_second)), x)

    hidden, h_above, h_below, stats_one, copies = call(
        body(first_kernel),
        "vvvvvv",
        [("v", full, F32), f("v", 3 * r, LANES), f("v", 3 * r, LANES), f("v", 2, LANES), ("V", pair, F32)],
        [z.pads(), z.chains(4)],
    )(x, pair_rims, other_rims, gathered, affine, w1)
    gathered = exchange(copies, AXES)
    extended, near_rows = z.total + 4 * r, z.total + 2 * r
    left_one, packed, teachers, spread_u, near_u = call(
        body(first_operand_kernel),
        "vvvvvvvvvhh",
        [("h", left, BF16), f("h", C, BACK_LANES), f("h", extended, LANES), f("h", near_rows, LANES), f("h", near_rows, LANES)],
        [
            z.pads(), z.chains(2), (left, BF16), (weight, BF16), ((near_rows, LANES), F32), ((extended, 128), F32),
            ((extended, LANES), F32), ((near_rows, LANES), F32), ((C, BACK_LANES), F32),
        ],
        7,
    )(x, hidden, h_above, h_below, pair_rims, other_rims, stats_one, affine, teacher, upstream, weights)
    gathered, near_u = lax.optimization_barrier((gathered, near_u))

    map_shape = (peers * z.slots, 128)
    out, o_above, o_below, near, stats_two, copies = call(
        body(second_kernel),
        "vvvvvvvvvv",
        [("v", full, F32), f("v", 2 * r, LANES), f("v", 2 * r, LANES), f("v", 2, r, LANES), f("v", 2, LANES), ("V", map_shape, F32)],
        [z.pads(), z.chains(3)],
    )(hidden, h_above, h_below, gathered, affine, w2, x, pair_rims, other_rims, teacher)
    gathered = exchange(copies, ("row",))
    out_copy, hidden_copy, left_two, shifts, by_map, by_teacher, up = call(
        body(second_operand_kernel),
        "vvvvvvvhhhh",
        [
            ("h", full, F32), f("h", near_rows, LANES), ("v", left, BF16), f("h", 3, near_rows, LANES),
            f("v", near_rows, LANES), f("v", near_rows, LANES), f("v", near_rows, LANES),
        ],
        [
            z.pads(), z.chains(2), ((extended, LANES), F32), ((near_rows, LANES), F32), (weight, BF16),
            ((3, near_rows, LANES), F32),
        ],
        14,
    )(hidden, near, stats_two, affine, out, o_above, o_below, teachers, spread_u, near_u, weights)

    dout, dshift, d_above, d_below, slabs = call(
        body(upstream_kernel),
        "vvhhvhvvhv",
        [("v", full, F32), ("v", full, F32), f("v", r, LANES), f("v", r, LANES), f("V", devices, 1, BACK_LANES)],
        [((3, near_rows, LANES), F32), (left, BF16), (full, F32), ((C, BACK_LANES), F32), z.pads(), z.pads()],
        7,
    )(gathered, up, shifts, left_one, left_two, packed, by_map, by_teacher, hidden_copy, stats_two)
    gathered = exchange(slabs, AXES)
    out_s, out_l, first_normed, second_normed, weight_back = call(
        body(write_kernel),
        "hhhhvvv",
        [("v", image_small.shape, F32), ("v", image_large.shape, F32), ("v", full, F32), f("v", near_rows, LANES), ("v", weight, BF16)],
        [(full, F32), (full, F32), ((near_rows, LANES), F32), (half, F32)],
        4,
    )(out_copy, x_copy, hidden_copy, weights, stats_one, stats_two, d_above)

    pre, gain_two, bias_two, slabs = call(
        body(hidden_kernel),
        "vvvvvvvvv",
        [("v", full, F32), f("v", 1, C), f("v", 1, C), f("V", devices, 1, LAST_LANES)],
        [z.pads()],
    )(gathered, dshift, d_above, d_below, second_normed, stats_two, affine, weight_back, first_normed)
    gathered = exchange(slabs, AXES)

    back_s, back_l, one, two, gain_one, bias_one = call(
        body(back_kernel),
        "vvvvvv",
        [("v", a.shape, F32) for a in (image_small, image_large, conv_first, conv_second)] + [f("v", 1, C), f("v", 1, C)],
        [(half, F32), ((C, LAST_LANES), F32)],
    )(gathered, pre, first_normed, stats_one, affine, dout)
    return (
        out_s, out_l, back_s, back_l,
        one, gain_one.reshape(C), bias_one.reshape(C),
        two, gain_two.reshape(C), bias_two.reshape(C),
    )


def solution(mesh):
    split_bands, everywhere = P("img", "row", None), P()
    return jax.shard_map(
        local,
        mesh=mesh,
        in_specs=(split_bands,) * 6 + (everywhere,) * 6,
        out_specs=(split_bands,) * 4 + (everywhere,) * 6,
        check_vma=False,
    )
```

```python
import functools
import math

import jax
import jax.numpy as jnp
from jax import lax
from jax.experimental import pallas as pl
from jax.experimental.pallas import tpu as pltpu
from jax.sharding import PartitionSpec as P

C = 32
HS = 32
HL = 64
HEIGHTS = (HS, HL)

norm_eps = 1e-05
map_eps = 1e-06
beta_weight = 1000.0
AXES = ("img", "row")
BLOCK = 8
LANES = BLOCK * C
TAPS = 3
DEPTH = TAPS * 128 + 256
TAP_ROWS = 128 + 2 * C
REACH = 4
ROOT = math.sqrt(2.0 / math.pi)
CUBE = 0.044715
F32 = jnp.float32
BF16 = jnp.bfloat16
VMEM_LIMIT = 32 * 1024 * 1024
BIAS, GAIN, SECOND, LEFT, HIDDEN, ONES = 0, 1, 2, 11, 20, 29
BACK_LANES = 1280
LAST_SECOND, LAST_FIRST, LAST_LANES = 2, 11, 640


class Sizes:
    def __init__(self, small, large, devices, peers):
        self.images = (small[0], large[0])
        self.rows = (small[1], large[1])
        self.blocks = (HS // BLOCK, HL // BLOCK)
        self.step = tuple(n * r for n, r in zip(self.images, self.rows))
        self.count = tuple(b * s for b, s in zip(self.blocks, self.step))
        self.edge = tuple(b * n for b, n in zip(self.blocks, self.images))
        self.start = (self.count[1], 0)
        self.rim = (self.edge[1], 0)
        self.total = sum(self.count)
        self.rims = sum(self.edge)
        self.slots = -(-sum(self.images) // 8) * 8
        self.guard = -(-max(self.images) // 8) * 8
        self.devices = devices
        self.peers = peers
        self.here = float(self.total * BLOCK)
        self.pixels = self.here * devices

    def pads(self):
        return [((TAPS, 2, self.count[k] + 2 * self.step[k], 128), F32) for k in (0, 1)]

    def chains(self, depth):
        return [((2, 2 * self.guard + (depth + 1) * self.rims, 128), F32)] * 2


def split(value):
    high = value.astype(BF16)
    return high, (value - high.astype(F32)).astype(BF16)


def dot(left, right):
    return lax.dot_general(left, right, (((1,), (0,)), ((), ())), preferred_element_type=F32)


def product(left, right):
    if left[0].shape[1] % 128:
        return dot(left[0], right[0]) + (dot(left[0], right[1]) + dot(left[1], right[0]))
    return dot(
        jnp.concatenate([left[0], left[0], left[1]], axis=1), jnp.concatenate([right[0], right[1], right[0]], axis=0)
    )


def spread(left, right):
    right = right.astype(BF16)
    return dot(jnp.concatenate(split(left), axis=1), jnp.concatenate([right, right], axis=0))


def gelu(s):
    return 0.5 * s * (1.0 + jnp.tanh(ROOT * (s + CUBE * s * s * s)))


def gelu_slope(s):
    square = s * s
    t = jnp.tanh(ROOT * s * (1.0 + CUBE * square))
    return 0.5 * (1.0 + t) + 0.5 * s * (1.0 - t * t) * ROOT * (1.0 + 3.0 * CUBE * square)


def spread_groups(row):
    row = row + pltpu.roll(row, 64, 1)
    return row + pltpu.roll(row, 32, 1)


def fold(row):
    return spread_groups(row[:, :128] + row[:, 128:])


def wide(row):
    return jnp.concatenate([row, row], axis=1)


def group_of(rows=1, lanes=128):
    return lax.broadcasted_iota(jnp.int32, (rows, lanes), 1) // C


def column_sum(value):
    return jnp.sum(value, axis=0, keepdims=True)


def send_lines(z, ref, lines):
    for n, line in enumerate(lines):
        ref[pl.ds(n, z.devices, stride=len(lines)), :] = jnp.broadcast_to(line, (z.devices, 128))


def moments(z, value, ref):
    few = min(8, z.total)
    pivot = fold(column_sum(value[:few])) / float(few * BLOCK)
    off = value - wide(pivot)
    first, second = fold(column_sum(off)), fold(column_sum(off * off))
    send_lines(z, ref, [pivot + first / z.here, second - first * first / z.here])


def merged(z, ref):
    means = ref[pl.ds(0, z.devices, stride=2), :]
    center = jnp.mean(means, axis=0, keepdims=True)
    off = means - center
    within = jnp.mean(ref[pl.ds(1, z.devices, stride=2), :], axis=0, keepdims=True)
    variance = within / z.here + jnp.mean(off * off, axis=0, keepdims=True)
    return wide(center), wide(lax.rsqrt(variance + norm_eps))


def put_halves(ref, value):
    ref[0] = value[:, :128]
    ref[1] = value[:, 128:]


def whole(ref):
    return jnp.concatenate([ref[0], ref[1]], axis=1)


def to_matrix(z, refs, half):
    for k in (0, 1):
        for j in range(z.blocks[k]):
            at = z.start[k] + j * z.step[k]
            for i in range(z.images[k]):
                for h in (0, 1):
                    half[h, pl.ds(at + i * z.rows[k], z.rows[k]), :] = refs[k][i, :, pl.ds(LANES * j + 128 * h, 128)]


def from_matrix(z, half, refs):
    for k in (0, 1):
        for j in range(z.blocks[k]):
            at = z.start[k] + j * z.step[k]
            for i in range(z.images[k]):
                for h in (0, 1):
                    refs[k][i, :, pl.ds(LANES * j + 128 * h, 128)] = half[h, pl.ds(at + i * z.rows[k], z.rows[k]), :]


def is_even():
    return lax.axis_index("row") % 2 == 0


def put_edges(pair, other, at, last, first):
    even = is_even()
    pair[at] = jnp.where(even, last, first)
    other[at] = jnp.where(even, first, last)


def above_of(pair, other, at):
    return jnp.where(is_even(), other[at], pair[at])


def below_of(pair, other, at):
    return jnp.where(is_even(), pair[at], other[at])


def take_rims(z, half, depth, pair, other):
    everything = pl.ds(0, 128)
    for k in (0, 1):
        nothing = jnp.zeros((z.edge[k], 128), F32)
        for n in range(depth):
            first, last = nothing, nothing
            if depth - n <= z.rows[k]:
                last = half[pl.ds(z.start[k] + z.rows[k] - depth + n, z.edge[k], stride=z.rows[k]), :]
            if n < z.rows[k]:
                first = half[pl.ds(z.start[k] + n, z.edge[k], stride=z.rows[k]), :]
            put_edges(pair, other, (pl.ds(n * z.rims + z.rim[k], z.edge[k]), everything), last, first)


def inside(z, depth, above):
    at = lax.axis_index("row")
    large = lax.broadcasted_iota(jnp.int32, (z.rims, 1), 0) < z.rim[0]
    parts = []
    for n in range(depth):
        if above:
            ok = [jnp.where(at * rows >= depth - n, 1.0, 0.0) for rows in z.rows]
        else:
            ok = [jnp.where((at + 1) * rows + n + 1 <= height, 1.0, 0.0) for rows, height in zip(z.rows, HEIGHTS)]
        parts.append(jnp.where(large, ok[1], ok[0]).astype(F32))
    return jnp.concatenate(parts, axis=0)


def clear_guards(z, pads, a):
    for k in (0, 1):
        pads[k][a, 1, pl.ds(0, z.step[k]), :] = jnp.zeros((z.step[k], 128), F32)
        pads[k][a, 0, pl.ds(z.step[k] + z.count[k], z.step[k]), :] = jnp.zeros((z.step[k], 128), F32)


def fill_center(z, pads, value):
    clear_guards(z, pads, 1)
    for k in (0, 1):
        for h in (0, 1):
            pads[k][1, h, pl.ds(z.step[k], z.count[k]), :] = value[z.start[k] : z.start[k] + z.count[k], 128 * h : 128 * h + 128]


def fill_shifted(z, pads, above, below):
    for k in (0, 1):
        ref, step, count, rows = pads[k], z.step[k], z.count[k], z.rows[k]
        rim = slice(z.rim[k], z.rim[k] + z.edge[k])
        for h in (0, 1):
            lanes = slice(128 * h, 128 * h + 128)
            ref[0, h, pl.ds(step, count), :] = ref[1, h, pl.ds(step - 1, count), :]
            ref[2, h, pl.ds(step, count), :] = ref[1, h, pl.ds(step + 1, count), :]
            ref[0, h, pl.ds(step, z.edge[k], stride=rows), :] = above[rim, lanes]
            ref[2, h, pl.ds(step + rows - 1, z.edge[k], stride=rows), :] = below[rim, lanes]


def fill_pads(z, pads, value, above, below):
    fill_center(z, pads, value)
    fill_shifted(z, pads, above, below)
    for a in (0, 2):
        clear_guards(z, pads, a)


def beside(left, right):
    lane = lax.broadcasted_iota(jnp.int32, (1, 128), 1)
    middle = pltpu.roll(jnp.where(lane >= 64, left[1], right[1]), 64, 1)
    return [
        jnp.where(lane >= 96, left[0], jnp.where(lane < 32, right[0], middle)),
        jnp.where(lane >= 96, left[2], jnp.where(lane < 32, right[2], 0.0)),
    ]


def band_operand(z, pads):
    parts = ([], [])
    for k in (1, 0):
        ref, step, count = pads[k], z.step[k], z.count[k]
        low, high = ([ref[a, h, pl.ds(step, count), :] for a in range(TAPS)] for h in (0, 1))
        before = [ref[a, 1, pl.ds(0, count), :] for a in range(TAPS)]
        after = [ref[a, 0, pl.ds(2 * step, count), :] for a in range(TAPS)]
        parts[0].append(jnp.concatenate(low + beside(before, high), axis=1))
        parts[1].append(jnp.concatenate(high + beside(low, after), axis=1))
    return [jnp.concatenate(part, axis=0) for part in parts]


def rim_operand(z, chain, depth):
    m = lax.broadcasted_iota(jnp.int32, (z.rims, 1), 0)
    large = m < z.rim[0]
    has_before = jnp.where(large, m, m - z.rim[0]) >= jnp.where(large, z.images[1], z.images[0])
    has_after = m < jnp.where(large, z.rim[0] - z.images[1], z.rims - z.images[0])
    low, high, before, after = [], [], [], []
    for r in range(depth + 1):
        at = z.guard + r * z.rims
        low.append(chain[0, pl.ds(at, z.rims), :])
        high.append(chain[1, pl.ds(at, z.rims), :])
        shifted = [chain[1, pl.ds(at - images, z.rims), :] for images in z.images]
        before.append(jnp.where(has_before, jnp.where(large, shifted[1], shifted[0]), 0.0))
        shifted = [chain[0, pl.ds(at + images, z.rims), :] for images in z.images]
        after.append(jnp.where(has_after, jnp.where(large, shifted[1], shifted[0]), 0.0))
    parts = ([], [])
    for n in range(depth - 1):
        rows = slice(n, n + TAPS)
        parts[0].append(jnp.concatenate(low[rows] + beside(before[rows], high[rows]), axis=1))
        parts[1].append(jnp.concatenate(high[rows] + beside(low[rows], after[rows]), axis=1))
    return [jnp.concatenate(part, axis=0) for part in parts]


def times(parts, weight):
    left = jnp.concatenate([part[h] for h in (0, 1) for part in parts], axis=0)
    both = jnp.concatenate([weight_matrix(weight.at[0]), weight_matrix(weight.at[1])], axis=1)
    result = dot(jnp.concatenate(split(left), axis=1), jnp.concatenate([both, both], axis=0))
    result = result[:, :128] + result[:, 128:]
    rows = result.shape[0] // 2
    return jnp.concatenate([result[:rows], result[rows:]], axis=1)


def convolve(z, own, above, below, depth, pads, chains, weight):
    r = z.rims
    fill_pads(z, pads, own, above[(depth - 1) * r :], below[:r])
    parts = [band_operand(z, pads)]
    if depth > 1:
        for side, (rim, chain) in enumerate(zip((above, below), chains)):
            rim_at, own_at = (z.guard, z.guard + depth * r) if side == 0 else (z.guard + r, z.guard)
            for h in (0, 1):
                chain[h, pl.ds(rim_at, depth * r), :] = rim[:, 128 * h : 128 * h + 128]
                for k in (0, 1):
                    row = z.step[k] + (0 if side == 0 else z.rows[k] - 1)
                    chain[h, pl.ds(own_at + z.rim[k], z.edge[k]), :] = pads[k][1, h, pl.ds(row, z.edge[k], stride=z.rows[k]), :]
            parts.append(rim_operand(z, chain, depth))
    result = times(parts, weight)
    n = z.total + (depth - 1) * r
    return result[: z.total], result[z.total : n], result[n:]


def image_sums(z, value):
    slot = lax.broadcasted_iota(jnp.int32, (z.slots, 1), 0)
    sums = jnp.zeros((z.slots, 128), F32)
    for k in (0, 1):
        line = value[z.start[k] : z.start[k] + z.step[k]]
        for j in range(1, z.blocks[k]):
            at = z.start[k] + j * z.step[k]
            line = line + value[at : at + z.step[k]]
        image = lax.broadcasted_iota(jnp.int32, (z.step[k], 1), 0) // z.rows[k]
        for i in range(z.images[k]):
            sums = jnp.where(slot == i + k * z.images[0], column_sum(jnp.where(image == i, line, 0.0)), sums)
    return sums


def image_rows(z, values, rims):
    parts = []
    for k in (1, 0):
        image = lax.broadcasted_iota(jnp.int32, (z.step[k], 1), 0) // z.rows[k]
        line = jnp.zeros((z.step[k], 128), F32)
        for i in range(z.images[k]):
            at = i + k * z.images[0]
            line = jnp.where(image == i, values[at : at + 1], line)
        parts += [line] * z.blocks[k]
    if rims:
        m = lax.broadcasted_iota(jnp.int32, (z.rims, 1), 0)
        image = jnp.where(m < z.rim[0], z.images[0] + m % z.images[1], (m - z.rim[0]) % z.images[0])
        line = jnp.zeros((z.rims, 128), F32)
        for at in range(sum(z.images)):
            line = jnp.where(image == at, values[at : at + 1], line)
        parts += [line] * rims
    return jnp.concatenate(parts, axis=0)


def channel_mean():
    a = lax.broadcasted_iota(jnp.int32, (LANES, 128), 0) // C
    b = lax.broadcasted_iota(jnp.int32, (LANES, 128), 1) % 64
    return jnp.where(a == b, 1.0 / C, 0.0).astype(F32)


def to_channels():
    a = lax.broadcasted_iota(jnp.int32, (128, LANES), 0)
    b = lax.broadcasted_iota(jnp.int32, (128, LANES), 1) // C
    return jnp.where(a == b, 1.0, 0.0).astype(F32)


def attention(value):
    return spread(value * value, channel_mean())


def pieces(source, target):
    return [(source.at[n], target.at[n]) for n in range(source.shape[0])]


def copies_of(pairs, sems, first=0):
    return [pltpu.make_async_copy(a, b, sems.at[first + n]) for n, (a, b) in enumerate(pairs)]


def start_all(copies):
    for copy in copies:
        copy.start()


def wait_all(copies):
    for copy in copies:
        copy.wait()


def start_kernel(z, small, large, up_s, up_l, t_s, t_l, x, pair, other, copies, raw, half, sems):
    images = [(small, raw[0])] + pieces(large, raw[1])
    rest = [(up_s, raw[2])] + pieces(up_l, raw[3]) + [(t_s, raw[4]), (t_l, raw[5])]
    loads = copies_of(images + rest, sems)
    start_all(loads)
    r, n = z.rims, REACH * z.rims
    tail = n + 2 * r
    for ref in (pair, other):
        ref[pl.ds(tail, z.slots), :] = jnp.zeros((z.slots, LANES), F32)
    wait_all(loads[: len(images)])
    to_matrix(z, raw[:2], half)
    value = whole(half)
    x[...] = value
    moments(z, value, copies)
    for h in (0, 1):
        lanes = pl.ds(128 * h, 128)
        take_rims(z, half.at[h], REACH, pair.at[pl.ds(0, n), lanes], other.at[pl.ds(0, n), lanes])
    wait_all(loads[len(images) :])
    for k in (0, 1):
        width, rows = HEIGHTS[k], z.rows[k]
        for i in range(z.images[k]):
            slot = pl.ds(tail + i + k * z.images[0], 1)
            for d in (0, 1):
                has_last, has_first = rows + d >= 2, d < rows
                last, first = pl.ds(max(rows - 2 + d, 0), 1), pl.ds(min(d, rows - 1), 1)
                for j in range(z.blocks[k]):
                    lanes = pl.ds(LANES * j, LANES)
                    at = (pl.ds(n + d * r + z.rim[k] + j * z.images[k] + i, 1), pl.ds(0, LANES))
                    nothing = jnp.zeros((1, LANES), F32)
                    put_edges(
                        pair, other, at,
                        raw[2 + k][i, last, lanes] if has_last else nothing,
                        raw[2 + k][i, first, lanes] if has_first else nothing,
                    )
                nothing = jnp.zeros((1, width), F32)
                put_edges(
                    pair, other, (slot, pl.ds(128 * d, width)),
                    raw[4 + k][i, last, :] if has_last else nothing,
                    raw[4 + k][i, first, :] if has_first else nothing,
                )


def banded(taps, ref):
    row = lax.broadcasted_iota(jnp.int32, (128, 128), 0) // C
    lane = group_of(128)
    for a in range(TAPS):
        main = jnp.zeros((128, 128), F32)
        for b in range(TAPS):
            main = jnp.where(row - lane + 1 == b, taps[a][b], main)
        before = jnp.where(lane[:C] == 0, taps[a][0][:C], 0.0)
        after = jnp.where(lane[:C] == 3, taps[a][2][:C], 0.0)
        for n, part in enumerate(split(jnp.concatenate([main, before, after], axis=0))):
            ref[n, pl.ds(a * TAP_ROWS, TAP_ROWS), :] = part


def weight_matrix(ref):
    main = [ref[pl.ds(a * TAP_ROWS, 128), :] for a in range(TAPS)]
    before, after = ([ref[pl.ds(a * TAP_ROWS + 128 + n * C, C), :] for a in range(TAPS)] for n in (0, 1))
    return jnp.concatenate(
        main + [after[0], before[1], after[1], before[0], after[2], jnp.zeros((2 * C, 128), BF16), before[2]], axis=0
    )


def prepare_kernel(z, first, second, up_s, up_l, t_s, t_l, g1, b1, g2, b2, x, w1, w2, weights, affine, upstream, teacher, x_copy, raw, kept, kept_u, rows, half, sems):
    targets = tuple(raw) + tuple(rows.at[pl.ds(n, 1), :] for n in range(4))
    refs = (first, second, up_s, up_l, t_s, t_l, g1, b1, g2, b2)
    loads = [pltpu.make_async_copy(a, b, sems.at[n]) for n, (a, b) in enumerate(zip(refs, targets))]
    start_all(loads)
    stores = [pltpu.make_async_copy(x, x_copy, sems.at[13])]
    stores[0].start()
    wait_all(loads)
    to_matrix(z, raw[2:4], half)
    kept_u[...] = whole(half)
    stores.append(pltpu.make_async_copy(kept_u, upstream, sems.at[10]))
    stores[1].start()
    for n, (source, forward) in enumerate(zip(raw[:2], (w1, w2))):
        tiles = []
        for a in range(TAPS):
            line = [jnp.concatenate([source[a, b]] * 4, axis=1) for b in range(TAPS)]
            tiles.append([jnp.concatenate([tap] * 4, axis=0) for tap in line])
        turned = [[tiles[TAPS - 1 - a][TAPS - 1 - b].T for b in range(TAPS)] for a in range(TAPS)]
        banded(tiles, forward)
        banded(turned, kept.at[n])
        stores.append(pltpu.make_async_copy(kept.at[n], weights.at[n], sems.at[11 + n]))
        stores[-1].start()
    taps = sum(raw[0][a, b] for a in range(TAPS) for b in range(TAPS))
    pivot = dot(jnp.broadcast_to(gelu(rows[1:2]), (8, C)), taps)[0:1]
    affine[...] = jnp.concatenate([jnp.concatenate([rows[...], pivot], axis=0)] * BLOCK, axis=1)
    teacher[...] = jnp.zeros(teacher.shape, F32)
    for k, ref in ((0, raw[4]), (1, raw[5])):
        for i in range(z.images[k]):
            line = ref[i]
            for j in range(z.blocks[k]):
                at = z.start[k] + j * z.step[k] + i * z.rows[k]
                for lane in (0, 64):
                    teacher[pl.ds(at, z.rows[k]), pl.ds(lane, BLOCK)] = line[:, j * BLOCK : (j + 1) * BLOCK]
    wait_all(stores)


def normed_by(stats):
    return lambda v: (v - stats[0:1]) * stats[1:2]


def activation(center, scale, gain, bias):
    factor = scale * gain
    offset = bias - center * factor
    return lambda v: gelu(v * factor + offset)


def first_kernel(z, x, pair, other, gathered, affine, weight, hidden, h_above, h_below, stats, copies, pads, chains):
    n = REACH * z.rims
    center, scale = merged(z, gathered)
    act = activation(center, scale, affine[0:1], affine[1:2])
    own = act(x[...])
    at = (pl.ds(0, n), pl.ds(0, LANES))
    up, down = act(above_of(pair, other, at)) * inside(z, 4, True), act(below_of(pair, other, at)) * inside(z, 4, False)
    own, up, down = convolve(z, own, up, down, 4, pads, chains, weight)
    moments(z, own, copies)
    hidden[...] = own
    h_above[...] = up
    h_below[...] = down
    stats[0:1] = center
    stats[1:2] = scale


def second_kernel(z, hidden, h_above, h_below, gathered, affine, weight, x, pair, other, teacher, out, o_above, o_below, near, stats, copies, pads, chains):
    center, scale = merged(z, gathered)
    act = activation(center, scale, affine[2:3], affine[3:4])
    r = z.rims
    own = act(hidden[...])
    up, down = act(h_above[...]) * inside(z, 3, True), act(h_below[...]) * inside(z, 3, False)
    own, up, down = convolve(z, own, up, down, 3, pads, chains, weight)
    own = x[...] + own
    amap = attention(own)
    lane = lax.broadcasted_iota(jnp.int32, (1, 128), 1)
    sums = image_sums(z, amap * jnp.where(lane < 64, amap, teacher[...]))
    copies[...] = jnp.concatenate([sums] * z.peers, axis=0)
    out[...] = own
    o_above[...] = above_of(pair, other, (pl.ds(2 * r, 2 * r), pl.ds(0, LANES))) + up
    o_below[...] = below_of(pair, other, (pl.ds(0, 2 * r), pl.ds(0, LANES))) + down
    near[0] = h_above[pl.ds(2 * r, r), :]
    near[1] = h_below[pl.ds(0, r), :]
    stats[0:1] = center
    stats[1:2] = scale


def tap_rows(q):
    return 128 + C if q < 0 else q * C


def tap_product(z, operand, own, above, below, pads):
    fill_center(z, pads, own)
    fill_shifted(z, pads, above, below)
    columns = []
    for a in range(TAPS):
        columns.append(
            jnp.concatenate([pads[k][TAPS - 1 - a, h, pl.ds(z.step[k], z.count[k]), :] for h in (0, 1) for k in (1, 0)], axis=0)
        )
    used = [jnp.concatenate([operand[n, pl.ds(0, 128 + C), :], operand[n, pl.ds(256 - C, C), :]], axis=0) for n in (0, 1)]
    return product(used, split(jnp.concatenate(columns, axis=1)))


def tap_sums(result, tiles, first_group):
    group = group_of()
    for a in range(TAPS):
        for b in range(TAPS):
            total = None
            for p in range(4):
                at = tap_rows(p + b - 1)
                part = result[at : at + C, 128 * a : 128 * a + 128]
                total = part if total is None else jnp.where(group == p, part, total)
            tile, slot = divmod(first_group + a * TAPS + b, 4)
            tiles[tile] = jnp.where(group == slot, spread_groups(total), tiles[tile])


def tap_counts(z, turned, tiles, first_group):
    group = group_of()
    m = lax.broadcasted_iota(jnp.int32, (1, 2 * z.total), 1) % z.total
    row = jnp.where(m < z.start[0], m % z.rows[1], (m - z.start[0]) % z.rows[0])
    height = jnp.where(m < z.start[0], z.rows[1], z.rows[0])
    at = lax.axis_index("row")
    lost = {
        0: (row == height - 1) & (at == z.peers - 1),
        2: (row == 0) & (at == 0),
    }
    for a in range(TAPS):
        column = jnp.sum(jnp.where(lost[a], 0.0, turned) if a in lost else turned, axis=1, keepdims=True)
        used = jnp.concatenate([column[: 128 + C], column[256 - C :]], axis=0)
        for b in range(TAPS):
            total = sum(used[tap_rows(p + b - 1) : tap_rows(p + b - 1) + C] for p in range(4))
            tile, slot = divmod(first_group + a * TAPS + b, 4)
            tiles[tile] = jnp.where(group == slot, total, tiles[tile])


def turned_operand(z, value, pads, kept):
    fill_center(z, pads, value)
    lane = lax.broadcasted_iota(jnp.int32, (1, 128), 1)
    halves = ([], [])
    for k in (1, 0):
        ref, step, count = pads[k], z.step[k], z.count[k]
        low, high = ref[1, 0, pl.ds(step, count), :], ref[1, 1, pl.ds(step, count), :]
        before, after = ref[1, 1, pl.ds(0, count), :], ref[1, 0, pl.ds(2 * step, count), :]
        for part, main, left, right in ((halves[0], low, before, high), (halves[1], high, low, after)):
            part.append(jnp.concatenate([main, jnp.where(lane >= 96, left, jnp.where(lane < 32, right, 0.0))], axis=1))
    turned = jnp.concatenate(halves[0] + halves[1], axis=0).T
    parts = split(turned)
    for n in (0, 1):
        kept[n] = parts[n]
    return turned


def first_operand_kernel(z, x, hidden, h_above, h_below, pair, other, stats, affine, teacher, upstream, weights, left, packed, teachers, spread_u, near_u, pads, chains, kept, kept_w, kept_u, pixels, kept_t, kept_c, kept_packed, sems):
    r, own = z.rims, pl.ds(0, z.total)
    loads = [pltpu.make_async_copy(upstream, kept_u.at[own, :], sems.at[0]), pltpu.make_async_copy(weights.at[1], kept_w, sems.at[1])]
    start_all(loads)
    act = activation(stats[0:1], stats[1:2], affine[0:1], affine[1:2])
    value = turned_operand(z, act(x[...]), pads, kept)
    stores = [pltpu.make_async_copy(kept, left, sems.at[2])]
    stores[0].start()
    tiles = [jnp.zeros((C, 128), F32) for _ in range(BACK_LANES // 128)]
    tap_counts(z, value, tiles, ONES)
    pivot = affine[4:5]
    result = tap_product(
        z, kept, hidden[...] - pivot, (h_above[pl.ds(2 * r, r), :] - pivot) * inside(z, 1, True),
        (h_below[pl.ds(0, r), :] - pivot) * inside(z, 1, False), pads,
    )
    tap_sums(result, tiles, HIDDEN)
    kept_packed[...] = jnp.concatenate(tiles, axis=1)
    stores.append(pltpu.make_async_copy(kept_packed, packed, sems.at[6]))
    stores[1].start()
    pixels[own, :] = teacher[...]
    pixels[pl.ds(z.total, 4 * r), :] = jnp.zeros((4 * r, 128), F32)
    n = (REACH + 2) * r
    for side, beyond_of in enumerate((above_of, below_of)):
        for d in (0, 1):
            for k in (0, 1):
                line = beyond_of(pair, other, (pl.ds(n + k * z.images[0], z.images[k]), pl.ds(128 * d, 128)))
                for j in range(z.blocks[k]):
                    at = z.total + (2 * side + d) * r + z.rim[k] + j * z.images[k]
                    pixels[pl.ds(at, z.images[k]), pl.ds(0, BLOCK)] = line[:, j * BLOCK : (j + 1) * BLOCK]
    kept_t[...] = spread(pixels[...], to_channels())
    stores.append(pltpu.make_async_copy(kept_t, teachers, sems.at[3]))
    stores[2].start()
    n = REACH * r
    at = (pl.ds(n, 2 * r), pl.ds(0, LANES))
    up, down = above_of(pair, other, at) * inside(z, 2, True), below_of(pair, other, at) * inside(z, 2, False)
    kept_u[pl.ds(z.total, r), :] = up[r:]
    kept_u[pl.ds(z.total + r, r), :] = down[:r]
    wait_all(loads)
    stores.append(pltpu.make_async_copy(kept_u, near_u, sems.at[5]))
    stores[3].start()
    kept_c[...] = jnp.concatenate(convolve(z, kept_u[own, :], up, down, 2, pads, chains, kept_w), axis=0)
    stores.append(pltpu.make_async_copy(kept_c, spread_u, sems.at[4]))
    stores[4].start()
    wait_all(stores)


def second_operand_kernel(z, hidden, near, stats, affine, out, o_above, o_below, teachers, spread_u, near_u, weights, out_copy, hidden_copy, left, shifts, by_map, by_teacher, up, pads, chains, kept_t, kept_u, kept_w, kept_s, sems):
    r, total = z.rims, z.total
    loads = [
        pltpu.make_async_copy(teachers, kept_t, sems.at[0]),
        pltpu.make_async_copy(weights.at[1], kept_w, sems.at[1]),
        pltpu.make_async_copy(spread_u, kept_u, sems.at[2]),
    ]
    start_all(loads)
    stores = [
        pltpu.make_async_copy(out, out_copy, sems.at[4]),
        pltpu.make_async_copy(hidden, hidden_copy.at[pl.ds(0, total), :], sems.at[7]),
        pltpu.make_async_copy(near.at[0], hidden_copy.at[pl.ds(total, r), :], sems.at[8]),
        pltpu.make_async_copy(near.at[1], hidden_copy.at[pl.ds(total + r, r), :], sems.at[9]),
        pltpu.make_async_copy(near_u, up, sems.at[10]),
    ]
    start_all(stores)
    normed = normed_by(stats)(jnp.concatenate([hidden[...], near[0], near[1]], axis=0))
    shifted = normed * affine[2:3] + affine[3:4]
    turned_operand(z, gelu(shifted[:total]), pads, left)
    ones = jnp.ones((total, 1), F32)
    masks = jnp.concatenate([ones, inside(z, 1, True), inside(z, 1, False)], axis=0)
    slopes = gelu_slope(shifted) * masks
    o = jnp.concatenate([out[...], o_above[...] * inside(z, 2, True), o_below[...] * inside(z, 2, False)], axis=0)
    for_map = spread(attention(o), to_channels()) * o
    wait_all(loads)
    for_teacher = kept_t[...] * o
    kept_s[0] = kept_u[...] * slopes
    stores += copies_of(pieces(kept_s, shifts), sems, 11)
    stores[-3].start()
    for n, value, ref in ((1, for_map, by_map), (2, for_teacher, by_teacher)):
        own, before, after = value[:total], value[total : total + 2 * r], value[total + 2 * r :]
        ref[...] = jnp.concatenate([own, before[r:], after[:r]], axis=0)
        kept_s[n] = jnp.concatenate(convolve(z, own, before, after, 2, pads, chains, kept_w), axis=0) * slopes
        stores[n - 3].start()
    wait_all(stores)


def upstream_kernel(z, gathered, up, shifts, left_1, left_2, packed, by_map, by_teacher, hidden, stats, dout, dshift, d_above, d_below, slabs, kept_s, kept_left, kept_h, kept_packed, pads, more_pads, sems):
    r, total = z.rims, z.total
    loads = copies_of(
        pieces(shifts, kept_s) + pieces(left_1, kept_left) + [(hidden.at[pl.ds(0, total), :], kept_h), (packed, kept_packed)], sems
    )
    start_all(loads)
    lane = lax.broadcasted_iota(jnp.int32, (z.slots, 128), 1)
    sums = sum(gathered[pl.ds(n * z.slots, z.slots), :] for n in range(z.peers))
    square = jnp.sum(jnp.where(lane < 64, sums, 0.0), axis=1, keepdims=True)
    cross = jnp.sum(jnp.where(lane < 64, 0.0, sums), axis=1, keepdims=True)
    inverse = lax.rsqrt(square + map_eps)
    inner = beta_weight * (square * inverse - cross) * inverse
    shape = (z.slots, 128)
    for_map = (beta_weight - inner) * inverse * inverse * (2.0 / C)
    for_teacher = beta_weight * inverse * (2.0 / C)
    for_map, for_teacher = (wide(image_rows(z, jnp.broadcast_to(v, shape), 2)) for v in (for_map, for_teacher))
    value = up[...] + for_map * by_map[...] - for_teacher * by_teacher[...]
    dout[...] = value[:total]
    wait_all(loads[:3])
    shift = kept_s[0] + for_map * kept_s[1] - for_teacher * kept_s[2]
    pre, above, below = shift[:total], shift[total : total + r], shift[total + r :]
    dshift[...] = pre
    d_above[...] = above
    d_below[...] = below
    second = tap_product(z, left_2, value[:total], value[total : total + r], value[total + r :], pads)
    wait_all(loads[3:5])
    first = tap_product(z, kept_left, pre, above, below, more_pads)
    wait_all(loads[5:])
    normed = normed_by(stats)(kept_h[...])
    tiles = [kept_packed[:, 128 * n : 128 * n + 128] for n in range(BACK_LANES // 128)]
    group = group_of()
    tiles[0] = jnp.where(group == BIAS, fold(column_sum(pre)), jnp.where(group == GAIN, fold(column_sum(pre * normed)), tiles[0]))
    tap_sums(second, tiles, SECOND)
    tap_sums(first, tiles, LEFT)
    line = jnp.concatenate(tiles, axis=1)
    for d in range(z.devices):
        slabs[d] = line[d % C : d % C + 1]


def write_kernel(z, out, x, hidden, weights, first_stats, stats, order, out_s, out_l, first_normed, normed, weight, kept, kept_x, kept_h, half, sems):
    loads = [pltpu.make_async_copy(a, b, sems.at[n]) for n, (a, b) in enumerate(((out, kept), (x, kept_x), (hidden, kept_h), (weights.at[0], weight)))]
    start_all(loads)
    loads[0].wait()
    put_halves(half, kept[...])
    from_matrix(z, half, (out_s, out_l))
    loads[1].wait()
    first_normed[...] = normed_by(first_stats)(kept_x[...])
    loads[2].wait()
    normed[...] = normed_by(stats)(kept_h[...])
    loads[3].wait()


def norm_sums(total):
    group = group_of()
    return [wide(spread_groups(jnp.where(group == n, total[:, :128], 0.0))) for n in (BIAS, GAIN)]


def hidden_kernel(z, gathered, dshift, d_above, d_below, second_normed, stats, affine, weight, first_normed, pre_ref, gain_out, bias_out, slabs, pads):
    total = jnp.sum(gathered[...], axis=0)
    bias_sum, gain_sum = norm_sums(total)
    bias_out[...] = bias_sum[:, :C]
    gain_out[...] = gain_sum[:, :C]
    bias_mean, gain_mean = bias_sum / z.pixels, gain_sum / z.pixels
    factor = affine[2:3] * stats[1:2]
    r, total_rows = z.rims, z.total

    def back(d, normed):
        return factor * (d - bias_mean - normed * gain_mean)

    own = back(dshift[...], second_normed[pl.ds(0, total_rows), :])
    up = back(d_above[...], second_normed[pl.ds(total_rows, r), :]) * inside(z, 1, True)
    down = back(d_below[...], second_normed[pl.ds(total_rows + r, r), :]) * inside(z, 1, False)
    grad, _, _ = convolve(z, own, up, down, 1, pads, None, weight)
    normed = first_normed[...]
    pre = grad * gelu_slope(normed * affine[0:1] + affine[1:2])
    pre_ref[...] = pre
    lane = lax.broadcasted_iota(jnp.int32, (1, 128), 1)
    taps = TAPS * TAPS * C

    def along(row):
        return jnp.concatenate([row[:, :128]] * 3, axis=1)[:, :taps]

    second, left, against, ones = (total[:, n * C : n * C + taps] for n in (SECOND, LEFT, HIDDEN, ONES))
    against = along(stats[1:2]) * (against - along(stats[0:1] - affine[4:5]) * ones)
    first = along(factor) * (left - along(bias_mean) * ones - along(gain_mean) * against)
    sums = jnp.where(lane < C, fold(column_sum(pre)), fold(column_sum(pre * normed)))
    line = jnp.concatenate([sums[:, : 2 * C], second, first], axis=1)
    slabs[...] = jnp.broadcast_to(line[None], slabs.shape)


def back_kernel(z, gathered, pre, normed, stats, affine, dout, back_s, back_l, one, two, gain_out, bias_out, half, lines):
    bias_sum, gain_sum = norm_sums(jnp.sum(gathered[:, :, pl.ds(0, 128)], axis=0))
    bias_out[...] = bias_sum[:, :C]
    gain_out[...] = gain_sum[:, :C]
    value = dout[...] + affine[0:1] * stats[1:2] * (pre[...] - bias_sum / z.pixels - normed[...] * (gain_sum / z.pixels))
    put_halves(half, value)
    from_matrix(z, half, (back_s, back_l))
    for d in range(C):
        lines[pl.ds(d, 1), :] = gathered[d]
    for ref, group in ((two, LAST_SECOND), (one, LAST_FIRST)):
        for a in range(TAPS):
            for b in range(TAPS):
                at = (group + a * TAPS + b) * C
                ref[a, b] = lines[:, pl.ds(at, C)]


def call(body, ins, outs, scratch=(), sems=0):
    space = {"v": pltpu.VMEM, "h": pltpu.HBM, "V": pltpu.VMEM}
    shapes = []
    for item in scratch:
        if isinstance(item, list):
            shapes.append([pltpu.VMEM(*s) for s in item])
        else:
            shapes.append(pltpu.VMEM(*item))
    if sems:
        shapes.append(pltpu.SemaphoreType.DMA((sems,)))
    run = pl.pallas_call(
        body,
        out_shape=[jax.ShapeDtypeStruct(shape, kind) if s == "v" else space[s](shape, kind) for s, shape, kind in outs],
        in_specs=[pl.BlockSpec(memory_space=space[s]) for s in ins],
        out_specs=[pl.BlockSpec(memory_space=space[s]) for s, _, _ in outs],
        scratch_shapes=shapes,
        compiler_params=pltpu.CompilerParams(vmem_limit_bytes=VMEM_LIMIT),
    )
    return lambda *args: run(
        *(pltpu.with_memory_space_constraint(arg, pltpu.HBM) if s == "h" else arg for s, arg in zip(ins, args))
    )


def exchange(lines, axes):
    shape = lines.shape
    if len(shape) == 2:
        lines = lines.reshape(math.prod(lax.axis_size(axis) for axis in axes), -1, 128)
    return lax.all_to_all(lines, axes, 0, 0, tiled=True).reshape(shape)


def beyond(z, pair, other, depths):
    hops = max(-(-depth // rows) for rows in z.rows for depth in depths)
    if hops == 1:
        swap = lambda value, start: lax.ppermute(
            value, "row", [(i + a, i + 1 - a) for i in range(start, z.peers - 1, 2) for a in (0, 1)]
        )
        others = swap(other, 1)
        return swap(pair, 0), others
    even = is_even()
    bottom, top = jnp.where(even, pair, other), jnp.where(even, other, pair)
    above, below = [], []
    for hop in range(1, hops + 1):
        above.append(lax.ppermute(bottom, "row", [(i, i + hop) for i in range(z.peers - hop)]))
        below.append(lax.ppermute(top, "row", [(i + hop, i) for i in range(z.peers - hop)]))
    up, down = [], []
    base = 0
    for depth in depths:
        for n in range(depth):
            for k in (1, 0):
                hop, back = divmod(depth - 1 - n, z.rows[k])
                at = base + (depth - 1 - back) * z.rims + z.rim[k]
                up.append(above[hop][at : at + z.edge[k]])
                hop, back = divmod(n, z.rows[k])
                at = base + back * z.rims + z.rim[k]
                down.append(below[hop][at : at + z.edge[k]])
        base += depth * z.rims
    up.append(jnp.concatenate([pixel_rows(z, above, base, 1, 1), pixel_rows(z, above, base, 0, 1)], axis=1))
    down.append(jnp.concatenate([pixel_rows(z, below, base, 0, 0), pixel_rows(z, below, base, 1, 0)], axis=1))
    up, down = jnp.concatenate(up, axis=0), jnp.concatenate(down, axis=0)
    return jnp.where(even, down, up), jnp.where(even, up, down)


def pixel_rows(z, bands, base, distance, last):
    lines = []
    for k in (0, 1):
        hop, back = divmod(distance, z.rows[k])
        at = base + k * z.images[0]
        half = 128 * abs(last - back)
        lines.append(bands[hop][at : at + z.images[k], half : half + 128])
    lines.append(jnp.zeros((z.slots - sum(z.images), 128), F32))
    return jnp.concatenate(lines, axis=0)


def local(
    image_small, image_large, teacher_small, teacher_large, upstream_small, upstream_large,
    conv_first, gain_first, bias_first, conv_second, gain_second, bias_second,
):
    peers = lax.axis_size("row")
    devices = lax.axis_size("img") * peers
    z = Sizes(image_small.shape, image_large.shape, devices, peers)
    body = lambda function: functools.partial(function, z)
    r = z.rims
    full, half, pair = (z.total, LANES), (2, z.total, 128), (2 * devices, 128)
    weight, left = (2, TAPS * TAP_ROWS, 128), (2, 256, 2 * z.total)
    images = [image_small, image_large, upstream_small, upstream_large, teacher_small, teacher_large]
    f = lambda space, *shape: (space, shape, F32)
    depths = (REACH, 2)
    rim_rows = sum(depths) * r + z.slots

    x, pair_edge, other_edge, copies = call(
        body(start_kernel),
        "hhhhhh",
        [("v", full, F32), f("v", rim_rows, LANES), f("v", rim_rows, LANES), ("V", pair, F32)],
        [[(a.shape, F32) for a in images], (half, F32)],
        4 + 2 * z.images[1],
    )(*images)
    gathered = exchange(copies, AXES)
    pair_rims, other_rims = beyond(z, pair_edge, other_edge, depths)
    params = [conv_first, conv_second] + images[2:]
    w1, w2, weights, affine, upstream, teacher, x_copy = call(
        body(prepare_kernel),
        "hhhhhhhhhhv",
        [("v", weight, BF16), ("v", weight, BF16), ("h", (2,) + weight, BF16), f("v", 5, LANES), ("h", full, F32), f("v", z.total, 128), ("h", full, F32)],
        [[(a.shape, F32) for a in params], ((2,) + weight, BF16), (full, F32), ((4, C), F32), (half, F32)],
        14,
    )(*params, *(v.reshape(1, C) for v in (gain_first, bias_first, gain_second, bias_second)), x)

    hidden, h_above, h_below, stats_one, copies = call(
        body(first_kernel),
        "vvvvvv",
        [("v", full, F32), f("v", 3 * r, LANES), f("v", 3 * r, LANES), f("v", 2, LANES), ("V", pair, F32)],
        [z.pads(), z.chains(4)],
    )(x, pair_rims, other_rims, gathered, affine, w1)
    gathered = exchange(copies, AXES)
    extended, near_rows = z.total + 4 * r, z.total + 2 * r
    left_one, packed, teachers, spread_u, near_u = call(
        body(first_operand_kernel),
        "vvvvvvvvvhh",
        [("h", left, BF16), f("h", C, BACK_LANES), f("h", extended, LANES), f("h", near_rows, LANES), f("h", near_rows, LANES)],
        [
            z.pads(), z.chains(2), (left, BF16), (weight, BF16), ((near_rows, LANES), F32), ((extended, 128), F32),
            ((extended, LANES), F32), ((near_rows, LANES), F32), ((C, BACK_LANES), F32),
        ],
        7,
    )(x, hidden, h_above, h_below, pair_rims, other_rims, stats_one, affine, teacher, upstream, weights)
    gathered, near_u = lax.optimization_barrier((gathered, near_u))

    map_shape = (peers * z.slots, 128)
    out, o_above, o_below, near, stats_two, copies = call(
        body(second_kernel),
        "vvvvvvvvvv",
        [("v", full, F32), f("v", 2 * r, LANES), f("v", 2 * r, LANES), f("v", 2, r, LANES), f("v", 2, LANES), ("V", map_shape, F32)],
        [z.pads(), z.chains(3)],
    )(hidden, h_above, h_below, gathered, affine, w2, x, pair_rims, other_rims, teacher)
    gathered = exchange(copies, ("row",))
    out_copy, hidden_copy, left_two, shifts, by_map, by_teacher, up = call(
        body(second_operand_kernel),
        "vvvvvvvhhhh",
        [
            ("h", full, F32), f("h", near_rows, LANES), ("v", left, BF16), f("h", 3, near_rows, LANES),
            f("v", near_rows, LANES), f("v", near_rows, LANES), f("v", near_rows, LANES),
        ],
        [
            z.pads(), z.chains(2), ((extended, LANES), F32), ((near_rows, LANES), F32), (weight, BF16),
            ((3, near_rows, LANES), F32),
        ],
        14,
    )(hidden, near, stats_two, affine, out, o_above, o_below, teachers, spread_u, near_u, weights)

    dout, dshift, d_above, d_below, slabs = call(
        body(upstream_kernel),
        "vvhhvhvvhv",
        [("v", full, F32), ("v", full, F32), f("v", r, LANES), f("v", r, LANES), f("V", devices, 1, BACK_LANES)],
        [((3, near_rows, LANES), F32), (left, BF16), (full, F32), ((C, BACK_LANES), F32), z.pads(), z.pads()],
        7,
    )(gathered, up, shifts, left_one, left_two, packed, by_map, by_teacher, hidden_copy, stats_two)
    gathered = exchange(slabs, AXES)
    out_s, out_l, first_normed, second_normed, weight_back = call(
        body(write_kernel),
        "hhhhvvv",
        [("v", image_small.shape, F32), ("v", image_large.shape, F32), ("v", full, F32), f("v", near_rows, LANES), ("v", weight, BF16)],
        [(full, F32), (full, F32), ((near_rows, LANES), F32), (half, F32)],
        4,
    )(out_copy, x_copy, hidden_copy, weights, stats_one, stats_two, d_above)

    pre, gain_two, bias_two, slabs = call(
        body(hidden_kernel),
        "vvvvvvvvv",
        [("v", full, F32), f("v", 1, C), f("v", 1, C), f("V", devices, 1, LAST_LANES)],
        [z.pads()],
    )(gathered, dshift, d_above, d_below, second_normed, stats_two, affine, weight_back, first_normed)
    gathered = exchange(slabs, AXES)

    back_s, back_l, one, two, gain_one, bias_one = call(
        body(back_kernel),
        "vvvvvv",
        [("v", a.shape, F32) for a in (image_small, image_large, conv_first, conv_second)] + [f("v", 1, C), f("v", 1, C)],
        [(half, F32), ((C, LAST_LANES), F32)],
    )(gathered, pre, first_normed, stats_one, affine, dout)
    return (
        out_s, out_l, back_s, back_l,
        one, gain_one.reshape(C), bias_one.reshape(C),
        two, gain_two.reshape(C), bias_two.reshape(C),
    )


def solution(mesh):
    split_bands, everywhere = P("img", "row", None), P()
    return jax.shard_map(
        local,
        mesh=mesh,
        in_specs=(split_bands,) * 6 + (everywhere,) * 6,
        out_specs=(split_bands,) * 4 + (everywhere,) * 6,
        check_vma=False,
    )
```

```python
import functools
import math

import jax
import jax.numpy as jnp
from jax import lax
from jax.experimental import pallas as pl
from jax.experimental.pallas import tpu as pltpu
from jax.sharding import PartitionSpec as P

C = 32
HS = 32
HL = 64
HEIGHTS = (HS, HL)

norm_eps = 1e-05
map_eps = 1e-06
beta_weight = 1000.0
AXES = ("img", "row")
BLOCK = 8
LANES = BLOCK * C
TAPS = 3
DEPTH = TAPS * 128 + 256
TAP_ROWS = 128 + 2 * C
REACH = 4
ROOT = math.sqrt(2.0 / math.pi)
CUBE = 0.044715
F32 = jnp.float32
BF16 = jnp.bfloat16
VMEM_LIMIT = 32 * 1024 * 1024
BIAS, GAIN, SECOND, LEFT, HIDDEN, ONES = 0, 1, 2, 11, 20, 29
BACK_LANES = 1280
LAST_SECOND, LAST_FIRST, LAST_LANES = 2, 11, 640


class Sizes:
    def __init__(self, small, large, devices, peers):
        self.images = (small[0], large[0])
        self.rows = (small[1], large[1])
        self.blocks = (HS // BLOCK, HL // BLOCK)
        self.step = tuple(n * r for n, r in zip(self.images, self.rows))
        self.count = tuple(b * s for b, s in zip(self.blocks, self.step))
        self.edge = tuple(b * n for b, n in zip(self.blocks, self.images))
        self.start = (self.count[1], 0)
        self.rim = (self.edge[1], 0)
        self.total = sum(self.count)
        self.rims = sum(self.edge)
        self.slots = -(-sum(self.images) // 8) * 8
        self.guard = -(-max(self.images) // 8) * 8
        self.devices = devices
        self.peers = peers
        self.here = float(self.total * BLOCK)
        self.pixels = self.here * devices

    def pads(self):
        return [((TAPS, 2, self.count[k] + 2 * self.step[k], 128), F32) for k in (0, 1)]

    def chains(self, depth):
        return [((2, 2 * self.guard + (depth + 1) * self.rims, 128), F32)] * 2


def split(value):
    high = value.astype(BF16)
    return high, (value - high.astype(F32)).astype(BF16)


def dot(left, right):
    return lax.dot_general(left, right, (((1,), (0,)), ((), ())), preferred_element_type=F32)


def product(left, right):
    if left[0].shape[1] % 128:
        return dot(left[0], right[0]) + (dot(left[0], right[1]) + dot(left[1], right[0]))
    return dot(
        jnp.concatenate([left[0], left[0], left[1]], axis=1), jnp.concatenate([right[0], right[1], right[0]], axis=0)
    )


def spread(left, right):
    right = right.astype(BF16)
    return dot(jnp.concatenate(split(left), axis=1), jnp.concatenate([right, right], axis=0))


def gelu(s):
    return 0.5 * s * (1.0 + jnp.tanh(ROOT * (s + CUBE * s * s * s)))


def gelu_slope(s):
    square = s * s
    t = jnp.tanh(ROOT * s * (1.0 + CUBE * square))
    return 0.5 * (1.0 + t) + 0.5 * s * (1.0 - t * t) * ROOT * (1.0 + 3.0 * CUBE * square)


def spread_groups(row):
    row = row + pltpu.roll(row, 64, 1)
    return row + pltpu.roll(row, 32, 1)


def fold(row):
    return spread_groups(row[:, :128] + row[:, 128:])


def wide(row):
    return jnp.concatenate([row, row], axis=1)


def group_of(rows=1, lanes=128):
    return lax.broadcasted_iota(jnp.int32, (rows, lanes), 1) // C


def column_sum(value):
    return jnp.sum(value, axis=0, keepdims=True)


def send_lines(z, ref, lines):
    for n, line in enumerate(lines):
        ref[pl.ds(n, z.devices, stride=len(lines)), :] = jnp.broadcast_to(line, (z.devices, 128))


def moments(z, value, ref):
    few = min(8, z.total)
    pivot = fold(column_sum(value[:few])) / float(few * BLOCK)
    off = value - wide(pivot)
    first, second = fold(column_sum(off)), fold(column_sum(off * off))
    send_lines(z, ref, [pivot + first / z.here, second - first * first / z.here])


def merged(z, ref):
    means = ref[pl.ds(0, z.devices, stride=2), :]
    center = jnp.mean(means, axis=0, keepdims=True)
    off = means - center
    within = jnp.mean(ref[pl.ds(1, z.devices, stride=2), :], axis=0, keepdims=True)
    variance = within / z.here + jnp.mean(off * off, axis=0, keepdims=True)
    return wide(center), wide(lax.rsqrt(variance + norm_eps))


def put_halves(ref, value):
    ref[0] = value[:, :128]
    ref[1] = value[:, 128:]


def whole(ref):
    return jnp.concatenate([ref[0], ref[1]], axis=1)


def to_matrix(z, refs, half):
    for k in (0, 1):
        for j in range(z.blocks[k]):
            at = z.start[k] + j * z.step[k]
            for i in range(z.images[k]):
                for h in (0, 1):
                    half[h, pl.ds(at + i * z.rows[k], z.rows[k]), :] = refs[k][i, :, pl.ds(LANES * j + 128 * h, 128)]


def from_matrix(z, half, refs):
    for k in (0, 1):
        for j in range(z.blocks[k]):
            at = z.start[k] + j * z.step[k]
            for i in range(z.images[k]):
                for h in (0, 1):
                    refs[k][i, :, pl.ds(LANES * j + 128 * h, 128)] = half[h, pl.ds(at + i * z.rows[k], z.rows[k]), :]


def is_even():
    return lax.axis_index("row") % 2 == 0


def put_edges(pair, other, at, last, first):
    even = is_even()
    pair[at] = jnp.where(even, last, first)
    other[at] = jnp.where(even, first, last)


def above_of(pair, other, at):
    return jnp.where(is_even(), other[at], pair[at])


def below_of(pair, other, at):
    return jnp.where(is_even(), pair[at], other[at])


def take_rims(z, half, depth, pair, other):
    everything = pl.ds(0, 128)
    for k in (0, 1):
        nothing = jnp.zeros((z.edge[k], 128), F32)
        for n in range(depth):
            first, last = nothing, nothing
            if depth - n <= z.rows[k]:
                last = half[pl.ds(z.start[k] + z.rows[k] - depth + n, z.edge[k], stride=z.rows[k]), :]
            if n < z.rows[k]:
                first = half[pl.ds(z.start[k] + n, z.edge[k], stride=z.rows[k]), :]
            put_edges(pair, other, (pl.ds(n * z.rims + z.rim[k], z.edge[k]), everything), last, first)


def inside(z, depth, above):
    at = lax.axis_index("row")
    large = lax.broadcasted_iota(jnp.int32, (z.rims, 1), 0) < z.rim[0]
    parts = []
    for n in range(depth):
        if above:
            ok = [jnp.where(at * rows >= depth - n, 1.0, 0.0) for rows in z.rows]
        else:
            ok = [jnp.where((at + 1) * rows + n + 1 <= height, 1.0, 0.0) for rows, height in zip(z.rows, HEIGHTS)]
        parts.append(jnp.where(large, ok[1], ok[0]).astype(F32))
    return jnp.concatenate(parts, axis=0)


def clear_guards(z, pads, a):
    for k in (0, 1):
        pads[k][a, 1, pl.ds(0, z.step[k]), :] = jnp.zeros((z.step[k], 128), F32)
        pads[k][a, 0, pl.ds(z.step[k] + z.count[k], z.step[k]), :] = jnp.zeros((z.step[k], 128), F32)


def fill_center(z, pads, value):
    clear_guards(z, pads, 1)
    for k in (0, 1):
        for h in (0, 1):
            pads[k][1, h, pl.ds(z.step[k], z.count[k]), :] = value[z.start[k] : z.start[k] + z.count[k], 128 * h : 128 * h + 128]


def fill_shifted(z, pads, above, below):
    for k in (0, 1):
        ref, step, count, rows = pads[k], z.step[k], z.count[k], z.rows[k]
        rim = slice(z.rim[k], z.rim[k] + z.edge[k])
        for h in (0, 1):
            lanes = slice(128 * h, 128 * h + 128)
            ref[0, h, pl.ds(step, count), :] = ref[1, h, pl.ds(step - 1, count), :]
            ref[2, h, pl.ds(step, count), :] = ref[1, h, pl.ds(step + 1, count), :]
            ref[0, h, pl.ds(step, z.edge[k], stride=rows), :] = above[rim, lanes]
            ref[2, h, pl.ds(step + rows - 1, z.edge[k], stride=rows), :] = below[rim, lanes]


def fill_pads(z, pads, value, above, below):
    fill_center(z, pads, value)
    fill_shifted(z, pads, above, below)
    for a in (0, 2):
        clear_guards(z, pads, a)


def beside(left, right):
    lane = lax.broadcasted_iota(jnp.int32, (1, 128), 1)
    middle = pltpu.roll(jnp.where(lane >= 64, left[1], right[1]), 64, 1)
    return [
        jnp.where(lane >= 96, left[0], jnp.where(lane < 32, right[0], middle)),
        jnp.where(lane >= 96, left[2], jnp.where(lane < 32, right[2], 0.0)),
    ]


def band_operand(z, pads):
    parts = ([], [])
    for k in (1, 0):
        ref, step, count = pads[k], z.step[k], z.count[k]
        low, high = ([ref[a, h, pl.ds(step, count), :] for a in range(TAPS)] for h in (0, 1))
        before = [ref[a, 1, pl.ds(0, count), :] for a in range(TAPS)]
        after = [ref[a, 0, pl.ds(2 * step, count), :] for a in range(TAPS)]
        parts[0].append(jnp.concatenate(low + beside(before, high), axis=1))
        parts[1].append(jnp.concatenate(high + beside(low, after), axis=1))
    return [jnp.concatenate(part, axis=0) for part in parts]


def rim_operand(z, chain, depth):
    m = lax.broadcasted_iota(jnp.int32, (z.rims, 1), 0)
    large = m < z.rim[0]
    has_before = jnp.where(large, m, m - z.rim[0]) >= jnp.where(large, z.images[1], z.images[0])
    has_after = m < jnp.where(large, z.rim[0] - z.images[1], z.rims - z.images[0])
    low, high, before, after = [], [], [], []
    for r in range(depth + 1):
        at = z.guard + r * z.rims
        low.append(chain[0, pl.ds(at, z.rims), :])
        high.append(chain[1, pl.ds(at, z.rims), :])
        shifted = [chain[1, pl.ds(at - images, z.rims), :] for images in z.images]
        before.append(jnp.where(has_before, jnp.where(large, shifted[1], shifted[0]), 0.0))
        shifted = [chain[0, pl.ds(at + images, z.rims), :] for images in z.images]
        after.append(jnp.where(has_after, jnp.where(large, shifted[1], shifted[0]), 0.0))
    parts = ([], [])
    for n in range(depth - 1):
        rows = slice(n, n + TAPS)
        parts[0].append(jnp.concatenate(low[rows] + beside(before[rows], high[rows]), axis=1))
        parts[1].append(jnp.concatenate(high[rows] + beside(low[rows], after[rows]), axis=1))
    return [jnp.concatenate(part, axis=0) for part in parts]


def times(parts, weight):
    left = jnp.concatenate([part[h] for h in (0, 1) for part in parts], axis=0)
    both = jnp.concatenate([weight_matrix(weight.at[0]), weight_matrix(weight.at[1])], axis=1)
    result = dot(jnp.concatenate(split(left), axis=1), jnp.concatenate([both, both], axis=0))
    result = result[:, :128] + result[:, 128:]
    rows = result.shape[0] // 2
    return jnp.concatenate([result[:rows], result[rows:]], axis=1)


def convolve(z, own, above, below, depth, pads, chains, weight):
    r = z.rims
    fill_pads(z, pads, own, above[(depth - 1) * r :], below[:r])
    parts = [band_operand(z, pads)]
    if depth > 1:
        for side, (rim, chain) in enumerate(zip((above, below), chains)):
            rim_at, own_at = (z.guard, z.guard + depth * r) if side == 0 else (z.guard + r, z.guard)
            for h in (0, 1):
                chain[h, pl.ds(rim_at, depth * r), :] = rim[:, 128 * h : 128 * h + 128]
                for k in (0, 1):
                    row = z.step[k] + (0 if side == 0 else z.rows[k] - 1)
                    chain[h, pl.ds(own_at + z.rim[k], z.edge[k]), :] = pads[k][1, h, pl.ds(row, z.edge[k], stride=z.rows[k]), :]
            parts.append(rim_operand(z, chain, depth))
    result = times(parts, weight)
    n = z.total + (depth - 1) * r
    return result[: z.total], result[z.total : n], result[n:]


def image_sums(z, value):
    slot = lax.broadcasted_iota(jnp.int32, (z.slots, 1), 0)
    sums = jnp.zeros((z.slots, 128), F32)
    for k in (0, 1):
        line = value[z.start[k] : z.start[k] + z.step[k]]
        for j in range(1, z.blocks[k]):
            at = z.start[k] + j * z.step[k]
            line = line + value[at : at + z.step[k]]
        image = lax.broadcasted_iota(jnp.int32, (z.step[k], 1), 0) // z.rows[k]
        for i in range(z.images[k]):
            sums = jnp.where(slot == i + k * z.images[0], column_sum(jnp.where(image == i, line, 0.0)), sums)
    return sums


def image_rows(z, values, rims):
    parts = []
    for k in (1, 0):
        image = lax.broadcasted_iota(jnp.int32, (z.step[k], 1), 0) // z.rows[k]
        line = jnp.zeros((z.step[k], 128), F32)
        for i in range(z.images[k]):
            at = i + k * z.images[0]
            line = jnp.where(image == i, values[at : at + 1], line)
        parts += [line] * z.blocks[k]
    if rims:
        m = lax.broadcasted_iota(jnp.int32, (z.rims, 1), 0)
        image = jnp.where(m < z.rim[0], z.images[0] + m % z.images[1], (m - z.rim[0]) % z.images[0])
        line = jnp.zeros((z.rims, 128), F32)
        for at in range(sum(z.images)):
            line = jnp.where(image == at, values[at : at + 1], line)
        parts += [line] * rims
    return jnp.concatenate(parts, axis=0)


def channel_mean():
    a = lax.broadcasted_iota(jnp.int32, (LANES, 128), 0) // C
    b = lax.broadcasted_iota(jnp.int32, (LANES, 128), 1) % 64
    return jnp.where(a == b, 1.0 / C, 0.0).astype(F32)


def to_channels():
    a = lax.broadcasted_iota(jnp.int32, (128, LANES), 0)
    b = lax.broadcasted_iota(jnp.int32, (128, LANES), 1) // C
    return jnp.where(a == b, 1.0, 0.0).astype(F32)


def attention(value):
    return spread(value * value, channel_mean())


def pieces(source, target):
    return [(source.at[n], target.at[n]) for n in range(source.shape[0])]


def copies_of(pairs, sems, first=0):
    return [pltpu.make_async_copy(a, b, sems.at[first + n]) for n, (a, b) in enumerate(pairs)]


def start_all(copies):
    for copy in copies:
        copy.start()


def wait_all(copies):
    for copy in copies:
        copy.wait()


def start_kernel(z, small, large, up_s, up_l, t_s, t_l, x, pair, other, copies, raw, half, sems):
    images = [(small, raw[0])] + pieces(large, raw[1])
    rest = [(up_s, raw[2])] + pieces(up_l, raw[3]) + [(t_s, raw[4]), (t_l, raw[5])]
    loads = copies_of(images + rest, sems)
    start_all(loads)
    r, n = z.rims, REACH * z.rims
    tail = n + 2 * r
    for ref in (pair, other):
        ref[pl.ds(tail, z.slots), :] = jnp.zeros((z.slots, LANES), F32)
    wait_all(loads[: len(images)])
    to_matrix(z, raw[:2], half)
    value = whole(half)
    x[...] = value
    moments(z, value, copies)
    for h in (0, 1):
        lanes = pl.ds(128 * h, 128)
        take_rims(z, half.at[h], REACH, pair.at[pl.ds(0, n), lanes], other.at[pl.ds(0, n), lanes])
    wait_all(loads[len(images) :])
    for k in (0, 1):
        width, rows = HEIGHTS[k], z.rows[k]
        for i in range(z.images[k]):
            slot = pl.ds(tail + i + k * z.images[0], 1)
            for d in (0, 1):
                has_last, has_first = rows + d >= 2, d < rows
                last, first = pl.ds(max(rows - 2 + d, 0), 1), pl.ds(min(d, rows - 1), 1)
                for j in range(z.blocks[k]):
                    lanes = pl.ds(LANES * j, LANES)
                    at = (pl.ds(n + d * r + z.rim[k] + j * z.images[k] + i, 1), pl.ds(0, LANES))
                    nothing = jnp.zeros((1, LANES), F32)
                    put_edges(
                        pair, other, at,
                        raw[2 + k][i, last, lanes] if has_last else nothing,
                        raw[2 + k][i, first, lanes] if has_first else nothing,
                    )
                nothing = jnp.zeros((1, width), F32)
                put_edges(
                    pair, other, (slot, pl.ds(128 * d, width)),
                    raw[4 + k][i, last, :] if has_last else nothing,
                    raw[4 + k][i, first, :] if has_first else nothing,
                )


def banded(taps, ref):
    row = lax.broadcasted_iota(jnp.int32, (128, 128), 0) // C
    lane = group_of(128)
    for a in range(TAPS):
        main = jnp.zeros((128, 128), F32)
        for b in range(TAPS):
            main = jnp.where(row - lane + 1 == b, taps[a][b], main)
        before = jnp.where(lane[:C] == 0, taps[a][0][:C], 0.0)
        after = jnp.where(lane[:C] == 3, taps[a][2][:C], 0.0)
        for n, part in enumerate(split(jnp.concatenate([main, before, after], axis=0))):
            ref[n, pl.ds(a * TAP_ROWS, TAP_ROWS), :] = part


def weight_matrix(ref):
    main = [ref[pl.ds(a * TAP_ROWS, 128), :] for a in range(TAPS)]
    before, after = ([ref[pl.ds(a * TAP_ROWS + 128 + n * C, C), :] for a in range(TAPS)] for n in (0, 1))
    return jnp.concatenate(
        main + [after[0], before[1], after[1], before[0], after[2], jnp.zeros((2 * C, 128), BF16), before[2]], axis=0
    )


def prepare_kernel(z, first, second, up_s, up_l, t_s, t_l, g1, b1, g2, b2, x, w1, w2, weights, affine, upstream, teacher, x_copy, raw, kept, kept_u, rows, half, sems):
    targets = tuple(raw) + tuple(rows.at[pl.ds(n, 1), :] for n in range(4))
    refs = (first, second, up_s, up_l, t_s, t_l, g1, b1, g2, b2)
    loads = [pltpu.make_async_copy(a, b, sems.at[n]) for n, (a, b) in enumerate(zip(refs, targets))]
    start_all(loads)
    stores = [pltpu.make_async_copy(x, x_copy, sems.at[13])]
    stores[0].start()
    wait_all(loads)
    to_matrix(z, raw[2:4], half)
    kept_u[...] = whole(half)
    stores.append(pltpu.make_async_copy(kept_u, upstream, sems.at[10]))
    stores[1].start()
    for n, (source, forward) in enumerate(zip(raw[:2], (w1, w2))):
        tiles = []
        for a in range(TAPS):
            line = [jnp.concatenate([source[a, b]] * 4, axis=1) for b in range(TAPS)]
            tiles.append([jnp.concatenate([tap] * 4, axis=0) for tap in line])
        turned = [[tiles[TAPS - 1 - a][TAPS - 1 - b].T for b in range(TAPS)] for a in range(TAPS)]
        banded(tiles, forward)
        banded(turned, kept.at[n])
        stores.append(pltpu.make_async_copy(kept.at[n], weights.at[n], sems.at[11 + n]))
        stores[-1].start()
    taps = sum(raw[0][a, b] for a in range(TAPS) for b in range(TAPS))
    pivot = dot(jnp.broadcast_to(gelu(rows[1:2]), (8, C)), taps)[0:1]
    affine[...] = jnp.concatenate([jnp.concatenate([rows[...], pivot], axis=0)] * BLOCK, axis=1)
    teacher[...] = jnp.zeros(teacher.shape, F32)
    for k, ref in ((0, raw[4]), (1, raw[5])):
        for i in range(z.images[k]):
            line = ref[i]
            for j in range(z.blocks[k]):
                at = z.start[k] + j * z.step[k] + i * z.rows[k]
                for lane in (0, 64):
                    teacher[pl.ds(at, z.rows[k]), pl.ds(lane, BLOCK)] = line[:, j * BLOCK : (j + 1) * BLOCK]
    wait_all(stores)


def normed_by(stats):
    return lambda v: (v - stats[0:1]) * stats[1:2]


def activation(center, scale, gain, bias):
    factor = scale * gain
    offset = bias - center * factor
    return lambda v: gelu(v * factor + offset)


def first_kernel(z, x, other, pair, gathered, affine, weight, hidden, h_above, h_below, stats, copies, pads, chains):
    n = REACH * z.rims
    center, scale = merged(z, gathered)
    act = activation(center, scale, affine[0:1], affine[1:2])
    own = act(x[...])
    at = (pl.ds(0, n), pl.ds(0, LANES))
    up, down = act(above_of(pair, other, at)) * inside(z, 4, True), act(below_of(pair, other, at)) * inside(z, 4, False)
    own, up, down = convolve(z, own, up, down, 4, pads, chains, weight)
    moments(z, own, copies)
    hidden[...] = own
    h_above[...] = up
    h_below[...] = down
    stats[0:1] = center
    stats[1:2] = scale


def second_kernel(z, hidden, h_above, h_below, gathered, affine, weight, x, other, pair, teacher, out, o_above, o_below, near, stats, copies, pads, chains):
    center, scale = merged(z, gathered)
    act = activation(center, scale, affine[2:3], affine[3:4])
    r = z.rims
    own = act(hidden[...])
    up, down = act(h_above[...]) * inside(z, 3, True), act(h_below[...]) * inside(z, 3, False)
    own, up, down = convolve(z, own, up, down, 3, pads, chains, weight)
    own = x[...] + own
    amap = attention(own)
    lane = lax.broadcasted_iota(jnp.int32, (1, 128), 1)
    sums = image_sums(z, amap * jnp.where(lane < 64, amap, teacher[...]))
    copies[...] = jnp.concatenate([sums] * z.peers, axis=0)
    out[...] = own
    o_above[...] = above_of(pair, other, (pl.ds(2 * r, 2 * r), pl.ds(0, LANES))) + up
    o_below[...] = below_of(pair, other, (pl.ds(0, 2 * r), pl.ds(0, LANES))) + down
    near[0] = h_above[pl.ds(2 * r, r), :]
    near[1] = h_below[pl.ds(0, r), :]
    stats[0:1] = center
    stats[1:2] = scale


def tap_rows(q):
    return 128 + C if q < 0 else q * C


def tap_product(z, operand, own, above, below, pads):
    fill_center(z, pads, own)
    fill_shifted(z, pads, above, below)
    columns = []
    for a in range(TAPS):
        columns.append(
            jnp.concatenate([pads[k][TAPS - 1 - a, h, pl.ds(z.step[k], z.count[k]), :] for h in (0, 1) for k in (1, 0)], axis=0)
        )
    used = [jnp.concatenate([operand[n, pl.ds(0, 128 + C), :], operand[n, pl.ds(256 - C, C), :]], axis=0) for n in (0, 1)]
    return product(used, split(jnp.concatenate(columns, axis=1)))


def tap_sums(result, tiles, first_group):
    group = group_of()
    for a in range(TAPS):
        for b in range(TAPS):
            total = None
            for p in range(4):
                at = tap_rows(p + b - 1)
                part = result[at : at + C, 128 * a : 128 * a + 128]
                total = part if total is None else jnp.where(group == p, part, total)
            tile, slot = divmod(first_group + a * TAPS + b, 4)
            tiles[tile] = jnp.where(group == slot, spread_groups(total), tiles[tile])


def tap_counts(z, turned, tiles, first_group):
    group = group_of()
    m = lax.broadcasted_iota(jnp.int32, (1, 2 * z.total), 1) % z.total
    row = jnp.where(m < z.start[0], m % z.rows[1], (m - z.start[0]) % z.rows[0])
    height = jnp.where(m < z.start[0], z.rows[1], z.rows[0])
    at = lax.axis_index("row")
    lost = {
        0: (row == height - 1) & (at == z.peers - 1),
        2: (row == 0) & (at == 0),
    }
    for a in range(TAPS):
        column = jnp.sum(jnp.where(lost[a], 0.0, turned) if a in lost else turned, axis=1, keepdims=True)
        used = jnp.concatenate([column[: 128 + C], column[256 - C :]], axis=0)
        for b in range(TAPS):
            total = sum(used[tap_rows(p + b - 1) : tap_rows(p + b - 1) + C] for p in range(4))
            tile, slot = divmod(first_group + a * TAPS + b, 4)
            tiles[tile] = jnp.where(group == slot, total, tiles[tile])


def turned_operand(z, value, pads, kept):
    fill_center(z, pads, value)
    lane = lax.broadcasted_iota(jnp.int32, (1, 128), 1)
    halves = ([], [])
    for k in (1, 0):
        ref, step, count = pads[k], z.step[k], z.count[k]
        low, high = ref[1, 0, pl.ds(step, count), :], ref[1, 1, pl.ds(step, count), :]
        before, after = ref[1, 1, pl.ds(0, count), :], ref[1, 0, pl.ds(2 * step, count), :]
        for part, main, left, right in ((halves[0], low, before, high), (halves[1], high, low, after)):
            part.append(jnp.concatenate([main, jnp.where(lane >= 96, left, jnp.where(lane < 32, right, 0.0))], axis=1))
    turned = jnp.concatenate(halves[0] + halves[1], axis=0).T
    parts = split(turned)
    for n in (0, 1):
        kept[n] = parts[n]
    return turned


def first_operand_kernel(z, x, hidden, h_above, h_below, other, pair, stats, affine, teacher, upstream, weights, left, packed, teachers, spread_u, near_u, pads, chains, kept, kept_w, kept_u, pixels, kept_t, kept_c, kept_packed, sems):
    r, own = z.rims, pl.ds(0, z.total)
    loads = [pltpu.make_async_copy(upstream, kept_u.at[own, :], sems.at[0]), pltpu.make_async_copy(weights.at[1], kept_w, sems.at[1])]
    start_all(loads)
    act = activation(stats[0:1], stats[1:2], affine[0:1], affine[1:2])
    value = turned_operand(z, act(x[...]), pads, kept)
    stores = [pltpu.make_async_copy(kept, left, sems.at[2])]
    stores[0].start()
    tiles = [jnp.zeros((C, 128), F32) for _ in range(BACK_LANES // 128)]
    tap_counts(z, value, tiles, ONES)
    pivot = affine[4:5]
    result = tap_product(
        z, kept, hidden[...] - pivot, (h_above[pl.ds(2 * r, r), :] - pivot) * inside(z, 1, True),
        (h_below[pl.ds(0, r), :] - pivot) * inside(z, 1, False), pads,
    )
    tap_sums(result, tiles, HIDDEN)
    kept_packed[...] = jnp.concatenate(tiles, axis=1)
    stores.append(pltpu.make_async_copy(kept_packed, packed, sems.at[6]))
    stores[1].start()
    pixels[own, :] = teacher[...]
    pixels[pl.ds(z.total, 4 * r), :] = jnp.zeros((4 * r, 128), F32)
    n = (REACH + 2) * r
    for side, beyond_of in enumerate((above_of, below_of)):
        for d in (0, 1):
            for k in (0, 1):
                line = beyond_of(pair, other, (pl.ds(n + k * z.images[0], z.images[k]), pl.ds(128 * d, 128)))
                for j in range(z.blocks[k]):
                    at = z.total + (2 * side + d) * r + z.rim[k] + j * z.images[k]
                    pixels[pl.ds(at, z.images[k]), pl.ds(0, BLOCK)] = line[:, j * BLOCK : (j + 1) * BLOCK]
    kept_t[...] = spread(pixels[...], to_channels())
    stores.append(pltpu.make_async_copy(kept_t, teachers, sems.at[3]))
    stores[2].start()
    n = REACH * r
    at = (pl.ds(n, 2 * r), pl.ds(0, LANES))
    up, down = above_of(pair, other, at) * inside(z, 2, True), below_of(pair, other, at) * inside(z, 2, False)
    kept_u[pl.ds(z.total, r), :] = up[r:]
    kept_u[pl.ds(z.total + r, r), :] = down[:r]
    wait_all(loads)
    stores.append(pltpu.make_async_copy(kept_u, near_u, sems.at[5]))
    stores[3].start()
    kept_c[...] = jnp.concatenate(convolve(z, kept_u[own, :], up, down, 2, pads, chains, kept_w), axis=0)
    stores.append(pltpu.make_async_copy(kept_c, spread_u, sems.at[4]))
    stores[4].start()
    wait_all(stores)


def second_operand_kernel(z, hidden, near, stats, affine, out, o_above, o_below, teachers, spread_u, near_u, weights, out_copy, hidden_copy, left, shifts, by_map, by_teacher, up, pads, chains, kept_t, kept_u, kept_w, kept_s, sems):
    r, total = z.rims, z.total
    loads = [
        pltpu.make_async_copy(teachers, kept_t, sems.at[0]),
        pltpu.make_async_copy(weights.at[1], kept_w, sems.at[1]),
        pltpu.make_async_copy(spread_u, kept_u, sems.at[2]),
    ]
    start_all(loads)
    stores = [
        pltpu.make_async_copy(out, out_copy, sems.at[4]),
        pltpu.make_async_copy(hidden, hidden_copy.at[pl.ds(0, total), :], sems.at[7]),
        pltpu.make_async_copy(near.at[0], hidden_copy.at[pl.ds(total, r), :], sems.at[8]),
        pltpu.make_async_copy(near.at[1], hidden_copy.at[pl.ds(total + r, r), :], sems.at[9]),
        pltpu.make_async_copy(near_u, up, sems.at[10]),
    ]
    start_all(stores)
    normed = normed_by(stats)(jnp.concatenate([hidden[...], near[0], near[1]], axis=0))
    shifted = normed * affine[2:3] + affine[3:4]
    turned_operand(z, gelu(shifted[:total]), pads, left)
    ones = jnp.ones((total, 1), F32)
    masks = jnp.concatenate([ones, inside(z, 1, True), inside(z, 1, False)], axis=0)
    slopes = gelu_slope(shifted) * masks
    o = jnp.concatenate([out[...], o_above[...] * inside(z, 2, True), o_below[...] * inside(z, 2, False)], axis=0)
    for_map = spread(attention(o), to_channels()) * o
    wait_all(loads)
    for_teacher = kept_t[...] * o
    kept_s[0] = kept_u[...] * slopes
    stores += copies_of(pieces(kept_s, shifts), sems, 11)
    stores[-3].start()
    for n, value, ref in ((1, for_map, by_map), (2, for_teacher, by_teacher)):
        own, before, after = value[:total], value[total : total + 2 * r], value[total + 2 * r :]
        ref[...] = jnp.concatenate([own, before[r:], after[:r]], axis=0)
        kept_s[n] = jnp.concatenate(convolve(z, own, before, after, 2, pads, chains, kept_w), axis=0) * slopes
        stores[n - 3].start()
    wait_all(stores)


def upstream_kernel(z, gathered, up, shifts, left_1, left_2, packed, by_map, by_teacher, hidden, stats, dout, dshift, d_above, d_below, slabs, kept_s, kept_left, kept_h, kept_packed, pads, more_pads, sems):
    r, total = z.rims, z.total
    loads = copies_of(
        pieces(shifts, kept_s) + pieces(left_1, kept_left) + [(hidden.at[pl.ds(0, total), :], kept_h), (packed, kept_packed)], sems
    )
    start_all(loads)
    lane = lax.broadcasted_iota(jnp.int32, (z.slots, 128), 1)
    sums = sum(gathered[pl.ds(n * z.slots, z.slots), :] for n in range(z.peers))
    square = jnp.sum(jnp.where(lane < 64, sums, 0.0), axis=1, keepdims=True)
    cross = jnp.sum(jnp.where(lane < 64, 0.0, sums), axis=1, keepdims=True)
    inverse = lax.rsqrt(square + map_eps)
    inner = beta_weight * (square * inverse - cross) * inverse
    shape = (z.slots, 128)
    for_map = (beta_weight - inner) * inverse * inverse * (2.0 / C)
    for_teacher = beta_weight * inverse * (2.0 / C)
    for_map, for_teacher = (wide(image_rows(z, jnp.broadcast_to(v, shape), 2)) for v in (for_map, for_teacher))
    value = up[...] + for_map * by_map[...] - for_teacher * by_teacher[...]
    dout[...] = value[:total]
    wait_all(loads[:3])
    shift = kept_s[0] + for_map * kept_s[1] - for_teacher * kept_s[2]
    pre, above, below = shift[:total], shift[total : total + r], shift[total + r :]
    dshift[...] = pre
    d_above[...] = above
    d_below[...] = below
    second = tap_product(z, left_2, value[:total], value[total : total + r], value[total + r :], pads)
    wait_all(loads[3:5])
    first = tap_product(z, kept_left, pre, above, below, more_pads)
    wait_all(loads[5:])
    normed = normed_by(stats)(kept_h[...])
    tiles = [kept_packed[:, 128 * n : 128 * n + 128] for n in range(BACK_LANES // 128)]
    group = group_of()
    tiles[0] = jnp.where(group == BIAS, fold(column_sum(pre)), jnp.where(group == GAIN, fold(column_sum(pre * normed)), tiles[0]))
    tap_sums(second, tiles, SECOND)
    tap_sums(first, tiles, LEFT)
    line = jnp.concatenate(tiles, axis=1)
    for d in range(z.devices):
        slabs[d] = line[d % C : d % C + 1]


def write_kernel(z, out, x, hidden, weights, first_stats, stats, order, out_s, out_l, first_normed, normed, weight, kept, kept_x, kept_h, half, sems):
    loads = [pltpu.make_async_copy(a, b, sems.at[n]) for n, (a, b) in enumerate(((out, kept), (x, kept_x), (hidden, kept_h), (weights.at[0], weight)))]
    start_all(loads)
    loads[0].wait()
    put_halves(half, kept[...])
    from_matrix(z, half, (out_s, out_l))
    loads[1].wait()
    first_normed[...] = normed_by(first_stats)(kept_x[...])
    loads[2].wait()
    normed[...] = normed_by(stats)(kept_h[...])
    loads[3].wait()


def norm_sums(total):
    group = group_of()
    return [wide(spread_groups(jnp.where(group == n, total[:, :128], 0.0))) for n in (BIAS, GAIN)]


def hidden_kernel(z, gathered, dshift, d_above, d_below, second_normed, stats, affine, weight, first_normed, pre_ref, gain_out, bias_out, slabs, pads):
    total = jnp.sum(gathered[...], axis=0)
    bias_sum, gain_sum = norm_sums(total)
    bias_out[...] = bias_sum[:, :C]
    gain_out[...] = gain_sum[:, :C]
    bias_mean, gain_mean = bias_sum / z.pixels, gain_sum / z.pixels
    factor = affine[2:3] * stats[1:2]
    r, total_rows = z.rims, z.total

    def back(d, normed):
        return factor * (d - bias_mean - normed * gain_mean)

    own = back(dshift[...], second_normed[pl.ds(0, total_rows), :])
    up = back(d_above[...], second_normed[pl.ds(total_rows, r), :]) * inside(z, 1, True)
    down = back(d_below[...], second_normed[pl.ds(total_rows + r, r), :]) * inside(z, 1, False)
    grad, _, _ = convolve(z, own, up, down, 1, pads, None, weight)
    normed = first_normed[...]
    pre = grad * gelu_slope(normed * affine[0:1] + affine[1:2])
    pre_ref[...] = pre
    lane = lax.broadcasted_iota(jnp.int32, (1, 128), 1)
    taps = TAPS * TAPS * C

    def along(row):
        return jnp.concatenate([row[:, :128]] * 3, axis=1)[:, :taps]

    second, left, against, ones = (total[:, n * C : n * C + taps] for n in (SECOND, LEFT, HIDDEN, ONES))
    against = along(stats[1:2]) * (against - along(stats[0:1] - affine[4:5]) * ones)
    first = along(factor) * (left - along(bias_mean) * ones - along(gain_mean) * against)
    sums = jnp.where(lane < C, fold(column_sum(pre)), fold(column_sum(pre * normed)))
    line = jnp.concatenate([sums[:, : 2 * C], second, first], axis=1)
    slabs[...] = jnp.broadcast_to(line[None], slabs.shape)


def back_kernel(z, gathered, pre, normed, stats, affine, dout, back_s, back_l, one, two, gain_out, bias_out, half, lines):
    bias_sum, gain_sum = norm_sums(jnp.sum(gathered[:, :, pl.ds(0, 128)], axis=0))
    bias_out[...] = bias_sum[:, :C]
    gain_out[...] = gain_sum[:, :C]
    value = dout[...] + affine[0:1] * stats[1:2] * (pre[...] - bias_sum / z.pixels - normed[...] * (gain_sum / z.pixels))
    put_halves(half, value)
    from_matrix(z, half, (back_s, back_l))
    for d in range(C):
        lines[pl.ds(d, 1), :] = gathered[d]
    for ref, group in ((two, LAST_SECOND), (one, LAST_FIRST)):
        for a in range(TAPS):
            for b in range(TAPS):
                at = (group + a * TAPS + b) * C
                ref[a, b] = lines[:, pl.ds(at, C)]


def call(body, ins, outs, scratch=(), sems=0):
    space = {"v": pltpu.VMEM, "h": pltpu.HBM, "V": pltpu.VMEM}
    shapes = []
    for item in scratch:
        if isinstance(item, list):
            shapes.append([pltpu.VMEM(*s) for s in item])
        else:
            shapes.append(pltpu.VMEM(*item))
    if sems:
        shapes.append(pltpu.SemaphoreType.DMA((sems,)))
    run = pl.pallas_call(
        body,
        out_shape=[jax.ShapeDtypeStruct(shape, kind) if s == "v" else space[s](shape, kind) for s, shape, kind in outs],
        in_specs=[pl.BlockSpec(memory_space=space[s]) for s in ins],
        out_specs=[pl.BlockSpec(memory_space=space[s]) for s, _, _ in outs],
        scratch_shapes=shapes,
        compiler_params=pltpu.CompilerParams(vmem_limit_bytes=VMEM_LIMIT),
    )
    return lambda *args: run(
        *(pltpu.with_memory_space_constraint(arg, pltpu.HBM) if s == "h" else arg for s, arg in zip(ins, args))
    )


def exchange(lines, axes):
    shape = lines.shape
    if len(shape) == 2:
        lines = lines.reshape(math.prod(lax.axis_size(axis) for axis in axes), -1, 128)
    return lax.all_to_all(lines, axes, 0, 0, tiled=True).reshape(shape)


def beyond(z, pair, other, depths):
    hops = max(-(-depth // rows) for rows in z.rows for depth in depths)
    if hops == 1:
        swap = lambda value, start: lax.ppermute(
            value, "row", [(i + a, i + 1 - a) for i in range(start, z.peers - 1, 2) for a in (0, 1)]
        )
        others = swap(other, 1)
        return swap(pair, 0), others
    even = is_even()
    bottom, top = jnp.where(even, pair, other), jnp.where(even, other, pair)
    above, below = [], []
    for hop in range(1, hops + 1):
        above.append(lax.ppermute(bottom, "row", [(i, i + hop) for i in range(z.peers - hop)]))
        below.append(lax.ppermute(top, "row", [(i + hop, i) for i in range(z.peers - hop)]))
    up, down = [], []
    base = 0
    for depth in depths:
        for n in range(depth):
            for k in (1, 0):
                hop, back = divmod(depth - 1 - n, z.rows[k])
                at = base + (depth - 1 - back) * z.rims + z.rim[k]
                up.append(above[hop][at : at + z.edge[k]])
                hop, back = divmod(n, z.rows[k])
                at = base + back * z.rims + z.rim[k]
                down.append(below[hop][at : at + z.edge[k]])
        base += depth * z.rims
    up.append(jnp.concatenate([pixel_rows(z, above, base, 1, 1), pixel_rows(z, above, base, 0, 1)], axis=1))
    down.append(jnp.concatenate([pixel_rows(z, below, base, 0, 0), pixel_rows(z, below, base, 1, 0)], axis=1))
    up, down = jnp.concatenate(up, axis=0), jnp.concatenate(down, axis=0)
    return jnp.where(even, down, up), jnp.where(even, up, down)


def pixel_rows(z, bands, base, distance, last):
    lines = []
    for k in (0, 1):
        hop, back = divmod(distance, z.rows[k])
        at = base + k * z.images[0]
        half = 128 * abs(last - back)
        lines.append(bands[hop][at : at + z.images[k], half : half + 128])
    lines.append(jnp.zeros((z.slots - sum(z.images), 128), F32))
    return jnp.concatenate(lines, axis=0)


def local(
    image_small, image_large, teacher_small, teacher_large, upstream_small, upstream_large,
    conv_first, gain_first, bias_first, conv_second, gain_second, bias_second,
):
    peers = lax.axis_size("row")
    devices = lax.axis_size("img") * peers
    z = Sizes(image_small.shape, image_large.shape, devices, peers)
    body = lambda function: functools.partial(function, z)
    r = z.rims
    full, half, pair = (z.total, LANES), (2, z.total, 128), (2 * devices, 128)
    weight, left = (2, TAPS * TAP_ROWS, 128), (2, 256, 2 * z.total)
    images = [image_small, image_large, upstream_small, upstream_large, teacher_small, teacher_large]
    f = lambda space, *shape: (space, shape, F32)
    depths = (REACH, 2)
    rim_rows = sum(depths) * r + z.slots

    x, pair_edge, other_edge, copies = call(
        body(start_kernel),
        "hhhhhh",
        [("v", full, F32), f("v", rim_rows, LANES), f("v", rim_rows, LANES), ("V", pair, F32)],
        [[(a.shape, F32) for a in images], (half, F32)],
        4 + 2 * z.images[1],
    )(*images)
    gathered = exchange(copies, AXES)
    pair_rims, other_rims = beyond(z, pair_edge, other_edge, depths)
    params = [conv_first, conv_second] + images[2:]
    w1, w2, weights, affine, upstream, teacher, x_copy = call(
        body(prepare_kernel),
        "hhhhhhhhhhv",
        [("v", weight, BF16), ("v", weight, BF16), ("h", (2,) + weight, BF16), f("v", 5, LANES), ("h", full, F32), f("v", z.total, 128), ("h", full, F32)],
        [[(a.shape, F32) for a in params], ((2,) + weight, BF16), (full, F32), ((4, C), F32), (half, F32)],
        14,
    )(*params, *(v.reshape(1, C) for v in (gain_first, bias_first, gain_second, bias_second)), x)

    hidden, h_above, h_below, stats_one, copies = call(
        body(first_kernel),
        "vvvvvv",
        [("v", full, F32), f("v", 3 * r, LANES), f("v", 3 * r, LANES), f("v", 2, LANES), ("V", pair, F32)],
        [z.pads(), z.chains(4)],
    )(x, other_rims, pair_rims, gathered, affine, w1)
    gathered = exchange(copies, AXES)
    extended, near_rows = z.total + 4 * r, z.total + 2 * r
    left_one, packed, teachers, spread_u, near_u = call(
        body(first_operand_kernel),
        "vvvvvvvvvhh",
        [("h", left, BF16), f("h", C, BACK_LANES), f("h", extended, LANES), f("h", near_rows, LANES), f("h", near_rows, LANES)],
        [
            z.pads(), z.chains(2), (left, BF16), (weight, BF16), ((near_rows, LANES), F32), ((extended, 128), F32),
            ((extended, LANES), F32), ((near_rows, LANES), F32), ((C, BACK_LANES), F32),
        ],
        7,
    )(x, hidden, h_above, h_below, other_rims, pair_rims, stats_one, affine, teacher, upstream, weights)
    gathered, near_u = lax.optimization_barrier((gathered, near_u))

    map_shape = (peers * z.slots, 128)
    out, o_above, o_below, near, stats_two, copies = call(
        body(second_kernel),
        "vvvvvvvvvv",
        [("v", full, F32), f("v", 2 * r, LANES), f("v", 2 * r, LANES), f("v", 2, r, LANES), f("v", 2, LANES), ("V", map_shape, F32)],
        [z.pads(), z.chains(3)],
    )(hidden, h_above, h_below, gathered, affine, w2, x, other_rims, pair_rims, teacher)
    gathered = exchange(copies, ("row",))
    out_copy, hidden_copy, left_two, shifts, by_map, by_teacher, up = call(
        body(second_operand_kernel),
        "vvvvvvvhhhh",
        [
            ("h", full, F32), f("h", near_rows, LANES), ("v", left, BF16), f("h", 3, near_rows, LANES),
            f("v", near_rows, LANES), f("v", near_rows, LANES), f("v", near_rows, LANES),
        ],
        [
            z.pads(), z.chains(2), ((extended, LANES), F32), ((near_rows, LANES), F32), (weight, BF16),
            ((3, near_rows, LANES), F32),
        ],
        14,
    )(hidden, near, stats_two, affine, out, o_above, o_below, teachers, spread_u, near_u, weights)

    dout, dshift, d_above, d_below, slabs = call(
        body(upstream_kernel),
        "vvhhvhvvhv",
        [("v", full, F32), ("v", full, F32), f("v", r, LANES), f("v", r, LANES), f("V", devices, 1, BACK_LANES)],
        [((3, near_rows, LANES), F32), (left, BF16), (full, F32), ((C, BACK_LANES), F32), z.pads(), z.pads()],
        7,
    )(gathered, up, shifts, left_one, left_two, packed, by_map, by_teacher, hidden_copy, stats_two)
    gathered = exchange(slabs, AXES)
    out_s, out_l, first_normed, second_normed, weight_back = call(
        body(write_kernel),
        "hhhhvvv",
        [("v", image_small.shape, F32), ("v", image_large.shape, F32), ("v", full, F32), f("v", near_rows, LANES), ("v", weight, BF16)],
        [(full, F32), (full, F32), ((near_rows, LANES), F32), (half, F32)],
        4,
    )(out_copy, x_copy, hidden_copy, weights, stats_one, stats_two, d_above)

    pre, gain_two, bias_two, slabs = call(
        body(hidden_kernel),
        "vvvvvvvvv",
        [("v", full, F32), f("v", 1, C), f("v", 1, C), f("V", devices, 1, LAST_LANES)],
        [z.pads()],
    )(gathered, dshift, d_above, d_below, second_normed, stats_two, affine, weight_back, first_normed)
    gathered = exchange(slabs, AXES)

    back_s, back_l, one, two, gain_one, bias_one = call(
        body(back_kernel),
        "vvvvvv",
        [("v", a.shape, F32) for a in (image_small, image_large, conv_first, conv_second)] + [f("v", 1, C), f("v", 1, C)],
        [(half, F32), ((C, LAST_LANES), F32)],
    )(gathered, pre, first_normed, stats_one, affine, dout)
    return (
        out_s, out_l, back_s, back_l,
        one, gain_one.reshape(C), bias_one.reshape(C),
        two, gain_two.reshape(C), bias_two.reshape(C),
    )


def solution(mesh):
    split_bands, everywhere = P("img", "row", None), P()
    return jax.shard_map(
        local,
        mesh=mesh,
        in_specs=(split_bands,) * 6 + (everywhere,) * 6,
        out_specs=(split_bands,) * 4 + (everywhere,) * 6,
        check_vma=False,
    )
```

```python
import functools
import math

import jax
import jax.numpy as jnp
from jax import lax
from jax.experimental import pallas as pl
from jax.experimental.pallas import tpu as pltpu
from jax.sharding import PartitionSpec as P

C = 32
HS = 32
HL = 64
HEIGHTS = (HS, HL)

norm_eps = 1e-05
map_eps = 1e-06
beta_weight = 1000.0
AXES = ("img", "row")
BLOCK = 8
LANES = BLOCK * C
TAPS = 3
DEPTH = TAPS * 128 + 256
TAP_ROWS = 128 + 2 * C
REACH = 4
ROOT = math.sqrt(2.0 / math.pi)
CUBE = 0.044715
F32 = jnp.float32
BF16 = jnp.bfloat16
VMEM_LIMIT = 32 * 1024 * 1024
BIAS, GAIN, SECOND, LEFT, HIDDEN, ONES = 0, 1, 2, 11, 20, 29
BACK_LANES = 1280
LAST_SECOND, LAST_FIRST, LAST_LANES = 2, 11, 640


class Sizes:
    def __init__(self, small, large, devices, peers):
        self.images = (small[0], large[0])
        self.rows = (small[1], large[1])
        self.blocks = (HS // BLOCK, HL // BLOCK)
        self.step = tuple(n * r for n, r in zip(self.images, self.rows))
        self.count = tuple(b * s for b, s in zip(self.blocks, self.step))
        self.edge = tuple(b * n for b, n in zip(self.blocks, self.images))
        self.start = (self.count[1], 0)
        self.rim = (self.edge[1], 0)
        self.total = sum(self.count)
        self.rims = sum(self.edge)
        self.slots = -(-sum(self.images) // 8) * 8
        self.guard = -(-max(self.images) // 8) * 8
        self.devices = devices
        self.peers = peers
        self.here = float(self.total * BLOCK)
        self.pixels = self.here * devices

    def pads(self):
        return [((TAPS, 2, self.count[k] + 2 * self.step[k], 128), F32) for k in (0, 1)]

    def chains(self, depth):
        return [((2, 2 * self.guard + (depth + 1) * self.rims, 128), F32)] * 2


def split(value):
    high = value.astype(BF16)
    return high, (value - high.astype(F32)).astype(BF16)


def dot(left, right):
    return lax.dot_general(left, right, (((1,), (0,)), ((), ())), preferred_element_type=F32)


def product(left, right):
    if left[0].shape[1] % 128:
        return dot(left[0], right[0]) + (dot(left[0], right[1]) + dot(left[1], right[0]))
    return dot(
        jnp.concatenate([left[0], left[0], left[1]], axis=1), jnp.concatenate([right[0], right[1], right[0]], axis=0)
    )


def spread(left, right):
    right = right.astype(BF16)
    return dot(jnp.concatenate(split(left), axis=1), jnp.concatenate([right, right], axis=0))


def gelu(s):
    return 0.5 * s * (1.0 + jnp.tanh(ROOT * (s + CUBE * s * s * s)))


def gelu_slope(s):
    square = s * s
    t = jnp.tanh(ROOT * s * (1.0 + CUBE * square))
    return 0.5 * (1.0 + t) + 0.5 * s * (1.0 - t * t) * ROOT * (1.0 + 3.0 * CUBE * square)


def spread_groups(row):
    row = row + pltpu.roll(row, 64, 1)
    return row + pltpu.roll(row, 32, 1)


def fold(row):
    return spread_groups(row[:, :128] + row[:, 128:])


def wide(row):
    return jnp.concatenate([row, row], axis=1)


def group_of(rows=1, lanes=128):
    return lax.broadcasted_iota(jnp.int32, (rows, lanes), 1) // C


def column_sum(value):
    return jnp.sum(value, axis=0, keepdims=True)


def send_lines(z, ref, lines):
    for n, line in enumerate(lines):
        ref[pl.ds(n, z.devices, stride=len(lines)), :] = jnp.broadcast_to(line, (z.devices, 128))


def moments(z, value, ref):
    few = min(8, z.total)
    pivot = fold(column_sum(value[:few])) / float(few * BLOCK)
    off = value - wide(pivot)
    first, second = fold(column_sum(off)), fold(column_sum(off * off))
    send_lines(z, ref, [pivot + first / z.here, second - first * first / z.here])


def merged(z, ref):
    means = ref[pl.ds(0, z.devices, stride=2), :]
    center = jnp.mean(means, axis=0, keepdims=True)
    off = means - center
    within = jnp.mean(ref[pl.ds(1, z.devices, stride=2), :], axis=0, keepdims=True)
    variance = within / z.here + jnp.mean(off * off, axis=0, keepdims=True)
    return wide(center), wide(lax.rsqrt(variance + norm_eps))


def put_halves(ref, value):
    ref[0] = value[:, :128]
    ref[1] = value[:, 128:]


def whole(ref):
    return jnp.concatenate([ref[0], ref[1]], axis=1)


def to_matrix(z, refs, half):
    for k in (0, 1):
        for j in range(z.blocks[k]):
            at = z.start[k] + j * z.step[k]
            for i in range(z.images[k]):
                for h in (0, 1):
                    half[h, pl.ds(at + i * z.rows[k], z.rows[k]), :] = refs[k][i, :, pl.ds(LANES * j + 128 * h, 128)]


def from_matrix(z, half, refs):
    for k in (0, 1):
        for j in range(z.blocks[k]):
            at = z.start[k] + j * z.step[k]
            for i in range(z.images[k]):
                for h in (0, 1):
                    refs[k][i, :, pl.ds(LANES * j + 128 * h, 128)] = half[h, pl.ds(at + i * z.rows[k], z.rows[k]), :]


def is_even():
    return lax.axis_index("row") % 2 == 0


def put_edges(pair, other, at, last, first):
    even = is_even()
    pair[at] = jnp.where(even, last, first)
    other[at] = jnp.where(even, first, last)


def above_of(pair, other, at):
    return jnp.where(is_even(), other[at], pair[at])


def below_of(pair, other, at):
    return jnp.where(is_even(), pair[at], other[at])


def take_rims(z, half, depth, pair, other):
    everything = pl.ds(0, 128)
    for k in (0, 1):
        nothing = jnp.zeros((z.edge[k], 128), F32)
        for n in range(depth):
            first, last = nothing, nothing
            if depth - n <= z.rows[k]:
                last = half[pl.ds(z.start[k] + z.rows[k] - depth + n, z.edge[k], stride=z.rows[k]), :]
            if n < z.rows[k]:
                first = half[pl.ds(z.start[k] + n, z.edge[k], stride=z.rows[k]), :]
            put_edges(pair, other, (pl.ds(n * z.rims + z.rim[k], z.edge[k]), everything), last, first)


def inside(z, depth, above):
    at = lax.axis_index("row")
    large = lax.broadcasted_iota(jnp.int32, (z.rims, 1), 0) < z.rim[0]
    parts = []
    for n in range(depth):
        if above:
            ok = [jnp.where(at * rows >= depth - n, 1.0, 0.0) for rows in z.rows]
        else:
            ok = [jnp.where((at + 1) * rows + n + 1 <= height, 1.0, 0.0) for rows, height in zip(z.rows, HEIGHTS)]
        parts.append(jnp.where(large, ok[1], ok[0]).astype(F32))
    return jnp.concatenate(parts, axis=0)


def clear_guards(z, pads, a):
    for k in (0, 1):
        pads[k][a, 1, pl.ds(0, z.step[k]), :] = jnp.zeros((z.step[k], 128), F32)
        pads[k][a, 0, pl.ds(z.step[k] + z.count[k], z.step[k]), :] = jnp.zeros((z.step[k], 128), F32)


def fill_center(z, pads, value):
    clear_guards(z, pads, 1)
    for k in (0, 1):
        for h in (0, 1):
            pads[k][1, h, pl.ds(z.step[k], z.count[k]), :] = value[z.start[k] : z.start[k] + z.count[k], 128 * h : 128 * h + 128]


def fill_shifted(z, pads, above, below):
    for k in (0, 1):
        ref, step, count, rows = pads[k], z.step[k], z.count[k], z.rows[k]
        rim = slice(z.rim[k], z.rim[k] + z.edge[k])
        for h in (0, 1):
            lanes = slice(128 * h, 128 * h + 128)
            ref[0, h, pl.ds(step, count), :] = ref[1, h, pl.ds(step - 1, count), :]
            ref[2, h, pl.ds(step, count), :] = ref[1, h, pl.ds(step + 1, count), :]
            ref[0, h, pl.ds(step, z.edge[k], stride=rows), :] = above[rim, lanes]
            ref[2, h, pl.ds(step + rows - 1, z.edge[k], stride=rows), :] = below[rim, lanes]


def fill_pads(z, pads, value, above, below):
    fill_center(z, pads, value)
    fill_shifted(z, pads, above, below)
    for a in (0, 2):
        clear_guards(z, pads, a)


def beside(left, right):
    lane = lax.broadcasted_iota(jnp.int32, (1, 128), 1)
    middle = pltpu.roll(jnp.where(lane >= 64, left[1], right[1]), 64, 1)
    return [
        jnp.where(lane >= 96, left[0], jnp.where(lane < 32, right[0], middle)),
        jnp.where(lane >= 96, left[2], jnp.where(lane < 32, right[2], 0.0)),
    ]


def band_operand(z, pads):
    parts = ([], [])
    for k in (1, 0):
        ref, step, count = pads[k], z.step[k], z.count[k]
        low, high = ([ref[a, h, pl.ds(step, count), :] for a in range(TAPS)] for h in (0, 1))
        before = [ref[a, 1, pl.ds(0, count), :] for a in range(TAPS)]
        after = [ref[a, 0, pl.ds(2 * step, count), :] for a in range(TAPS)]
        parts[0].append(jnp.concatenate(low + beside(before, high), axis=1))
        parts[1].append(jnp.concatenate(high + beside(low, after), axis=1))
    return [jnp.concatenate(part, axis=0) for part in parts]


def rim_operand(z, chain, depth):
    m = lax.broadcasted_iota(jnp.int32, (z.rims, 1), 0)
    large = m < z.rim[0]
    has_before = jnp.where(large, m, m - z.rim[0]) >= jnp.where(large, z.images[1], z.images[0])
    has_after = m < jnp.where(large, z.rim[0] - z.images[1], z.rims - z.images[0])
    low, high, before, after = [], [], [], []
    for r in range(depth + 1):
        at = z.guard + r * z.rims
        low.append(chain[0, pl.ds(at, z.rims), :])
        high.append(chain[1, pl.ds(at, z.rims), :])
        shifted = [chain[1, pl.ds(at - images, z.rims), :] for images in z.images]
        before.append(jnp.where(has_before, jnp.where(large, shifted[1], shifted[0]), 0.0))
        shifted = [chain[0, pl.ds(at + images, z.rims), :] for images in z.images]
        after.append(jnp.where(has_after, jnp.where(large, shifted[1], shifted[0]), 0.0))
    parts = ([], [])
    for n in range(depth - 1):
        rows = slice(n, n + TAPS)
        parts[0].append(jnp.concatenate(low[rows] + beside(before[rows], high[rows]), axis=1))
        parts[1].append(jnp.concatenate(high[rows] + beside(low[rows], after[rows]), axis=1))
    return [jnp.concatenate(part, axis=0) for part in parts]


def times(parts, weight):
    left = jnp.concatenate([part[h] for h in (0, 1) for part in parts], axis=0)
    both = jnp.concatenate([weight_matrix(weight.at[0]), weight_matrix(weight.at[1])], axis=1)
    result = dot(jnp.concatenate(split(left), axis=1), jnp.concatenate([both, both], axis=0))
    result = result[:, :128] + result[:, 128:]
    rows = result.shape[0] // 2
    return jnp.concatenate([result[:rows], result[rows:]], axis=1)


def rim_operands(z, pads, above, below, depth, chains):
    parts = []
    for side, (rim, chain) in enumerate(zip((above, below), chains)):
        rim_at, own_at = (z.guard, z.guard + depth * z.rims) if side == 0 else (z.guard + z.rims, z.guard)
        for h in (0, 1):
            chain[h, pl.ds(rim_at, depth * z.rims), :] = rim[:, 128 * h : 128 * h + 128]
            for k in (0, 1):
                row = z.step[k] + (0 if side == 0 else z.rows[k] - 1)
                chain[h, pl.ds(own_at + z.rim[k], z.edge[k]), :] = pads[k][1, h, pl.ds(row, z.edge[k], stride=z.rows[k]), :]
        parts.append(rim_operand(z, chain, depth))
    return parts


def convolve(z, own, above, below, depth, pads, chains, weight):
    r = z.rims
    fill_pads(z, pads, own, above[(depth - 1) * r :], below[:r])
    parts = [band_operand(z, pads)]
    if depth > 1:
        parts += rim_operands(z, pads, above, below, depth, chains)
    result = times(parts, weight)
    n = z.total + (depth - 1) * r
    return result[: z.total], result[z.total : n], result[n:]


def convolve_rims(z, pads, above, below, depth, chains, weight):
    result = times(rim_operands(z, pads, above, below, depth, chains), weight)
    n = (depth - 1) * z.rims
    return result[:n], result[n:]


def image_sums(z, value):
    slot = lax.broadcasted_iota(jnp.int32, (z.slots, 1), 0)
    sums = jnp.zeros((z.slots, 128), F32)
    for k in (0, 1):
        line = value[z.start[k] : z.start[k] + z.step[k]]
        for j in range(1, z.blocks[k]):
            at = z.start[k] + j * z.step[k]
            line = line + value[at : at + z.step[k]]
        image = lax.broadcasted_iota(jnp.int32, (z.step[k], 1), 0) // z.rows[k]
        for i in range(z.images[k]):
            sums = jnp.where(slot == i + k * z.images[0], column_sum(jnp.where(image == i, line, 0.0)), sums)
    return sums


def image_rows(z, values, rims):
    parts = []
    for k in (1, 0):
        image = lax.broadcasted_iota(jnp.int32, (z.step[k], 1), 0) // z.rows[k]
        line = jnp.zeros((z.step[k], 128), F32)
        for i in range(z.images[k]):
            at = i + k * z.images[0]
            line = jnp.where(image == i, values[at : at + 1], line)
        parts += [line] * z.blocks[k]
    if rims:
        m = lax.broadcasted_iota(jnp.int32, (z.rims, 1), 0)
        image = jnp.where(m < z.rim[0], z.images[0] + m % z.images[1], (m - z.rim[0]) % z.images[0])
        line = jnp.zeros((z.rims, 128), F32)
        for at in range(sum(z.images)):
            line = jnp.where(image == at, values[at : at + 1], line)
        parts += [line] * rims
    return jnp.concatenate(parts, axis=0)


def channel_mean():
    a = lax.broadcasted_iota(jnp.int32, (LANES, 128), 0) // C
    b = lax.broadcasted_iota(jnp.int32, (LANES, 128), 1) % 64
    return jnp.where(a == b, 1.0 / C, 0.0).astype(F32)


def to_channels():
    a = lax.broadcasted_iota(jnp.int32, (128, LANES), 0)
    b = lax.broadcasted_iota(jnp.int32, (128, LANES), 1) // C
    return jnp.where(a == b, 1.0, 0.0).astype(F32)


def attention(value):
    return spread(value * value, channel_mean())


def pieces(source, target):
    return [(source.at[n], target.at[n]) for n in range(source.shape[0])]


def copies_of(pairs, sems, first=0):
    return [pltpu.make_async_copy(a, b, sems.at[first + n]) for n, (a, b) in enumerate(pairs)]


def start_all(copies):
    for copy in copies:
        copy.start()


def wait_all(copies):
    for copy in copies:
        copy.wait()


def start_kernel(z, small, large, up_s, up_l, t_s, t_l, x, pair, other, copies, raw, half, sems):
    images = [(small, raw[0])] + pieces(large, raw[1])
    rest = [(up_s, raw[2])] + pieces(up_l, raw[3]) + [(t_s, raw[4]), (t_l, raw[5])]
    loads = copies_of(images + rest, sems)
    start_all(loads)
    r, n = z.rims, REACH * z.rims
    tail = n + 2 * r
    for ref in (pair, other):
        ref[pl.ds(tail, z.slots), :] = jnp.zeros((z.slots, LANES), F32)
    wait_all(loads[: len(images)])
    to_matrix(z, raw[:2], half)
    value = whole(half)
    x[...] = value
    moments(z, value, copies)
    for h in (0, 1):
        lanes = pl.ds(128 * h, 128)
        take_rims(z, half.at[h], REACH, pair.at[pl.ds(0, n), lanes], other.at[pl.ds(0, n), lanes])
    wait_all(loads[len(images) :])
    for k in (0, 1):
        width, rows = HEIGHTS[k], z.rows[k]
        for i in range(z.images[k]):
            slot = pl.ds(tail + i + k * z.images[0], 1)
            for d in (0, 1):
                has_last, has_first = rows + d >= 2, d < rows
                last, first = pl.ds(max(rows - 2 + d, 0), 1), pl.ds(min(d, rows - 1), 1)
                for j in range(z.blocks[k]):
                    lanes = pl.ds(LANES * j, LANES)
                    at = (pl.ds(n + d * r + z.rim[k] + j * z.images[k] + i, 1), pl.ds(0, LANES))
                    nothing = jnp.zeros((1, LANES), F32)
                    put_edges(
                        pair, other, at,
                        raw[2 + k][i, last, lanes] if has_last else nothing,
                        raw[2 + k][i, first, lanes] if has_first else nothing,
                    )
                nothing = jnp.zeros((1, width), F32)
                put_edges(
                    pair, other, (slot, pl.ds(128 * d, width)),
                    raw[4 + k][i, last, :] if has_last else nothing,
                    raw[4 + k][i, first, :] if has_first else nothing,
                )


def banded(taps, ref):
    row = lax.broadcasted_iota(jnp.int32, (128, 128), 0) // C
    lane = group_of(128)
    for a in range(TAPS):
        main = jnp.zeros((128, 128), F32)
        for b in range(TAPS):
            main = jnp.where(row - lane + 1 == b, taps[a][b], main)
        before = jnp.where(lane[:C] == 0, taps[a][0][:C], 0.0)
        after = jnp.where(lane[:C] == 3, taps[a][2][:C], 0.0)
        for n, part in enumerate(split(jnp.concatenate([main, before, after], axis=0))):
            ref[n, pl.ds(a * TAP_ROWS, TAP_ROWS), :] = part


def weight_matrix(ref):
    main = [ref[pl.ds(a * TAP_ROWS, 128), :] for a in range(TAPS)]
    before, after = ([ref[pl.ds(a * TAP_ROWS + 128 + n * C, C), :] for a in range(TAPS)] for n in (0, 1))
    return jnp.concatenate(
        main + [after[0], before[1], after[1], before[0], after[2], jnp.zeros((2 * C, 128), BF16), before[2]], axis=0
    )


def prepare_kernel(z, first, second, up_s, up_l, t_s, t_l, g1, b1, g2, b2, x, w1, w2, weights, affine, upstream, teacher, x_copy, raw, kept, kept_u, rows, half, sems):
    targets = tuple(raw) + tuple(rows.at[pl.ds(n, 1), :] for n in range(4))
    refs = (first, second, up_s, up_l, t_s, t_l, g1, b1, g2, b2)
    loads = [pltpu.make_async_copy(a, b, sems.at[n]) for n, (a, b) in enumerate(zip(refs, targets))]
    start_all(loads)
    stores = [pltpu.make_async_copy(x, x_copy, sems.at[13])]
    stores[0].start()
    wait_all(loads)
    to_matrix(z, raw[2:4], half)
    kept_u[...] = whole(half)
    stores.append(pltpu.make_async_copy(kept_u, upstream, sems.at[10]))
    stores[1].start()
    for n, (source, forward) in enumerate(zip(raw[:2], (w1, w2))):
        tiles = []
        for a in range(TAPS):
            line = [jnp.concatenate([source[a, b]] * 4, axis=1) for b in range(TAPS)]
            tiles.append([jnp.concatenate([tap] * 4, axis=0) for tap in line])
        turned = [[tiles[TAPS - 1 - a][TAPS - 1 - b].T for b in range(TAPS)] for a in range(TAPS)]
        banded(tiles, forward)
        if n == 0:
            stores.append(pltpu.make_async_copy(forward, weights.at[2], sems.at[14]))
            stores[-1].start()
        banded(turned, kept.at[n])
        stores.append(pltpu.make_async_copy(kept.at[n], weights.at[n], sems.at[11 + n]))
        stores[-1].start()
    taps = sum(raw[0][a, b] for a in range(TAPS) for b in range(TAPS))
    pivot = dot(jnp.broadcast_to(gelu(rows[1:2]), (8, C)), taps)[0:1]
    affine[...] = jnp.concatenate([jnp.concatenate([rows[...], pivot], axis=0)] * BLOCK, axis=1)
    teacher[...] = jnp.zeros(teacher.shape, F32)
    for k, ref in ((0, raw[4]), (1, raw[5])):
        for i in range(z.images[k]):
            line = ref[i]
            for j in range(z.blocks[k]):
                at = z.start[k] + j * z.step[k] + i * z.rows[k]
                for lane in (0, 64):
                    teacher[pl.ds(at, z.rows[k]), pl.ds(lane, BLOCK)] = line[:, j * BLOCK : (j + 1) * BLOCK]
    wait_all(stores)


def normed_by(stats):
    return lambda v: (v - stats[0:1]) * stats[1:2]


def activation(center, scale, gain, bias):
    factor = scale * gain
    offset = bias - center * factor
    return lambda v: gelu(v * factor + offset)


def first_kernel(z, x, pair, other, gathered, affine, weight, hidden, stats, copies, pads):
    center, scale = merged(z, gathered)
    act = activation(center, scale, affine[0:1], affine[1:2])
    r, lanes = z.rims, pl.ds(0, LANES)
    up = act(above_of(pair, other, (pl.ds((REACH - 1) * r, r), lanes))) * inside(z, 1, True)
    down = act(below_of(pair, other, (pl.ds(0, r), lanes))) * inside(z, 1, False)
    own, _, _ = convolve(z, act(x[...]), up, down, 1, pads, None, weight)
    moments(z, own, copies)
    hidden[...] = own
    stats[0:1] = center
    stats[1:2] = scale


def second_kernel(z, hidden, h_above, h_below, gathered, affine, weight, x, pair, other, teacher, out, o_above, o_below, near, stats, copies, pads, chains):
    center, scale = merged(z, gathered)
    act = activation(center, scale, affine[2:3], affine[3:4])
    r = z.rims
    own = act(hidden[...])
    up, down = act(h_above[...]) * inside(z, 3, True), act(h_below[...]) * inside(z, 3, False)
    own, up, down = convolve(z, own, up, down, 3, pads, chains, weight)
    own = x[...] + own
    amap = attention(own)
    lane = lax.broadcasted_iota(jnp.int32, (1, 128), 1)
    sums = image_sums(z, amap * jnp.where(lane < 64, amap, teacher[...]))
    copies[...] = jnp.concatenate([sums] * z.peers, axis=0)
    out[...] = own
    o_above[...] = above_of(pair, other, (pl.ds(2 * r, 2 * r), pl.ds(0, LANES))) + up
    o_below[...] = below_of(pair, other, (pl.ds(0, 2 * r), pl.ds(0, LANES))) + down
    near[0] = h_above[pl.ds(2 * r, r), :]
    near[1] = h_below[pl.ds(0, r), :]
    stats[0:1] = center
    stats[1:2] = scale


def tap_rows(q):
    return 128 + C if q < 0 else q * C


def tap_product(z, operand, own, above, below, pads):
    fill_center(z, pads, own)
    fill_shifted(z, pads, above, below)
    columns = []
    for a in range(TAPS):
        columns.append(
            jnp.concatenate([pads[k][TAPS - 1 - a, h, pl.ds(z.step[k], z.count[k]), :] for h in (0, 1) for k in (1, 0)], axis=0)
        )
    used = [jnp.concatenate([operand[n, pl.ds(0, 128 + C), :], operand[n, pl.ds(256 - C, C), :]], axis=0) for n in (0, 1)]
    return product(used, split(jnp.concatenate(columns, axis=1)))


def tap_sums(result, tiles, first_group):
    group = group_of()
    for a in range(TAPS):
        for b in range(TAPS):
            total = None
            for p in range(4):
                at = tap_rows(p + b - 1)
                part = result[at : at + C, 128 * a : 128 * a + 128]
                total = part if total is None else jnp.where(group == p, part, total)
            tile, slot = divmod(first_group + a * TAPS + b, 4)
            tiles[tile] = jnp.where(group == slot, spread_groups(total), tiles[tile])


def tap_counts(z, turned, tiles, first_group):
    group = group_of()
    m = lax.broadcasted_iota(jnp.int32, (1, 2 * z.total), 1) % z.total
    row = jnp.where(m < z.start[0], m % z.rows[1], (m - z.start[0]) % z.rows[0])
    height = jnp.where(m < z.start[0], z.rows[1], z.rows[0])
    at = lax.axis_index("row")
    lost = {
        0: (row == height - 1) & (at == z.peers - 1),
        2: (row == 0) & (at == 0),
    }
    for a in range(TAPS):
        column = jnp.sum(jnp.where(lost[a], 0.0, turned) if a in lost else turned, axis=1, keepdims=True)
        used = jnp.concatenate([column[: 128 + C], column[256 - C :]], axis=0)
        for b in range(TAPS):
            total = sum(used[tap_rows(p + b - 1) : tap_rows(p + b - 1) + C] for p in range(4))
            tile, slot = divmod(first_group + a * TAPS + b, 4)
            tiles[tile] = jnp.where(group == slot, total, tiles[tile])


def turned_operand(z, value, pads, kept):
    fill_center(z, pads, value)
    lane = lax.broadcasted_iota(jnp.int32, (1, 128), 1)
    halves = ([], [])
    for k in (1, 0):
        ref, step, count = pads[k], z.step[k], z.count[k]
        low, high = ref[1, 0, pl.ds(step, count), :], ref[1, 1, pl.ds(step, count), :]
        before, after = ref[1, 1, pl.ds(0, count), :], ref[1, 0, pl.ds(2 * step, count), :]
        for part, main, left, right in ((halves[0], low, before, high), (halves[1], high, low, after)):
            part.append(jnp.concatenate([main, jnp.where(lane >= 96, left, jnp.where(lane < 32, right, 0.0))], axis=1))
    turned = jnp.concatenate(halves[0] + halves[1], axis=0).T
    parts = split(turned)
    for n in (0, 1):
        kept[n] = parts[n]
    return turned


def first_operand_kernel(z, x, hidden, pair, other, stats, affine, teacher, upstream, weights, h_above, h_below, left, packed, teachers, spread_u, near_u, pads, chains, deep_chains, kept, kept_w, kept_u, pixels, kept_t, kept_c, kept_packed, sems):
    r, own = z.rims, pl.ds(0, z.total)
    loads = copies_of([(upstream, kept_u.at[own, :]), (weights.at[1], kept_w.at[1])], sems)
    first = pltpu.make_async_copy(weights.at[2], kept_w.at[0], sems.at[7])
    first.start()
    start_all(loads)
    act = activation(stats[0:1], stats[1:2], affine[0:1], affine[1:2])
    value = turned_operand(z, act(x[...]), pads, kept)
    stores = [pltpu.make_async_copy(kept, left, sems.at[2])]
    stores[0].start()
    n, lanes = REACH * r, pl.ds(0, LANES)
    up = act(above_of(pair, other, (pl.ds(0, n), lanes))) * inside(z, REACH, True)
    down = act(below_of(pair, other, (pl.ds(0, n), lanes))) * inside(z, REACH, False)
    first.wait()
    up, down = convolve_rims(z, pads, up, down, REACH, deep_chains, kept_w.at[0])
    h_above[...] = up
    h_below[...] = down
    tiles = [jnp.zeros((C, 128), F32) for _ in range(BACK_LANES // 128)]
    tap_counts(z, value, tiles, ONES)
    pivot = affine[4:5]
    result = tap_product(
        z, kept, hidden[...] - pivot, (up[2 * r :] - pivot) * inside(z, 1, True),
        (down[:r] - pivot) * inside(z, 1, False), pads,
    )
    tap_sums(result, tiles, HIDDEN)
    kept_packed[...] = jnp.concatenate(tiles, axis=1)
    stores.append(pltpu.make_async_copy(kept_packed, packed, sems.at[6]))
    stores[1].start()
    pixels[own, :] = teacher[...]
    pixels[pl.ds(z.total, 4 * r), :] = jnp.zeros((4 * r, 128), F32)
    n = (REACH + 2) * r
    for side, beyond_of in enumerate((above_of, below_of)):
        for d in (0, 1):
            for k in (0, 1):
                line = beyond_of(pair, other, (pl.ds(n + k * z.images[0], z.images[k]), pl.ds(128 * d, 128)))
                for j in range(z.blocks[k]):
                    at = z.total + (2 * side + d) * r + z.rim[k] + j * z.images[k]
                    pixels[pl.ds(at, z.images[k]), pl.ds(0, BLOCK)] = line[:, j * BLOCK : (j + 1) * BLOCK]
    kept_t[...] = spread(pixels[...], to_channels())
    stores.append(pltpu.make_async_copy(kept_t, teachers, sems.at[3]))
    stores[2].start()
    n = REACH * r
    at = (pl.ds(n, 2 * r), pl.ds(0, LANES))
    up, down = above_of(pair, other, at) * inside(z, 2, True), below_of(pair, other, at) * inside(z, 2, False)
    kept_u[pl.ds(z.total, r), :] = up[r:]
    kept_u[pl.ds(z.total + r, r), :] = down[:r]
    wait_all(loads)
    stores.append(pltpu.make_async_copy(kept_u, near_u, sems.at[5]))
    stores[3].start()
    kept_c[...] = jnp.concatenate(convolve(z, kept_u[own, :], up, down, 2, pads, chains, kept_w.at[1]), axis=0)
    stores.append(pltpu.make_async_copy(kept_c, spread_u, sems.at[4]))
    stores[4].start()
    wait_all(stores)


def second_operand_kernel(z, hidden, near, stats, affine, out, o_above, o_below, teachers, spread_u, near_u, weights, out_copy, hidden_copy, left, shifts, by_map, by_teacher, up, pads, chains, kept_t, kept_u, kept_w, kept_s, sems):
    r, total = z.rims, z.total
    loads = [
        pltpu.make_async_copy(teachers, kept_t, sems.at[0]),
        pltpu.make_async_copy(weights.at[1], kept_w, sems.at[1]),
        pltpu.make_async_copy(spread_u, kept_u, sems.at[2]),
    ]
    start_all(loads)
    stores = [
        pltpu.make_async_copy(out, out_copy, sems.at[4]),
        pltpu.make_async_copy(hidden, hidden_copy.at[pl.ds(0, total), :], sems.at[7]),
        pltpu.make_async_copy(near.at[0], hidden_copy.at[pl.ds(total, r), :], sems.at[8]),
        pltpu.make_async_copy(near.at[1], hidden_copy.at[pl.ds(total + r, r), :], sems.at[9]),
        pltpu.make_async_copy(near_u, up, sems.at[10]),
    ]
    start_all(stores)
    normed = normed_by(stats)(jnp.concatenate([hidden[...], near[0], near[1]], axis=0))
    shifted = normed * affine[2:3] + affine[3:4]
    turned_operand(z, gelu(shifted[:total]), pads, left)
    ones = jnp.ones((total, 1), F32)
    masks = jnp.concatenate([ones, inside(z, 1, True), inside(z, 1, False)], axis=0)
    slopes = gelu_slope(shifted) * masks
    o = jnp.concatenate([out[...], o_above[...] * inside(z, 2, True), o_below[...] * inside(z, 2, False)], axis=0)
    for_map = spread(attention(o), to_channels()) * o
    wait_all(loads)
    for_teacher = kept_t[...] * o
    kept_s[0] = kept_u[...] * slopes
    stores += copies_of(pieces(kept_s, shifts), sems, 11)
    stores[-3].start()
    for n, value, ref in ((1, for_map, by_map), (2, for_teacher, by_teacher)):
        own, before, after = value[:total], value[total : total + 2 * r], value[total + 2 * r :]
        ref[...] = jnp.concatenate([own, before[r:], after[:r]], axis=0)
        kept_s[n] = jnp.concatenate(convolve(z, own, before, after, 2, pads, chains, kept_w), axis=0) * slopes
        stores[n - 3].start()
    wait_all(stores)


def upstream_kernel(z, gathered, up, shifts, left_1, left_2, packed, by_map, by_teacher, hidden, stats, dout, dshift, d_above, d_below, slabs, kept_s, kept_left, kept_h, kept_packed, pads, more_pads, sems):
    r, total = z.rims, z.total
    loads = copies_of(
        pieces(shifts, kept_s) + pieces(left_1, kept_left) + [(hidden.at[pl.ds(0, total), :], kept_h), (packed, kept_packed)], sems
    )
    start_all(loads)
    lane = lax.broadcasted_iota(jnp.int32, (z.slots, 128), 1)
    sums = sum(gathered[pl.ds(n * z.slots, z.slots), :] for n in range(z.peers))
    square = jnp.sum(jnp.where(lane < 64, sums, 0.0), axis=1, keepdims=True)
    cross = jnp.sum(jnp.where(lane < 64, 0.0, sums), axis=1, keepdims=True)
    inverse = lax.rsqrt(square + map_eps)
    inner = beta_weight * (square * inverse - cross) * inverse
    shape = (z.slots, 128)
    for_map = (beta_weight - inner) * inverse * inverse * (2.0 / C)
    for_teacher = beta_weight * inverse * (2.0 / C)
    for_map, for_teacher = (wide(image_rows(z, jnp.broadcast_to(v, shape), 2)) for v in (for_map, for_teacher))
    value = up[...] + for_map * by_map[...] - for_teacher * by_teacher[...]
    dout[...] = value[:total]
    wait_all(loads[:3])
    shift = kept_s[0] + for_map * kept_s[1] - for_teacher * kept_s[2]
    pre, above, below = shift[:total], shift[total : total + r], shift[total + r :]
    dshift[...] = pre
    d_above[...] = above
    d_below[...] = below
    second = tap_product(z, left_2, value[:total], value[total : total + r], value[total + r :], pads)
    wait_all(loads[3:5])
    first = tap_product(z, kept_left, pre, above, below, more_pads)
    wait_all(loads[5:])
    normed = normed_by(stats)(kept_h[...])
    tiles = [kept_packed[:, 128 * n : 128 * n + 128] for n in range(BACK_LANES // 128)]
    group = group_of()
    tiles[0] = jnp.where(group == BIAS, fold(column_sum(pre)), jnp.where(group == GAIN, fold(column_sum(pre * normed)), tiles[0]))
    tap_sums(second, tiles, SECOND)
    tap_sums(first, tiles, LEFT)
    line = jnp.concatenate(tiles, axis=1)
    for d in range(z.devices):
        slabs[d] = line[d % C : d % C + 1]


def write_kernel(z, out, x, hidden, weights, first_stats, stats, order, out_s, out_l, first_normed, normed, weight, kept, kept_x, kept_h, half, sems):
    loads = [pltpu.make_async_copy(a, b, sems.at[n]) for n, (a, b) in enumerate(((out, kept), (x, kept_x), (hidden, kept_h), (weights.at[0], weight)))]
    start_all(loads)
    loads[0].wait()
    put_halves(half, kept[...])
    from_matrix(z, half, (out_s, out_l))
    loads[1].wait()
    first_normed[...] = normed_by(first_stats)(kept_x[...])
    loads[2].wait()
    normed[...] = normed_by(stats)(kept_h[...])
    loads[3].wait()


def norm_sums(total):
    group = group_of()
    return [wide(spread_groups(jnp.where(group == n, total[:, :128], 0.0))) for n in (BIAS, GAIN)]


def hidden_kernel(z, gathered, dshift, d_above, d_below, second_normed, stats, affine, weight, first_normed, pre_ref, gain_out, bias_out, slabs, pads):
    total = jnp.sum(gathered[...], axis=0)
    bias_sum, gain_sum = norm_sums(total)
    bias_out[...] = bias_sum[:, :C]
    gain_out[...] = gain_sum[:, :C]
    bias_mean, gain_mean = bias_sum / z.pixels, gain_sum / z.pixels
    factor = affine[2:3] * stats[1:2]
    r, total_rows = z.rims, z.total

    def back(d, normed):
        return factor * (d - bias_mean - normed * gain_mean)

    own = back(dshift[...], second_normed[pl.ds(0, total_rows), :])
    up = back(d_above[...], second_normed[pl.ds(total_rows, r), :]) * inside(z, 1, True)
    down = back(d_below[...], second_normed[pl.ds(total_rows + r, r), :]) * inside(z, 1, False)
    grad, _, _ = convolve(z, own, up, down, 1, pads, None, weight)
    normed = first_normed[...]
    pre = grad * gelu_slope(normed * affine[0:1] + affine[1:2])
    pre_ref[...] = pre
    lane = lax.broadcasted_iota(jnp.int32, (1, 128), 1)
    taps = TAPS * TAPS * C

    def along(row):
        return jnp.concatenate([row[:, :128]] * 3, axis=1)[:, :taps]

    second, left, against, ones = (total[:, n * C : n * C + taps] for n in (SECOND, LEFT, HIDDEN, ONES))
    against = along(stats[1:2]) * (against - along(stats[0:1] - affine[4:5]) * ones)
    first = along(factor) * (left - along(bias_mean) * ones - along(gain_mean) * against)
    sums = jnp.where(lane < C, fold(column_sum(pre)), fold(column_sum(pre * normed)))
    line = jnp.concatenate([sums[:, : 2 * C], second, first], axis=1)
    slabs[...] = jnp.broadcast_to(line[None], slabs.shape)


def back_kernel(z, gathered, pre, normed, stats, affine, dout, back_s, back_l, one, two, gain_out, bias_out, half, lines):
    bias_sum, gain_sum = norm_sums(jnp.sum(gathered[:, :, pl.ds(0, 128)], axis=0))
    bias_out[...] = bias_sum[:, :C]
    gain_out[...] = gain_sum[:, :C]
    value = dout[...] + affine[0:1] * stats[1:2] * (pre[...] - bias_sum / z.pixels - normed[...] * (gain_sum / z.pixels))
    put_halves(half, value)
    from_matrix(z, half, (back_s, back_l))
    for d in range(C):
        lines[pl.ds(d, 1), :] = gathered[d]
    for ref, group in ((two, LAST_SECOND), (one, LAST_FIRST)):
        for a in range(TAPS):
            for b in range(TAPS):
                at = (group + a * TAPS + b) * C
                ref[a, b] = lines[:, pl.ds(at, C)]


def call(body, ins, outs, scratch=(), sems=0):
    space = {"v": pltpu.VMEM, "h": pltpu.HBM, "V": pltpu.VMEM}
    shapes = []
    for item in scratch:
        if isinstance(item, list):
            shapes.append([pltpu.VMEM(*s) for s in item])
        else:
            shapes.append(pltpu.VMEM(*item))
    if sems:
        shapes.append(pltpu.SemaphoreType.DMA((sems,)))
    run = pl.pallas_call(
        body,
        out_shape=[jax.ShapeDtypeStruct(shape, kind) if s == "v" else space[s](shape, kind) for s, shape, kind in outs],
        in_specs=[pl.BlockSpec(memory_space=space[s]) for s in ins],
        out_specs=[pl.BlockSpec(memory_space=space[s]) for s, _, _ in outs],
        scratch_shapes=shapes,
        compiler_params=pltpu.CompilerParams(vmem_limit_bytes=VMEM_LIMIT),
    )
    return lambda *args: run(
        *(pltpu.with_memory_space_constraint(arg, pltpu.HBM) if s == "h" else arg for s, arg in zip(ins, args))
    )


def exchange(lines, axes):
    shape = lines.shape
    if len(shape) == 2:
        lines = lines.reshape(math.prod(lax.axis_size(axis) for axis in axes), -1, 128)
    return lax.all_to_all(lines, axes, 0, 0, tiled=True).reshape(shape)


def beyond(z, pair, other, depths):
    hops = max(-(-depth // rows) for rows in z.rows for depth in depths)
    if hops == 1:
        swap = lambda value, start: lax.ppermute(
            value, "row", [(i + a, i + 1 - a) for i in range(start, z.peers - 1, 2) for a in (0, 1)]
        )
        others = swap(other, 1)
        return swap(pair, 0), others
    even = is_even()
    bottom, top = jnp.where(even, pair, other), jnp.where(even, other, pair)
    above, below = [], []
    for hop in range(1, hops + 1):
        above.append(lax.ppermute(bottom, "row", [(i, i + hop) for i in range(z.peers - hop)]))
        below.append(lax.ppermute(top, "row", [(i + hop, i) for i in range(z.peers - hop)]))
    up, down = [], []
    base = 0
    for depth in depths:
        for n in range(depth):
            for k in (1, 0):
                hop, back = divmod(depth - 1 - n, z.rows[k])
                at = base + (depth - 1 - back) * z.rims + z.rim[k]
                up.append(above[hop][at : at + z.edge[k]])
                hop, back = divmod(n, z.rows[k])
                at = base + back * z.rims + z.rim[k]
                down.append(below[hop][at : at + z.edge[k]])
        base += depth * z.rims
    up.append(jnp.concatenate([pixel_rows(z, above, base, 1, 1), pixel_rows(z, above, base, 0, 1)], axis=1))
    down.append(jnp.concatenate([pixel_rows(z, below, base, 0, 0), pixel_rows(z, below, base, 1, 0)], axis=1))
    up, down = jnp.concatenate(up, axis=0), jnp.concatenate(down, axis=0)
    return jnp.where(even, down, up), jnp.where(even, up, down)


def pixel_rows(z, bands, base, distance, last):
    lines = []
    for k in (0, 1):
        hop, back = divmod(distance, z.rows[k])
        at = base + k * z.images[0]
        half = 128 * abs(last - back)
        lines.append(bands[hop][at : at + z.images[k], half : half + 128])
    lines.append(jnp.zeros((z.slots - sum(z.images), 128), F32))
    return jnp.concatenate(lines, axis=0)


def local(
    image_small, image_large, teacher_small, teacher_large, upstream_small, upstream_large,
    conv_first, gain_first, bias_first, conv_second, gain_second, bias_second,
):
    peers = lax.axis_size("row")
    devices = lax.axis_size("img") * peers
    z = Sizes(image_small.shape, image_large.shape, devices, peers)
    body = lambda function: functools.partial(function, z)
    r = z.rims
    full, half, pair = (z.total, LANES), (2, z.total, 128), (2 * devices, 128)
    weight, left = (2, TAPS * TAP_ROWS, 128), (2, 256, 2 * z.total)
    images = [image_small, image_large, upstream_small, upstream_large, teacher_small, teacher_large]
    f = lambda space, *shape: (space, shape, F32)
    depths = (REACH, 2)
    rim_rows = sum(depths) * r + z.slots

    x, pair_edge, other_edge, copies = call(
        body(start_kernel),
        "hhhhhh",
        [("v", full, F32), f("v", rim_rows, LANES), f("v", rim_rows, LANES), ("V", pair, F32)],
        [[(a.shape, F32) for a in images], (half, F32)],
        4 + 2 * z.images[1],
    )(*images)
    gathered = exchange(copies, AXES)
    pair_rims, other_rims = beyond(z, pair_edge, other_edge, depths)
    params = [conv_first, conv_second] + images[2:]
    w1, w2, weights, affine, upstream, teacher, x_copy = call(
        body(prepare_kernel),
        "hhhhhhhhhhv",
        [("v", weight, BF16), ("v", weight, BF16), ("h", (3,) + weight, BF16), f("v", 5, LANES), ("h", full, F32), f("v", z.total, 128), ("h", full, F32)],
        [[(a.shape, F32) for a in params], ((2,) + weight, BF16), (full, F32), ((4, C), F32), (half, F32)],
        15,
    )(*params, *(v.reshape(1, C) for v in (gain_first, bias_first, gain_second, bias_second)), x)

    hidden, stats_one, copies = call(
        body(first_kernel),
        "vvvvvv",
        [("v", full, F32), f("v", 2, LANES), ("V", pair, F32)],
        [z.pads()],
    )(x, pair_rims, other_rims, gathered, affine, w1)
    gathered = exchange(copies, AXES)
    extended, near_rows = z.total + 4 * r, z.total + 2 * r
    h_above, h_below, left_one, packed, teachers, spread_u, near_u = call(
        body(first_operand_kernel),
        "vvvvvvvhh",
        [f("v", 3 * r, LANES), f("v", 3 * r, LANES), ("h", left, BF16), f("h", C, BACK_LANES), f("h", extended, LANES), f("h", near_rows, LANES), f("h", near_rows, LANES)],
        [
            z.pads(), z.chains(2), z.chains(REACH), (left, BF16), ((2,) + weight, BF16), ((near_rows, LANES), F32), ((extended, 128), F32),
            ((extended, LANES), F32), ((near_rows, LANES), F32), ((C, BACK_LANES), F32),
        ],
        8,
    )(x, hidden, pair_rims, other_rims, stats_one, affine, teacher, upstream, weights)
    gathered, near_u = lax.optimization_barrier((gathered, near_u))

    map_shape = (peers * z.slots, 128)
    out, o_above, o_below, near, stats_two, copies = call(
        body(second_kernel),
        "vvvvvvvvvv",
        [("v", full, F32), f("v", 2 * r, LANES), f("v", 2 * r, LANES), f("v", 2, r, LANES), f("v", 2, LANES), ("V", map_shape, F32)],
        [z.pads(), z.chains(3)],
    )(hidden, h_above, h_below, gathered, affine, w2, x, pair_rims, other_rims, teacher)
    gathered = exchange(copies, ("row",))
    out_copy, hidden_copy, left_two, shifts, by_map, by_teacher, up = call(
        body(second_operand_kernel),
        "vvvvvvvhhhh",
        [
            ("h", full, F32), f("h", near_rows, LANES), ("v", left, BF16), f("h", 3, near_rows, LANES),
            f("v", near_rows, LANES), f("v", near_rows, LANES), f("v", near_rows, LANES),
        ],
        [
            z.pads(), z.chains(2), ((extended, LANES), F32), ((near_rows, LANES), F32), (weight, BF16),
            ((3, near_rows, LANES), F32),
        ],
        14,
    )(hidden, near, stats_two, affine, out, o_above, o_below, teachers, spread_u, near_u, weights)

    dout, dshift, d_above, d_below, slabs = call(
        body(upstream_kernel),
        "vvhhvhvvhv",
        [("v", full, F32), ("v", full, F32), f("v", r, LANES), f("v", r, LANES), f("V", devices, 1, BACK_LANES)],
        [((3, near_rows, LANES), F32), (left, BF16), (full, F32), ((C, BACK_LANES), F32), z.pads(), z.pads()],
        7,
    )(gathered, up, shifts, left_one, left_two, packed, by_map, by_teacher, hidden_copy, stats_two)
    gathered = exchange(slabs, AXES)
    out_s, out_l, first_normed, second_normed, weight_back = call(
        body(write_kernel),
        "hhhhvvv",
        [("v", image_small.shape, F32), ("v", image_large.shape, F32), ("v", full, F32), f("v", near_rows, LANES), ("v", weight, BF16)],
        [(full, F32), (full, F32), ((near_rows, LANES), F32), (half, F32)],
        4,
    )(out_copy, x_copy, hidden_copy, weights, stats_one, stats_two, d_above)

    pre, gain_two, bias_two, slabs = call(
        body(hidden_kernel),
        "vvvvvvvvv",
        [("v", full, F32), f("v", 1, C), f("v", 1, C), f("V", devices, 1, LAST_LANES)],
        [z.pads()],
    )(gathered, dshift, d_above, d_below, second_normed, stats_two, affine, weight_back, first_normed)
    gathered = exchange(slabs, AXES)

    back_s, back_l, one, two, gain_one, bias_one = call(
        body(back_kernel),
        "vvvvvv",
        [("v", a.shape, F32) for a in (image_small, image_large, conv_first, conv_second)] + [f("v", 1, C), f("v", 1, C)],
        [(half, F32), ((C, LAST_LANES), F32)],
    )(gathered, pre, first_normed, stats_one, affine, dout)
    return (
        out_s, out_l, back_s, back_l,
        one, gain_one.reshape(C), bias_one.reshape(C),
        two, gain_two.reshape(C), bias_two.reshape(C),
    )


def solution(mesh):
    split_bands, everywhere = P("img", "row", None), P()
    return jax.shard_map(
        local,
        mesh=mesh,
        in_specs=(split_bands,) * 6 + (everywhere,) * 6,
        out_specs=(split_bands,) * 4 + (everywhere,) * 6,
        check_vma=False,
    )
```

```python
import functools
import math

import jax
import jax.numpy as jnp
from jax import lax
from jax.experimental import pallas as pl
from jax.experimental.pallas import tpu as pltpu
from jax.sharding import PartitionSpec as P

C = 32
HS = 32
HL = 64
HEIGHTS = (HS, HL)

norm_eps = 1e-05
map_eps = 1e-06
beta_weight = 1000.0
AXES = ("img", "row")
BLOCK = 8
LANES = BLOCK * C
TAPS = 3
DEPTH = TAPS * 128 + 256
TAP_ROWS = 128 + 2 * C
REACH = 4
ROOT = math.sqrt(2.0 / math.pi)
CUBE = 0.044715
F32 = jnp.float32
BF16 = jnp.bfloat16
VMEM_LIMIT = 32 * 1024 * 1024
BIAS, GAIN, SECOND, LEFT, HIDDEN, ONES = 0, 1, 2, 11, 20, 29
BACK_LANES = 1280
LAST_SECOND, LAST_FIRST, LAST_LANES = 2, 11, 640


class Sizes:
    def __init__(self, small, large, devices, peers):
        self.images = (small[0], large[0])
        self.rows = (small[1], large[1])
        self.blocks = (HS // BLOCK, HL // BLOCK)
        self.step = tuple(n * r for n, r in zip(self.images, self.rows))
        self.count = tuple(b * s for b, s in zip(self.blocks, self.step))
        self.edge = tuple(b * n for b, n in zip(self.blocks, self.images))
        self.start = (self.count[1], 0)
        self.rim = (self.edge[1], 0)
        self.total = sum(self.count)
        self.rims = sum(self.edge)
        self.slots = -(-sum(self.images) // 8) * 8
        self.guard = -(-max(self.images) // 8) * 8
        self.devices = devices
        self.peers = peers
        self.here = float(self.total * BLOCK)
        self.pixels = self.here * devices

    def pads(self):
        return [((TAPS, 2, self.count[k] + 2 * self.step[k], 128), F32) for k in (0, 1)]

    def chains(self, depth):
        return [((2, 2 * self.guard + (depth + 1) * self.rims, 128), F32)] * 2


def split(value):
    high = value.astype(BF16)
    return high, (value - high.astype(F32)).astype(BF16)


def dot(left, right):
    return lax.dot_general(left, right, (((1,), (0,)), ((), ())), preferred_element_type=F32)


def product(left, right):
    if left[0].shape[1] % 128:
        return dot(left[0], right[0]) + (dot(left[0], right[1]) + dot(left[1], right[0]))
    return dot(
        jnp.concatenate([left[0], left[0], left[1]], axis=1), jnp.concatenate([right[0], right[1], right[0]], axis=0)
    )


def spread(left, right):
    right = right.astype(BF16)
    return dot(jnp.concatenate(split(left), axis=1), jnp.concatenate([right, right], axis=0))


def gelu(s):
    return 0.5 * s * (1.0 + jnp.tanh(ROOT * (s + CUBE * s * s * s)))


def gelu_slope(s):
    square = s * s
    t = jnp.tanh(ROOT * s * (1.0 + CUBE * square))
    return 0.5 * (1.0 + t) + 0.5 * s * (1.0 - t * t) * ROOT * (1.0 + 3.0 * CUBE * square)


def spread_groups(row):
    row = row + pltpu.roll(row, 64, 1)
    return row + pltpu.roll(row, 32, 1)


def fold(row):
    return spread_groups(row[:, :128] + row[:, 128:])


def wide(row):
    return jnp.concatenate([row, row], axis=1)


def group_of(rows=1, lanes=128):
    return lax.broadcasted_iota(jnp.int32, (rows, lanes), 1) // C


def column_sum(value):
    return jnp.sum(value, axis=0, keepdims=True)


def send_lines(z, ref, lines):
    for n, line in enumerate(lines):
        ref[pl.ds(n, z.devices, stride=len(lines)), :] = jnp.broadcast_to(line, (z.devices, 128))


def moments(z, value, ref):
    few = min(8, z.total)
    pivot = fold(column_sum(value[:few])) / float(few * BLOCK)
    off = value - wide(pivot)
    first, second = fold(column_sum(off)), fold(column_sum(off * off))
    send_lines(z, ref, [pivot + first / z.here, second - first * first / z.here])


def merged(z, ref):
    means = ref[pl.ds(0, z.devices, stride=2), :]
    center = jnp.mean(means, axis=0, keepdims=True)
    off = means - center
    within = jnp.mean(ref[pl.ds(1, z.devices, stride=2), :], axis=0, keepdims=True)
    variance = within / z.here + jnp.mean(off * off, axis=0, keepdims=True)
    return wide(center), wide(lax.rsqrt(variance + norm_eps))


def put_halves(ref, value):
    ref[0] = value[:, :128]
    ref[1] = value[:, 128:]


def whole(ref):
    return jnp.concatenate([ref[0], ref[1]], axis=1)


def to_matrix(z, refs, half):
    for k in (0, 1):
        for j in range(z.blocks[k]):
            at = z.start[k] + j * z.step[k]
            for i in range(z.images[k]):
                for h in (0, 1):
                    half[h, pl.ds(at + i * z.rows[k], z.rows[k]), :] = refs[k][i, :, pl.ds(LANES * j + 128 * h, 128)]


def from_matrix(z, half, refs):
    for k in (0, 1):
        for j in range(z.blocks[k]):
            at = z.start[k] + j * z.step[k]
            for i in range(z.images[k]):
                for h in (0, 1):
                    refs[k][i, :, pl.ds(LANES * j + 128 * h, 128)] = half[h, pl.ds(at + i * z.rows[k], z.rows[k]), :]


def is_even():
    return lax.axis_index("row") % 2 == 0


def put_edges(pair, other, at, last, first):
    even = is_even()
    pair[at] = jnp.where(even, last, first)
    other[at] = jnp.where(even, first, last)


def above_of(pair, other, at):
    return jnp.where(is_even(), other[at], pair[at])


def below_of(pair, other, at):
    return jnp.where(is_even(), pair[at], other[at])


def take_rims(z, half, depth, pair, other):
    everything = pl.ds(0, 128)
    for k in (0, 1):
        nothing = jnp.zeros((z.edge[k], 128), F32)
        for n in range(depth):
            first, last = nothing, nothing
            if depth - n <= z.rows[k]:
                last = half[pl.ds(z.start[k] + z.rows[k] - depth + n, z.edge[k], stride=z.rows[k]), :]
            if n < z.rows[k]:
                first = half[pl.ds(z.start[k] + n, z.edge[k], stride=z.rows[k]), :]
            put_edges(pair, other, (pl.ds(n * z.rims + z.rim[k], z.edge[k]), everything), last, first)


def inside(z, depth, above):
    at = lax.axis_index("row")
    large = lax.broadcasted_iota(jnp.int32, (z.rims, 1), 0) < z.rim[0]
    parts = []
    for n in range(depth):
        if above:
            ok = [jnp.where(at * rows >= depth - n, 1.0, 0.0) for rows in z.rows]
        else:
            ok = [jnp.where((at + 1) * rows + n + 1 <= height, 1.0, 0.0) for rows, height in zip(z.rows, HEIGHTS)]
        parts.append(jnp.where(large, ok[1], ok[0]).astype(F32))
    return jnp.concatenate(parts, axis=0)


def clear_guards(z, pads, a):
    for k in (0, 1):
        pads[k][a, 1, pl.ds(0, z.step[k]), :] = jnp.zeros((z.step[k], 128), F32)
        pads[k][a, 0, pl.ds(z.step[k] + z.count[k], z.step[k]), :] = jnp.zeros((z.step[k], 128), F32)


def fill_center(z, pads, value):
    clear_guards(z, pads, 1)
    for k in (0, 1):
        for h in (0, 1):
            pads[k][1, h, pl.ds(z.step[k], z.count[k]), :] = value[z.start[k] : z.start[k] + z.count[k], 128 * h : 128 * h + 128]


def fill_shifted(z, pads, above, below):
    for k in (0, 1):
        ref, step, count, rows = pads[k], z.step[k], z.count[k], z.rows[k]
        rim = slice(z.rim[k], z.rim[k] + z.edge[k])
        for h in (0, 1):
            lanes = slice(128 * h, 128 * h + 128)
            ref[0, h, pl.ds(step, count), :] = ref[1, h, pl.ds(step - 1, count), :]
            ref[2, h, pl.ds(step, count), :] = ref[1, h, pl.ds(step + 1, count), :]
            ref[0, h, pl.ds(step, z.edge[k], stride=rows), :] = above[rim, lanes]
            ref[2, h, pl.ds(step + rows - 1, z.edge[k], stride=rows), :] = below[rim, lanes]


def fill_pads(z, pads, value, above, below):
    fill_center(z, pads, value)
    fill_shifted(z, pads, above, below)
    for a in (0, 2):
        clear_guards(z, pads, a)


def beside(left, right):
    lane = lax.broadcasted_iota(jnp.int32, (1, 128), 1)
    middle = pltpu.roll(jnp.where(lane >= 64, left[1], right[1]), 64, 1)
    return [
        jnp.where(lane >= 96, left[0], jnp.where(lane < 32, right[0], middle)),
        jnp.where(lane >= 96, left[2], jnp.where(lane < 32, right[2], 0.0)),
    ]


def band_operand(z, pads):
    parts = ([], [])
    for k in (1, 0):
        ref, step, count = pads[k], z.step[k], z.count[k]
        low, high = ([ref[a, h, pl.ds(step, count), :] for a in range(TAPS)] for h in (0, 1))
        before = [ref[a, 1, pl.ds(0, count), :] for a in range(TAPS)]
        after = [ref[a, 0, pl.ds(2 * step, count), :] for a in range(TAPS)]
        parts[0].append(jnp.concatenate(low + beside(before, high), axis=1))
        parts[1].append(jnp.concatenate(high + beside(low, after), axis=1))
    return [jnp.concatenate(part, axis=0) for part in parts]


def rim_operand(z, chain, depth):
    m = lax.broadcasted_iota(jnp.int32, (z.rims, 1), 0)
    large = m < z.rim[0]
    has_before = jnp.where(large, m, m - z.rim[0]) >= jnp.where(large, z.images[1], z.images[0])
    has_after = m < jnp.where(large, z.rim[0] - z.images[1], z.rims - z.images[0])
    low, high, before, after = [], [], [], []
    for r in range(depth + 1):
        at = z.guard + r * z.rims
        low.append(chain[0, pl.ds(at, z.rims), :])
        high.append(chain[1, pl.ds(at, z.rims), :])
        shifted = [chain[1, pl.ds(at - images, z.rims), :] for images in z.images]
        before.append(jnp.where(has_before, jnp.where(large, shifted[1], shifted[0]), 0.0))
        shifted = [chain[0, pl.ds(at + images, z.rims), :] for images in z.images]
        after.append(jnp.where(has_after, jnp.where(large, shifted[1], shifted[0]), 0.0))
    parts = ([], [])
    for n in range(depth - 1):
        rows = slice(n, n + TAPS)
        parts[0].append(jnp.concatenate(low[rows] + beside(before[rows], high[rows]), axis=1))
        parts[1].append(jnp.concatenate(high[rows] + beside(low[rows], after[rows]), axis=1))
    return [jnp.concatenate(part, axis=0) for part in parts]


def times(parts, weight):
    left = jnp.concatenate([part[h] for h in (0, 1) for part in parts], axis=0)
    both = jnp.concatenate([weight_matrix(weight.at[0]), weight_matrix(weight.at[1])], axis=1)
    result = dot(jnp.concatenate(split(left), axis=1), jnp.concatenate([both, both], axis=0))
    result = result[:, :128] + result[:, 128:]
    rows = result.shape[0] // 2
    return jnp.concatenate([result[:rows], result[rows:]], axis=1)


def rim_operands(z, pads, above, below, depth, chains):
    parts = []
    for side, (rim, chain) in enumerate(zip((above, below), chains)):
        rim_at, own_at = (z.guard, z.guard + depth * z.rims) if side == 0 else (z.guard + z.rims, z.guard)
        for h in (0, 1):
            chain[h, pl.ds(rim_at, depth * z.rims), :] = rim[:, 128 * h : 128 * h + 128]
            for k in (0, 1):
                row = z.step[k] + (0 if side == 0 else z.rows[k] - 1)
                chain[h, pl.ds(own_at + z.rim[k], z.edge[k]), :] = pads[k][1, h, pl.ds(row, z.edge[k], stride=z.rows[k]), :]
        parts.append(rim_operand(z, chain, depth))
    return parts


def convolve(z, own, above, below, depth, pads, chains, weight):
    r = z.rims
    fill_pads(z, pads, own, above[(depth - 1) * r :], below[:r])
    parts = [band_operand(z, pads)]
    if depth > 1:
        parts += rim_operands(z, pads, above, below, depth, chains)
    result = times(parts, weight)
    n = z.total + (depth - 1) * r
    return result[: z.total], result[z.total : n], result[n:]


def convolve_rims(z, pads, above, below, depth, chains, weight):
    result = times(rim_operands(z, pads, above, below, depth, chains), weight)
    n = (depth - 1) * z.rims
    return result[:n], result[n:]


def image_sums(z, value):
    slot = lax.broadcasted_iota(jnp.int32, (z.slots, 1), 0)
    sums = jnp.zeros((z.slots, 128), F32)
    for k in (0, 1):
        line = value[z.start[k] : z.start[k] + z.step[k]]
        for j in range(1, z.blocks[k]):
            at = z.start[k] + j * z.step[k]
            line = line + value[at : at + z.step[k]]
        image = lax.broadcasted_iota(jnp.int32, (z.step[k], 1), 0) // z.rows[k]
        for i in range(z.images[k]):
            sums = jnp.where(slot == i + k * z.images[0], column_sum(jnp.where(image == i, line, 0.0)), sums)
    return sums


def image_rows(z, values, rims):
    parts = []
    for k in (1, 0):
        image = lax.broadcasted_iota(jnp.int32, (z.step[k], 1), 0) // z.rows[k]
        line = jnp.zeros((z.step[k], 128), F32)
        for i in range(z.images[k]):
            at = i + k * z.images[0]
            line = jnp.where(image == i, values[at : at + 1], line)
        parts += [line] * z.blocks[k]
    if rims:
        m = lax.broadcasted_iota(jnp.int32, (z.rims, 1), 0)
        image = jnp.where(m < z.rim[0], z.images[0] + m % z.images[1], (m - z.rim[0]) % z.images[0])
        line = jnp.zeros((z.rims, 128), F32)
        for at in range(sum(z.images)):
            line = jnp.where(image == at, values[at : at + 1], line)
        parts += [line] * rims
    return jnp.concatenate(parts, axis=0)


def channel_mean():
    a = lax.broadcasted_iota(jnp.int32, (LANES, 128), 0) // C
    b = lax.broadcasted_iota(jnp.int32, (LANES, 128), 1) % 64
    return jnp.where(a == b, 1.0 / C, 0.0).astype(F32)


def to_channels():
    a = lax.broadcasted_iota(jnp.int32, (128, LANES), 0)
    b = lax.broadcasted_iota(jnp.int32, (128, LANES), 1) // C
    return jnp.where(a == b, 1.0, 0.0).astype(F32)


def attention(value):
    return spread(value * value, channel_mean())


def pieces(source, target):
    return [(source.at[n], target.at[n]) for n in range(source.shape[0])]


def copies_of(pairs, sems, first=0):
    return [pltpu.make_async_copy(a, b, sems.at[first + n]) for n, (a, b) in enumerate(pairs)]


def start_all(copies):
    for copy in copies:
        copy.start()


def wait_all(copies):
    for copy in copies:
        copy.wait()


def start_kernel(z, small, large, up_s, up_l, t_s, t_l, x, pair, other, copies, raw, half, sems):
    images = [(small, raw[0])] + pieces(large, raw[1])
    rest = [(up_s, raw[2])] + pieces(up_l, raw[3]) + [(t_s, raw[4]), (t_l, raw[5])]
    loads = copies_of(images + rest, sems)
    start_all(loads)
    r, n = z.rims, REACH * z.rims
    tail = n + 2 * r
    for ref in (pair, other):
        ref[pl.ds(tail, z.slots), :] = jnp.zeros((z.slots, LANES), F32)
    wait_all(loads[: len(images)])
    to_matrix(z, raw[:2], half)
    value = whole(half)
    x[...] = value
    moments(z, value, copies)
    for h in (0, 1):
        lanes = pl.ds(128 * h, 128)
        take_rims(z, half.at[h], REACH, pair.at[pl.ds(0, n), lanes], other.at[pl.ds(0, n), lanes])
    wait_all(loads[len(images) :])
    for k in (0, 1):
        width, rows = HEIGHTS[k], z.rows[k]
        for i in range(z.images[k]):
            slot = pl.ds(tail + i + k * z.images[0], 1)
            for d in (0, 1):
                has_last, has_first = rows + d >= 2, d < rows
                last, first = pl.ds(max(rows - 2 + d, 0), 1), pl.ds(min(d, rows - 1), 1)
                for j in range(z.blocks[k]):
                    lanes = pl.ds(LANES * j, LANES)
                    at = (pl.ds(n + d * r + z.rim[k] + j * z.images[k] + i, 1), pl.ds(0, LANES))
                    nothing = jnp.zeros((1, LANES), F32)
                    put_edges(
                        pair, other, at,
                        raw[2 + k][i, last, lanes] if has_last else nothing,
                        raw[2 + k][i, first, lanes] if has_first else nothing,
                    )
                nothing = jnp.zeros((1, width), F32)
                put_edges(
                    pair, other, (slot, pl.ds(128 * d, width)),
                    raw[4 + k][i, last, :] if has_last else nothing,
                    raw[4 + k][i, first, :] if has_first else nothing,
                )


def banded(taps, ref):
    row = lax.broadcasted_iota(jnp.int32, (128, 128), 0) // C
    lane = group_of(128)
    for a in range(TAPS):
        main = jnp.zeros((128, 128), F32)
        for b in range(TAPS):
            main = jnp.where(row - lane + 1 == b, taps[a][b], main)
        before = jnp.where(lane[:C] == 0, taps[a][0][:C], 0.0)
        after = jnp.where(lane[:C] == 3, taps[a][2][:C], 0.0)
        for n, part in enumerate(split(jnp.concatenate([main, before, after], axis=0))):
            ref[n, pl.ds(a * TAP_ROWS, TAP_ROWS), :] = part


def weight_matrix(ref):
    main = [ref[pl.ds(a * TAP_ROWS, 128), :] for a in range(TAPS)]
    before, after = ([ref[pl.ds(a * TAP_ROWS + 128 + n * C, C), :] for a in range(TAPS)] for n in (0, 1))
    return jnp.concatenate(
        main + [after[0], before[1], after[1], before[0], after[2], jnp.zeros((2 * C, 128), BF16), before[2]], axis=0
    )


def prepare_kernel(z, first, second, up_s, up_l, t_s, t_l, g1, b1, g2, b2, x, w1, w2, weights, affine, upstream, teacher, x_copy, raw, kept, kept_u, rows, half, sems):
    targets = tuple(raw) + tuple(rows.at[pl.ds(n, 1), :] for n in range(4))
    refs = (first, second, up_s, up_l, t_s, t_l, g1, b1, g2, b2)
    loads = [pltpu.make_async_copy(a, b, sems.at[n]) for n, (a, b) in enumerate(zip(refs, targets))]
    start_all(loads)
    stores = [pltpu.make_async_copy(x, x_copy, sems.at[13])]
    stores[0].start()
    wait_all(loads)
    to_matrix(z, raw[2:4], half)
    kept_u[...] = whole(half)
    stores.append(pltpu.make_async_copy(kept_u, upstream, sems.at[10]))
    stores[1].start()
    for n, (source, forward) in enumerate(zip(raw[:2], (w1, w2))):
        tiles = []
        for a in range(TAPS):
            line = [jnp.concatenate([source[a, b]] * 4, axis=1) for b in range(TAPS)]
            tiles.append([jnp.concatenate([tap] * 4, axis=0) for tap in line])
        turned = [[tiles[TAPS - 1 - a][TAPS - 1 - b].T for b in range(TAPS)] for a in range(TAPS)]
        banded(tiles, forward)
        if n == 0:
            stores.append(pltpu.make_async_copy(forward, weights.at[2], sems.at[14]))
            stores[-1].start()
        banded(turned, kept.at[n])
        stores.append(pltpu.make_async_copy(kept.at[n], weights.at[n], sems.at[11 + n]))
        stores[-1].start()
    taps = sum(raw[0][a, b] for a in range(TAPS) for b in range(TAPS))
    pivot = dot(jnp.broadcast_to(gelu(rows[1:2]), (8, C)), taps)[0:1]
    affine[...] = jnp.concatenate([jnp.concatenate([rows[...], pivot], axis=0)] * BLOCK, axis=1)
    teacher[...] = jnp.zeros(teacher.shape, F32)
    for k, ref in ((0, raw[4]), (1, raw[5])):
        for i in range(z.images[k]):
            line = ref[i]
            for j in range(z.blocks[k]):
                at = z.start[k] + j * z.step[k] + i * z.rows[k]
                for lane in (0, 64):
                    teacher[pl.ds(at, z.rows[k]), pl.ds(lane, BLOCK)] = line[:, j * BLOCK : (j + 1) * BLOCK]
    wait_all(stores)


def normed_by(stats):
    return lambda v: (v - stats[0:1]) * stats[1:2]


def activation(center, scale, gain, bias):
    factor = scale * gain
    offset = bias - center * factor
    return lambda v: gelu(v * factor + offset)


def first_kernel(z, x, pair, other, gathered, affine, weight, hidden, stats, copies, pads):
    center, scale = merged(z, gathered)
    act = activation(center, scale, affine[0:1], affine[1:2])
    r, lanes = z.rims, pl.ds(0, LANES)
    up = act(above_of(pair, other, (pl.ds((REACH - 1) * r, r), lanes))) * inside(z, 1, True)
    down = act(below_of(pair, other, (pl.ds(0, r), lanes))) * inside(z, 1, False)
    own, _, _ = convolve(z, act(x[...]), up, down, 1, pads, None, weight)
    moments(z, own, copies)
    hidden[...] = own
    stats[0:1] = center
    stats[1:2] = scale


def second_kernel(z, hidden, h_above, h_below, gathered, affine, weight, x, pair, other, teacher, out, o_above, o_below, near, stats, copies, pads, chains):
    center, scale = merged(z, gathered)
    act = activation(center, scale, affine[2:3], affine[3:4])
    r = z.rims
    own = act(hidden[...])
    up, down = act(h_above[...]) * inside(z, 3, True), act(h_below[...]) * inside(z, 3, False)
    own, up, down = convolve(z, own, up, down, 3, pads, chains, weight)
    own = x[...] + own
    amap = attention(own)
    lane = lax.broadcasted_iota(jnp.int32, (1, 128), 1)
    sums = image_sums(z, amap * jnp.where(lane < 64, amap, teacher[...]))
    copies[...] = jnp.concatenate([sums] * z.peers, axis=0)
    out[...] = own
    o_above[...] = above_of(pair, other, (pl.ds(2 * r, 2 * r), pl.ds(0, LANES))) + up
    o_below[...] = below_of(pair, other, (pl.ds(0, 2 * r), pl.ds(0, LANES))) + down
    near[0] = h_above[pl.ds(2 * r, r), :]
    near[1] = h_below[pl.ds(0, r), :]
    stats[0:1] = center
    stats[1:2] = scale


def tap_rows(q):
    return 128 + C if q < 0 else q * C


def tap_product(z, operand, own, above, below, pads):
    fill_center(z, pads, own)
    fill_shifted(z, pads, above, below)
    columns = []
    for a in range(TAPS):
        columns.append(
            jnp.concatenate([pads[k][TAPS - 1 - a, h, pl.ds(z.step[k], z.count[k]), :] for h in (0, 1) for k in (1, 0)], axis=0)
        )
    used = [jnp.concatenate([operand[n, pl.ds(0, 128 + C), :], operand[n, pl.ds(256 - C, C), :]], axis=0) for n in (0, 1)]
    return product(used, split(jnp.concatenate(columns, axis=1)))


def tap_sums(result, tiles, first_group):
    group = group_of()
    for a in range(TAPS):
        for b in range(TAPS):
            total = None
            for p in range(4):
                at = tap_rows(p + b - 1)
                part = result[at : at + C, 128 * a : 128 * a + 128]
                total = part if total is None else jnp.where(group == p, part, total)
            tile, slot = divmod(first_group + a * TAPS + b, 4)
            tiles[tile] = jnp.where(group == slot, spread_groups(total), tiles[tile])


def tap_counts(z, turned, tiles, first_group):
    group = group_of()
    m = lax.broadcasted_iota(jnp.int32, (1, 2 * z.total), 1) % z.total
    row = jnp.where(m < z.start[0], m % z.rows[1], (m - z.start[0]) % z.rows[0])
    height = jnp.where(m < z.start[0], z.rows[1], z.rows[0])
    at = lax.axis_index("row")
    lost = {
        0: (row == height - 1) & (at == z.peers - 1),
        2: (row == 0) & (at == 0),
    }
    for a in range(TAPS):
        column = jnp.sum(jnp.where(lost[a], 0.0, turned) if a in lost else turned, axis=1, keepdims=True)
        used = jnp.concatenate([column[: 128 + C], column[256 - C :]], axis=0)
        for b in range(TAPS):
            total = sum(used[tap_rows(p + b - 1) : tap_rows(p + b - 1) + C] for p in range(4))
            tile, slot = divmod(first_group + a * TAPS + b, 4)
            tiles[tile] = jnp.where(group == slot, total, tiles[tile])


def turned_operand(z, value, pads, kept):
    fill_center(z, pads, value)
    lane = lax.broadcasted_iota(jnp.int32, (1, 128), 1)
    halves = ([], [])
    for k in (1, 0):
        ref, step, count = pads[k], z.step[k], z.count[k]
        low, high = ref[1, 0, pl.ds(step, count), :], ref[1, 1, pl.ds(step, count), :]
        before, after = ref[1, 1, pl.ds(0, count), :], ref[1, 0, pl.ds(2 * step, count), :]
        for part, main, left, right in ((halves[0], low, before, high), (halves[1], high, low, after)):
            part.append(jnp.concatenate([main, jnp.where(lane >= 96, left, jnp.where(lane < 32, right, 0.0))], axis=1))
    turned = jnp.concatenate(halves[0] + halves[1], axis=0).T
    parts = split(turned)
    for n in (0, 1):
        kept[n] = parts[n]
    return turned


def first_operand_kernel(z, x, hidden, pair, other, stats, affine, teacher, upstream, weights, h_above, h_below, left, packed, teachers, spread_u, near_u, pads, chains, deep_chains, kept, kept_w, kept_u, pixels, kept_t, kept_c, kept_packed, sems):
    r, own = z.rims, pl.ds(0, z.total)
    loads = copies_of([(upstream, kept_u.at[own, :]), (weights.at[1], kept_w.at[1])], sems)
    first = pltpu.make_async_copy(weights.at[2], kept_w.at[0], sems.at[7])
    first.start()
    start_all(loads)
    act = activation(stats[0:1], stats[1:2], affine[0:1], affine[1:2])
    value = turned_operand(z, act(x[...]), pads, kept)
    stores = [pltpu.make_async_copy(kept, left, sems.at[2])]
    stores[0].start()
    n, lanes = REACH * r, pl.ds(0, LANES)
    up = act(above_of(pair, other, (pl.ds(0, n), lanes))) * inside(z, REACH, True)
    down = act(below_of(pair, other, (pl.ds(0, n), lanes))) * inside(z, REACH, False)
    first.wait()
    up, down = convolve_rims(z, pads, up, down, REACH, deep_chains, kept_w.at[0])
    h_above[...] = up
    h_below[...] = down
    tiles = [jnp.zeros((C, 128), F32) for _ in range(BACK_LANES // 128)]
    tap_counts(z, value, tiles, ONES)
    pivot = affine[4:5]
    result = tap_product(
        z, kept, hidden[...] - pivot, (up[2 * r :] - pivot) * inside(z, 1, True),
        (down[:r] - pivot) * inside(z, 1, False), pads,
    )
    tap_sums(result, tiles, HIDDEN)
    kept_packed[...] = jnp.concatenate(tiles, axis=1)
    stores.append(pltpu.make_async_copy(kept_packed, packed, sems.at[6]))
    stores[1].start()
    pixels[own, :] = teacher[...]
    pixels[pl.ds(z.total, 4 * r), :] = jnp.zeros((4 * r, 128), F32)
    n = (REACH + 2) * r
    for side, beyond_of in enumerate((above_of, below_of)):
        for d in (0, 1):
            for k in (0, 1):
                line = beyond_of(pair, other, (pl.ds(n + k * z.images[0], z.images[k]), pl.ds(128 * d, 128)))
                for j in range(z.blocks[k]):
                    at = z.total + (2 * side + d) * r + z.rim[k] + j * z.images[k]
                    pixels[pl.ds(at, z.images[k]), pl.ds(0, BLOCK)] = line[:, j * BLOCK : (j + 1) * BLOCK]
    kept_t[...] = spread(pixels[...], to_channels())
    stores.append(pltpu.make_async_copy(kept_t, teachers, sems.at[3]))
    stores[2].start()
    n = REACH * r
    at = (pl.ds(n, 2 * r), pl.ds(0, LANES))
    up, down = above_of(pair, other, at) * inside(z, 2, True), below_of(pair, other, at) * inside(z, 2, False)
    kept_u[pl.ds(z.total, r), :] = up[r:]
    kept_u[pl.ds(z.total + r, r), :] = down[:r]
    wait_all(loads)
    stores.append(pltpu.make_async_copy(kept_u, near_u, sems.at[5]))
    stores[3].start()
    kept_c[...] = jnp.concatenate(convolve(z, kept_u[own, :], up, down, 2, pads, chains, kept_w.at[1]), axis=0)
    stores.append(pltpu.make_async_copy(kept_c, spread_u, sems.at[4]))
    stores[4].start()
    wait_all(stores)


def second_operand_kernel(z, hidden, near, stats, affine, out, o_above, o_below, teachers, spread_u, near_u, weights, out_copy, hidden_copy, left, shifts, by_map, by_teacher, up, pads, chains, kept_t, kept_u, kept_w, kept_s, sems):
    r, total = z.rims, z.total
    loads = [
        pltpu.make_async_copy(teachers, kept_t, sems.at[0]),
        pltpu.make_async_copy(weights.at[1], kept_w, sems.at[1]),
        pltpu.make_async_copy(spread_u, kept_u, sems.at[2]),
    ]
    start_all(loads)
    stores = [
        pltpu.make_async_copy(out, out_copy, sems.at[4]),
        pltpu.make_async_copy(hidden, hidden_copy.at[pl.ds(0, total), :], sems.at[7]),
        pltpu.make_async_copy(near.at[0], hidden_copy.at[pl.ds(total, r), :], sems.at[8]),
        pltpu.make_async_copy(near.at[1], hidden_copy.at[pl.ds(total + r, r), :], sems.at[9]),
        pltpu.make_async_copy(near_u, up, sems.at[10]),
    ]
    start_all(stores)
    normed = normed_by(stats)(jnp.concatenate([hidden[...], near[0], near[1]], axis=0))
    shifted = normed * affine[2:3] + affine[3:4]
    turned_operand(z, gelu(shifted[:total]), pads, left)
    ones = jnp.ones((total, 1), F32)
    masks = jnp.concatenate([ones, inside(z, 1, True), inside(z, 1, False)], axis=0)
    slopes = gelu_slope(shifted) * masks
    o = jnp.concatenate([out[...], o_above[...] * inside(z, 2, True), o_below[...] * inside(z, 2, False)], axis=0)
    for_map = spread(attention(o), to_channels()) * o
    wait_all(loads)
    for_teacher = kept_t[...] * o
    kept_s[0] = kept_u[...] * slopes
    stores += copies_of(pieces(kept_s, shifts), sems, 11)
    stores[-3].start()
    for n, value, ref in ((1, for_map, by_map), (2, for_teacher, by_teacher)):
        own, before, after = value[:total], value[total : total + 2 * r], value[total + 2 * r :]
        ref[...] = jnp.concatenate([own, before[r:], after[:r]], axis=0)
        kept_s[n] = jnp.concatenate(convolve(z, own, before, after, 2, pads, chains, kept_w), axis=0) * slopes
        stores[n - 3].start()
    wait_all(stores)


def upstream_kernel(z, gathered, up, shifts, left_1, left_2, packed, by_map, by_teacher, hidden, stats, dout, dshift, d_above, d_below, slabs, kept_s, kept_left, kept_h, kept_packed, pads, more_pads, sems):
    r, total = z.rims, z.total
    loads = copies_of(
        pieces(shifts, kept_s) + pieces(left_1, kept_left) + [(hidden.at[pl.ds(0, total), :], kept_h), (packed, kept_packed)], sems
    )
    start_all(loads)
    lane = lax.broadcasted_iota(jnp.int32, (z.slots, 128), 1)
    sums = sum(gathered[pl.ds(n * z.slots, z.slots), :] for n in range(z.peers))
    square = jnp.sum(jnp.where(lane < 64, sums, 0.0), axis=1, keepdims=True)
    cross = jnp.sum(jnp.where(lane < 64, 0.0, sums), axis=1, keepdims=True)
    inverse = lax.rsqrt(square + map_eps)
    inner = beta_weight * (square * inverse - cross) * inverse
    shape = (z.slots, 128)
    for_map = (beta_weight - inner) * inverse * inverse * (2.0 / C)
    for_teacher = beta_weight * inverse * (2.0 / C)
    for_map, for_teacher = (wide(image_rows(z, jnp.broadcast_to(v, shape), 2)) for v in (for_map, for_teacher))
    value = up[...] + for_map * by_map[...] - for_teacher * by_teacher[...]
    dout[...] = value[:total]
    wait_all(loads[:3])
    shift = kept_s[0] + for_map * kept_s[1] - for_teacher * kept_s[2]
    pre, above, below = shift[:total], shift[total : total + r], shift[total + r :]
    dshift[...] = pre
    d_above[...] = above
    d_below[...] = below
    second = tap_product(z, left_2, value[:total], value[total : total + r], value[total + r :], pads)
    wait_all(loads[3:5])
    first = tap_product(z, kept_left, pre, above, below, more_pads)
    wait_all(loads[5:])
    normed = normed_by(stats)(kept_h[...])
    tiles = [kept_packed[:, 128 * n : 128 * n + 128] for n in range(BACK_LANES // 128)]
    group = group_of()
    tiles[0] = jnp.where(group == BIAS, fold(column_sum(pre)), jnp.where(group == GAIN, fold(column_sum(pre * normed)), tiles[0]))
    tap_sums(second, tiles, SECOND)
    tap_sums(first, tiles, LEFT)
    line = jnp.concatenate(tiles, axis=1)
    for d in range(z.devices):
        slabs[d] = line[d % C : d % C + 1]


def write_kernel(z, out, x, hidden, weights, first_stats, stats, order, out_s, out_l, first_normed, normed, weight, kept, kept_x, kept_h, half, sems):
    loads = [pltpu.make_async_copy(a, b, sems.at[n]) for n, (a, b) in enumerate(((out, kept), (x, kept_x), (hidden, kept_h), (weights.at[0], weight)))]
    start_all(loads)
    loads[0].wait()
    put_halves(half, kept[...])
    from_matrix(z, half, (out_s, out_l))
    loads[1].wait()
    first_normed[...] = normed_by(first_stats)(kept_x[...])
    loads[2].wait()
    normed[...] = normed_by(stats)(kept_h[...])
    loads[3].wait()


def norm_sums(total):
    group = group_of()
    return [wide(spread_groups(jnp.where(group == n, total[:, :128], 0.0))) for n in (BIAS, GAIN)]


def hidden_kernel(z, gathered, dshift, d_above, d_below, second_normed, stats, affine, weight, first_normed, pre_ref, norm_grads, slabs, pads):
    total = jnp.sum(gathered[...], axis=0)
    bias_sum, gain_sum = norm_sums(total)
    norm_grads[0:1] = bias_sum[:, :128]
    norm_grads[1:2] = gain_sum[:, :128]
    bias_mean, gain_mean = bias_sum / z.pixels, gain_sum / z.pixels
    factor = affine[2:3] * stats[1:2]
    r, total_rows = z.rims, z.total

    def back(d, normed):
        return factor * (d - bias_mean - normed * gain_mean)

    own = back(dshift[...], second_normed[pl.ds(0, total_rows), :])
    up = back(d_above[...], second_normed[pl.ds(total_rows, r), :]) * inside(z, 1, True)
    down = back(d_below[...], second_normed[pl.ds(total_rows + r, r), :]) * inside(z, 1, False)
    grad, _, _ = convolve(z, own, up, down, 1, pads, None, weight)
    normed = first_normed[...]
    pre = grad * gelu_slope(normed * affine[0:1] + affine[1:2])
    pre_ref[...] = pre
    lane = lax.broadcasted_iota(jnp.int32, (1, 128), 1)
    taps = TAPS * TAPS * C

    def along(row):
        return jnp.concatenate([row[:, :128]] * 3, axis=1)[:, :taps]

    second, left, against, ones = (total[:, n * C : n * C + taps] for n in (SECOND, LEFT, HIDDEN, ONES))
    against = along(stats[1:2]) * (against - along(stats[0:1] - affine[4:5]) * ones)
    first = along(factor) * (left - along(bias_mean) * ones - along(gain_mean) * against)
    sums = jnp.where(lane < C, fold(column_sum(pre)), fold(column_sum(pre * normed)))
    line = jnp.concatenate([sums[:, : 2 * C], second, first], axis=1)
    slabs[...] = jnp.broadcast_to(line[None], slabs.shape)


def back_kernel(z, gathered, pre, normed, stats, affine, dout, second_grads, back_s, back_l, one, two, gain_out, bias_out, second_gain, second_bias, half, lines):
    bias_sum, gain_sum = norm_sums(jnp.sum(gathered[:, :, pl.ds(0, 128)], axis=0))
    bias_out[...] = bias_sum[:, :C]
    gain_out[...] = gain_sum[:, :C]
    second_bias[...] = second_grads[0:1, pl.ds(0, C)]
    second_gain[...] = second_grads[1:2, pl.ds(0, C)]
    value = dout[...] + affine[0:1] * stats[1:2] * (pre[...] - bias_sum / z.pixels - normed[...] * (gain_sum / z.pixels))
    put_halves(half, value)
    from_matrix(z, half, (back_s, back_l))
    for d in range(C):
        lines[pl.ds(d, 1), :] = gathered[d]
    for ref, group in ((two, LAST_SECOND), (one, LAST_FIRST)):
        for a in range(TAPS):
            for b in range(TAPS):
                at = (group + a * TAPS + b) * C
                ref[a, b] = lines[:, pl.ds(at, C)]


def call(body, ins, outs, scratch=(), sems=0):
    space = {"v": pltpu.VMEM, "h": pltpu.HBM, "V": pltpu.VMEM}
    shapes = []
    for item in scratch:
        if isinstance(item, list):
            shapes.append([pltpu.VMEM(*s) for s in item])
        else:
            shapes.append(pltpu.VMEM(*item))
    if sems:
        shapes.append(pltpu.SemaphoreType.DMA((sems,)))
    run = pl.pallas_call(
        body,
        out_shape=[jax.ShapeDtypeStruct(shape, kind) if s == "v" else space[s](shape, kind) for s, shape, kind in outs],
        in_specs=[pl.BlockSpec(memory_space=space[s]) for s in ins],
        out_specs=[pl.BlockSpec(memory_space=space[s]) for s, _, _ in outs],
        scratch_shapes=shapes,
        compiler_params=pltpu.CompilerParams(vmem_limit_bytes=VMEM_LIMIT),
    )
    return lambda *args: run(
        *(pltpu.with_memory_space_constraint(arg, pltpu.HBM) if s == "h" else arg for s, arg in zip(ins, args))
    )


def exchange(lines, axes):
    shape = lines.shape
    if len(shape) == 2:
        lines = lines.reshape(math.prod(lax.axis_size(axis) for axis in axes), -1, 128)
    return lax.all_to_all(lines, axes, 0, 0, tiled=True).reshape(shape)


def beyond(z, pair, other, depths):
    hops = max(-(-depth // rows) for rows in z.rows for depth in depths)
    if hops == 1:
        swap = lambda value, start: lax.ppermute(
            value, "row", [(i + a, i + 1 - a) for i in range(start, z.peers - 1, 2) for a in (0, 1)]
        )
        others = swap(other, 1)
        return swap(pair, 0), others
    even = is_even()
    bottom, top = jnp.where(even, pair, other), jnp.where(even, other, pair)
    above, below = [], []
    for hop in range(1, hops + 1):
        above.append(lax.ppermute(bottom, "row", [(i, i + hop) for i in range(z.peers - hop)]))
        below.append(lax.ppermute(top, "row", [(i + hop, i) for i in range(z.peers - hop)]))
    up, down = [], []
    base = 0
    for depth in depths:
        for n in range(depth):
            for k in (1, 0):
                hop, back = divmod(depth - 1 - n, z.rows[k])
                at = base + (depth - 1 - back) * z.rims + z.rim[k]
                up.append(above[hop][at : at + z.edge[k]])
                hop, back = divmod(n, z.rows[k])
                at = base + back * z.rims + z.rim[k]
                down.append(below[hop][at : at + z.edge[k]])
        base += depth * z.rims
    up.append(jnp.concatenate([pixel_rows(z, above, base, 1, 1), pixel_rows(z, above, base, 0, 1)], axis=1))
    down.append(jnp.concatenate([pixel_rows(z, below, base, 0, 0), pixel_rows(z, below, base, 1, 0)], axis=1))
    up, down = jnp.concatenate(up, axis=0), jnp.concatenate(down, axis=0)
    return jnp.where(even, down, up), jnp.where(even, up, down)


def pixel_rows(z, bands, base, distance, last):
    lines = []
    for k in (0, 1):
        hop, back = divmod(distance, z.rows[k])
        at = base + k * z.images[0]
        half = 128 * abs(last - back)
        lines.append(bands[hop][at : at + z.images[k], half : half + 128])
    lines.append(jnp.zeros((z.slots - sum(z.images), 128), F32))
    return jnp.concatenate(lines, axis=0)


def local(
    image_small, image_large, teacher_small, teacher_large, upstream_small, upstream_large,
    conv_first, gain_first, bias_first, conv_second, gain_second, bias_second,
):
    peers = lax.axis_size("row")
    devices = lax.axis_size("img") * peers
    z = Sizes(image_small.shape, image_large.shape, devices, peers)
    body = lambda function: functools.partial(function, z)
    r = z.rims
    full, half, pair = (z.total, LANES), (2, z.total, 128), (2 * devices, 128)
    weight, left = (2, TAPS * TAP_ROWS, 128), (2, 256, 2 * z.total)
    images = [image_small, image_large, upstream_small, upstream_large, teacher_small, teacher_large]
    f = lambda space, *shape: (space, shape, F32)
    depths = (REACH, 2)
    rim_rows = sum(depths) * r + z.slots

    x, pair_edge, other_edge, copies = call(
        body(start_kernel),
        "hhhhhh",
        [("v", full, F32), f("v", rim_rows, LANES), f("v", rim_rows, LANES), ("V", pair, F32)],
        [[(a.shape, F32) for a in images], (half, F32)],
        4 + 2 * z.images[1],
    )(*images)
    gathered = exchange(copies, AXES)
    pair_rims, other_rims = beyond(z, pair_edge, other_edge, depths)
    params = [conv_first, conv_second] + images[2:]
    w1, w2, weights, affine, upstream, teacher, x_copy = call(
        body(prepare_kernel),
        "hhhhhhhhhhv",
        [("v", weight, BF16), ("v", weight, BF16), ("h", (3,) + weight, BF16), f("v", 5, LANES), ("h", full, F32), f("v", z.total, 128), ("h", full, F32)],
        [[(a.shape, F32) for a in params], ((2,) + weight, BF16), (full, F32), ((4, C), F32), (half, F32)],
        15,
    )(*params, *(v.reshape(1, C) for v in (gain_first, bias_first, gain_second, bias_second)), x)

    hidden, stats_one, copies = call(
        body(first_kernel),
        "vvvvvv",
        [("v", full, F32), f("v", 2, LANES), ("V", pair, F32)],
        [z.pads()],
    )(x, pair_rims, other_rims, gathered, affine, w1)
    gathered = exchange(copies, AXES)
    extended, near_rows = z.total + 4 * r, z.total + 2 * r
    h_above, h_below, left_one, packed, teachers, spread_u, near_u = call(
        body(first_operand_kernel),
        "vvvvvvvhh",
        [f("v", 3 * r, LANES), f("v", 3 * r, LANES), ("h", left, BF16), f("h", C, BACK_LANES), f("h", extended, LANES), f("h", near_rows, LANES), f("h", near_rows, LANES)],
        [
            z.pads(), z.chains(2), z.chains(REACH), (left, BF16), ((2,) + weight, BF16), ((near_rows, LANES), F32), ((extended, 128), F32),
            ((extended, LANES), F32), ((near_rows, LANES), F32), ((C, BACK_LANES), F32),
        ],
        8,
    )(x, hidden, pair_rims, other_rims, stats_one, affine, teacher, upstream, weights)
    gathered, near_u = lax.optimization_barrier((gathered, near_u))

    map_shape = (peers * z.slots, 128)
    out, o_above, o_below, near, stats_two, copies = call(
        body(second_kernel),
        "vvvvvvvvvv",
        [("v", full, F32), f("v", 2 * r, LANES), f("v", 2 * r, LANES), f("v", 2, r, LANES), f("v", 2, LANES), ("V", map_shape, F32)],
        [z.pads(), z.chains(3)],
    )(hidden, h_above, h_below, gathered, affine, w2, x, pair_rims, other_rims, teacher)
    gathered = exchange(copies, ("row",))
    out_copy, hidden_copy, left_two, shifts, by_map, by_teacher, up = call(
        body(second_operand_kernel),
        "vvvvvvvhhhh",
        [
            ("h", full, F32), f("h", near_rows, LANES), ("v", left, BF16), f("h", 3, near_rows, LANES),
            f("v", near_rows, LANES), f("v", near_rows, LANES), f("v", near_rows, LANES),
        ],
        [
            z.pads(), z.chains(2), ((extended, LANES), F32), ((near_rows, LANES), F32), (weight, BF16),
            ((3, near_rows, LANES), F32),
        ],
        14,
    )(hidden, near, stats_two, affine, out, o_above, o_below, teachers, spread_u, near_u, weights)

    dout, dshift, d_above, d_below, slabs = call(
        body(upstream_kernel),
        "vvhhvhvvhv",
        [("v", full, F32), ("v", full, F32), f("v", r, LANES), f("v", r, LANES), f("V", devices, 1, BACK_LANES)],
        [((3, near_rows, LANES), F32), (left, BF16), (full, F32), ((C, BACK_LANES), F32), z.pads(), z.pads()],
        7,
    )(gathered, up, shifts, left_one, left_two, packed, by_map, by_teacher, hidden_copy, stats_two)
    gathered = exchange(slabs, AXES)
    out_s, out_l, first_normed, second_normed, weight_back = call(
        body(write_kernel),
        "hhhhvvv",
        [("v", image_small.shape, F32), ("v", image_large.shape, F32), ("v", full, F32), f("v", near_rows, LANES), ("v", weight, BF16)],
        [(full, F32), (full, F32), ((near_rows, LANES), F32), (half, F32)],
        4,
    )(out_copy, x_copy, hidden_copy, weights, stats_one, stats_two, d_above)

    pre, norm_grads, slabs = call(
        body(hidden_kernel),
        "vvvvvvvvv",
        [("v", full, F32), f("v", 2, 128), f("V", devices, 1, LAST_LANES)],
        [z.pads()],
    )(gathered, dshift, d_above, d_below, second_normed, stats_two, affine, weight_back, first_normed)
    gathered = exchange(slabs, AXES)

    back_s, back_l, one, two, gain_one, bias_one, gain_two, bias_two = call(
        body(back_kernel),
        "vvvvvvv",
        [("v", a.shape, F32) for a in (image_small, image_large, conv_first, conv_second)] + [f("v", 1, C)] * 4,
        [(half, F32), ((C, LAST_LANES), F32)],
    )(gathered, pre, first_normed, stats_one, affine, dout, norm_grads)
    return (
        out_s, out_l, back_s, back_l,
        one, gain_one.reshape(C), bias_one.reshape(C),
        two, gain_two.reshape(C), bias_two.reshape(C),
    )


def solution(mesh):
    split_bands, everywhere = P("img", "row", None), P()
    return jax.shard_map(
        local,
        mesh=mesh,
        in_specs=(split_bands,) * 6 + (everywhere,) * 6,
        out_specs=(split_bands,) * 4 + (everywhere,) * 6,
        check_vma=False,
    )
```

```python
import functools
import math

import jax
import jax.numpy as jnp
from jax import lax
from jax.experimental import pallas as pl
from jax.experimental.pallas import tpu as pltpu
from jax.sharding import PartitionSpec as P

C = 32
HS = 32
HL = 64
HEIGHTS = (HS, HL)

norm_eps = 1e-05
map_eps = 1e-06
beta_weight = 1000.0
AXES = ("img", "row")
BLOCK = 8
LANES = BLOCK * C
TAPS = 3
DEPTH = TAPS * 128 + 256
TAP_ROWS = 128 + 2 * C
REACH = 4
ROOT = math.sqrt(2.0 / math.pi)
CUBE = 0.044715
F32 = jnp.float32
BF16 = jnp.bfloat16
VMEM_LIMIT = 32 * 1024 * 1024
BIAS, GAIN, SECOND, LEFT, HIDDEN, ONES = 0, 1, 2, 11, 20, 29
BACK_LANES = 1280
LAST_SECOND, LAST_FIRST, LAST_LANES = 2, 11, 640


class Sizes:
    def __init__(self, small, large, devices, peers):
        self.images = (small[0], large[0])
        self.rows = (small[1], large[1])
        self.blocks = (HS // BLOCK, HL // BLOCK)
        self.step = tuple(n * r for n, r in zip(self.images, self.rows))
        self.count = tuple(b * s for b, s in zip(self.blocks, self.step))
        self.edge = tuple(b * n for b, n in zip(self.blocks, self.images))
        self.start = (self.count[1], 0)
        self.rim = (self.edge[1], 0)
        self.total = sum(self.count)
        self.rims = sum(self.edge)
        self.slots = -(-sum(self.images) // 8) * 8
        self.guard = -(-max(self.images) // 8) * 8
        self.devices = devices
        self.peers = peers
        self.here = float(self.total * BLOCK)
        self.pixels = self.here * devices

    def pads(self):
        return [((TAPS, 2, self.count[k] + 2 * self.step[k], 128), F32) for k in (0, 1)]

    def chains(self, depth):
        return [((2, 2 * self.guard + (depth + 1) * self.rims, 128), F32)] * 2


def split(value):
    high = value.astype(BF16)
    return high, (value - high.astype(F32)).astype(BF16)


def dot(left, right):
    return lax.dot_general(left, right, (((1,), (0,)), ((), ())), preferred_element_type=F32)


def product(left, right):
    if left[0].shape[1] % 128:
        return dot(left[0], right[0]) + (dot(left[0], right[1]) + dot(left[1], right[0]))
    return dot(
        jnp.concatenate([left[0], left[0], left[1]], axis=1), jnp.concatenate([right[0], right[1], right[0]], axis=0)
    )


def spread(left, right):
    right = right.astype(BF16)
    return dot(jnp.concatenate(split(left), axis=1), jnp.concatenate([right, right], axis=0))


def gelu(s):
    return 0.5 * s * (1.0 + jnp.tanh(ROOT * (s + CUBE * s * s * s)))


def gelu_slope(s):
    square = s * s
    t = jnp.tanh(ROOT * s * (1.0 + CUBE * square))
    return 0.5 * (1.0 + t) + 0.5 * s * (1.0 - t * t) * ROOT * (1.0 + 3.0 * CUBE * square)


def spread_groups(row):
    row = row + pltpu.roll(row, 64, 1)
    return row + pltpu.roll(row, 32, 1)


def fold(row):
    return spread_groups(row[:, :128] + row[:, 128:])


def wide(row):
    return jnp.concatenate([row, row], axis=1)


def group_of(rows=1, lanes=128):
    return lax.broadcasted_iota(jnp.int32, (rows, lanes), 1) // C


def column_sum(value):
    return jnp.sum(value, axis=0, keepdims=True)


def send_lines(z, ref, lines):
    for n, line in enumerate(lines):
        ref[pl.ds(n, z.devices, stride=len(lines)), :] = jnp.broadcast_to(line, (z.devices, 128))


def moments(z, value, ref):
    few = min(8, z.total)
    pivot = fold(column_sum(value[:few])) / float(few * BLOCK)
    off = value - wide(pivot)
    first, second = fold(column_sum(off)), fold(column_sum(off * off))
    send_lines(z, ref, [pivot + first / z.here, second - first * first / z.here])


def merged(z, ref):
    means = ref[pl.ds(0, z.devices, stride=2), :]
    center = jnp.mean(means, axis=0, keepdims=True)
    off = means - center
    within = jnp.mean(ref[pl.ds(1, z.devices, stride=2), :], axis=0, keepdims=True)
    variance = within / z.here + jnp.mean(off * off, axis=0, keepdims=True)
    return wide(center), wide(lax.rsqrt(variance + norm_eps))


def put_halves(ref, value):
    ref[0] = value[:, :128]
    ref[1] = value[:, 128:]


def whole(ref):
    return jnp.concatenate([ref[0], ref[1]], axis=1)


def to_matrix(z, refs, half):
    for k in (0, 1):
        for j in range(z.blocks[k]):
            at = z.start[k] + j * z.step[k]
            for i in range(z.images[k]):
                for h in (0, 1):
                    half[h, pl.ds(at + i * z.rows[k], z.rows[k]), :] = refs[k][i, :, pl.ds(LANES * j + 128 * h, 128)]


def from_matrix(z, half, refs):
    for k in (0, 1):
        for j in range(z.blocks[k]):
            at = z.start[k] + j * z.step[k]
            for i in range(z.images[k]):
                for h in (0, 1):
                    refs[k][i, :, pl.ds(LANES * j + 128 * h, 128)] = half[h, pl.ds(at + i * z.rows[k], z.rows[k]), :]


def is_even():
    return lax.axis_index("row") % 2 == 0


def put_edges(pair, other, at, last, first):
    even = is_even()
    pair[at] = jnp.where(even, last, first)
    other[at] = jnp.where(even, first, last)


def above_of(pair, other, at):
    return jnp.where(is_even(), other[at], pair[at])


def below_of(pair, other, at):
    return jnp.where(is_even(), pair[at], other[at])


def take_rims(z, half, depth, pair, other):
    everything = pl.ds(0, 128)
    for k in (0, 1):
        nothing = jnp.zeros((z.edge[k], 128), F32)
        for n in range(depth):
            first, last = nothing, nothing
            if depth - n <= z.rows[k]:
                last = half[pl.ds(z.start[k] + z.rows[k] - depth + n, z.edge[k], stride=z.rows[k]), :]
            if n < z.rows[k]:
                first = half[pl.ds(z.start[k] + n, z.edge[k], stride=z.rows[k]), :]
            put_edges(pair, other, (pl.ds(n * z.rims + z.rim[k], z.edge[k]), everything), last, first)


def inside(z, depth, above):
    at = lax.axis_index("row")
    large = lax.broadcasted_iota(jnp.int32, (z.rims, 1), 0) < z.rim[0]
    parts = []
    for n in range(depth):
        if above:
            ok = [jnp.where(at * rows >= depth - n, 1.0, 0.0) for rows in z.rows]
        else:
            ok = [jnp.where((at + 1) * rows + n + 1 <= height, 1.0, 0.0) for rows, height in zip(z.rows, HEIGHTS)]
        parts.append(jnp.where(large, ok[1], ok[0]).astype(F32))
    return jnp.concatenate(parts, axis=0)


def clear_guards(z, pads, a):
    for k in (0, 1):
        pads[k][a, 1, pl.ds(0, z.step[k]), :] = jnp.zeros((z.step[k], 128), F32)
        pads[k][a, 0, pl.ds(z.step[k] + z.count[k], z.step[k]), :] = jnp.zeros((z.step[k], 128), F32)


def fill_center(z, pads, value):
    clear_guards(z, pads, 1)
    for k in (0, 1):
        for h in (0, 1):
            pads[k][1, h, pl.ds(z.step[k], z.count[k]), :] = value[z.start[k] : z.start[k] + z.count[k], 128 * h : 128 * h + 128]


def fill_shifted(z, pads, above, below):
    for k in (0, 1):
        ref, step, count, rows = pads[k], z.step[k], z.count[k], z.rows[k]
        rim = slice(z.rim[k], z.rim[k] + z.edge[k])
        for h in (0, 1):
            lanes = slice(128 * h, 128 * h + 128)
            ref[0, h, pl.ds(step, count), :] = ref[1, h, pl.ds(step - 1, count), :]
            ref[2, h, pl.ds(step, count), :] = ref[1, h, pl.ds(step + 1, count), :]
            ref[0, h, pl.ds(step, z.edge[k], stride=rows), :] = above[rim, lanes]
            ref[2, h, pl.ds(step + rows - 1, z.edge[k], stride=rows), :] = below[rim, lanes]


def fill_pads(z, pads, value, above, below):
    fill_center(z, pads, value)
    fill_shifted(z, pads, above, below)
    for a in (0, 2):
        clear_guards(z, pads, a)


def beside(left, right):
    lane = lax.broadcasted_iota(jnp.int32, (1, 128), 1)
    middle = pltpu.roll(jnp.where(lane >= 64, left[1], right[1]), 64, 1)
    return [
        jnp.where(lane >= 96, left[0], jnp.where(lane < 32, right[0], middle)),
        jnp.where(lane >= 96, left[2], jnp.where(lane < 32, right[2], 0.0)),
    ]


def band_operand(z, pads):
    parts = ([], [])
    for k in (1, 0):
        ref, step, count = pads[k], z.step[k], z.count[k]
        low, high = ([ref[a, h, pl.ds(step, count), :] for a in range(TAPS)] for h in (0, 1))
        before = [ref[a, 1, pl.ds(0, count), :] for a in range(TAPS)]
        after = [ref[a, 0, pl.ds(2 * step, count), :] for a in range(TAPS)]
        parts[0].append(jnp.concatenate(low + beside(before, high), axis=1))
        parts[1].append(jnp.concatenate(high + beside(low, after), axis=1))
    return [jnp.concatenate(part, axis=0) for part in parts]


def rim_operand(z, chain, depth):
    m = lax.broadcasted_iota(jnp.int32, (z.rims, 1), 0)
    large = m < z.rim[0]
    has_before = jnp.where(large, m, m - z.rim[0]) >= jnp.where(large, z.images[1], z.images[0])
    has_after = m < jnp.where(large, z.rim[0] - z.images[1], z.rims - z.images[0])
    low, high, before, after = [], [], [], []
    for r in range(depth + 1):
        at = z.guard + r * z.rims
        low.append(chain[0, pl.ds(at, z.rims), :])
        high.append(chain[1, pl.ds(at, z.rims), :])
        shifted = [chain[1, pl.ds(at - images, z.rims), :] for images in z.images]
        before.append(jnp.where(has_before, jnp.where(large, shifted[1], shifted[0]), 0.0))
        shifted = [chain[0, pl.ds(at + images, z.rims), :] for images in z.images]
        after.append(jnp.where(has_after, jnp.where(large, shifted[1], shifted[0]), 0.0))
    parts = ([], [])
    for n in range(depth - 1):
        rows = slice(n, n + TAPS)
        parts[0].append(jnp.concatenate(low[rows] + beside(before[rows], high[rows]), axis=1))
        parts[1].append(jnp.concatenate(high[rows] + beside(low[rows], after[rows]), axis=1))
    return [jnp.concatenate(part, axis=0) for part in parts]


def times(parts, weight):
    left = jnp.concatenate([part[h] for h in (0, 1) for part in parts], axis=0)
    both = jnp.concatenate([weight_matrix(weight.at[0]), weight_matrix(weight.at[1])], axis=1)
    result = dot(jnp.concatenate(split(left), axis=1), jnp.concatenate([both, both], axis=0))
    result = result[:, :128] + result[:, 128:]
    rows = result.shape[0] // 2
    return jnp.concatenate([result[:rows], result[rows:]], axis=1)


def rim_operands(z, pads, above, below, depth, chains):
    parts = []
    for side, (rim, chain) in enumerate(zip((above, below), chains)):
        rim_at, own_at = (z.guard, z.guard + depth * z.rims) if side == 0 else (z.guard + z.rims, z.guard)
        for h in (0, 1):
            chain[h, pl.ds(rim_at, depth * z.rims), :] = rim[:, 128 * h : 128 * h + 128]
            for k in (0, 1):
                row = z.step[k] + (0 if side == 0 else z.rows[k] - 1)
                chain[h, pl.ds(own_at + z.rim[k], z.edge[k]), :] = pads[k][1, h, pl.ds(row, z.edge[k], stride=z.rows[k]), :]
        parts.append(rim_operand(z, chain, depth))
    return parts


def convolve(z, own, above, below, depth, pads, chains, weight):
    r = z.rims
    fill_pads(z, pads, own, above[(depth - 1) * r :], below[:r])
    parts = [band_operand(z, pads)]
    if depth > 1:
        parts += rim_operands(z, pads, above, below, depth, chains)
    result = times(parts, weight)
    n = z.total + (depth - 1) * r
    return result[: z.total], result[z.total : n], result[n:]


def convolve_rims(z, pads, above, below, depth, chains, weight):
    result = times(rim_operands(z, pads, above, below, depth, chains), weight)
    n = (depth - 1) * z.rims
    return result[:n], result[n:]


def image_sums(z, value):
    slot = lax.broadcasted_iota(jnp.int32, (z.slots, 1), 0)
    sums = jnp.zeros((z.slots, 128), F32)
    for k in (0, 1):
        line = value[z.start[k] : z.start[k] + z.step[k]]
        for j in range(1, z.blocks[k]):
            at = z.start[k] + j * z.step[k]
            line = line + value[at : at + z.step[k]]
        image = lax.broadcasted_iota(jnp.int32, (z.step[k], 1), 0) // z.rows[k]
        for i in range(z.images[k]):
            sums = jnp.where(slot == i + k * z.images[0], column_sum(jnp.where(image == i, line, 0.0)), sums)
    return sums


def image_rows(z, values, rims):
    parts = []
    for k in (1, 0):
        image = lax.broadcasted_iota(jnp.int32, (z.step[k], 1), 0) // z.rows[k]
        line = jnp.zeros((z.step[k], 128), F32)
        for i in range(z.images[k]):
            at = i + k * z.images[0]
            line = jnp.where(image == i, values[at : at + 1], line)
        parts += [line] * z.blocks[k]
    if rims:
        m = lax.broadcasted_iota(jnp.int32, (z.rims, 1), 0)
        image = jnp.where(m < z.rim[0], z.images[0] + m % z.images[1], (m - z.rim[0]) % z.images[0])
        line = jnp.zeros((z.rims, 128), F32)
        for at in range(sum(z.images)):
            line = jnp.where(image == at, values[at : at + 1], line)
        parts += [line] * rims
    return jnp.concatenate(parts, axis=0)


def channel_mean():
    a = lax.broadcasted_iota(jnp.int32, (LANES, 128), 0) // C
    b = lax.broadcasted_iota(jnp.int32, (LANES, 128), 1) % 64
    return jnp.where(a == b, 1.0 / C, 0.0).astype(F32)


def to_channels():
    a = lax.broadcasted_iota(jnp.int32, (128, LANES), 0)
    b = lax.broadcasted_iota(jnp.int32, (128, LANES), 1) // C
    return jnp.where(a == b, 1.0, 0.0).astype(F32)


def attention(value):
    return spread(value * value, channel_mean())


def pieces(source, target):
    return [(source.at[n], target.at[n]) for n in range(source.shape[0])]


def copies_of(pairs, sems, first=0):
    return [pltpu.make_async_copy(a, b, sems.at[first + n]) for n, (a, b) in enumerate(pairs)]


def start_all(copies):
    for copy in copies:
        copy.start()


def wait_all(copies):
    for copy in copies:
        copy.wait()


def start_kernel(z, small, large, up_s, up_l, t_s, t_l, x, pair, other, copies, raw, half, sems):
    images = [(small, raw[0])] + pieces(large, raw[1])
    rest = [(up_s, raw[2])] + pieces(up_l, raw[3]) + [(t_s, raw[4]), (t_l, raw[5])]
    loads = copies_of(images + rest, sems)
    start_all(loads)
    r, n = z.rims, REACH * z.rims
    tail = n + 2 * r
    for ref in (pair, other):
        ref[pl.ds(tail, z.slots), :] = jnp.zeros((z.slots, LANES), F32)
    wait_all(loads[: len(images)])
    to_matrix(z, raw[:2], half)
    value = whole(half)
    x[...] = value
    moments(z, value, copies)
    for h in (0, 1):
        lanes = pl.ds(128 * h, 128)
        take_rims(z, half.at[h], REACH, pair.at[pl.ds(0, n), lanes], other.at[pl.ds(0, n), lanes])
    wait_all(loads[len(images) :])
    for k in (0, 1):
        width, rows = HEIGHTS[k], z.rows[k]
        for i in range(z.images[k]):
            slot = pl.ds(tail + i + k * z.images[0], 1)
            for d in (0, 1):
                has_last, has_first = rows + d >= 2, d < rows
                last, first = pl.ds(max(rows - 2 + d, 0), 1), pl.ds(min(d, rows - 1), 1)
                for j in range(z.blocks[k]):
                    lanes = pl.ds(LANES * j, LANES)
                    at = (pl.ds(n + d * r + z.rim[k] + j * z.images[k] + i, 1), pl.ds(0, LANES))
                    nothing = jnp.zeros((1, LANES), F32)
                    put_edges(
                        pair, other, at,
                        raw[2 + k][i, last, lanes] if has_last else nothing,
                        raw[2 + k][i, first, lanes] if has_first else nothing,
                    )
                nothing = jnp.zeros((1, width), F32)
                put_edges(
                    pair, other, (slot, pl.ds(128 * d, width)),
                    raw[4 + k][i, last, :] if has_last else nothing,
                    raw[4 + k][i, first, :] if has_first else nothing,
                )


def banded(taps, ref):
    row = lax.broadcasted_iota(jnp.int32, (128, 128), 0) // C
    lane = group_of(128)
    for a in range(TAPS):
        main = jnp.zeros((128, 128), F32)
        for b in range(TAPS):
            main = jnp.where(row - lane + 1 == b, taps[a][b], main)
        before = jnp.where(lane[:C] == 0, taps[a][0][:C], 0.0)
        after = jnp.where(lane[:C] == 3, taps[a][2][:C], 0.0)
        for n, part in enumerate(split(jnp.concatenate([main, before, after], axis=0))):
            ref[n, pl.ds(a * TAP_ROWS, TAP_ROWS), :] = part


def weight_matrix(ref):
    main = [ref[pl.ds(a * TAP_ROWS, 128), :] for a in range(TAPS)]
    before, after = ([ref[pl.ds(a * TAP_ROWS + 128 + n * C, C), :] for a in range(TAPS)] for n in (0, 1))
    return jnp.concatenate(
        main + [after[0], before[1], after[1], before[0], after[2], jnp.zeros((2 * C, 128), BF16), before[2]], axis=0
    )


def prepare_kernel(z, first, second, up_s, up_l, t_s, t_l, g1, b1, g2, b2, x, w1, w2, weights, affine, upstream, teacher, x_copy, raw, kept, kept_u, rows, half, sems):
    targets = tuple(raw) + tuple(rows.at[pl.ds(n, 1), :] for n in range(4))
    refs = (first, second, up_s, up_l, t_s, t_l, g1, b1, g2, b2)
    loads = [pltpu.make_async_copy(a, b, sems.at[n]) for n, (a, b) in enumerate(zip(refs, targets))]
    start_all(loads)
    stores = [pltpu.make_async_copy(x, x_copy, sems.at[13])]
    stores[0].start()
    wait_all(loads)
    to_matrix(z, raw[2:4], half)
    kept_u[...] = whole(half)
    stores.append(pltpu.make_async_copy(kept_u, upstream, sems.at[10]))
    stores[1].start()
    for n, (source, forward) in enumerate(zip(raw[:2], (w1, w2))):
        tiles = []
        for a in range(TAPS):
            line = [jnp.concatenate([source[a, b]] * 4, axis=1) for b in range(TAPS)]
            tiles.append([jnp.concatenate([tap] * 4, axis=0) for tap in line])
        turned = [[tiles[TAPS - 1 - a][TAPS - 1 - b].T for b in range(TAPS)] for a in range(TAPS)]
        banded(tiles, forward)
        if n == 0:
            stores.append(pltpu.make_async_copy(forward, weights.at[2], sems.at[14]))
            stores[-1].start()
        banded(turned, kept.at[n])
        stores.append(pltpu.make_async_copy(kept.at[n], weights.at[n], sems.at[11 + n]))
        stores[-1].start()
    taps = sum(raw[0][a, b] for a in range(TAPS) for b in range(TAPS))
    pivot = dot(jnp.broadcast_to(gelu(rows[1:2]), (8, C)), taps)[0:1]
    affine[...] = jnp.concatenate([jnp.concatenate([rows[...], pivot], axis=0)] * BLOCK, axis=1)
    teacher[...] = jnp.zeros(teacher.shape, F32)
    for k, ref in ((0, raw[4]), (1, raw[5])):
        for i in range(z.images[k]):
            line = ref[i]
            for j in range(z.blocks[k]):
                at = z.start[k] + j * z.step[k] + i * z.rows[k]
                for lane in (0, 64):
                    teacher[pl.ds(at, z.rows[k]), pl.ds(lane, BLOCK)] = line[:, j * BLOCK : (j + 1) * BLOCK]
    wait_all(stores)


def normed_by(stats):
    return lambda v: (v - stats[0:1]) * stats[1:2]


def activation(center, scale, gain, bias):
    factor = scale * gain
    offset = bias - center * factor
    return lambda v: gelu(v * factor + offset)


def first_kernel(z, x, pair, other, gathered, affine, weight, hidden, stats, copies, pads):
    center, scale = merged(z, gathered)
    act = activation(center, scale, affine[0:1], affine[1:2])
    r, lanes = z.rims, pl.ds(0, LANES)
    up = act(above_of(pair, other, (pl.ds((REACH - 1) * r, r), lanes))) * inside(z, 1, True)
    down = act(below_of(pair, other, (pl.ds(0, r), lanes))) * inside(z, 1, False)
    own, _, _ = convolve(z, act(x[...]), up, down, 1, pads, None, weight)
    moments(z, own, copies)
    hidden[...] = own
    stats[0:1] = center
    stats[1:2] = scale


def second_kernel(z, hidden, h_above, h_below, gathered, affine, weight, x, pair, other, teacher, out, o_above, o_below, near, stats, copies, pads, chains):
    center, scale = merged(z, gathered)
    act = activation(center, scale, affine[2:3], affine[3:4])
    r = z.rims
    own = act(hidden[...])
    up, down = act(h_above[...]) * inside(z, 3, True), act(h_below[...]) * inside(z, 3, False)
    own, up, down = convolve(z, own, up, down, 3, pads, chains, weight)
    own = x[...] + own
    amap = attention(own)
    lane = lax.broadcasted_iota(jnp.int32, (1, 128), 1)
    sums = image_sums(z, amap * jnp.where(lane < 64, amap, teacher[...]))
    copies[...] = jnp.concatenate([sums] * z.peers, axis=0)
    out[...] = own
    o_above[...] = above_of(pair, other, (pl.ds(2 * r, 2 * r), pl.ds(0, LANES))) + up
    o_below[...] = below_of(pair, other, (pl.ds(0, 2 * r), pl.ds(0, LANES))) + down
    near[0] = h_above[pl.ds(2 * r, r), :]
    near[1] = h_below[pl.ds(0, r), :]
    stats[0:1] = center
    stats[1:2] = scale


def tap_rows(q):
    return 128 + C if q < 0 else q * C


def tap_product(z, operand, own, above, below, pads):
    fill_center(z, pads, own)
    fill_shifted(z, pads, above, below)
    columns = []
    for a in range(TAPS):
        columns.append(
            jnp.concatenate([pads[k][TAPS - 1 - a, h, pl.ds(z.step[k], z.count[k]), :] for h in (0, 1) for k in (1, 0)], axis=0)
        )
    used = [jnp.concatenate([operand[n, pl.ds(0, 128 + C), :], operand[n, pl.ds(256 - C, C), :]], axis=0) for n in (0, 1)]
    return product(used, split(jnp.concatenate(columns, axis=1)))


def tap_sums(result, tiles, first_group):
    group = group_of()
    for a in range(TAPS):
        for b in range(TAPS):
            total = None
            for p in range(4):
                at = tap_rows(p + b - 1)
                part = result[at : at + C, 128 * a : 128 * a + 128]
                total = part if total is None else jnp.where(group == p, part, total)
            tile, slot = divmod(first_group + a * TAPS + b, 4)
            tiles[tile] = jnp.where(group == slot, spread_groups(total), tiles[tile])


def tap_counts(z, turned, tiles, first_group):
    group = group_of()
    m = lax.broadcasted_iota(jnp.int32, (1, 2 * z.total), 1) % z.total
    row = jnp.where(m < z.start[0], m % z.rows[1], (m - z.start[0]) % z.rows[0])
    height = jnp.where(m < z.start[0], z.rows[1], z.rows[0])
    at = lax.axis_index("row")
    lost = {
        0: (row == height - 1) & (at == z.peers - 1),
        2: (row == 0) & (at == 0),
    }
    for a in range(TAPS):
        column = jnp.sum(jnp.where(lost[a], 0.0, turned) if a in lost else turned, axis=1, keepdims=True)
        used = jnp.concatenate([column[: 128 + C], column[256 - C :]], axis=0)
        for b in range(TAPS):
            total = sum(used[tap_rows(p + b - 1) : tap_rows(p + b - 1) + C] for p in range(4))
            tile, slot = divmod(first_group + a * TAPS + b, 4)
            tiles[tile] = jnp.where(group == slot, total, tiles[tile])


def turned_operand(z, value, pads, kept):
    fill_center(z, pads, value)
    lane = lax.broadcasted_iota(jnp.int32, (1, 128), 1)
    halves = ([], [])
    for k in (1, 0):
        ref, step, count = pads[k], z.step[k], z.count[k]
        low, high = ref[1, 0, pl.ds(step, count), :], ref[1, 1, pl.ds(step, count), :]
        before, after = ref[1, 1, pl.ds(0, count), :], ref[1, 0, pl.ds(2 * step, count), :]
        for part, main, left, right in ((halves[0], low, before, high), (halves[1], high, low, after)):
            part.append(jnp.concatenate([main, jnp.where(lane >= 96, left, jnp.where(lane < 32, right, 0.0))], axis=1))
    turned = jnp.concatenate(halves[0] + halves[1], axis=0).T
    parts = split(turned)
    for n in (0, 1):
        kept[n] = parts[n]
    return turned


def first_operand_kernel(z, x, hidden, pair, other, stats, affine, teacher, upstream, weights, h_above, h_below, left, packed, teachers, spread_u, near_u, pads, chains, deep_chains, kept, kept_w, kept_u, pixels, kept_t, kept_c, kept_packed, sems):
    r, own = z.rims, pl.ds(0, z.total)
    loads = copies_of([(upstream, kept_u.at[own, :]), (weights.at[1], kept_w.at[1])], sems)
    first = pltpu.make_async_copy(weights.at[2], kept_w.at[0], sems.at[7])
    first.start()
    start_all(loads)
    act = activation(stats[0:1], stats[1:2], affine[0:1], affine[1:2])
    value = turned_operand(z, act(x[...]), pads, kept)
    stores = [pltpu.make_async_copy(kept, left, sems.at[2])]
    stores[0].start()
    n, lanes = REACH * r, pl.ds(0, LANES)
    up = act(above_of(pair, other, (pl.ds(0, n), lanes))) * inside(z, REACH, True)
    down = act(below_of(pair, other, (pl.ds(0, n), lanes))) * inside(z, REACH, False)
    first.wait()
    up, down = convolve_rims(z, pads, up, down, REACH, deep_chains, kept_w.at[0])
    h_above[...] = up
    h_below[...] = down
    tiles = [jnp.zeros((C, 128), F32) for _ in range(BACK_LANES // 128)]
    tap_counts(z, value, tiles, ONES)
    pivot = affine[4:5]
    result = tap_product(
        z, kept, hidden[...] - pivot, (up[2 * r :] - pivot) * inside(z, 1, True),
        (down[:r] - pivot) * inside(z, 1, False), pads,
    )
    tap_sums(result, tiles, HIDDEN)
    kept_packed[...] = jnp.concatenate(tiles, axis=1)
    stores.append(pltpu.make_async_copy(kept_packed, packed, sems.at[6]))
    stores[1].start()
    pixels[own, :] = teacher[...]
    pixels[pl.ds(z.total, 4 * r), :] = jnp.zeros((4 * r, 128), F32)
    n = (REACH + 2) * r
    for side, beyond_of in enumerate((above_of, below_of)):
        for d in (0, 1):
            for k in (0, 1):
                line = beyond_of(pair, other, (pl.ds(n + k * z.images[0], z.images[k]), pl.ds(128 * d, 128)))
                for j in range(z.blocks[k]):
                    at = z.total + (2 * side + d) * r + z.rim[k] + j * z.images[k]
                    pixels[pl.ds(at, z.images[k]), pl.ds(0, BLOCK)] = line[:, j * BLOCK : (j + 1) * BLOCK]
    kept_t[...] = spread(pixels[...], to_channels())
    stores.append(pltpu.make_async_copy(kept_t, teachers, sems.at[3]))
    stores[2].start()
    n = REACH * r
    at = (pl.ds(n, 2 * r), pl.ds(0, LANES))
    up, down = above_of(pair, other, at) * inside(z, 2, True), below_of(pair, other, at) * inside(z, 2, False)
    kept_u[pl.ds(z.total, r), :] = up[r:]
    kept_u[pl.ds(z.total + r, r), :] = down[:r]
    wait_all(loads)
    stores.append(pltpu.make_async_copy(kept_u, near_u, sems.at[5]))
    stores[3].start()
    kept_c[...] = jnp.concatenate(convolve(z, kept_u[own, :], up, down, 2, pads, chains, kept_w.at[1]), axis=0)
    stores.append(pltpu.make_async_copy(kept_c, spread_u, sems.at[4]))
    stores[4].start()
    wait_all(stores)


def second_operand_kernel(z, hidden, near, stats, affine, out, o_above, o_below, teachers, spread_u, near_u, weights, out_copy, hidden_copy, left, shifts, by_map, by_teacher, up, pads, chains, kept_t, kept_u, kept_w, kept_s, sems):
    r, total = z.rims, z.total
    loads = [
        pltpu.make_async_copy(teachers, kept_t, sems.at[0]),
        pltpu.make_async_copy(weights.at[1], kept_w, sems.at[1]),
        pltpu.make_async_copy(spread_u, kept_u, sems.at[2]),
    ]
    start_all(loads)
    stores = [
        pltpu.make_async_copy(out, out_copy, sems.at[4]),
        pltpu.make_async_copy(hidden, hidden_copy.at[pl.ds(0, total), :], sems.at[7]),
        pltpu.make_async_copy(near.at[0], hidden_copy.at[pl.ds(total, r), :], sems.at[8]),
        pltpu.make_async_copy(near.at[1], hidden_copy.at[pl.ds(total + r, r), :], sems.at[9]),
        pltpu.make_async_copy(near_u, up, sems.at[10]),
    ]
    start_all(stores)
    normed = normed_by(stats)(jnp.concatenate([hidden[...], near[0], near[1]], axis=0))
    shifted = normed * affine[2:3] + affine[3:4]
    turned_operand(z, gelu(shifted[:total]), pads, left)
    ones = jnp.ones((total, 1), F32)
    masks = jnp.concatenate([ones, inside(z, 1, True), inside(z, 1, False)], axis=0)
    slopes = gelu_slope(shifted) * masks
    o = jnp.concatenate([out[...], o_above[...] * inside(z, 2, True), o_below[...] * inside(z, 2, False)], axis=0)
    for_map = spread(attention(o), to_channels()) * o
    wait_all(loads)
    for_teacher = kept_t[...] * o
    kept_s[0] = kept_u[...] * slopes
    stores += copies_of(pieces(kept_s, shifts), sems, 11)
    stores[-3].start()
    for n, value, ref in ((1, for_map, by_map), (2, for_teacher, by_teacher)):
        own, before, after = value[:total], value[total : total + 2 * r], value[total + 2 * r :]
        ref[...] = jnp.concatenate([own, before[r:], after[:r]], axis=0)
        kept_s[n] = jnp.concatenate(convolve(z, own, before, after, 2, pads, chains, kept_w), axis=0) * slopes
        stores[n - 3].start()
    wait_all(stores)


def upstream_kernel(z, gathered, up, shifts, left_1, left_2, packed, by_map, by_teacher, hidden, stats, dout, dshift, d_above, d_below, slabs, kept_s, kept_left, kept_h, kept_packed, pads, more_pads, sems):
    r, total = z.rims, z.total
    loads = copies_of(
        pieces(shifts, kept_s) + pieces(left_1, kept_left) + [(hidden.at[pl.ds(0, total), :], kept_h), (packed, kept_packed)], sems
    )
    start_all(loads)
    lane = lax.broadcasted_iota(jnp.int32, (z.slots, 128), 1)
    sums = sum(gathered[pl.ds(n * z.slots, z.slots), :] for n in range(z.peers))
    square = jnp.sum(jnp.where(lane < 64, sums, 0.0), axis=1, keepdims=True)
    cross = jnp.sum(jnp.where(lane < 64, 0.0, sums), axis=1, keepdims=True)
    inverse = lax.rsqrt(square + map_eps)
    inner = beta_weight * (square * inverse - cross) * inverse
    shape = (z.slots, 128)
    for_map = (beta_weight - inner) * inverse * inverse * (2.0 / C)
    for_teacher = beta_weight * inverse * (2.0 / C)
    for_map, for_teacher = (wide(image_rows(z, jnp.broadcast_to(v, shape), 2)) for v in (for_map, for_teacher))
    value = up[...] + for_map * by_map[...] - for_teacher * by_teacher[...]
    dout[...] = value[:total]
    second = tap_product(z, left_2, value[:total], value[total : total + r], value[total + r :], pads)
    wait_all(loads[:3])
    shift = kept_s[0] + for_map * kept_s[1] - for_teacher * kept_s[2]
    pre, above, below = shift[:total], shift[total : total + r], shift[total + r :]
    dshift[...] = pre
    d_above[...] = above
    d_below[...] = below
    wait_all(loads[3:5])
    first = tap_product(z, kept_left, pre, above, below, more_pads)
    wait_all(loads[5:])
    normed = normed_by(stats)(kept_h[...])
    tiles = [kept_packed[:, 128 * n : 128 * n + 128] for n in range(BACK_LANES // 128)]
    group = group_of()
    tiles[0] = jnp.where(group == BIAS, fold(column_sum(pre)), jnp.where(group == GAIN, fold(column_sum(pre * normed)), tiles[0]))
    tap_sums(second, tiles, SECOND)
    tap_sums(first, tiles, LEFT)
    line = jnp.concatenate(tiles, axis=1)
    for d in range(z.devices):
        slabs[d] = line[d % C : d % C + 1]


def write_kernel(z, out, x, hidden, weights, first_stats, stats, order, out_s, out_l, first_normed, normed, weight, kept, kept_x, kept_h, half, sems):
    loads = [pltpu.make_async_copy(a, b, sems.at[n]) for n, (a, b) in enumerate(((out, kept), (x, kept_x), (hidden, kept_h), (weights.at[0], weight)))]
    start_all(loads)
    loads[0].wait()
    put_halves(half, kept[...])
    from_matrix(z, half, (out_s, out_l))
    loads[1].wait()
    first_normed[...] = normed_by(first_stats)(kept_x[...])
    loads[2].wait()
    normed[...] = normed_by(stats)(kept_h[...])
    loads[3].wait()


def norm_sums(total):
    group = group_of()
    return [wide(spread_groups(jnp.where(group == n, total[:, :128], 0.0))) for n in (BIAS, GAIN)]


def hidden_kernel(z, gathered, dshift, d_above, d_below, second_normed, stats, affine, weight, first_normed, pre_ref, norm_grads, slabs, pads):
    total = jnp.sum(gathered[...], axis=0)
    bias_sum, gain_sum = norm_sums(total)
    norm_grads[0:1] = bias_sum[:, :128]
    norm_grads[1:2] = gain_sum[:, :128]
    bias_mean, gain_mean = bias_sum / z.pixels, gain_sum / z.pixels
    factor = affine[2:3] * stats[1:2]
    r, total_rows = z.rims, z.total

    def back(d, normed):
        return factor * (d - bias_mean - normed * gain_mean)

    own = back(dshift[...], second_normed[pl.ds(0, total_rows), :])
    up = back(d_above[...], second_normed[pl.ds(total_rows, r), :]) * inside(z, 1, True)
    down = back(d_below[...], second_normed[pl.ds(total_rows + r, r), :]) * inside(z, 1, False)
    grad, _, _ = convolve(z, own, up, down, 1, pads, None, weight)
    normed = first_normed[...]
    pre = grad * gelu_slope(normed * affine[0:1] + affine[1:2])
    pre_ref[...] = pre
    lane = lax.broadcasted_iota(jnp.int32, (1, 128), 1)
    taps = TAPS * TAPS * C

    def along(row):
        return jnp.concatenate([row[:, :128]] * 3, axis=1)[:, :taps]

    second, left, against, ones = (total[:, n * C : n * C + taps] for n in (SECOND, LEFT, HIDDEN, ONES))
    against = along(stats[1:2]) * (against - along(stats[0:1] - affine[4:5]) * ones)
    first = along(factor) * (left - along(bias_mean) * ones - along(gain_mean) * against)
    sums = jnp.where(lane < C, fold(column_sum(pre)), fold(column_sum(pre * normed)))
    line = jnp.concatenate([sums[:, : 2 * C], second, first], axis=1)
    slabs[...] = jnp.broadcast_to(line[None], slabs.shape)


def back_kernel(z, gathered, pre, normed, stats, affine, dout, second_grads, back_s, back_l, one, two, gain_out, bias_out, second_gain, second_bias, half, lines):
    bias_sum, gain_sum = norm_sums(jnp.sum(gathered[:, :, pl.ds(0, 128)], axis=0))
    bias_out[...] = bias_sum[:, :C]
    gain_out[...] = gain_sum[:, :C]
    second_bias[...] = second_grads[0:1, pl.ds(0, C)]
    second_gain[...] = second_grads[1:2, pl.ds(0, C)]
    value = dout[...] + affine[0:1] * stats[1:2] * (pre[...] - bias_sum / z.pixels - normed[...] * (gain_sum / z.pixels))
    put_halves(half, value)
    from_matrix(z, half, (back_s, back_l))
    for d in range(C):
        lines[pl.ds(d, 1), :] = gathered[d]
    for ref, group in ((two, LAST_SECOND), (one, LAST_FIRST)):
        for a in range(TAPS):
            for b in range(TAPS):
                at = (group + a * TAPS + b) * C
                ref[a, b] = lines[:, pl.ds(at, C)]


def call(body, ins, outs, scratch=(), sems=0):
    space = {"v": pltpu.VMEM, "h": pltpu.HBM, "V": pltpu.VMEM}
    shapes = []
    for item in scratch:
        if isinstance(item, list):
            shapes.append([pltpu.VMEM(*s) for s in item])
        else:
            shapes.append(pltpu.VMEM(*item))
    if sems:
        shapes.append(pltpu.SemaphoreType.DMA((sems,)))
    run = pl.pallas_call(
        body,
        out_shape=[jax.ShapeDtypeStruct(shape, kind) if s == "v" else space[s](shape, kind) for s, shape, kind in outs],
        in_specs=[pl.BlockSpec(memory_space=space[s]) for s in ins],
        out_specs=[pl.BlockSpec(memory_space=space[s]) for s, _, _ in outs],
        scratch_shapes=shapes,
        compiler_params=pltpu.CompilerParams(vmem_limit_bytes=VMEM_LIMIT),
    )
    return lambda *args: run(
        *(pltpu.with_memory_space_constraint(arg, pltpu.HBM) if s == "h" else arg for s, arg in zip(ins, args))
    )


def exchange(lines, axes):
    shape = lines.shape
    if len(shape) == 2:
        lines = lines.reshape(math.prod(lax.axis_size(axis) for axis in axes), -1, 128)
    return lax.all_to_all(lines, axes, 0, 0, tiled=True).reshape(shape)


def beyond(z, pair, other, depths):
    hops = max(-(-depth // rows) for rows in z.rows for depth in depths)
    if hops == 1:
        swap = lambda value, start: lax.ppermute(
            value, "row", [(i + a, i + 1 - a) for i in range(start, z.peers - 1, 2) for a in (0, 1)]
        )
        others = swap(other, 1)
        return swap(pair, 0), others
    even = is_even()
    bottom, top = jnp.where(even, pair, other), jnp.where(even, other, pair)
    above, below = [], []
    for hop in range(1, hops + 1):
        above.append(lax.ppermute(bottom, "row", [(i, i + hop) for i in range(z.peers - hop)]))
        below.append(lax.ppermute(top, "row", [(i + hop, i) for i in range(z.peers - hop)]))
    up, down = [], []
    base = 0
    for depth in depths:
        for n in range(depth):
            for k in (1, 0):
                hop, back = divmod(depth - 1 - n, z.rows[k])
                at = base + (depth - 1 - back) * z.rims + z.rim[k]
                up.append(above[hop][at : at + z.edge[k]])
                hop, back = divmod(n, z.rows[k])
                at = base + back * z.rims + z.rim[k]
                down.append(below[hop][at : at + z.edge[k]])
        base += depth * z.rims
    up.append(jnp.concatenate([pixel_rows(z, above, base, 1, 1), pixel_rows(z, above, base, 0, 1)], axis=1))
    down.append(jnp.concatenate([pixel_rows(z, below, base, 0, 0), pixel_rows(z, below, base, 1, 0)], axis=1))
    up, down = jnp.concatenate(up, axis=0), jnp.concatenate(down, axis=0)
    return jnp.where(even, down, up), jnp.where(even, up, down)


def pixel_rows(z, bands, base, distance, last):
    lines = []
    for k in (0, 1):
        hop, back = divmod(distance, z.rows[k])
        at = base + k * z.images[0]
        half = 128 * abs(last - back)
        lines.append(bands[hop][at : at + z.images[k], half : half + 128])
    lines.append(jnp.zeros((z.slots - sum(z.images), 128), F32))
    return jnp.concatenate(lines, axis=0)


def local(
    image_small, image_large, teacher_small, teacher_large, upstream_small, upstream_large,
    conv_first, gain_first, bias_first, conv_second, gain_second, bias_second,
):
    peers = lax.axis_size("row")
    devices = lax.axis_size("img") * peers
    z = Sizes(image_small.shape, image_large.shape, devices, peers)
    body = lambda function: functools.partial(function, z)
    r = z.rims
    full, half, pair = (z.total, LANES), (2, z.total, 128), (2 * devices, 128)
    weight, left = (2, TAPS * TAP_ROWS, 128), (2, 256, 2 * z.total)
    images = [image_small, image_large, upstream_small, upstream_large, teacher_small, teacher_large]
    f = lambda space, *shape: (space, shape, F32)
    depths = (REACH, 2)
    rim_rows = sum(depths) * r + z.slots

    x, pair_edge, other_edge, copies = call(
        body(start_kernel),
        "hhhhhh",
        [("v", full, F32), f("v", rim_rows, LANES), f("v", rim_rows, LANES), ("V", pair, F32)],
        [[(a.shape, F32) for a in images], (half, F32)],
        4 + 2 * z.images[1],
    )(*images)
    gathered = exchange(copies, AXES)
    pair_rims, other_rims = beyond(z, pair_edge, other_edge, depths)
    params = [conv_first, conv_second] + images[2:]
    w1, w2, weights, affine, upstream, teacher, x_copy = call(
        body(prepare_kernel),
        "hhhhhhhhhhv",
        [("v", weight, BF16), ("v", weight, BF16), ("h", (3,) + weight, BF16), f("v", 5, LANES), ("h", full, F32), f("v", z.total, 128), ("h", full, F32)],
        [[(a.shape, F32) for a in params], ((2,) + weight, BF16), (full, F32), ((4, C), F32), (half, F32)],
        15,
    )(*params, *(v.reshape(1, C) for v in (gain_first, bias_first, gain_second, bias_second)), x)

    hidden, stats_one, copies = call(
        body(first_kernel),
        "vvvvvv",
        [("v", full, F32), f("v", 2, LANES), ("V", pair, F32)],
        [z.pads()],
    )(x, pair_rims, other_rims, gathered, affine, w1)
    gathered = exchange(copies, AXES)
    extended, near_rows = z.total + 4 * r, z.total + 2 * r
    h_above, h_below, left_one, packed, teachers, spread_u, near_u = call(
        body(first_operand_kernel),
        "vvvvvvvhh",
        [f("v", 3 * r, LANES), f("v", 3 * r, LANES), ("h", left, BF16), f("h", C, BACK_LANES), f("h", extended, LANES), f("h", near_rows, LANES), f("h", near_rows, LANES)],
        [
            z.pads(), z.chains(2), z.chains(REACH), (left, BF16), ((2,) + weight, BF16), ((near_rows, LANES), F32), ((extended, 128), F32),
            ((extended, LANES), F32), ((near_rows, LANES), F32), ((C, BACK_LANES), F32),
        ],
        8,
    )(x, hidden, pair_rims, other_rims, stats_one, affine, teacher, upstream, weights)
    gathered, near_u = lax.optimization_barrier((gathered, near_u))

    map_shape = (peers * z.slots, 128)
    out, o_above, o_below, near, stats_two, copies = call(
        body(second_kernel),
        "vvvvvvvvvv",
        [("v", full, F32), f("v", 2 * r, LANES), f("v", 2 * r, LANES), f("v", 2, r, LANES), f("v", 2, LANES), ("V", map_shape, F32)],
        [z.pads(), z.chains(3)],
    )(hidden, h_above, h_below, gathered, affine, w2, x, pair_rims, other_rims, teacher)
    gathered = exchange(copies, ("row",))
    out_copy, hidden_copy, left_two, shifts, by_map, by_teacher, up = call(
        body(second_operand_kernel),
        "vvvvvvvhhhh",
        [
            ("h", full, F32), f("h", near_rows, LANES), ("v", left, BF16), f("h", 3, near_rows, LANES),
            f("v", near_rows, LANES), f("v", near_rows, LANES), f("v", near_rows, LANES),
        ],
        [
            z.pads(), z.chains(2), ((extended, LANES), F32), ((near_rows, LANES), F32), (weight, BF16),
            ((3, near_rows, LANES), F32),
        ],
        14,
    )(hidden, near, stats_two, affine, out, o_above, o_below, teachers, spread_u, near_u, weights)

    dout, dshift, d_above, d_below, slabs = call(
        body(upstream_kernel),
        "vvhhvhvvhv",
        [("v", full, F32), ("v", full, F32), f("v", r, LANES), f("v", r, LANES), f("V", devices, 1, BACK_LANES)],
        [((3, near_rows, LANES), F32), (left, BF16), (full, F32), ((C, BACK_LANES), F32), z.pads(), z.pads()],
        7,
    )(gathered, up, shifts, left_one, left_two, packed, by_map, by_teacher, hidden_copy, stats_two)
    gathered = exchange(slabs, AXES)
    out_s, out_l, first_normed, second_normed, weight_back = call(
        body(write_kernel),
        "hhhhvvv",
        [("v", image_small.shape, F32), ("v", image_large.shape, F32), ("v", full, F32), f("v", near_rows, LANES), ("v", weight, BF16)],
        [(full, F32), (full, F32), ((near_rows, LANES), F32), (half, F32)],
        4,
    )(out_copy, x_copy, hidden_copy, weights, stats_one, stats_two, d_above)

    pre, norm_grads, slabs = call(
        body(hidden_kernel),
        "vvvvvvvvv",
        [("v", full, F32), f("v", 2, 128), f("V", devices, 1, LAST_LANES)],
        [z.pads()],
    )(gathered, dshift, d_above, d_below, second_normed, stats_two, affine, weight_back, first_normed)
    gathered = exchange(slabs, AXES)

    back_s, back_l, one, two, gain_one, bias_one, gain_two, bias_two = call(
        body(back_kernel),
        "vvvvvvv",
        [("v", a.shape, F32) for a in (image_small, image_large, conv_first, conv_second)] + [f("v", 1, C)] * 4,
        [(half, F32), ((C, LAST_LANES), F32)],
    )(gathered, pre, first_normed, stats_one, affine, dout, norm_grads)
    return (
        out_s, out_l, back_s, back_l,
        one, gain_one.reshape(C), bias_one.reshape(C),
        two, gain_two.reshape(C), bias_two.reshape(C),
    )


def solution(mesh):
    split_bands, everywhere = P("img", "row", None), P()
    return jax.shard_map(
        local,
        mesh=mesh,
        in_specs=(split_bands,) * 6 + (everywhere,) * 6,
        out_specs=(split_bands,) * 4 + (everywhere,) * 6,
        check_vma=False,
    )
```

```python
import functools
import math

import jax
import jax.numpy as jnp
from jax import lax
from jax.experimental import pallas as pl
from jax.experimental.pallas import tpu as pltpu
from jax.sharding import PartitionSpec as P

C = 32
HS = 32
HL = 64
HEIGHTS = (HS, HL)

norm_eps = 1e-05
map_eps = 1e-06
beta_weight = 1000.0
AXES = ("img", "row")
BLOCK = 8
LANES = BLOCK * C
TAPS = 3
DEPTH = TAPS * 128 + 256
TAP_ROWS = 128 + 2 * C
REACH = 4
ROOT = math.sqrt(2.0 / math.pi)
CUBE = 0.044715
F32 = jnp.float32
BF16 = jnp.bfloat16
VMEM_LIMIT = 32 * 1024 * 1024
BIAS, GAIN, SECOND, LEFT, HIDDEN, ONES = 0, 1, 2, 11, 20, 29
BACK_LANES = 1280
EARLY = HIDDEN * C
LAST_SECOND, LAST_FIRST, LAST_LANES = 2, 11, 640


class Sizes:
    def __init__(self, small, large, devices, peers):
        self.images = (small[0], large[0])
        self.rows = (small[1], large[1])
        self.blocks = (HS // BLOCK, HL // BLOCK)
        self.step = tuple(n * r for n, r in zip(self.images, self.rows))
        self.count = tuple(b * s for b, s in zip(self.blocks, self.step))
        self.edge = tuple(b * n for b, n in zip(self.blocks, self.images))
        self.start = (self.count[1], 0)
        self.rim = (self.edge[1], 0)
        self.total = sum(self.count)
        self.rims = sum(self.edge)
        self.slots = -(-sum(self.images) // 8) * 8
        self.guard = -(-max(self.images) // 8) * 8
        self.devices = devices
        self.peers = peers
        self.here = float(self.total * BLOCK)
        self.pixels = self.here * devices

    def pads(self):
        return [((TAPS, 2, self.count[k] + 2 * self.step[k], 128), F32) for k in (0, 1)]

    def chains(self, depth):
        return [((2, 2 * self.guard + (depth + 1) * self.rims, 128), F32)] * 2


def split(value):
    high = value.astype(BF16)
    return high, (value - high.astype(F32)).astype(BF16)


def dot(left, right):
    return lax.dot_general(left, right, (((1,), (0,)), ((), ())), preferred_element_type=F32)


def product(left, right):
    if left[0].shape[1] % 128:
        return dot(left[0], right[0]) + (dot(left[0], right[1]) + dot(left[1], right[0]))
    return dot(
        jnp.concatenate([left[0], left[0], left[1]], axis=1), jnp.concatenate([right[0], right[1], right[0]], axis=0)
    )


def spread(left, right):
    right = right.astype(BF16)
    return dot(jnp.concatenate(split(left), axis=1), jnp.concatenate([right, right], axis=0))


def gelu(s):
    return 0.5 * s * (1.0 + jnp.tanh(ROOT * (s + CUBE * s * s * s)))


def gelu_slope(s):
    square = s * s
    t = jnp.tanh(ROOT * s * (1.0 + CUBE * square))
    return 0.5 * (1.0 + t) + 0.5 * s * (1.0 - t * t) * ROOT * (1.0 + 3.0 * CUBE * square)


def spread_groups(row):
    row = row + pltpu.roll(row, 64, 1)
    return row + pltpu.roll(row, 32, 1)


def fold(row):
    return spread_groups(row[:, :128] + row[:, 128:])


def wide(row):
    return jnp.concatenate([row, row], axis=1)


def group_of(rows=1, lanes=128):
    return lax.broadcasted_iota(jnp.int32, (rows, lanes), 1) // C


def column_sum(value):
    return jnp.sum(value, axis=0, keepdims=True)


def send_lines(z, ref, lines):
    for n, line in enumerate(lines):
        ref[pl.ds(n, z.devices, stride=len(lines)), :] = jnp.broadcast_to(line, (z.devices, 128))


def moments(z, value, ref):
    few = min(8, z.total)
    pivot = fold(column_sum(value[:few])) / float(few * BLOCK)
    off = value - wide(pivot)
    first, second = fold(column_sum(off)), fold(column_sum(off * off))
    send_lines(z, ref, [pivot + first / z.here, second - first * first / z.here])


def merged(z, ref):
    means = ref[pl.ds(0, z.devices, stride=2), :]
    center = jnp.mean(means, axis=0, keepdims=True)
    off = means - center
    within = jnp.mean(ref[pl.ds(1, z.devices, stride=2), :], axis=0, keepdims=True)
    variance = within / z.here + jnp.mean(off * off, axis=0, keepdims=True)
    return wide(center), wide(lax.rsqrt(variance + norm_eps))


def put_halves(ref, value):
    ref[0] = value[:, :128]
    ref[1] = value[:, 128:]


def whole(ref):
    return jnp.concatenate([ref[0], ref[1]], axis=1)


def to_matrix(z, refs, half):
    for k in (0, 1):
        for j in range(z.blocks[k]):
            at = z.start[k] + j * z.step[k]
            for i in range(z.images[k]):
                for h in (0, 1):
                    half[h, pl.ds(at + i * z.rows[k], z.rows[k]), :] = refs[k][i, :, pl.ds(LANES * j + 128 * h, 128)]


def from_matrix(z, half, refs):
    for k in (0, 1):
        for j in range(z.blocks[k]):
            at = z.start[k] + j * z.step[k]
            for i in range(z.images[k]):
                for h in (0, 1):
                    refs[k][i, :, pl.ds(LANES * j + 128 * h, 128)] = half[h, pl.ds(at + i * z.rows[k], z.rows[k]), :]


def is_even():
    return lax.axis_index("row") % 2 == 0


def put_edges(pair, other, at, last, first):
    even = is_even()
    pair[at] = jnp.where(even, last, first)
    other[at] = jnp.where(even, first, last)


def above_of(pair, other, at):
    return jnp.where(is_even(), other[at], pair[at])


def below_of(pair, other, at):
    return jnp.where(is_even(), pair[at], other[at])


def take_rims(z, half, depth, pair, other):
    everything = pl.ds(0, 128)
    for k in (0, 1):
        nothing = jnp.zeros((z.edge[k], 128), F32)
        for n in range(depth):
            first, last = nothing, nothing
            if depth - n <= z.rows[k]:
                last = half[pl.ds(z.start[k] + z.rows[k] - depth + n, z.edge[k], stride=z.rows[k]), :]
            if n < z.rows[k]:
                first = half[pl.ds(z.start[k] + n, z.edge[k], stride=z.rows[k]), :]
            put_edges(pair, other, (pl.ds(n * z.rims + z.rim[k], z.edge[k]), everything), last, first)


def inside(z, depth, above):
    at = lax.axis_index("row")
    large = lax.broadcasted_iota(jnp.int32, (z.rims, 1), 0) < z.rim[0]
    parts = []
    for n in range(depth):
        if above:
            ok = [jnp.where(at * rows >= depth - n, 1.0, 0.0) for rows in z.rows]
        else:
            ok = [jnp.where((at + 1) * rows + n + 1 <= height, 1.0, 0.0) for rows, height in zip(z.rows, HEIGHTS)]
        parts.append(jnp.where(large, ok[1], ok[0]).astype(F32))
    return jnp.concatenate(parts, axis=0)


def clear_guards(z, pads, a):
    for k in (0, 1):
        pads[k][a, 1, pl.ds(0, z.step[k]), :] = jnp.zeros((z.step[k], 128), F32)
        pads[k][a, 0, pl.ds(z.step[k] + z.count[k], z.step[k]), :] = jnp.zeros((z.step[k], 128), F32)


def fill_center(z, pads, value):
    clear_guards(z, pads, 1)
    for k in (0, 1):
        for h in (0, 1):
            pads[k][1, h, pl.ds(z.step[k], z.count[k]), :] = value[z.start[k] : z.start[k] + z.count[k], 128 * h : 128 * h + 128]


def fill_shifted(z, pads, above, below):
    for k in (0, 1):
        ref, step, count, rows = pads[k], z.step[k], z.count[k], z.rows[k]
        rim = slice(z.rim[k], z.rim[k] + z.edge[k])
        for h in (0, 1):
            lanes = slice(128 * h, 128 * h + 128)
            ref[0, h, pl.ds(step, count), :] = ref[1, h, pl.ds(step - 1, count), :]
            ref[2, h, pl.ds(step, count), :] = ref[1, h, pl.ds(step + 1, count), :]
            ref[0, h, pl.ds(step, z.edge[k], stride=rows), :] = above[rim, lanes]
            ref[2, h, pl.ds(step + rows - 1, z.edge[k], stride=rows), :] = below[rim, lanes]


def fill_pads(z, pads, value, above, below):
    fill_center(z, pads, value)
    fill_shifted(z, pads, above, below)
    for a in (0, 2):
        clear_guards(z, pads, a)


def beside(left, right):
    lane = lax.broadcasted_iota(jnp.int32, (1, 128), 1)
    middle = pltpu.roll(jnp.where(lane >= 64, left[1], right[1]), 64, 1)
    return [
        jnp.where(lane >= 96, left[0], jnp.where(lane < 32, right[0], middle)),
        jnp.where(lane >= 96, left[2], jnp.where(lane < 32, right[2], 0.0)),
    ]


def band_operand(z, pads):
    parts = ([], [])
    for k in (1, 0):
        ref, step, count = pads[k], z.step[k], z.count[k]
        low, high = ([ref[a, h, pl.ds(step, count), :] for a in range(TAPS)] for h in (0, 1))
        before = [ref[a, 1, pl.ds(0, count), :] for a in range(TAPS)]
        after = [ref[a, 0, pl.ds(2 * step, count), :] for a in range(TAPS)]
        parts[0].append(jnp.concatenate(low + beside(before, high), axis=1))
        parts[1].append(jnp.concatenate(high + beside(low, after), axis=1))
    return [jnp.concatenate(part, axis=0) for part in parts]


def rim_operand(z, chain, depth):
    m = lax.broadcasted_iota(jnp.int32, (z.rims, 1), 0)
    large = m < z.rim[0]
    has_before = jnp.where(large, m, m - z.rim[0]) >= jnp.where(large, z.images[1], z.images[0])
    has_after = m < jnp.where(large, z.rim[0] - z.images[1], z.rims - z.images[0])
    low, high, before, after = [], [], [], []
    for r in range(depth + 1):
        at = z.guard + r * z.rims
        low.append(chain[0, pl.ds(at, z.rims), :])
        high.append(chain[1, pl.ds(at, z.rims), :])
        shifted = [chain[1, pl.ds(at - images, z.rims), :] for images in z.images]
        before.append(jnp.where(has_before, jnp.where(large, shifted[1], shifted[0]), 0.0))
        shifted = [chain[0, pl.ds(at + images, z.rims), :] for images in z.images]
        after.append(jnp.where(has_after, jnp.where(large, shifted[1], shifted[0]), 0.0))
    parts = ([], [])
    for n in range(depth - 1):
        rows = slice(n, n + TAPS)
        parts[0].append(jnp.concatenate(low[rows] + beside(before[rows], high[rows]), axis=1))
        parts[1].append(jnp.concatenate(high[rows] + beside(low[rows], after[rows]), axis=1))
    return [jnp.concatenate(part, axis=0) for part in parts]


def times(parts, weight):
    left = jnp.concatenate([part[h] for h in (0, 1) for part in parts], axis=0)
    both = jnp.concatenate([weight_matrix(weight.at[0]), weight_matrix(weight.at[1])], axis=1)
    result = dot(jnp.concatenate(split(left), axis=1), jnp.concatenate([both, both], axis=0))
    result = result[:, :128] + result[:, 128:]
    rows = result.shape[0] // 2
    return jnp.concatenate([result[:rows], result[rows:]], axis=1)


def rim_operands(z, pads, above, below, depth, chains):
    parts = []
    for side, (rim, chain) in enumerate(zip((above, below), chains)):
        rim_at, own_at = (z.guard, z.guard + depth * z.rims) if side == 0 else (z.guard + z.rims, z.guard)
        for h in (0, 1):
            chain[h, pl.ds(rim_at, depth * z.rims), :] = rim[:, 128 * h : 128 * h + 128]
            for k in (0, 1):
                row = z.step[k] + (0 if side == 0 else z.rows[k] - 1)
                chain[h, pl.ds(own_at + z.rim[k], z.edge[k]), :] = pads[k][1, h, pl.ds(row, z.edge[k], stride=z.rows[k]), :]
        parts.append(rim_operand(z, chain, depth))
    return parts


def convolve(z, own, above, below, depth, pads, chains, weight):
    r = z.rims
    fill_pads(z, pads, own, above[(depth - 1) * r :], below[:r])
    parts = [band_operand(z, pads)]
    if depth > 1:
        parts += rim_operands(z, pads, above, below, depth, chains)
    result = times(parts, weight)
    n = z.total + (depth - 1) * r
    return result[: z.total], result[z.total : n], result[n:]


def convolve_rims(z, pads, above, below, depth, chains, weight):
    result = times(rim_operands(z, pads, above, below, depth, chains), weight)
    n = (depth - 1) * z.rims
    return result[:n], result[n:]


def image_sums(z, value):
    slot = lax.broadcasted_iota(jnp.int32, (z.slots, 1), 0)
    sums = jnp.zeros((z.slots, 128), F32)
    for k in (0, 1):
        line = value[z.start[k] : z.start[k] + z.step[k]]
        for j in range(1, z.blocks[k]):
            at = z.start[k] + j * z.step[k]
            line = line + value[at : at + z.step[k]]
        image = lax.broadcasted_iota(jnp.int32, (z.step[k], 1), 0) // z.rows[k]
        for i in range(z.images[k]):
            sums = jnp.where(slot == i + k * z.images[0], column_sum(jnp.where(image == i, line, 0.0)), sums)
    return sums


def image_rows(z, values, rims):
    parts = []
    for k in (1, 0):
        image = lax.broadcasted_iota(jnp.int32, (z.step[k], 1), 0) // z.rows[k]
        line = jnp.zeros((z.step[k], 128), F32)
        for i in range(z.images[k]):
            at = i + k * z.images[0]
            line = jnp.where(image == i, values[at : at + 1], line)
        parts += [line] * z.blocks[k]
    if rims:
        m = lax.broadcasted_iota(jnp.int32, (z.rims, 1), 0)
        image = jnp.where(m < z.rim[0], z.images[0] + m % z.images[1], (m - z.rim[0]) % z.images[0])
        line = jnp.zeros((z.rims, 128), F32)
        for at in range(sum(z.images)):
            line = jnp.where(image == at, values[at : at + 1], line)
        parts += [line] * rims
    return jnp.concatenate(parts, axis=0)


def channel_mean():
    a = lax.broadcasted_iota(jnp.int32, (LANES, 128), 0) // C
    b = lax.broadcasted_iota(jnp.int32, (LANES, 128), 1) % 64
    return jnp.where(a == b, 1.0 / C, 0.0).astype(F32)


def to_channels():
    a = lax.broadcasted_iota(jnp.int32, (128, LANES), 0)
    b = lax.broadcasted_iota(jnp.int32, (128, LANES), 1) // C
    return jnp.where(a == b, 1.0, 0.0).astype(F32)


def attention(value):
    return spread(value * value, channel_mean())


def pieces(source, target):
    return [(source.at[n], target.at[n]) for n in range(source.shape[0])]


def copies_of(pairs, sems, first=0):
    return [pltpu.make_async_copy(a, b, sems.at[first + n]) for n, (a, b) in enumerate(pairs)]


def start_all(copies):
    for copy in copies:
        copy.start()


def wait_all(copies):
    for copy in copies:
        copy.wait()


def start_kernel(z, small, large, up_s, up_l, t_s, t_l, x, pair, other, copies, raw, half, sems):
    images = [(small, raw[0])] + pieces(large, raw[1])
    rest = [(up_s, raw[2])] + pieces(up_l, raw[3]) + [(t_s, raw[4]), (t_l, raw[5])]
    loads = copies_of(images + rest, sems)
    start_all(loads)
    r, n = z.rims, REACH * z.rims
    tail = n + 2 * r
    for ref in (pair, other):
        ref[pl.ds(tail, z.slots), :] = jnp.zeros((z.slots, LANES), F32)
    wait_all(loads[: len(images)])
    to_matrix(z, raw[:2], half)
    value = whole(half)
    x[...] = value
    moments(z, value, copies)
    for h in (0, 1):
        lanes = pl.ds(128 * h, 128)
        take_rims(z, half.at[h], REACH, pair.at[pl.ds(0, n), lanes], other.at[pl.ds(0, n), lanes])
    wait_all(loads[len(images) :])
    for k in (0, 1):
        width, rows = HEIGHTS[k], z.rows[k]
        for i in range(z.images[k]):
            slot = pl.ds(tail + i + k * z.images[0], 1)
            for d in (0, 1):
                has_last, has_first = rows + d >= 2, d < rows
                last, first = pl.ds(max(rows - 2 + d, 0), 1), pl.ds(min(d, rows - 1), 1)
                for j in range(z.blocks[k]):
                    lanes = pl.ds(LANES * j, LANES)
                    at = (pl.ds(n + d * r + z.rim[k] + j * z.images[k] + i, 1), pl.ds(0, LANES))
                    nothing = jnp.zeros((1, LANES), F32)
                    put_edges(
                        pair, other, at,
                        raw[2 + k][i, last, lanes] if has_last else nothing,
                        raw[2 + k][i, first, lanes] if has_first else nothing,
                    )
                nothing = jnp.zeros((1, width), F32)
                put_edges(
                    pair, other, (slot, pl.ds(128 * d, width)),
                    raw[4 + k][i, last, :] if has_last else nothing,
                    raw[4 + k][i, first, :] if has_first else nothing,
                )


def banded(taps, ref):
    row = lax.broadcasted_iota(jnp.int32, (128, 128), 0) // C
    lane = group_of(128)
    for a in range(TAPS):
        main = jnp.zeros((128, 128), F32)
        for b in range(TAPS):
            main = jnp.where(row - lane + 1 == b, taps[a][b], main)
        before = jnp.where(lane[:C] == 0, taps[a][0][:C], 0.0)
        after = jnp.where(lane[:C] == 3, taps[a][2][:C], 0.0)
        for n, part in enumerate(split(jnp.concatenate([main, before, after], axis=0))):
            ref[n, pl.ds(a * TAP_ROWS, TAP_ROWS), :] = part


def weight_matrix(ref):
    main = [ref[pl.ds(a * TAP_ROWS, 128), :] for a in range(TAPS)]
    before, after = ([ref[pl.ds(a * TAP_ROWS + 128 + n * C, C), :] for a in range(TAPS)] for n in (0, 1))
    return jnp.concatenate(
        main + [after[0], before[1], after[1], before[0], after[2], jnp.zeros((2 * C, 128), BF16), before[2]], axis=0
    )


def prepare_kernel(z, first, second, up_s, up_l, t_s, t_l, g1, b1, g2, b2, x, w1, w2, weights, affine, upstream, teacher, x_copy, raw, kept, kept_u, rows, half, sems):
    targets = tuple(raw) + tuple(rows.at[pl.ds(n, 1), :] for n in range(4))
    refs = (first, second, up_s, up_l, t_s, t_l, g1, b1, g2, b2)
    loads = [pltpu.make_async_copy(a, b, sems.at[n]) for n, (a, b) in enumerate(zip(refs, targets))]
    start_all(loads)
    stores = [pltpu.make_async_copy(x, x_copy, sems.at[13])]
    stores[0].start()
    wait_all(loads)
    to_matrix(z, raw[2:4], half)
    kept_u[...] = whole(half)
    stores.append(pltpu.make_async_copy(kept_u, upstream, sems.at[10]))
    stores[1].start()
    for n, (source, forward) in enumerate(zip(raw[:2], (w1, w2))):
        tiles = []
        for a in range(TAPS):
            line = [jnp.concatenate([source[a, b]] * 4, axis=1) for b in range(TAPS)]
            tiles.append([jnp.concatenate([tap] * 4, axis=0) for tap in line])
        turned = [[tiles[TAPS - 1 - a][TAPS - 1 - b].T for b in range(TAPS)] for a in range(TAPS)]
        banded(tiles, forward)
        if n == 0:
            stores.append(pltpu.make_async_copy(forward, weights.at[2], sems.at[14]))
            stores[-1].start()
        banded(turned, kept.at[n])
        stores.append(pltpu.make_async_copy(kept.at[n], weights.at[n], sems.at[11 + n]))
        stores[-1].start()
    taps = sum(raw[0][a, b] for a in range(TAPS) for b in range(TAPS))
    pivot = dot(jnp.broadcast_to(gelu(rows[1:2]), (8, C)), taps)[0:1]
    affine[...] = jnp.concatenate([jnp.concatenate([rows[...], pivot], axis=0)] * BLOCK, axis=1)
    teacher[...] = jnp.zeros(teacher.shape, F32)
    for k, ref in ((0, raw[4]), (1, raw[5])):
        for i in range(z.images[k]):
            line = ref[i]
            for j in range(z.blocks[k]):
                at = z.start[k] + j * z.step[k] + i * z.rows[k]
                for lane in (0, 64):
                    teacher[pl.ds(at, z.rows[k]), pl.ds(lane, BLOCK)] = line[:, j * BLOCK : (j + 1) * BLOCK]
    wait_all(stores)


def normed_by(stats):
    return lambda v: (v - stats[0:1]) * stats[1:2]


def activation(center, scale, gain, bias):
    factor = scale * gain
    offset = bias - center * factor
    return lambda v: gelu(v * factor + offset)


def first_kernel(z, x, pair, other, gathered, affine, weight, hidden, stats, copies, pads):
    center, scale = merged(z, gathered)
    act = activation(center, scale, affine[0:1], affine[1:2])
    r, lanes = z.rims, pl.ds(0, LANES)
    up = act(above_of(pair, other, (pl.ds((REACH - 1) * r, r), lanes))) * inside(z, 1, True)
    down = act(below_of(pair, other, (pl.ds(0, r), lanes))) * inside(z, 1, False)
    own, _, _ = convolve(z, act(x[...]), up, down, 1, pads, None, weight)
    moments(z, own, copies)
    hidden[...] = own
    stats[0:1] = center
    stats[1:2] = scale


def second_kernel(z, hidden, h_above, h_below, gathered, affine, weight, x, pair, other, teacher, out, o_above, o_below, near, stats, copies, pads, chains):
    center, scale = merged(z, gathered)
    act = activation(center, scale, affine[2:3], affine[3:4])
    r = z.rims
    own = act(hidden[...])
    up, down = act(h_above[...]) * inside(z, 3, True), act(h_below[...]) * inside(z, 3, False)
    own, up, down = convolve(z, own, up, down, 3, pads, chains, weight)
    own = x[...] + own
    amap = attention(own)
    lane = lax.broadcasted_iota(jnp.int32, (1, 128), 1)
    sums = image_sums(z, amap * jnp.where(lane < 64, amap, teacher[...]))
    copies[...] = jnp.concatenate([sums] * z.peers, axis=0)
    out[...] = own
    o_above[...] = above_of(pair, other, (pl.ds(2 * r, 2 * r), pl.ds(0, LANES))) + up
    o_below[...] = below_of(pair, other, (pl.ds(0, 2 * r), pl.ds(0, LANES))) + down
    near[0] = h_above[pl.ds(2 * r, r), :]
    near[1] = h_below[pl.ds(0, r), :]
    stats[0:1] = center
    stats[1:2] = scale


def tap_rows(q):
    return 128 + C if q < 0 else q * C


def tap_product(z, operand, own, above, below, pads):
    fill_center(z, pads, own)
    fill_shifted(z, pads, above, below)
    columns = []
    for a in range(TAPS):
        columns.append(
            jnp.concatenate([pads[k][TAPS - 1 - a, h, pl.ds(z.step[k], z.count[k]), :] for h in (0, 1) for k in (1, 0)], axis=0)
        )
    used = [jnp.concatenate([operand[n, pl.ds(0, 128 + C), :], operand[n, pl.ds(256 - C, C), :]], axis=0) for n in (0, 1)]
    return product(used, split(jnp.concatenate(columns, axis=1)))


def tap_sums(result, tiles, first_group):
    group = group_of()
    for a in range(TAPS):
        for b in range(TAPS):
            total = None
            for p in range(4):
                at = tap_rows(p + b - 1)
                part = result[at : at + C, 128 * a : 128 * a + 128]
                total = part if total is None else jnp.where(group == p, part, total)
            tile, slot = divmod(first_group + a * TAPS + b, 4)
            tiles[tile] = jnp.where(group == slot, spread_groups(total), tiles[tile])


def tap_counts(z, turned, tiles, first_group):
    group = group_of()
    m = lax.broadcasted_iota(jnp.int32, (1, 2 * z.total), 1) % z.total
    row = jnp.where(m < z.start[0], m % z.rows[1], (m - z.start[0]) % z.rows[0])
    height = jnp.where(m < z.start[0], z.rows[1], z.rows[0])
    at = lax.axis_index("row")
    lost = {
        0: (row == height - 1) & (at == z.peers - 1),
        2: (row == 0) & (at == 0),
    }
    for a in range(TAPS):
        column = jnp.sum(jnp.where(lost[a], 0.0, turned) if a in lost else turned, axis=1, keepdims=True)
        used = jnp.concatenate([column[: 128 + C], column[256 - C :]], axis=0)
        for b in range(TAPS):
            total = sum(used[tap_rows(p + b - 1) : tap_rows(p + b - 1) + C] for p in range(4))
            tile, slot = divmod(first_group + a * TAPS + b, 4)
            tiles[tile] = jnp.where(group == slot, total, tiles[tile])


def turned_operand(z, value, pads, kept):
    fill_center(z, pads, value)
    lane = lax.broadcasted_iota(jnp.int32, (1, 128), 1)
    halves = ([], [])
    for k in (1, 0):
        ref, step, count = pads[k], z.step[k], z.count[k]
        low, high = ref[1, 0, pl.ds(step, count), :], ref[1, 1, pl.ds(step, count), :]
        before, after = ref[1, 1, pl.ds(0, count), :], ref[1, 0, pl.ds(2 * step, count), :]
        for part, main, left, right in ((halves[0], low, before, high), (halves[1], high, low, after)):
            part.append(jnp.concatenate([main, jnp.where(lane >= 96, left, jnp.where(lane < 32, right, 0.0))], axis=1))
    turned = jnp.concatenate(halves[0] + halves[1], axis=0).T
    parts = split(turned)
    for n in (0, 1):
        kept[n] = parts[n]
    return turned


def first_operand_kernel(z, x, hidden, pair, other, stats, affine, teacher, upstream, weights, h_above, h_below, left, packed, teachers, spread_u, near_u, pads, chains, deep_chains, kept, kept_w, kept_u, pixels, kept_t, kept_c, kept_packed, sems):
    r, own = z.rims, pl.ds(0, z.total)
    loads = copies_of([(upstream, kept_u.at[own, :]), (weights.at[1], kept_w.at[1])], sems)
    first = pltpu.make_async_copy(weights.at[2], kept_w.at[0], sems.at[7])
    first.start()
    start_all(loads)
    act = activation(stats[0:1], stats[1:2], affine[0:1], affine[1:2])
    value = turned_operand(z, act(x[...]), pads, kept)
    stores = [pltpu.make_async_copy(kept, left, sems.at[2])]
    stores[0].start()
    n, lanes = REACH * r, pl.ds(0, LANES)
    up = act(above_of(pair, other, (pl.ds(0, n), lanes))) * inside(z, REACH, True)
    down = act(below_of(pair, other, (pl.ds(0, n), lanes))) * inside(z, REACH, False)
    first.wait()
    up, down = convolve_rims(z, pads, up, down, REACH, deep_chains, kept_w.at[0])
    h_above[...] = up
    h_below[...] = down
    tiles = [jnp.zeros((C, 128), F32) for _ in range(BACK_LANES // 128)]
    tap_counts(z, value, tiles, ONES)
    pivot = affine[4:5]
    result = tap_product(
        z, kept, hidden[...] - pivot, (up[2 * r :] - pivot) * inside(z, 1, True),
        (down[:r] - pivot) * inside(z, 1, False), pads,
    )
    tap_sums(result, tiles, HIDDEN)
    line = jnp.concatenate(tiles[EARLY // 128 :], axis=1)
    for d in range(z.devices):
        kept_packed[d] = line[d % C : d % C + 1]
    stores.append(pltpu.make_async_copy(kept_packed, packed, sems.at[6]))
    stores[1].start()
    pixels[own, :] = teacher[...]
    pixels[pl.ds(z.total, 4 * r), :] = jnp.zeros((4 * r, 128), F32)
    n = (REACH + 2) * r
    for side, beyond_of in enumerate((above_of, below_of)):
        for d in (0, 1):
            for k in (0, 1):
                line = beyond_of(pair, other, (pl.ds(n + k * z.images[0], z.images[k]), pl.ds(128 * d, 128)))
                for j in range(z.blocks[k]):
                    at = z.total + (2 * side + d) * r + z.rim[k] + j * z.images[k]
                    pixels[pl.ds(at, z.images[k]), pl.ds(0, BLOCK)] = line[:, j * BLOCK : (j + 1) * BLOCK]
    kept_t[...] = spread(pixels[...], to_channels())
    stores.append(pltpu.make_async_copy(kept_t, teachers, sems.at[3]))
    stores[2].start()
    n = REACH * r
    at = (pl.ds(n, 2 * r), pl.ds(0, LANES))
    up, down = above_of(pair, other, at) * inside(z, 2, True), below_of(pair, other, at) * inside(z, 2, False)
    kept_u[pl.ds(z.total, r), :] = up[r:]
    kept_u[pl.ds(z.total + r, r), :] = down[:r]
    wait_all(loads)
    stores.append(pltpu.make_async_copy(kept_u, near_u, sems.at[5]))
    stores[3].start()
    kept_c[...] = jnp.concatenate(convolve(z, kept_u[own, :], up, down, 2, pads, chains, kept_w.at[1]), axis=0)
    stores.append(pltpu.make_async_copy(kept_c, spread_u, sems.at[4]))
    stores[4].start()
    wait_all(stores)


def second_operand_kernel(z, hidden, near, stats, affine, out, o_above, o_below, teachers, spread_u, near_u, weights, out_copy, hidden_copy, left, shifts, by_map, by_teacher, up, pads, chains, kept_t, kept_u, kept_w, kept_s, sems):
    r, total = z.rims, z.total
    loads = [
        pltpu.make_async_copy(teachers, kept_t, sems.at[0]),
        pltpu.make_async_copy(weights.at[1], kept_w, sems.at[1]),
        pltpu.make_async_copy(spread_u, kept_u, sems.at[2]),
    ]
    start_all(loads)
    stores = [
        pltpu.make_async_copy(out, out_copy, sems.at[4]),
        pltpu.make_async_copy(hidden, hidden_copy.at[pl.ds(0, total), :], sems.at[7]),
        pltpu.make_async_copy(near.at[0], hidden_copy.at[pl.ds(total, r), :], sems.at[8]),
        pltpu.make_async_copy(near.at[1], hidden_copy.at[pl.ds(total + r, r), :], sems.at[9]),
        pltpu.make_async_copy(near_u, up, sems.at[10]),
    ]
    start_all(stores)
    normed = normed_by(stats)(jnp.concatenate([hidden[...], near[0], near[1]], axis=0))
    shifted = normed * affine[2:3] + affine[3:4]
    turned_operand(z, gelu(shifted[:total]), pads, left)
    ones = jnp.ones((total, 1), F32)
    masks = jnp.concatenate([ones, inside(z, 1, True), inside(z, 1, False)], axis=0)
    slopes = gelu_slope(shifted) * masks
    o = jnp.concatenate([out[...], o_above[...] * inside(z, 2, True), o_below[...] * inside(z, 2, False)], axis=0)
    for_map = spread(attention(o), to_channels()) * o
    wait_all(loads)
    for_teacher = kept_t[...] * o
    kept_s[0] = kept_u[...] * slopes
    stores += copies_of(pieces(kept_s, shifts), sems, 11)
    stores[-3].start()
    for n, value, ref in ((1, for_map, by_map), (2, for_teacher, by_teacher)):
        own, before, after = value[:total], value[total : total + 2 * r], value[total + 2 * r :]
        ref[...] = jnp.concatenate([own, before[r:], after[:r]], axis=0)
        kept_s[n] = jnp.concatenate(convolve(z, own, before, after, 2, pads, chains, kept_w), axis=0) * slopes
        stores[n - 3].start()
    wait_all(stores)


def upstream_kernel(z, gathered, up, shifts, left_1, left_2, packed, by_map, by_teacher, hidden, stats, dout, dshift, d_above, d_below, slabs, kept_s, kept_left, kept_h, kept, pads, more_pads, sems):
    r, total = z.rims, z.total
    loads = copies_of(
        pieces(shifts, kept_s) + pieces(left_1, kept_left) + [(hidden.at[pl.ds(0, total), :], kept_h), (packed, slabs.at[:, :, pl.ds(EARLY, BACK_LANES - EARLY)])], sems
    )
    start_all(loads)
    lane = lax.broadcasted_iota(jnp.int32, (z.slots, 128), 1)
    sums = sum(gathered[pl.ds(n * z.slots, z.slots), :] for n in range(z.peers))
    square = jnp.sum(jnp.where(lane < 64, sums, 0.0), axis=1, keepdims=True)
    cross = jnp.sum(jnp.where(lane < 64, 0.0, sums), axis=1, keepdims=True)
    inverse = lax.rsqrt(square + map_eps)
    inner = beta_weight * (square * inverse - cross) * inverse
    shape = (z.slots, 128)
    for_map = (beta_weight - inner) * inverse * inverse * (2.0 / C)
    for_teacher = beta_weight * inverse * (2.0 / C)
    for_map, for_teacher = (wide(image_rows(z, jnp.broadcast_to(v, shape), 2)) for v in (for_map, for_teacher))
    value = up[...] + for_map * by_map[...] - for_teacher * by_teacher[...]
    dout[...] = value[:total]
    second = tap_product(z, left_2, value[:total], value[total : total + r], value[total + r :], pads)
    wait_all(loads[:3])
    shift = kept_s[0] + for_map * kept_s[1] - for_teacher * kept_s[2]
    pre, above, below = shift[:total], shift[total : total + r], shift[total + r :]
    dshift[...] = pre
    d_above[...] = above
    d_below[...] = below
    wait_all(loads[3:5])
    first = tap_product(z, kept_left, pre, above, below, more_pads)
    loads[5].wait()
    normed = normed_by(stats)(kept_h[...])
    tiles = [jnp.zeros((C, 128), F32) for _ in range(EARLY // 128)]
    group = group_of()
    tiles[0] = jnp.where(group == BIAS, fold(column_sum(pre)), jnp.where(group == GAIN, fold(column_sum(pre * normed)), tiles[0]))
    tap_sums(second, tiles, SECOND)
    tap_sums(first, tiles, LEFT)
    line = jnp.concatenate(tiles, axis=1)
    for d in range(z.devices):
        kept[d] = line[d % C : d % C + 1]
    send = pltpu.make_async_copy(kept, slabs.at[:, :, pl.ds(0, EARLY)], sems.at[7])
    send.start()
    wait_all([loads[6], send])


def write_kernel(z, out, x, hidden, weights, first_stats, stats, order, out_s, out_l, first_normed, normed, weight, kept, kept_x, kept_h, half, sems):
    loads = [pltpu.make_async_copy(a, b, sems.at[n]) for n, (a, b) in enumerate(((out, kept), (x, kept_x), (hidden, kept_h), (weights.at[0], weight)))]
    start_all(loads)
    loads[0].wait()
    put_halves(half, kept[...])
    from_matrix(z, half, (out_s, out_l))
    loads[1].wait()
    first_normed[...] = normed_by(first_stats)(kept_x[...])
    loads[2].wait()
    normed[...] = normed_by(stats)(kept_h[...])
    loads[3].wait()


def norm_sums(total):
    group = group_of()
    return [wide(spread_groups(jnp.where(group == n, total[:, :128], 0.0))) for n in (BIAS, GAIN)]


def hidden_kernel(z, gathered, dshift, d_above, d_below, second_normed, stats, affine, weight, first_normed, pre_ref, norm_grads, slabs, pads):
    total = jnp.sum(gathered[...], axis=0)
    bias_sum, gain_sum = norm_sums(total)
    norm_grads[0:1] = bias_sum[:, :128]
    norm_grads[1:2] = gain_sum[:, :128]
    bias_mean, gain_mean = bias_sum / z.pixels, gain_sum / z.pixels
    factor = affine[2:3] * stats[1:2]
    r, total_rows = z.rims, z.total

    def back(d, normed):
        return factor * (d - bias_mean - normed * gain_mean)

    own = back(dshift[...], second_normed[pl.ds(0, total_rows), :])
    up = back(d_above[...], second_normed[pl.ds(total_rows, r), :]) * inside(z, 1, True)
    down = back(d_below[...], second_normed[pl.ds(total_rows + r, r), :]) * inside(z, 1, False)
    grad, _, _ = convolve(z, own, up, down, 1, pads, None, weight)
    normed = first_normed[...]
    pre = grad * gelu_slope(normed * affine[0:1] + affine[1:2])
    pre_ref[...] = pre
    lane = lax.broadcasted_iota(jnp.int32, (1, 128), 1)
    taps = TAPS * TAPS * C

    def along(row):
        return jnp.concatenate([row[:, :128]] * 3, axis=1)[:, :taps]

    second, left, against, ones = (total[:, n * C : n * C + taps] for n in (SECOND, LEFT, HIDDEN, ONES))
    against = along(stats[1:2]) * (against - along(stats[0:1] - affine[4:5]) * ones)
    first = along(factor) * (left - along(bias_mean) * ones - along(gain_mean) * against)
    sums = jnp.where(lane < C, fold(column_sum(pre)), fold(column_sum(pre * normed)))
    line = jnp.concatenate([sums[:, : 2 * C], second, first], axis=1)
    slabs[...] = jnp.broadcast_to(line[None], slabs.shape)


def back_kernel(z, gathered, pre, normed, stats, affine, dout, second_grads, back_s, back_l, one, two, gain_out, bias_out, second_gain, second_bias, half, lines):
    bias_sum, gain_sum = norm_sums(jnp.sum(gathered[:, :, pl.ds(0, 128)], axis=0))
    bias_out[...] = bias_sum[:, :C]
    gain_out[...] = gain_sum[:, :C]
    second_bias[...] = second_grads[0:1, pl.ds(0, C)]
    second_gain[...] = second_grads[1:2, pl.ds(0, C)]
    value = dout[...] + affine[0:1] * stats[1:2] * (pre[...] - bias_sum / z.pixels - normed[...] * (gain_sum / z.pixels))
    put_halves(half, value)
    from_matrix(z, half, (back_s, back_l))
    for d in range(C):
        lines[pl.ds(d, 1), :] = gathered[d]
    for ref, group in ((two, LAST_SECOND), (one, LAST_FIRST)):
        for a in range(TAPS):
            for b in range(TAPS):
                at = (group + a * TAPS + b) * C
                ref[a, b] = lines[:, pl.ds(at, C)]


def call(body, ins, outs, scratch=(), sems=0):
    space = {"v": pltpu.VMEM, "h": pltpu.HBM, "V": pltpu.VMEM}
    shapes = []
    for item in scratch:
        if isinstance(item, list):
            shapes.append([pltpu.VMEM(*s) for s in item])
        else:
            shapes.append(pltpu.VMEM(*item))
    if sems:
        shapes.append(pltpu.SemaphoreType.DMA((sems,)))
    run = pl.pallas_call(
        body,
        out_shape=[jax.ShapeDtypeStruct(shape, kind) if s == "v" else space[s](shape, kind) for s, shape, kind in outs],
        in_specs=[pl.BlockSpec(memory_space=space[s]) for s in ins],
        out_specs=[pl.BlockSpec(memory_space=space[s]) for s, _, _ in outs],
        scratch_shapes=shapes,
        compiler_params=pltpu.CompilerParams(vmem_limit_bytes=VMEM_LIMIT),
    )
    return lambda *args: run(
        *(pltpu.with_memory_space_constraint(arg, pltpu.HBM) if s == "h" else arg for s, arg in zip(ins, args))
    )


def exchange(lines, axes):
    shape = lines.shape
    if len(shape) == 2:
        lines = lines.reshape(math.prod(lax.axis_size(axis) for axis in axes), -1, 128)
    return lax.all_to_all(lines, axes, 0, 0, tiled=True).reshape(shape)


def beyond(z, pair, other, depths):
    hops = max(-(-depth // rows) for rows in z.rows for depth in depths)
    if hops == 1:
        swap = lambda value, start: lax.ppermute(
            value, "row", [(i + a, i + 1 - a) for i in range(start, z.peers - 1, 2) for a in (0, 1)]
        )
        others = swap(other, 1)
        return swap(pair, 0), others
    even = is_even()
    bottom, top = jnp.where(even, pair, other), jnp.where(even, other, pair)
    above, below = [], []
    for hop in range(1, hops + 1):
        above.append(lax.ppermute(bottom, "row", [(i, i + hop) for i in range(z.peers - hop)]))
        below.append(lax.ppermute(top, "row", [(i + hop, i) for i in range(z.peers - hop)]))
    up, down = [], []
    base = 0
    for depth in depths:
        for n in range(depth):
            for k in (1, 0):
                hop, back = divmod(depth - 1 - n, z.rows[k])
                at = base + (depth - 1 - back) * z.rims + z.rim[k]
                up.append(above[hop][at : at + z.edge[k]])
                hop, back = divmod(n, z.rows[k])
                at = base + back * z.rims + z.rim[k]
                down.append(below[hop][at : at + z.edge[k]])
        base += depth * z.rims
    up.append(jnp.concatenate([pixel_rows(z, above, base, 1, 1), pixel_rows(z, above, base, 0, 1)], axis=1))
    down.append(jnp.concatenate([pixel_rows(z, below, base, 0, 0), pixel_rows(z, below, base, 1, 0)], axis=1))
    up, down = jnp.concatenate(up, axis=0), jnp.concatenate(down, axis=0)
    return jnp.where(even, down, up), jnp.where(even, up, down)


def pixel_rows(z, bands, base, distance, last):
    lines = []
    for k in (0, 1):
        hop, back = divmod(distance, z.rows[k])
        at = base + k * z.images[0]
        half = 128 * abs(last - back)
        lines.append(bands[hop][at : at + z.images[k], half : half + 128])
    lines.append(jnp.zeros((z.slots - sum(z.images), 128), F32))
    return jnp.concatenate(lines, axis=0)


def local(
    image_small, image_large, teacher_small, teacher_large, upstream_small, upstream_large,
    conv_first, gain_first, bias_first, conv_second, gain_second, bias_second,
):
    peers = lax.axis_size("row")
    devices = lax.axis_size("img") * peers
    z = Sizes(image_small.shape, image_large.shape, devices, peers)
    body = lambda function: functools.partial(function, z)
    r = z.rims
    full, half, pair = (z.total, LANES), (2, z.total, 128), (2 * devices, 128)
    weight, left = (2, TAPS * TAP_ROWS, 128), (2, 256, 2 * z.total)
    images = [image_small, image_large, upstream_small, upstream_large, teacher_small, teacher_large]
    f = lambda space, *shape: (space, shape, F32)
    depths = (REACH, 2)
    rim_rows = sum(depths) * r + z.slots

    x, pair_edge, other_edge, copies = call(
        body(start_kernel),
        "hhhhhh",
        [("v", full, F32), f("v", rim_rows, LANES), f("v", rim_rows, LANES), ("V", pair, F32)],
        [[(a.shape, F32) for a in images], (half, F32)],
        4 + 2 * z.images[1],
    )(*images)
    gathered = exchange(copies, AXES)
    pair_rims, other_rims = beyond(z, pair_edge, other_edge, depths)
    params = [conv_first, conv_second] + images[2:]
    w1, w2, weights, affine, upstream, teacher, x_copy = call(
        body(prepare_kernel),
        "hhhhhhhhhhv",
        [("v", weight, BF16), ("v", weight, BF16), ("h", (3,) + weight, BF16), f("v", 5, LANES), ("h", full, F32), f("v", z.total, 128), ("h", full, F32)],
        [[(a.shape, F32) for a in params], ((2,) + weight, BF16), (full, F32), ((4, C), F32), (half, F32)],
        15,
    )(*params, *(v.reshape(1, C) for v in (gain_first, bias_first, gain_second, bias_second)), x)

    hidden, stats_one, copies = call(
        body(first_kernel),
        "vvvvvv",
        [("v", full, F32), f("v", 2, LANES), ("V", pair, F32)],
        [z.pads()],
    )(x, pair_rims, other_rims, gathered, affine, w1)
    gathered = exchange(copies, AXES)
    extended, near_rows = z.total + 4 * r, z.total + 2 * r
    h_above, h_below, left_one, packed, teachers, spread_u, near_u = call(
        body(first_operand_kernel),
        "vvvvvvvhh",
        [f("v", 3 * r, LANES), f("v", 3 * r, LANES), ("h", left, BF16), f("h", devices, 1, BACK_LANES - EARLY), f("h", extended, LANES), f("h", near_rows, LANES), f("h", near_rows, LANES)],
        [
            z.pads(), z.chains(2), z.chains(REACH), (left, BF16), ((2,) + weight, BF16), ((near_rows, LANES), F32), ((extended, 128), F32),
            ((extended, LANES), F32), ((near_rows, LANES), F32), ((devices, 1, BACK_LANES - EARLY), F32),
        ],
        8,
    )(x, hidden, pair_rims, other_rims, stats_one, affine, teacher, upstream, weights)
    gathered, near_u = lax.optimization_barrier((gathered, near_u))

    map_shape = (peers * z.slots, 128)
    out, o_above, o_below, near, stats_two, copies = call(
        body(second_kernel),
        "vvvvvvvvvv",
        [("v", full, F32), f("v", 2 * r, LANES), f("v", 2 * r, LANES), f("v", 2, r, LANES), f("v", 2, LANES), ("V", map_shape, F32)],
        [z.pads(), z.chains(3)],
    )(hidden, h_above, h_below, gathered, affine, w2, x, pair_rims, other_rims, teacher)
    gathered = exchange(copies, ("row",))
    out_copy, hidden_copy, left_two, shifts, by_map, by_teacher, up = call(
        body(second_operand_kernel),
        "vvvvvvvhhhh",
        [
            ("h", full, F32), f("h", near_rows, LANES), ("v", left, BF16), f("h", 3, near_rows, LANES),
            f("v", near_rows, LANES), f("v", near_rows, LANES), f("v", near_rows, LANES),
        ],
        [
            z.pads(), z.chains(2), ((extended, LANES), F32), ((near_rows, LANES), F32), (weight, BF16),
            ((3, near_rows, LANES), F32),
        ],
        14,
    )(hidden, near, stats_two, affine, out, o_above, o_below, teachers, spread_u, near_u, weights)

    dout, dshift, d_above, d_below, slabs = call(
        body(upstream_kernel),
        "vvhhvhvvhv",
        [("v", full, F32), ("v", full, F32), f("v", r, LANES), f("v", r, LANES), f("h", devices, 1, BACK_LANES)],
        [((3, near_rows, LANES), F32), (left, BF16), (full, F32), ((devices, 1, EARLY), F32), z.pads(), z.pads()],
        8,
    )(gathered, up, shifts, left_one, left_two, packed, by_map, by_teacher, hidden_copy, stats_two)
    gathered = exchange(slabs, AXES)
    out_s, out_l, first_normed, second_normed, weight_back = call(
        body(write_kernel),
        "hhhhvvv",
        [("v", image_small.shape, F32), ("v", image_large.shape, F32), ("v", full, F32), f("v", near_rows, LANES), ("v", weight, BF16)],
        [(full, F32), (full, F32), ((near_rows, LANES), F32), (half, F32)],
        4,
    )(out_copy, x_copy, hidden_copy, weights, stats_one, stats_two, d_above)

    pre, norm_grads, slabs = call(
        body(hidden_kernel),
        "vvvvvvvvv",
        [("v", full, F32), f("v", 2, 128), f("V", devices, 1, LAST_LANES)],
        [z.pads()],
    )(gathered, dshift, d_above, d_below, second_normed, stats_two, affine, weight_back, first_normed)
    gathered = exchange(slabs, AXES)

    back_s, back_l, one, two, gain_one, bias_one, gain_two, bias_two = call(
        body(back_kernel),
        "vvvvvvv",
        [("v", a.shape, F32) for a in (image_small, image_large, conv_first, conv_second)] + [f("v", 1, C)] * 4,
        [(half, F32), ((C, LAST_LANES), F32)],
    )(gathered, pre, first_normed, stats_one, affine, dout, norm_grads)
    return (
        out_s, out_l, back_s, back_l,
        one, gain_one.reshape(C), bias_one.reshape(C),
        two, gain_two.reshape(C), bias_two.reshape(C),
    )


def solution(mesh):
    split_bands, everywhere = P("img", "row", None), P()
    return jax.shard_map(
        local,
        mesh=mesh,
        in_specs=(split_bands,) * 6 + (everywhere,) * 6,
        out_specs=(split_bands,) * 4 + (everywhere,) * 6,
        check_vma=False,
    )
```

```python
import functools
import math

import jax
import jax.numpy as jnp
from jax import lax
from jax.experimental import pallas as pl
from jax.experimental.pallas import tpu as pltpu
from jax.sharding import PartitionSpec as P

C = 32
HS = 32
HL = 64
HEIGHTS = (HS, HL)

norm_eps = 1e-05
map_eps = 1e-06
beta_weight = 1000.0
AXES = ("img", "row")
BLOCK = 8
LANES = BLOCK * C
TAPS = 3
DEPTH = TAPS * 128 + 256
TAP_ROWS = 128 + 2 * C
REACH = 4
ROOT = math.sqrt(2.0 / math.pi)
CUBE = 0.044715
F32 = jnp.float32
BF16 = jnp.bfloat16
VMEM_LIMIT = 32 * 1024 * 1024
BIAS, GAIN, SECOND, LEFT, HIDDEN, ONES = 0, 1, 2, 11, 20, 29
BACK_LANES = 1280
LAST_SECOND, LAST_FIRST, LAST_LANES = 2, 11, 640


class Sizes:
    def __init__(self, small, large, devices, peers):
        self.images = (small[0], large[0])
        self.rows = (small[1], large[1])
        self.blocks = (HS // BLOCK, HL // BLOCK)
        self.step = tuple(n * r for n, r in zip(self.images, self.rows))
        self.count = tuple(b * s for b, s in zip(self.blocks, self.step))
        self.edge = tuple(b * n for b, n in zip(self.blocks, self.images))
        self.start = (self.count[1], 0)
        self.rim = (self.edge[1], 0)
        self.total = sum(self.count)
        self.rims = sum(self.edge)
        self.slots = -(-sum(self.images) // 8) * 8
        self.guard = -(-max(self.images) // 8) * 8
        self.devices = devices
        self.peers = peers
        self.here = float(self.total * BLOCK)
        self.pixels = self.here * devices

    def pads(self):
        return [((TAPS, 2, self.count[k] + 2 * self.step[k], 128), F32) for k in (0, 1)]

    def chains(self, depth):
        return [((2, 2 * self.guard + (depth + 1) * self.rims, 128), F32)] * 2


def split(value):
    high = value.astype(BF16)
    return high, (value - high.astype(F32)).astype(BF16)


def dot(left, right):
    return lax.dot_general(left, right, (((1,), (0,)), ((), ())), preferred_element_type=F32)


def product(left, right):
    if left[0].shape[1] % 128:
        return dot(left[0], right[0]) + (dot(left[0], right[1]) + dot(left[1], right[0]))
    return dot(
        jnp.concatenate([left[0], left[0], left[1]], axis=1), jnp.concatenate([right[0], right[1], right[0]], axis=0)
    )


def spread(left, right):
    right = right.astype(BF16)
    return dot(jnp.concatenate(split(left), axis=1), jnp.concatenate([right, right], axis=0))


def gelu(s):
    return 0.5 * s * (1.0 + jnp.tanh(ROOT * (s + CUBE * s * s * s)))


def gelu_slope(s):
    square = s * s
    t = jnp.tanh(ROOT * s * (1.0 + CUBE * square))
    return 0.5 * (1.0 + t) + 0.5 * s * (1.0 - t * t) * ROOT * (1.0 + 3.0 * CUBE * square)


def spread_groups(row):
    row = row + pltpu.roll(row, 64, 1)
    return row + pltpu.roll(row, 32, 1)


def fold(row):
    return spread_groups(row[:, :128] + row[:, 128:])


def wide(row):
    return jnp.concatenate([row, row], axis=1)


def group_of(rows=1, lanes=128):
    return lax.broadcasted_iota(jnp.int32, (rows, lanes), 1) // C


def column_sum(value):
    return jnp.sum(value, axis=0, keepdims=True)


def send_lines(z, ref, lines):
    for n, line in enumerate(lines):
        ref[pl.ds(n, z.devices, stride=len(lines)), :] = jnp.broadcast_to(line, (z.devices, 128))


def moments(z, value, ref):
    few = min(8, z.total)
    pivot = fold(column_sum(value[:few])) / float(few * BLOCK)
    off = value - wide(pivot)
    first, second = fold(column_sum(off)), fold(column_sum(off * off))
    send_lines(z, ref, [pivot + first / z.here, second - first * first / z.here])


def merged(z, ref):
    means = ref[pl.ds(0, z.devices, stride=2), :]
    center = jnp.mean(means, axis=0, keepdims=True)
    off = means - center
    within = jnp.mean(ref[pl.ds(1, z.devices, stride=2), :], axis=0, keepdims=True)
    variance = within / z.here + jnp.mean(off * off, axis=0, keepdims=True)
    return wide(center), wide(lax.rsqrt(variance + norm_eps))


def put_halves(ref, value):
    ref[0] = value[:, :128]
    ref[1] = value[:, 128:]


def whole(ref):
    return jnp.concatenate([ref[0], ref[1]], axis=1)


def to_matrix(z, refs, half):
    for k in (0, 1):
        for j in range(z.blocks[k]):
            at = z.start[k] + j * z.step[k]
            for i in range(z.images[k]):
                for h in (0, 1):
                    half[h, pl.ds(at + i * z.rows[k], z.rows[k]), :] = refs[k][i, :, pl.ds(LANES * j + 128 * h, 128)]


def from_matrix(z, half, refs):
    for k in (0, 1):
        for j in range(z.blocks[k]):
            at = z.start[k] + j * z.step[k]
            for i in range(z.images[k]):
                for h in (0, 1):
                    refs[k][i, :, pl.ds(LANES * j + 128 * h, 128)] = half[h, pl.ds(at + i * z.rows[k], z.rows[k]), :]


def is_even():
    return lax.axis_index("row") % 2 == 0


def put_edges(pair, other, at, last, first):
    even = is_even()
    pair[at] = jnp.where(even, last, first)
    other[at] = jnp.where(even, first, last)


def above_of(pair, other, at):
    return jnp.where(is_even(), other[at], pair[at])


def below_of(pair, other, at):
    return jnp.where(is_even(), pair[at], other[at])


def take_rims(z, half, depth, pair, other):
    everything = pl.ds(0, 128)
    for k in (0, 1):
        nothing = jnp.zeros((z.edge[k], 128), F32)
        for n in range(depth):
            first, last = nothing, nothing
            if depth - n <= z.rows[k]:
                last = half[pl.ds(z.start[k] + z.rows[k] - depth + n, z.edge[k], stride=z.rows[k]), :]
            if n < z.rows[k]:
                first = half[pl.ds(z.start[k] + n, z.edge[k], stride=z.rows[k]), :]
            put_edges(pair, other, (pl.ds(n * z.rims + z.rim[k], z.edge[k]), everything), last, first)


def inside(z, depth, above):
    at = lax.axis_index("row")
    large = lax.broadcasted_iota(jnp.int32, (z.rims, 1), 0) < z.rim[0]
    parts = []
    for n in range(depth):
        if above:
            ok = [jnp.where(at * rows >= depth - n, 1.0, 0.0) for rows in z.rows]
        else:
            ok = [jnp.where((at + 1) * rows + n + 1 <= height, 1.0, 0.0) for rows, height in zip(z.rows, HEIGHTS)]
        parts.append(jnp.where(large, ok[1], ok[0]).astype(F32))
    return jnp.concatenate(parts, axis=0)


def clear_guards(z, pads, a):
    for k in (0, 1):
        pads[k][a, 1, pl.ds(0, z.step[k]), :] = jnp.zeros((z.step[k], 128), F32)
        pads[k][a, 0, pl.ds(z.step[k] + z.count[k], z.step[k]), :] = jnp.zeros((z.step[k], 128), F32)


def fill_center(z, pads, value):
    clear_guards(z, pads, 1)
    for k in (0, 1):
        for h in (0, 1):
            pads[k][1, h, pl.ds(z.step[k], z.count[k]), :] = value[z.start[k] : z.start[k] + z.count[k], 128 * h : 128 * h + 128]


def fill_shifted(z, pads, above, below):
    for k in (0, 1):
        ref, step, count, rows = pads[k], z.step[k], z.count[k], z.rows[k]
        rim = slice(z.rim[k], z.rim[k] + z.edge[k])
        for h in (0, 1):
            lanes = slice(128 * h, 128 * h + 128)
            ref[0, h, pl.ds(step, count), :] = ref[1, h, pl.ds(step - 1, count), :]
            ref[2, h, pl.ds(step, count), :] = ref[1, h, pl.ds(step + 1, count), :]
            ref[0, h, pl.ds(step, z.edge[k], stride=rows), :] = above[rim, lanes]
            ref[2, h, pl.ds(step + rows - 1, z.edge[k], stride=rows), :] = below[rim, lanes]


def fill_pads(z, pads, value, above, below):
    fill_center(z, pads, value)
    fill_shifted(z, pads, above, below)
    for a in (0, 2):
        clear_guards(z, pads, a)


def beside(left, right):
    lane = lax.broadcasted_iota(jnp.int32, (1, 128), 1)
    middle = pltpu.roll(jnp.where(lane >= 64, left[1], right[1]), 64, 1)
    return [
        jnp.where(lane >= 96, left[0], jnp.where(lane < 32, right[0], middle)),
        jnp.where(lane >= 96, left[2], jnp.where(lane < 32, right[2], 0.0)),
    ]


def band_operand(z, pads):
    parts = ([], [])
    for k in (1, 0):
        ref, step, count = pads[k], z.step[k], z.count[k]
        low, high = ([ref[a, h, pl.ds(step, count), :] for a in range(TAPS)] for h in (0, 1))
        before = [ref[a, 1, pl.ds(0, count), :] for a in range(TAPS)]
        after = [ref[a, 0, pl.ds(2 * step, count), :] for a in range(TAPS)]
        parts[0].append(jnp.concatenate(low + beside(before, high), axis=1))
        parts[1].append(jnp.concatenate(high + beside(low, after), axis=1))
    return [jnp.concatenate(part, axis=0) for part in parts]


def rim_operand(z, chain, depth):
    m = lax.broadcasted_iota(jnp.int32, (z.rims, 1), 0)
    large = m < z.rim[0]
    has_before = jnp.where(large, m, m - z.rim[0]) >= jnp.where(large, z.images[1], z.images[0])
    has_after = m < jnp.where(large, z.rim[0] - z.images[1], z.rims - z.images[0])
    low, high, before, after = [], [], [], []
    for r in range(depth + 1):
        at = z.guard + r * z.rims
        low.append(chain[0, pl.ds(at, z.rims), :])
        high.append(chain[1, pl.ds(at, z.rims), :])
        shifted = [chain[1, pl.ds(at - images, z.rims), :] for images in z.images]
        before.append(jnp.where(has_before, jnp.where(large, shifted[1], shifted[0]), 0.0))
        shifted = [chain[0, pl.ds(at + images, z.rims), :] for images in z.images]
        after.append(jnp.where(has_after, jnp.where(large, shifted[1], shifted[0]), 0.0))
    parts = ([], [])
    for n in range(depth - 1):
        rows = slice(n, n + TAPS)
        parts[0].append(jnp.concatenate(low[rows] + beside(before[rows], high[rows]), axis=1))
        parts[1].append(jnp.concatenate(high[rows] + beside(low[rows], after[rows]), axis=1))
    return [jnp.concatenate(part, axis=0) for part in parts]


def times(parts, weight):
    left = jnp.concatenate([part[h] for h in (0, 1) for part in parts], axis=0)
    both = jnp.concatenate([weight_matrix(weight.at[0]), weight_matrix(weight.at[1])], axis=1)
    result = dot(jnp.concatenate(split(left), axis=1), jnp.concatenate([both, both], axis=0))
    result = result[:, :128] + result[:, 128:]
    rows = result.shape[0] // 2
    return jnp.concatenate([result[:rows], result[rows:]], axis=1)


def rim_operands(z, pads, above, below, depth, chains):
    parts = []
    for side, (rim, chain) in enumerate(zip((above, below), chains)):
        rim_at, own_at = (z.guard, z.guard + depth * z.rims) if side == 0 else (z.guard + z.rims, z.guard)
        for h in (0, 1):
            chain[h, pl.ds(rim_at, depth * z.rims), :] = rim[:, 128 * h : 128 * h + 128]
            for k in (0, 1):
                row = z.step[k] + (0 if side == 0 else z.rows[k] - 1)
                chain[h, pl.ds(own_at + z.rim[k], z.edge[k]), :] = pads[k][1, h, pl.ds(row, z.edge[k], stride=z.rows[k]), :]
        parts.append(rim_operand(z, chain, depth))
    return parts


def convolve(z, own, above, below, depth, pads, chains, weight):
    r = z.rims
    fill_pads(z, pads, own, above[(depth - 1) * r :], below[:r])
    parts = [band_operand(z, pads)]
    if depth > 1:
        parts += rim_operands(z, pads, above, below, depth, chains)
    result = times(parts, weight)
    n = z.total + (depth - 1) * r
    return result[: z.total], result[z.total : n], result[n:]


def convolve_rims(z, pads, above, below, depth, chains, weight):
    result = times(rim_operands(z, pads, above, below, depth, chains), weight)
    n = (depth - 1) * z.rims
    return result[:n], result[n:]


def image_sums(z, value):
    slot = lax.broadcasted_iota(jnp.int32, (z.slots, 1), 0)
    sums = jnp.zeros((z.slots, 128), F32)
    for k in (0, 1):
        line = value[z.start[k] : z.start[k] + z.step[k]]
        for j in range(1, z.blocks[k]):
            at = z.start[k] + j * z.step[k]
            line = line + value[at : at + z.step[k]]
        image = lax.broadcasted_iota(jnp.int32, (z.step[k], 1), 0) // z.rows[k]
        for i in range(z.images[k]):
            sums = jnp.where(slot == i + k * z.images[0], column_sum(jnp.where(image == i, line, 0.0)), sums)
    return sums


def image_rows(z, values, rims):
    parts = []
    for k in (1, 0):
        image = lax.broadcasted_iota(jnp.int32, (z.step[k], 1), 0) // z.rows[k]
        line = jnp.zeros((z.step[k], 128), F32)
        for i in range(z.images[k]):
            at = i + k * z.images[0]
            line = jnp.where(image == i, values[at : at + 1], line)
        parts += [line] * z.blocks[k]
    if rims:
        m = lax.broadcasted_iota(jnp.int32, (z.rims, 1), 0)
        image = jnp.where(m < z.rim[0], z.images[0] + m % z.images[1], (m - z.rim[0]) % z.images[0])
        line = jnp.zeros((z.rims, 128), F32)
        for at in range(sum(z.images)):
            line = jnp.where(image == at, values[at : at + 1], line)
        parts += [line] * rims
    return jnp.concatenate(parts, axis=0)


def channel_mean():
    a = lax.broadcasted_iota(jnp.int32, (LANES, 128), 0) // C
    b = lax.broadcasted_iota(jnp.int32, (LANES, 128), 1) % 64
    return jnp.where(a == b, 1.0 / C, 0.0).astype(F32)


def to_channels():
    a = lax.broadcasted_iota(jnp.int32, (128, LANES), 0)
    b = lax.broadcasted_iota(jnp.int32, (128, LANES), 1) // C
    return jnp.where(a == b, 1.0, 0.0).astype(F32)


def attention(value):
    return spread(value * value, channel_mean())


def pieces(source, target):
    return [(source.at[n], target.at[n]) for n in range(source.shape[0])]


def copies_of(pairs, sems, first=0):
    return [pltpu.make_async_copy(a, b, sems.at[first + n]) for n, (a, b) in enumerate(pairs)]


def start_all(copies):
    for copy in copies:
        copy.start()


def wait_all(copies):
    for copy in copies:
        copy.wait()


def start_kernel(z, small, large, up_s, up_l, t_s, t_l, x, pair, other, copies, raw, half, sems):
    images = [(small, raw[0])] + pieces(large, raw[1])
    rest = [(up_s, raw[2])] + pieces(up_l, raw[3]) + [(t_s, raw[4]), (t_l, raw[5])]
    loads = copies_of(images + rest, sems)
    start_all(loads)
    r, n = z.rims, REACH * z.rims
    tail = n + 2 * r
    for ref in (pair, other):
        ref[pl.ds(tail, z.slots), :] = jnp.zeros((z.slots, LANES), F32)
    wait_all(loads[: len(images)])
    to_matrix(z, raw[:2], half)
    value = whole(half)
    x[...] = value
    moments(z, value, copies)
    for h in (0, 1):
        lanes = pl.ds(128 * h, 128)
        take_rims(z, half.at[h], REACH, pair.at[pl.ds(0, n), lanes], other.at[pl.ds(0, n), lanes])
    wait_all(loads[len(images) :])
    for k in (0, 1):
        width, rows = HEIGHTS[k], z.rows[k]
        for i in range(z.images[k]):
            slot = pl.ds(tail + i + k * z.images[0], 1)
            for d in (0, 1):
                has_last, has_first = rows + d >= 2, d < rows
                last, first = pl.ds(max(rows - 2 + d, 0), 1), pl.ds(min(d, rows - 1), 1)
                for j in range(z.blocks[k]):
                    lanes = pl.ds(LANES * j, LANES)
                    at = (pl.ds(n + d * r + z.rim[k] + j * z.images[k] + i, 1), pl.ds(0, LANES))
                    nothing = jnp.zeros((1, LANES), F32)
                    put_edges(
                        pair, other, at,
                        raw[2 + k][i, last, lanes] if has_last else nothing,
                        raw[2 + k][i, first, lanes] if has_first else nothing,
                    )
                nothing = jnp.zeros((1, width), F32)
                put_edges(
                    pair, other, (slot, pl.ds(128 * d, width)),
                    raw[4 + k][i, last, :] if has_last else nothing,
                    raw[4 + k][i, first, :] if has_first else nothing,
                )


def banded(taps, ref):
    row = lax.broadcasted_iota(jnp.int32, (128, 128), 0) // C
    lane = group_of(128)
    for a in range(TAPS):
        main = jnp.zeros((128, 128), F32)
        for b in range(TAPS):
            main = jnp.where(row - lane + 1 == b, taps[a][b], main)
        before = jnp.where(lane[:C] == 0, taps[a][0][:C], 0.0)
        after = jnp.where(lane[:C] == 3, taps[a][2][:C], 0.0)
        for n, part in enumerate(split(jnp.concatenate([main, before, after], axis=0))):
            ref[n, pl.ds(a * TAP_ROWS, TAP_ROWS), :] = part


def weight_matrix(ref):
    main = [ref[pl.ds(a * TAP_ROWS, 128), :] for a in range(TAPS)]
    before, after = ([ref[pl.ds(a * TAP_ROWS + 128 + n * C, C), :] for a in range(TAPS)] for n in (0, 1))
    return jnp.concatenate(
        main + [after[0], before[1], after[1], before[0], after[2], jnp.zeros((2 * C, 128), BF16), before[2]], axis=0
    )


def prepare_kernel(z, first, second, up_s, up_l, t_s, t_l, g1, b1, g2, b2, x, w1, w2, weights, affine, upstream, teacher, x_copy, raw, kept, kept_u, rows, half, sems):
    targets = tuple(raw) + tuple(rows.at[pl.ds(n, 1), :] for n in range(4))
    refs = (first, second, up_s, up_l, t_s, t_l, g1, b1, g2, b2)
    loads = [pltpu.make_async_copy(a, b, sems.at[n]) for n, (a, b) in enumerate(zip(refs, targets))]
    start_all(loads)
    stores = [pltpu.make_async_copy(x, x_copy, sems.at[13])]
    stores[0].start()
    wait_all(loads)
    to_matrix(z, raw[2:4], half)
    kept_u[...] = whole(half)
    stores.append(pltpu.make_async_copy(kept_u, upstream, sems.at[10]))
    stores[1].start()
    for n, (source, forward) in enumerate(zip(raw[:2], (w1, w2))):
        tiles = []
        for a in range(TAPS):
            line = [jnp.concatenate([source[a, b]] * 4, axis=1) for b in range(TAPS)]
            tiles.append([jnp.concatenate([tap] * 4, axis=0) for tap in line])
        turned = [[tiles[TAPS - 1 - a][TAPS - 1 - b].T for b in range(TAPS)] for a in range(TAPS)]
        banded(tiles, forward)
        if n == 0:
            stores.append(pltpu.make_async_copy(forward, weights.at[2], sems.at[14]))
            stores[-1].start()
        banded(turned, kept.at[n])
        stores.append(pltpu.make_async_copy(kept.at[n], weights.at[n], sems.at[11 + n]))
        stores[-1].start()
    taps = sum(raw[0][a, b] for a in range(TAPS) for b in range(TAPS))
    pivot = dot(jnp.broadcast_to(gelu(rows[1:2]), (8, C)), taps)[0:1]
    affine[...] = jnp.concatenate([jnp.concatenate([rows[...], pivot], axis=0)] * BLOCK, axis=1)
    teacher[...] = jnp.zeros(teacher.shape, F32)
    for k, ref in ((0, raw[4]), (1, raw[5])):
        for i in range(z.images[k]):
            line = ref[i]
            for j in range(z.blocks[k]):
                at = z.start[k] + j * z.step[k] + i * z.rows[k]
                for lane in (0, 64):
                    teacher[pl.ds(at, z.rows[k]), pl.ds(lane, BLOCK)] = line[:, j * BLOCK : (j + 1) * BLOCK]
    wait_all(stores)


def normed_by(stats):
    return lambda v: (v - stats[0:1]) * stats[1:2]


def activation(center, scale, gain, bias):
    factor = scale * gain
    offset = bias - center * factor
    return lambda v: gelu(v * factor + offset)


def first_kernel(z, x, pair, other, gathered, affine, weight, hidden, stats, copies, pads):
    center, scale = merged(z, gathered)
    act = activation(center, scale, affine[0:1], affine[1:2])
    r, lanes = z.rims, pl.ds(0, LANES)
    up = act(above_of(pair, other, (pl.ds((REACH - 1) * r, r), lanes))) * inside(z, 1, True)
    down = act(below_of(pair, other, (pl.ds(0, r), lanes))) * inside(z, 1, False)
    own, _, _ = convolve(z, act(x[...]), up, down, 1, pads, None, weight)
    moments(z, own, copies)
    hidden[...] = own
    stats[0:1] = center
    stats[1:2] = scale


def second_kernel(z, hidden, h_above, h_below, gathered, affine, weight, x, pair, other, teacher, out, o_above, o_below, near, stats, copies, pads, chains):
    center, scale = merged(z, gathered)
    act = activation(center, scale, affine[2:3], affine[3:4])
    r = z.rims
    own = act(hidden[...])
    up, down = act(h_above[...]) * inside(z, 3, True), act(h_below[...]) * inside(z, 3, False)
    own, up, down = convolve(z, own, up, down, 3, pads, chains, weight)
    own = x[...] + own
    amap = attention(own)
    lane = lax.broadcasted_iota(jnp.int32, (1, 128), 1)
    sums = image_sums(z, amap * jnp.where(lane < 64, amap, teacher[...]))
    copies[...] = jnp.concatenate([sums] * z.peers, axis=0)
    out[...] = own
    o_above[...] = above_of(pair, other, (pl.ds(2 * r, 2 * r), pl.ds(0, LANES))) + up
    o_below[...] = below_of(pair, other, (pl.ds(0, 2 * r), pl.ds(0, LANES))) + down
    near[0] = h_above[pl.ds(2 * r, r), :]
    near[1] = h_below[pl.ds(0, r), :]
    stats[0:1] = center
    stats[1:2] = scale


def tap_rows(q):
    return 128 + C if q < 0 else q * C


def tap_product(z, operand, own, above, below, pads):
    fill_center(z, pads, own)
    fill_shifted(z, pads, above, below)
    columns = []
    for a in range(TAPS):
        if a == 1:
            columns.append(jnp.concatenate([own[:, :128], own[:, 128:]], axis=0))
            continue
        columns.append(
            jnp.concatenate([pads[k][TAPS - 1 - a, h, pl.ds(z.step[k], z.count[k]), :] for h in (0, 1) for k in (1, 0)], axis=0)
        )
    used = [jnp.concatenate([operand[n, pl.ds(0, 128 + C), :], operand[n, pl.ds(256 - C, C), :]], axis=0) for n in (0, 1)]
    return product(used, split(jnp.concatenate(columns, axis=1)))


def tap_sums(result, tiles, first_group):
    group = group_of()
    for a in range(TAPS):
        for b in range(TAPS):
            total = None
            for p in range(4):
                at = tap_rows(p + b - 1)
                part = result[at : at + C, 128 * a : 128 * a + 128]
                total = part if total is None else jnp.where(group == p, part, total)
            tile, slot = divmod(first_group + a * TAPS + b, 4)
            tiles[tile] = jnp.where(group == slot, spread_groups(total), tiles[tile])


def tap_counts(z, turned, tiles, first_group):
    group = group_of()
    m = lax.broadcasted_iota(jnp.int32, (1, 2 * z.total), 1) % z.total
    row = jnp.where(m < z.start[0], m % z.rows[1], (m - z.start[0]) % z.rows[0])
    height = jnp.where(m < z.start[0], z.rows[1], z.rows[0])
    at = lax.axis_index("row")
    lost = {
        0: (row == height - 1) & (at == z.peers - 1),
        2: (row == 0) & (at == 0),
    }
    for a in range(TAPS):
        column = jnp.sum(jnp.where(lost[a], 0.0, turned) if a in lost else turned, axis=1, keepdims=True)
        used = jnp.concatenate([column[: 128 + C], column[256 - C :]], axis=0)
        for b in range(TAPS):
            total = sum(used[tap_rows(p + b - 1) : tap_rows(p + b - 1) + C] for p in range(4))
            tile, slot = divmod(first_group + a * TAPS + b, 4)
            tiles[tile] = jnp.where(group == slot, total, tiles[tile])


def turned_operand(z, value, pads, kept):
    fill_center(z, pads, value)
    lane = lax.broadcasted_iota(jnp.int32, (1, 128), 1)
    halves = ([], [])
    for k in (1, 0):
        ref, step, count = pads[k], z.step[k], z.count[k]
        low, high = ref[1, 0, pl.ds(step, count), :], ref[1, 1, pl.ds(step, count), :]
        before, after = ref[1, 1, pl.ds(0, count), :], ref[1, 0, pl.ds(2 * step, count), :]
        for part, main, left, right in ((halves[0], low, before, high), (halves[1], high, low, after)):
            part.append(jnp.concatenate([main, jnp.where(lane >= 96, left, jnp.where(lane < 32, right, 0.0))], axis=1))
    turned = jnp.concatenate(halves[0] + halves[1], axis=0).T
    parts = split(turned)
    for n in (0, 1):
        kept[n] = parts[n]
    return turned


def first_operand_kernel(z, x, hidden, pair, other, stats, affine, teacher, upstream, weights, h_above, h_below, left, packed, teachers, spread_u, near_u, pads, chains, deep_chains, kept, kept_w, kept_u, pixels, kept_t, kept_c, kept_packed, sems):
    r, own = z.rims, pl.ds(0, z.total)
    loads = copies_of([(upstream, kept_u.at[own, :]), (weights.at[1], kept_w.at[1])], sems)
    first = pltpu.make_async_copy(weights.at[2], kept_w.at[0], sems.at[7])
    first.start()
    start_all(loads)
    act = activation(stats[0:1], stats[1:2], affine[0:1], affine[1:2])
    value = turned_operand(z, act(x[...]), pads, kept)
    stores = [pltpu.make_async_copy(kept, left, sems.at[2])]
    stores[0].start()
    n, lanes = REACH * r, pl.ds(0, LANES)
    up = act(above_of(pair, other, (pl.ds(0, n), lanes))) * inside(z, REACH, True)
    down = act(below_of(pair, other, (pl.ds(0, n), lanes))) * inside(z, REACH, False)
    first.wait()
    up, down = convolve_rims(z, pads, up, down, REACH, deep_chains, kept_w.at[0])
    h_above[...] = up
    h_below[...] = down
    tiles = [jnp.zeros((C, 128), F32) for _ in range(BACK_LANES // 128)]
    tap_counts(z, value, tiles, ONES)
    pivot = affine[4:5]
    result = tap_product(
        z, kept, hidden[...] - pivot, (up[2 * r :] - pivot) * inside(z, 1, True),
        (down[:r] - pivot) * inside(z, 1, False), pads,
    )
    tap_sums(result, tiles, HIDDEN)
    kept_packed[...] = jnp.concatenate(tiles, axis=1)
    stores.append(pltpu.make_async_copy(kept_packed, packed, sems.at[6]))
    stores[1].start()
    pixels[own, :] = teacher[...]
    pixels[pl.ds(z.total, 4 * r), :] = jnp.zeros((4 * r, 128), F32)
    n = (REACH + 2) * r
    for side, beyond_of in enumerate((above_of, below_of)):
        for d in (0, 1):
            for k in (0, 1):
                line = beyond_of(pair, other, (pl.ds(n + k * z.images[0], z.images[k]), pl.ds(128 * d, 128)))
                for j in range(z.blocks[k]):
                    at = z.total + (2 * side + d) * r + z.rim[k] + j * z.images[k]
                    pixels[pl.ds(at, z.images[k]), pl.ds(0, BLOCK)] = line[:, j * BLOCK : (j + 1) * BLOCK]
    kept_t[...] = spread(pixels[...], to_channels())
    stores.append(pltpu.make_async_copy(kept_t, teachers, sems.at[3]))
    stores[2].start()
    n = REACH * r
    at = (pl.ds(n, 2 * r), pl.ds(0, LANES))
    up, down = above_of(pair, other, at) * inside(z, 2, True), below_of(pair, other, at) * inside(z, 2, False)
    kept_u[pl.ds(z.total, r), :] = up[r:]
    kept_u[pl.ds(z.total + r, r), :] = down[:r]
    wait_all(loads)
    stores.append(pltpu.make_async_copy(kept_u, near_u, sems.at[5]))
    stores[3].start()
    kept_c[...] = jnp.concatenate(convolve(z, kept_u[own, :], up, down, 2, pads, chains, kept_w.at[1]), axis=0)
    stores.append(pltpu.make_async_copy(kept_c, spread_u, sems.at[4]))
    stores[4].start()
    wait_all(stores)


def second_operand_kernel(z, hidden, near, stats, affine, out, o_above, o_below, teachers, spread_u, near_u, weights, out_copy, hidden_copy, left, shifts, by_map, by_teacher, up, pads, chains, kept_t, kept_u, kept_w, kept_s, sems):
    r, total = z.rims, z.total
    loads = [
        pltpu.make_async_copy(teachers, kept_t, sems.at[0]),
        pltpu.make_async_copy(weights.at[1], kept_w, sems.at[1]),
        pltpu.make_async_copy(spread_u, kept_u, sems.at[2]),
    ]
    start_all(loads)
    stores = [
        pltpu.make_async_copy(out, out_copy, sems.at[4]),
        pltpu.make_async_copy(hidden, hidden_copy.at[pl.ds(0, total), :], sems.at[7]),
        pltpu.make_async_copy(near.at[0], hidden_copy.at[pl.ds(total, r), :], sems.at[8]),
        pltpu.make_async_copy(near.at[1], hidden_copy.at[pl.ds(total + r, r), :], sems.at[9]),
        pltpu.make_async_copy(near_u, up, sems.at[10]),
    ]
    start_all(stores)
    normed = normed_by(stats)(jnp.concatenate([hidden[...], near[0], near[1]], axis=0))
    shifted = normed * affine[2:3] + affine[3:4]
    turned_operand(z, gelu(shifted[:total]), pads, left)
    ones = jnp.ones((total, 1), F32)
    masks = jnp.concatenate([ones, inside(z, 1, True), inside(z, 1, False)], axis=0)
    slopes = gelu_slope(shifted) * masks
    o = jnp.concatenate([out[...], o_above[...] * inside(z, 2, True), o_below[...] * inside(z, 2, False)], axis=0)
    for_map = spread(attention(o), to_channels()) * o
    wait_all(loads)
    for_teacher = kept_t[...] * o
    kept_s[0] = kept_u[...] * slopes
    stores += copies_of(pieces(kept_s, shifts), sems, 11)
    stores[-3].start()
    for n, value, ref in ((1, for_map, by_map), (2, for_teacher, by_teacher)):
        own, before, after = value[:total], value[total : total + 2 * r], value[total + 2 * r :]
        ref[...] = jnp.concatenate([own, before[r:], after[:r]], axis=0)
        kept_s[n] = jnp.concatenate(convolve(z, own, before, after, 2, pads, chains, kept_w), axis=0) * slopes
        stores[n - 3].start()
    wait_all(stores)


def upstream_kernel(z, gathered, up, shifts, left_1, left_2, packed, by_map, by_teacher, hidden, stats, dout, dshift, d_above, d_below, slabs, kept_s, kept_left, kept_h, kept_packed, pads, more_pads, sems):
    r, total = z.rims, z.total
    loads = copies_of(
        pieces(shifts, kept_s) + pieces(left_1, kept_left) + [(hidden.at[pl.ds(0, total), :], kept_h), (packed, kept_packed)], sems
    )
    start_all(loads)
    lane = lax.broadcasted_iota(jnp.int32, (z.slots, 128), 1)
    sums = sum(gathered[pl.ds(n * z.slots, z.slots), :] for n in range(z.peers))
    square = jnp.sum(jnp.where(lane < 64, sums, 0.0), axis=1, keepdims=True)
    cross = jnp.sum(jnp.where(lane < 64, 0.0, sums), axis=1, keepdims=True)
    inverse = lax.rsqrt(square + map_eps)
    inner = beta_weight * (square * inverse - cross) * inverse
    shape = (z.slots, 128)
    for_map = (beta_weight - inner) * inverse * inverse * (2.0 / C)
    for_teacher = beta_weight * inverse * (2.0 / C)
    for_map, for_teacher = (wide(image_rows(z, jnp.broadcast_to(v, shape), 2)) for v in (for_map, for_teacher))
    value = up[...] + for_map * by_map[...] - for_teacher * by_teacher[...]
    dout[...] = value[:total]
    second = tap_product(z, left_2, value[:total], value[total : total + r], value[total + r :], pads)
    wait_all(loads[:3])
    shift = kept_s[0] + for_map * kept_s[1] - for_teacher * kept_s[2]
    pre, above, below = shift[:total], shift[total : total + r], shift[total + r :]
    dshift[...] = pre
    d_above[...] = above
    d_below[...] = below
    wait_all(loads[3:5])
    first = tap_product(z, kept_left, pre, above, below, more_pads)
    wait_all(loads[5:])
    normed = normed_by(stats)(kept_h[...])
    tiles = [kept_packed[:, 128 * n : 128 * n + 128] for n in range(BACK_LANES // 128)]
    group = group_of()
    tiles[0] = jnp.where(group == BIAS, fold(column_sum(pre)), jnp.where(group == GAIN, fold(column_sum(pre * normed)), tiles[0]))
    tap_sums(second, tiles, SECOND)
    tap_sums(first, tiles, LEFT)
    line = jnp.concatenate(tiles, axis=1)
    for d in range(z.devices):
        slabs[d] = line[d % C : d % C + 1]


def write_kernel(z, out, x, hidden, weights, first_stats, stats, order, out_s, out_l, first_normed, normed, weight, kept, kept_x, kept_h, half, sems):
    loads = [pltpu.make_async_copy(a, b, sems.at[n]) for n, (a, b) in enumerate(((out, kept), (x, kept_x), (hidden, kept_h), (weights.at[0], weight)))]
    start_all(loads)
    loads[0].wait()
    put_halves(half, kept[...])
    from_matrix(z, half, (out_s, out_l))
    loads[1].wait()
    first_normed[...] = normed_by(first_stats)(kept_x[...])
    loads[2].wait()
    normed[...] = normed_by(stats)(kept_h[...])
    loads[3].wait()


def norm_sums(total):
    group = group_of()
    return [wide(spread_groups(jnp.where(group == n, total[:, :128], 0.0))) for n in (BIAS, GAIN)]


def hidden_kernel(z, gathered, dshift, d_above, d_below, second_normed, stats, affine, weight, first_normed, pre_ref, norm_grads, slabs, pads):
    total = jnp.sum(gathered[...], axis=0)
    bias_sum, gain_sum = norm_sums(total)
    norm_grads[0:1] = bias_sum[:, :128]
    norm_grads[1:2] = gain_sum[:, :128]
    bias_mean, gain_mean = bias_sum / z.pixels, gain_sum / z.pixels
    factor = affine[2:3] * stats[1:2]
    r, total_rows = z.rims, z.total

    def back(d, normed):
        return factor * (d - bias_mean - normed * gain_mean)

    own = back(dshift[...], second_normed[pl.ds(0, total_rows), :])
    up = back(d_above[...], second_normed[pl.ds(total_rows, r), :]) * inside(z, 1, True)
    down = back(d_below[...], second_normed[pl.ds(total_rows + r, r), :]) * inside(z, 1, False)
    grad, _, _ = convolve(z, own, up, down, 1, pads, None, weight)
    normed = first_normed[...]
    pre = grad * gelu_slope(normed * affine[0:1] + affine[1:2])
    pre_ref[...] = pre
    lane = lax.broadcasted_iota(jnp.int32, (1, 128), 1)
    taps = TAPS * TAPS * C

    def along(row):
        return jnp.concatenate([row[:, :128]] * 3, axis=1)[:, :taps]

    second, left, against, ones = (total[:, n * C : n * C + taps] for n in (SECOND, LEFT, HIDDEN, ONES))
    against = along(stats[1:2]) * (against - along(stats[0:1] - affine[4:5]) * ones)
    first = along(factor) * (left - along(bias_mean) * ones - along(gain_mean) * against)
    sums = jnp.where(lane < C, fold(column_sum(pre)), fold(column_sum(pre * normed)))
    line = jnp.concatenate([sums[:, : 2 * C], second, first], axis=1)
    slabs[...] = jnp.broadcast_to(line[None], slabs.shape)


def back_kernel(z, gathered, pre, normed, stats, affine, dout, second_grads, back_s, back_l, one, two, gain_out, bias_out, second_gain, second_bias, half, lines):
    bias_sum, gain_sum = norm_sums(jnp.sum(gathered[:, :, pl.ds(0, 128)], axis=0))
    bias_out[...] = bias_sum[:, :C]
    gain_out[...] = gain_sum[:, :C]
    second_bias[...] = second_grads[0:1, pl.ds(0, C)]
    second_gain[...] = second_grads[1:2, pl.ds(0, C)]
    value = dout[...] + affine[0:1] * stats[1:2] * (pre[...] - bias_sum / z.pixels - normed[...] * (gain_sum / z.pixels))
    put_halves(half, value)
    from_matrix(z, half, (back_s, back_l))
    for d in range(C):
        lines[pl.ds(d, 1), :] = gathered[d]
    for ref, group in ((two, LAST_SECOND), (one, LAST_FIRST)):
        for a in range(TAPS):
            for b in range(TAPS):
                at = (group + a * TAPS + b) * C
                ref[a, b] = lines[:, pl.ds(at, C)]


def call(body, ins, outs, scratch=(), sems=0):
    space = {"v": pltpu.VMEM, "h": pltpu.HBM, "V": pltpu.VMEM}
    shapes = []
    for item in scratch:
        if isinstance(item, list):
            shapes.append([pltpu.VMEM(*s) for s in item])
        else:
            shapes.append(pltpu.VMEM(*item))
    if sems:
        shapes.append(pltpu.SemaphoreType.DMA((sems,)))
    run = pl.pallas_call(
        body,
        out_shape=[jax.ShapeDtypeStruct(shape, kind) if s == "v" else space[s](shape, kind) for s, shape, kind in outs],
        in_specs=[pl.BlockSpec(memory_space=space[s]) for s in ins],
        out_specs=[pl.BlockSpec(memory_space=space[s]) for s, _, _ in outs],
        scratch_shapes=shapes,
        compiler_params=pltpu.CompilerParams(vmem_limit_bytes=VMEM_LIMIT),
    )
    return lambda *args: run(
        *(pltpu.with_memory_space_constraint(arg, pltpu.HBM) if s == "h" else arg for s, arg in zip(ins, args))
    )


def exchange(lines, axes):
    shape = lines.shape
    if len(shape) == 2:
        lines = lines.reshape(math.prod(lax.axis_size(axis) for axis in axes), -1, 128)
    return lax.all_to_all(lines, axes, 0, 0, tiled=True).reshape(shape)


def beyond(z, pair, other, depths):
    hops = max(-(-depth // rows) for rows in z.rows for depth in depths)
    if hops == 1:
        swap = lambda value, start: lax.ppermute(
            value, "row", [(i + a, i + 1 - a) for i in range(start, z.peers - 1, 2) for a in (0, 1)]
        )
        others = swap(other, 1)
        return swap(pair, 0), others
    even = is_even()
    bottom, top = jnp.where(even, pair, other), jnp.where(even, other, pair)
    above, below = [], []
    for hop in range(1, hops + 1):
        above.append(lax.ppermute(bottom, "row", [(i, i + hop) for i in range(z.peers - hop)]))
        below.append(lax.ppermute(top, "row", [(i + hop, i) for i in range(z.peers - hop)]))
    up, down = [], []
    base = 0
    for depth in depths:
        for n in range(depth):
            for k in (1, 0):
                hop, back = divmod(depth - 1 - n, z.rows[k])
                at = base + (depth - 1 - back) * z.rims + z.rim[k]
                up.append(above[hop][at : at + z.edge[k]])
                hop, back = divmod(n, z.rows[k])
                at = base + back * z.rims + z.rim[k]
                down.append(below[hop][at : at + z.edge[k]])
        base += depth * z.rims
    up.append(jnp.concatenate([pixel_rows(z, above, base, 1, 1), pixel_rows(z, above, base, 0, 1)], axis=1))
    down.append(jnp.concatenate([pixel_rows(z, below, base, 0, 0), pixel_rows(z, below, base, 1, 0)], axis=1))
    up, down = jnp.concatenate(up, axis=0), jnp.concatenate(down, axis=0)
    return jnp.where(even, down, up), jnp.where(even, up, down)


def pixel_rows(z, bands, base, distance, last):
    lines = []
    for k in (0, 1):
        hop, back = divmod(distance, z.rows[k])
        at = base + k * z.images[0]
        half = 128 * abs(last - back)
        lines.append(bands[hop][at : at + z.images[k], half : half + 128])
    lines.append(jnp.zeros((z.slots - sum(z.images), 128), F32))
    return jnp.concatenate(lines, axis=0)


def local(
    image_small, image_large, teacher_small, teacher_large, upstream_small, upstream_large,
    conv_first, gain_first, bias_first, conv_second, gain_second, bias_second,
):
    peers = lax.axis_size("row")
    devices = lax.axis_size("img") * peers
    z = Sizes(image_small.shape, image_large.shape, devices, peers)
    body = lambda function: functools.partial(function, z)
    r = z.rims
    full, half, pair = (z.total, LANES), (2, z.total, 128), (2 * devices, 128)
    weight, left = (2, TAPS * TAP_ROWS, 128), (2, 256, 2 * z.total)
    images = [image_small, image_large, upstream_small, upstream_large, teacher_small, teacher_large]
    f = lambda space, *shape: (space, shape, F32)
    depths = (REACH, 2)
    rim_rows = sum(depths) * r + z.slots

    x, pair_edge, other_edge, copies = call(
        body(start_kernel),
        "hhhhhh",
        [("v", full, F32), f("v", rim_rows, LANES), f("v", rim_rows, LANES), ("V", pair, F32)],
        [[(a.shape, F32) for a in images], (half, F32)],
        4 + 2 * z.images[1],
    )(*images)
    gathered = exchange(copies, AXES)
    pair_rims, other_rims = beyond(z, pair_edge, other_edge, depths)
    params = [conv_first, conv_second] + images[2:]
    w1, w2, weights, affine, upstream, teacher, x_copy = call(
        body(prepare_kernel),
        "hhhhhhhhhhv",
        [("v", weight, BF16), ("v", weight, BF16), ("h", (3,) + weight, BF16), f("v", 5, LANES), ("h", full, F32), f("v", z.total, 128), ("h", full, F32)],
        [[(a.shape, F32) for a in params], ((2,) + weight, BF16), (full, F32), ((4, C), F32), (half, F32)],
        15,
    )(*params, *(v.reshape(1, C) for v in (gain_first, bias_first, gain_second, bias_second)), x)

    hidden, stats_one, copies = call(
        body(first_kernel),
        "vvvvvv",
        [("v", full, F32), f("v", 2, LANES), ("V", pair, F32)],
        [z.pads()],
    )(x, pair_rims, other_rims, gathered, affine, w1)
    gathered = exchange(copies, AXES)
    extended, near_rows = z.total + 4 * r, z.total + 2 * r
    h_above, h_below, left_one, packed, teachers, spread_u, near_u = call(
        body(first_operand_kernel),
        "vvvvvvvhh",
        [f("v", 3 * r, LANES), f("v", 3 * r, LANES), ("h", left, BF16), f("h", C, BACK_LANES), f("h", extended, LANES), f("h", near_rows, LANES), f("h", near_rows, LANES)],
        [
            z.pads(), z.chains(2), z.chains(REACH), (left, BF16), ((2,) + weight, BF16), ((near_rows, LANES), F32), ((extended, 128), F32),
            ((extended, LANES), F32), ((near_rows, LANES), F32), ((C, BACK_LANES), F32),
        ],
        8,
    )(x, hidden, pair_rims, other_rims, stats_one, affine, teacher, upstream, weights)
    gathered, near_u = lax.optimization_barrier((gathered, near_u))

    map_shape = (peers * z.slots, 128)
    out, o_above, o_below, near, stats_two, copies = call(
        body(second_kernel),
        "vvvvvvvvvv",
        [("v", full, F32), f("v", 2 * r, LANES), f("v", 2 * r, LANES), f("v", 2, r, LANES), f("v", 2, LANES), ("V", map_shape, F32)],
        [z.pads(), z.chains(3)],
    )(hidden, h_above, h_below, gathered, affine, w2, x, pair_rims, other_rims, teacher)
    gathered = exchange(copies, ("row",))
    out_copy, hidden_copy, left_two, shifts, by_map, by_teacher, up = call(
        body(second_operand_kernel),
        "vvvvvvvhhhh",
        [
            ("h", full, F32), f("h", near_rows, LANES), ("v", left, BF16), f("h", 3, near_rows, LANES),
            f("v", near_rows, LANES), f("v", near_rows, LANES), f("v", near_rows, LANES),
        ],
        [
            z.pads(), z.chains(2), ((extended, LANES), F32), ((near_rows, LANES), F32), (weight, BF16),
            ((3, near_rows, LANES), F32),
        ],
        14,
    )(hidden, near, stats_two, affine, out, o_above, o_below, teachers, spread_u, near_u, weights)

    dout, dshift, d_above, d_below, slabs = call(
        body(upstream_kernel),
        "vvhhvhvvhv",
        [("v", full, F32), ("v", full, F32), f("v", r, LANES), f("v", r, LANES), f("V", devices, 1, BACK_LANES)],
        [((3, near_rows, LANES), F32), (left, BF16), (full, F32), ((C, BACK_LANES), F32), z.pads(), z.pads()],
        7,
    )(gathered, up, shifts, left_one, left_two, packed, by_map, by_teacher, hidden_copy, stats_two)
    gathered = exchange(slabs, AXES)
    out_s, out_l, first_normed, second_normed, weight_back = call(
        body(write_kernel),
        "hhhhvvv",
        [("v", image_small.shape, F32), ("v", image_large.shape, F32), ("v", full, F32), f("v", near_rows, LANES), ("v", weight, BF16)],
        [(full, F32), (full, F32), ((near_rows, LANES), F32), (half, F32)],
        4,
    )(out_copy, x_copy, hidden_copy, weights, stats_one, stats_two, d_above)

    pre, norm_grads, slabs = call(
        body(hidden_kernel),
        "vvvvvvvvv",
        [("v", full, F32), f("v", 2, 128), f("V", devices, 1, LAST_LANES)],
        [z.pads()],
    )(gathered, dshift, d_above, d_below, second_normed, stats_two, affine, weight_back, first_normed)
    gathered = exchange(slabs, AXES)

    back_s, back_l, one, two, gain_one, bias_one, gain_two, bias_two = call(
        body(back_kernel),
        "vvvvvvv",
        [("v", a.shape, F32) for a in (image_small, image_large, conv_first, conv_second)] + [f("v", 1, C)] * 4,
        [(half, F32), ((C, LAST_LANES), F32)],
    )(gathered, pre, first_normed, stats_one, affine, dout, norm_grads)
    return (
        out_s, out_l, back_s, back_l,
        one, gain_one.reshape(C), bias_one.reshape(C),
        two, gain_two.reshape(C), bias_two.reshape(C),
    )


def solution(mesh):
    split_bands, everywhere = P("img", "row", None), P()
    return jax.shard_map(
        local,
        mesh=mesh,
        in_specs=(split_bands,) * 6 + (everywhere,) * 6,
        out_specs=(split_bands,) * 4 + (everywhere,) * 6,
        check_vma=False,
    )
```
